32 devices in a mesh: groups: 2 (over y), grid: 4 (over z), atoms: 4 (over x, core).
Axes of the slice: x: 2, y: 2, z: 4, core: 2. Of those that a mesh axis runs over, the one named last changes fastest.
Arguments:
- basis: bfloat16 [512, 128, 4, 128], P(('groups', 'grid', 'atoms')), parts along dimension 0, may hold values from -6 to 6
- basis_grad: bfloat16 [3, 512, 128, 4, 128], P(None, ('groups', 'grid', 'atoms')), parts along dimension 1, may hold values from -6 to 6
- exchange_field: bfloat16 [512, 128, 4, 128], P(('groups', 'grid', 'atoms')), parts along dimension 0, may hold values from -6 to 6
- weights: float32 [512, 128], P(('groups', 'grid', 'atoms')), parts along dimension 0, may hold values from 0.0005 to 0.02
- weight_grad: float32 [3, 512, 128], P(None, ('groups', 'grid', 'atoms')), parts along dimension 1, may hold values from -0.06 to 0.06
- density: bfloat16 [120, 3, 128, 128], P(('groups', 'grid')), parts along dimension 0, may hold values from -0.375 to 0.375
- region: int32 [8, 4], P('groups'), parts along dimension 0, may hold values from 0 to 59, as said below
- pattern: int32 [512, 4], P(('groups', 'grid', 'atoms')), parts along dimension 0, may hold values from 0 to 3, as said below
- fn_atom: int32 [15360], P('groups'), parts along dimension 0, may hold values from 0 to 767, never falling along the last dimension, each value on 1 to 18 neighbouring positions
- batch_atom: int32 [512], P(('groups', 'grid', 'atoms')), parts along dimension 0, may hold values from 0 to 767
Outputs:
- contracted: bfloat16 [512, 128, 4, 128], P(('groups', 'grid', 'atoms')), parts along dimension 0
- gradient: float32 [3, 1536], P(None, ('groups', 'atoms')), parts along dimension 1
The draws below stay inside these ranges and needn't reach their ends.
There are 2 independent parts, one for each index of `groups`. The reference program is written for one: setup_inputs(seed, part) draws one part's arguments, and reference() takes and returns one part's arrays. A program takes and returns all parts, laid end to end along the dimension named above; each array names one. Nothing has to cross between parts.
Inputs may be any that keep to these rules, and one draw needn't show every extreme that they name: `region`: each row lists 4 increasing basis blocks; block r lies on grid index r // 15; at most 2 blocks of a row lie on one grid index, and in every row some grid index holds exactly 2; two blocks of a row on one grid index are consecutive blocks. `pattern`: each row names 4 different positions. `fn_atom`: never falls along the functions; each atom owns 1 to 18 consecutive functions.
All inputs are finite; a program needn't handle non-finite values.
Results may differ from the reference program's by a relative error of at most 0.008.
Values may be sent and summed in bfloat16 or wider, within the bound.
No kernel may reach another device: no remote copies, remote signals or barrier semaphores. Data moves between devices by JAX's collectives and lax.ppermute only.
A program may use at most 128 MiB of HBM per device.

```python
import math
import jax
import jax.numpy as jnp
import numpy as np
from jax import lax

PTS = 128
BS = 128
PB = 4
W = 3
HALF = 1
BLK_G = 15
SLABS = 4
REG = 4
SLAB_BATCHES = 64
NBATCH = 256
NBLK = 60
NBAS = 7680
NATOM = 768


def draw_region(key, part):
    key = jax.random.fold_in(key, 17)
    key_double, key_order, key_start = jax.random.split(key, 3)
    doubled = jax.random.randint(key_double, (SLABS, 1), 1, SLABS // 2 + 1)
    scores = jax.random.randint(key_order, (SLABS, SLABS), 0, 1 << 20) * SLABS + jnp.arange(SLABS)[None, :]
    ranking = jnp.argsort(jnp.argsort(scores, axis=1), axis=1)
    counts = jnp.where(ranking < doubled, 2, jnp.where(ranking < 2 * doubled, 0, 1))
    starts = jax.random.randint(key_start, (SLABS, SLABS), 0, BLK_G - 1)
    owner_ids = jnp.arange(SLABS)[None, :, None]
    within = jnp.arange(2)[None, None, :]
    candidates = owner_ids * BLK_G + starts[:, :, None] + within
    valid = within < counts[:, :, None]
    order_key = jnp.where(valid, owner_ids * 2 + within, 4 * SLABS).reshape(SLABS, 2 * SLABS)
    chosen = jnp.argsort(order_key, axis=1)[:, :REG]
    return jnp.take_along_axis(candidates.reshape(SLABS, 2 * SLABS), chosen, axis=1).astype(jnp.int32)


def draw_pattern(key, part):
    key = jax.random.fold_in(key, 29)
    scores = jax.random.randint(key, (NBATCH, REG), 0, 1 << 20) * REG + jnp.arange(REG)[None, :]
    return jnp.argsort(scores, axis=1)[:, :PB].astype(jnp.int32)


def plant(array, rng, least, largest):
    spot = [jax.random.randint(jax.random.fold_in(rng, axis), (), 0, length) for axis, length in enumerate(array.shape)]
    longest = array.shape.index(max(array.shape))
    next_to = spot[:longest] + [(spot[longest] + 1) % array.shape[longest]] + spot[longest + 1:]
    return array.at[tuple(spot)].set(least).at[tuple(next_to)].set(largest)


def level_of(stream_key, dims, cuts, smallest, top_value):
    level = 1.0
    for dim, blocks in cuts:
        heights = jax.random.uniform(jax.random.fold_in(jax.random.fold_in(stream_key, 6), dim), (blocks,), jnp.float32, smallest / len(cuts), top_value / len(cuts))
        level = level * jnp.repeat(jnp.exp(heights), dims[dim] // blocks).reshape((-1,) + (1,) * (len(dims) - 1 - dim))
    return level


def profile(number_of, total, most, lean):
    weights = [(1 << 20) // math.isqrt(grade ** lean) + 1 for grade in range(2, number_of + 1)]
    rest, given = total - most - (number_of - 1), [1] * (number_of - 1)
    while rest > 0:
        free = [i for i in range(number_of - 1) if given[i] < most]
        mass, remaining = sum([weights[i] for i in free]), rest
        for i in free:
            extra = min(most - given[i], max(1, remaining * weights[i] // mass), rest)
            given[i] = given[i] + extra
            rest = rest - extra
    return np.array([most] + given)


def ragged_sizes(stream_key, number_of, total, reach, skew):
    if number_of == 2:
        one = jax.random.randint(stream_key, (), max(1, total - reach), min(reach, total - 1) + 1)
        return jnp.stack([one, total - one])
    sizes = jnp.asarray(profile(number_of, total, reach, skew), jnp.int32)
    pairs = (number_of - 1) // 2
    source_of, taker = sizes[1:1 + 2 * pairs:2], sizes[2:2 + 2 * pairs:2]
    room = jnp.minimum(source_of - 1, reach - taker)
    shifted = jax.random.randint(jax.random.fold_in(stream_key, 1), (pairs,), 0, 1 << 20) % (room + 1)
    sizes = sizes.at[1:1 + 2 * pairs:2].set(source_of - shifted).at[2:2 + 2 * pairs:2].set(taker + shifted)
    return sizes[jax.random.permutation(jax.random.fold_in(stream_key, 2), number_of)]


def gaussian(rng, shape, width, reach, cuts=(), kind=jnp.bfloat16):
    drawn = width * jax.random.normal(rng, shape, jnp.float32)
    if cuts:
        drawn = drawn * level_of(rng, shape, cuts, -0.22, 0.18)
    return jnp.clip(drawn, -reach, reach).astype(kind)


def setup_inputs(seed: int = 0, part: int = 0) -> dict:
    keys = jax.random.split(jax.random.key(seed), 11)
    own_keys = jax.random.split(jax.random.fold_in(keys[10], part), 11)
    return {
        "basis": gaussian(own_keys[0], (NBATCH, PTS, PB, BS), 1.0, 6.0, ((0, 16),)),
        "basis_grad": gaussian(own_keys[1], (3, NBATCH, PTS, PB, BS), 1.0, 6.0, ((1, 16),)),
        "exchange_field": gaussian(own_keys[2], (NBATCH, PTS, PB, BS), 1.0, 6.0, ((0, 16),)),
        "weights": jnp.clip(jnp.exp(math.log(0.02) - 3.6888794 * jax.random.uniform(own_keys[3], (NBATCH, PTS), jnp.float32) ** level_of(own_keys[3], (NBATCH, PTS), ((0, 16),), -0.2, 0.2)), 0.0005, 0.02),
        "weight_grad": gaussian(own_keys[4], (3, NBATCH, PTS), 0.01, 0.06, ((1, 16),), jnp.float32),
        "density": gaussian(own_keys[5], (NBLK, W, BS, BS), (2 * BS) ** -0.5, 0.375, ((0, 4),)),
        "region": draw_region(jax.random.fold_in(jax.random.fold_in(keys[10], part), 71), part),
        "pattern": draw_pattern(jax.random.fold_in(jax.random.fold_in(keys[10], part), 71), part),
        "fn_atom": jnp.searchsorted(jnp.cumsum(ragged_sizes(own_keys[8], NATOM, NBAS, 18, 1)), jnp.arange(NBAS), side="right").astype(jnp.int32),
        "batch_atom": plant(jax.random.randint(own_keys[9], (NBATCH,), 0, NATOM), jax.random.fold_in(own_keys[9], 1), 0, NATOM - 1).astype(jnp.int32),
    }


def reference(basis, basis_grad, exchange_field, weights, weight_grad, density, region, pattern, fn_atom, batch_atom):
    slab_index = jnp.arange(NBATCH, dtype=jnp.int32) // SLAB_BATCHES
    block_rows = region[slab_index[:, None], pattern].astype(jnp.int32)
    offsets = jnp.arange(W, dtype=jnp.int32) - HALF

    def one_batch(index):
        rows_here = block_rows[index]
        density_tiles = density[rows_here].astype(jnp.float32)
        matches = (rows_here[None, :, None] == rows_here[:, None, None] + offsets[None, None, :]).astype(jnp.float32)
        spread = jnp.einsum("gsm,skmn->gskn", basis[index].astype(jnp.float32), density_tiles)
        product = jnp.einsum("gskn,stk->gtn", spread, matches)
        field = exchange_field[index].astype(jnp.float32)
        energy = jnp.sum(product * field, axis=(1, 2))
        picked = jnp.einsum("gtn,stk->gskn", field, matches)
        potential = jnp.einsum("gskn,skmn->gsm", picked, density_tiles)
        scaled = weights[index][:, None, None] * potential
        contribution = jnp.sum(basis_grad[:, index].astype(jnp.float32) * scaled[None], axis=1)
        weight_term = jnp.sum(weight_grad[:, index] * energy[None, :], axis=1)
        return product.astype(jnp.bfloat16), contribution, weight_term

    contracted, contribution, weight_term = lax.map(one_batch, jnp.arange(NBATCH, dtype=jnp.int32))
    function_index = block_rows[:, :, None] * BS + jnp.arange(BS, dtype=jnp.int32)[None, None, :]
    flat_ids = fn_atom[function_index].reshape(-1)
    results = []
    for component in range(3):
        derivative_part = jax.ops.segment_sum(contribution[:, component].reshape(-1), flat_ids, NATOM)
        weight_part = jax.ops.segment_sum(weight_term[:, component], batch_atom, NATOM)
        results.append(-2.0 * derivative_part + weight_part)
    return contracted, jnp.stack(results, axis=0)
```

```python
import functools

import jax
import jax.numpy as jnp
from jax import lax
from jax.experimental import pallas as pl
from jax.experimental.pallas import tpu as pltpu
from jax.sharding import PartitionSpec as P

CAP = 2
PARTS = 3
F32 = jnp.float32
BF16 = jnp.bfloat16
NT = (((1,), (1,)), ((), ()))
VMEM_LIMIT = 32 * 1024 * 1024


def owner_and_slot(region, slab, position, owner_rows):
    row = region[slab, position]
    owner = lax.div(row, owner_rows)
    slot = jnp.int32(0)
    for earlier in range(position):
        same = lax.div(region[slab, earlier], owner_rows) == owner
        slot = slot + jnp.where(same, 1, 0)
    return owner, slot


def pick_kernel(region, density, out, sems, *, owner_rows, quarter):
    me = lax.axis_index("grid")
    part = lax.axis_index("atoms")
    slabs, size = region.shape
    first = pl.multiple_of(part * quarter, quarter)

    def copies(slab):
        found = []
        for position in range(size):
            owner, slot = owner_and_slot(region, slab, position, owner_rows)
            mine = owner == me
            local_row = jnp.where(mine, region[slab, position] - me * owner_rows, 0)
            copy = pltpu.make_async_copy(
                density.at[local_row, :, pl.ds(first, quarter), :],
                out.at[slab, jnp.minimum(slot, CAP - 1)],
                sems.at[slab, position],
            )
            found.append((mine, copy))
        return found

    @pl.loop(0, slabs)
    def _(slab):
        for mine, copy in copies(slab):
            pl.when(mine)(copy.start)

    @pl.loop(0, slabs)
    def _(slab):
        for mine, copy in copies(slab):
            pl.when(mine)(copy.wait)


def pick_rows(region, density, slabs, atom_devices):
    owner_rows, width, size, _ = density.shape
    quarter = size // atom_devices
    return pl.pallas_call(
        functools.partial(pick_kernel, owner_rows=owner_rows, quarter=quarter),
        out_shape=jax.ShapeDtypeStruct((slabs, CAP, width, quarter, size), density.dtype),
        in_specs=[pl.BlockSpec(memory_space=pltpu.SMEM), pl.BlockSpec(memory_space=pl.ANY)],
        out_specs=pl.BlockSpec(memory_space=pltpu.VMEM),
        scratch_shapes=[pltpu.SemaphoreType.DMA(region.shape)],
        compiler_params=pltpu.CompilerParams(vmem_limit_bytes=VMEM_LIMIT),
    )(region, density)


def block_major(x_ref, wide, points, blocks):
    wide[...] = x_ref[0].astype(F32)
    return [wide[pl.ds(s, points, stride=blocks), :] for s in range(blocks)]


def relayout_kernel(basis, field, basis_out, field_out, wide, *, points, blocks):
    size = basis.shape[-1]
    for source, target in ((basis, basis_out), (field, field_out)):
        for s, part in enumerate(block_major(source, wide, points, blocks)):
            target[0, :, s * size : (s + 1) * size] = part.astype(BF16)


def relayout(basis, field, points, blocks):
    batches, rows, size = basis.shape
    here = pl.BlockSpec((1, rows, size), lambda b: (b, 0, 0))
    there = pl.BlockSpec((1, points, blocks * size), lambda b: (b, 0, 0))
    shape = jax.ShapeDtypeStruct((batches, points, blocks * size), BF16)
    return pl.pallas_call(
        functools.partial(relayout_kernel, points=points, blocks=blocks),
        grid=(batches,),
        out_shape=(shape, shape),
        in_specs=[here, here],
        out_specs=(there, there),
        scratch_shapes=[pltpu.VMEM((rows, size), F32)],
        compiler_params=pltpu.CompilerParams(vmem_limit_bytes=VMEM_LIMIT),
        cost_estimate=pl.CostEstimate(flops=0, bytes_accessed=8 * batches * rows * size, transcendentals=0),
    )(basis, field)


def batch_matrix(region, pattern, tiles, slab, batch, blocks, width):
    half = (width - 1) // 2
    none = tiles.shape[0] - 1
    places = [pattern[batch, s] for s in range(blocks)]
    rows = [region[slab, place] for place in places]
    strips = []
    for s in range(blocks):
        strip = []
        for t in range(blocks):
            k = rows[t] - rows[s] + half
            inside = jnp.logical_and(k >= 0, k < width)
            strip.append(tiles[jnp.where(inside, places[s] * width + k, none)])
        strips.append(jnp.concatenate(strip, axis=1))
    return jnp.concatenate(strips, axis=0)


def split(values):
    high = values.astype(BF16)
    rest = values - high.astype(F32)
    middle = rest.astype(BF16)
    low = (rest - middle.astype(F32)).astype(BF16)
    return high, middle, low


def gradient_kernel(
    region,
    pattern,
    basis,
    field,
    basis_grad,
    weights,
    weight_grad,
    fn_atom,
    batch_atom,
    places,
    *rest,
    points,
    blocks,
    width,
    owner_rows,
    slabs,
):
    *pieces, tiles, out, spread, sums, energy_sums = rest
    batch = pl.program_id(0)
    batches = pl.num_programs(0)
    me = lax.axis_index("grid")
    part = lax.axis_index("atoms")
    size = tiles.shape[-1]
    quarter = pieces[0].shape[-2]
    region_size = region.shape[1]

    @pl.when(batch == 0)
    def _():
        tiles[region_size * width] = jnp.zeros((size, size), BF16)
        for position in range(region_size):
            owner, slot = owner_and_slot(region, me, position, owner_rows)
            for step, piece in enumerate(pieces):
                first = pl.multiple_of(jnp.bitwise_xor(part, step) * quarter, quarter)
                for k in range(width):
                    tiles[position * width + k, pl.ds(first, quarter), :] = piece[owner, slot, k]

    matrix = batch_matrix(region, pattern, tiles, me, batch, blocks, width)
    potential = lax.dot_general(field[0], matrix, NT, preferred_element_type=F32)
    rows = jnp.concatenate(
        [weights[pl.ds(batch, 1), :]]
        + [weight_grad[c, pl.ds(batch, 1), :] for c in range(PARTS)]
        + [jnp.zeros((8 - 1 - PARTS, points), F32)],
        axis=0,
    )
    columns = rows.T
    weight = columns[:, 0:1]
    energy = jnp.zeros((points, size), F32)
    for s in range(blocks):
        here = potential[:, s * size : (s + 1) * size]
        energy = energy + basis[0, :, s * size : (s + 1) * size].astype(F32) * here
        spread[pl.ds(s, points, stride=blocks), :] = here * weight
    scaled = spread[...]
    place = pl.ds(pl.multiple_of(batch * 8, 8), 8)
    for c in range(PARTS):
        terms = basis_grad[c, 0].astype(F32) * scaled
        sums[c, place, :] = jnp.sum(terms.reshape(-1, 8, size), axis=0)
        terms = energy * columns[:, 1 + c : 2 + c]
        energy_sums[c, place, :] = jnp.sum(terms.reshape(-1, 8, size), axis=0)

    @pl.when(batch == batches - 1)
    def _():
        padded = max(8, region_size)
        chosen = lax.broadcasted_iota(jnp.int32, (padded, places.shape[1]), 0) == places[...]
        chosen = chosen.astype(BF16)
        blocks_sum = []
        for c in range(PARTS):
            total = jnp.zeros((padded, size), F32)
            for piece in split(sums[c]):
                total = total + jnp.dot(chosen, piece, preferred_element_type=F32)
            blocks_sum.append(-2.0 * total)
        lefts = []
        for position in range(region_size):
            stack = jnp.concatenate([total[position : position + 1] for total in blocks_sum], axis=0)
            high, middle, low = (piece.astype(F32) for piece in split(stack))
            lefts.append(jnp.concatenate([high, middle, low, jnp.zeros((16 - 3 * PARTS, size), F32)], axis=0))
        left = jnp.concatenate(lefts, axis=1).astype(BF16)
        chunk = out.shape[-1]
        scale = [jnp.sum(energy_sums[c], axis=1, keepdims=True) for c in range(PARTS)]
        for device in range(out.shape[1]):
            atoms = lax.broadcasted_iota(jnp.int32, (chunk, size), 0) + device * chunk
            hot = [
                jnp.where(atoms == fn_atom[pl.ds(region[me, position], 1), :], 1.0, 0.0).astype(BF16)
                for position in range(region_size)
            ]
            found = lax.dot_general(left, jnp.concatenate(hot, axis=1), NT, preferred_element_type=F32)
            atoms = lax.broadcasted_iota(jnp.int32, (batch_atom.shape[0], chunk), 1) + device * chunk
            mine = atoms == batch_atom[...]
            for c in range(PARTS):
                value = found[c : c + 1] + found[PARTS + c : PARTS + c + 1] + found[2 * PARTS + c : 2 * PARTS + c + 1]
                value = value + jnp.sum(jnp.where(mine, scale[c], 0.0), axis=0, keepdims=True)
                for slab in range(slabs):
                    out[slab, device, c : c + 1, :] = value


def partial_gradient(
    region, pattern, basis, field, basis_grad, weights, weight_grad, fn_atom, batch_atom, pieces, shapes
):
    slabs, atom_devices, atom_total, points, blocks, width, owner_rows = shapes
    batches, _, columns = basis.shape
    size = columns // blocks
    region_size = region.shape[1]
    fn_atom = fn_atom.reshape(-1, size)
    places = jnp.broadcast_to(pattern[:, None, :], (batches, 8 // blocks, blocks)).reshape(1, -1)
    batch_atom = jnp.broadcast_to(batch_atom[:, None], (batches, 8)).reshape(-1, 1)
    block = pl.BlockSpec((1, points, columns), lambda b, *_: (b, 0, 0))
    whole = pl.BlockSpec(memory_space=pltpu.VMEM)
    tile_shape = (region_size * width + 1, size, size)
    out_shape = (slabs, atom_devices, PARTS, atom_total // atom_devices)
    return pl.pallas_call(
        functools.partial(
            gradient_kernel, points=points, blocks=blocks, width=width, owner_rows=owner_rows, slabs=slabs
        ),
        grid_spec=pltpu.PrefetchScalarGridSpec(
            num_scalar_prefetch=2,
            grid=(batches,),
            in_specs=[
                block,
                block,
                pl.BlockSpec((PARTS, 1, points * blocks, size), lambda b, *_: (0, b, 0, 0)),
            ]
            + [whole] * (5 + len(pieces)),
            out_specs=(whole, whole),
            scratch_shapes=[
                pltpu.VMEM((points * blocks, size), F32),
                pltpu.VMEM((PARTS, batches * 8, size), F32),
                pltpu.VMEM((PARTS, batches * 8, size), F32),
            ],
        ),
        out_shape=(jax.ShapeDtypeStruct(tile_shape, BF16), jax.ShapeDtypeStruct(out_shape, F32)),
        compiler_params=pltpu.CompilerParams(vmem_limit_bytes=VMEM_LIMIT),
    )(region, pattern, basis, field, basis_grad, weights, weight_grad, fn_atom, batch_atom, places, *pieces)


def product_kernel(region, pattern, basis, tiles, out, spread, *, points, blocks, width):
    me = lax.axis_index("grid")
    size = tiles.shape[-1]
    matrix = batch_matrix(region, pattern, tiles, me, pl.program_id(0), blocks, width)
    product = jnp.dot(basis[0], matrix, preferred_element_type=F32)
    for t in range(blocks):
        spread[pl.ds(t, points, stride=blocks), :] = product[:, t * size : (t + 1) * size]
    out[0] = spread[...].astype(BF16)


def contract(region, pattern, basis, tiles, points, blocks, width):
    batches, _, columns = basis.shape
    size = columns // blocks
    return pl.pallas_call(
        functools.partial(product_kernel, points=points, blocks=blocks, width=width),
        grid_spec=pltpu.PrefetchScalarGridSpec(
            num_scalar_prefetch=2,
            grid=(batches,),
            in_specs=[
                pl.BlockSpec((1, points, columns), lambda b, *_: (b, 0, 0)),
                pl.BlockSpec(memory_space=pltpu.VMEM),
            ],
            out_specs=pl.BlockSpec((1, points * blocks, size), lambda b, *_: (b, 0, 0)),
            scratch_shapes=[pltpu.VMEM((points * blocks, size), F32)],
        ),
        out_shape=jax.ShapeDtypeStruct((batches, points * blocks, size), BF16),
        compiler_params=pltpu.CompilerParams(vmem_limit_bytes=VMEM_LIMIT),
        cost_estimate=pl.CostEstimate(
            flops=2 * batches * points * columns * columns,
            bytes_accessed=4 * batches * points * columns,
            transcendentals=0,
        ),
    )(region, pattern, basis, tiles)


def gather_atoms(piece, atom_devices):
    pieces = {0: piece}
    bit = atom_devices // 2
    while bit:
        swap = [(i, i ^ bit) for i in range(atom_devices)]
        for step in list(pieces):
            pieces[step ^ bit] = lax.ppermute(pieces[step], "atoms", swap)
        bit //= 2
    return [pieces[step] for step in range(atom_devices)]


def local(
    basis,
    basis_grad,
    exchange_field,
    weights,
    weight_grad,
    density,
    region,
    pattern,
    fn_atom,
    batch_atom,
):
    batches, points, blocks, size = basis.shape
    owner_rows, width = density.shape[:2]
    slabs = lax.axis_size("grid")
    atom_devices = lax.axis_size("atoms")
    atom_total = fn_atom.shape[0] // (10 * slabs * atom_devices) * slabs * atom_devices
    outgoing = pick_rows(region, density, slabs, atom_devices)
    arrived = lax.all_to_all(outgoing, "grid", split_axis=0, concat_axis=0, tiled=True)
    pieces = gather_atoms(arrived, atom_devices)
    basis_wide, field_wide = relayout(
        basis.reshape(batches, points * blocks, size),
        exchange_field.reshape(batches, points * blocks, size),
        points,
        blocks,
    )
    shapes = (slabs, atom_devices, atom_total, points, blocks, width, owner_rows)
    tiles, partial_grad = partial_gradient(
        region,
        pattern,
        basis_wide,
        field_wide,
        basis_grad.reshape(PARTS, batches, points * blocks, size),
        weights,
        weight_grad,
        fn_atom,
        batch_atom,
        pieces,
        shapes,
    )
    chunk = atom_total // atom_devices
    parts = lax.all_to_all(
        partial_grad.reshape(slabs * atom_devices, PARTS, chunk),
        ("grid", "atoms"),
        split_axis=0,
        concat_axis=0,
        tiled=True,
    )
    contracted = contract(region, pattern, basis_wide, tiles, points, blocks, width)
    return contracted.reshape(basis.shape), jnp.sum(parts, axis=0)


def solution(mesh):
    placed = (
        P(("groups", "grid", "atoms"), None, None, None),
        P(None, ("groups", "grid", "atoms"), None, None, None),
        P(("groups", "grid", "atoms"), None, None, None),
        P(("groups", "grid", "atoms"), None),
        P(None, ("groups", "grid", "atoms"), None),
        P(("groups", "grid"), None, None, None),
        P("groups", None),
        P(("groups", "grid", "atoms"), None),
        P("groups"),
        P(("groups", "grid", "atoms")),
    )
    return jax.shard_map(
        local,
        mesh=mesh,
        in_specs=placed,
        out_specs=(P(("groups", "grid", "atoms"), None, None, None), P(None, ("groups", "atoms"))),
        check_vma=False,
    )
```

```python
import functools

import jax
import jax.numpy as jnp
from jax import lax
from jax.experimental import pallas as pl
from jax.experimental.pallas import tpu as pltpu
from jax.sharding import PartitionSpec as P

TRAVEL = 5
SHARE = 2
PARTS = 3
F32 = jnp.float32
BF16 = jnp.bfloat16
NT = (((1,), (1,)), ((), ()))
VMEM_LIMIT = 32 * 1024 * 1024


def owner_and_slot(region, slab, position, owner_rows):
    owner = lax.div(region[slab, position], owner_rows)
    slot = jnp.int32(0)
    count = jnp.int32(0)
    for other in range(region.shape[1]):
        same = jnp.where(lax.div(region[slab, other], owner_rows) == owner, 1, 0)
        count = count + same
        if other < position:
            slot = slot + same
    return owner, slot, count


def travel_place(slot, count, k):
    if k == 0:
        return jnp.where(slot == 0, 4, 2)
    if k == 1:
        return jnp.where(slot == 0, 0, 3)
    return jnp.where(jnp.logical_and(slot == 0, count == 2), 1, 4)


def send_kernel(region, density, *rest, share):
    *outs, sems = rest
    me = lax.axis_index("grid")
    part = lax.rem(lax.axis_index("atoms"), share)
    slabs, size = region.shape
    owner_rows = density.shape[0]
    rows = density.shape[-2]
    copies = []
    for shift, out in enumerate(outs):
        slab = lax.rem(me + shift, slabs)
        base = jnp.int32(owner_rows)
        count = jnp.int32(0)
        for position in range(size):
            row = region[slab, position] - me * owner_rows
            mine = jnp.logical_and(row >= 0, row < owner_rows)
            base = jnp.minimum(base, jnp.where(mine, row, owner_rows))
            count = count + jnp.where(mine, 1, 0)
        base = jnp.where(count == 0, 0, base)
        after = jnp.minimum(base + 1, owner_rows - 1)
        lower = base == 0
        edge = jnp.where(jnp.logical_and(count == 2, jnp.logical_not(lower)), after, base)
        kept = out.shape[1]
        first = 0 if kept == rows else pl.multiple_of(part * kept, kept)
        here = pl.ds(first, kept)
        pairs = (
            (density.at[base, pl.ds(1, 2), here, :], out.at[pl.ds(0, 2)]),
            (density.at[after, pl.ds(0, 2), here, :], out.at[pl.ds(2, 2)]),
            (density.at[edge, jnp.where(lower, 0, 2), here, :], out.at[4]),
        )
        for number, (source, target) in enumerate(pairs):
            copies.append(pltpu.make_async_copy(source, target, sems.at[shift, number]))
    for copy in copies:
        copy.start()
    for copy in copies:
        copy.wait()


def in_hbm(array):
    return pltpu.with_memory_space_constraint(array, pltpu.HBM)


def rows_to_send(region, density, slabs, share):
    size = density.shape[-1]
    kept = [size] + [size // share] * (slabs - 1)
    return pl.pallas_call(
        functools.partial(send_kernel, share=share),
        out_shape=[jax.ShapeDtypeStruct((TRAVEL, rows, size), density.dtype) for rows in kept],
        in_specs=[pl.BlockSpec(memory_space=pltpu.SMEM), pl.BlockSpec(memory_space=pl.ANY)],
        out_specs=[pl.BlockSpec(memory_space=pltpu.VMEM)] * slabs,
        scratch_shapes=[pltpu.SemaphoreType.DMA((slabs, 3))],
        compiler_params=pltpu.CompilerParams(vmem_limit_bytes=VMEM_LIMIT),
    )(in_hbm(region), in_hbm(density))


def fetch_rows(region, density, slabs, share):
    own, *outgoing = rows_to_send(region, density, slabs, share)
    near = []
    for shift, piece in enumerate(outgoing, 1):
        near.append(lax.ppermute(piece, "grid", [(i, (i + shift) % slabs) for i in range(slabs)]))
    return own, near


def stage_rows(stage, own, near, far, share):
    part = lax.rem(lax.axis_index("atoms"), share)
    kept = near[0].shape[1]
    for place in range(TRAVEL):
        stage[place] = own[place]
        for shift, (here, there) in enumerate(zip(near, far), 1):
            stage[shift * TRAVEL + place, pl.ds(pl.multiple_of(part * kept, kept), kept), :] = here[place]
            stage[shift * TRAVEL + place, pl.ds(pl.multiple_of((1 - part) * kept, kept), kept), :] = there[place]


def block_major(x_ref, wide, points, blocks):
    wide[...] = x_ref[0].astype(F32)
    return [wide[pl.ds(s, points, stride=blocks), :] for s in range(blocks)]


def relayout_kernel(basis, field, basis_out, field_out, wide, *, points, blocks):
    size = basis.shape[-1]
    for source, target in ((basis, basis_out), (field, field_out)):
        for s, part in enumerate(block_major(source, wide, points, blocks)):
            target[0, :, s * size : (s + 1) * size] = part.astype(BF16)


def relayout(basis, field, points, blocks):
    batches, rows, size = basis.shape
    here = pl.BlockSpec((1, rows, size), lambda b: (b, 0, 0))
    there = pl.BlockSpec((1, points, blocks * size), lambda b: (b, 0, 0))
    shape = jax.ShapeDtypeStruct((batches, points, blocks * size), BF16)
    return pl.pallas_call(
        functools.partial(relayout_kernel, points=points, blocks=blocks),
        grid=(batches,),
        out_shape=(shape, shape),
        in_specs=[here, here],
        out_specs=(there, there),
        scratch_shapes=[pltpu.VMEM((rows, size), F32)],
        compiler_params=pltpu.CompilerParams(vmem_limit_bytes=VMEM_LIMIT),
        cost_estimate=pl.CostEstimate(flops=0, bytes_accessed=8 * batches * rows * size, transcendentals=0),
    )(basis, field)


def batch_matrix(region, pattern, tiles, slab, batch, blocks, width):
    half = (width - 1) // 2
    none = tiles.shape[0] - 1
    places = [pattern[batch, s] for s in range(blocks)]
    rows = [region[slab, place] for place in places]
    strips = []
    for s in range(blocks):
        strip = []
        for t in range(blocks):
            k = rows[t] - rows[s] + half
            inside = jnp.logical_and(k >= 0, k < width)
            strip.append(tiles[jnp.where(inside, places[s] * width + k, none)])
        strips.append(jnp.concatenate(strip, axis=1))
    return jnp.concatenate(strips, axis=0)


def split(values):
    high = values.astype(BF16)
    rest = values - high.astype(F32)
    middle = rest.astype(BF16)
    low = (rest - middle.astype(F32)).astype(BF16)
    return high, middle, low


def gradient_kernel(
    region,
    pattern,
    basis,
    field,
    basis_grad,
    weights,
    weight_grad,
    fn_atom,
    batch_atom,
    places,
    *rest,
    points,
    blocks,
    width,
    owner_rows,
    slabs,
):
    *pieces, tiles, out, stage, spread, sums, energy_sums = rest
    batch = pl.program_id(0)
    batches = pl.num_programs(0)
    me = lax.axis_index("grid")
    size = tiles.shape[-1]
    region_size = region.shape[1]

    @pl.when(batch == 0)
    def _():
        tiles[region_size * width] = jnp.zeros((size, size), BF16)
        stage_rows(stage, pieces[0], pieces[1:slabs], pieces[slabs:], SHARE)
        for position in range(region_size):
            owner, slot, count = owner_and_slot(region, me, position, owner_rows)
            shift = lax.rem(me - owner + slabs, slabs)
            for k in range(width):
                tiles[position * width + k] = stage[shift * TRAVEL + travel_place(slot, count, k)]

    matrix = batch_matrix(region, pattern, tiles, me, batch, blocks, width)
    potential = lax.dot_general(field[0], matrix, NT, preferred_element_type=F32)
    rows = jnp.concatenate(
        [weights[pl.ds(batch, 1), :]]
        + [weight_grad[c, pl.ds(batch, 1), :] for c in range(PARTS)]
        + [jnp.zeros((8 - 1 - PARTS, points), F32)],
        axis=0,
    )
    columns = rows.T
    weight = columns[:, 0:1]
    energy = jnp.zeros((points, size), F32)
    for s in range(blocks):
        here = potential[:, s * size : (s + 1) * size]
        energy = energy + basis[0, :, s * size : (s + 1) * size].astype(F32) * here
        spread[pl.ds(s, points, stride=blocks), :] = here * weight
    scaled = spread[...]
    place = pl.ds(pl.multiple_of(batch * 8, 8), 8)
    for c in range(PARTS):
        terms = basis_grad[c, 0].astype(F32) * scaled
        sums[c, place, :] = jnp.sum(terms.reshape(-1, 8, size), axis=0)
        terms = energy * columns[:, 1 + c : 2 + c]
        energy_sums[c, place, :] = jnp.sum(terms.reshape(-1, 8, size), axis=0)

    @pl.when(batch == batches - 1)
    def _():
        padded = max(8, region_size)
        chosen = lax.broadcasted_iota(jnp.int32, (padded, places.shape[1]), 0) == places[...]
        chosen = chosen.astype(BF16)
        blocks_sum = []
        for c in range(PARTS):
            total = jnp.zeros((padded, size), F32)
            for piece in split(sums[c]):
                total = total + jnp.dot(chosen, piece, preferred_element_type=F32)
            blocks_sum.append(-2.0 * total)
        lefts = []
        for position in range(region_size):
            stack = jnp.concatenate([total[position : position + 1] for total in blocks_sum], axis=0)
            high, middle, low = (piece.astype(F32) for piece in split(stack))
            lefts.append(jnp.concatenate([high, middle, low, jnp.zeros((16 - 3 * PARTS, size), F32)], axis=0))
        left = jnp.concatenate(lefts, axis=1).astype(BF16)
        chunk = out.shape[-1]
        scale = [jnp.sum(energy_sums[c], axis=1, keepdims=True) for c in range(PARTS)]
        for device in range(out.shape[1]):
            atoms = lax.broadcasted_iota(jnp.int32, (chunk, size), 0) + device * chunk
            hot = [
                jnp.where(atoms == fn_atom[pl.ds(region[me, position], 1), :], 1.0, 0.0).astype(BF16)
                for position in range(region_size)
            ]
            found = lax.dot_general(left, jnp.concatenate(hot, axis=1), NT, preferred_element_type=F32)
            atoms = lax.broadcasted_iota(jnp.int32, (batch_atom.shape[0], chunk), 1) + device * chunk
            mine = atoms == batch_atom[...]
            for c in range(PARTS):
                value = found[c : c + 1] + found[PARTS + c : PARTS + c + 1] + found[2 * PARTS + c : 2 * PARTS + c + 1]
                value = value + jnp.sum(jnp.where(mine, scale[c], 0.0), axis=0, keepdims=True)
                for slab in range(slabs):
                    out[slab, device, c : c + 1, :] = value


def partial_gradient(
    region, pattern, basis, field, basis_grad, weights, weight_grad, fn_atom, batch_atom, pieces, shapes
):
    slabs, atom_devices, atom_total, points, blocks, width, owner_rows = shapes
    batches, _, columns = basis.shape
    size = columns // blocks
    region_size = region.shape[1]
    fn_atom = fn_atom.reshape(-1, size)
    places = jnp.broadcast_to(pattern[:, None, :], (batches, 8 // blocks, blocks)).reshape(1, -1)
    batch_atom = jnp.broadcast_to(batch_atom[:, None], (batches, 8)).reshape(-1, 1)
    block = pl.BlockSpec((1, points, columns), lambda b, *_: (b, 0, 0))
    whole = pl.BlockSpec(memory_space=pltpu.VMEM)
    tile_shape = (region_size * width + 1, size, size)
    out_shape = (slabs, atom_devices, PARTS, atom_total // atom_devices)
    return pl.pallas_call(
        functools.partial(
            gradient_kernel, points=points, blocks=blocks, width=width, owner_rows=owner_rows, slabs=slabs
        ),
        grid_spec=pltpu.PrefetchScalarGridSpec(
            num_scalar_prefetch=2,
            grid=(batches,),
            in_specs=[
                block,
                block,
                pl.BlockSpec((PARTS, 1, points * blocks, size), lambda b, *_: (0, b, 0, 0)),
            ]
            + [whole] * (5 + len(pieces)),
            out_specs=(whole, whole),
            scratch_shapes=[
                pltpu.VMEM((slabs * TRAVEL, size, size), BF16),
                pltpu.VMEM((points * blocks, size), F32),
                pltpu.VMEM((PARTS, batches * 8, size), F32),
                pltpu.VMEM((PARTS, batches * 8, size), F32),
            ],
        ),
        out_shape=(jax.ShapeDtypeStruct(tile_shape, BF16), jax.ShapeDtypeStruct(out_shape, F32)),
        compiler_params=pltpu.CompilerParams(vmem_limit_bytes=VMEM_LIMIT),
    )(region, pattern, basis, field, basis_grad, weights, weight_grad, fn_atom, batch_atom, places, *pieces)


def product_kernel(region, pattern, basis, tiles, out, spread, *, points, blocks, width):
    me = lax.axis_index("grid")
    size = tiles.shape[-1]
    matrix = batch_matrix(region, pattern, tiles, me, pl.program_id(0), blocks, width)
    product = jnp.dot(basis[0], matrix, preferred_element_type=F32)
    for t in range(blocks):
        spread[pl.ds(t, points, stride=blocks), :] = product[:, t * size : (t + 1) * size]
    out[0] = spread[...].astype(BF16)


def contract(region, pattern, basis, tiles, points, blocks, width):
    batches, _, columns = basis.shape
    size = columns // blocks
    return pl.pallas_call(
        functools.partial(product_kernel, points=points, blocks=blocks, width=width),
        grid_spec=pltpu.PrefetchScalarGridSpec(
            num_scalar_prefetch=2,
            grid=(batches,),
            in_specs=[
                pl.BlockSpec((1, points, columns), lambda b, *_: (b, 0, 0)),
                pl.BlockSpec(memory_space=pltpu.VMEM),
            ],
            out_specs=pl.BlockSpec((1, points * blocks, size), lambda b, *_: (b, 0, 0)),
            scratch_shapes=[pltpu.VMEM((points * blocks, size), F32)],
        ),
        out_shape=jax.ShapeDtypeStruct((batches, points * blocks, size), BF16),
        compiler_params=pltpu.CompilerParams(vmem_limit_bytes=VMEM_LIMIT),
        cost_estimate=pl.CostEstimate(
            flops=2 * batches * points * columns * columns,
            bytes_accessed=4 * batches * points * columns,
            transcendentals=0,
        ),
    )(region, pattern, basis, tiles)


def local(
    basis,
    basis_grad,
    exchange_field,
    weights,
    weight_grad,
    density,
    region,
    pattern,
    fn_atom,
    batch_atom,
):
    batches, points, blocks, size = basis.shape
    owner_rows, width = density.shape[:2]
    slabs = lax.axis_size("grid")
    atom_devices = lax.axis_size("atoms")
    atom_total = fn_atom.shape[0] // (10 * slabs * atom_devices) * slabs * atom_devices
    own, near = fetch_rows(region, density, slabs, SHARE)
    basis_wide, field_wide = relayout(
        in_hbm(basis.reshape(batches, points * blocks, size)),
        in_hbm(exchange_field.reshape(batches, points * blocks, size)),
        points,
        blocks,
    )
    near, basis_wide, field_wide = lax.optimization_barrier((near, basis_wide, field_wide))
    swap = [(i, i ^ 1) for i in range(atom_devices)]
    far = [lax.ppermute(piece, "atoms", swap) for piece in near]
    pieces = [own, *near, *far]
    shapes = (slabs, atom_devices, atom_total, points, blocks, width, owner_rows)
    tiles, partial_grad = partial_gradient(
        region,
        pattern,
        basis_wide,
        field_wide,
        in_hbm(basis_grad.reshape(PARTS, batches, points * blocks, size)),
        weights,
        weight_grad,
        fn_atom,
        batch_atom,
        pieces,
        shapes,
    )
    chunk = atom_total // atom_devices
    parts = lax.all_to_all(
        partial_grad.reshape(slabs * atom_devices, PARTS, chunk),
        ("grid", "atoms"),
        split_axis=0,
        concat_axis=0,
        tiled=True,
    )
    contracted = contract(region, pattern, basis_wide, tiles, points, blocks, width)
    return contracted.reshape(basis.shape), jnp.sum(parts, axis=0)


def solution(mesh):
    placed = (
        P(("groups", "grid", "atoms"), None, None, None),
        P(None, ("groups", "grid", "atoms"), None, None, None),
        P(("groups", "grid", "atoms"), None, None, None),
        P(("groups", "grid", "atoms"), None),
        P(None, ("groups", "grid", "atoms"), None),
        P(("groups", "grid"), None, None, None),
        P("groups", None),
        P(("groups", "grid", "atoms"), None),
        P("groups"),
        P(("groups", "grid", "atoms")),
    )
    return jax.shard_map(
        local,
        mesh=mesh,
        in_specs=placed,
        out_specs=(P(("groups", "grid", "atoms"), None, None, None), P(None, ("groups", "atoms"))),
        check_vma=False,
    )
```

```python
import functools
import math

import jax
import jax.numpy as jnp
from jax import lax
from jax.experimental import pallas as pl
from jax.experimental.pallas import tpu as pltpu
from jax.sharding import PartitionSpec as P

TRAVEL = 5
SHARE = 2
PARTS = 3
F32 = jnp.float32
BF16 = jnp.bfloat16
NT = (((1,), (1,)), ((), ()))
VMEM_LIMIT = 32 * 1024 * 1024


def owner_and_slot(region, slab, position, owner_rows):
    owner = lax.div(region[slab, position], owner_rows)
    slot = jnp.int32(0)
    count = jnp.int32(0)
    for other in range(region.shape[1]):
        same = jnp.where(lax.div(region[slab, other], owner_rows) == owner, 1, 0)
        count = count + same
        if other < position:
            slot = slot + same
    return owner, slot, count


def travel_place(slot, count, k):
    if k == 0:
        return jnp.where(slot == 0, 4, 2)
    if k == 1:
        return jnp.where(slot == 0, 0, 3)
    return jnp.where(jnp.logical_and(slot == 0, count == 2), 1, 4)


def send_kernel(region, density, *rest, share):
    *outs, sems = rest
    me = lax.axis_index("grid")
    part = lax.rem(lax.axis_index("atoms"), share)
    size = region.shape[1]
    owner_rows = density.shape[0]
    rows = density.shape[-2]
    copies = []
    for shift, out in enumerate(outs):
        slab = jnp.bitwise_xor(me, shift)
        base = jnp.int32(owner_rows)
        count = jnp.int32(0)
        for position in range(size):
            row = region[slab, position] - me * owner_rows
            mine = jnp.logical_and(row >= 0, row < owner_rows)
            base = jnp.minimum(base, jnp.where(mine, row, owner_rows))
            count = count + jnp.where(mine, 1, 0)
        base = jnp.where(count == 0, 0, base)
        after = jnp.minimum(base + 1, owner_rows - 1)
        lower = base == 0
        edge = jnp.where(jnp.logical_and(count == 2, jnp.logical_not(lower)), after, base)
        kept = out.shape[1]
        first = 0 if kept == rows else pl.multiple_of(part * kept, kept)
        here = pl.ds(first, kept)
        pairs = (
            (density.at[base, pl.ds(1, 2), here, :], out.at[pl.ds(0, 2)]),
            (density.at[after, pl.ds(0, 2), here, :], out.at[pl.ds(2, 2)]),
            (density.at[edge, jnp.where(lower, 0, 2), here, :], out.at[4]),
        )
        for number, (source, target) in enumerate(pairs):
            copies.append(pltpu.make_async_copy(source, target, sems.at[shift, number]))
    for copy in copies:
        copy.start()
    for copy in copies:
        copy.wait()


def in_hbm(array):
    return pltpu.with_memory_space_constraint(array, pltpu.HBM)


def rows_to_send(region, density, slabs, share):
    size = density.shape[-1]
    kept = [size] + [size // share] * (slabs - 1)
    return pl.pallas_call(
        functools.partial(send_kernel, share=share),
        out_shape=[jax.ShapeDtypeStruct((TRAVEL, rows, size), density.dtype) for rows in kept],
        in_specs=[pl.BlockSpec(memory_space=pltpu.SMEM), pl.BlockSpec(memory_space=pl.ANY)],
        out_specs=[pl.BlockSpec(memory_space=pltpu.VMEM)] * slabs,
        scratch_shapes=[pltpu.SemaphoreType.DMA((slabs, 3))],
        compiler_params=pltpu.CompilerParams(vmem_limit_bytes=VMEM_LIMIT),
    )(in_hbm(region), in_hbm(density))


def fetch_rows(region, density, slabs, share):
    own, *outgoing = rows_to_send(region, density, slabs, share)
    near = []
    for shift, piece in enumerate(outgoing, 1):
        near.append(lax.ppermute(piece, "grid", [(i, i ^ shift) for i in range(slabs)]))
    return own, near


def stage_rows(stage, own, near, far, share):
    part = lax.rem(lax.axis_index("atoms"), share)
    kept = near[0].shape[1]
    for place in range(TRAVEL):
        stage[place] = own[place]
        for shift, (here, there) in enumerate(zip(near, far), 1):
            stage[shift * TRAVEL + place, pl.ds(pl.multiple_of(part * kept, kept), kept), :] = here[place]
            stage[shift * TRAVEL + place, pl.ds(pl.multiple_of((1 - part) * kept, kept), kept), :] = there[place]


def block_major(x_ref, wide, points, blocks):
    wide[...] = x_ref[0].astype(F32)
    return [wide[pl.ds(s, points, stride=blocks), :] for s in range(blocks)]


def relayout_kernel(basis, field, basis_out, field_out, wide, *, points, blocks):
    size = basis.shape[-1]
    for source, target in ((basis, basis_out), (field, field_out)):
        for s, part in enumerate(block_major(source, wide, points, blocks)):
            target[0, :, s * size : (s + 1) * size] = part.astype(BF16)


def relayout(basis, field, points, blocks):
    batches, rows, size = basis.shape
    here = pl.BlockSpec((1, rows, size), lambda b: (b, 0, 0))
    there = pl.BlockSpec((1, points, blocks * size), lambda b: (b, 0, 0))
    shape = jax.ShapeDtypeStruct((batches, points, blocks * size), BF16)
    return pl.pallas_call(
        functools.partial(relayout_kernel, points=points, blocks=blocks),
        grid=(batches,),
        out_shape=(shape, shape),
        in_specs=[here, here],
        out_specs=(there, there),
        scratch_shapes=[pltpu.VMEM((rows, size), F32)],
        compiler_params=pltpu.CompilerParams(vmem_limit_bytes=VMEM_LIMIT),
        cost_estimate=pl.CostEstimate(flops=0, bytes_accessed=8 * batches * rows * size, transcendentals=0),
    )(basis, field)


def batch_matrix(region, pattern, tiles, slab, batch, blocks, width):
    half = (width - 1) // 2
    none = tiles.shape[0] - 1
    places = [pattern[batch, s] for s in range(blocks)]
    rows = [region[slab, place] for place in places]
    strips = []
    for s in range(blocks):
        strip = []
        for t in range(blocks):
            k = rows[t] - rows[s] + half
            inside = jnp.logical_and(k >= 0, k < width)
            strip.append(tiles[jnp.where(inside, places[s] * width + k, none)])
        strips.append(jnp.concatenate(strip, axis=1))
    return jnp.concatenate(strips, axis=0)


def split(values):
    high = values.astype(BF16)
    rest = values - high.astype(F32)
    middle = rest.astype(BF16)
    low = (rest - middle.astype(F32)).astype(BF16)
    return high, middle, low


def gradient_kernel(
    region,
    pattern,
    basis,
    field,
    basis_grad,
    weights,
    weight_grad,
    fn_atom,
    batch_atom,
    places,
    *rest,
    points,
    blocks,
    width,
    owner_rows,
    slabs,
):
    *pieces, tiles, out, stage, spread, sums, energy_sums = rest
    batch = pl.program_id(0)
    batches = pl.num_programs(0)
    me = lax.axis_index("grid")
    size = tiles.shape[-1]
    region_size = region.shape[1]

    @pl.when(batch == 0)
    def _():
        tiles[region_size * width] = jnp.zeros((size, size), BF16)
        stage_rows(stage, pieces[0], pieces[1:slabs], pieces[slabs:], SHARE)
        for position in range(region_size):
            owner, slot, count = owner_and_slot(region, me, position, owner_rows)
            shift = jnp.bitwise_xor(me, owner)
            for k in range(width):
                tiles[position * width + k] = stage[shift * TRAVEL + travel_place(slot, count, k)]

    matrix = batch_matrix(region, pattern, tiles, me, batch, blocks, width)
    potential = lax.dot_general(field[0], matrix, NT, preferred_element_type=F32)
    rows = jnp.concatenate(
        [weights[pl.ds(batch, 1), :]]
        + [weight_grad[c, pl.ds(batch, 1), :] for c in range(PARTS)]
        + [jnp.zeros((8 - 1 - PARTS, points), F32)],
        axis=0,
    )
    columns = rows.T
    weight = columns[:, 0:1]
    energy = jnp.zeros((points, size), F32)
    for s in range(blocks):
        here = potential[:, s * size : (s + 1) * size]
        energy = energy + basis[0, :, s * size : (s + 1) * size].astype(F32) * here
        spread[pl.ds(s, points, stride=blocks), :] = here * weight
    scaled = spread[...]
    place = pl.ds(pl.multiple_of(batch * 8, 8), 8)
    for c in range(PARTS):
        terms = basis_grad[c, 0].astype(F32) * scaled
        sums[c, place, :] = jnp.sum(terms.reshape(-1, 8, size), axis=0)
        terms = energy * columns[:, 1 + c : 2 + c]
        energy_sums[c, place, :] = jnp.sum(terms.reshape(-1, 8, size), axis=0)

    @pl.when(batch == batches - 1)
    def _():
        padded = max(8, region_size)
        chosen = lax.broadcasted_iota(jnp.int32, (padded, places.shape[1]), 0) == places[...]
        chosen = chosen.astype(BF16)
        blocks_sum = []
        for c in range(PARTS):
            total = jnp.zeros((padded, size), F32)
            for piece in split(sums[c]):
                total = total + jnp.dot(chosen, piece, preferred_element_type=F32)
            blocks_sum.append(-2.0 * total)
        lefts = []
        for position in range(region_size):
            stack = jnp.concatenate([total[position : position + 1] for total in blocks_sum], axis=0)
            high, middle, low = (piece.astype(F32) for piece in split(stack))
            lefts.append(jnp.concatenate([high, middle, low, jnp.zeros((16 - 3 * PARTS, size), F32)], axis=0))
        left = jnp.concatenate(lefts, axis=1).astype(BF16)
        chunk = out.shape[-1]
        scale = [jnp.sum(energy_sums[c], axis=1, keepdims=True) for c in range(PARTS)]
        for device in range(out.shape[1]):
            atoms = lax.broadcasted_iota(jnp.int32, (chunk, size), 0) + device * chunk
            hot = [
                jnp.where(atoms == fn_atom[pl.ds(region[me, position], 1), :], 1.0, 0.0).astype(BF16)
                for position in range(region_size)
            ]
            found = lax.dot_general(left, jnp.concatenate(hot, axis=1), NT, preferred_element_type=F32)
            atoms = lax.broadcasted_iota(jnp.int32, (batch_atom.shape[0], chunk), 1) + device * chunk
            mine = atoms == batch_atom[...]
            for c in range(PARTS):
                value = found[c : c + 1] + found[PARTS + c : PARTS + c + 1] + found[2 * PARTS + c : 2 * PARTS + c + 1]
                value = value + jnp.sum(jnp.where(mine, scale[c], 0.0), axis=0, keepdims=True)
                for slab in range(slabs):
                    out[slab, device, c : c + 1, :] = value


def partial_gradient(
    region, pattern, basis, field, basis_grad, weights, weight_grad, fn_atom, batch_atom, pieces, shapes
):
    slabs, atom_devices, atom_total, points, blocks, width, owner_rows = shapes
    batches, _, columns = basis.shape
    size = columns // blocks
    region_size = region.shape[1]
    fn_atom = fn_atom.reshape(-1, size)
    places = jnp.broadcast_to(pattern[:, None, :], (batches, 8 // blocks, blocks)).reshape(1, -1)
    batch_atom = jnp.broadcast_to(batch_atom[:, None], (batches, 8)).reshape(-1, 1)
    block = pl.BlockSpec((1, points, columns), lambda b, *_: (b, 0, 0))
    whole = pl.BlockSpec(memory_space=pltpu.VMEM)
    tile_shape = (region_size * width + 1, size, size)
    out_shape = (slabs, atom_devices, PARTS, atom_total // atom_devices)
    return pl.pallas_call(
        functools.partial(
            gradient_kernel, points=points, blocks=blocks, width=width, owner_rows=owner_rows, slabs=slabs
        ),
        grid_spec=pltpu.PrefetchScalarGridSpec(
            num_scalar_prefetch=2,
            grid=(batches,),
            in_specs=[
                block,
                block,
                pl.BlockSpec((PARTS, 1, points * blocks, size), lambda b, *_: (0, b, 0, 0)),
            ]
            + [whole] * (5 + len(pieces)),
            out_specs=(whole, whole),
            scratch_shapes=[
                pltpu.VMEM((slabs * TRAVEL, size, size), BF16),
                pltpu.VMEM((points * blocks, size), F32),
                pltpu.VMEM((PARTS, batches * 8, size), F32),
                pltpu.VMEM((PARTS, batches * 8, size), F32),
            ],
        ),
        out_shape=(jax.ShapeDtypeStruct(tile_shape, BF16), jax.ShapeDtypeStruct(out_shape, F32)),
        compiler_params=pltpu.CompilerParams(vmem_limit_bytes=VMEM_LIMIT),
    )(region, pattern, basis, field, basis_grad, weights, weight_grad, fn_atom, batch_atom, places, *pieces)


def product_kernel(region, pattern, basis, tiles, out, spread, *, points, blocks, width):
    me = lax.axis_index("grid")
    size = tiles.shape[-1]
    matrix = batch_matrix(region, pattern, tiles, me, pl.program_id(0), blocks, width)
    product = jnp.dot(basis[0], matrix, preferred_element_type=F32)
    for t in range(blocks):
        spread[pl.ds(t, points, stride=blocks), :] = product[:, t * size : (t + 1) * size]
    out[0] = spread[...].astype(BF16)


def contract(region, pattern, basis, tiles, points, blocks, width):
    batches, _, columns = basis.shape
    size = columns // blocks
    return pl.pallas_call(
        functools.partial(product_kernel, points=points, blocks=blocks, width=width),
        grid_spec=pltpu.PrefetchScalarGridSpec(
            num_scalar_prefetch=2,
            grid=(batches,),
            in_specs=[
                pl.BlockSpec((1, points, columns), lambda b, *_: (b, 0, 0)),
                pl.BlockSpec(memory_space=pltpu.VMEM),
            ],
            out_specs=pl.BlockSpec((1, points * blocks, size), lambda b, *_: (b, 0, 0)),
            scratch_shapes=[pltpu.VMEM((points * blocks, size), F32)],
        ),
        out_shape=jax.ShapeDtypeStruct((batches, points * blocks, size), BF16),
        compiler_params=pltpu.CompilerParams(vmem_limit_bytes=VMEM_LIMIT),
        cost_estimate=pl.CostEstimate(
            flops=2 * batches * points * columns * columns,
            bytes_accessed=4 * batches * points * columns,
            transcendentals=0,
        ),
    )(region, pattern, basis, tiles)


def prepare_kernel(
    region,
    pattern,
    basis,
    field,
    basis_grad,
    weights,
    weight_grad,
    fn_atom,
    batch_atom,
    basis_out,
    field_out,
    moments,
    hot,
    grad_columns,
    basis_in,
    field_in,
    grad_in,
    wide,
    turned,
    grad_wide,
    sems,
    *,
    points,
    blocks,
    step,
):
    batches, _, size = basis.shape
    groups = batches // step
    me = lax.axis_index("grid")

    def copies(group):
        here = pl.ds(group * step, step)
        return (
            pltpu.make_async_copy(field.at[here], field_in.at[here], sems.at[group, 0]),
            pltpu.make_async_copy(basis_grad.at[:, here], grad_in.at[:, here], sems.at[group, 1]),
            pltpu.make_async_copy(basis.at[here], basis_in.at[here], sems.at[group, 2]),
        )

    for group in range(groups):
        for copy in copies(group):
            copy.start()

    atoms = lax.broadcasted_iota(jnp.int32, (hot.shape[0], size), 0)
    for position in range(blocks):
        ids = fn_atom[pl.ds(region[me, position], 1), :]
        hot[:, position * size : (position + 1) * size] = jnp.where(atoms == ids, 1.0, 0.0).astype(BF16)
    ids = jnp.concatenate([batch_atom[...], jnp.full((1, size - batches), -1, jnp.int32)], axis=1)
    hot[:, blocks * size :] = jnp.where(atoms == ids, 1.0, 0.0).astype(BF16)
    for c in range(PARTS):
        rows = jnp.concatenate([weight_grad[c], jnp.zeros((size - batches, points), F32)], axis=0)
        grad_columns[c] = rows.T

    @pl.loop(0, groups)
    def _(group):
        for copy in copies(group):
            copy.wait()
        for inner in range(step):
            batch = group * step + inner
            points_here = pl.ds(pl.multiple_of(batch * points, points), points)
            places = [pattern[s, batch] for s in range(blocks)]
            weight = weights[pl.ds(batch, 1), :]
            wide[0] = field_in[batch].astype(F32)
            wide[1] = basis_in[batch].astype(F32)
            for c in range(PARTS):
                wide[2 + c] = grad_in[c, batch].astype(F32)
            for s, place in enumerate(places):
                strided = pl.ds(s, points, stride=blocks)
                values = wide[0, strided, :]
                field_out[batch, place] = values.astype(BF16)
                turned[pl.ds(pl.multiple_of(place * size, size), size), points_here] = (values.T * weight).astype(BF16)
                basis_out[batch, place] = wide[1, strided, :].astype(BF16)
                for c in range(PARTS):
                    grad_wide[c, place, points_here, :] = wide[2 + c, strided, :].astype(BF16)

    for c in range(PARTS):
        right = jnp.concatenate([grad_wide[c, place] for place in range(blocks)], axis=1)
        moments[c] = jnp.dot(turned[...], right, preferred_element_type=F32)


def prepare(region, pattern, basis, field, basis_grad, weights, weight_grad, fn_atom, batch_atom, atom_total):
    batches, points, blocks, size = basis.shape
    rows = points * blocks
    step = 2 if batches % 2 == 0 else 1
    smem = pl.BlockSpec(memory_space=pltpu.SMEM)
    hbm = pl.BlockSpec(memory_space=pl.ANY)
    vmem = pl.BlockSpec(memory_space=pltpu.VMEM)
    ordered = jax.ShapeDtypeStruct((batches, blocks, points, size), BF16)
    return pl.pallas_call(
        functools.partial(prepare_kernel, points=points, blocks=blocks, step=step),
        out_shape=(
            ordered,
            ordered,
            jax.ShapeDtypeStruct((PARTS, blocks * size, blocks * size), F32),
            jax.ShapeDtypeStruct((atom_total, (blocks + 1) * size), BF16),
            jax.ShapeDtypeStruct((PARTS, points, size), F32),
        ),
        in_specs=[smem, smem, hbm, hbm, hbm, vmem, vmem, vmem, vmem],
        out_specs=(vmem,) * 5,
        scratch_shapes=[
            pltpu.VMEM((batches, rows, size), BF16),
            pltpu.VMEM((batches, rows, size), BF16),
            pltpu.VMEM((PARTS, batches, rows, size), BF16),
            pltpu.VMEM((2 + PARTS, rows, size), F32),
            pltpu.VMEM((blocks * size, batches * points), BF16),
            pltpu.VMEM((PARTS, blocks, batches * points, size), BF16),
            pltpu.SemaphoreType.DMA((batches // step, 3)),
        ],
        compiler_params=pltpu.CompilerParams(vmem_limit_bytes=VMEM_LIMIT),
        cost_estimate=pl.CostEstimate(
            flops=2 * PARTS * batches * points * (blocks * size) ** 2,
            bytes_accessed=2 * (2 + PARTS) * batches * rows * size,
            transcendentals=0,
        ),
    )(
        in_hbm(region),
        in_hbm(pattern.T),
        in_hbm(basis.reshape(batches, rows, size)),
        in_hbm(field.reshape(batches, rows, size)),
        in_hbm(basis_grad.reshape(PARTS, batches, rows, size)),
        in_hbm(weights),
        in_hbm(weight_grad),
        in_hbm(fn_atom.reshape(-1, size)),
        in_hbm(batch_atom.reshape(1, -1)),
    )


def combine_kernel(
    region, basis, field, moments, hot, grad_columns, *rest, owner_rows, slabs, width, step
):
    *pieces, product_out, out, stage, matrix, energies = rest
    batches, blocks, points, size = basis.shape
    me = lax.axis_index("grid")
    half = (width - 1) // 2
    stage_rows(stage, pieces[0], pieces[1:slabs], pieces[slabs:], SHARE)
    rows = [region[me, position] for position in range(blocks)]
    found = [owner_and_slot(region, me, position, owner_rows) for position in range(blocks)]
    totals = [[jnp.zeros((8, size), F32) for _ in range(blocks)] for _ in range(PARTS)]
    for p in range(blocks):
        owner, slot, count = found[p]
        first = jnp.bitwise_xor(me, owner) * TRAVEL
        for q in range(blocks):
            k = rows[q] - rows[p] + half
            place = jnp.where(
                k == 0,
                travel_place(slot, count, 0),
                jnp.where(k == 1, travel_place(slot, count, 1), travel_place(slot, count, 2)),
            )
            inside = jnp.logical_and(k >= 0, k < width)
            tile = stage[first + place].astype(F32)
            tile = jnp.where(inside, tile, 0.0)
            matrix[p * size : (p + 1) * size, q * size : (q + 1) * size] = tile.astype(BF16)
            turned = tile.T
            for c in range(PARTS):
                terms = turned * moments[c, q * size : (q + 1) * size, p * size : (p + 1) * size]
                totals[c][p] = totals[c][p] + jnp.sum(terms.reshape(-1, 8, size), axis=0)
    derivative = [
        jnp.concatenate([jnp.sum(total, axis=0, keepdims=True) for total in totals[c]], axis=1) for c in range(PARTS)
    ]

    energies[...] = jnp.zeros_like(energies)
    lanes = lax.broadcasted_iota(jnp.int32, (points, size), 1)

    @pl.loop(0, batches // step)
    def _(group):
        left = [
            jnp.concatenate([basis[group * step + inner, p] for p in range(blocks)], axis=1) for inner in range(step)
        ]
        product = jnp.dot(jnp.concatenate(left, axis=0), matrix[...], preferred_element_type=F32)
        for inner in range(step):
            batch = group * step + inner
            energy = jnp.zeros((points, size), F32)
            for q in range(blocks):
                part = product[inner * points : (inner + 1) * points, q * size : (q + 1) * size]
                product_out[batch, q] = part.astype(BF16)
                energy = energy + part * field[batch, q].astype(F32)
            energy = jnp.sum(energy, axis=1, keepdims=True)
            energies[...] = jnp.where(lanes == batch, energy, energies[...])

    lefts = []
    for c in range(PARTS):
        term = jnp.sum(energies[...] * grad_columns[c], axis=0, keepdims=True)
        lefts.append(jnp.concatenate([-2.0 * derivative[c], term], axis=1))
    left = jnp.concatenate(lefts, axis=0)
    high, middle, low = (piece.astype(F32) for piece in split(left))
    left = jnp.concatenate([high, middle, low, jnp.zeros((16 - 3 * PARTS, left.shape[1]), F32)], axis=0).astype(BF16)
    chunk = out.shape[-1]
    for device in range(out.shape[1]):
        sums = lax.dot_general(
            left, hot[device * chunk : (device + 1) * chunk, :], NT, preferred_element_type=F32
        )
        value = sums[:PARTS] + sums[PARTS : 2 * PARTS] + sums[2 * PARTS : 3 * PARTS]
        for slab in range(slabs):
            out[slab, device] = value


def combine(region, prepared, pieces, shapes):
    basis, field, moments, hot, grad_columns = prepared
    slabs, atom_devices, atom_total, points, blocks, width, owner_rows = shapes
    batches, _, _, size = basis.shape
    step = 4 if batches % 4 == 0 else 1
    vmem = pl.BlockSpec(memory_space=pltpu.VMEM)
    return pl.pallas_call(
        functools.partial(combine_kernel, owner_rows=owner_rows, slabs=slabs, width=width, step=step),
        out_shape=(
            jax.ShapeDtypeStruct(basis.shape, BF16),
            jax.ShapeDtypeStruct((slabs, atom_devices, PARTS, atom_total // atom_devices), F32),
        ),
        in_specs=[pl.BlockSpec(memory_space=pltpu.SMEM)] + [vmem] * (5 + len(pieces)),
        out_specs=(vmem, vmem),
        scratch_shapes=[
            pltpu.VMEM((slabs * TRAVEL, size, size), BF16),
            pltpu.VMEM((blocks * size, blocks * size), BF16),
            pltpu.VMEM((points, size), F32),
        ],
        compiler_params=pltpu.CompilerParams(vmem_limit_bytes=VMEM_LIMIT),
    )(in_hbm(region), basis, field, moments, hot, grad_columns, *pieces)


def write_kernel(pattern, product, out, wide, staged, sems):
    batches, blocks, points, size = product.shape

    def copy(batch):
        return pltpu.make_async_copy(staged.at[batch], out.at[batch], sems.at[batch])

    @pl.loop(0, batches // 2)
    def _(pair):
        for inner in range(2):
            batch = pair * 2 + inner
            for t in range(blocks):
                wide[inner, pl.ds(t, points, stride=blocks), :] = product[batch, pattern[t, batch]].astype(F32)
            staged[batch] = wide[inner].astype(BF16)
            copy(batch).start()

    @pl.loop(0, batches)
    def _(batch):
        copy(batch).wait()


def write(pattern, product):
    batches, blocks, points, size = product.shape
    shape = (batches, points * blocks, size)
    return pl.pallas_call(
        write_kernel,
        out_shape=jax.ShapeDtypeStruct(shape, BF16),
        in_specs=[pl.BlockSpec(memory_space=pltpu.SMEM), pl.BlockSpec(memory_space=pltpu.VMEM)],
        out_specs=pl.BlockSpec(memory_space=pl.ANY),
        scratch_shapes=[
            pltpu.VMEM((2, points * blocks, size), F32),
            pltpu.VMEM(shape, BF16),
            pltpu.SemaphoreType.DMA((batches,)),
        ],
        compiler_params=pltpu.CompilerParams(vmem_limit_bytes=VMEM_LIMIT),
        cost_estimate=pl.CostEstimate(flops=0, bytes_accessed=4 * math.prod(shape), transcendentals=0),
    )(in_hbm(pattern.T), product)


def swap_halves(near, ready, atom_devices):
    near, ready = lax.optimization_barrier((near, ready))
    swap = [(i, i ^ 1) for i in range(atom_devices)]
    return near, [lax.ppermute(piece, "atoms", swap) for piece in near], ready


def sum_parts(partial_grad):
    parts = partial_grad.reshape((-1,) + partial_grad.shape[2:])
    parts = lax.all_to_all(parts, ("grid", "atoms"), split_axis=0, concat_axis=0, tiled=True)
    return jnp.sum(parts, axis=0)


def local(
    basis,
    basis_grad,
    exchange_field,
    weights,
    weight_grad,
    density,
    region,
    pattern,
    fn_atom,
    batch_atom,
):
    batches, points, blocks, size = basis.shape
    owner_rows, width = density.shape[:2]
    slabs = lax.axis_size("grid")
    atom_devices = lax.axis_size("atoms")
    atom_total = fn_atom.shape[0] // (10 * slabs * atom_devices) * slabs * atom_devices
    shapes = (slabs, atom_devices, atom_total, points, blocks, width, owner_rows)
    own, near = fetch_rows(region, density, slabs, SHARE)
    if region.shape[1] == blocks:
        ready = prepare(
            region, pattern, basis, exchange_field, basis_grad, weights, weight_grad, fn_atom, batch_atom, atom_total
        )
        near, far, ready = swap_halves(near, ready, atom_devices)
        product, partial_grad = combine(region, ready, [own, *near, *far], shapes)
        gradient = sum_parts(partial_grad)
        contracted = write(pattern, product)
        return contracted.reshape(basis.shape), gradient
    ready = relayout(
        in_hbm(basis.reshape(batches, points * blocks, size)),
        in_hbm(exchange_field.reshape(batches, points * blocks, size)),
        points,
        blocks,
    )
    near, far, (basis_wide, field_wide) = swap_halves(near, ready, atom_devices)
    tiles, partial_grad = partial_gradient(
        region,
        pattern,
        basis_wide,
        field_wide,
        in_hbm(basis_grad.reshape(PARTS, batches, points * blocks, size)),
        weights,
        weight_grad,
        fn_atom,
        batch_atom,
        [own, *near, *far],
        shapes,
    )
    gradient = sum_parts(partial_grad)
    contracted = contract(region, pattern, basis_wide, tiles, points, blocks, width)
    return contracted.reshape(basis.shape), gradient


def solution(mesh):
    placed = (
        P(("groups", "grid", "atoms"), None, None, None),
        P(None, ("groups", "grid", "atoms"), None, None, None),
        P(("groups", "grid", "atoms"), None, None, None),
        P(("groups", "grid", "atoms"), None),
        P(None, ("groups", "grid", "atoms"), None),
        P(("groups", "grid"), None, None, None),
        P("groups", None),
        P(("groups", "grid", "atoms"), None),
        P("groups"),
        P(("groups", "grid", "atoms")),
    )
    return jax.shard_map(
        local,
        mesh=mesh,
        in_specs=placed,
        out_specs=(P(("groups", "grid", "atoms"), None, None, None), P(None, ("groups", "atoms"))),
        check_vma=False,
    )
```

```python
import functools
import math

import jax
import jax.numpy as jnp
from jax import lax
from jax.experimental import pallas as pl
from jax.experimental.pallas import tpu as pltpu
from jax.sharding import PartitionSpec as P

TRAVEL = 5
SHARE = 2
PARTS = 3
F32 = jnp.float32
BF16 = jnp.bfloat16
NT = (((1,), (1,)), ((), ()))
VMEM_LIMIT = 32 * 1024 * 1024


def owner_and_slot(region, slab, position, owner_rows):
    owner = lax.div(region[slab, position], owner_rows)
    slot = jnp.int32(0)
    count = jnp.int32(0)
    for other in range(region.shape[1]):
        same = jnp.where(lax.div(region[slab, other], owner_rows) == owner, 1, 0)
        count = count + same
        if other < position:
            slot = slot + same
    return owner, slot, count


def travel_place(slot, count, k):
    if k == 0:
        return jnp.where(slot == 0, 4, 2)
    if k == 1:
        return jnp.where(slot == 0, 0, 3)
    return jnp.where(jnp.logical_and(slot == 0, count == 2), 1, 4)


def send_kernel(region, density, *rest, share):
    *outs, sems = rest
    me = lax.axis_index("grid")
    part = lax.rem(lax.axis_index("atoms"), share)
    size = region.shape[1]
    owner_rows = density.shape[0]
    rows = density.shape[-2]
    copies = []
    for shift, out in enumerate(outs):
        slab = jnp.bitwise_xor(me, shift)
        base = jnp.int32(owner_rows)
        count = jnp.int32(0)
        for position in range(size):
            row = region[slab, position] - me * owner_rows
            mine = jnp.logical_and(row >= 0, row < owner_rows)
            base = jnp.minimum(base, jnp.where(mine, row, owner_rows))
            count = count + jnp.where(mine, 1, 0)
        base = jnp.where(count == 0, 0, base)
        after = jnp.minimum(base + 1, owner_rows - 1)
        lower = base == 0
        edge = jnp.where(jnp.logical_and(count == 2, jnp.logical_not(lower)), after, base)
        kept = out.shape[1]
        first = 0 if kept == rows else pl.multiple_of(part * kept, kept)
        here = pl.ds(first, kept)
        pairs = (
            (density.at[base, pl.ds(1, 2), here, :], out.at[pl.ds(0, 2)]),
            (density.at[after, pl.ds(0, 2), here, :], out.at[pl.ds(2, 2)]),
            (density.at[edge, jnp.where(lower, 0, 2), here, :], out.at[4]),
        )
        for number, (source, target) in enumerate(pairs):
            copies.append(pltpu.make_async_copy(source, target, sems.at[shift, number]))
    for copy in copies:
        copy.start()
    for copy in copies:
        copy.wait()


def in_hbm(array):
    return pltpu.with_memory_space_constraint(array, pltpu.HBM)


def rows_to_send(region, density, slabs, share):
    size = density.shape[-1]
    kept = [size] + [size // share] * (slabs - 1)
    return pl.pallas_call(
        functools.partial(send_kernel, share=share),
        out_shape=[jax.ShapeDtypeStruct((TRAVEL, rows, size), density.dtype) for rows in kept],
        in_specs=[pl.BlockSpec(memory_space=pltpu.SMEM), pl.BlockSpec(memory_space=pl.ANY)],
        out_specs=[pl.BlockSpec(memory_space=pltpu.VMEM)] * slabs,
        scratch_shapes=[pltpu.SemaphoreType.DMA((slabs, 3))],
        compiler_params=pltpu.CompilerParams(vmem_limit_bytes=VMEM_LIMIT),
    )(in_hbm(region), in_hbm(density))


def fetch_rows(region, density, slabs, share):
    own, *outgoing = rows_to_send(region, density, slabs, share)
    near = []
    for shift, piece in enumerate(outgoing, 1):
        near.append(lax.ppermute(piece, "grid", [(i, i ^ shift) for i in range(slabs)]))
    return own, near


def stage_rows(stage, own, near, far, share):
    part = lax.rem(lax.axis_index("atoms"), share)
    kept = near[0].shape[1]
    for place in range(TRAVEL):
        stage[place] = own[place]
        for shift, (here, there) in enumerate(zip(near, far), 1):
            stage[shift * TRAVEL + place, pl.ds(pl.multiple_of(part * kept, kept), kept), :] = here[place]
            stage[shift * TRAVEL + place, pl.ds(pl.multiple_of((1 - part) * kept, kept), kept), :] = there[place]


def block_major(x_ref, wide, points, blocks):
    wide[...] = x_ref[0].astype(F32)
    return [wide[pl.ds(s, points, stride=blocks), :] for s in range(blocks)]


def relayout_kernel(basis, field, basis_out, field_out, wide, *, points, blocks):
    size = basis.shape[-1]
    for source, target in ((basis, basis_out), (field, field_out)):
        for s, part in enumerate(block_major(source, wide, points, blocks)):
            target[0, :, s * size : (s + 1) * size] = part.astype(BF16)


def relayout(basis, field, points, blocks):
    batches, rows, size = basis.shape
    here = pl.BlockSpec((1, rows, size), lambda b: (b, 0, 0))
    there = pl.BlockSpec((1, points, blocks * size), lambda b: (b, 0, 0))
    shape = jax.ShapeDtypeStruct((batches, points, blocks * size), BF16)
    return pl.pallas_call(
        functools.partial(relayout_kernel, points=points, blocks=blocks),
        grid=(batches,),
        out_shape=(shape, shape),
        in_specs=[here, here],
        out_specs=(there, there),
        scratch_shapes=[pltpu.VMEM((rows, size), F32)],
        compiler_params=pltpu.CompilerParams(vmem_limit_bytes=VMEM_LIMIT),
        cost_estimate=pl.CostEstimate(flops=0, bytes_accessed=8 * batches * rows * size, transcendentals=0),
    )(basis, field)


def batch_matrix(region, pattern, tiles, slab, batch, blocks, width):
    half = (width - 1) // 2
    none = tiles.shape[0] - 1
    places = [pattern[batch, s] for s in range(blocks)]
    rows = [region[slab, place] for place in places]
    strips = []
    for s in range(blocks):
        strip = []
        for t in range(blocks):
            k = rows[t] - rows[s] + half
            inside = jnp.logical_and(k >= 0, k < width)
            strip.append(tiles[jnp.where(inside, places[s] * width + k, none)])
        strips.append(jnp.concatenate(strip, axis=1))
    return jnp.concatenate(strips, axis=0)


def split(values):
    high = values.astype(BF16)
    rest = values - high.astype(F32)
    middle = rest.astype(BF16)
    low = (rest - middle.astype(F32)).astype(BF16)
    return high, middle, low


def gradient_kernel(
    region,
    pattern,
    basis,
    field,
    basis_grad,
    weights,
    weight_grad,
    fn_atom,
    batch_atom,
    places,
    *rest,
    points,
    blocks,
    width,
    owner_rows,
    slabs,
):
    *pieces, tiles, out, stage, spread, sums, energy_sums = rest
    batch = pl.program_id(0)
    batches = pl.num_programs(0)
    me = lax.axis_index("grid")
    me_atoms = lax.axis_index("atoms")
    size = tiles.shape[-1]
    region_size = region.shape[1]

    @pl.when(batch == 0)
    def _():
        tiles[region_size * width] = jnp.zeros((size, size), BF16)
        stage_rows(stage, pieces[0], pieces[1:slabs], pieces[slabs:], SHARE)
        for position in range(region_size):
            owner, slot, count = owner_and_slot(region, me, position, owner_rows)
            shift = jnp.bitwise_xor(me, owner)
            for k in range(width):
                tiles[position * width + k] = stage[shift * TRAVEL + travel_place(slot, count, k)]

    matrix = batch_matrix(region, pattern, tiles, me, batch, blocks, width)
    potential = lax.dot_general(field[0], matrix, NT, preferred_element_type=F32)
    rows = jnp.concatenate(
        [weights[pl.ds(batch, 1), :]]
        + [weight_grad[c, pl.ds(batch, 1), :] for c in range(PARTS)]
        + [jnp.zeros((8 - 1 - PARTS, points), F32)],
        axis=0,
    )
    columns = rows.T
    weight = columns[:, 0:1]
    energy = jnp.zeros((points, size), F32)
    for s in range(blocks):
        here = potential[:, s * size : (s + 1) * size]
        energy = energy + basis[0, :, s * size : (s + 1) * size].astype(F32) * here
        spread[pl.ds(s, points, stride=blocks), :] = here * weight
    scaled = spread[...]
    place = pl.ds(pl.multiple_of(batch * 8, 8), 8)
    for c in range(PARTS):
        terms = basis_grad[c, 0].astype(F32) * scaled
        sums[c, place, :] = jnp.sum(terms.reshape(-1, 8, size), axis=0)
        terms = energy * columns[:, 1 + c : 2 + c]
        energy_sums[c, place, :] = jnp.sum(terms.reshape(-1, 8, size), axis=0)

    @pl.when(batch == batches - 1)
    def _():
        padded = max(8, region_size)
        chosen = lax.broadcasted_iota(jnp.int32, (padded, places.shape[1]), 0) == places[...]
        chosen = chosen.astype(BF16)
        blocks_sum = []
        for c in range(PARTS):
            total = jnp.zeros((padded, size), F32)
            for piece in split(sums[c]):
                total = total + jnp.dot(chosen, piece, preferred_element_type=F32)
            blocks_sum.append(-2.0 * total)
        lefts = []
        for position in range(region_size):
            stack = jnp.concatenate([total[position : position + 1] for total in blocks_sum], axis=0)
            high, middle, low = (piece.astype(F32) for piece in split(stack))
            lefts.append(jnp.concatenate([high, middle, low, jnp.zeros((16 - 3 * PARTS, size), F32)], axis=0))
        left = jnp.concatenate(lefts, axis=1).astype(BF16)
        chunk = out.shape[-1]
        scale = [jnp.sum(energy_sums[c], axis=1, keepdims=True) for c in range(PARTS)]
        for device in range(out.shape[0]):
            atoms = lax.broadcasted_iota(jnp.int32, (chunk, size), 0) + device * chunk
            hot = [
                jnp.where(atoms == fn_atom[pl.ds(region[me, position], 1), :], 1.0, 0.0).astype(BF16)
                for position in range(region_size)
            ]
            found = lax.dot_general(left, jnp.concatenate(hot, axis=1), NT, preferred_element_type=F32)
            atoms = lax.broadcasted_iota(jnp.int32, (batch_atom.shape[0], chunk), 1) + device * chunk
            mine = atoms == batch_atom[...]
            for c in range(PARTS):
                value = found[c : c + 1] + found[PARTS + c : PARTS + c + 1] + found[2 * PARTS + c : 2 * PARTS + c + 1]
                value = value + jnp.sum(jnp.where(mine, scale[c], 0.0), axis=0, keepdims=True)
                out[jnp.bitwise_xor(me_atoms, device), c : c + 1, :] = value


def partial_gradient(
    region, pattern, basis, field, basis_grad, weights, weight_grad, fn_atom, batch_atom, pieces, shapes
):
    slabs, atom_devices, atom_total, points, blocks, width, owner_rows = shapes
    batches, _, columns = basis.shape
    size = columns // blocks
    region_size = region.shape[1]
    fn_atom = fn_atom.reshape(-1, size)
    places = jnp.broadcast_to(pattern[:, None, :], (batches, 8 // blocks, blocks)).reshape(1, -1)
    batch_atom = jnp.broadcast_to(batch_atom[:, None], (batches, 8)).reshape(-1, 1)
    block = pl.BlockSpec((1, points, columns), lambda b, *_: (b, 0, 0))
    whole = pl.BlockSpec(memory_space=pltpu.VMEM)
    tile_shape = (region_size * width + 1, size, size)
    out_shape = (atom_devices, PARTS, atom_total // atom_devices)
    return pl.pallas_call(
        functools.partial(
            gradient_kernel, points=points, blocks=blocks, width=width, owner_rows=owner_rows, slabs=slabs
        ),
        grid_spec=pltpu.PrefetchScalarGridSpec(
            num_scalar_prefetch=2,
            grid=(batches,),
            in_specs=[
                block,
                block,
                pl.BlockSpec((PARTS, 1, points * blocks, size), lambda b, *_: (0, b, 0, 0)),
            ]
            + [whole] * (5 + len(pieces)),
            out_specs=(whole, whole),
            scratch_shapes=[
                pltpu.VMEM((slabs * TRAVEL, size, size), BF16),
                pltpu.VMEM((points * blocks, size), F32),
                pltpu.VMEM((PARTS, batches * 8, size), F32),
                pltpu.VMEM((PARTS, batches * 8, size), F32),
            ],
        ),
        out_shape=(jax.ShapeDtypeStruct(tile_shape, BF16), jax.ShapeDtypeStruct(out_shape, F32)),
        compiler_params=pltpu.CompilerParams(vmem_limit_bytes=VMEM_LIMIT),
    )(region, pattern, basis, field, basis_grad, weights, weight_grad, fn_atom, batch_atom, places, *pieces)


def product_kernel(region, pattern, basis, tiles, out, spread, *, points, blocks, width):
    me = lax.axis_index("grid")
    size = tiles.shape[-1]
    matrix = batch_matrix(region, pattern, tiles, me, pl.program_id(0), blocks, width)
    product = jnp.dot(basis[0], matrix, preferred_element_type=F32)
    for t in range(blocks):
        spread[pl.ds(t, points, stride=blocks), :] = product[:, t * size : (t + 1) * size]
    out[0] = spread[...].astype(BF16)


def contract(region, pattern, basis, tiles, points, blocks, width):
    batches, _, columns = basis.shape
    size = columns // blocks
    return pl.pallas_call(
        functools.partial(product_kernel, points=points, blocks=blocks, width=width),
        grid_spec=pltpu.PrefetchScalarGridSpec(
            num_scalar_prefetch=2,
            grid=(batches,),
            in_specs=[
                pl.BlockSpec((1, points, columns), lambda b, *_: (b, 0, 0)),
                pl.BlockSpec(memory_space=pltpu.VMEM),
            ],
            out_specs=pl.BlockSpec((1, points * blocks, size), lambda b, *_: (b, 0, 0)),
            scratch_shapes=[pltpu.VMEM((points * blocks, size), F32)],
        ),
        out_shape=jax.ShapeDtypeStruct((batches, points * blocks, size), BF16),
        compiler_params=pltpu.CompilerParams(vmem_limit_bytes=VMEM_LIMIT),
        cost_estimate=pl.CostEstimate(
            flops=2 * batches * points * columns * columns,
            bytes_accessed=4 * batches * points * columns,
            transcendentals=0,
        ),
    )(region, pattern, basis, tiles)


def prepare_kernel(
    region,
    pattern,
    basis,
    field,
    basis_grad,
    weights,
    weight_grad,
    fn_atom,
    batch_atom,
    basis_out,
    field_out,
    moments,
    hot,
    grad_columns,
    basis_in,
    field_in,
    grad_in,
    wide,
    turned,
    grad_wide,
    sems,
    *,
    points,
    blocks,
    step,
):
    batches, _, size = basis.shape
    groups = batches // step
    me = lax.axis_index("grid")

    def copies(group):
        here = pl.ds(group * step, step)
        return (
            pltpu.make_async_copy(field.at[here], field_in.at[here], sems.at[group, 0]),
            pltpu.make_async_copy(basis_grad.at[:, here], grad_in.at[:, here], sems.at[group, 1]),
            pltpu.make_async_copy(basis.at[here], basis_in.at[here], sems.at[group, 2]),
        )

    for group in range(groups):
        for copy in copies(group):
            copy.start()

    atoms = lax.broadcasted_iota(jnp.int32, (hot.shape[0], size), 0)
    for position in range(blocks):
        ids = fn_atom[pl.ds(region[me, position], 1), :]
        hot[:, position * size : (position + 1) * size] = jnp.where(atoms == ids, 1.0, 0.0).astype(BF16)
    ids = jnp.concatenate([batch_atom[...], jnp.full((1, size - batches), -1, jnp.int32)], axis=1)
    hot[:, blocks * size :] = jnp.where(atoms == ids, 1.0, 0.0).astype(BF16)
    for c in range(PARTS):
        rows = jnp.concatenate([weight_grad[c], jnp.zeros((size - batches, points), F32)], axis=0)
        grad_columns[c] = rows.T

    @pl.loop(0, groups)
    def _(group):
        for copy in copies(group):
            copy.wait()
        for inner in range(step):
            batch = group * step + inner
            points_here = pl.ds(pl.multiple_of(batch * points, points), points)
            places = [pattern[s, batch] for s in range(blocks)]
            weight = weights[pl.ds(batch, 1), :]
            wide[0] = field_in[batch].astype(F32)
            wide[1] = basis_in[batch].astype(F32)
            for c in range(PARTS):
                wide[2 + c] = grad_in[c, batch].astype(F32)
            for s, place in enumerate(places):
                strided = pl.ds(s, points, stride=blocks)
                values = wide[0, strided, :]
                field_out[batch, place] = values.astype(BF16)
                turned[pl.ds(pl.multiple_of(place * size, size), size), points_here] = (values.T * weight).astype(BF16)
                basis_out[batch, place] = wide[1, strided, :].astype(BF16)
                for c in range(PARTS):
                    grad_wide[c, place, points_here, :] = wide[2 + c, strided, :].astype(BF16)

    for c in range(PARTS):
        right = jnp.concatenate([grad_wide[c, place] for place in range(blocks)], axis=1)
        moments[c] = jnp.dot(turned[...], right, preferred_element_type=F32)


def prepare(region, pattern, basis, field, basis_grad, weights, weight_grad, fn_atom, batch_atom, atom_total):
    batches, points, blocks, size = basis.shape
    rows = points * blocks
    step = 2 if batches % 2 == 0 else 1
    smem = pl.BlockSpec(memory_space=pltpu.SMEM)
    hbm = pl.BlockSpec(memory_space=pl.ANY)
    vmem = pl.BlockSpec(memory_space=pltpu.VMEM)
    ordered = jax.ShapeDtypeStruct((batches, blocks, points, size), BF16)
    return pl.pallas_call(
        functools.partial(prepare_kernel, points=points, blocks=blocks, step=step),
        out_shape=(
            ordered,
            ordered,
            jax.ShapeDtypeStruct((PARTS, blocks * size, blocks * size), F32),
            jax.ShapeDtypeStruct((atom_total, (blocks + 1) * size), BF16),
            jax.ShapeDtypeStruct((PARTS, points, size), F32),
        ),
        in_specs=[smem, smem, hbm, hbm, hbm, vmem, vmem, vmem, vmem],
        out_specs=(vmem,) * 5,
        scratch_shapes=[
            pltpu.VMEM((batches, rows, size), BF16),
            pltpu.VMEM((batches, rows, size), BF16),
            pltpu.VMEM((PARTS, batches, rows, size), BF16),
            pltpu.VMEM((2 + PARTS, rows, size), F32),
            pltpu.VMEM((blocks * size, batches * points), BF16),
            pltpu.VMEM((PARTS, blocks, batches * points, size), BF16),
            pltpu.SemaphoreType.DMA((batches // step, 3)),
        ],
        compiler_params=pltpu.CompilerParams(vmem_limit_bytes=VMEM_LIMIT),
        cost_estimate=pl.CostEstimate(
            flops=2 * PARTS * batches * points * (blocks * size) ** 2,
            bytes_accessed=2 * (2 + PARTS) * batches * rows * size,
            transcendentals=0,
        ),
    )(
        in_hbm(region),
        in_hbm(pattern.T),
        in_hbm(basis.reshape(batches, rows, size)),
        in_hbm(field.reshape(batches, rows, size)),
        in_hbm(basis_grad.reshape(PARTS, batches, rows, size)),
        in_hbm(weights),
        in_hbm(weight_grad),
        in_hbm(fn_atom.reshape(-1, size)),
        in_hbm(batch_atom.reshape(1, -1)),
    )


def combine_kernel(
    region, basis, field, moments, hot, grad_columns, *rest, owner_rows, slabs, width, step
):
    *pieces, product_out, out, stage, matrix, energies = rest
    batches, blocks, points, size = basis.shape
    me = lax.axis_index("grid")
    me_atoms = lax.axis_index("atoms")
    half = (width - 1) // 2
    stage_rows(stage, pieces[0], pieces[1:slabs], pieces[slabs:], SHARE)
    rows = [region[me, position] for position in range(blocks)]
    found = [owner_and_slot(region, me, position, owner_rows) for position in range(blocks)]
    totals = [[jnp.zeros((8, size), F32) for _ in range(blocks)] for _ in range(PARTS)]
    for p in range(blocks):
        owner, slot, count = found[p]
        first = jnp.bitwise_xor(me, owner) * TRAVEL
        for q in range(blocks):
            if abs(q - p) > half:
                matrix[p * size : (p + 1) * size, q * size : (q + 1) * size] = jnp.zeros((size, size), BF16)
                continue
            k = rows[q] - rows[p] + half
            place = jnp.where(
                k == 0,
                travel_place(slot, count, 0),
                jnp.where(k == 1, travel_place(slot, count, 1), travel_place(slot, count, 2)),
            )
            inside = jnp.logical_and(k >= 0, k < width)
            tile = stage[first + place].astype(F32)
            tile = jnp.where(inside, tile, 0.0)
            matrix[p * size : (p + 1) * size, q * size : (q + 1) * size] = tile.astype(BF16)
            turned = tile.T
            for c in range(PARTS):
                terms = turned * moments[c, q * size : (q + 1) * size, p * size : (p + 1) * size]
                totals[c][p] = totals[c][p] + jnp.sum(terms.reshape(-1, 8, size), axis=0)
    derivative = [
        jnp.concatenate([jnp.sum(total, axis=0, keepdims=True) for total in totals[c]], axis=1) for c in range(PARTS)
    ]

    energies[...] = jnp.zeros_like(energies)
    lanes = lax.broadcasted_iota(jnp.int32, (points, size), 1)

    @pl.loop(0, batches // step)
    def _(group):
        left = [
            jnp.concatenate([basis[group * step + inner, p] for p in range(blocks)], axis=1) for inner in range(step)
        ]
        product = jnp.dot(jnp.concatenate(left, axis=0), matrix[...], preferred_element_type=F32)
        for inner in range(step):
            batch = group * step + inner
            energy = jnp.zeros((points, size), F32)
            for q in range(blocks):
                part = product[inner * points : (inner + 1) * points, q * size : (q + 1) * size]
                product_out[batch, q] = part.astype(BF16)
                energy = energy + part * field[batch, q].astype(F32)
            energy = jnp.sum(energy, axis=1, keepdims=True)
            energies[...] = jnp.where(lanes == batch, energy, energies[...])

    lefts = []
    for c in range(PARTS):
        term = jnp.sum(energies[...] * grad_columns[c], axis=0, keepdims=True)
        lefts.append(jnp.concatenate([-2.0 * derivative[c], term], axis=1))
    left = jnp.concatenate(lefts, axis=0)
    high, middle, low = (piece.astype(F32) for piece in split(left))
    left = jnp.concatenate([high, middle, low, jnp.zeros((16 - 3 * PARTS, left.shape[1]), F32)], axis=0).astype(BF16)
    chunk = out.shape[-1]
    for device in range(out.shape[0]):
        sums = lax.dot_general(
            left, hot[device * chunk : (device + 1) * chunk, :], NT, preferred_element_type=F32
        )
        value = sums[:PARTS] + sums[PARTS : 2 * PARTS] + sums[2 * PARTS : 3 * PARTS]
        out[jnp.bitwise_xor(me_atoms, device)] = value


def combine(region, prepared, pieces, shapes):
    basis, field, moments, hot, grad_columns = prepared
    slabs, atom_devices, atom_total, points, blocks, width, owner_rows = shapes
    batches, _, _, size = basis.shape
    step = 4 if batches % 4 == 0 else 1
    vmem = pl.BlockSpec(memory_space=pltpu.VMEM)
    return pl.pallas_call(
        functools.partial(combine_kernel, owner_rows=owner_rows, slabs=slabs, width=width, step=step),
        out_shape=(
            jax.ShapeDtypeStruct(basis.shape, BF16),
            jax.ShapeDtypeStruct((atom_devices, PARTS, atom_total // atom_devices), F32),
        ),
        in_specs=[pl.BlockSpec(memory_space=pltpu.SMEM)] + [vmem] * (5 + len(pieces)),
        out_specs=(vmem, vmem),
        scratch_shapes=[
            pltpu.VMEM((slabs * TRAVEL, size, size), BF16),
            pltpu.VMEM((blocks * size, blocks * size), BF16),
            pltpu.VMEM((points, size), F32),
        ],
        compiler_params=pltpu.CompilerParams(vmem_limit_bytes=VMEM_LIMIT),
    )(in_hbm(region), basis, field, moments, hot, grad_columns, *pieces)


def write_kernel(pattern, product, out, wide, staged, sems):
    batches, blocks, points, size = product.shape

    def copy(batch):
        return pltpu.make_async_copy(staged.at[batch], out.at[batch], sems.at[batch])

    @pl.loop(0, batches // 2)
    def _(pair):
        for inner in range(2):
            batch = pair * 2 + inner
            for t in range(blocks):
                wide[inner, pl.ds(t, points, stride=blocks), :] = product[batch, pattern[t, batch]].astype(F32)
            staged[batch] = wide[inner].astype(BF16)
            copy(batch).start()

    @pl.loop(0, batches)
    def _(batch):
        copy(batch).wait()


def write(pattern, product):
    batches, blocks, points, size = product.shape
    shape = (batches, points * blocks, size)
    return pl.pallas_call(
        write_kernel,
        out_shape=jax.ShapeDtypeStruct(shape, BF16),
        in_specs=[pl.BlockSpec(memory_space=pltpu.SMEM), pl.BlockSpec(memory_space=pltpu.VMEM)],
        out_specs=pl.BlockSpec(memory_space=pl.ANY),
        scratch_shapes=[
            pltpu.VMEM((2, points * blocks, size), F32),
            pltpu.VMEM(shape, BF16),
            pltpu.SemaphoreType.DMA((batches,)),
        ],
        compiler_params=pltpu.CompilerParams(vmem_limit_bytes=VMEM_LIMIT),
        cost_estimate=pl.CostEstimate(flops=0, bytes_accessed=4 * math.prod(shape), transcendentals=0),
    )(in_hbm(pattern.T), product)


def swap_halves(near, ready, atom_devices):
    near, ready = lax.optimization_barrier((near, ready))
    swap = [(i, i ^ 1) for i in range(atom_devices)]
    return near, [lax.ppermute(piece, "atoms", swap) for piece in near], ready


def exchange(values, axis, bit):
    return lax.ppermute(values, axis, [(i, i ^ bit) for i in range(lax.axis_size(axis))])


def sum_parts(partial_grad, slabs):
    parts = partial_grad
    while parts.shape[0] > 1:
        half = parts.shape[0] // 2
        parts = parts[:half] + exchange(parts[half:], "atoms", half)
    total = parts[0]
    bit = 1
    while bit < slabs:
        total = total + exchange(total, "grid", bit)
        bit *= 2
    return total


def local(
    basis,
    basis_grad,
    exchange_field,
    weights,
    weight_grad,
    density,
    region,
    pattern,
    fn_atom,
    batch_atom,
):
    batches, points, blocks, size = basis.shape
    owner_rows, width = density.shape[:2]
    slabs = lax.axis_size("grid")
    atom_devices = lax.axis_size("atoms")
    atom_total = fn_atom.shape[0] // (10 * slabs * atom_devices) * slabs * atom_devices
    shapes = (slabs, atom_devices, atom_total, points, blocks, width, owner_rows)
    own, near = fetch_rows(region, density, slabs, SHARE)
    if region.shape[1] == blocks:
        ready = prepare(
            region, pattern, basis, exchange_field, basis_grad, weights, weight_grad, fn_atom, batch_atom, atom_total
        )
        near, far, ready = swap_halves(near, ready, atom_devices)
        product, partial_grad = combine(region, ready, [own, *near, *far], shapes)
        gradient = sum_parts(partial_grad, slabs)
        contracted = write(pattern, product)
        return contracted.reshape(basis.shape), gradient
    ready = relayout(
        in_hbm(basis.reshape(batches, points * blocks, size)),
        in_hbm(exchange_field.reshape(batches, points * blocks, size)),
        points,
        blocks,
    )
    near, far, (basis_wide, field_wide) = swap_halves(near, ready, atom_devices)
    tiles, partial_grad = partial_gradient(
        region,
        pattern,
        basis_wide,
        field_wide,
        in_hbm(basis_grad.reshape(PARTS, batches, points * blocks, size)),
        weights,
        weight_grad,
        fn_atom,
        batch_atom,
        [own, *near, *far],
        shapes,
    )
    gradient = sum_parts(partial_grad, slabs)
    contracted = contract(region, pattern, basis_wide, tiles, points, blocks, width)
    return contracted.reshape(basis.shape), gradient


def solution(mesh):
    placed = (
        P(("groups", "grid", "atoms"), None, None, None),
        P(None, ("groups", "grid", "atoms"), None, None, None),
        P(("groups", "grid", "atoms"), None, None, None),
        P(("groups", "grid", "atoms"), None),
        P(None, ("groups", "grid", "atoms"), None),
        P(("groups", "grid"), None, None, None),
        P("groups", None),
        P(("groups", "grid", "atoms"), None),
        P("groups"),
        P(("groups", "grid", "atoms")),
    )
    return jax.shard_map(
        local,
        mesh=mesh,
        in_specs=placed,
        out_specs=(P(("groups", "grid", "atoms"), None, None, None), P(None, ("groups", "atoms"))),
        check_vma=False,
    )
```

```python
import functools
import math

import jax
import jax.numpy as jnp
from jax import lax
from jax.experimental import pallas as pl
from jax.experimental.pallas import tpu as pltpu
from jax.sharding import PartitionSpec as P

TRAVEL = 5
SHARE = 2
PARTS = 3
F32 = jnp.float32
BF16 = jnp.bfloat16
NT = (((1,), (1,)), ((), ()))
VMEM_LIMIT = 32 * 1024 * 1024


def owner_and_slot(region, slab, position, owner_rows):
    owner = lax.div(region[slab, position], owner_rows)
    slot = jnp.int32(0)
    count = jnp.int32(0)
    for other in range(region.shape[1]):
        same = jnp.where(lax.div(region[slab, other], owner_rows) == owner, 1, 0)
        count = count + same
        if other < position:
            slot = slot + same
    return owner, slot, count


def travel_place(slot, count, k):
    if k == 0:
        return jnp.where(slot == 0, 4, 2)
    if k == 1:
        return jnp.where(slot == 0, 0, 3)
    return jnp.where(jnp.logical_and(slot == 0, count == 2), 1, 4)


def send_kernel(region, density, *rest, share):
    *outs, sems = rest
    me = lax.axis_index("grid")
    part = lax.rem(lax.axis_index("atoms"), share)
    size = region.shape[1]
    owner_rows = density.shape[0]
    rows = density.shape[-2]
    copies = []
    for shift, out in enumerate(outs):
        slab = jnp.bitwise_xor(me, shift)
        base = jnp.int32(owner_rows)
        count = jnp.int32(0)
        for position in range(size):
            row = region[slab, position] - me * owner_rows
            mine = jnp.logical_and(row >= 0, row < owner_rows)
            base = jnp.minimum(base, jnp.where(mine, row, owner_rows))
            count = count + jnp.where(mine, 1, 0)
        base = jnp.where(count == 0, 0, base)
        after = jnp.minimum(base + 1, owner_rows - 1)
        lower = base == 0
        edge = jnp.where(jnp.logical_and(count == 2, jnp.logical_not(lower)), after, base)
        kept = out.shape[1]
        first = 0 if kept == rows else pl.multiple_of(part * kept, kept)
        here = pl.ds(first, kept)
        pairs = (
            (density.at[base, pl.ds(1, 2), here, :], out.at[pl.ds(0, 2)]),
            (density.at[after, pl.ds(0, 2), here, :], out.at[pl.ds(2, 2)]),
            (density.at[edge, jnp.where(lower, 0, 2), here, :], out.at[4]),
        )
        for number, (source, target) in enumerate(pairs):
            copies.append(pltpu.make_async_copy(source, target, sems.at[shift, number]))
    for copy in copies:
        copy.start()
    for copy in copies:
        copy.wait()


def in_hbm(array):
    return pltpu.with_memory_space_constraint(array, pltpu.HBM)


def rows_to_send(region, density, slabs, share):
    size = density.shape[-1]
    kept = [size] + [size // share] * (slabs - 1)
    return pl.pallas_call(
        functools.partial(send_kernel, share=share),
        out_shape=[jax.ShapeDtypeStruct((TRAVEL, rows, size), density.dtype) for rows in kept],
        in_specs=[pl.BlockSpec(memory_space=pltpu.SMEM), pl.BlockSpec(memory_space=pl.ANY)],
        out_specs=[pl.BlockSpec(memory_space=pltpu.VMEM)] * slabs,
        scratch_shapes=[pltpu.SemaphoreType.DMA((slabs, 3))],
        compiler_params=pltpu.CompilerParams(vmem_limit_bytes=VMEM_LIMIT),
    )(in_hbm(region), in_hbm(density))


def fetch_rows(region, density, slabs, share):
    own, *outgoing = rows_to_send(region, density, slabs, share)
    near = []
    for shift, piece in enumerate(outgoing, 1):
        near.append(lax.ppermute(piece, "grid", [(i, i ^ shift) for i in range(slabs)]))
    return own, near


def stage_rows(stage, own, near, far, share):
    part = lax.rem(lax.axis_index("atoms"), share)
    kept = near[0].shape[1]
    for place in range(TRAVEL):
        stage[place] = own[place]
        for shift, (here, there) in enumerate(zip(near, far), 1):
            stage[shift * TRAVEL + place, pl.ds(pl.multiple_of(part * kept, kept), kept), :] = here[place]
            stage[shift * TRAVEL + place, pl.ds(pl.multiple_of((1 - part) * kept, kept), kept), :] = there[place]


def block_major(x_ref, wide, points, blocks):
    wide[...] = x_ref[0].astype(F32)
    return [wide[pl.ds(s, points, stride=blocks), :] for s in range(blocks)]


def relayout_kernel(basis, field, basis_out, field_out, wide, *, points, blocks):
    size = basis.shape[-1]
    for source, target in ((basis, basis_out), (field, field_out)):
        for s, part in enumerate(block_major(source, wide, points, blocks)):
            target[0, :, s * size : (s + 1) * size] = part.astype(BF16)


def relayout(basis, field, points, blocks):
    batches, rows, size = basis.shape
    here = pl.BlockSpec((1, rows, size), lambda b: (b, 0, 0))
    there = pl.BlockSpec((1, points, blocks * size), lambda b: (b, 0, 0))
    shape = jax.ShapeDtypeStruct((batches, points, blocks * size), BF16)
    return pl.pallas_call(
        functools.partial(relayout_kernel, points=points, blocks=blocks),
        grid=(batches,),
        out_shape=(shape, shape),
        in_specs=[here, here],
        out_specs=(there, there),
        scratch_shapes=[pltpu.VMEM((rows, size), F32)],
        compiler_params=pltpu.CompilerParams(vmem_limit_bytes=VMEM_LIMIT),
        cost_estimate=pl.CostEstimate(flops=0, bytes_accessed=8 * batches * rows * size, transcendentals=0),
    )(basis, field)


def batch_matrix(region, pattern, tiles, slab, batch, blocks, width):
    half = (width - 1) // 2
    none = tiles.shape[0] - 1
    places = [pattern[batch, s] for s in range(blocks)]
    rows = [region[slab, place] for place in places]
    strips = []
    for s in range(blocks):
        strip = []
        for t in range(blocks):
            k = rows[t] - rows[s] + half
            inside = jnp.logical_and(k >= 0, k < width)
            strip.append(tiles[jnp.where(inside, places[s] * width + k, none)])
        strips.append(jnp.concatenate(strip, axis=1))
    return jnp.concatenate(strips, axis=0)


def split(values):
    high = values.astype(BF16)
    rest = values - high.astype(F32)
    middle = rest.astype(BF16)
    low = (rest - middle.astype(F32)).astype(BF16)
    return high, middle, low


def gradient_kernel(
    region,
    pattern,
    basis,
    field,
    basis_grad,
    weights,
    weight_grad,
    fn_atom,
    batch_atom,
    places,
    *rest,
    points,
    blocks,
    width,
    owner_rows,
    slabs,
):
    *pieces, tiles, out, stage, spread, sums, energy_sums = rest
    batch = pl.program_id(0)
    batches = pl.num_programs(0)
    me = lax.axis_index("grid")
    size = tiles.shape[-1]
    region_size = region.shape[1]

    @pl.when(batch == 0)
    def _():
        tiles[region_size * width] = jnp.zeros((size, size), BF16)
        stage_rows(stage, pieces[0], pieces[1:slabs], pieces[slabs:], SHARE)
        for position in range(region_size):
            owner, slot, count = owner_and_slot(region, me, position, owner_rows)
            shift = jnp.bitwise_xor(me, owner)
            for k in range(width):
                tiles[position * width + k] = stage[shift * TRAVEL + travel_place(slot, count, k)]

    matrix = batch_matrix(region, pattern, tiles, me, batch, blocks, width)
    potential = lax.dot_general(field[0], matrix, NT, preferred_element_type=F32)
    rows = jnp.concatenate(
        [weights[pl.ds(batch, 1), :]]
        + [weight_grad[c, pl.ds(batch, 1), :] for c in range(PARTS)]
        + [jnp.zeros((8 - 1 - PARTS, points), F32)],
        axis=0,
    )
    columns = rows.T
    weight = columns[:, 0:1]
    energy = jnp.zeros((points, size), F32)
    for s in range(blocks):
        here = potential[:, s * size : (s + 1) * size]
        energy = energy + basis[0, :, s * size : (s + 1) * size].astype(F32) * here
        spread[pl.ds(s, points, stride=blocks), :] = here * weight
    scaled = spread[...]
    place = pl.ds(pl.multiple_of(batch * 8, 8), 8)
    for c in range(PARTS):
        terms = basis_grad[c, 0].astype(F32) * scaled
        sums[c, place, :] = jnp.sum(terms.reshape(-1, 8, size), axis=0)
        terms = energy * columns[:, 1 + c : 2 + c]
        energy_sums[c, place, :] = jnp.sum(terms.reshape(-1, 8, size), axis=0)

    @pl.when(batch == batches - 1)
    def _():
        padded = max(8, region_size)
        chosen = lax.broadcasted_iota(jnp.int32, (padded, places.shape[1]), 0) == places[...]
        chosen = chosen.astype(BF16)
        blocks_sum = []
        for c in range(PARTS):
            total = jnp.zeros((padded, size), F32)
            for piece in split(sums[c]):
                total = total + jnp.dot(chosen, piece, preferred_element_type=F32)
            blocks_sum.append(-2.0 * total)
        lefts = []
        for position in range(region_size):
            stack = jnp.concatenate([total[position : position + 1] for total in blocks_sum], axis=0)
            high, middle, low = (piece.astype(F32) for piece in split(stack))
            lefts.append(jnp.concatenate([high, middle, low, jnp.zeros((16 - 3 * PARTS, size), F32)], axis=0))
        left = jnp.concatenate(lefts, axis=1).astype(BF16)
        chunk = out.shape[-1]
        scale = [jnp.sum(energy_sums[c], axis=1, keepdims=True) for c in range(PARTS)]
        for device in range(out.shape[1]):
            atoms = lax.broadcasted_iota(jnp.int32, (chunk, size), 0) + device * chunk
            hot = [
                jnp.where(atoms == fn_atom[pl.ds(region[me, position], 1), :], 1.0, 0.0).astype(BF16)
                for position in range(region_size)
            ]
            found = lax.dot_general(left, jnp.concatenate(hot, axis=1), NT, preferred_element_type=F32)
            atoms = lax.broadcasted_iota(jnp.int32, (batch_atom.shape[0], chunk), 1) + device * chunk
            mine = atoms == batch_atom[...]
            for c in range(PARTS):
                value = found[c : c + 1] + found[PARTS + c : PARTS + c + 1] + found[2 * PARTS + c : 2 * PARTS + c + 1]
                value = value + jnp.sum(jnp.where(mine, scale[c], 0.0), axis=0, keepdims=True)
                for slab in range(slabs):
                    out[slab, device, c : c + 1, :] = value


def partial_gradient(
    region, pattern, basis, field, basis_grad, weights, weight_grad, fn_atom, batch_atom, pieces, shapes
):
    slabs, atom_devices, atom_total, points, blocks, width, owner_rows = shapes
    batches, _, columns = basis.shape
    size = columns // blocks
    region_size = region.shape[1]
    fn_atom = fn_atom.reshape(-1, size)
    places = jnp.broadcast_to(pattern[:, None, :], (batches, 8 // blocks, blocks)).reshape(1, -1)
    batch_atom = jnp.broadcast_to(batch_atom[:, None], (batches, 8)).reshape(-1, 1)
    block = pl.BlockSpec((1, points, columns), lambda b, *_: (b, 0, 0))
    whole = pl.BlockSpec(memory_space=pltpu.VMEM)
    tile_shape = (region_size * width + 1, size, size)
    out_shape = (slabs, atom_devices, PARTS, atom_total // atom_devices)
    return pl.pallas_call(
        functools.partial(
            gradient_kernel, points=points, blocks=blocks, width=width, owner_rows=owner_rows, slabs=slabs
        ),
        grid_spec=pltpu.PrefetchScalarGridSpec(
            num_scalar_prefetch=2,
            grid=(batches,),
            in_specs=[
                block,
                block,
                pl.BlockSpec((PARTS, 1, points * blocks, size), lambda b, *_: (0, b, 0, 0)),
            ]
            + [whole] * (5 + len(pieces)),
            out_specs=(whole, whole),
            scratch_shapes=[
                pltpu.VMEM((slabs * TRAVEL, size, size), BF16),
                pltpu.VMEM((points * blocks, size), F32),
                pltpu.VMEM((PARTS, batches * 8, size), F32),
                pltpu.VMEM((PARTS, batches * 8, size), F32),
            ],
        ),
        out_shape=(jax.ShapeDtypeStruct(tile_shape, BF16), jax.ShapeDtypeStruct(out_shape, F32)),
        compiler_params=pltpu.CompilerParams(vmem_limit_bytes=VMEM_LIMIT),
    )(region, pattern, basis, field, basis_grad, weights, weight_grad, fn_atom, batch_atom, places, *pieces)


def product_kernel(region, pattern, basis, tiles, out, spread, *, points, blocks, width):
    me = lax.axis_index("grid")
    size = tiles.shape[-1]
    matrix = batch_matrix(region, pattern, tiles, me, pl.program_id(0), blocks, width)
    product = jnp.dot(basis[0], matrix, preferred_element_type=F32)
    for t in range(blocks):
        spread[pl.ds(t, points, stride=blocks), :] = product[:, t * size : (t + 1) * size]
    out[0] = spread[...].astype(BF16)


def contract(region, pattern, basis, tiles, points, blocks, width):
    batches, _, columns = basis.shape
    size = columns // blocks
    return pl.pallas_call(
        functools.partial(product_kernel, points=points, blocks=blocks, width=width),
        grid_spec=pltpu.PrefetchScalarGridSpec(
            num_scalar_prefetch=2,
            grid=(batches,),
            in_specs=[
                pl.BlockSpec((1, points, columns), lambda b, *_: (b, 0, 0)),
                pl.BlockSpec(memory_space=pltpu.VMEM),
            ],
            out_specs=pl.BlockSpec((1, points * blocks, size), lambda b, *_: (b, 0, 0)),
            scratch_shapes=[pltpu.VMEM((points * blocks, size), F32)],
        ),
        out_shape=jax.ShapeDtypeStruct((batches, points * blocks, size), BF16),
        compiler_params=pltpu.CompilerParams(vmem_limit_bytes=VMEM_LIMIT),
        cost_estimate=pl.CostEstimate(
            flops=2 * batches * points * columns * columns,
            bytes_accessed=4 * batches * points * columns,
            transcendentals=0,
        ),
    )(region, pattern, basis, tiles)


def reorder_kernel(
    pattern, basis, field, basis_grad, weights, basis_out, field_out, turned, grad_wide, basis_in, field_in, grad_in, wide, sems
):
    batches, blocks, points, size = basis_out.shape
    groups = sems.shape[0]
    step = batches // groups

    def copies(group):
        here = pl.ds(group * step, step)
        return (
            pltpu.make_async_copy(field.at[here], field_in.at[here], sems.at[group, 0]),
            pltpu.make_async_copy(basis_grad.at[:, here], grad_in.at[:, here], sems.at[group, 1]),
            pltpu.make_async_copy(basis.at[here], basis_in.at[here], sems.at[group, 2]),
        )

    for group in range(groups):
        for copy in copies(group):
            copy.start()

    @pl.loop(0, groups)
    def _(group):
        for copy in copies(group):
            copy.wait()
        for inner in range(step):
            batch = group * step + inner
            points_here = pl.ds(pl.multiple_of(batch * points, points), points)
            places = [pattern[s, batch] for s in range(blocks)]
            weight = weights[pl.ds(batch, 1), :]
            wide[0] = field_in[batch].astype(F32)
            wide[1] = basis_in[batch].astype(F32)
            for c in range(PARTS):
                wide[2 + c] = grad_in[c, batch].astype(F32)
            for s, place in enumerate(places):
                strided = pl.ds(s, points, stride=blocks)
                values = wide[0, strided, :]
                field_out[batch, place] = values.astype(BF16)
                turned[pl.ds(pl.multiple_of(place * size, size), size), points_here] = (values.T * weight).astype(BF16)
                basis_out[batch, place] = wide[1, strided, :].astype(BF16)
                for c in range(PARTS):
                    grad_wide[c, place, points_here, :] = wide[2 + c, strided, :].astype(BF16)


def reorder(pattern, basis, field, basis_grad, weights):
    batches, points, blocks, size = basis.shape
    rows = points * blocks
    step = 2 if batches % 2 == 0 else 1
    hbm = pl.BlockSpec(memory_space=pl.ANY)
    vmem = pl.BlockSpec(memory_space=pltpu.VMEM)
    ordered = jax.ShapeDtypeStruct((batches, blocks, points, size), BF16)
    return pl.pallas_call(
        reorder_kernel,
        out_shape=(
            ordered,
            ordered,
            jax.ShapeDtypeStruct((blocks * size, batches * points), BF16),
            jax.ShapeDtypeStruct((PARTS, blocks, batches * points, size), BF16),
        ),
        in_specs=[pl.BlockSpec(memory_space=pltpu.SMEM), hbm, hbm, hbm, vmem],
        out_specs=(vmem,) * 4,
        scratch_shapes=[
            pltpu.VMEM((batches, rows, size), BF16),
            pltpu.VMEM((batches, rows, size), BF16),
            pltpu.VMEM((PARTS, batches, rows, size), BF16),
            pltpu.VMEM((2 + PARTS, rows, size), F32),
            pltpu.SemaphoreType.DMA((batches // step, 3)),
        ],
        compiler_params=pltpu.CompilerParams(vmem_limit_bytes=VMEM_LIMIT),
        cost_estimate=pl.CostEstimate(
            flops=0, bytes_accessed=2 * (2 + PARTS) * batches * rows * size, transcendentals=0
        ),
    )(
        in_hbm(pattern.T),
        in_hbm(basis.reshape(batches, rows, size)),
        in_hbm(field.reshape(batches, rows, size)),
        in_hbm(basis_grad.reshape(PARTS, batches, rows, size)),
        in_hbm(weights),
    )


def moment_kernel(region, turned, grad_wide, weight_grad, fn_atom, batch_atom, moments, hot, grad_columns):
    blocks, _, size = grad_wide.shape[1:]
    batches = weight_grad.shape[1]
    me = lax.axis_index("grid")
    for c in range(PARTS):
        spans = [(p, min(p + 2, blocks), p, min(p + 2, blocks)) for p in range(0, blocks, 2)]
        for p in range(2, blocks, 2):
            spans += [(p - 1, p, p, p + 1), (p, p + 1, p - 1, p)]
        for top, bottom, first, last in spans:
            right = jnp.concatenate([grad_wide[c, place] for place in range(first, last)], axis=1)
            moments[c, top * size : bottom * size, first * size : last * size] = jnp.dot(
                turned[top * size : bottom * size, :], right, preferred_element_type=F32
            )
    atoms = lax.broadcasted_iota(jnp.int32, (size, hot.shape[1]), 1).astype(F32)
    rows = [fn_atom[pl.ds(region[me, position], 1), :] for position in range(blocks)]
    rows.append(jnp.concatenate([batch_atom[...], jnp.full((1, size - batches), -1, jnp.int32)], axis=1))
    for number, row in enumerate(rows):
        ids = jnp.broadcast_to(row.astype(F32), (size, size)).T[:, 0:1]
        hot[number * size : (number + 1) * size, :] = jnp.where(atoms == ids, 1.0, 0.0).astype(BF16)
    for c in range(PARTS):
        padded = jnp.concatenate([weight_grad[c], jnp.zeros((size - batches, weight_grad.shape[2]), F32)], axis=0)
        grad_columns[c] = padded.T


def moments_and_atoms(region, turned, grad_wide, weight_grad, fn_atom, batch_atom, atom_total):
    blocks, depth, size = grad_wide.shape[1:]
    points = weight_grad.shape[2]
    vmem = pl.BlockSpec(memory_space=pltpu.VMEM)
    return pl.pallas_call(
        moment_kernel,
        out_shape=(
            jax.ShapeDtypeStruct((PARTS, blocks * size, blocks * size), F32),
            jax.ShapeDtypeStruct(((blocks + 1) * size, atom_total), BF16),
            jax.ShapeDtypeStruct((PARTS, points, size), F32),
        ),
        in_specs=[pl.BlockSpec(memory_space=pltpu.SMEM)] + [vmem] * 5,
        out_specs=(vmem,) * 3,
        compiler_params=pltpu.CompilerParams(vmem_limit_bytes=VMEM_LIMIT),
        cost_estimate=pl.CostEstimate(
            flops=2 * PARTS * depth * (blocks * size) ** 2, bytes_accessed=0, transcendentals=0
        ),
    )(
        in_hbm(region),
        turned,
        grad_wide,
        in_hbm(weight_grad),
        in_hbm(fn_atom.reshape(-1, size)),
        in_hbm(batch_atom.reshape(1, -1)),
    )


def combine_kernel(
    region, basis, field, moments, hot, grad_columns, *rest, owner_rows, slabs, width, step
):
    *pieces, product_out, out, stage, matrix, energies = rest
    batches, blocks, points, size = basis.shape
    me = lax.axis_index("grid")
    half = (width - 1) // 2
    stage_rows(stage, pieces[0], pieces[1:slabs], pieces[slabs:], SHARE)
    rows = [region[me, position] for position in range(blocks)]
    found = [owner_and_slot(region, me, position, owner_rows) for position in range(blocks)]
    totals = [[jnp.zeros((8, size), F32) for _ in range(blocks)] for _ in range(PARTS)]
    for p in range(blocks):
        owner, slot, count = found[p]
        first = jnp.bitwise_xor(me, owner) * TRAVEL
        for q in range(blocks):
            if abs(q - p) > half:
                matrix[p * size : (p + 1) * size, q * size : (q + 1) * size] = jnp.zeros((size, size), BF16)
                continue
            k = rows[q] - rows[p] + half
            place = jnp.where(
                k == 0,
                travel_place(slot, count, 0),
                jnp.where(k == 1, travel_place(slot, count, 1), travel_place(slot, count, 2)),
            )
            inside = jnp.logical_and(k >= 0, k < width)
            tile = stage[first + place].astype(F32)
            tile = jnp.where(inside, tile, 0.0)
            matrix[p * size : (p + 1) * size, q * size : (q + 1) * size] = tile.astype(BF16)
            turned = tile.T
            for c in range(PARTS):
                terms = turned * moments[c, q * size : (q + 1) * size, p * size : (p + 1) * size]
                totals[c][p] = totals[c][p] + jnp.sum(terms.reshape(-1, 8, size), axis=0)
    derivative = [
        jnp.concatenate([jnp.sum(total, axis=0, keepdims=True) for total in totals[c]], axis=1) for c in range(PARTS)
    ]

    energies[...] = jnp.zeros_like(energies)
    lanes = lax.broadcasted_iota(jnp.int32, (points, size), 1)

    @pl.loop(0, batches // step)
    def _(group):
        left = [
            jnp.concatenate([basis[group * step + inner, p] for p in range(blocks)], axis=1) for inner in range(step)
        ]
        product = jnp.dot(jnp.concatenate(left, axis=0), matrix[...], preferred_element_type=F32)
        for inner in range(step):
            batch = group * step + inner
            energy = jnp.zeros((points, size), F32)
            for q in range(blocks):
                part = product[inner * points : (inner + 1) * points, q * size : (q + 1) * size]
                product_out[batch, q] = part.astype(BF16)
                energy = energy + part * field[batch, q].astype(F32)
            energy = jnp.sum(energy, axis=1, keepdims=True)
            energies[...] = jnp.where(lanes == batch, energy, energies[...])

    lefts = []
    for c in range(PARTS):
        term = jnp.sum(energies[...] * grad_columns[c], axis=0, keepdims=True)
        lefts.append(jnp.concatenate([-2.0 * derivative[c], term], axis=1))
    left = jnp.concatenate(lefts, axis=0)
    high, middle, low = (piece.astype(F32) for piece in split(left))
    left = jnp.concatenate([high, middle, low, jnp.zeros((16 - 3 * PARTS, left.shape[1]), F32)], axis=0).astype(BF16)
    sums = jnp.dot(left, hot[...], preferred_element_type=F32)
    value = sums[:PARTS] + sums[PARTS : 2 * PARTS] + sums[2 * PARTS : 3 * PARTS]
    chunk = out.shape[-1]
    for device in range(out.shape[1]):
        for slab in range(slabs):
            out[slab, device] = value[:, device * chunk : (device + 1) * chunk]


def combine(region, prepared, pieces, shapes):
    basis, field, moments, hot, grad_columns = prepared
    slabs, atom_devices, atom_total, points, blocks, width, owner_rows = shapes
    batches, _, _, size = basis.shape
    step = 4 if batches % 4 == 0 else 1
    vmem = pl.BlockSpec(memory_space=pltpu.VMEM)
    return pl.pallas_call(
        functools.partial(combine_kernel, owner_rows=owner_rows, slabs=slabs, width=width, step=step),
        out_shape=(
            jax.ShapeDtypeStruct(basis.shape, BF16),
            jax.ShapeDtypeStruct((slabs, atom_devices, PARTS, atom_total // atom_devices), F32),
        ),
        in_specs=[pl.BlockSpec(memory_space=pltpu.SMEM)] + [vmem] * (5 + len(pieces)),
        out_specs=(vmem, vmem),
        scratch_shapes=[
            pltpu.VMEM((slabs * TRAVEL, size, size), BF16),
            pltpu.VMEM((blocks * size, blocks * size), BF16),
            pltpu.VMEM((points, size), F32),
        ],
        compiler_params=pltpu.CompilerParams(vmem_limit_bytes=VMEM_LIMIT),
    )(in_hbm(region), basis, field, moments, hot, grad_columns, *pieces)


def write_kernel(pattern, product, out, wide, staged, sems):
    batches, blocks, points, size = product.shape

    def copy(batch):
        return pltpu.make_async_copy(staged.at[batch], out.at[batch], sems.at[batch])

    @pl.loop(0, batches // 2)
    def _(pair):
        for inner in range(2):
            batch = pair * 2 + inner
            for t in range(blocks):
                wide[inner, pl.ds(t, points, stride=blocks), :] = product[batch, pattern[t, batch]].astype(F32)
            staged[batch] = wide[inner].astype(BF16)
            copy(batch).start()

    @pl.loop(0, batches)
    def _(batch):
        copy(batch).wait()


def write(pattern, product):
    batches, blocks, points, size = product.shape
    shape = (batches, points * blocks, size)
    return pl.pallas_call(
        write_kernel,
        out_shape=jax.ShapeDtypeStruct(shape, BF16),
        in_specs=[pl.BlockSpec(memory_space=pltpu.SMEM), pl.BlockSpec(memory_space=pltpu.VMEM)],
        out_specs=pl.BlockSpec(memory_space=pl.ANY),
        scratch_shapes=[
            pltpu.VMEM((2, points * blocks, size), F32),
            pltpu.VMEM(shape, BF16),
            pltpu.SemaphoreType.DMA((batches,)),
        ],
        compiler_params=pltpu.CompilerParams(vmem_limit_bytes=VMEM_LIMIT),
        cost_estimate=pl.CostEstimate(flops=0, bytes_accessed=4 * math.prod(shape), transcendentals=0),
    )(in_hbm(pattern.T), product)


def swap_halves(near, ready, atom_devices):
    near, ready = lax.optimization_barrier((near, ready))
    swap = [(i, i ^ 1) for i in range(atom_devices)]
    return near, [lax.ppermute(piece, "atoms", swap) for piece in near], ready


def sum_parts(partial_grad):
    parts = partial_grad.reshape((-1,) + partial_grad.shape[2:])
    parts = lax.all_to_all(parts, ("grid", "atoms"), split_axis=0, concat_axis=0, tiled=True)
    return jnp.sum(parts, axis=0)


def local(
    basis,
    basis_grad,
    exchange_field,
    weights,
    weight_grad,
    density,
    region,
    pattern,
    fn_atom,
    batch_atom,
):
    batches, points, blocks, size = basis.shape
    owner_rows, width = density.shape[:2]
    slabs = lax.axis_size("grid")
    atom_devices = lax.axis_size("atoms")
    atom_total = fn_atom.shape[0] // (10 * slabs * atom_devices) * slabs * atom_devices
    shapes = (slabs, atom_devices, atom_total, points, blocks, width, owner_rows)
    own, near = fetch_rows(region, density, slabs, SHARE)
    if region.shape[1] == blocks:
        ready = reorder(pattern, basis, exchange_field, basis_grad, weights)
        near, far, (basis_wide, field_wide, turned, grad_wide) = swap_halves(near, ready, atom_devices)
        built = moments_and_atoms(region, turned, grad_wide, weight_grad, fn_atom, batch_atom, atom_total)
        ready = (basis_wide, field_wide, *built)
        product, partial_grad = combine(region, ready, [own, *near, *far], shapes)
        gradient = sum_parts(partial_grad)
        contracted = write(pattern, product)
        return contracted.reshape(basis.shape), gradient
    ready = relayout(
        in_hbm(basis.reshape(batches, points * blocks, size)),
        in_hbm(exchange_field.reshape(batches, points * blocks, size)),
        points,
        blocks,
    )
    near, far, (basis_wide, field_wide) = swap_halves(near, ready, atom_devices)
    tiles, partial_grad = partial_gradient(
        region,
        pattern,
        basis_wide,
        field_wide,
        in_hbm(basis_grad.reshape(PARTS, batches, points * blocks, size)),
        weights,
        weight_grad,
        fn_atom,
        batch_atom,
        [own, *near, *far],
        shapes,
    )
    gradient = sum_parts(partial_grad)
    contracted = contract(region, pattern, basis_wide, tiles, points, blocks, width)
    return contracted.reshape(basis.shape), gradient


def solution(mesh):
    placed = (
        P(("groups", "grid", "atoms"), None, None, None),
        P(None, ("groups", "grid", "atoms"), None, None, None),
        P(("groups", "grid", "atoms"), None, None, None),
        P(("groups", "grid", "atoms"), None),
        P(None, ("groups", "grid", "atoms"), None),
        P(("groups", "grid"), None, None, None),
        P("groups", None),
        P(("groups", "grid", "atoms"), None),
        P("groups"),
        P(("groups", "grid", "atoms")),
    )
    return jax.shard_map(
        local,
        mesh=mesh,
        in_specs=placed,
        out_specs=(P(("groups", "grid", "atoms"), None, None, None), P(None, ("groups", "atoms"))),
        check_vma=False,
    )
```

```python
import functools
import math

import jax
import jax.numpy as jnp
from jax import lax
from jax.experimental import pallas as pl
from jax.experimental.pallas import tpu as pltpu
from jax.sharding import PartitionSpec as P

TRAVEL = 5
SHARE = 2
PARTS = 3
F32 = jnp.float32
BF16 = jnp.bfloat16
NT = (((1,), (1,)), ((), ()))
VMEM_LIMIT = 32 * 1024 * 1024


def owner_and_slot(region, slab, position, owner_rows):
    owner = lax.div(region[slab, position], owner_rows)
    slot = jnp.int32(0)
    count = jnp.int32(0)
    for other in range(region.shape[1]):
        same = jnp.where(lax.div(region[slab, other], owner_rows) == owner, 1, 0)
        count = count + same
        if other < position:
            slot = slot + same
    return owner, slot, count


def travel_place(slot, count, k):
    if k == 0:
        return jnp.where(slot == 0, 4, 2)
    if k == 1:
        return jnp.where(slot == 0, 0, 3)
    return jnp.where(jnp.logical_and(slot == 0, count == 2), 1, 4)


def send_kernel(region, density, *rest, share):
    *outs, sems = rest
    me = lax.axis_index("grid")
    part = lax.rem(lax.axis_index("atoms"), share)
    size = region.shape[1]
    owner_rows = density.shape[0]
    rows = density.shape[-2]
    copies = []
    for shift, out in enumerate(outs):
        slab = jnp.bitwise_xor(me, shift)
        base = jnp.int32(owner_rows)
        count = jnp.int32(0)
        for position in range(size):
            row = region[slab, position] - me * owner_rows
            mine = jnp.logical_and(row >= 0, row < owner_rows)
            base = jnp.minimum(base, jnp.where(mine, row, owner_rows))
            count = count + jnp.where(mine, 1, 0)
        base = jnp.where(count == 0, 0, base)
        after = jnp.minimum(base + 1, owner_rows - 1)
        lower = base == 0
        edge = jnp.where(jnp.logical_and(count == 2, jnp.logical_not(lower)), after, base)
        kept = out.shape[1]
        first = 0 if kept == rows else pl.multiple_of(part * kept, kept)
        here = pl.ds(first, kept)
        pairs = (
            (density.at[base, pl.ds(1, 2), here, :], out.at[pl.ds(0, 2)]),
            (density.at[after, pl.ds(0, 2), here, :], out.at[pl.ds(2, 2)]),
            (density.at[edge, jnp.where(lower, 0, 2), here, :], out.at[4]),
        )
        for number, (source, target) in enumerate(pairs):
            copies.append(pltpu.make_async_copy(source, target, sems.at[shift, number]))
    for copy in copies:
        copy.start()
    for copy in copies:
        copy.wait()


def in_hbm(array):
    return pltpu.with_memory_space_constraint(array, pltpu.HBM)


def rows_to_send(region, density, slabs, share):
    size = density.shape[-1]
    kept = [size] + [size // share] * (slabs - 1)
    return pl.pallas_call(
        functools.partial(send_kernel, share=share),
        out_shape=[jax.ShapeDtypeStruct((TRAVEL, rows, size), density.dtype) for rows in kept],
        in_specs=[pl.BlockSpec(memory_space=pltpu.SMEM), pl.BlockSpec(memory_space=pl.ANY)],
        out_specs=[pl.BlockSpec(memory_space=pltpu.VMEM)] * slabs,
        scratch_shapes=[pltpu.SemaphoreType.DMA((slabs, 3))],
        compiler_params=pltpu.CompilerParams(vmem_limit_bytes=VMEM_LIMIT),
    )(in_hbm(region), in_hbm(density))


def fetch_rows(region, density, slabs, share):
    own, *outgoing = rows_to_send(region, density, slabs, share)
    near = {}
    for shift in reversed(range(1, slabs)):
        near[shift] = lax.ppermute(outgoing[shift - 1], "grid", [(i, i ^ shift) for i in range(slabs)])
    return own, [near[shift] for shift in range(1, slabs)]


def stage_rows(stage, own, near, far, share):
    part = lax.rem(lax.axis_index("atoms"), share)
    kept = near[0].shape[1]
    for place in range(TRAVEL):
        stage[place] = own[place]
        for shift, (here, there) in enumerate(zip(near, far), 1):
            stage[shift * TRAVEL + place, pl.ds(pl.multiple_of(part * kept, kept), kept), :] = here[place]
            stage[shift * TRAVEL + place, pl.ds(pl.multiple_of((1 - part) * kept, kept), kept), :] = there[place]


def block_major(x_ref, wide, points, blocks):
    wide[...] = x_ref[0].astype(F32)
    return [wide[pl.ds(s, points, stride=blocks), :] for s in range(blocks)]


def relayout_kernel(basis, field, basis_out, field_out, wide, *, points, blocks):
    size = basis.shape[-1]
    for source, target in ((basis, basis_out), (field, field_out)):
        for s, part in enumerate(block_major(source, wide, points, blocks)):
            target[0, :, s * size : (s + 1) * size] = part.astype(BF16)


def relayout(basis, field, points, blocks):
    batches, rows, size = basis.shape
    here = pl.BlockSpec((1, rows, size), lambda b: (b, 0, 0))
    there = pl.BlockSpec((1, points, blocks * size), lambda b: (b, 0, 0))
    shape = jax.ShapeDtypeStruct((batches, points, blocks * size), BF16)
    return pl.pallas_call(
        functools.partial(relayout_kernel, points=points, blocks=blocks),
        grid=(batches,),
        out_shape=(shape, shape),
        in_specs=[here, here],
        out_specs=(there, there),
        scratch_shapes=[pltpu.VMEM((rows, size), F32)],
        compiler_params=pltpu.CompilerParams(vmem_limit_bytes=VMEM_LIMIT),
        cost_estimate=pl.CostEstimate(flops=0, bytes_accessed=8 * batches * rows * size, transcendentals=0),
    )(basis, field)


def batch_matrix(region, pattern, tiles, slab, batch, blocks, width):
    half = (width - 1) // 2
    none = tiles.shape[0] - 1
    places = [pattern[batch, s] for s in range(blocks)]
    rows = [region[slab, place] for place in places]
    strips = []
    for s in range(blocks):
        strip = []
        for t in range(blocks):
            k = rows[t] - rows[s] + half
            inside = jnp.logical_and(k >= 0, k < width)
            strip.append(tiles[jnp.where(inside, places[s] * width + k, none)])
        strips.append(jnp.concatenate(strip, axis=1))
    return jnp.concatenate(strips, axis=0)


def split(values):
    high = values.astype(BF16)
    rest = values - high.astype(F32)
    middle = rest.astype(BF16)
    low = (rest - middle.astype(F32)).astype(BF16)
    return high, middle, low


def gradient_kernel(
    region,
    pattern,
    basis,
    field,
    basis_grad,
    weights,
    weight_grad,
    fn_atom,
    batch_atom,
    places,
    *rest,
    points,
    blocks,
    width,
    owner_rows,
    slabs,
):
    *pieces, tiles, out, stage, spread, sums, energy_sums = rest
    batch = pl.program_id(0)
    batches = pl.num_programs(0)
    me = lax.axis_index("grid")
    size = tiles.shape[-1]
    region_size = region.shape[1]

    @pl.when(batch == 0)
    def _():
        tiles[region_size * width] = jnp.zeros((size, size), BF16)
        stage_rows(stage, pieces[0], pieces[1:slabs], pieces[slabs:], SHARE)
        for position in range(region_size):
            owner, slot, count = owner_and_slot(region, me, position, owner_rows)
            shift = jnp.bitwise_xor(me, owner)
            for k in range(width):
                tiles[position * width + k] = stage[shift * TRAVEL + travel_place(slot, count, k)]

    matrix = batch_matrix(region, pattern, tiles, me, batch, blocks, width)
    potential = lax.dot_general(field[0], matrix, NT, preferred_element_type=F32)
    rows = jnp.concatenate(
        [weights[pl.ds(batch, 1), :]]
        + [weight_grad[c, pl.ds(batch, 1), :] for c in range(PARTS)]
        + [jnp.zeros((8 - 1 - PARTS, points), F32)],
        axis=0,
    )
    columns = rows.T
    weight = columns[:, 0:1]
    energy = jnp.zeros((points, size), F32)
    for s in range(blocks):
        here = potential[:, s * size : (s + 1) * size]
        energy = energy + basis[0, :, s * size : (s + 1) * size].astype(F32) * here
        spread[pl.ds(s, points, stride=blocks), :] = here * weight
    scaled = spread[...]
    place = pl.ds(pl.multiple_of(batch * 8, 8), 8)
    for c in range(PARTS):
        terms = basis_grad[c, 0].astype(F32) * scaled
        sums[c, place, :] = jnp.sum(terms.reshape(-1, 8, size), axis=0)
        terms = energy * columns[:, 1 + c : 2 + c]
        energy_sums[c, place, :] = jnp.sum(terms.reshape(-1, 8, size), axis=0)

    @pl.when(batch == batches - 1)
    def _():
        padded = max(8, region_size)
        chosen = lax.broadcasted_iota(jnp.int32, (padded, places.shape[1]), 0) == places[...]
        chosen = chosen.astype(BF16)
        blocks_sum = []
        for c in range(PARTS):
            total = jnp.zeros((padded, size), F32)
            for piece in split(sums[c]):
                total = total + jnp.dot(chosen, piece, preferred_element_type=F32)
            blocks_sum.append(-2.0 * total)
        lefts = []
        for position in range(region_size):
            stack = jnp.concatenate([total[position : position + 1] for total in blocks_sum], axis=0)
            high, middle, low = (piece.astype(F32) for piece in split(stack))
            lefts.append(jnp.concatenate([high, middle, low, jnp.zeros((16 - 3 * PARTS, size), F32)], axis=0))
        left = jnp.concatenate(lefts, axis=1).astype(BF16)
        chunk = out.shape[-1]
        scale = [jnp.sum(energy_sums[c], axis=1, keepdims=True) for c in range(PARTS)]
        for device in range(out.shape[1]):
            atoms = lax.broadcasted_iota(jnp.int32, (chunk, size), 0) + device * chunk
            hot = [
                jnp.where(atoms == fn_atom[pl.ds(region[me, position], 1), :], 1.0, 0.0).astype(BF16)
                for position in range(region_size)
            ]
            found = lax.dot_general(left, jnp.concatenate(hot, axis=1), NT, preferred_element_type=F32)
            atoms = lax.broadcasted_iota(jnp.int32, (batch_atom.shape[0], chunk), 1) + device * chunk
            mine = atoms == batch_atom[...]
            for c in range(PARTS):
                value = found[c : c + 1] + found[PARTS + c : PARTS + c + 1] + found[2 * PARTS + c : 2 * PARTS + c + 1]
                value = value + jnp.sum(jnp.where(mine, scale[c], 0.0), axis=0, keepdims=True)
                for slab in range(slabs):
                    out[slab, device, c : c + 1, :] = value


def partial_gradient(
    region, pattern, basis, field, basis_grad, weights, weight_grad, fn_atom, batch_atom, pieces, shapes
):
    slabs, atom_devices, atom_total, points, blocks, width, owner_rows = shapes
    batches, _, columns = basis.shape
    size = columns // blocks
    region_size = region.shape[1]
    fn_atom = fn_atom.reshape(-1, size)
    places = jnp.broadcast_to(pattern[:, None, :], (batches, 8 // blocks, blocks)).reshape(1, -1)
    batch_atom = jnp.broadcast_to(batch_atom[:, None], (batches, 8)).reshape(-1, 1)
    block = pl.BlockSpec((1, points, columns), lambda b, *_: (b, 0, 0))
    whole = pl.BlockSpec(memory_space=pltpu.VMEM)
    tile_shape = (region_size * width + 1, size, size)
    out_shape = (slabs, atom_devices, PARTS, atom_total // atom_devices)
    return pl.pallas_call(
        functools.partial(
            gradient_kernel, points=points, blocks=blocks, width=width, owner_rows=owner_rows, slabs=slabs
        ),
        grid_spec=pltpu.PrefetchScalarGridSpec(
            num_scalar_prefetch=2,
            grid=(batches,),
            in_specs=[
                block,
                block,
                pl.BlockSpec((PARTS, 1, points * blocks, size), lambda b, *_: (0, b, 0, 0)),
            ]
            + [whole] * (5 + len(pieces)),
            out_specs=(whole, whole),
            scratch_shapes=[
                pltpu.VMEM((slabs * TRAVEL, size, size), BF16),
                pltpu.VMEM((points * blocks, size), F32),
                pltpu.VMEM((PARTS, batches * 8, size), F32),
                pltpu.VMEM((PARTS, batches * 8, size), F32),
            ],
        ),
        out_shape=(jax.ShapeDtypeStruct(tile_shape, BF16), jax.ShapeDtypeStruct(out_shape, F32)),
        compiler_params=pltpu.CompilerParams(vmem_limit_bytes=VMEM_LIMIT),
    )(region, pattern, basis, field, basis_grad, weights, weight_grad, fn_atom, batch_atom, places, *pieces)


def product_kernel(region, pattern, basis, tiles, out, spread, *, points, blocks, width):
    me = lax.axis_index("grid")
    size = tiles.shape[-1]
    matrix = batch_matrix(region, pattern, tiles, me, pl.program_id(0), blocks, width)
    product = jnp.dot(basis[0], matrix, preferred_element_type=F32)
    for t in range(blocks):
        spread[pl.ds(t, points, stride=blocks), :] = product[:, t * size : (t + 1) * size]
    out[0] = spread[...].astype(BF16)


def contract(region, pattern, basis, tiles, points, blocks, width):
    batches, _, columns = basis.shape
    size = columns // blocks
    return pl.pallas_call(
        functools.partial(product_kernel, points=points, blocks=blocks, width=width),
        grid_spec=pltpu.PrefetchScalarGridSpec(
            num_scalar_prefetch=2,
            grid=(batches,),
            in_specs=[
                pl.BlockSpec((1, points, columns), lambda b, *_: (b, 0, 0)),
                pl.BlockSpec(memory_space=pltpu.VMEM),
            ],
            out_specs=pl.BlockSpec((1, points * blocks, size), lambda b, *_: (b, 0, 0)),
            scratch_shapes=[pltpu.VMEM((points * blocks, size), F32)],
        ),
        out_shape=jax.ShapeDtypeStruct((batches, points * blocks, size), BF16),
        compiler_params=pltpu.CompilerParams(vmem_limit_bytes=VMEM_LIMIT),
        cost_estimate=pl.CostEstimate(
            flops=2 * batches * points * columns * columns,
            bytes_accessed=4 * batches * points * columns,
            transcendentals=0,
        ),
    )(region, pattern, basis, tiles)


def add_moments(moments, turned, grads, fresh):
    blocks, _, size = grads.shape[1:]
    for c in range(PARTS):
        for p in range(0, blocks, 2):
            rows = slice(max(p - 1, 0) * size, min(p + 3, blocks) * size)
            columns = slice(p * size, min(p + 2, blocks) * size)
            right = jnp.concatenate([grads[c, place] for place in range(p, min(p + 2, blocks))], axis=1)
            value = jnp.dot(turned[rows, :], right, preferred_element_type=F32)
            moments[c, rows, columns] = value if fresh else moments[c, rows, columns] + value


def reorder_kernel(
    pattern,
    basis,
    field,
    basis_grad,
    weights,
    basis_out,
    field_out,
    moments,
    last_turned,
    last_grads,
    basis_in,
    field_in,
    grad_in,
    wide,
    turned,
    grads,
    sems,
):
    batches, blocks, points, size = basis_out.shape
    groups = sems.shape[0]
    step = batches // groups
    turned = [last_turned if (groups - 1 - group) % 2 == 0 else turned for group in range(groups)]
    grads = [last_grads if (groups - 1 - group) % 2 == 0 else grads for group in range(groups)]

    def copies(group):
        here = pl.ds(group * step, step)
        return (
            pltpu.make_async_copy(field.at[here], field_in.at[here], sems.at[group, 0]),
            pltpu.make_async_copy(basis_grad.at[:, here], grad_in.at[:, here], sems.at[group, 1]),
            pltpu.make_async_copy(basis.at[here], basis_in.at[here], sems.at[group, 2]),
        )

    for group in range(groups):
        for copy in copies(group):
            copy.start()

    for group in range(groups):
        for copy in copies(group):
            copy.wait()
        for inner in range(step):
            batch = group * step + inner
            points_here = slice(inner * points, (inner + 1) * points)
            places = [pattern[s, batch] for s in range(blocks)]
            weight = weights[batch : batch + 1, :]
            wide[0] = field_in[batch].astype(F32)
            wide[1] = basis_in[batch].astype(F32)
            for c in range(PARTS):
                wide[2 + c] = grad_in[c, batch].astype(F32)
            for s, place in enumerate(places):
                strided = pl.ds(s, points, stride=blocks)
                values = wide[0, strided, :]
                field_out[batch, place] = values.astype(BF16)
                rows = pl.ds(pl.multiple_of(place * size, size), size)
                turned[group][rows, points_here] = (values.T * weight).astype(BF16)
                basis_out[batch, place] = wide[1, strided, :].astype(BF16)
                for c in range(PARTS):
                    grads[group][c, place, points_here, :] = wide[2 + c, strided, :].astype(BF16)
        if group > 0:
            add_moments(moments, turned[group - 1], grads[group - 1], group == 1)
    if groups == 1:
        moments[...] = jnp.zeros_like(moments)


def reorder(pattern, basis, field, basis_grad, weights):
    batches, points, blocks, size = basis.shape
    rows = points * blocks
    step = 4 if batches % 4 == 0 else 1
    hbm = pl.BlockSpec(memory_space=pl.ANY)
    vmem = pl.BlockSpec(memory_space=pltpu.VMEM)
    ordered = jax.ShapeDtypeStruct((batches, blocks, points, size), BF16)
    turned = (blocks * size, step * points)
    grads = (PARTS, blocks, step * points, size)
    return pl.pallas_call(
        reorder_kernel,
        out_shape=(
            ordered,
            ordered,
            jax.ShapeDtypeStruct((PARTS, blocks * size, blocks * size), F32),
            jax.ShapeDtypeStruct(turned, BF16),
            jax.ShapeDtypeStruct(grads, BF16),
        ),
        in_specs=[pl.BlockSpec(memory_space=pltpu.SMEM), hbm, hbm, hbm, vmem],
        out_specs=(vmem,) * 5,
        scratch_shapes=[
            pltpu.VMEM((batches, rows, size), BF16),
            pltpu.VMEM((batches, rows, size), BF16),
            pltpu.VMEM((PARTS, batches, rows, size), BF16),
            pltpu.VMEM((2 + PARTS, rows, size), F32),
            pltpu.VMEM(turned, BF16),
            pltpu.VMEM(grads, BF16),
            pltpu.SemaphoreType.DMA((batches // step, 3)),
        ],
        compiler_params=pltpu.CompilerParams(vmem_limit_bytes=VMEM_LIMIT),
        cost_estimate=pl.CostEstimate(
            flops=2 * PARTS * batches * points * (blocks * size) ** 2,
            bytes_accessed=2 * (2 + PARTS) * batches * rows * size,
            transcendentals=0,
        ),
    )(
        in_hbm(pattern.T),
        in_hbm(basis.reshape(batches, rows, size)),
        in_hbm(field.reshape(batches, rows, size)),
        in_hbm(basis_grad.reshape(PARTS, batches, rows, size)),
        in_hbm(weights),
    )


def moment_kernel(
    region, before, turned, grads, weight_grad, fn_atom, batch_atom, moments, hot, grad_columns
):
    blocks, _, size = grads.shape[1:]
    batches = weight_grad.shape[1]
    me = lax.axis_index("grid")
    atoms = lax.broadcasted_iota(jnp.int32, (hot.shape[0], size), 0)
    rows = [fn_atom[pl.ds(region[me, position], 1), :] for position in range(blocks)]
    rows.append(jnp.concatenate([batch_atom[...], jnp.full((1, size - batches), -1, jnp.int32)], axis=1))
    for number, ids in enumerate(rows):
        hot[:, number * size : (number + 1) * size] = jnp.where(atoms == ids, 1.0, 0.0).astype(BF16)
    for c in range(PARTS):
        padded = jnp.concatenate([weight_grad[c], jnp.zeros((size - batches, weight_grad.shape[2]), F32)], axis=0)
        grad_columns[c] = padded.T
    add_moments(moments, turned, grads, False)


def moments_and_atoms(region, before, turned, grads, weight_grad, fn_atom, batch_atom, atom_total):
    blocks, depth, size = grads.shape[1:]
    points = weight_grad.shape[2]
    vmem = pl.BlockSpec(memory_space=pltpu.VMEM)
    return pl.pallas_call(
        moment_kernel,
        out_shape=(
            jax.ShapeDtypeStruct(before.shape, F32),
            jax.ShapeDtypeStruct((atom_total, (blocks + 1) * size), BF16),
            jax.ShapeDtypeStruct((PARTS, points, size), F32),
        ),
        in_specs=[pl.BlockSpec(memory_space=pltpu.SMEM)] + [vmem] * 6,
        out_specs=(vmem,) * 3,
        input_output_aliases={1: 0},
        compiler_params=pltpu.CompilerParams(vmem_limit_bytes=VMEM_LIMIT),
        cost_estimate=pl.CostEstimate(
            flops=2 * PARTS * depth * (blocks * size) ** 2, bytes_accessed=0, transcendentals=0
        ),
    )(
        in_hbm(region),
        before,
        turned,
        grads,
        in_hbm(weight_grad),
        in_hbm(fn_atom.reshape(-1, size)),
        in_hbm(batch_atom.reshape(1, -1)),
    )


def combine_kernel(
    region, basis, field, moments, hot, grad_columns, *rest, owner_rows, slabs, width, step
):
    *pieces, product_out, out, stage, matrix, energies = rest
    batches, blocks, points, size = basis.shape
    me = lax.axis_index("grid")
    half = (width - 1) // 2
    stage_rows(stage, pieces[0], pieces[1:slabs], pieces[slabs:], SHARE)
    rows = [region[me, position] for position in range(blocks)]
    found = [owner_and_slot(region, me, position, owner_rows) for position in range(blocks)]
    totals = [[jnp.zeros((8, size), F32) for _ in range(blocks)] for _ in range(PARTS)]
    for p in range(blocks):
        owner, slot, count = found[p]
        first = jnp.bitwise_xor(me, owner) * TRAVEL
        for q in range(blocks):
            if abs(q - p) > half:
                matrix[p * size : (p + 1) * size, q * size : (q + 1) * size] = jnp.zeros((size, size), BF16)
                continue
            k = rows[q] - rows[p] + half
            place = jnp.where(
                k == 0,
                travel_place(slot, count, 0),
                jnp.where(k == 1, travel_place(slot, count, 1), travel_place(slot, count, 2)),
            )
            inside = jnp.logical_and(k >= 0, k < width)
            tile = stage[first + place].astype(F32)
            tile = jnp.where(inside, tile, 0.0)
            matrix[p * size : (p + 1) * size, q * size : (q + 1) * size] = tile.astype(BF16)
            turned = tile.T
            for c in range(PARTS):
                terms = turned * moments[c, q * size : (q + 1) * size, p * size : (p + 1) * size]
                totals[c][p] = totals[c][p] + jnp.sum(terms.reshape(-1, 8, size), axis=0)
    derivative = [
        jnp.concatenate([jnp.sum(total, axis=0, keepdims=True) for total in totals[c]], axis=1) for c in range(PARTS)
    ]

    energies[...] = jnp.zeros_like(energies)
    lanes = lax.broadcasted_iota(jnp.int32, (points, size), 1)

    @pl.loop(0, batches // step)
    def _(group):
        left = [
            jnp.concatenate([basis[group * step + inner, p] for p in range(blocks)], axis=1) for inner in range(step)
        ]
        product = jnp.dot(jnp.concatenate(left, axis=0), matrix[...], preferred_element_type=F32)
        for inner in range(step):
            batch = group * step + inner
            energy = jnp.zeros((points, size), F32)
            for q in range(blocks):
                part = product[inner * points : (inner + 1) * points, q * size : (q + 1) * size]
                product_out[batch, q] = part.astype(BF16)
                energy = energy + part * field[batch, q].astype(F32)
            energy = jnp.sum(energy, axis=1, keepdims=True)
            energies[...] = jnp.where(lanes == batch, energy, energies[...])

    lefts = []
    for c in range(PARTS):
        term = jnp.sum(energies[...] * grad_columns[c], axis=0, keepdims=True)
        lefts.append(jnp.concatenate([-2.0 * derivative[c], term], axis=1))
    left = jnp.concatenate(lefts, axis=0)
    high, middle, low = (piece.astype(F32) for piece in split(left))
    left = jnp.concatenate([high, middle, low, jnp.zeros((16 - 3 * PARTS, left.shape[1]), F32)], axis=0).astype(BF16)
    chunk = out.shape[-1]
    for device in range(out.shape[1]):
        sums = lax.dot_general(
            left, hot[device * chunk : (device + 1) * chunk, :], NT, preferred_element_type=F32
        )
        value = sums[:PARTS] + sums[PARTS : 2 * PARTS] + sums[2 * PARTS : 3 * PARTS]
        for slab in range(slabs):
            out[slab, device] = value


def combine(region, prepared, pieces, shapes):
    basis, field, moments, hot, grad_columns = prepared
    slabs, atom_devices, atom_total, points, blocks, width, owner_rows = shapes
    batches, _, _, size = basis.shape
    step = 4 if batches % 4 == 0 else 1
    vmem = pl.BlockSpec(memory_space=pltpu.VMEM)
    return pl.pallas_call(
        functools.partial(combine_kernel, owner_rows=owner_rows, slabs=slabs, width=width, step=step),
        out_shape=(
            jax.ShapeDtypeStruct(basis.shape, BF16),
            jax.ShapeDtypeStruct((slabs, atom_devices, PARTS, atom_total // atom_devices), F32),
        ),
        in_specs=[pl.BlockSpec(memory_space=pltpu.SMEM)] + [vmem] * (5 + len(pieces)),
        out_specs=(vmem, vmem),
        scratch_shapes=[
            pltpu.VMEM((slabs * TRAVEL, size, size), BF16),
            pltpu.VMEM((blocks * size, blocks * size), BF16),
            pltpu.VMEM((points, size), F32),
        ],
        compiler_params=pltpu.CompilerParams(vmem_limit_bytes=VMEM_LIMIT),
    )(in_hbm(region), basis, field, moments, hot, grad_columns, *pieces)


def write_kernel(pattern, product, out, wide, staged, sems):
    batches, blocks, points, size = product.shape

    def copy(batch):
        return pltpu.make_async_copy(staged.at[batch], out.at[batch], sems.at[batch])

    @pl.loop(0, batches // 2)
    def _(pair):
        for inner in range(2):
            batch = pair * 2 + inner
            for t in range(blocks):
                wide[inner, pl.ds(t, points, stride=blocks), :] = product[batch, pattern[t, batch]].astype(F32)
            staged[batch] = wide[inner].astype(BF16)
            copy(batch).start()

    @pl.loop(0, batches)
    def _(batch):
        copy(batch).wait()


def write(pattern, product):
    batches, blocks, points, size = product.shape
    shape = (batches, points * blocks, size)
    return pl.pallas_call(
        write_kernel,
        out_shape=jax.ShapeDtypeStruct(shape, BF16),
        in_specs=[pl.BlockSpec(memory_space=pltpu.SMEM), pl.BlockSpec(memory_space=pltpu.VMEM)],
        out_specs=pl.BlockSpec(memory_space=pl.ANY),
        scratch_shapes=[
            pltpu.VMEM((2, points * blocks, size), F32),
            pltpu.VMEM(shape, BF16),
            pltpu.SemaphoreType.DMA((batches,)),
        ],
        compiler_params=pltpu.CompilerParams(vmem_limit_bytes=VMEM_LIMIT),
        cost_estimate=pl.CostEstimate(flops=0, bytes_accessed=4 * math.prod(shape), transcendentals=0),
    )(in_hbm(pattern.T), product)


def swap_halves(near, ready, atom_devices):
    near, ready = lax.optimization_barrier((near, ready))
    swap = [(i, i ^ 1) for i in range(atom_devices)]
    return near, [lax.ppermute(piece, "atoms", swap) for piece in near], ready


def sum_parts(partial_grad):
    parts = partial_grad.reshape((-1,) + partial_grad.shape[2:])
    parts = lax.all_to_all(parts, ("grid", "atoms"), split_axis=0, concat_axis=0, tiled=True)
    return jnp.sum(parts, axis=0)


def local(
    basis,
    basis_grad,
    exchange_field,
    weights,
    weight_grad,
    density,
    region,
    pattern,
    fn_atom,
    batch_atom,
):
    batches, points, blocks, size = basis.shape
    owner_rows, width = density.shape[:2]
    slabs = lax.axis_size("grid")
    atom_devices = lax.axis_size("atoms")
    atom_total = fn_atom.shape[0] // (10 * slabs * atom_devices) * slabs * atom_devices
    shapes = (slabs, atom_devices, atom_total, points, blocks, width, owner_rows)
    own, near = fetch_rows(region, density, slabs, SHARE)
    if region.shape[1] == blocks:
        ready = reorder(pattern, basis, exchange_field, basis_grad, weights)
        near, far, (basis_wide, field_wide, *partial) = swap_halves(near, ready, atom_devices)
        built = moments_and_atoms(region, *partial, weight_grad, fn_atom, batch_atom, atom_total)
        ready = (basis_wide, field_wide, *built)
        product, partial_grad = combine(region, ready, [own, *near, *far], shapes)
        gradient = sum_parts(partial_grad)
        contracted = write(pattern, product)
        return contracted.reshape(basis.shape), gradient
    ready = relayout(
        in_hbm(basis.reshape(batches, points * blocks, size)),
        in_hbm(exchange_field.reshape(batches, points * blocks, size)),
        points,
        blocks,
    )
    near, far, (basis_wide, field_wide) = swap_halves(near, ready, atom_devices)
    tiles, partial_grad = partial_gradient(
        region,
        pattern,
        basis_wide,
        field_wide,
        in_hbm(basis_grad.reshape(PARTS, batches, points * blocks, size)),
        weights,
        weight_grad,
        fn_atom,
        batch_atom,
        [own, *near, *far],
        shapes,
    )
    gradient = sum_parts(partial_grad)
    contracted = contract(region, pattern, basis_wide, tiles, points, blocks, width)
    return contracted.reshape(basis.shape), gradient


def solution(mesh):
    placed = (
        P(("groups", "grid", "atoms"), None, None, None),
        P(None, ("groups", "grid", "atoms"), None, None, None),
        P(("groups", "grid", "atoms"), None, None, None),
        P(("groups", "grid", "atoms"), None),
        P(None, ("groups", "grid", "atoms"), None),
        P(("groups", "grid"), None, None, None),
        P("groups", None),
        P(("groups", "grid", "atoms"), None),
        P("groups"),
        P(("groups", "grid", "atoms")),
    )
    return jax.shard_map(
        local,
        mesh=mesh,
        in_specs=placed,
        out_specs=(P(("groups", "grid", "atoms"), None, None, None), P(None, ("groups", "atoms"))),
        check_vma=False,
    )
```

```python
import functools
import math

import jax
import jax.numpy as jnp
from jax import lax
from jax.experimental import pallas as pl
from jax.experimental.pallas import tpu as pltpu
from jax.sharding import PartitionSpec as P

TRAVEL = 5
SHARE = 2
PARTS = 3
F32 = jnp.float32
BF16 = jnp.bfloat16
NT = (((1,), (1,)), ((), ()))
VMEM_LIMIT = 32 * 1024 * 1024


def owner_and_slot(region, slab, position, owner_rows):
    owner = lax.div(region[slab, position], owner_rows)
    slot = jnp.int32(0)
    count = jnp.int32(0)
    for other in range(region.shape[1]):
        same = jnp.where(lax.div(region[slab, other], owner_rows) == owner, 1, 0)
        count = count + same
        if other < position:
            slot = slot + same
    return owner, slot, count


def travel_place(slot, count, k):
    if k == 0:
        return jnp.where(slot == 0, 4, 2)
    if k == 1:
        return jnp.where(slot == 0, 0, 3)
    return jnp.where(jnp.logical_and(slot == 0, count == 2), 1, 4)


def send_kernel(region, density, *rest, share):
    *outs, sems = rest
    me = lax.axis_index("grid")
    part = lax.rem(lax.axis_index("atoms"), share)
    size = region.shape[1]
    owner_rows = density.shape[0]
    rows = density.shape[-2]
    copies = []
    for shift, out in zip((0, *reversed(range(1, len(outs)))), outs):
        slab = jnp.bitwise_xor(me, shift)
        base = jnp.int32(owner_rows)
        count = jnp.int32(0)
        for position in range(size):
            row = region[slab, position] - me * owner_rows
            mine = jnp.logical_and(row >= 0, row < owner_rows)
            base = jnp.minimum(base, jnp.where(mine, row, owner_rows))
            count = count + jnp.where(mine, 1, 0)
        base = jnp.where(count == 0, 0, base)
        after = jnp.minimum(base + 1, owner_rows - 1)
        lower = base == 0
        edge = jnp.where(jnp.logical_and(count == 2, jnp.logical_not(lower)), after, base)
        kept = out.shape[1]
        first = 0 if kept == rows else pl.multiple_of(part * kept, kept)
        here = pl.ds(first, kept)
        pairs = (
            (density.at[base, pl.ds(1, 2), here, :], out.at[pl.ds(0, 2)]),
            (density.at[after, pl.ds(0, 2), here, :], out.at[pl.ds(2, 2)]),
            (density.at[edge, jnp.where(lower, 0, 2), here, :], out.at[4]),
        )
        for number, (source, target) in enumerate(pairs):
            copies.append(pltpu.make_async_copy(source, target, sems.at[shift, number]))
    for copy in copies:
        copy.start()
    for copy in copies:
        copy.wait()


def in_hbm(array):
    return pltpu.with_memory_space_constraint(array, pltpu.HBM)


def rows_to_send(region, density, slabs, share):
    size = density.shape[-1]
    kept = [size] + [size // share] * (slabs - 1)
    return pl.pallas_call(
        functools.partial(send_kernel, share=share),
        out_shape=[jax.ShapeDtypeStruct((TRAVEL, rows, size), density.dtype) for rows in kept],
        in_specs=[pl.BlockSpec(memory_space=pltpu.SMEM), pl.BlockSpec(memory_space=pl.ANY)],
        out_specs=[pl.BlockSpec(memory_space=pltpu.VMEM)] * slabs,
        scratch_shapes=[pltpu.SemaphoreType.DMA((slabs, 3))],
        compiler_params=pltpu.CompilerParams(vmem_limit_bytes=VMEM_LIMIT),
    )(in_hbm(region), in_hbm(density))


def fetch_rows(region, density, slabs, share):
    own, *outgoing = rows_to_send(region, density, slabs, share)
    near = {}
    for shift in reversed(range(1, slabs)):
        near[shift] = lax.ppermute(outgoing[slabs - 1 - shift], "grid", [(i, i ^ shift) for i in range(slabs)])
    return own, [near[shift] for shift in range(1, slabs)]


def stage_rows(stage, own, near, far, share):
    part = lax.rem(lax.axis_index("atoms"), share)
    kept = near[0].shape[1]
    for place in range(TRAVEL):
        stage[place] = own[place]
        for shift, (here, there) in enumerate(zip(near, far), 1):
            stage[shift * TRAVEL + place, pl.ds(pl.multiple_of(part * kept, kept), kept), :] = here[place]
            stage[shift * TRAVEL + place, pl.ds(pl.multiple_of((1 - part) * kept, kept), kept), :] = there[place]


def block_major(x_ref, wide, points, blocks):
    wide[...] = x_ref[0].astype(F32)
    return [wide[pl.ds(s, points, stride=blocks), :] for s in range(blocks)]


def relayout_kernel(basis, field, basis_out, field_out, wide, *, points, blocks):
    size = basis.shape[-1]
    for source, target in ((basis, basis_out), (field, field_out)):
        for s, part in enumerate(block_major(source, wide, points, blocks)):
            target[0, :, s * size : (s + 1) * size] = part.astype(BF16)


def relayout(basis, field, points, blocks):
    batches, rows, size = basis.shape
    here = pl.BlockSpec((1, rows, size), lambda b: (b, 0, 0))
    there = pl.BlockSpec((1, points, blocks * size), lambda b: (b, 0, 0))
    shape = jax.ShapeDtypeStruct((batches, points, blocks * size), BF16)
    return pl.pallas_call(
        functools.partial(relayout_kernel, points=points, blocks=blocks),
        grid=(batches,),
        out_shape=(shape, shape),
        in_specs=[here, here],
        out_specs=(there, there),
        scratch_shapes=[pltpu.VMEM((rows, size), F32)],
        compiler_params=pltpu.CompilerParams(vmem_limit_bytes=VMEM_LIMIT),
        cost_estimate=pl.CostEstimate(flops=0, bytes_accessed=8 * batches * rows * size, transcendentals=0),
    )(basis, field)


def batch_matrix(region, pattern, tiles, slab, batch, blocks, width):
    half = (width - 1) // 2
    none = tiles.shape[0] - 1
    places = [pattern[batch, s] for s in range(blocks)]
    rows = [region[slab, place] for place in places]
    strips = []
    for s in range(blocks):
        strip = []
        for t in range(blocks):
            k = rows[t] - rows[s] + half
            inside = jnp.logical_and(k >= 0, k < width)
            strip.append(tiles[jnp.where(inside, places[s] * width + k, none)])
        strips.append(jnp.concatenate(strip, axis=1))
    return jnp.concatenate(strips, axis=0)


def split(values):
    high = values.astype(BF16)
    rest = values - high.astype(F32)
    middle = rest.astype(BF16)
    low = (rest - middle.astype(F32)).astype(BF16)
    return high, middle, low


def gradient_kernel(
    region,
    pattern,
    basis,
    field,
    basis_grad,
    weights,
    weight_grad,
    fn_atom,
    batch_atom,
    places,
    *rest,
    points,
    blocks,
    width,
    owner_rows,
    slabs,
):
    *pieces, tiles, out, stage, spread, sums, energy_sums = rest
    batch = pl.program_id(0)
    batches = pl.num_programs(0)
    me = lax.axis_index("grid")
    me_atoms = lax.axis_index("atoms")
    size = tiles.shape[-1]
    region_size = region.shape[1]

    @pl.when(batch == 0)
    def _():
        tiles[region_size * width] = jnp.zeros((size, size), BF16)
        stage_rows(stage, pieces[0], pieces[1:slabs], pieces[slabs:], SHARE)
        for position in range(region_size):
            owner, slot, count = owner_and_slot(region, me, position, owner_rows)
            shift = jnp.bitwise_xor(me, owner)
            for k in range(width):
                tiles[position * width + k] = stage[shift * TRAVEL + travel_place(slot, count, k)]

    matrix = batch_matrix(region, pattern, tiles, me, batch, blocks, width)
    potential = lax.dot_general(field[0], matrix, NT, preferred_element_type=F32)
    rows = jnp.concatenate(
        [weights[pl.ds(batch, 1), :]]
        + [weight_grad[c, pl.ds(batch, 1), :] for c in range(PARTS)]
        + [jnp.zeros((8 - 1 - PARTS, points), F32)],
        axis=0,
    )
    columns = rows.T
    weight = columns[:, 0:1]
    energy = jnp.zeros((points, size), F32)
    for s in range(blocks):
        here = potential[:, s * size : (s + 1) * size]
        energy = energy + basis[0, :, s * size : (s + 1) * size].astype(F32) * here
        spread[pl.ds(s, points, stride=blocks), :] = here * weight
    scaled = spread[...]
    place = pl.ds(pl.multiple_of(batch * 8, 8), 8)
    for c in range(PARTS):
        terms = basis_grad[c, 0].astype(F32) * scaled
        sums[c, place, :] = jnp.sum(terms.reshape(-1, 8, size), axis=0)
        terms = energy * columns[:, 1 + c : 2 + c]
        energy_sums[c, place, :] = jnp.sum(terms.reshape(-1, 8, size), axis=0)

    @pl.when(batch == batches - 1)
    def _():
        padded = max(8, region_size)
        chosen = lax.broadcasted_iota(jnp.int32, (padded, places.shape[1]), 0) == places[...]
        chosen = chosen.astype(BF16)
        blocks_sum = []
        for c in range(PARTS):
            total = jnp.zeros((padded, size), F32)
            for piece in split(sums[c]):
                total = total + jnp.dot(chosen, piece, preferred_element_type=F32)
            blocks_sum.append(-2.0 * total)
        lefts = []
        for position in range(region_size):
            stack = jnp.concatenate([total[position : position + 1] for total in blocks_sum], axis=0)
            high, middle, low = (piece.astype(F32) for piece in split(stack))
            lefts.append(jnp.concatenate([high, middle, low, jnp.zeros((16 - 3 * PARTS, size), F32)], axis=0))
        left = jnp.concatenate(lefts, axis=1).astype(BF16)
        chunk = out.shape[-1]
        scale = [jnp.sum(energy_sums[c], axis=1, keepdims=True) for c in range(PARTS)]
        for device in range(out.shape[0]):
            atoms = lax.broadcasted_iota(jnp.int32, (chunk, size), 0) + device * chunk
            hot = [
                jnp.where(atoms == fn_atom[pl.ds(region[me, position], 1), :], 1.0, 0.0).astype(BF16)
                for position in range(region_size)
            ]
            found = lax.dot_general(left, jnp.concatenate(hot, axis=1), NT, preferred_element_type=F32)
            atoms = lax.broadcasted_iota(jnp.int32, (batch_atom.shape[0], chunk), 1) + device * chunk
            mine = atoms == batch_atom[...]
            for c in range(PARTS):
                value = found[c : c + 1] + found[PARTS + c : PARTS + c + 1] + found[2 * PARTS + c : 2 * PARTS + c + 1]
                value = value + jnp.sum(jnp.where(mine, scale[c], 0.0), axis=0, keepdims=True)
                out[jnp.bitwise_xor(me_atoms, device), c : c + 1, :] = value


def partial_gradient(
    region, pattern, basis, field, basis_grad, weights, weight_grad, fn_atom, batch_atom, pieces, shapes
):
    slabs, atom_devices, atom_total, points, blocks, width, owner_rows = shapes
    batches, _, columns = basis.shape
    size = columns // blocks
    region_size = region.shape[1]
    fn_atom = fn_atom.reshape(-1, size)
    places = jnp.broadcast_to(pattern[:, None, :], (batches, 8 // blocks, blocks)).reshape(1, -1)
    batch_atom = jnp.broadcast_to(batch_atom[:, None], (batches, 8)).reshape(-1, 1)
    block = pl.BlockSpec((1, points, columns), lambda b, *_: (b, 0, 0))
    whole = pl.BlockSpec(memory_space=pltpu.VMEM)
    tile_shape = (region_size * width + 1, size, size)
    out_shape = (atom_devices, PARTS, atom_total // atom_devices)
    return pl.pallas_call(
        functools.partial(
            gradient_kernel, points=points, blocks=blocks, width=width, owner_rows=owner_rows, slabs=slabs
        ),
        grid_spec=pltpu.PrefetchScalarGridSpec(
            num_scalar_prefetch=2,
            grid=(batches,),
            in_specs=[
                block,
                block,
                pl.BlockSpec((PARTS, 1, points * blocks, size), lambda b, *_: (0, b, 0, 0)),
            ]
            + [whole] * (5 + len(pieces)),
            out_specs=(whole, whole),
            scratch_shapes=[
                pltpu.VMEM((slabs * TRAVEL, size, size), BF16),
                pltpu.VMEM((points * blocks, size), F32),
                pltpu.VMEM((PARTS, batches * 8, size), F32),
                pltpu.VMEM((PARTS, batches * 8, size), F32),
            ],
        ),
        out_shape=(jax.ShapeDtypeStruct(tile_shape, BF16), jax.ShapeDtypeStruct(out_shape, F32)),
        compiler_params=pltpu.CompilerParams(vmem_limit_bytes=VMEM_LIMIT),
    )(region, pattern, basis, field, basis_grad, weights, weight_grad, fn_atom, batch_atom, places, *pieces)


def product_kernel(region, pattern, basis, tiles, out, spread, *, points, blocks, width):
    me = lax.axis_index("grid")
    size = tiles.shape[-1]
    matrix = batch_matrix(region, pattern, tiles, me, pl.program_id(0), blocks, width)
    product = jnp.dot(basis[0], matrix, preferred_element_type=F32)
    for t in range(blocks):
        spread[pl.ds(t, points, stride=blocks), :] = product[:, t * size : (t + 1) * size]
    out[0] = spread[...].astype(BF16)


def contract(region, pattern, basis, tiles, points, blocks, width):
    batches, _, columns = basis.shape
    size = columns // blocks
    return pl.pallas_call(
        functools.partial(product_kernel, points=points, blocks=blocks, width=width),
        grid_spec=pltpu.PrefetchScalarGridSpec(
            num_scalar_prefetch=2,
            grid=(batches,),
            in_specs=[
                pl.BlockSpec((1, points, columns), lambda b, *_: (b, 0, 0)),
                pl.BlockSpec(memory_space=pltpu.VMEM),
            ],
            out_specs=pl.BlockSpec((1, points * blocks, size), lambda b, *_: (b, 0, 0)),
            scratch_shapes=[pltpu.VMEM((points * blocks, size), F32)],
        ),
        out_shape=jax.ShapeDtypeStruct((batches, points * blocks, size), BF16),
        compiler_params=pltpu.CompilerParams(vmem_limit_bytes=VMEM_LIMIT),
        cost_estimate=pl.CostEstimate(
            flops=2 * batches * points * columns * columns,
            bytes_accessed=4 * batches * points * columns,
            transcendentals=0,
        ),
    )(region, pattern, basis, tiles)


def moment_terms(blocks):
    return [(c, p) for c in range(PARTS) for p in range(0, blocks, 2)]


def add_moments(moments, turned, grads, fresh, term):
    c, p = term
    blocks, _, size = grads.shape[1:]
    rows = slice(max(p - 1, 0) * size, min(p + 3, blocks) * size)
    columns = slice(p * size, min(p + 2, blocks) * size)
    right = jnp.concatenate([grads[c, place] for place in range(p, min(p + 2, blocks))], axis=1)
    value = jnp.dot(turned[rows, :], right, preferred_element_type=F32)
    moments[c, rows, columns] = value if fresh else moments[c, rows, columns] + value


def reorder_kernel(
    pattern_hbm,
    basis,
    field,
    basis_grad,
    weights_hbm,
    basis_out,
    field_out,
    moments,
    last_turned,
    last_grads,
    pattern,
    weights,
    basis_in,
    field_in,
    grad_in,
    wide,
    turned,
    grads,
    sems,
    small_sems,
):
    batches, blocks, points, size = basis_out.shape
    groups = sems.shape[0]
    step = batches // groups
    turned = [last_turned if (groups - 1 - group) % 2 == 0 else turned for group in range(groups)]
    grads = [last_grads if (groups - 1 - group) % 2 == 0 else grads for group in range(groups)]

    def copies(group):
        here = pl.ds(group * step, step)
        return (
            pltpu.make_async_copy(field.at[here], field_in.at[here], sems.at[group, 0]),
            pltpu.make_async_copy(basis_grad.at[:, here], grad_in.at[:, here], sems.at[group, 1]),
            pltpu.make_async_copy(basis.at[here], basis_in.at[here], sems.at[group, 2]),
        )

    for copy in copies(0):
        copy.start()
    small = (
        pltpu.make_async_copy(pattern_hbm, pattern, small_sems.at[0]),
        pltpu.make_async_copy(weights_hbm, weights, small_sems.at[1]),
    )
    for copy in small:
        copy.start()
    for group in range(1, groups):
        for copy in copies(group):
            copy.start()
    for copy in small:
        copy.wait()

    def put_in_order(group, inner, array):
        batch = group * step + inner
        points_here = slice(inner * points, (inner + 1) * points)
        source = (field_in, basis_in)[array].at[batch] if array < 2 else grad_in.at[array - 2, batch]
        wide[array] = source[...].astype(F32)
        for s in range(blocks):
            place = pattern[s, batch]
            values = wide[array, pl.ds(s, points, stride=blocks), :]
            if array == 0:
                field_out[batch, place] = values.astype(BF16)
                rows = pl.ds(pl.multiple_of(place * size, size), size)
                turned[group][rows, points_here] = (values.T * weights[batch : batch + 1, :]).astype(BF16)
            elif array == 1:
                basis_out[batch, place] = values.astype(BF16)
            else:
                grads[group][array - 2, place, points_here, :] = values.astype(BF16)

    for group in range(groups):
        for copy in copies(group):
            copy.wait()
        products = moment_terms(blocks) if group > 0 else []
        work = [(inner, array) for inner in range(step) for array in range(2 + PARTS)]
        done = 0
        for number, (inner, array) in enumerate(work):
            put_in_order(group, inner, array)
            while done < len(products) and done * len(work) < (number + 1) * len(products):
                add_moments(moments, turned[group - 1], grads[group - 1], group == 1, products[done])
                done += 1
    if groups == 1:
        moments[...] = jnp.zeros_like(moments)


def reorder(pattern, basis, field, basis_grad, weights):
    batches, points, blocks, size = basis.shape
    rows = points * blocks
    step = 4 if batches % 4 == 0 else 1
    hbm = pl.BlockSpec(memory_space=pl.ANY)
    vmem = pl.BlockSpec(memory_space=pltpu.VMEM)
    ordered = jax.ShapeDtypeStruct((batches, blocks, points, size), BF16)
    turned = (blocks * size, step * points)
    grads = (PARTS, blocks, step * points, size)
    return pl.pallas_call(
        reorder_kernel,
        out_shape=(
            ordered,
            ordered,
            jax.ShapeDtypeStruct((PARTS, blocks * size, blocks * size), F32),
            jax.ShapeDtypeStruct(turned, BF16),
            jax.ShapeDtypeStruct(grads, BF16),
        ),
        in_specs=[hbm] * 5,
        out_specs=(vmem,) * 5,
        scratch_shapes=[
            pltpu.SMEM((blocks, batches), jnp.int32),
            pltpu.VMEM(weights.shape, F32),
            pltpu.VMEM((batches, rows, size), BF16),
            pltpu.VMEM((batches, rows, size), BF16),
            pltpu.VMEM((PARTS, batches, rows, size), BF16),
            pltpu.VMEM((2 + PARTS, rows, size), F32),
            pltpu.VMEM(turned, BF16),
            pltpu.VMEM(grads, BF16),
            pltpu.SemaphoreType.DMA((batches // step, 3)),
            pltpu.SemaphoreType.DMA((2,)),
        ],
        compiler_params=pltpu.CompilerParams(vmem_limit_bytes=VMEM_LIMIT),
        cost_estimate=pl.CostEstimate(
            flops=2 * PARTS * batches * points * (blocks * size) ** 2,
            bytes_accessed=2 * (2 + PARTS) * batches * rows * size,
            transcendentals=0,
        ),
    )(
        in_hbm(pattern.T),
        in_hbm(basis.reshape(batches, rows, size)),
        in_hbm(field.reshape(batches, rows, size)),
        in_hbm(basis_grad.reshape(PARTS, batches, rows, size)),
        in_hbm(weights),
    )


def moment_kernel(
    region, before, turned, grads, weight_grad, fn_atom, batch_atom, moments, hot, grad_columns
):
    blocks, _, size = grads.shape[1:]
    batches = weight_grad.shape[1]
    me = lax.axis_index("grid")
    atoms = lax.broadcasted_iota(jnp.int32, (hot.shape[0], size), 0)
    rows = [fn_atom[pl.ds(region[me, position], 1), :] for position in range(blocks)]
    rows.append(jnp.concatenate([batch_atom[...], jnp.full((1, size - batches), -1, jnp.int32)], axis=1))
    for number, ids in enumerate(rows):
        hot[:, number * size : (number + 1) * size] = jnp.where(atoms == ids, 1.0, 0.0).astype(BF16)
    for c in range(PARTS):
        padded = jnp.concatenate([weight_grad[c], jnp.zeros((size - batches, weight_grad.shape[2]), F32)], axis=0)
        grad_columns[c] = padded.T
    for term in moment_terms(blocks):
        add_moments(moments, turned, grads, False, term)


def moments_and_atoms(region, before, turned, grads, weight_grad, fn_atom, batch_atom, atom_total):
    blocks, depth, size = grads.shape[1:]
    points = weight_grad.shape[2]
    vmem = pl.BlockSpec(memory_space=pltpu.VMEM)
    return pl.pallas_call(
        moment_kernel,
        out_shape=(
            jax.ShapeDtypeStruct(before.shape, F32),
            jax.ShapeDtypeStruct((atom_total, (blocks + 1) * size), BF16),
            jax.ShapeDtypeStruct((PARTS, points, size), F32),
        ),
        in_specs=[pl.BlockSpec(memory_space=pltpu.SMEM)] + [vmem] * 6,
        out_specs=(vmem,) * 3,
        input_output_aliases={1: 0},
        compiler_params=pltpu.CompilerParams(vmem_limit_bytes=VMEM_LIMIT),
        cost_estimate=pl.CostEstimate(
            flops=2 * PARTS * depth * (blocks * size) ** 2, bytes_accessed=0, transcendentals=0
        ),
    )(region, before, turned, grads, weight_grad, fn_atom.reshape(-1, size), batch_atom.reshape(1, -1))


def combine_kernel(
    region, basis, field, moments, hot, grad_columns, *rest, owner_rows, slabs, width, step
):
    *pieces, product_out, out, stage, matrix, energies = rest
    batches, blocks, points, size = basis.shape
    me = lax.axis_index("grid")
    me_atoms = lax.axis_index("atoms")
    half = (width - 1) // 2
    stage_rows(stage, pieces[0], pieces[1:slabs], pieces[slabs:], SHARE)
    rows = [region[me, position] for position in range(blocks)]
    found = [owner_and_slot(region, me, position, owner_rows) for position in range(blocks)]
    totals = [[jnp.zeros((8, size), F32) for _ in range(blocks)] for _ in range(PARTS)]
    for p in range(blocks):
        owner, slot, count = found[p]
        first = jnp.bitwise_xor(me, owner) * TRAVEL
        for q in range(blocks):
            if abs(q - p) > half:
                matrix[p * size : (p + 1) * size, q * size : (q + 1) * size] = jnp.zeros((size, size), BF16)
                continue
            k = rows[q] - rows[p] + half
            place = jnp.where(
                k == 0,
                travel_place(slot, count, 0),
                jnp.where(k == 1, travel_place(slot, count, 1), travel_place(slot, count, 2)),
            )
            inside = jnp.logical_and(k >= 0, k < width)
            tile = stage[first + place].astype(F32)
            tile = jnp.where(inside, tile, 0.0)
            matrix[p * size : (p + 1) * size, q * size : (q + 1) * size] = tile.astype(BF16)
            turned = tile.T
            for c in range(PARTS):
                terms = turned * moments[c, q * size : (q + 1) * size, p * size : (p + 1) * size]
                totals[c][p] = totals[c][p] + jnp.sum(terms.reshape(-1, 8, size), axis=0)
    derivative = [
        jnp.concatenate([jnp.sum(total, axis=0, keepdims=True) for total in totals[c]], axis=1) for c in range(PARTS)
    ]

    energies[...] = jnp.zeros_like(energies)
    lanes = lax.broadcasted_iota(jnp.int32, (points, size), 1)

    @pl.loop(0, batches // step)
    def _(group):
        left = [
            jnp.concatenate([basis[group * step + inner, p] for p in range(blocks)], axis=1) for inner in range(step)
        ]
        product = jnp.dot(jnp.concatenate(left, axis=0), matrix[...], preferred_element_type=F32)
        for inner in range(step):
            batch = group * step + inner
            energy = jnp.zeros((points, size), F32)
            for q in range(blocks):
                part = product[inner * points : (inner + 1) * points, q * size : (q + 1) * size]
                product_out[batch, q] = part.astype(BF16)
                energy = energy + part * field[batch, q].astype(F32)
            energy = jnp.sum(energy, axis=1, keepdims=True)
            energies[...] = jnp.where(lanes == batch, energy, energies[...])

    lefts = []
    for c in range(PARTS):
        term = jnp.sum(energies[...] * grad_columns[c], axis=0, keepdims=True)
        lefts.append(jnp.concatenate([-2.0 * derivative[c], term], axis=1))
    left = jnp.concatenate(lefts, axis=0)
    high, middle, low = (piece.astype(F32) for piece in split(left))
    left = jnp.concatenate([high, middle, low, jnp.zeros((16 - 3 * PARTS, left.shape[1]), F32)], axis=0).astype(BF16)
    chunk = out.shape[-1]
    for device in range(out.shape[0]):
        sums = lax.dot_general(
            left, hot[device * chunk : (device + 1) * chunk, :], NT, preferred_element_type=F32
        )
        value = sums[:PARTS] + sums[PARTS : 2 * PARTS] + sums[2 * PARTS : 3 * PARTS]
        out[jnp.bitwise_xor(me_atoms, device)] = value


def combine(region, prepared, pieces, shapes):
    basis, field, moments, hot, grad_columns = prepared
    slabs, atom_devices, atom_total, points, blocks, width, owner_rows = shapes
    batches, _, _, size = basis.shape
    step = 4 if batches % 4 == 0 else 1
    vmem = pl.BlockSpec(memory_space=pltpu.VMEM)
    return pl.pallas_call(
        functools.partial(combine_kernel, owner_rows=owner_rows, slabs=slabs, width=width, step=step),
        out_shape=(
            jax.ShapeDtypeStruct(basis.shape, BF16),
            jax.ShapeDtypeStruct((atom_devices, PARTS, atom_total // atom_devices), F32),
        ),
        in_specs=[pl.BlockSpec(memory_space=pltpu.SMEM)] + [vmem] * (5 + len(pieces)),
        out_specs=(vmem, vmem),
        scratch_shapes=[
            pltpu.VMEM((slabs * TRAVEL, size, size), BF16),
            pltpu.VMEM((blocks * size, blocks * size), BF16),
            pltpu.VMEM((points, size), F32),
        ],
        compiler_params=pltpu.CompilerParams(vmem_limit_bytes=VMEM_LIMIT),
    )(region, basis, field, moments, hot, grad_columns, *pieces)


def write_kernel(pattern, product, out, wide, staged, sems):
    batches, blocks, points, size = product.shape

    def copy(batch):
        return pltpu.make_async_copy(staged.at[batch], out.at[batch], sems.at[batch])

    @pl.loop(0, batches // 2)
    def _(pair):
        for inner in range(2):
            batch = pair * 2 + inner
            for t in range(blocks):
                wide[inner, pl.ds(t, points, stride=blocks), :] = product[batch, pattern[t, batch]].astype(F32)
            staged[batch] = wide[inner].astype(BF16)
            copy(batch).start()

    @pl.loop(0, batches)
    def _(batch):
        copy(batch).wait()


def write(pattern, product):
    batches, blocks, points, size = product.shape
    shape = (batches, points * blocks, size)
    return pl.pallas_call(
        write_kernel,
        out_shape=jax.ShapeDtypeStruct(shape, BF16),
        in_specs=[pl.BlockSpec(memory_space=pltpu.SMEM), pl.BlockSpec(memory_space=pltpu.VMEM)],
        out_specs=pl.BlockSpec(memory_space=pl.ANY),
        scratch_shapes=[
            pltpu.VMEM((2, points * blocks, size), F32),
            pltpu.VMEM(shape, BF16),
            pltpu.SemaphoreType.DMA((batches,)),
        ],
        compiler_params=pltpu.CompilerParams(vmem_limit_bytes=VMEM_LIMIT),
        cost_estimate=pl.CostEstimate(flops=0, bytes_accessed=4 * math.prod(shape), transcendentals=0),
    )(pattern.T, product)


def swap_halves(near, ready, atom_devices):
    near, ready = lax.optimization_barrier((near, ready))
    swap = [(i, i ^ 1) for i in range(atom_devices)]
    return near, [lax.ppermute(piece, "atoms", swap) for piece in near], ready


def tree_sum(values):
    if len(values) == 1:
        return values[0]
    half = len(values) // 2
    return tree_sum(values[:half]) + tree_sum(values[half:])


def exchange_all(parts, axis, count):
    moved = {d: lax.ppermute(parts[d], axis, [(i, i ^ d) for i in range(count)]) for d in range(1, count)}
    return [parts[0]] + [moved[d] for d in range(1, count)]


def sum_parts(partial_grad, product, slabs, atom_devices):
    total = tree_sum(exchange_all([partial_grad[d] for d in range(atom_devices)], "atoms", atom_devices))
    total, product = lax.optimization_barrier((total, product))
    return tree_sum(exchange_all([total] * slabs, "grid", slabs)), product


def local(
    basis,
    basis_grad,
    exchange_field,
    weights,
    weight_grad,
    density,
    region,
    pattern,
    fn_atom,
    batch_atom,
):
    batches, points, blocks, size = basis.shape
    owner_rows, width = density.shape[:2]
    slabs = lax.axis_size("grid")
    atom_devices = lax.axis_size("atoms")
    atom_total = fn_atom.shape[0] // (10 * slabs * atom_devices) * slabs * atom_devices
    shapes = (slabs, atom_devices, atom_total, points, blocks, width, owner_rows)
    own, near = fetch_rows(region, density, slabs, SHARE)
    if region.shape[1] == blocks:
        ready = reorder(pattern, basis, exchange_field, basis_grad, weights)
        near, far, (basis_wide, field_wide, *partial) = swap_halves(near, ready, atom_devices)
        built = moments_and_atoms(region, *partial, weight_grad, fn_atom, batch_atom, atom_total)
        ready = (basis_wide, field_wide, *built)
        product, partial_grad = combine(region, ready, [own, *near, *far], shapes)
        gradient, product = sum_parts(partial_grad, product, slabs, atom_devices)
        contracted = write(pattern, product)
        return contracted.reshape(basis.shape), gradient
    ready = relayout(
        in_hbm(basis.reshape(batches, points * blocks, size)),
        in_hbm(exchange_field.reshape(batches, points * blocks, size)),
        points,
        blocks,
    )
    near, far, (basis_wide, field_wide) = swap_halves(near, ready, atom_devices)
    tiles, partial_grad = partial_gradient(
        region,
        pattern,
        basis_wide,
        field_wide,
        in_hbm(basis_grad.reshape(PARTS, batches, points * blocks, size)),
        weights,
        weight_grad,
        fn_atom,
        batch_atom,
        [own, *near, *far],
        shapes,
    )
    gradient, basis_wide = sum_parts(partial_grad, basis_wide, slabs, atom_devices)
    contracted = contract(region, pattern, basis_wide, tiles, points, blocks, width)
    return contracted.reshape(basis.shape), gradient


def solution(mesh):
    placed = (
        P(("groups", "grid", "atoms"), None, None, None),
        P(None, ("groups", "grid", "atoms"), None, None, None),
        P(("groups", "grid", "atoms"), None, None, None),
        P(("groups", "grid", "atoms"), None),
        P(None, ("groups", "grid", "atoms"), None),
        P(("groups", "grid"), None, None, None),
        P("groups", None),
        P(("groups", "grid", "atoms"), None),
        P("groups"),
        P(("groups", "grid", "atoms")),
    )
    return jax.shard_map(
        local,
        mesh=mesh,
        in_specs=placed,
        out_specs=(P(("groups", "grid", "atoms"), None, None, None), P(None, ("groups", "atoms"))),
        check_vma=False,
    )
```

```python
import functools
import math

import jax
import jax.numpy as jnp
from jax import lax
from jax.experimental import pallas as pl
from jax.experimental.pallas import tpu as pltpu
from jax.sharding import PartitionSpec as P

TRAVEL = 5
SHARE = 2
CHUNK = 2
PARTS = 3
F32 = jnp.float32
BF16 = jnp.bfloat16
NT = (((1,), (1,)), ((), ()))
VMEM_LIMIT = 32 * 1024 * 1024


def owner_and_slot(region, slab, position, owner_rows):
    owner = lax.div(region[slab, position], owner_rows)
    slot = jnp.int32(0)
    count = jnp.int32(0)
    for other in range(region.shape[1]):
        same = jnp.where(lax.div(region[slab, other], owner_rows) == owner, 1, 0)
        count = count + same
        if other < position:
            slot = slot + same
    return owner, slot, count


def travel_place(slot, count, k):
    if k == 0:
        return jnp.where(slot == 0, 4, 2)
    if k == 1:
        return jnp.where(slot == 0, 0, 3)
    return jnp.where(jnp.logical_and(slot == 0, count == 2), 1, 4)


def send_kernel(region_hbm, density, basis, field, basis_grad, *rest, share):
    *outs, first_basis, first_field, first_grad, region, sems, small_sems = rest
    fetches = (
        pltpu.make_async_copy(region_hbm, region, small_sems.at[0]),
        pltpu.make_async_copy(field.at[pl.ds(0, first_field.shape[0])], first_field, small_sems.at[1]),
        pltpu.make_async_copy(basis_grad.at[:, pl.ds(0, first_grad.shape[1])], first_grad, small_sems.at[2]),
        pltpu.make_async_copy(basis.at[pl.ds(0, first_basis.shape[0])], first_basis, small_sems.at[3]),
    )
    for copy in fetches:
        copy.start()
    fetches[0].wait()
    me = lax.axis_index("grid")
    part = lax.rem(lax.axis_index("atoms"), share)
    size = region.shape[1]
    owner_rows = density.shape[0]
    rows = density.shape[-2]
    copies = []
    for shift, out in zip((0, *reversed(range(1, len(outs)))), outs):
        slab = jnp.bitwise_xor(me, shift)
        base = jnp.int32(owner_rows)
        count = jnp.int32(0)
        for position in range(size):
            row = region[slab, position] - me * owner_rows
            mine = jnp.logical_and(row >= 0, row < owner_rows)
            base = jnp.minimum(base, jnp.where(mine, row, owner_rows))
            count = count + jnp.where(mine, 1, 0)
        base = jnp.where(count == 0, 0, base)
        after = jnp.minimum(base + 1, owner_rows - 1)
        lower = base == 0
        edge = jnp.where(jnp.logical_and(count == 2, jnp.logical_not(lower)), after, base)
        kept = out.shape[1]
        first = 0 if kept == rows else pl.multiple_of(part * kept, kept)
        here = pl.ds(first, kept)
        pairs = (
            (density.at[base, pl.ds(1, 2), here, :], out.at[pl.ds(0, 2)]),
            (density.at[after, pl.ds(0, 2), here, :], out.at[pl.ds(2, 2)]),
            (density.at[edge, jnp.where(lower, 0, 2), here, :], out.at[4]),
        )
        for number, (source, target) in enumerate(pairs):
            copies.append(pltpu.make_async_copy(source, target, sems.at[shift, number]))
    for copy in copies:
        copy.start()
    for copy in (*copies, *fetches[1:]):
        copy.wait()


def in_hbm(array):
    return pltpu.with_memory_space_constraint(array, pltpu.HBM)


def rows_to_send(region, density, basis, field, basis_grad, slabs, share):
    size = density.shape[-1]
    kept = [size] + [size // share] * (slabs - 1)
    first = jax.ShapeDtypeStruct((CHUNK, *basis.shape[1:]), BF16)
    first_grad = jax.ShapeDtypeStruct((PARTS, CHUNK, *basis.shape[1:]), BF16)
    hbm = pl.BlockSpec(memory_space=pl.ANY)
    return pl.pallas_call(
        functools.partial(send_kernel, share=share),
        out_shape=[
            *(jax.ShapeDtypeStruct((TRAVEL, rows, size), density.dtype) for rows in kept),
            first,
            first,
            first_grad,
        ],
        in_specs=[hbm] * 5,
        out_specs=[pl.BlockSpec(memory_space=pltpu.VMEM)] * (slabs + 3),
        scratch_shapes=[
            pltpu.SMEM(region.shape, jnp.int32),
            pltpu.SemaphoreType.DMA((slabs, 3)),
            pltpu.SemaphoreType.DMA((4,)),
        ],
        compiler_params=pltpu.CompilerParams(vmem_limit_bytes=VMEM_LIMIT),
    )(in_hbm(region), in_hbm(density), in_hbm(basis), in_hbm(field), in_hbm(basis_grad))


def fetch_rows(region, density, basis, field, basis_grad, slabs, share):
    own, *rest = rows_to_send(region, density, basis, field, basis_grad, slabs, share)
    outgoing, first = rest[: slabs - 1], rest[slabs - 1 :]
    near = {}
    for shift in reversed(range(1, slabs)):
        near[shift] = lax.ppermute(outgoing[slabs - 1 - shift], "grid", [(i, i ^ shift) for i in range(slabs)])
    return own, [near[shift] for shift in range(1, slabs)], first


def stage_rows(stage, own, near, far, share):
    part = lax.rem(lax.axis_index("atoms"), share)
    kept = near[0].shape[1]
    for place in range(TRAVEL):
        stage[place] = own[place]
        for shift, (here, there) in enumerate(zip(near, far), 1):
            stage[shift * TRAVEL + place, pl.ds(pl.multiple_of(part * kept, kept), kept), :] = here[place]
            stage[shift * TRAVEL + place, pl.ds(pl.multiple_of((1 - part) * kept, kept), kept), :] = there[place]


def block_major(x_ref, wide, points, blocks):
    wide[...] = x_ref[0].astype(F32)
    return [wide[pl.ds(s, points, stride=blocks), :] for s in range(blocks)]


def relayout_kernel(basis, field, basis_out, field_out, wide, *, points, blocks):
    size = basis.shape[-1]
    for source, target in ((basis, basis_out), (field, field_out)):
        for s, part in enumerate(block_major(source, wide, points, blocks)):
            target[0, :, s * size : (s + 1) * size] = part.astype(BF16)


def relayout(basis, field, points, blocks):
    batches, rows, size = basis.shape
    here = pl.BlockSpec((1, rows, size), lambda b: (b, 0, 0))
    there = pl.BlockSpec((1, points, blocks * size), lambda b: (b, 0, 0))
    shape = jax.ShapeDtypeStruct((batches, points, blocks * size), BF16)
    return pl.pallas_call(
        functools.partial(relayout_kernel, points=points, blocks=blocks),
        grid=(batches,),
        out_shape=(shape, shape),
        in_specs=[here, here],
        out_specs=(there, there),
        scratch_shapes=[pltpu.VMEM((rows, size), F32)],
        compiler_params=pltpu.CompilerParams(vmem_limit_bytes=VMEM_LIMIT),
        cost_estimate=pl.CostEstimate(flops=0, bytes_accessed=8 * batches * rows * size, transcendentals=0),
    )(basis, field)


def batch_matrix(region, pattern, tiles, slab, batch, blocks, width):
    half = (width - 1) // 2
    none = tiles.shape[0] - 1
    places = [pattern[batch, s] for s in range(blocks)]
    rows = [region[slab, place] for place in places]
    strips = []
    for s in range(blocks):
        strip = []
        for t in range(blocks):
            k = rows[t] - rows[s] + half
            inside = jnp.logical_and(k >= 0, k < width)
            strip.append(tiles[jnp.where(inside, places[s] * width + k, none)])
        strips.append(jnp.concatenate(strip, axis=1))
    return jnp.concatenate(strips, axis=0)


def split(values):
    high = values.astype(BF16)
    rest = values - high.astype(F32)
    middle = rest.astype(BF16)
    low = (rest - middle.astype(F32)).astype(BF16)
    return high, middle, low


def gradient_kernel(
    region,
    pattern,
    basis,
    field,
    basis_grad,
    weights,
    weight_grad,
    fn_atom,
    batch_atom,
    places,
    *rest,
    points,
    blocks,
    width,
    owner_rows,
    slabs,
):
    *pieces, tiles, out, stage, spread, sums, energy_sums = rest
    batch = pl.program_id(0)
    batches = pl.num_programs(0)
    me = lax.axis_index("grid")
    me_atoms = lax.axis_index("atoms")
    size = tiles.shape[-1]
    region_size = region.shape[1]

    @pl.when(batch == 0)
    def _():
        tiles[region_size * width] = jnp.zeros((size, size), BF16)
        stage_rows(stage, pieces[0], pieces[1:slabs], pieces[slabs:], SHARE)
        for position in range(region_size):
            owner, slot, count = owner_and_slot(region, me, position, owner_rows)
            shift = jnp.bitwise_xor(me, owner)
            for k in range(width):
                tiles[position * width + k] = stage[shift * TRAVEL + travel_place(slot, count, k)]

    matrix = batch_matrix(region, pattern, tiles, me, batch, blocks, width)
    potential = lax.dot_general(field[0], matrix, NT, preferred_element_type=F32)
    rows = jnp.concatenate(
        [weights[pl.ds(batch, 1), :]]
        + [weight_grad[c, pl.ds(batch, 1), :] for c in range(PARTS)]
        + [jnp.zeros((8 - 1 - PARTS, points), F32)],
        axis=0,
    )
    columns = rows.T
    weight = columns[:, 0:1]
    energy = jnp.zeros((points, size), F32)
    for s in range(blocks):
        here = potential[:, s * size : (s + 1) * size]
        energy = energy + basis[0, :, s * size : (s + 1) * size].astype(F32) * here
        spread[pl.ds(s, points, stride=blocks), :] = here * weight
    scaled = spread[...]
    place = pl.ds(pl.multiple_of(batch * 8, 8), 8)
    for c in range(PARTS):
        terms = basis_grad[c, 0].astype(F32) * scaled
        sums[c, place, :] = jnp.sum(terms.reshape(-1, 8, size), axis=0)
        terms = energy * columns[:, 1 + c : 2 + c]
        energy_sums[c, place, :] = jnp.sum(terms.reshape(-1, 8, size), axis=0)

    @pl.when(batch == batches - 1)
    def _():
        padded = max(8, region_size)
        chosen = lax.broadcasted_iota(jnp.int32, (padded, places.shape[1]), 0) == places[...]
        chosen = chosen.astype(BF16)
        blocks_sum = []
        for c in range(PARTS):
            total = jnp.zeros((padded, size), F32)
            for piece in split(sums[c]):
                total = total + jnp.dot(chosen, piece, preferred_element_type=F32)
            blocks_sum.append(-2.0 * total)
        lefts = []
        for position in range(region_size):
            stack = jnp.concatenate([total[position : position + 1] for total in blocks_sum], axis=0)
            high, middle, low = (piece.astype(F32) for piece in split(stack))
            lefts.append(jnp.concatenate([high, middle, low, jnp.zeros((16 - 3 * PARTS, size), F32)], axis=0))
        left = jnp.concatenate(lefts, axis=1).astype(BF16)
        chunk = out.shape[-1]
        scale = [jnp.sum(energy_sums[c], axis=1, keepdims=True) for c in range(PARTS)]
        for device in range(out.shape[0]):
            atoms = lax.broadcasted_iota(jnp.int32, (chunk, size), 0) + device * chunk
            hot = [
                jnp.where(atoms == fn_atom[pl.ds(region[me, position], 1), :], 1.0, 0.0).astype(BF16)
                for position in range(region_size)
            ]
            found = lax.dot_general(left, jnp.concatenate(hot, axis=1), NT, preferred_element_type=F32)
            atoms = lax.broadcasted_iota(jnp.int32, (batch_atom.shape[0], chunk), 1) + device * chunk
            mine = atoms == batch_atom[...]
            for c in range(PARTS):
                value = found[c : c + 1] + found[PARTS + c : PARTS + c + 1] + found[2 * PARTS + c : 2 * PARTS + c + 1]
                value = value + jnp.sum(jnp.where(mine, scale[c], 0.0), axis=0, keepdims=True)
                out[jnp.bitwise_xor(me_atoms, device), c : c + 1, :] = value


def partial_gradient(
    region, pattern, basis, field, basis_grad, weights, weight_grad, fn_atom, batch_atom, pieces, shapes
):
    slabs, atom_devices, atom_total, points, blocks, width, owner_rows = shapes
    batches, _, columns = basis.shape
    size = columns // blocks
    region_size = region.shape[1]
    fn_atom = fn_atom.reshape(-1, size)
    places = jnp.broadcast_to(pattern[:, None, :], (batches, 8 // blocks, blocks)).reshape(1, -1)
    batch_atom = jnp.broadcast_to(batch_atom[:, None], (batches, 8)).reshape(-1, 1)
    block = pl.BlockSpec((1, points, columns), lambda b, *_: (b, 0, 0))
    whole = pl.BlockSpec(memory_space=pltpu.VMEM)
    tile_shape = (region_size * width + 1, size, size)
    out_shape = (atom_devices, PARTS, atom_total // atom_devices)
    return pl.pallas_call(
        functools.partial(
            gradient_kernel, points=points, blocks=blocks, width=width, owner_rows=owner_rows, slabs=slabs
        ),
        grid_spec=pltpu.PrefetchScalarGridSpec(
            num_scalar_prefetch=2,
            grid=(batches,),
            in_specs=[
                block,
                block,
                pl.BlockSpec((PARTS, 1, points * blocks, size), lambda b, *_: (0, b, 0, 0)),
            ]
            + [whole] * (5 + len(pieces)),
            out_specs=(whole, whole),
            scratch_shapes=[
                pltpu.VMEM((slabs * TRAVEL, size, size), BF16),
                pltpu.VMEM((points * blocks, size), F32),
                pltpu.VMEM((PARTS, batches * 8, size), F32),
                pltpu.VMEM((PARTS, batches * 8, size), F32),
            ],
        ),
        out_shape=(jax.ShapeDtypeStruct(tile_shape, BF16), jax.ShapeDtypeStruct(out_shape, F32)),
        compiler_params=pltpu.CompilerParams(vmem_limit_bytes=VMEM_LIMIT),
    )(region, pattern, basis, field, basis_grad, weights, weight_grad, fn_atom, batch_atom, places, *pieces)


def product_kernel(region, pattern, basis, tiles, out, spread, *, points, blocks, width):
    me = lax.axis_index("grid")
    size = tiles.shape[-1]
    matrix = batch_matrix(region, pattern, tiles, me, pl.program_id(0), blocks, width)
    product = jnp.dot(basis[0], matrix, preferred_element_type=F32)
    for t in range(blocks):
        spread[pl.ds(t, points, stride=blocks), :] = product[:, t * size : (t + 1) * size]
    out[0] = spread[...].astype(BF16)


def contract(region, pattern, basis, tiles, points, blocks, width):
    batches, _, columns = basis.shape
    size = columns // blocks
    return pl.pallas_call(
        functools.partial(product_kernel, points=points, blocks=blocks, width=width),
        grid_spec=pltpu.PrefetchScalarGridSpec(
            num_scalar_prefetch=2,
            grid=(batches,),
            in_specs=[
                pl.BlockSpec((1, points, columns), lambda b, *_: (b, 0, 0)),
                pl.BlockSpec(memory_space=pltpu.VMEM),
            ],
            out_specs=pl.BlockSpec((1, points * blocks, size), lambda b, *_: (b, 0, 0)),
            scratch_shapes=[pltpu.VMEM((points * blocks, size), F32)],
        ),
        out_shape=jax.ShapeDtypeStruct((batches, points * blocks, size), BF16),
        compiler_params=pltpu.CompilerParams(vmem_limit_bytes=VMEM_LIMIT),
        cost_estimate=pl.CostEstimate(
            flops=2 * batches * points * columns * columns,
            bytes_accessed=4 * batches * points * columns,
            transcendentals=0,
        ),
    )(region, pattern, basis, tiles)


def moment_terms(blocks):
    return [(c, p) for c in range(PARTS) for p in range(0, blocks, 2)]


def add_moments(moments, turned, grads, fresh, term):
    c, p = term
    blocks, _, size = grads.shape[1:]
    rows = slice(max(p - 1, 0) * size, min(p + 3, blocks) * size)
    columns = slice(p * size, min(p + 2, blocks) * size)
    right = jnp.concatenate([grads[c, place] for place in range(p, min(p + 2, blocks))], axis=1)
    value = jnp.dot(turned[rows, :], right, preferred_element_type=F32)
    moments[c, rows, columns] = value if fresh else moments[c, rows, columns] + value


def reorder_kernel(
    pattern_hbm,
    basis,
    field,
    basis_grad,
    weights_hbm,
    first_basis,
    first_field,
    first_grad,
    basis_out,
    field_out,
    moments,
    last_turned,
    last_grads,
    pattern,
    weights,
    basis_in,
    field_in,
    grad_in,
    wide,
    turned,
    grads,
    sems,
    small_sems,
):
    batches, blocks, points, size = basis_out.shape
    step = last_turned.shape[1] // points
    groups = batches // step
    turned = [last_turned if (groups - 1 - group) % 2 == 0 else turned for group in range(groups)]
    grads = [last_grads if (groups - 1 - group) % 2 == 0 else grads for group in range(groups)]

    def copies(chunk):
        here = pl.ds(chunk * CHUNK, CHUNK)
        pairs = [(field.at[here], field_in.at[here]), (basis.at[here], basis_in.at[here])]
        pairs += [(basis_grad.at[c, here], grad_in.at[c, here]) for c in range(PARTS)]
        return [
            pltpu.make_async_copy(source, target, sems.at[chunk, number])
            for number, (source, target) in enumerate(pairs)
        ]

    small = (
        pltpu.make_async_copy(pattern_hbm, pattern, small_sems.at[0]),
        pltpu.make_async_copy(weights_hbm, weights, small_sems.at[1]),
    )
    for copy in small:
        copy.start()
    for chunk in range(1, batches // CHUNK):
        for copy in copies(chunk):
            copy.start()
    for copy in small:
        copy.wait()
    diagonal = lax.broadcasted_iota(jnp.int32, (size, size), 0) == lax.broadcasted_iota(jnp.int32, (size, size), 1)
    identity = jnp.where(diagonal, 1.0, 0.0).astype(BF16)

    for group in range(groups):
        for inner in range(step):
            batch = group * step + inner
            if batch >= CHUNK and batch % CHUNK == 0:
                for copy in copies(batch // CHUNK):
                    copy.wait()
            if batch < CHUNK:
                sources = [first_field.at[batch], first_basis.at[batch]] + [first_grad.at[c, batch] for c in range(PARTS)]
            else:
                sources = [field_in.at[batch], basis_in.at[batch]] + [grad_in.at[c, batch] for c in range(PARTS)]
            points_here = slice(inner * points, (inner + 1) * points)
            places = [pattern[s, batch] for s in range(blocks)]
            weight = weights[batch : batch + 1, :]
            for array, source in enumerate(sources):
                wide[array] = source[...].astype(F32)
            values = [
                [wide[array, pl.ds(s, points, stride=blocks), :].astype(BF16) for s in range(blocks)]
                for array in range(2 + PARTS)
            ]
            across = lax.dot_general(identity, jnp.concatenate(values[0], axis=0), NT, preferred_element_type=F32)
            for s, place in enumerate(places):
                field_out[batch, place] = values[0][s]
                rows = pl.ds(pl.multiple_of(place * size, size), size)
                turned[group][rows, points_here] = (across[:, s * points : (s + 1) * points] * weight).astype(BF16)
                basis_out[batch, place] = values[1][s]
                for c in range(PARTS):
                    grads[group][c, place, points_here, :] = values[2 + c][s]
        if group > 0:
            for term in moment_terms(blocks):
                add_moments(moments, turned[group - 1], grads[group - 1], group == 1, term)
    if groups == 1:
        moments[...] = jnp.zeros_like(moments)


def reorder(pattern, basis, field, basis_grad, weights, first, points, blocks):
    batches, rows, size = basis.shape
    step = 4 if batches % 4 == 0 else CHUNK
    hbm = pl.BlockSpec(memory_space=pl.ANY)
    vmem = pl.BlockSpec(memory_space=pltpu.VMEM)
    ordered = jax.ShapeDtypeStruct((batches, blocks, points, size), BF16)
    turned = (blocks * size, step * points)
    grads = (PARTS, blocks, step * points, size)
    return pl.pallas_call(
        reorder_kernel,
        out_shape=(
            ordered,
            ordered,
            jax.ShapeDtypeStruct((PARTS, blocks * size, blocks * size), F32),
            jax.ShapeDtypeStruct(turned, BF16),
            jax.ShapeDtypeStruct(grads, BF16),
        ),
        in_specs=[hbm] * 5 + [vmem] * 3,
        out_specs=(vmem,) * 5,
        scratch_shapes=[
            pltpu.SMEM((blocks, batches), jnp.int32),
            pltpu.VMEM(weights.shape, F32),
            pltpu.VMEM((batches, rows, size), BF16),
            pltpu.VMEM((batches, rows, size), BF16),
            pltpu.VMEM((PARTS, batches, rows, size), BF16),
            pltpu.VMEM((2 + PARTS, rows, size), F32),
            pltpu.VMEM(turned, BF16),
            pltpu.VMEM(grads, BF16),
            pltpu.SemaphoreType.DMA((batches // CHUNK, 2 + PARTS)),
            pltpu.SemaphoreType.DMA((2,)),
        ],
        compiler_params=pltpu.CompilerParams(vmem_limit_bytes=VMEM_LIMIT),
        cost_estimate=pl.CostEstimate(
            flops=2 * PARTS * batches * points * (blocks * size) ** 2,
            bytes_accessed=2 * (2 + PARTS) * batches * rows * size,
            transcendentals=0,
        ),
    )(in_hbm(pattern.T), in_hbm(basis), in_hbm(field), in_hbm(basis_grad), in_hbm(weights), *first)


def moment_kernel(
    region, before, turned, grads, weight_grad, fn_atom, batch_atom, moments, hot, grad_columns
):
    blocks, _, size = grads.shape[1:]
    batches = weight_grad.shape[1]
    me = lax.axis_index("grid")
    atoms = lax.broadcasted_iota(jnp.int32, (hot.shape[0], size), 0)
    rows = [fn_atom[pl.ds(region[me, position], 1), :] for position in range(blocks)]
    rows.append(jnp.concatenate([batch_atom[...], jnp.full((1, size - batches), -1, jnp.int32)], axis=1))
    for number, ids in enumerate(rows):
        hot[:, number * size : (number + 1) * size] = jnp.where(atoms == ids, 1.0, 0.0).astype(BF16)
    for c in range(PARTS):
        padded = jnp.concatenate([weight_grad[c], jnp.zeros((size - batches, weight_grad.shape[2]), F32)], axis=0)
        grad_columns[c] = padded.T
    for term in moment_terms(blocks):
        add_moments(moments, turned, grads, False, term)


def moments_and_atoms(region, before, turned, grads, weight_grad, fn_atom, batch_atom, atom_total):
    blocks, depth, size = grads.shape[1:]
    points = weight_grad.shape[2]
    vmem = pl.BlockSpec(memory_space=pltpu.VMEM)
    return pl.pallas_call(
        moment_kernel,
        out_shape=(
            jax.ShapeDtypeStruct(before.shape, F32),
            jax.ShapeDtypeStruct((atom_total, (blocks + 1) * size), BF16),
            jax.ShapeDtypeStruct((PARTS, points, size), F32),
        ),
        in_specs=[pl.BlockSpec(memory_space=pltpu.SMEM)] + [vmem] * 6,
        out_specs=(vmem,) * 3,
        input_output_aliases={1: 0},
        compiler_params=pltpu.CompilerParams(vmem_limit_bytes=VMEM_LIMIT),
        cost_estimate=pl.CostEstimate(
            flops=2 * PARTS * depth * (blocks * size) ** 2, bytes_accessed=0, transcendentals=0
        ),
    )(region, before, turned, grads, weight_grad, fn_atom.reshape(-1, size), batch_atom.reshape(1, -1))


def combine_kernel(
    region, basis, field, moments, hot, grad_columns, *rest, owner_rows, slabs, width, step
):
    *pieces, product_out, out, stage, matrix, energies = rest
    batches, blocks, points, size = basis.shape
    me = lax.axis_index("grid")
    me_atoms = lax.axis_index("atoms")
    half = (width - 1) // 2
    stage_rows(stage, pieces[0], pieces[1:slabs], pieces[slabs:], SHARE)
    rows = [region[me, position] for position in range(blocks)]
    found = [owner_and_slot(region, me, position, owner_rows) for position in range(blocks)]
    totals = [[jnp.zeros((8, size), F32) for _ in range(blocks)] for _ in range(PARTS)]
    for p in range(blocks):
        owner, slot, count = found[p]
        first = jnp.bitwise_xor(me, owner) * TRAVEL
        for q in range(blocks):
            if abs(q - p) > half:
                matrix[p * size : (p + 1) * size, q * size : (q + 1) * size] = jnp.zeros((size, size), BF16)
                continue
            k = rows[q] - rows[p] + half
            place = jnp.where(
                k == 0,
                travel_place(slot, count, 0),
                jnp.where(k == 1, travel_place(slot, count, 1), travel_place(slot, count, 2)),
            )
            inside = jnp.logical_and(k >= 0, k < width)
            tile = stage[first + place].astype(F32)
            tile = jnp.where(inside, tile, 0.0)
            matrix[p * size : (p + 1) * size, q * size : (q + 1) * size] = tile.astype(BF16)
            turned = tile.T
            for c in range(PARTS):
                terms = turned * moments[c, q * size : (q + 1) * size, p * size : (p + 1) * size]
                totals[c][p] = totals[c][p] + jnp.sum(terms.reshape(-1, 8, size), axis=0)
    derivative = [
        jnp.concatenate([jnp.sum(total, axis=0, keepdims=True) for total in totals[c]], axis=1) for c in range(PARTS)
    ]

    energies[...] = jnp.zeros_like(energies)
    lanes = lax.broadcasted_iota(jnp.int32, (points, size), 1)

    @pl.loop(0, batches // step)
    def _(group):
        left = [
            jnp.concatenate([basis[group * step + inner, p] for p in range(blocks)], axis=1) for inner in range(step)
        ]
        product = jnp.dot(jnp.concatenate(left, axis=0), matrix[...], preferred_element_type=F32)
        for inner in range(step):
            batch = group * step + inner
            energy = jnp.zeros((points, size), F32)
            for q in range(blocks):
                part = product[inner * points : (inner + 1) * points, q * size : (q + 1) * size]
                product_out[batch, q] = part.astype(BF16)
                energy = energy + part * field[batch, q].astype(F32)
            energy = jnp.sum(energy, axis=1, keepdims=True)
            energies[...] = jnp.where(lanes == batch, energy, energies[...])

    lefts = []
    for c in range(PARTS):
        term = jnp.sum(energies[...] * grad_columns[c], axis=0, keepdims=True)
        lefts.append(jnp.concatenate([-2.0 * derivative[c], term], axis=1))
    left = jnp.concatenate(lefts, axis=0)
    high, middle, low = (piece.astype(F32) for piece in split(left))
    left = jnp.concatenate([high, middle, low, jnp.zeros((16 - 3 * PARTS, left.shape[1]), F32)], axis=0).astype(BF16)
    chunk = out.shape[-1]
    for device in range(out.shape[0]):
        sums = lax.dot_general(
            left, hot[device * chunk : (device + 1) * chunk, :], NT, preferred_element_type=F32
        )
        value = sums[:PARTS] + sums[PARTS : 2 * PARTS] + sums[2 * PARTS : 3 * PARTS]
        out[jnp.bitwise_xor(me_atoms, device)] = value


def combine(region, prepared, pieces, shapes):
    basis, field, moments, hot, grad_columns = prepared
    slabs, atom_devices, atom_total, points, blocks, width, owner_rows = shapes
    batches, _, _, size = basis.shape
    step = 4 if batches % 4 == 0 else 1
    vmem = pl.BlockSpec(memory_space=pltpu.VMEM)
    return pl.pallas_call(
        functools.partial(combine_kernel, owner_rows=owner_rows, slabs=slabs, width=width, step=step),
        out_shape=(
            jax.ShapeDtypeStruct(basis.shape, BF16),
            jax.ShapeDtypeStruct((atom_devices, PARTS, atom_total // atom_devices), F32),
        ),
        in_specs=[pl.BlockSpec(memory_space=pltpu.SMEM)] + [vmem] * (5 + len(pieces)),
        out_specs=(vmem, vmem),
        scratch_shapes=[
            pltpu.VMEM((slabs * TRAVEL, size, size), BF16),
            pltpu.VMEM((blocks * size, blocks * size), BF16),
            pltpu.VMEM((points, size), F32),
        ],
        compiler_params=pltpu.CompilerParams(vmem_limit_bytes=VMEM_LIMIT),
    )(region, basis, field, moments, hot, grad_columns, *pieces)


def write_kernel(pattern, product, out, wide, staged, sems):
    batches, blocks, points, size = product.shape

    def copy(batch):
        return pltpu.make_async_copy(staged.at[batch], out.at[batch], sems.at[batch])

    @pl.loop(0, batches // 2)
    def _(pair):
        for inner in range(2):
            batch = pair * 2 + inner
            for t in range(blocks):
                wide[inner, pl.ds(t, points, stride=blocks), :] = product[batch, pattern[t, batch]].astype(F32)
            staged[batch] = wide[inner].astype(BF16)
            copy(batch).start()

    @pl.loop(0, batches)
    def _(batch):
        copy(batch).wait()


def write(pattern, product):
    batches, blocks, points, size = product.shape
    shape = (batches, points * blocks, size)
    return pl.pallas_call(
        write_kernel,
        out_shape=jax.ShapeDtypeStruct(shape, BF16),
        in_specs=[pl.BlockSpec(memory_space=pltpu.SMEM), pl.BlockSpec(memory_space=pltpu.VMEM)],
        out_specs=pl.BlockSpec(memory_space=pl.ANY),
        scratch_shapes=[
            pltpu.VMEM((2, points * blocks, size), F32),
            pltpu.VMEM(shape, BF16),
            pltpu.SemaphoreType.DMA((batches,)),
        ],
        compiler_params=pltpu.CompilerParams(vmem_limit_bytes=VMEM_LIMIT),
        cost_estimate=pl.CostEstimate(flops=0, bytes_accessed=4 * math.prod(shape), transcendentals=0),
    )(pattern.T, product)


def swap_halves(near, ready, atom_devices):
    near, ready = lax.optimization_barrier((near, ready))
    swap = [(i, i ^ 1) for i in range(atom_devices)]
    return near, [lax.ppermute(piece, "atoms", swap) for piece in near], ready


def tree_sum(values):
    if len(values) == 1:
        return values[0]
    half = len(values) // 2
    return tree_sum(values[:half]) + tree_sum(values[half:])


def exchange_all(parts, axis, count):
    moved = {d: lax.ppermute(parts[d], axis, [(i, i ^ d) for i in range(count)]) for d in range(1, count)}
    return [parts[0]] + [moved[d] for d in range(1, count)]


def sum_parts(partial_grad, product, slabs, atom_devices):
    total = tree_sum(exchange_all([partial_grad[d] for d in range(atom_devices)], "atoms", atom_devices))
    total, product = lax.optimization_barrier((total, product))
    return tree_sum(exchange_all([total] * slabs, "grid", slabs)), product


def local(
    basis,
    basis_grad,
    exchange_field,
    weights,
    weight_grad,
    density,
    region,
    pattern,
    fn_atom,
    batch_atom,
):
    batches, points, blocks, size = basis.shape
    owner_rows, width = density.shape[:2]
    slabs = lax.axis_size("grid")
    atom_devices = lax.axis_size("atoms")
    atom_total = fn_atom.shape[0] // (10 * slabs * atom_devices) * slabs * atom_devices
    shapes = (slabs, atom_devices, atom_total, points, blocks, width, owner_rows)
    flat_basis = basis.reshape(batches, points * blocks, size)
    flat_field = exchange_field.reshape(batches, points * blocks, size)
    flat_grad = basis_grad.reshape(PARTS, batches, points * blocks, size)
    own, near, first = fetch_rows(region, density, flat_basis, flat_field, flat_grad, slabs, SHARE)
    if region.shape[1] == blocks:
        ready = reorder(pattern, flat_basis, flat_field, flat_grad, weights, first, points, blocks)
        near, far, (basis_wide, field_wide, *partial) = swap_halves(near, ready, atom_devices)
        built = moments_and_atoms(region, *partial, weight_grad, fn_atom, batch_atom, atom_total)
        ready = (basis_wide, field_wide, *built)
        product, partial_grad = combine(region, ready, [own, *near, *far], shapes)
        gradient, product = sum_parts(partial_grad, product, slabs, atom_devices)
        contracted = write(pattern, product)
        return contracted.reshape(basis.shape), gradient
    ready = relayout(in_hbm(flat_basis), in_hbm(flat_field), points, blocks)
    near, far, (basis_wide, field_wide) = swap_halves(near, ready, atom_devices)
    tiles, partial_grad = partial_gradient(
        region,
        pattern,
        basis_wide,
        field_wide,
        in_hbm(flat_grad),
        weights,
        weight_grad,
        fn_atom,
        batch_atom,
        [own, *near, *far],
        shapes,
    )
    gradient, basis_wide = sum_parts(partial_grad, basis_wide, slabs, atom_devices)
    contracted = contract(region, pattern, basis_wide, tiles, points, blocks, width)
    return contracted.reshape(basis.shape), gradient


def solution(mesh):
    placed = (
        P(("groups", "grid", "atoms"), None, None, None),
        P(None, ("groups", "grid", "atoms"), None, None, None),
        P(("groups", "grid", "atoms"), None, None, None),
        P(("groups", "grid", "atoms"), None),
        P(None, ("groups", "grid", "atoms"), None),
        P(("groups", "grid"), None, None, None),
        P("groups", None),
        P(("groups", "grid", "atoms"), None),
        P("groups"),
        P(("groups", "grid", "atoms")),
    )
    return jax.shard_map(
        local,
        mesh=mesh,
        in_specs=placed,
        out_specs=(P(("groups", "grid", "atoms"), None, None, None), P(None, ("groups", "atoms"))),
        check_vma=False,
    )
```

```python
import functools
import math

import jax
import jax.numpy as jnp
from jax import lax
from jax.experimental import pallas as pl
from jax.experimental.pallas import tpu as pltpu
from jax.sharding import PartitionSpec as P

TRAVEL = 5
SHARE = 2
CHUNK = 2
PARTS = 3
F32 = jnp.float32
BF16 = jnp.bfloat16
NT = (((1,), (1,)), ((), ()))
VMEM_LIMIT = 32 * 1024 * 1024


def owner_and_slot(region, slab, position, owner_rows):
    owner = lax.div(region[slab, position], owner_rows)
    slot = jnp.int32(0)
    count = jnp.int32(0)
    for other in range(region.shape[1]):
        same = jnp.where(lax.div(region[slab, other], owner_rows) == owner, 1, 0)
        count = count + same
        if other < position:
            slot = slot + same
    return owner, slot, count


def travel_place(slot, count, k):
    if k == 0:
        return jnp.where(slot == 0, 4, 2)
    if k == 1:
        return jnp.where(slot == 0, 0, 3)
    return jnp.where(jnp.logical_and(slot == 0, count == 2), 1, 4)


def send_kernel(region_hbm, density, basis, field, basis_grad, *rest, share):
    *outs, first_basis, first_field, first_grad, region, sems, small_sems = rest
    fetches = (
        pltpu.make_async_copy(region_hbm, region, small_sems.at[0]),
        pltpu.make_async_copy(field.at[pl.ds(0, first_field.shape[0])], first_field, small_sems.at[1]),
        pltpu.make_async_copy(basis_grad.at[:, pl.ds(0, first_grad.shape[1])], first_grad, small_sems.at[2]),
        pltpu.make_async_copy(basis.at[pl.ds(0, first_basis.shape[0])], first_basis, small_sems.at[3]),
    )
    for copy in fetches:
        copy.start()
    fetches[0].wait()
    me = lax.axis_index("grid")
    part = lax.rem(lax.axis_index("atoms"), share)
    size = region.shape[1]
    owner_rows = density.shape[0]
    rows = density.shape[-2]
    copies = []
    for shift, out in zip((0, *reversed(range(1, len(outs)))), outs):
        slab = jnp.bitwise_xor(me, shift)
        base = jnp.int32(owner_rows)
        count = jnp.int32(0)
        for position in range(size):
            row = region[slab, position] - me * owner_rows
            mine = jnp.logical_and(row >= 0, row < owner_rows)
            base = jnp.minimum(base, jnp.where(mine, row, owner_rows))
            count = count + jnp.where(mine, 1, 0)
        base = jnp.where(count == 0, 0, base)
        after = jnp.minimum(base + 1, owner_rows - 1)
        lower = base == 0
        edge = jnp.where(jnp.logical_and(count == 2, jnp.logical_not(lower)), after, base)
        kept = out.shape[1]
        first = 0 if kept == rows else pl.multiple_of(part * kept, kept)
        here = pl.ds(first, kept)
        pairs = (
            (density.at[base, pl.ds(1, 2), here, :], out.at[pl.ds(0, 2)]),
            (density.at[after, pl.ds(0, 2), here, :], out.at[pl.ds(2, 2)]),
            (density.at[edge, jnp.where(lower, 0, 2), here, :], out.at[4]),
        )
        for number, (source, target) in enumerate(pairs):
            copies.append(pltpu.make_async_copy(source, target, sems.at[shift, number]))
    for copy in copies:
        copy.start()
    for copy in (*copies, *fetches[1:]):
        copy.wait()


def in_hbm(array):
    return pltpu.with_memory_space_constraint(array, pltpu.HBM)


def rows_to_send(region, density, basis, field, basis_grad, slabs, share):
    size = density.shape[-1]
    kept = [size] + [size // share] * (slabs - 1)
    first = jax.ShapeDtypeStruct((CHUNK, *basis.shape[1:]), BF16)
    first_grad = jax.ShapeDtypeStruct((PARTS, CHUNK, *basis.shape[1:]), BF16)
    hbm = pl.BlockSpec(memory_space=pl.ANY)
    return pl.pallas_call(
        functools.partial(send_kernel, share=share),
        out_shape=[
            *(jax.ShapeDtypeStruct((TRAVEL, rows, size), density.dtype) for rows in kept),
            first,
            first,
            first_grad,
        ],
        in_specs=[hbm] * 5,
        out_specs=[pl.BlockSpec(memory_space=pltpu.VMEM)] * (slabs + 3),
        scratch_shapes=[
            pltpu.SMEM(region.shape, jnp.int32),
            pltpu.SemaphoreType.DMA((slabs, 3)),
            pltpu.SemaphoreType.DMA((4,)),
        ],
        compiler_params=pltpu.CompilerParams(vmem_limit_bytes=VMEM_LIMIT),
    )(in_hbm(region), in_hbm(density), in_hbm(basis), in_hbm(field), in_hbm(basis_grad))


def fetch_rows(region, density, basis, field, basis_grad, slabs, share):
    own, *rest = rows_to_send(region, density, basis, field, basis_grad, slabs, share)
    outgoing, first = rest[: slabs - 1], rest[slabs - 1 :]
    near = {}
    for shift in reversed(range(1, slabs)):
        near[shift] = lax.ppermute(outgoing[slabs - 1 - shift], "grid", [(i, i ^ shift) for i in range(slabs)])
    return own, [near[shift] for shift in range(1, slabs)], first


def stage_rows(stage, own, near, far, share):
    part = lax.rem(lax.axis_index("atoms"), share)
    kept = near[0].shape[1]
    for place in range(TRAVEL):
        stage[place] = own[place]
        for shift, (here, there) in enumerate(zip(near, far), 1):
            stage[shift * TRAVEL + place, pl.ds(pl.multiple_of(part * kept, kept), kept), :] = here[place]
            stage[shift * TRAVEL + place, pl.ds(pl.multiple_of((1 - part) * kept, kept), kept), :] = there[place]


def block_major(x_ref, wide, points, blocks):
    wide[...] = x_ref[0].astype(F32)
    return [wide[pl.ds(s, points, stride=blocks), :] for s in range(blocks)]


def relayout_kernel(basis, field, basis_out, field_out, wide, *, points, blocks):
    size = basis.shape[-1]
    for source, target in ((basis, basis_out), (field, field_out)):
        for s, part in enumerate(block_major(source, wide, points, blocks)):
            target[0, :, s * size : (s + 1) * size] = part.astype(BF16)


def relayout(basis, field, points, blocks):
    batches, rows, size = basis.shape
    here = pl.BlockSpec((1, rows, size), lambda b: (b, 0, 0))
    there = pl.BlockSpec((1, points, blocks * size), lambda b: (b, 0, 0))
    shape = jax.ShapeDtypeStruct((batches, points, blocks * size), BF16)
    return pl.pallas_call(
        functools.partial(relayout_kernel, points=points, blocks=blocks),
        grid=(batches,),
        out_shape=(shape, shape),
        in_specs=[here, here],
        out_specs=(there, there),
        scratch_shapes=[pltpu.VMEM((rows, size), F32)],
        compiler_params=pltpu.CompilerParams(vmem_limit_bytes=VMEM_LIMIT),
        cost_estimate=pl.CostEstimate(flops=0, bytes_accessed=8 * batches * rows * size, transcendentals=0),
    )(basis, field)


def batch_matrix(region, pattern, tiles, slab, batch, blocks, width):
    half = (width - 1) // 2
    none = tiles.shape[0] - 1
    places = [pattern[batch, s] for s in range(blocks)]
    rows = [region[slab, place] for place in places]
    strips = []
    for s in range(blocks):
        strip = []
        for t in range(blocks):
            k = rows[t] - rows[s] + half
            inside = jnp.logical_and(k >= 0, k < width)
            strip.append(tiles[jnp.where(inside, places[s] * width + k, none)])
        strips.append(jnp.concatenate(strip, axis=1))
    return jnp.concatenate(strips, axis=0)


def split(values):
    high = values.astype(BF16)
    rest = values - high.astype(F32)
    middle = rest.astype(BF16)
    low = (rest - middle.astype(F32)).astype(BF16)
    return high, middle, low


def gradient_kernel(
    region,
    pattern,
    basis,
    field,
    basis_grad,
    weights,
    weight_grad,
    fn_atom,
    batch_atom,
    places,
    *rest,
    points,
    blocks,
    width,
    owner_rows,
    slabs,
):
    *pieces, tiles, out, stage, spread, sums, energy_sums = rest
    batch = pl.program_id(0)
    batches = pl.num_programs(0)
    me = lax.axis_index("grid")
    me_atoms = lax.axis_index("atoms")
    size = tiles.shape[-1]
    region_size = region.shape[1]

    @pl.when(batch == 0)
    def _():
        tiles[region_size * width] = jnp.zeros((size, size), BF16)
        stage_rows(stage, pieces[0], pieces[1:slabs], pieces[slabs:], SHARE)
        for position in range(region_size):
            owner, slot, count = owner_and_slot(region, me, position, owner_rows)
            shift = jnp.bitwise_xor(me, owner)
            for k in range(width):
                tiles[position * width + k] = stage[shift * TRAVEL + travel_place(slot, count, k)]

    matrix = batch_matrix(region, pattern, tiles, me, batch, blocks, width)
    potential = lax.dot_general(field[0], matrix, NT, preferred_element_type=F32)
    rows = jnp.concatenate(
        [weights[pl.ds(batch, 1), :]]
        + [weight_grad[c, pl.ds(batch, 1), :] for c in range(PARTS)]
        + [jnp.zeros((8 - 1 - PARTS, points), F32)],
        axis=0,
    )
    columns = rows.T
    weight = columns[:, 0:1]
    energy = jnp.zeros((points, size), F32)
    for s in range(blocks):
        here = potential[:, s * size : (s + 1) * size]
        energy = energy + basis[0, :, s * size : (s + 1) * size].astype(F32) * here
        spread[pl.ds(s, points, stride=blocks), :] = here * weight
    scaled = spread[...]
    place = pl.ds(pl.multiple_of(batch * 8, 8), 8)
    for c in range(PARTS):
        terms = basis_grad[c, 0].astype(F32) * scaled
        sums[c, place, :] = jnp.sum(terms.reshape(-1, 8, size), axis=0)
        terms = energy * columns[:, 1 + c : 2 + c]
        energy_sums[c, place, :] = jnp.sum(terms.reshape(-1, 8, size), axis=0)

    @pl.when(batch == batches - 1)
    def _():
        padded = max(8, region_size)
        chosen = lax.broadcasted_iota(jnp.int32, (padded, places.shape[1]), 0) == places[...]
        chosen = chosen.astype(BF16)
        blocks_sum = []
        for c in range(PARTS):
            total = jnp.zeros((padded, size), F32)
            for piece in split(sums[c]):
                total = total + jnp.dot(chosen, piece, preferred_element_type=F32)
            blocks_sum.append(-2.0 * total)
        lefts = []
        for position in range(region_size):
            stack = jnp.concatenate([total[position : position + 1] for total in blocks_sum], axis=0)
            high, middle, low = (piece.astype(F32) for piece in split(stack))
            lefts.append(jnp.concatenate([high, middle, low, jnp.zeros((16 - 3 * PARTS, size), F32)], axis=0))
        left = jnp.concatenate(lefts, axis=1).astype(BF16)
        chunk = out.shape[-1]
        scale = [jnp.sum(energy_sums[c], axis=1, keepdims=True) for c in range(PARTS)]
        for device in range(out.shape[0]):
            atoms = lax.broadcasted_iota(jnp.int32, (chunk, size), 0) + device * chunk
            hot = [
                jnp.where(atoms == fn_atom[pl.ds(region[me, position], 1), :], 1.0, 0.0).astype(BF16)
                for position in range(region_size)
            ]
            found = lax.dot_general(left, jnp.concatenate(hot, axis=1), NT, preferred_element_type=F32)
            atoms = lax.broadcasted_iota(jnp.int32, (batch_atom.shape[0], chunk), 1) + device * chunk
            mine = atoms == batch_atom[...]
            for c in range(PARTS):
                value = found[c : c + 1] + found[PARTS + c : PARTS + c + 1] + found[2 * PARTS + c : 2 * PARTS + c + 1]
                value = value + jnp.sum(jnp.where(mine, scale[c], 0.0), axis=0, keepdims=True)
                out[jnp.bitwise_xor(me_atoms, device), c : c + 1, :] = value


def partial_gradient(
    region, pattern, basis, field, basis_grad, weights, weight_grad, fn_atom, batch_atom, pieces, shapes
):
    slabs, atom_devices, atom_total, points, blocks, width, owner_rows = shapes
    batches, _, columns = basis.shape
    size = columns // blocks
    region_size = region.shape[1]
    fn_atom = fn_atom.reshape(-1, size)
    places = jnp.broadcast_to(pattern[:, None, :], (batches, 8 // blocks, blocks)).reshape(1, -1)
    batch_atom = jnp.broadcast_to(batch_atom[:, None], (batches, 8)).reshape(-1, 1)
    block = pl.BlockSpec((1, points, columns), lambda b, *_: (b, 0, 0))
    whole = pl.BlockSpec(memory_space=pltpu.VMEM)
    tile_shape = (region_size * width + 1, size, size)
    out_shape = (atom_devices, PARTS, atom_total // atom_devices)
    return pl.pallas_call(
        functools.partial(
            gradient_kernel, points=points, blocks=blocks, width=width, owner_rows=owner_rows, slabs=slabs
        ),
        grid_spec=pltpu.PrefetchScalarGridSpec(
            num_scalar_prefetch=2,
            grid=(batches,),
            in_specs=[
                block,
                block,
                pl.BlockSpec((PARTS, 1, points * blocks, size), lambda b, *_: (0, b, 0, 0)),
            ]
            + [whole] * (5 + len(pieces)),
            out_specs=(whole, whole),
            scratch_shapes=[
                pltpu.VMEM((slabs * TRAVEL, size, size), BF16),
                pltpu.VMEM((points * blocks, size), F32),
                pltpu.VMEM((PARTS, batches * 8, size), F32),
                pltpu.VMEM((PARTS, batches * 8, size), F32),
            ],
        ),
        out_shape=(jax.ShapeDtypeStruct(tile_shape, BF16), jax.ShapeDtypeStruct(out_shape, F32)),
        compiler_params=pltpu.CompilerParams(vmem_limit_bytes=VMEM_LIMIT),
    )(region, pattern, basis, field, basis_grad, weights, weight_grad, fn_atom, batch_atom, places, *pieces)


def product_kernel(region, pattern, basis, tiles, out, spread, *, points, blocks, width):
    me = lax.axis_index("grid")
    size = tiles.shape[-1]
    matrix = batch_matrix(region, pattern, tiles, me, pl.program_id(0), blocks, width)
    product = jnp.dot(basis[0], matrix, preferred_element_type=F32)
    for t in range(blocks):
        spread[pl.ds(t, points, stride=blocks), :] = product[:, t * size : (t + 1) * size]
    out[0] = spread[...].astype(BF16)


def contract(region, pattern, basis, tiles, points, blocks, width):
    batches, _, columns = basis.shape
    size = columns // blocks
    return pl.pallas_call(
        functools.partial(product_kernel, points=points, blocks=blocks, width=width),
        grid_spec=pltpu.PrefetchScalarGridSpec(
            num_scalar_prefetch=2,
            grid=(batches,),
            in_specs=[
                pl.BlockSpec((1, points, columns), lambda b, *_: (b, 0, 0)),
                pl.BlockSpec(memory_space=pltpu.VMEM),
            ],
            out_specs=pl.BlockSpec((1, points * blocks, size), lambda b, *_: (b, 0, 0)),
            scratch_shapes=[pltpu.VMEM((points * blocks, size), F32)],
        ),
        out_shape=jax.ShapeDtypeStruct((batches, points * blocks, size), BF16),
        compiler_params=pltpu.CompilerParams(vmem_limit_bytes=VMEM_LIMIT),
        cost_estimate=pl.CostEstimate(
            flops=2 * batches * points * columns * columns,
            bytes_accessed=4 * batches * points * columns,
            transcendentals=0,
        ),
    )(region, pattern, basis, tiles)


def moment_terms(blocks):
    return [(c, p) for c in range(PARTS) for p in range(0, blocks, 2)]


def add_moments(moments, turned, grads, fresh, term):
    c, p = term
    blocks, _, size = grads.shape[1:]
    rows = slice(max(p - 1, 0) * size, min(p + 3, blocks) * size)
    columns = slice(p * size, min(p + 2, blocks) * size)
    right = jnp.concatenate([grads[c, place] for place in range(p, min(p + 2, blocks))], axis=1)
    value = jnp.dot(turned[rows, :], right, preferred_element_type=F32)
    moments[c, rows, columns] = value if fresh else moments[c, rows, columns] + value


def reorder_kernel(
    pattern_hbm,
    basis,
    field,
    basis_grad,
    weights_hbm,
    first_basis,
    first_field,
    first_grad,
    basis_out,
    field_out,
    moments,
    last_turned,
    last_grads,
    pattern,
    weights,
    basis_in,
    field_in,
    grad_in,
    wide,
    turned,
    grads,
    sems,
    small_sems,
):
    batches, blocks, points, size = basis_out.shape
    step = last_turned.shape[1] // points
    groups = batches // step
    turned = [last_turned if (groups - 1 - group) % 2 == 0 else turned for group in range(groups)]
    grads = [last_grads if (groups - 1 - group) % 2 == 0 else grads for group in range(groups)]

    def copies(chunk):
        here = pl.ds(chunk * CHUNK, CHUNK)
        pairs = [(field.at[here], field_in.at[here]), (basis.at[here], basis_in.at[here])]
        pairs += [(basis_grad.at[c, here], grad_in.at[c, here]) for c in range(PARTS)]
        return [
            pltpu.make_async_copy(source, target, sems.at[chunk, number])
            for number, (source, target) in enumerate(pairs)
        ]

    small = (
        pltpu.make_async_copy(pattern_hbm, pattern, small_sems.at[0]),
        pltpu.make_async_copy(weights_hbm, weights, small_sems.at[1]),
    )
    for copy in small:
        copy.start()
    for chunk in range(1, batches // CHUNK):
        for copy in copies(chunk):
            copy.start()
    for copy in small:
        copy.wait()

    def put_in_order(group, inner, array, starts):
        batch = group * step + inner
        points_here = slice(inner * points, (inner + 1) * points)
        if array < 2:
            source = ((first_field, first_basis) if batch < CHUNK else (field_in, basis_in))[array].at[batch]
        else:
            source = (first_grad if batch < CHUNK else grad_in).at[array - 2, batch]
        wide[array] = source[...].astype(F32)
        for place in range(blocks):
            values = wide[array, pl.ds(starts[place], points, stride=blocks), :].astype(BF16)
            if array == 0:
                field_out[batch, place] = values
                across = values.T.astype(F32) * weights[batch : batch + 1, :]
                turned[group][place * size : (place + 1) * size, points_here] = across.astype(BF16)
            elif array == 1:
                basis_out[batch, place] = values
            else:
                grads[group][array - 2, place, points_here, :] = values

    for group in range(groups):
        products = moment_terms(blocks) if group > 0 else []
        work = step * (2 + PARTS)
        done = 0
        for number in range(work):
            inner, array = divmod(number, 2 + PARTS)
            batch = group * step + inner
            if array == 0:
                if batch >= CHUNK and batch % CHUNK == 0:
                    for copy in copies(batch // CHUNK):
                        copy.wait()
                starts = [
                    sum(jnp.where(pattern[s, batch] == place, s, 0) for s in range(blocks)) for place in range(blocks)
                ]
            put_in_order(group, inner, array, starts)
            while done < len(products) and done * work < (number + 1) * len(products):
                add_moments(moments, turned[group - 1], grads[group - 1], group == 1, products[done])
                done += 1
    if groups == 1:
        moments[...] = jnp.zeros_like(moments)


def reorder(pattern, basis, field, basis_grad, weights, first, points, blocks):
    batches, rows, size = basis.shape
    step = 4 if batches % 4 == 0 else CHUNK
    hbm = pl.BlockSpec(memory_space=pl.ANY)
    vmem = pl.BlockSpec(memory_space=pltpu.VMEM)
    ordered = jax.ShapeDtypeStruct((batches, blocks, points, size), BF16)
    turned = (blocks * size, step * points)
    grads = (PARTS, blocks, step * points, size)
    return pl.pallas_call(
        reorder_kernel,
        out_shape=(
            ordered,
            ordered,
            jax.ShapeDtypeStruct((PARTS, blocks * size, blocks * size), F32),
            jax.ShapeDtypeStruct(turned, BF16),
            jax.ShapeDtypeStruct(grads, BF16),
        ),
        in_specs=[hbm] * 5 + [vmem] * 3,
        out_specs=(vmem,) * 5,
        scratch_shapes=[
            pltpu.SMEM((blocks, batches), jnp.int32),
            pltpu.VMEM(weights.shape, F32),
            pltpu.VMEM((batches, rows, size), BF16),
            pltpu.VMEM((batches, rows, size), BF16),
            pltpu.VMEM((PARTS, batches, rows, size), BF16),
            pltpu.VMEM((2 + PARTS, rows, size), F32),
            pltpu.VMEM(turned, BF16),
            pltpu.VMEM(grads, BF16),
            pltpu.SemaphoreType.DMA((batches // CHUNK, 2 + PARTS)),
            pltpu.SemaphoreType.DMA((2,)),
        ],
        compiler_params=pltpu.CompilerParams(vmem_limit_bytes=VMEM_LIMIT),
        cost_estimate=pl.CostEstimate(
            flops=2 * PARTS * batches * points * (blocks * size) ** 2,
            bytes_accessed=2 * (2 + PARTS) * batches * rows * size,
            transcendentals=0,
        ),
    )(in_hbm(pattern.T), in_hbm(basis), in_hbm(field), in_hbm(basis_grad), in_hbm(weights), *first)


def moment_kernel(
    region, before, turned, grads, weight_grad, fn_atom, batch_atom, moments, hot, grad_columns
):
    blocks, _, size = grads.shape[1:]
    batches = weight_grad.shape[1]
    me = lax.axis_index("grid")
    atoms = lax.broadcasted_iota(jnp.int32, (hot.shape[0], size), 0)
    rows = [fn_atom[pl.ds(region[me, position], 1), :] for position in range(blocks)]
    rows.append(jnp.concatenate([batch_atom[...], jnp.full((1, size - batches), -1, jnp.int32)], axis=1))
    for number, ids in enumerate(rows):
        hot[:, number * size : (number + 1) * size] = jnp.where(atoms == ids, 1.0, 0.0).astype(BF16)
    for c in range(PARTS):
        padded = jnp.concatenate([weight_grad[c], jnp.zeros((size - batches, weight_grad.shape[2]), F32)], axis=0)
        grad_columns[c] = padded.T
    for term in moment_terms(blocks):
        add_moments(moments, turned, grads, False, term)


def moments_and_atoms(region, before, turned, grads, weight_grad, fn_atom, batch_atom, atom_total):
    blocks, depth, size = grads.shape[1:]
    points = weight_grad.shape[2]
    vmem = pl.BlockSpec(memory_space=pltpu.VMEM)
    return pl.pallas_call(
        moment_kernel,
        out_shape=(
            jax.ShapeDtypeStruct(before.shape, F32),
            jax.ShapeDtypeStruct((atom_total, (blocks + 1) * size), BF16),
            jax.ShapeDtypeStruct((PARTS, points, size), F32),
        ),
        in_specs=[pl.BlockSpec(memory_space=pltpu.SMEM)] + [vmem] * 6,
        out_specs=(vmem,) * 3,
        input_output_aliases={1: 0},
        compiler_params=pltpu.CompilerParams(vmem_limit_bytes=VMEM_LIMIT),
        cost_estimate=pl.CostEstimate(
            flops=2 * PARTS * depth * (blocks * size) ** 2, bytes_accessed=0, transcendentals=0
        ),
    )(region, before, turned, grads, weight_grad, fn_atom.reshape(-1, size), batch_atom.reshape(1, -1))


def combine_kernel(
    region, basis, field, moments, hot, grad_columns, *rest, owner_rows, slabs, width, step
):
    *pieces, product_out, out, stage, matrix, energies = rest
    batches, blocks, points, size = basis.shape
    me = lax.axis_index("grid")
    me_atoms = lax.axis_index("atoms")
    half = (width - 1) // 2
    stage_rows(stage, pieces[0], pieces[1:slabs], pieces[slabs:], SHARE)
    rows = [region[me, position] for position in range(blocks)]
    found = [owner_and_slot(region, me, position, owner_rows) for position in range(blocks)]
    totals = [[jnp.zeros((8, size), F32) for _ in range(blocks)] for _ in range(PARTS)]
    for p in range(blocks):
        owner, slot, count = found[p]
        first = jnp.bitwise_xor(me, owner) * TRAVEL
        for q in range(blocks):
            if abs(q - p) > half:
                matrix[p * size : (p + 1) * size, q * size : (q + 1) * size] = jnp.zeros((size, size), BF16)
                continue
            k = rows[q] - rows[p] + half
            place = jnp.where(
                k == 0,
                travel_place(slot, count, 0),
                jnp.where(k == 1, travel_place(slot, count, 1), travel_place(slot, count, 2)),
            )
            inside = jnp.logical_and(k >= 0, k < width)
            tile = stage[first + place].astype(F32)
            tile = jnp.where(inside, tile, 0.0)
            matrix[p * size : (p + 1) * size, q * size : (q + 1) * size] = tile.astype(BF16)
            turned = tile.T
            for c in range(PARTS):
                terms = turned * moments[c, q * size : (q + 1) * size, p * size : (p + 1) * size]
                totals[c][p] = totals[c][p] + jnp.sum(terms.reshape(-1, 8, size), axis=0)
    derivative = [
        jnp.concatenate([jnp.sum(total, axis=0, keepdims=True) for total in totals[c]], axis=1) for c in range(PARTS)
    ]

    energies[...] = jnp.zeros_like(energies)
    lanes = lax.broadcasted_iota(jnp.int32, (points, size), 1)

    @pl.loop(0, batches // step)
    def _(group):
        left = [
            jnp.concatenate([basis[group * step + inner, p] for p in range(blocks)], axis=1) for inner in range(step)
        ]
        product = jnp.dot(jnp.concatenate(left, axis=0), matrix[...], preferred_element_type=F32)
        for inner in range(step):
            batch = group * step + inner
            energy = jnp.zeros((points, size), F32)
            for q in range(blocks):
                part = product[inner * points : (inner + 1) * points, q * size : (q + 1) * size]
                product_out[batch, q] = part.astype(BF16)
                energy = energy + part * field[batch, q].astype(F32)
            energy = jnp.sum(energy, axis=1, keepdims=True)
            energies[...] = jnp.where(lanes == batch, energy, energies[...])

    lefts = []
    for c in range(PARTS):
        term = jnp.sum(energies[...] * grad_columns[c], axis=0, keepdims=True)
        lefts.append(jnp.concatenate([-2.0 * derivative[c], term], axis=1))
    left = jnp.concatenate(lefts, axis=0)
    high, middle, low = (piece.astype(F32) for piece in split(left))
    left = jnp.concatenate([high, middle, low, jnp.zeros((16 - 3 * PARTS, left.shape[1]), F32)], axis=0).astype(BF16)
    chunk = out.shape[-1]
    for device in range(out.shape[0]):
        sums = lax.dot_general(
            left, hot[device * chunk : (device + 1) * chunk, :], NT, preferred_element_type=F32
        )
        value = sums[:PARTS] + sums[PARTS : 2 * PARTS] + sums[2 * PARTS : 3 * PARTS]
        out[jnp.bitwise_xor(me_atoms, device)] = value


def combine(region, prepared, pieces, shapes):
    basis, field, moments, hot, grad_columns = prepared
    slabs, atom_devices, atom_total, points, blocks, width, owner_rows = shapes
    batches, _, _, size = basis.shape
    step = 4 if batches % 4 == 0 else 1
    vmem = pl.BlockSpec(memory_space=pltpu.VMEM)
    return pl.pallas_call(
        functools.partial(combine_kernel, owner_rows=owner_rows, slabs=slabs, width=width, step=step),
        out_shape=(
            jax.ShapeDtypeStruct(basis.shape, BF16),
            jax.ShapeDtypeStruct((atom_devices, PARTS, atom_total // atom_devices), F32),
        ),
        in_specs=[pl.BlockSpec(memory_space=pltpu.SMEM)] + [vmem] * (5 + len(pieces)),
        out_specs=(vmem, vmem),
        scratch_shapes=[
            pltpu.VMEM((slabs * TRAVEL, size, size), BF16),
            pltpu.VMEM((blocks * size, blocks * size), BF16),
            pltpu.VMEM((points, size), F32),
        ],
        compiler_params=pltpu.CompilerParams(vmem_limit_bytes=VMEM_LIMIT),
    )(region, basis, field, moments, hot, grad_columns, *pieces)


def write_kernel(pattern, product, out, wide, staged, sems):
    batches, blocks, points, size = product.shape

    def copy(batch):
        return pltpu.make_async_copy(staged.at[batch], out.at[batch], sems.at[batch])

    @pl.loop(0, batches // 2)
    def _(pair):
        for inner in range(2):
            batch = pair * 2 + inner
            for t in range(blocks):
                wide[inner, pl.ds(t, points, stride=blocks), :] = product[batch, pattern[t, batch]].astype(F32)
            staged[batch] = wide[inner].astype(BF16)
            copy(batch).start()

    @pl.loop(0, batches)
    def _(batch):
        copy(batch).wait()


def write(pattern, product):
    batches, blocks, points, size = product.shape
    shape = (batches, points * blocks, size)
    return pl.pallas_call(
        write_kernel,
        out_shape=jax.ShapeDtypeStruct(shape, BF16),
        in_specs=[pl.BlockSpec(memory_space=pltpu.SMEM), pl.BlockSpec(memory_space=pltpu.VMEM)],
        out_specs=pl.BlockSpec(memory_space=pl.ANY),
        scratch_shapes=[
            pltpu.VMEM((2, points * blocks, size), F32),
            pltpu.VMEM(shape, BF16),
            pltpu.SemaphoreType.DMA((batches,)),
        ],
        compiler_params=pltpu.CompilerParams(vmem_limit_bytes=VMEM_LIMIT),
        cost_estimate=pl.CostEstimate(flops=0, bytes_accessed=4 * math.prod(shape), transcendentals=0),
    )(pattern.T, product)


def swap_halves(near, ready, atom_devices):
    near, ready = lax.optimization_barrier((near, ready))
    swap = [(i, i ^ 1) for i in range(atom_devices)]
    return near, [lax.ppermute(piece, "atoms", swap) for piece in near], ready


def tree_sum(values):
    if len(values) == 1:
        return values[0]
    half = len(values) // 2
    return tree_sum(values[:half]) + tree_sum(values[half:])


def exchange_all(parts, axis, count):
    moved = {d: lax.ppermute(parts[d], axis, [(i, i ^ d) for i in range(count)]) for d in range(1, count)}
    return [parts[0]] + [moved[d] for d in range(1, count)]


def sum_parts(partial_grad, product, slabs, atom_devices):
    total = tree_sum(exchange_all([partial_grad[d] for d in range(atom_devices)], "atoms", atom_devices))
    total, product = lax.optimization_barrier((total, product))
    return tree_sum(exchange_all([total] * slabs, "grid", slabs)), product


def local(
    basis,
    basis_grad,
    exchange_field,
    weights,
    weight_grad,
    density,
    region,
    pattern,
    fn_atom,
    batch_atom,
):
    batches, points, blocks, size = basis.shape
    owner_rows, width = density.shape[:2]
    slabs = lax.axis_size("grid")
    atom_devices = lax.axis_size("atoms")
    atom_total = fn_atom.shape[0] // (10 * slabs * atom_devices) * slabs * atom_devices
    shapes = (slabs, atom_devices, atom_total, points, blocks, width, owner_rows)
    flat_basis = basis.reshape(batches, points * blocks, size)
    flat_field = exchange_field.reshape(batches, points * blocks, size)
    flat_grad = basis_grad.reshape(PARTS, batches, points * blocks, size)
    own, near, first = fetch_rows(region, density, flat_basis, flat_field, flat_grad, slabs, SHARE)
    if region.shape[1] == blocks:
        ready = reorder(pattern, flat_basis, flat_field, flat_grad, weights, first, points, blocks)
        near, far, (basis_wide, field_wide, *partial) = swap_halves(near, ready, atom_devices)
        built = moments_and_atoms(region, *partial, weight_grad, fn_atom, batch_atom, atom_total)
        ready = (basis_wide, field_wide, *built)
        product, partial_grad = combine(region, ready, [own, *near, *far], shapes)
        gradient, product = sum_parts(partial_grad, product, slabs, atom_devices)
        contracted = write(pattern, product)
        return contracted.reshape(basis.shape), gradient
    ready = relayout(in_hbm(flat_basis), in_hbm(flat_field), points, blocks)
    near, far, (basis_wide, field_wide) = swap_halves(near, ready, atom_devices)
    tiles, partial_grad = partial_gradient(
        region,
        pattern,
        basis_wide,
        field_wide,
        in_hbm(flat_grad),
        weights,
        weight_grad,
        fn_atom,
        batch_atom,
        [own, *near, *far],
        shapes,
    )
    gradient, basis_wide = sum_parts(partial_grad, basis_wide, slabs, atom_devices)
    contracted = contract(region, pattern, basis_wide, tiles, points, blocks, width)
    return contracted.reshape(basis.shape), gradient


def solution(mesh):
    placed = (
        P(("groups", "grid", "atoms"), None, None, None),
        P(None, ("groups", "grid", "atoms"), None, None, None),
        P(("groups", "grid", "atoms"), None, None, None),
        P(("groups", "grid", "atoms"), None),
        P(None, ("groups", "grid", "atoms"), None),
        P(("groups", "grid"), None, None, None),
        P("groups", None),
        P(("groups", "grid", "atoms"), None),
        P("groups"),
        P(("groups", "grid", "atoms")),
    )
    return jax.shard_map(
        local,
        mesh=mesh,
        in_specs=placed,
        out_specs=(P(("groups", "grid", "atoms"), None, None, None), P(None, ("groups", "atoms"))),
        check_vma=False,
    )
```

```python
import functools
import math

import jax
import jax.numpy as jnp
from jax import lax
from jax.experimental import pallas as pl
from jax.experimental.pallas import tpu as pltpu
from jax.sharding import PartitionSpec as P

TRAVEL = 5
SHARE = 2
PARTS = 3
F32 = jnp.float32
BF16 = jnp.bfloat16
NT = (((1,), (1,)), ((), ()))
VMEM_LIMIT = 32 * 1024 * 1024


def owner_and_slot(region, slab, position, owner_rows):
    owner = lax.div(region[slab, position], owner_rows)
    slot = jnp.int32(0)
    count = jnp.int32(0)
    for other in range(region.shape[1]):
        same = jnp.where(lax.div(region[slab, other], owner_rows) == owner, 1, 0)
        count = count + same
        slot = slot + jnp.where(other < position, same, 0)
    return owner, slot, count


def travel_place(slot, count, k):
    if k == 0:
        return jnp.where(slot == 0, 4, 2)
    if k == 1:
        return jnp.where(slot == 0, 0, 3)
    return jnp.where(jnp.logical_and(slot == 0, count == 2), 1, 4)


def send_kernel(region, density, *rest, share):
    *outs, sems = rest
    me = lax.axis_index("grid")
    part = lax.rem(lax.axis_index("atoms"), share)
    size = region.shape[1]
    owner_rows = density.shape[0]
    rows = density.shape[-2]
    copies = []
    for shift, out in zip((0, *reversed(range(1, len(outs)))), outs):
        slab = jnp.bitwise_xor(me, shift)
        base = jnp.int32(owner_rows)
        count = jnp.int32(0)
        for position in range(size):
            row = region[slab, position] - me * owner_rows
            mine = jnp.logical_and(row >= 0, row < owner_rows)
            base = jnp.minimum(base, jnp.where(mine, row, owner_rows))
            count = count + jnp.where(mine, 1, 0)
        base = jnp.where(count == 0, 0, base)
        after = jnp.minimum(base + 1, owner_rows - 1)
        lower = base == 0
        edge = jnp.where(jnp.logical_and(count == 2, jnp.logical_not(lower)), after, base)
        kept = out.shape[1]
        first = 0 if kept == rows else pl.multiple_of(part * kept, kept)
        here = pl.ds(first, kept)
        pairs = (
            (density.at[base, pl.ds(1, 2), here, :], out.at[pl.ds(0, 2)]),
            (density.at[after, pl.ds(0, 2), here, :], out.at[pl.ds(2, 2)]),
            (density.at[edge, jnp.where(lower, 0, 2), here, :], out.at[4]),
        )
        for number, (source, target) in enumerate(pairs):
            copies.append(pltpu.make_async_copy(source, target, sems.at[shift, number]))
    for copy in copies:
        copy.start()
    for copy in copies:
        copy.wait()


def in_hbm(array):
    return pltpu.with_memory_space_constraint(array, pltpu.HBM)


def rows_to_send(region, density, slabs, share):
    size = density.shape[-1]
    kept = [size] + [size // share] * (slabs - 1)
    return pl.pallas_call(
        functools.partial(send_kernel, share=share),
        out_shape=[jax.ShapeDtypeStruct((TRAVEL, rows, size), density.dtype) for rows in kept],
        in_specs=[pl.BlockSpec(memory_space=pltpu.SMEM), pl.BlockSpec(memory_space=pl.ANY)],
        out_specs=[pl.BlockSpec(memory_space=pltpu.VMEM)] * slabs,
        scratch_shapes=[pltpu.SemaphoreType.DMA((slabs, 3))],
        compiler_params=pltpu.CompilerParams(vmem_limit_bytes=VMEM_LIMIT),
    )(in_hbm(region), in_hbm(density))


def fetch_rows(region, density, slabs, share):
    own, *outgoing = rows_to_send(region, density, slabs, share)
    near = {}
    for shift in reversed(range(1, slabs)):
        near[shift] = lax.ppermute(outgoing[slabs - 1 - shift], "grid", [(i, i ^ shift) for i in range(slabs)])
    return own, [near[shift] for shift in range(1, slabs)]


def stage_rows(stage, own, near, far, share):
    part = lax.rem(lax.axis_index("atoms"), share)
    kept = near[0].shape[1]
    for place in range(TRAVEL):
        stage[place] = own[place]
        for shift, (here, there) in enumerate(zip(near, far), 1):
            stage[shift * TRAVEL + place, pl.ds(pl.multiple_of(part * kept, kept), kept), :] = here[place]
            stage[shift * TRAVEL + place, pl.ds(pl.multiple_of((1 - part) * kept, kept), kept), :] = there[place]


def block_major(x_ref, wide, points, blocks):
    wide[...] = x_ref[0].astype(F32)
    return [wide[pl.ds(s, points, stride=blocks), :] for s in range(blocks)]


def relayout_kernel(basis, field, basis_out, field_out, wide, *, points, blocks):
    size = basis.shape[-1]
    for source, target in ((basis, basis_out), (field, field_out)):
        for s, part in enumerate(block_major(source, wide, points, blocks)):
            target[0, :, s * size : (s + 1) * size] = part.astype(BF16)


def relayout(basis, field, points, blocks):
    batches, rows, size = basis.shape
    here = pl.BlockSpec((1, rows, size), lambda b: (b, 0, 0))
    there = pl.BlockSpec((1, points, blocks * size), lambda b: (b, 0, 0))
    shape = jax.ShapeDtypeStruct((batches, points, blocks * size), BF16)
    return pl.pallas_call(
        functools.partial(relayout_kernel, points=points, blocks=blocks),
        grid=(batches,),
        out_shape=(shape, shape),
        in_specs=[here, here],
        out_specs=(there, there),
        scratch_shapes=[pltpu.VMEM((rows, size), F32)],
        compiler_params=pltpu.CompilerParams(vmem_limit_bytes=VMEM_LIMIT),
        cost_estimate=pl.CostEstimate(flops=0, bytes_accessed=8 * batches * rows * size, transcendentals=0),
    )(basis, field)


def batch_matrix(region, pattern, tiles, slab, batch, blocks, width):
    half = (width - 1) // 2
    none = tiles.shape[0] - 1
    places = [pattern[batch, s] for s in range(blocks)]
    rows = [region[slab, place] for place in places]
    strips = []
    for s in range(blocks):
        strip = []
        for t in range(blocks):
            k = rows[t] - rows[s] + half
            inside = jnp.logical_and(k >= 0, k < width)
            strip.append(tiles[jnp.where(inside, places[s] * width + k, none)])
        strips.append(jnp.concatenate(strip, axis=1))
    return jnp.concatenate(strips, axis=0)


def split(values):
    high = values.astype(BF16)
    rest = values - high.astype(F32)
    middle = rest.astype(BF16)
    low = (rest - middle.astype(F32)).astype(BF16)
    return high, middle, low


def gradient_kernel(
    region,
    pattern,
    basis,
    field,
    basis_grad,
    weights,
    weight_grad,
    fn_atom,
    batch_atom,
    places,
    *rest,
    points,
    blocks,
    width,
    owner_rows,
    slabs,
):
    *pieces, tiles, out, stage, spread, sums, energy_sums = rest
    batch = pl.program_id(0)
    batches = pl.num_programs(0)
    me = lax.axis_index("grid")
    me_atoms = lax.axis_index("atoms")
    size = tiles.shape[-1]
    region_size = region.shape[1]

    @pl.when(batch == 0)
    def _():
        tiles[region_size * width] = jnp.zeros((size, size), BF16)
        stage_rows(stage, pieces[0], pieces[1:slabs], pieces[slabs:], SHARE)
        for position in range(region_size):
            owner, slot, count = owner_and_slot(region, me, position, owner_rows)
            shift = jnp.bitwise_xor(me, owner)
            for k in range(width):
                tiles[position * width + k] = stage[shift * TRAVEL + travel_place(slot, count, k)]

    matrix = batch_matrix(region, pattern, tiles, me, batch, blocks, width)
    potential = lax.dot_general(field[0], matrix, NT, preferred_element_type=F32)
    rows = jnp.concatenate(
        [weights[pl.ds(batch, 1), :]]
        + [weight_grad[c, pl.ds(batch, 1), :] for c in range(PARTS)]
        + [jnp.zeros((8 - 1 - PARTS, points), F32)],
        axis=0,
    )
    columns = rows.T
    weight = columns[:, 0:1]
    energy = jnp.zeros((points, size), F32)
    for s in range(blocks):
        here = potential[:, s * size : (s + 1) * size]
        energy = energy + basis[0, :, s * size : (s + 1) * size].astype(F32) * here
        spread[pl.ds(s, points, stride=blocks), :] = here * weight
    scaled = spread[...]
    place = pl.ds(pl.multiple_of(batch * 8, 8), 8)
    for c in range(PARTS):
        terms = basis_grad[c, 0].astype(F32) * scaled
        sums[c, place, :] = jnp.sum(terms.reshape(-1, 8, size), axis=0)
        terms = energy * columns[:, 1 + c : 2 + c]
        energy_sums[c, place, :] = jnp.sum(terms.reshape(-1, 8, size), axis=0)

    @pl.when(batch == batches - 1)
    def _():
        padded = max(8, region_size)
        chosen = lax.broadcasted_iota(jnp.int32, (padded, places.shape[1]), 0) == places[...]
        chosen = chosen.astype(BF16)
        blocks_sum = []
        for c in range(PARTS):
            total = jnp.zeros((padded, size), F32)
            for piece in split(sums[c]):
                total = total + jnp.dot(chosen, piece, preferred_element_type=F32)
            blocks_sum.append(-2.0 * total)
        lefts = []
        for position in range(region_size):
            stack = jnp.concatenate([total[position : position + 1] for total in blocks_sum], axis=0)
            high, middle, low = (piece.astype(F32) for piece in split(stack))
            lefts.append(jnp.concatenate([high, middle, low, jnp.zeros((16 - 3 * PARTS, size), F32)], axis=0))
        left = jnp.concatenate(lefts, axis=1).astype(BF16)
        chunk = out.shape[-1]
        scale = [jnp.sum(energy_sums[c], axis=1, keepdims=True) for c in range(PARTS)]
        for device in range(out.shape[0]):
            atoms = lax.broadcasted_iota(jnp.int32, (chunk, size), 0) + device * chunk
            hot = [
                jnp.where(atoms == fn_atom[pl.ds(region[me, position], 1), :], 1.0, 0.0).astype(BF16)
                for position in range(region_size)
            ]
            found = lax.dot_general(left, jnp.concatenate(hot, axis=1), NT, preferred_element_type=F32)
            atoms = lax.broadcasted_iota(jnp.int32, (batch_atom.shape[0], chunk), 1) + device * chunk
            mine = atoms == batch_atom[...]
            for c in range(PARTS):
                value = found[c : c + 1] + found[PARTS + c : PARTS + c + 1] + found[2 * PARTS + c : 2 * PARTS + c + 1]
                value = value + jnp.sum(jnp.where(mine, scale[c], 0.0), axis=0, keepdims=True)
                out[jnp.bitwise_xor(me_atoms, device), c : c + 1, :] = value


def partial_gradient(
    region, pattern, basis, field, basis_grad, weights, weight_grad, fn_atom, batch_atom, pieces, shapes
):
    slabs, atom_devices, atom_total, points, blocks, width, owner_rows = shapes
    batches, _, columns = basis.shape
    size = columns // blocks
    region_size = region.shape[1]
    fn_atom = fn_atom.reshape(-1, size)
    places = jnp.broadcast_to(pattern[:, None, :], (batches, 8 // blocks, blocks)).reshape(1, -1)
    batch_atom = jnp.broadcast_to(batch_atom[:, None], (batches, 8)).reshape(-1, 1)
    block = pl.BlockSpec((1, points, columns), lambda b, *_: (b, 0, 0))
    whole = pl.BlockSpec(memory_space=pltpu.VMEM)
    tile_shape = (region_size * width + 1, size, size)
    out_shape = (atom_devices, PARTS, atom_total // atom_devices)
    return pl.pallas_call(
        functools.partial(
            gradient_kernel, points=points, blocks=blocks, width=width, owner_rows=owner_rows, slabs=slabs
        ),
        grid_spec=pltpu.PrefetchScalarGridSpec(
            num_scalar_prefetch=2,
            grid=(batches,),
            in_specs=[
                block,
                block,
                pl.BlockSpec((PARTS, 1, points * blocks, size), lambda b, *_: (0, b, 0, 0)),
            ]
            + [whole] * (5 + len(pieces)),
            out_specs=(whole, whole),
            scratch_shapes=[
                pltpu.VMEM((slabs * TRAVEL, size, size), BF16),
                pltpu.VMEM((points * blocks, size), F32),
                pltpu.VMEM((PARTS, batches * 8, size), F32),
                pltpu.VMEM((PARTS, batches * 8, size), F32),
            ],
        ),
        out_shape=(jax.ShapeDtypeStruct(tile_shape, BF16), jax.ShapeDtypeStruct(out_shape, F32)),
        compiler_params=pltpu.CompilerParams(vmem_limit_bytes=VMEM_LIMIT),
    )(region, pattern, basis, field, basis_grad, weights, weight_grad, fn_atom, batch_atom, places, *pieces)


def product_kernel(region, pattern, basis, tiles, out, spread, *, points, blocks, width):
    me = lax.axis_index("grid")
    size = tiles.shape[-1]
    matrix = batch_matrix(region, pattern, tiles, me, pl.program_id(0), blocks, width)
    product = jnp.dot(basis[0], matrix, preferred_element_type=F32)
    for t in range(blocks):
        spread[pl.ds(t, points, stride=blocks), :] = product[:, t * size : (t + 1) * size]
    out[0] = spread[...].astype(BF16)


def contract(region, pattern, basis, tiles, points, blocks, width):
    batches, _, columns = basis.shape
    size = columns // blocks
    return pl.pallas_call(
        functools.partial(product_kernel, points=points, blocks=blocks, width=width),
        grid_spec=pltpu.PrefetchScalarGridSpec(
            num_scalar_prefetch=2,
            grid=(batches,),
            in_specs=[
                pl.BlockSpec((1, points, columns), lambda b, *_: (b, 0, 0)),
                pl.BlockSpec(memory_space=pltpu.VMEM),
            ],
            out_specs=pl.BlockSpec((1, points * blocks, size), lambda b, *_: (b, 0, 0)),
            scratch_shapes=[pltpu.VMEM((points * blocks, size), F32)],
        ),
        out_shape=jax.ShapeDtypeStruct((batches, points * blocks, size), BF16),
        compiler_params=pltpu.CompilerParams(vmem_limit_bytes=VMEM_LIMIT),
        cost_estimate=pl.CostEstimate(
            flops=2 * batches * points * columns * columns,
            bytes_accessed=4 * batches * points * columns,
            transcendentals=0,
        ),
    )(region, pattern, basis, tiles)


def reorder_kernel(
    pattern_hbm,
    basis,
    field,
    basis_grad,
    weights_hbm,
    basis_out,
    field_out,
    turned,
    grads,
    pattern,
    weights,
    basis_in,
    field_in,
    grad_in,
    wide,
    sems,
    small_sems,
):
    batches, blocks, points, size = basis_out.shape

    def copies(batch):
        return (
            pltpu.make_async_copy(field.at[batch], field_in.at[batch], sems.at[batch, 0]),
            pltpu.make_async_copy(basis.at[batch], basis_in.at[batch], sems.at[batch, 1]),
            pltpu.make_async_copy(basis_grad.at[:, batch], grad_in.at[:, batch], sems.at[batch, 2]),
        )

    small = (
        pltpu.make_async_copy(pattern_hbm, pattern, small_sems.at[0]),
        pltpu.make_async_copy(weights_hbm, weights, small_sems.at[1]),
    )
    for copy in small:
        copy.start()

    @pl.loop(0, batches)
    def _(batch):
        for copy in copies(batch):
            copy.start()

    for copy in small:
        copy.wait()

    @pl.loop(0, batches)
    def _(batch):
        for copy in copies(batch):
            copy.wait()
        points_here = pl.ds(pl.multiple_of(batch * points, points), points)
        places = [pattern[s, batch] for s in range(blocks)]
        weight = weights[pl.ds(batch, 1), :]
        wide[0] = field_in[batch].astype(F32)
        wide[1] = basis_in[batch].astype(F32)
        for c in range(PARTS):
            wide[2 + c] = grad_in[c, batch].astype(F32)
        for s, place in enumerate(places):
            strided = pl.ds(s, points, stride=blocks)
            values = wide[0, strided, :]
            field_out[batch, place] = values.astype(BF16)
            turned[pl.ds(pl.multiple_of(place * size, size), size), points_here] = (values.T * weight).astype(BF16)
            basis_out[batch, place] = wide[1, strided, :].astype(BF16)
            for c in range(PARTS):
                grads[c, place, points_here, :] = wide[2 + c, strided, :].astype(BF16)


def reorder(pattern, basis, field, basis_grad, weights):
    batches, points, blocks, size = basis.shape
    rows = points * blocks
    hbm = pl.BlockSpec(memory_space=pl.ANY)
    vmem = pl.BlockSpec(memory_space=pltpu.VMEM)
    ordered = jax.ShapeDtypeStruct((batches, blocks, points, size), BF16)
    return pl.pallas_call(
        reorder_kernel,
        out_shape=(
            ordered,
            ordered,
            jax.ShapeDtypeStruct((blocks * size, batches * points), BF16),
            jax.ShapeDtypeStruct((PARTS, blocks, batches * points, size), BF16),
        ),
        in_specs=[hbm] * 5,
        out_specs=(vmem,) * 4,
        scratch_shapes=[
            pltpu.SMEM((blocks, batches), jnp.int32),
            pltpu.VMEM(weights.shape, F32),
            pltpu.VMEM((batches, rows, size), BF16),
            pltpu.VMEM((batches, rows, size), BF16),
            pltpu.VMEM((PARTS, batches, rows, size), BF16),
            pltpu.VMEM((2 + PARTS, rows, size), F32),
            pltpu.SemaphoreType.DMA((batches, 3)),
            pltpu.SemaphoreType.DMA((2,)),
        ],
        compiler_params=pltpu.CompilerParams(vmem_limit_bytes=VMEM_LIMIT),
        cost_estimate=pl.CostEstimate(
            flops=0, bytes_accessed=2 * (2 + PARTS) * batches * rows * size, transcendentals=0
        ),
    )(
        in_hbm(pattern.T),
        in_hbm(basis.reshape(batches, rows, size)),
        in_hbm(field.reshape(batches, rows, size)),
        in_hbm(basis_grad.reshape(PARTS, batches, rows, size)),
        in_hbm(weights),
    )


def moment_kernel(region, turned, grads, weight_grad, fn_atom, batch_atom, moments, hot, grad_columns):
    blocks, _, size = grads.shape[1:]
    batches = weight_grad.shape[1]
    me = lax.axis_index("grid")
    taken = min(3, blocks) * size

    @pl.loop(0, PARTS * (blocks // 2))
    def _(number):
        c = lax.div(number, blocks // 2)
        p = lax.rem(number, blocks // 2) * 2
        start = jnp.minimum(jnp.maximum(p - 1, 0), blocks - min(3, blocks)) * size
        rows = pl.ds(pl.multiple_of(start, size), taken)
        right = jnp.concatenate([grads[c, p], grads[c, p + 1]], axis=1)
        columns = pl.ds(pl.multiple_of(p * size, size), 2 * size)
        moments[c, rows, columns] = jnp.dot(turned[rows, :], right, preferred_element_type=F32)

    atoms = lax.broadcasted_iota(jnp.int32, (hot.shape[0], size), 0)
    ids = jnp.concatenate([batch_atom[...], jnp.full((1, size - batches), -1, jnp.int32)], axis=1)
    hot[:, blocks * size :] = jnp.where(atoms == ids, 1.0, 0.0).astype(BF16)

    @pl.loop(0, blocks)
    def _(position):
        ids = fn_atom[pl.ds(region[me, position], 1), :]
        columns = pl.ds(pl.multiple_of(position * size, size), size)
        hot[:, columns] = jnp.where(atoms == ids, 1.0, 0.0).astype(BF16)

    for c in range(PARTS):
        padded = jnp.concatenate([weight_grad[c], jnp.zeros((size - batches, weight_grad.shape[2]), F32)], axis=0)
        grad_columns[c] = padded.T


def moments_and_atoms(region, turned, grads, weight_grad, fn_atom, batch_atom, atom_total):
    blocks, depth, size = grads.shape[1:]
    points = weight_grad.shape[2]
    vmem = pl.BlockSpec(memory_space=pltpu.VMEM)
    return pl.pallas_call(
        moment_kernel,
        out_shape=(
            jax.ShapeDtypeStruct((PARTS, blocks * size, blocks * size), F32),
            jax.ShapeDtypeStruct((atom_total, (blocks + 1) * size), BF16),
            jax.ShapeDtypeStruct((PARTS, points, size), F32),
        ),
        in_specs=[pl.BlockSpec(memory_space=pltpu.SMEM)] + [vmem] * 5,
        out_specs=(vmem,) * 3,
        compiler_params=pltpu.CompilerParams(vmem_limit_bytes=VMEM_LIMIT),
        cost_estimate=pl.CostEstimate(
            flops=2 * PARTS * depth * (blocks * size) ** 2, bytes_accessed=0, transcendentals=0
        ),
    )(region, turned, grads, weight_grad, fn_atom.reshape(-1, size), batch_atom.reshape(1, -1))


def combine_kernel(
    region, basis, field, moments, hot, grad_columns, *rest, owner_rows, slabs, width, step
):
    *pieces, product_out, out, stage, matrix, energies, derivative = rest
    batches, blocks, points, size = basis.shape
    me = lax.axis_index("grid")
    me_atoms = lax.axis_index("atoms")
    half = (width - 1) // 2
    stage_rows(stage, pieces[0], pieces[1:slabs], pieces[slabs:], SHARE)
    matrix[...] = jnp.zeros_like(matrix)

    @pl.loop(0, blocks)
    def _(p):
        row = region[me, p]
        owner, slot, count = owner_and_slot(region, me, p, owner_rows)
        first = jnp.bitwise_xor(me, owner) * TRAVEL
        here = pl.ds(pl.multiple_of(p * size, size), size)
        totals = [jnp.zeros((8, size), F32) for _ in range(PARTS)]
        for k in range(width):
            q = jnp.minimum(jnp.maximum(p + k - half, 0), blocks - 1)
            inside = jnp.logical_and(q == p + k - half, region[me, q] == row + k - half)
            tile = stage[first + travel_place(slot, count, k)].astype(F32)
            tile = jnp.where(inside, tile, 0.0)
            there = pl.ds(pl.multiple_of(q * size, size), size)
            turned = tile.T
            for c in range(PARTS):
                terms = turned * moments[c, there, here]
                totals[c] = totals[c] + jnp.sum(terms.reshape(-1, 8, size), axis=0)

            @pl.when(inside)
            def _():
                matrix[here, there] = tile.astype(BF16)

        for c in range(PARTS):
            derivative[c : c + 1, here] = -2.0 * jnp.sum(totals[c], axis=0, keepdims=True)

    energies[...] = jnp.zeros_like(energies)
    lanes = lax.broadcasted_iota(jnp.int32, (points, size), 1)

    @pl.loop(0, batches // step)
    def _(group):
        left = [
            jnp.concatenate([basis[group * step + inner, p] for p in range(blocks)], axis=1) for inner in range(step)
        ]
        product = jnp.dot(jnp.concatenate(left, axis=0), matrix[...], preferred_element_type=F32)
        for inner in range(step):
            batch = group * step + inner
            energy = jnp.zeros((points, size), F32)
            for q in range(blocks):
                part = product[inner * points : (inner + 1) * points, q * size : (q + 1) * size]
                product_out[batch, q] = part.astype(BF16)
                energy = energy + part * field[batch, q].astype(F32)
            energy = jnp.sum(energy, axis=1, keepdims=True)
            energies[...] = jnp.where(lanes == batch, energy, energies[...])

    lefts = []
    for c in range(PARTS):
        term = jnp.sum(energies[...] * grad_columns[c], axis=0, keepdims=True)
        lefts.append(jnp.concatenate([derivative[c : c + 1, :], term], axis=1))
    left = jnp.concatenate(lefts, axis=0)
    high, middle, low = (piece.astype(F32) for piece in split(left))
    left = jnp.concatenate([high, middle, low, jnp.zeros((16 - 3 * PARTS, left.shape[1]), F32)], axis=0).astype(BF16)
    chunk = out.shape[-1]

    @pl.loop(0, out.shape[0])
    def _(device):
        atoms = pl.ds(pl.multiple_of(device * chunk, 16), chunk)
        sums = lax.dot_general(left, hot[atoms, :], NT, preferred_element_type=F32)
        out[jnp.bitwise_xor(me_atoms, device)] = sums[:PARTS] + sums[PARTS : 2 * PARTS] + sums[2 * PARTS : 3 * PARTS]


def combine(region, prepared, pieces, shapes):
    basis, field, moments, hot, grad_columns = prepared
    slabs, atom_devices, atom_total, points, blocks, width, owner_rows = shapes
    batches, _, _, size = basis.shape
    step = 2 if batches % 2 == 0 else 1
    vmem = pl.BlockSpec(memory_space=pltpu.VMEM)
    return pl.pallas_call(
        functools.partial(combine_kernel, owner_rows=owner_rows, slabs=slabs, width=width, step=step),
        out_shape=(
            jax.ShapeDtypeStruct(basis.shape, BF16),
            jax.ShapeDtypeStruct((atom_devices, PARTS, atom_total // atom_devices), F32),
        ),
        in_specs=[pl.BlockSpec(memory_space=pltpu.SMEM)] + [vmem] * (5 + len(pieces)),
        out_specs=(vmem, vmem),
        scratch_shapes=[
            pltpu.VMEM((slabs * TRAVEL, size, size), BF16),
            pltpu.VMEM((blocks * size, blocks * size), BF16),
            pltpu.VMEM((points, size), F32),
            pltpu.VMEM((PARTS, blocks * size), F32),
        ],
        compiler_params=pltpu.CompilerParams(vmem_limit_bytes=VMEM_LIMIT),
    )(region, basis, field, moments, hot, grad_columns, *pieces)


def write_kernel(pattern, product, out, wide, staged, sems):
    batches, blocks, points, size = product.shape

    def copy(batch):
        return pltpu.make_async_copy(staged.at[batch], out.at[batch], sems.at[batch])

    @pl.loop(0, batches // 2)
    def _(pair):
        for inner in range(2):
            batch = pair * 2 + inner
            for t in range(blocks):
                wide[inner, pl.ds(t, points, stride=blocks), :] = product[batch, pattern[t, batch]].astype(F32)
            staged[batch] = wide[inner].astype(BF16)
            copy(batch).start()

    @pl.loop(0, batches)
    def _(batch):
        copy(batch).wait()


def write(pattern, product):
    batches, blocks, points, size = product.shape
    shape = (batches, points * blocks, size)
    return pl.pallas_call(
        write_kernel,
        out_shape=jax.ShapeDtypeStruct(shape, BF16),
        in_specs=[pl.BlockSpec(memory_space=pltpu.SMEM), pl.BlockSpec(memory_space=pltpu.VMEM)],
        out_specs=pl.BlockSpec(memory_space=pl.ANY),
        scratch_shapes=[
            pltpu.VMEM((2, points * blocks, size), F32),
            pltpu.VMEM(shape, BF16),
            pltpu.SemaphoreType.DMA((batches,)),
        ],
        compiler_params=pltpu.CompilerParams(vmem_limit_bytes=VMEM_LIMIT),
        cost_estimate=pl.CostEstimate(flops=0, bytes_accessed=4 * math.prod(shape), transcendentals=0),
    )(pattern.T, product)


def swap_halves(near, ready, atom_devices):
    near, ready = lax.optimization_barrier((near, ready))
    swap = [(i, i ^ 1) for i in range(atom_devices)]
    return near, [lax.ppermute(piece, "atoms", swap) for piece in near], ready


def tree_sum(values):
    if len(values) == 1:
        return values[0]
    half = len(values) // 2
    return tree_sum(values[:half]) + tree_sum(values[half:])


def exchange_all(parts, axis, count):
    moved = {d: lax.ppermute(parts[d], axis, [(i, i ^ d) for i in range(count)]) for d in range(1, count)}
    return [parts[0]] + [moved[d] for d in range(1, count)]


def sum_parts(partial_grad, product, slabs, atom_devices):
    total = tree_sum(exchange_all([partial_grad[d] for d in range(atom_devices)], "atoms", atom_devices))
    total, product = lax.optimization_barrier((total, product))
    return tree_sum(exchange_all([total] * slabs, "grid", slabs)), product


def local(
    basis,
    basis_grad,
    exchange_field,
    weights,
    weight_grad,
    density,
    region,
    pattern,
    fn_atom,
    batch_atom,
):
    batches, points, blocks, size = basis.shape
    owner_rows, width = density.shape[:2]
    slabs = lax.axis_size("grid")
    atom_devices = lax.axis_size("atoms")
    atom_total = fn_atom.shape[0] // (10 * slabs * atom_devices) * slabs * atom_devices
    shapes = (slabs, atom_devices, atom_total, points, blocks, width, owner_rows)
    own, near = fetch_rows(region, density, slabs, SHARE)
    if region.shape[1] == blocks:
        ready = reorder(pattern, basis, exchange_field, basis_grad, weights)
        near, far, (basis_wide, field_wide, *partial) = swap_halves(near, ready, atom_devices)
        built = moments_and_atoms(region, *partial, weight_grad, fn_atom, batch_atom, atom_total)
        ready = (basis_wide, field_wide, *built)
        product, partial_grad = combine(region, ready, [own, *near, *far], shapes)
        gradient, product = sum_parts(partial_grad, product, slabs, atom_devices)
        contracted = write(pattern, product)
        return contracted.reshape(basis.shape), gradient
    ready = relayout(
        in_hbm(basis.reshape(batches, points * blocks, size)),
        in_hbm(exchange_field.reshape(batches, points * blocks, size)),
        points,
        blocks,
    )
    near, far, (basis_wide, field_wide) = swap_halves(near, ready, atom_devices)
    tiles, partial_grad = partial_gradient(
        region,
        pattern,
        basis_wide,
        field_wide,
        in_hbm(basis_grad.reshape(PARTS, batches, points * blocks, size)),
        weights,
        weight_grad,
        fn_atom,
        batch_atom,
        [own, *near, *far],
        shapes,
    )
    gradient, basis_wide = sum_parts(partial_grad, basis_wide, slabs, atom_devices)
    contracted = contract(region, pattern, basis_wide, tiles, points, blocks, width)
    return contracted.reshape(basis.shape), gradient


def solution(mesh):
    placed = (
        P(("groups", "grid", "atoms"), None, None, None),
        P(None, ("groups", "grid", "atoms"), None, None, None),
        P(("groups", "grid", "atoms"), None, None, None),
        P(("groups", "grid", "atoms"), None),
        P(None, ("groups", "grid", "atoms"), None),
        P(("groups", "grid"), None, None, None),
        P("groups", None),
        P(("groups", "grid", "atoms"), None),
        P("groups"),
        P(("groups", "grid", "atoms")),
    )
    return jax.shard_map(
        local,
        mesh=mesh,
        in_specs=placed,
        out_specs=(P(("groups", "grid", "atoms"), None, None, None), P(None, ("groups", "atoms"))),
        check_vma=False,
    )
```

```python
import functools
import math

import jax
import jax.numpy as jnp
from jax import lax
from jax.experimental import pallas as pl
from jax.experimental.pallas import tpu as pltpu
from jax.sharding import PartitionSpec as P

TRAVEL = 5
SHARE = 2
CHUNK = 2
PARTS = 3
F32 = jnp.float32
BF16 = jnp.bfloat16
NT = (((1,), (1,)), ((), ()))
VMEM_LIMIT = 32 * 1024 * 1024


def owner_and_slot(region, slab, position, owner_rows):
    owner = lax.div(region[slab, position], owner_rows)
    slot = jnp.int32(0)
    count = jnp.int32(0)
    for other in range(region.shape[1]):
        same = jnp.where(lax.div(region[slab, other], owner_rows) == owner, 1, 0)
        count = count + same
        slot = slot + jnp.where(other < position, same, 0)
    return owner, slot, count


def travel_place(slot, count, k):
    if k == 0:
        return jnp.where(slot == 0, 4, 2)
    if k == 1:
        return jnp.where(slot == 0, 0, 3)
    return jnp.where(jnp.logical_and(slot == 0, count == 2), 1, 4)


def send_kernel(
    region_hbm, density, basis, field, basis_grad, fn_atom_hbm, batch_atom_hbm, weight_grad_hbm, *rest, share
):
    *outs, first_basis, first_field, first_grad, hot, grad_columns = rest[:-7]
    region, fn_atom, batch_atom, weight_grad, sems, small_sems, first_sems = rest[-7:]
    small = (
        pltpu.make_async_copy(region_hbm, region, small_sems.at[0]),
        pltpu.make_async_copy(fn_atom_hbm, fn_atom, small_sems.at[1]),
        pltpu.make_async_copy(batch_atom_hbm, batch_atom, small_sems.at[2]),
        pltpu.make_async_copy(weight_grad_hbm, weight_grad, small_sems.at[3]),
    )
    firsts = (
        pltpu.make_async_copy(field.at[pl.ds(0, first_field.shape[0])], first_field, first_sems.at[0]),
        pltpu.make_async_copy(basis_grad.at[:, pl.ds(0, first_grad.shape[1])], first_grad, first_sems.at[1]),
        pltpu.make_async_copy(basis.at[pl.ds(0, first_basis.shape[0])], first_basis, first_sems.at[2]),
    )
    for copy in small:
        copy.start()
    small[0].wait()
    me = lax.axis_index("grid")
    part = lax.rem(lax.axis_index("atoms"), share)
    size = region.shape[1]
    owner_rows = density.shape[0]
    rows = density.shape[-2]
    copies = []
    for shift, out in zip((0, *reversed(range(1, len(outs)))), outs):
        slab = jnp.bitwise_xor(me, shift)
        base = jnp.int32(owner_rows)
        count = jnp.int32(0)
        for position in range(size):
            row = region[slab, position] - me * owner_rows
            mine = jnp.logical_and(row >= 0, row < owner_rows)
            base = jnp.minimum(base, jnp.where(mine, row, owner_rows))
            count = count + jnp.where(mine, 1, 0)
        base = jnp.where(count == 0, 0, base)
        after = jnp.minimum(base + 1, owner_rows - 1)
        lower = base == 0
        edge = jnp.where(jnp.logical_and(count == 2, jnp.logical_not(lower)), after, base)
        kept = out.shape[1]
        first = 0 if kept == rows else pl.multiple_of(part * kept, kept)
        here = pl.ds(first, kept)
        pairs = (
            (density.at[base, pl.ds(1, 2), here, :], out.at[pl.ds(0, 2)]),
            (density.at[after, pl.ds(0, 2), here, :], out.at[pl.ds(2, 2)]),
            (density.at[edge, jnp.where(lower, 0, 2), here, :], out.at[4]),
        )
        for number, (source, target) in enumerate(pairs):
            copies.append(pltpu.make_async_copy(source, target, sems.at[shift, number]))
    for copy in (*copies, *firsts):
        copy.start()
    for copy in small[1:]:
        copy.wait()
    length = density.shape[-1]
    batches = weight_grad.shape[1]
    atoms = lax.broadcasted_iota(jnp.int32, (hot.shape[0], length), 0)
    fill = jnp.full((1, length - batches), -1, jnp.int32)
    hot[:, size * length :] = jnp.where(
        atoms == jnp.concatenate([batch_atom[...], fill], axis=1), 1.0, 0.0
    ).astype(BF16)

    @pl.loop(0, size)
    def _(position):
        ids = fn_atom[pl.ds(region[me, position], 1), :]
        columns = pl.ds(pl.multiple_of(position * length, length), length)
        hot[:, columns] = jnp.where(atoms == ids, 1.0, 0.0).astype(BF16)

    for c in range(PARTS):
        padding = jnp.zeros((length - batches, weight_grad.shape[2]), F32)
        grad_columns[c] = jnp.concatenate([weight_grad[c], padding], axis=0).T
    for copy in (*copies, *firsts):
        copy.wait()


def in_hbm(array):
    return pltpu.with_memory_space_constraint(array, pltpu.HBM)


def send(region, density, basis, field, basis_grad, fn_atom, batch_atom, weight_grad, slabs, share, atom_total):
    size = density.shape[-1]
    kept = [size] + [size // share] * (slabs - 1)
    first = jax.ShapeDtypeStruct((CHUNK, *basis.shape[1:]), BF16)
    hbm = pl.BlockSpec(memory_space=pl.ANY)
    operands = (region, density, basis, field, basis_grad, fn_atom, batch_atom, weight_grad)
    return pl.pallas_call(
        functools.partial(send_kernel, share=share),
        out_shape=[
            *(jax.ShapeDtypeStruct((TRAVEL, rows, size), density.dtype) for rows in kept),
            first,
            first,
            jax.ShapeDtypeStruct((PARTS, CHUNK, *basis.shape[1:]), BF16),
            jax.ShapeDtypeStruct((atom_total, (region.shape[1] + 1) * size), BF16),
            jax.ShapeDtypeStruct((PARTS, weight_grad.shape[2], size), F32),
        ],
        in_specs=[hbm] * len(operands),
        out_specs=[pl.BlockSpec(memory_space=pltpu.VMEM)] * (slabs + 5),
        scratch_shapes=[
            pltpu.SMEM(region.shape, jnp.int32),
            pltpu.VMEM(fn_atom.shape, jnp.int32),
            pltpu.VMEM(batch_atom.shape, jnp.int32),
            pltpu.VMEM(weight_grad.shape, F32),
            pltpu.SemaphoreType.DMA((slabs, 3)),
            pltpu.SemaphoreType.DMA((4,)),
            pltpu.SemaphoreType.DMA((3,)),
        ],
        compiler_params=pltpu.CompilerParams(vmem_limit_bytes=VMEM_LIMIT),
    )(*(in_hbm(operand) for operand in operands))


def travel(outgoing, slabs):
    near = {}
    for shift in reversed(range(1, slabs)):
        near[shift] = lax.ppermute(outgoing[slabs - 1 - shift], "grid", [(i, i ^ shift) for i in range(slabs)])
    return [near[shift] for shift in range(1, slabs)]


def stage_rows(stage, own, near, far, share):
    part = lax.rem(lax.axis_index("atoms"), share)
    kept = near[0].shape[1]
    for place in range(TRAVEL):
        stage[place] = own[place]
        for shift, (here, there) in enumerate(zip(near, far), 1):
            stage[shift * TRAVEL + place, pl.ds(pl.multiple_of(part * kept, kept), kept), :] = here[place]
            stage[shift * TRAVEL + place, pl.ds(pl.multiple_of((1 - part) * kept, kept), kept), :] = there[place]


def block_major(x_ref, wide, points, blocks):
    wide[...] = x_ref[0].astype(F32)
    return [wide[pl.ds(s, points, stride=blocks), :] for s in range(blocks)]


def relayout_kernel(basis, field, basis_out, field_out, wide, *, points, blocks):
    size = basis.shape[-1]
    for source, target in ((basis, basis_out), (field, field_out)):
        for s, part in enumerate(block_major(source, wide, points, blocks)):
            target[0, :, s * size : (s + 1) * size] = part.astype(BF16)


def relayout(basis, field, points, blocks):
    batches, rows, size = basis.shape
    here = pl.BlockSpec((1, rows, size), lambda b: (b, 0, 0))
    there = pl.BlockSpec((1, points, blocks * size), lambda b: (b, 0, 0))
    shape = jax.ShapeDtypeStruct((batches, points, blocks * size), BF16)
    return pl.pallas_call(
        functools.partial(relayout_kernel, points=points, blocks=blocks),
        grid=(batches,),
        out_shape=(shape, shape),
        in_specs=[here, here],
        out_specs=(there, there),
        scratch_shapes=[pltpu.VMEM((rows, size), F32)],
        compiler_params=pltpu.CompilerParams(vmem_limit_bytes=VMEM_LIMIT),
        cost_estimate=pl.CostEstimate(flops=0, bytes_accessed=8 * batches * rows * size, transcendentals=0),
    )(basis, field)


def batch_matrix(region, pattern, tiles, slab, batch, blocks, width):
    half = (width - 1) // 2
    none = tiles.shape[0] - 1
    places = [pattern[batch, s] for s in range(blocks)]
    rows = [region[slab, place] for place in places]
    strips = []
    for s in range(blocks):
        strip = []
        for t in range(blocks):
            k = rows[t] - rows[s] + half
            inside = jnp.logical_and(k >= 0, k < width)
            strip.append(tiles[jnp.where(inside, places[s] * width + k, none)])
        strips.append(jnp.concatenate(strip, axis=1))
    return jnp.concatenate(strips, axis=0)


def split(values):
    high = values.astype(BF16)
    rest = values - high.astype(F32)
    middle = rest.astype(BF16)
    low = (rest - middle.astype(F32)).astype(BF16)
    return high, middle, low


def gradient_kernel(
    region,
    pattern,
    basis,
    field,
    basis_grad,
    weights,
    weight_grad,
    fn_atom,
    batch_atom,
    places,
    *rest,
    points,
    blocks,
    width,
    owner_rows,
    slabs,
):
    *pieces, tiles, out, stage, spread, sums, energy_sums = rest
    batch = pl.program_id(0)
    batches = pl.num_programs(0)
    me = lax.axis_index("grid")
    me_atoms = lax.axis_index("atoms")
    size = tiles.shape[-1]
    region_size = region.shape[1]

    @pl.when(batch == 0)
    def _():
        tiles[region_size * width] = jnp.zeros((size, size), BF16)
        stage_rows(stage, pieces[0], pieces[1:slabs], pieces[slabs:], SHARE)
        for position in range(region_size):
            owner, slot, count = owner_and_slot(region, me, position, owner_rows)
            shift = jnp.bitwise_xor(me, owner)
            for k in range(width):
                tiles[position * width + k] = stage[shift * TRAVEL + travel_place(slot, count, k)]

    matrix = batch_matrix(region, pattern, tiles, me, batch, blocks, width)
    potential = lax.dot_general(field[0], matrix, NT, preferred_element_type=F32)
    rows = jnp.concatenate(
        [weights[pl.ds(batch, 1), :]]
        + [weight_grad[c, pl.ds(batch, 1), :] for c in range(PARTS)]
        + [jnp.zeros((8 - 1 - PARTS, points), F32)],
        axis=0,
    )
    columns = rows.T
    weight = columns[:, 0:1]
    energy = jnp.zeros((points, size), F32)
    for s in range(blocks):
        here = potential[:, s * size : (s + 1) * size]
        energy = energy + basis[0, :, s * size : (s + 1) * size].astype(F32) * here
        spread[pl.ds(s, points, stride=blocks), :] = here * weight
    scaled = spread[...]
    place = pl.ds(pl.multiple_of(batch * 8, 8), 8)
    for c in range(PARTS):
        terms = basis_grad[c, 0].astype(F32) * scaled
        sums[c, place, :] = jnp.sum(terms.reshape(-1, 8, size), axis=0)
        terms = energy * columns[:, 1 + c : 2 + c]
        energy_sums[c, place, :] = jnp.sum(terms.reshape(-1, 8, size), axis=0)

    @pl.when(batch == batches - 1)
    def _():
        padded = max(8, region_size)
        chosen = lax.broadcasted_iota(jnp.int32, (padded, places.shape[1]), 0) == places[...]
        chosen = chosen.astype(BF16)
        blocks_sum = []
        for c in range(PARTS):
            total = jnp.zeros((padded, size), F32)
            for piece in split(sums[c]):
                total = total + jnp.dot(chosen, piece, preferred_element_type=F32)
            blocks_sum.append(-2.0 * total)
        lefts = []
        for position in range(region_size):
            stack = jnp.concatenate([total[position : position + 1] for total in blocks_sum], axis=0)
            high, middle, low = (piece.astype(F32) for piece in split(stack))
            lefts.append(jnp.concatenate([high, middle, low, jnp.zeros((16 - 3 * PARTS, size), F32)], axis=0))
        left = jnp.concatenate(lefts, axis=1).astype(BF16)
        chunk = out.shape[-1]
        scale = [jnp.sum(energy_sums[c], axis=1, keepdims=True) for c in range(PARTS)]
        for device in range(out.shape[0]):
            atoms = lax.broadcasted_iota(jnp.int32, (chunk, size), 0) + device * chunk
            hot = [
                jnp.where(atoms == fn_atom[pl.ds(region[me, position], 1), :], 1.0, 0.0).astype(BF16)
                for position in range(region_size)
            ]
            found = lax.dot_general(left, jnp.concatenate(hot, axis=1), NT, preferred_element_type=F32)
            atoms = lax.broadcasted_iota(jnp.int32, (batch_atom.shape[0], chunk), 1) + device * chunk
            mine = atoms == batch_atom[...]
            for c in range(PARTS):
                value = found[c : c + 1] + found[PARTS + c : PARTS + c + 1] + found[2 * PARTS + c : 2 * PARTS + c + 1]
                value = value + jnp.sum(jnp.where(mine, scale[c], 0.0), axis=0, keepdims=True)
                out[jnp.bitwise_xor(me_atoms, device), c : c + 1, :] = value


def partial_gradient(
    region, pattern, basis, field, basis_grad, weights, weight_grad, fn_atom, batch_atom, pieces, shapes
):
    slabs, atom_devices, atom_total, points, blocks, width, owner_rows = shapes
    batches, _, columns = basis.shape
    size = columns // blocks
    region_size = region.shape[1]
    fn_atom = fn_atom.reshape(-1, size)
    places = jnp.broadcast_to(pattern[:, None, :], (batches, 8 // blocks, blocks)).reshape(1, -1)
    batch_atom = jnp.broadcast_to(batch_atom[:, None], (batches, 8)).reshape(-1, 1)
    block = pl.BlockSpec((1, points, columns), lambda b, *_: (b, 0, 0))
    whole = pl.BlockSpec(memory_space=pltpu.VMEM)
    tile_shape = (region_size * width + 1, size, size)
    out_shape = (atom_devices, PARTS, atom_total // atom_devices)
    return pl.pallas_call(
        functools.partial(
            gradient_kernel, points=points, blocks=blocks, width=width, owner_rows=owner_rows, slabs=slabs
        ),
        grid_spec=pltpu.PrefetchScalarGridSpec(
            num_scalar_prefetch=2,
            grid=(batches,),
            in_specs=[
                block,
                block,
                pl.BlockSpec((PARTS, 1, points * blocks, size), lambda b, *_: (0, b, 0, 0)),
            ]
            + [whole] * (5 + len(pieces)),
            out_specs=(whole, whole),
            scratch_shapes=[
                pltpu.VMEM((slabs * TRAVEL, size, size), BF16),
                pltpu.VMEM((points * blocks, size), F32),
                pltpu.VMEM((PARTS, batches * 8, size), F32),
                pltpu.VMEM((PARTS, batches * 8, size), F32),
            ],
        ),
        out_shape=(jax.ShapeDtypeStruct(tile_shape, BF16), jax.ShapeDtypeStruct(out_shape, F32)),
        compiler_params=pltpu.CompilerParams(vmem_limit_bytes=VMEM_LIMIT),
    )(region, pattern, basis, field, basis_grad, weights, weight_grad, fn_atom, batch_atom, places, *pieces)


def product_kernel(region, pattern, basis, tiles, out, spread, *, points, blocks, width):
    me = lax.axis_index("grid")
    size = tiles.shape[-1]
    matrix = batch_matrix(region, pattern, tiles, me, pl.program_id(0), blocks, width)
    product = jnp.dot(basis[0], matrix, preferred_element_type=F32)
    for t in range(blocks):
        spread[pl.ds(t, points, stride=blocks), :] = product[:, t * size : (t + 1) * size]
    out[0] = spread[...].astype(BF16)


def contract(region, pattern, basis, tiles, points, blocks, width):
    batches, _, columns = basis.shape
    size = columns // blocks
    return pl.pallas_call(
        functools.partial(product_kernel, points=points, blocks=blocks, width=width),
        grid_spec=pltpu.PrefetchScalarGridSpec(
            num_scalar_prefetch=2,
            grid=(batches,),
            in_specs=[
                pl.BlockSpec((1, points, columns), lambda b, *_: (b, 0, 0)),
                pl.BlockSpec(memory_space=pltpu.VMEM),
            ],
            out_specs=pl.BlockSpec((1, points * blocks, size), lambda b, *_: (b, 0, 0)),
            scratch_shapes=[pltpu.VMEM((points * blocks, size), F32)],
        ),
        out_shape=jax.ShapeDtypeStruct((batches, points * blocks, size), BF16),
        compiler_params=pltpu.CompilerParams(vmem_limit_bytes=VMEM_LIMIT),
        cost_estimate=pl.CostEstimate(
            flops=2 * batches * points * columns * columns,
            bytes_accessed=4 * batches * points * columns,
            transcendentals=0,
        ),
    )(region, pattern, basis, tiles)


def reorder_kernel(
    pattern_hbm,
    basis,
    field,
    basis_grad,
    weights_hbm,
    first_basis,
    first_field,
    first_grad,
    basis_out,
    field_out,
    turned,
    grads,
    pattern,
    weights,
    basis_in,
    field_in,
    grad_in,
    wide,
    sems,
    small_sems,
):
    batches, blocks, points, size = basis_out.shape

    def copies(batch):
        return (
            pltpu.make_async_copy(field.at[batch], field_in.at[batch], sems.at[batch, 0]),
            pltpu.make_async_copy(basis.at[batch], basis_in.at[batch], sems.at[batch, 1]),
            pltpu.make_async_copy(basis_grad.at[:, batch], grad_in.at[:, batch], sems.at[batch, 2]),
        )

    small = (
        pltpu.make_async_copy(pattern_hbm, pattern, small_sems.at[0]),
        pltpu.make_async_copy(weights_hbm, weights, small_sems.at[1]),
    )
    for copy in small:
        copy.start()
    for batch in range(CHUNK):
        pltpu.make_async_copy(first_field.at[batch], field_in.at[batch], sems.at[batch, 0]).start()
        pltpu.make_async_copy(first_basis.at[batch], basis_in.at[batch], sems.at[batch, 1]).start()
        pltpu.make_async_copy(first_grad.at[:, batch], grad_in.at[:, batch], sems.at[batch, 2]).start()

    @pl.loop(CHUNK, batches)
    def _(batch):
        for copy in copies(batch):
            copy.start()

    for copy in small:
        copy.wait()

    @pl.loop(0, batches)
    def _(batch):
        for copy in copies(batch):
            copy.wait()
        points_here = pl.ds(pl.multiple_of(batch * points, points), points)
        places = [pattern[s, batch] for s in range(blocks)]
        weight = weights[pl.ds(batch, 1), :]
        wide[0] = field_in[batch].astype(F32)
        wide[1] = basis_in[batch].astype(F32)
        for c in range(PARTS):
            wide[2 + c] = grad_in[c, batch].astype(F32)
        for s, place in enumerate(places):
            strided = pl.ds(s, points, stride=blocks)
            values = wide[0, strided, :]
            field_out[batch, place] = values.astype(BF16)
            turned[pl.ds(pl.multiple_of(place * size, size), size), points_here] = (values.T * weight).astype(BF16)
            basis_out[batch, place] = wide[1, strided, :].astype(BF16)
            for c in range(PARTS):
                grads[c, place, points_here, :] = wide[2 + c, strided, :].astype(BF16)


def reorder(pattern, basis, field, basis_grad, weights, first, points, blocks):
    batches, rows, size = basis.shape
    hbm = pl.BlockSpec(memory_space=pl.ANY)
    vmem = pl.BlockSpec(memory_space=pltpu.VMEM)
    ordered = jax.ShapeDtypeStruct((batches, blocks, points, size), BF16)
    return pl.pallas_call(
        reorder_kernel,
        out_shape=(
            ordered,
            ordered,
            jax.ShapeDtypeStruct((blocks * size, batches * points), BF16),
            jax.ShapeDtypeStruct((PARTS, blocks, batches * points, size), BF16),
        ),
        in_specs=[hbm] * 5 + [vmem] * 3,
        out_specs=(vmem,) * 4,
        scratch_shapes=[
            pltpu.SMEM((blocks, batches), jnp.int32),
            pltpu.VMEM(weights.shape, F32),
            pltpu.VMEM((batches, rows, size), BF16),
            pltpu.VMEM((batches, rows, size), BF16),
            pltpu.VMEM((PARTS, batches, rows, size), BF16),
            pltpu.VMEM((2 + PARTS, rows, size), F32),
            pltpu.SemaphoreType.DMA((batches, 3)),
            pltpu.SemaphoreType.DMA((2,)),
        ],
        compiler_params=pltpu.CompilerParams(vmem_limit_bytes=VMEM_LIMIT),
        cost_estimate=pl.CostEstimate(
            flops=0, bytes_accessed=2 * (2 + PARTS) * batches * rows * size, transcendentals=0
        ),
    )(in_hbm(pattern.T), in_hbm(basis), in_hbm(field), in_hbm(basis_grad), in_hbm(weights), *first)


def moment_kernel(turned, grads, moments):
    blocks, _, size = grads.shape[1:]
    for c in range(PARTS):
        for p in range(0, blocks, 2):
            rows = slice(max(p - 1, 0) * size, min(p + 3, blocks) * size)
            right = jnp.concatenate([grads[c, p], grads[c, p + 1]], axis=1)
            moments[c, rows, p * size : (p + 2) * size] = jnp.dot(
                turned[rows, :], right, preferred_element_type=F32
            )


def build_moments(turned, grads):
    blocks, depth, size = grads.shape[1:]
    vmem = pl.BlockSpec(memory_space=pltpu.VMEM)
    return pl.pallas_call(
        moment_kernel,
        out_shape=jax.ShapeDtypeStruct((PARTS, blocks * size, blocks * size), F32),
        in_specs=[vmem, vmem],
        out_specs=vmem,
        compiler_params=pltpu.CompilerParams(vmem_limit_bytes=VMEM_LIMIT),
        cost_estimate=pl.CostEstimate(
            flops=2 * PARTS * depth * (blocks * size) ** 2, bytes_accessed=0, transcendentals=0
        ),
    )(turned, grads)


def combine_kernel(
    region, basis, field, moments, hot, grad_columns, *rest, owner_rows, slabs, width, step
):
    *pieces, product_out, out, stage, matrix, energies = rest
    batches, blocks, points, size = basis.shape
    me = lax.axis_index("grid")
    me_atoms = lax.axis_index("atoms")
    half = (width - 1) // 2
    stage_rows(stage, pieces[0], pieces[1:slabs], pieces[slabs:], SHARE)
    rows = [region[me, position] for position in range(blocks)]
    found = [owner_and_slot(region, me, position, owner_rows) for position in range(blocks)]
    totals = [[jnp.zeros((8, size), F32) for _ in range(blocks)] for _ in range(PARTS)]
    for p in range(blocks):
        owner, slot, count = found[p]
        first = jnp.bitwise_xor(me, owner) * TRAVEL
        for q in range(blocks):
            if abs(q - p) > half:
                matrix[p * size : (p + 1) * size, q * size : (q + 1) * size] = jnp.zeros((size, size), BF16)
                continue
            k = rows[q] - rows[p] + half
            place = jnp.where(
                k == 0,
                travel_place(slot, count, 0),
                jnp.where(k == 1, travel_place(slot, count, 1), travel_place(slot, count, 2)),
            )
            inside = jnp.logical_and(k >= 0, k < width)
            tile = stage[first + place].astype(F32)
            tile = jnp.where(inside, tile, 0.0)
            matrix[p * size : (p + 1) * size, q * size : (q + 1) * size] = tile.astype(BF16)
            turned = tile.T
            for c in range(PARTS):
                terms = turned * moments[c, q * size : (q + 1) * size, p * size : (p + 1) * size]
                totals[c][p] = totals[c][p] + jnp.sum(terms.reshape(-1, 8, size), axis=0)
    derivative = [
        jnp.concatenate([jnp.sum(total, axis=0, keepdims=True) for total in totals[c]], axis=1) for c in range(PARTS)
    ]

    energies[...] = jnp.zeros_like(energies)
    lanes = lax.broadcasted_iota(jnp.int32, (points, size), 1)

    @pl.loop(0, batches // step)
    def _(group):
        left = [
            jnp.concatenate([basis[group * step + inner, p] for p in range(blocks)], axis=1) for inner in range(step)
        ]
        left = jnp.concatenate(left, axis=0)
        energy = [jnp.zeros((points, size), F32) for _ in range(step)]
        for q in range(0, blocks, 2):
            product = jnp.dot(left, matrix[:, q * size : (q + 2) * size], preferred_element_type=F32)
            for inner in range(step):
                batch = group * step + inner
                for column in range(2):
                    part = product[inner * points : (inner + 1) * points, column * size : (column + 1) * size]
                    product_out[batch, q + column] = part.astype(BF16)
                    energy[inner] = energy[inner] + part * field[batch, q + column].astype(F32)
        for inner in range(step):
            total = jnp.sum(energy[inner], axis=1, keepdims=True)
            energies[...] = jnp.where(lanes == group * step + inner, total, energies[...])

    lefts = []
    for c in range(PARTS):
        term = jnp.sum(energies[...] * grad_columns[c], axis=0, keepdims=True)
        lefts.append(jnp.concatenate([-2.0 * derivative[c], term], axis=1))
    left = jnp.concatenate(lefts, axis=0)
    high, middle, low = (piece.astype(F32) for piece in split(left))
    left = jnp.concatenate([high, middle, low, jnp.zeros((16 - 3 * PARTS, left.shape[1]), F32)], axis=0).astype(BF16)
    chunk = out.shape[-1]
    for device in range(out.shape[0]):
        sums = lax.dot_general(
            left, hot[device * chunk : (device + 1) * chunk, :], NT, preferred_element_type=F32
        )
        value = sums[:PARTS] + sums[PARTS : 2 * PARTS] + sums[2 * PARTS : 3 * PARTS]
        out[jnp.bitwise_xor(me_atoms, device)] = value


def combine(region, prepared, pieces, shapes):
    basis, field, moments, hot, grad_columns = prepared
    slabs, atom_devices, atom_total, points, blocks, width, owner_rows = shapes
    batches, _, _, size = basis.shape
    step = 4 if batches % 4 == 0 else 1
    vmem = pl.BlockSpec(memory_space=pltpu.VMEM)
    return pl.pallas_call(
        functools.partial(combine_kernel, owner_rows=owner_rows, slabs=slabs, width=width, step=step),
        out_shape=(
            jax.ShapeDtypeStruct(basis.shape, BF16),
            jax.ShapeDtypeStruct((atom_devices, PARTS, atom_total // atom_devices), F32),
        ),
        in_specs=[pl.BlockSpec(memory_space=pltpu.SMEM)] + [vmem] * (5 + len(pieces)),
        out_specs=(vmem, vmem),
        scratch_shapes=[
            pltpu.VMEM((slabs * TRAVEL, size, size), BF16),
            pltpu.VMEM((blocks * size, blocks * size), BF16),
            pltpu.VMEM((points, size), F32),
        ],
        compiler_params=pltpu.CompilerParams(vmem_limit_bytes=VMEM_LIMIT),
    )(region, basis, field, moments, hot, grad_columns, *pieces)


def write_kernel(pattern, product, out, wide, staged, sems):
    batches, blocks, points, size = product.shape

    def copy(batch):
        return pltpu.make_async_copy(staged.at[batch], out.at[batch], sems.at[batch])

    @pl.loop(0, batches // 2)
    def _(pair):
        for inner in range(2):
            batch = pair * 2 + inner
            for t in range(blocks):
                wide[inner, pl.ds(t, points, stride=blocks), :] = product[batch, pattern[t, batch]].astype(F32)
            staged[batch] = wide[inner].astype(BF16)
            copy(batch).start()

    @pl.loop(0, batches)
    def _(batch):
        copy(batch).wait()


def write(pattern, product):
    batches, blocks, points, size = product.shape
    shape = (batches, points * blocks, size)
    return pl.pallas_call(
        write_kernel,
        out_shape=jax.ShapeDtypeStruct(shape, BF16),
        in_specs=[pl.BlockSpec(memory_space=pltpu.SMEM), pl.BlockSpec(memory_space=pltpu.VMEM)],
        out_specs=pl.BlockSpec(memory_space=pl.ANY),
        scratch_shapes=[
            pltpu.VMEM((2, points * blocks, size), F32),
            pltpu.VMEM(shape, BF16),
            pltpu.SemaphoreType.DMA((batches,)),
        ],
        compiler_params=pltpu.CompilerParams(vmem_limit_bytes=VMEM_LIMIT),
        cost_estimate=pl.CostEstimate(flops=0, bytes_accessed=4 * math.prod(shape), transcendentals=0),
    )(pattern.T, product)


def swap_halves(near, ready, atom_devices):
    near, ready = lax.optimization_barrier((near, ready))
    swap = [(i, i ^ 1) for i in range(atom_devices)]
    return near, [lax.ppermute(piece, "atoms", swap) for piece in near], ready


def tree_sum(values):
    if len(values) == 1:
        return values[0]
    half = len(values) // 2
    return tree_sum(values[:half]) + tree_sum(values[half:])


def exchange_all(parts, axis, count):
    moved = {d: lax.ppermute(parts[d], axis, [(i, i ^ d) for i in range(count)]) for d in range(1, count)}
    return [parts[0]] + [moved[d] for d in range(1, count)]


def sum_parts(partial_grad, product, slabs, atom_devices):
    total = tree_sum(exchange_all([partial_grad[d] for d in range(atom_devices)], "atoms", atom_devices))
    total, product = lax.optimization_barrier((total, product))
    return tree_sum(exchange_all([total] * slabs, "grid", slabs)), product


def local(
    basis,
    basis_grad,
    exchange_field,
    weights,
    weight_grad,
    density,
    region,
    pattern,
    fn_atom,
    batch_atom,
):
    batches, points, blocks, size = basis.shape
    owner_rows, width = density.shape[:2]
    slabs = lax.axis_size("grid")
    atom_devices = lax.axis_size("atoms")
    atom_total = fn_atom.shape[0] // (10 * slabs * atom_devices) * slabs * atom_devices
    shapes = (slabs, atom_devices, atom_total, points, blocks, width, owner_rows)
    flat_basis = basis.reshape(batches, points * blocks, size)
    flat_field = exchange_field.reshape(batches, points * blocks, size)
    flat_grad = basis_grad.reshape(PARTS, batches, points * blocks, size)
    own, *sent = send(
        region,
        density,
        flat_basis,
        flat_field,
        flat_grad,
        fn_atom.reshape(-1, size),
        batch_atom.reshape(1, -1),
        weight_grad,
        slabs,
        SHARE,
        atom_total,
    )
    near = travel(sent[: slabs - 1], slabs)
    *first, hot, grad_columns = sent[slabs - 1 :]
    if region.shape[1] == blocks:
        ready = reorder(pattern, flat_basis, flat_field, flat_grad, weights, first, points, blocks)
        near, far, (basis_wide, field_wide, turned, grads) = swap_halves(near, ready, atom_devices)
        ready = (basis_wide, field_wide, build_moments(turned, grads), hot, grad_columns)
        product, partial_grad = combine(region, ready, [own, *near, *far], shapes)
        gradient, product = sum_parts(partial_grad, product, slabs, atom_devices)
        contracted = write(pattern, product)
        return contracted.reshape(basis.shape), gradient
    ready = relayout(in_hbm(flat_basis), in_hbm(flat_field), points, blocks)
    near, far, (basis_wide, field_wide) = swap_halves(near, ready, atom_devices)
    tiles, partial_grad = partial_gradient(
        region,
        pattern,
        basis_wide,
        field_wide,
        in_hbm(flat_grad),
        weights,
        weight_grad,
        fn_atom,
        batch_atom,
        [own, *near, *far],
        shapes,
    )
    gradient, basis_wide = sum_parts(partial_grad, basis_wide, slabs, atom_devices)
    contracted = contract(region, pattern, basis_wide, tiles, points, blocks, width)
    return contracted.reshape(basis.shape), gradient


def solution(mesh):
    placed = (
        P(("groups", "grid", "atoms"), None, None, None),
        P(None, ("groups", "grid", "atoms"), None, None, None),
        P(("groups", "grid", "atoms"), None, None, None),
        P(("groups", "grid", "atoms"), None),
        P(None, ("groups", "grid", "atoms"), None),
        P(("groups", "grid"), None, None, None),
        P("groups", None),
        P(("groups", "grid", "atoms"), None),
        P("groups"),
        P(("groups", "grid", "atoms")),
    )
    return jax.shard_map(
        local,
        mesh=mesh,
        in_specs=placed,
        out_specs=(P(("groups", "grid", "atoms"), None, None, None), P(None, ("groups", "atoms"))),
        check_vma=False,
    )
```

```python
import functools
import math

import jax
import jax.numpy as jnp
from jax import lax
from jax.experimental import pallas as pl
from jax.experimental.pallas import tpu as pltpu
from jax.sharding import PartitionSpec as P

TRAVEL = 5
SHARE = 2
PARTS = 3
F32 = jnp.float32
BF16 = jnp.bfloat16
NT = (((1,), (1,)), ((), ()))
VMEM_LIMIT = 32 * 1024 * 1024


def owner_and_slot(region, slab, position, owner_rows):
    owner = lax.div(region[slab, position], owner_rows)
    slot = jnp.int32(0)
    count = jnp.int32(0)
    for other in range(region.shape[1]):
        same = jnp.where(lax.div(region[slab, other], owner_rows) == owner, 1, 0)
        count = count + same
        slot = slot + jnp.where(other < position, same, 0)
    return owner, slot, count


def travel_place(slot, count, k):
    if k == 0:
        return jnp.where(slot == 0, 4, 2)
    if k == 1:
        return jnp.where(slot == 0, 0, 3)
    return jnp.where(jnp.logical_and(slot == 0, count == 2), 1, 4)


def send_kernel(region, density, *rest, share):
    *outs, sems = rest
    me = lax.axis_index("grid")
    part = lax.rem(lax.axis_index("atoms"), share)
    size = region.shape[1]
    owner_rows = density.shape[0]
    rows = density.shape[-2]
    copies = []
    for shift, out in zip((0, *reversed(range(1, len(outs)))), outs):
        slab = jnp.bitwise_xor(me, shift)
        base = jnp.int32(owner_rows)
        count = jnp.int32(0)
        for position in range(size):
            row = region[slab, position] - me * owner_rows
            mine = jnp.logical_and(row >= 0, row < owner_rows)
            base = jnp.minimum(base, jnp.where(mine, row, owner_rows))
            count = count + jnp.where(mine, 1, 0)
        base = jnp.where(count == 0, 0, base)
        after = jnp.minimum(base + 1, owner_rows - 1)
        lower = base == 0
        edge = jnp.where(jnp.logical_and(count == 2, jnp.logical_not(lower)), after, base)
        kept = out.shape[1]
        first = 0 if kept == rows else pl.multiple_of(part * kept, kept)
        here = pl.ds(first, kept)
        pairs = (
            (density.at[base, pl.ds(1, 2), here, :], out.at[pl.ds(0, 2)]),
            (density.at[after, pl.ds(0, 2), here, :], out.at[pl.ds(2, 2)]),
            (density.at[edge, jnp.where(lower, 0, 2), here, :], out.at[4]),
        )
        for number, (source, target) in enumerate(pairs):
            copies.append(pltpu.make_async_copy(source, target, sems.at[shift, number]))
    for copy in copies:
        copy.start()
    for copy in copies:
        copy.wait()


def in_hbm(array):
    return pltpu.with_memory_space_constraint(array, pltpu.HBM)


def rows_to_send(region, density, slabs, share):
    size = density.shape[-1]
    kept = [size] + [size // share] * (slabs - 1)
    return pl.pallas_call(
        functools.partial(send_kernel, share=share),
        out_shape=[jax.ShapeDtypeStruct((TRAVEL, rows, size), density.dtype) for rows in kept],
        in_specs=[pl.BlockSpec(memory_space=pltpu.SMEM), pl.BlockSpec(memory_space=pl.ANY)],
        out_specs=[pl.BlockSpec(memory_space=pltpu.VMEM)] * slabs,
        scratch_shapes=[pltpu.SemaphoreType.DMA((slabs, 3))],
        compiler_params=pltpu.CompilerParams(vmem_limit_bytes=VMEM_LIMIT),
    )(in_hbm(region), in_hbm(density))


def fetch_rows(region, density, slabs, share):
    own, *outgoing = rows_to_send(region, density, slabs, share)
    near = {}
    for shift in reversed(range(1, slabs)):
        near[shift] = lax.ppermute(outgoing[slabs - 1 - shift], "grid", [(i, i ^ shift) for i in range(slabs)])
    return own, [near[shift] for shift in range(1, slabs)]


def stage_rows(stage, own, near, far, share):
    part = lax.rem(lax.axis_index("atoms"), share)
    kept = near[0].shape[1]
    for place in range(TRAVEL):
        stage[place] = own[place]
        for shift, (here, there) in enumerate(zip(near, far), 1):
            stage[shift * TRAVEL + place, pl.ds(pl.multiple_of(part * kept, kept), kept), :] = here[place]
            stage[shift * TRAVEL + place, pl.ds(pl.multiple_of((1 - part) * kept, kept), kept), :] = there[place]


def block_major(x_ref, wide, points, blocks):
    wide[...] = x_ref[0].astype(F32)
    return [wide[pl.ds(s, points, stride=blocks), :] for s in range(blocks)]


def relayout_kernel(basis, field, basis_out, field_out, wide, *, points, blocks):
    size = basis.shape[-1]
    for source, target in ((basis, basis_out), (field, field_out)):
        for s, part in enumerate(block_major(source, wide, points, blocks)):
            target[0, :, s * size : (s + 1) * size] = part.astype(BF16)


def relayout(basis, field, points, blocks):
    batches, rows, size = basis.shape
    here = pl.BlockSpec((1, rows, size), lambda b: (b, 0, 0))
    there = pl.BlockSpec((1, points, blocks * size), lambda b: (b, 0, 0))
    shape = jax.ShapeDtypeStruct((batches, points, blocks * size), BF16)
    return pl.pallas_call(
        functools.partial(relayout_kernel, points=points, blocks=blocks),
        grid=(batches,),
        out_shape=(shape, shape),
        in_specs=[here, here],
        out_specs=(there, there),
        scratch_shapes=[pltpu.VMEM((rows, size), F32)],
        compiler_params=pltpu.CompilerParams(vmem_limit_bytes=VMEM_LIMIT),
        cost_estimate=pl.CostEstimate(flops=0, bytes_accessed=8 * batches * rows * size, transcendentals=0),
    )(basis, field)


def batch_matrix(region, pattern, tiles, slab, batch, blocks, width):
    half = (width - 1) // 2
    none = tiles.shape[0] - 1
    places = [pattern[batch, s] for s in range(blocks)]
    rows = [region[slab, place] for place in places]
    strips = []
    for s in range(blocks):
        strip = []
        for t in range(blocks):
            k = rows[t] - rows[s] + half
            inside = jnp.logical_and(k >= 0, k < width)
            strip.append(tiles[jnp.where(inside, places[s] * width + k, none)])
        strips.append(jnp.concatenate(strip, axis=1))
    return jnp.concatenate(strips, axis=0)


def split(values):
    high = values.astype(BF16)
    rest = values - high.astype(F32)
    middle = rest.astype(BF16)
    low = (rest - middle.astype(F32)).astype(BF16)
    return high, middle, low


def gradient_kernel(
    region,
    pattern,
    basis,
    field,
    basis_grad,
    weights,
    weight_grad,
    fn_atom,
    batch_atom,
    places,
    *rest,
    points,
    blocks,
    width,
    owner_rows,
    slabs,
):
    *pieces, tiles, out, stage, spread, sums, energy_sums = rest
    batch = pl.program_id(0)
    batches = pl.num_programs(0)
    me = lax.axis_index("grid")
    me_atoms = lax.axis_index("atoms")
    size = tiles.shape[-1]
    region_size = region.shape[1]

    @pl.when(batch == 0)
    def _():
        tiles[region_size * width] = jnp.zeros((size, size), BF16)
        stage_rows(stage, pieces[0], pieces[1:slabs], pieces[slabs:], SHARE)
        for position in range(region_size):
            owner, slot, count = owner_and_slot(region, me, position, owner_rows)
            shift = jnp.bitwise_xor(me, owner)
            for k in range(width):
                tiles[position * width + k] = stage[shift * TRAVEL + travel_place(slot, count, k)]

    matrix = batch_matrix(region, pattern, tiles, me, batch, blocks, width)
    potential = lax.dot_general(field[0], matrix, NT, preferred_element_type=F32)
    rows = jnp.concatenate(
        [weights[pl.ds(batch, 1), :]]
        + [weight_grad[c, pl.ds(batch, 1), :] for c in range(PARTS)]
        + [jnp.zeros((8 - 1 - PARTS, points), F32)],
        axis=0,
    )
    columns = rows.T
    weight = columns[:, 0:1]
    energy = jnp.zeros((points, size), F32)
    for s in range(blocks):
        here = potential[:, s * size : (s + 1) * size]
        energy = energy + basis[0, :, s * size : (s + 1) * size].astype(F32) * here
        spread[pl.ds(s, points, stride=blocks), :] = here * weight
    scaled = spread[...]
    place = pl.ds(pl.multiple_of(batch * 8, 8), 8)
    for c in range(PARTS):
        terms = basis_grad[c, 0].astype(F32) * scaled
        sums[c, place, :] = jnp.sum(terms.reshape(-1, 8, size), axis=0)
        terms = energy * columns[:, 1 + c : 2 + c]
        energy_sums[c, place, :] = jnp.sum(terms.reshape(-1, 8, size), axis=0)

    @pl.when(batch == batches - 1)
    def _():
        padded = max(8, region_size)
        chosen = lax.broadcasted_iota(jnp.int32, (padded, places.shape[1]), 0) == places[...]
        chosen = chosen.astype(BF16)
        blocks_sum = []
        for c in range(PARTS):
            total = jnp.zeros((padded, size), F32)
            for piece in split(sums[c]):
                total = total + jnp.dot(chosen, piece, preferred_element_type=F32)
            blocks_sum.append(-2.0 * total)
        lefts = []
        for position in range(region_size):
            stack = jnp.concatenate([total[position : position + 1] for total in blocks_sum], axis=0)
            high, middle, low = (piece.astype(F32) for piece in split(stack))
            lefts.append(jnp.concatenate([high, middle, low, jnp.zeros((16 - 3 * PARTS, size), F32)], axis=0))
        left = jnp.concatenate(lefts, axis=1).astype(BF16)
        chunk = out.shape[-1]
        scale = [jnp.sum(energy_sums[c], axis=1, keepdims=True) for c in range(PARTS)]
        for device in range(out.shape[0]):
            atoms = lax.broadcasted_iota(jnp.int32, (chunk, size), 0) + device * chunk
            hot = [
                jnp.where(atoms == fn_atom[pl.ds(region[me, position], 1), :], 1.0, 0.0).astype(BF16)
                for position in range(region_size)
            ]
            found = lax.dot_general(left, jnp.concatenate(hot, axis=1), NT, preferred_element_type=F32)
            atoms = lax.broadcasted_iota(jnp.int32, (batch_atom.shape[0], chunk), 1) + device * chunk
            mine = atoms == batch_atom[...]
            for c in range(PARTS):
                value = found[c : c + 1] + found[PARTS + c : PARTS + c + 1] + found[2 * PARTS + c : 2 * PARTS + c + 1]
                value = value + jnp.sum(jnp.where(mine, scale[c], 0.0), axis=0, keepdims=True)
                out[jnp.bitwise_xor(me_atoms, device), c : c + 1, :] = value


def partial_gradient(
    region, pattern, basis, field, basis_grad, weights, weight_grad, fn_atom, batch_atom, pieces, shapes
):
    slabs, atom_devices, atom_total, points, blocks, width, owner_rows = shapes
    batches, _, columns = basis.shape
    size = columns // blocks
    region_size = region.shape[1]
    fn_atom = fn_atom.reshape(-1, size)
    places = jnp.broadcast_to(pattern[:, None, :], (batches, 8 // blocks, blocks)).reshape(1, -1)
    batch_atom = jnp.broadcast_to(batch_atom[:, None], (batches, 8)).reshape(-1, 1)
    block = pl.BlockSpec((1, points, columns), lambda b, *_: (b, 0, 0))
    whole = pl.BlockSpec(memory_space=pltpu.VMEM)
    tile_shape = (region_size * width + 1, size, size)
    out_shape = (atom_devices, PARTS, atom_total // atom_devices)
    return pl.pallas_call(
        functools.partial(
            gradient_kernel, points=points, blocks=blocks, width=width, owner_rows=owner_rows, slabs=slabs
        ),
        grid_spec=pltpu.PrefetchScalarGridSpec(
            num_scalar_prefetch=2,
            grid=(batches,),
            in_specs=[
                block,
                block,
                pl.BlockSpec((PARTS, 1, points * blocks, size), lambda b, *_: (0, b, 0, 0)),
            ]
            + [whole] * (5 + len(pieces)),
            out_specs=(whole, whole),
            scratch_shapes=[
                pltpu.VMEM((slabs * TRAVEL, size, size), BF16),
                pltpu.VMEM((points * blocks, size), F32),
                pltpu.VMEM((PARTS, batches * 8, size), F32),
                pltpu.VMEM((PARTS, batches * 8, size), F32),
            ],
        ),
        out_shape=(jax.ShapeDtypeStruct(tile_shape, BF16), jax.ShapeDtypeStruct(out_shape, F32)),
        compiler_params=pltpu.CompilerParams(vmem_limit_bytes=VMEM_LIMIT),
    )(region, pattern, basis, field, basis_grad, weights, weight_grad, fn_atom, batch_atom, places, *pieces)


def product_kernel(region, pattern, basis, tiles, out, spread, *, points, blocks, width):
    me = lax.axis_index("grid")
    size = tiles.shape[-1]
    matrix = batch_matrix(region, pattern, tiles, me, pl.program_id(0), blocks, width)
    product = jnp.dot(basis[0], matrix, preferred_element_type=F32)
    for t in range(blocks):
        spread[pl.ds(t, points, stride=blocks), :] = product[:, t * size : (t + 1) * size]
    out[0] = spread[...].astype(BF16)


def contract(region, pattern, basis, tiles, points, blocks, width):
    batches, _, columns = basis.shape
    size = columns // blocks
    return pl.pallas_call(
        functools.partial(product_kernel, points=points, blocks=blocks, width=width),
        grid_spec=pltpu.PrefetchScalarGridSpec(
            num_scalar_prefetch=2,
            grid=(batches,),
            in_specs=[
                pl.BlockSpec((1, points, columns), lambda b, *_: (b, 0, 0)),
                pl.BlockSpec(memory_space=pltpu.VMEM),
            ],
            out_specs=pl.BlockSpec((1, points * blocks, size), lambda b, *_: (b, 0, 0)),
            scratch_shapes=[pltpu.VMEM((points * blocks, size), F32)],
        ),
        out_shape=jax.ShapeDtypeStruct((batches, points * blocks, size), BF16),
        compiler_params=pltpu.CompilerParams(vmem_limit_bytes=VMEM_LIMIT),
        cost_estimate=pl.CostEstimate(
            flops=2 * batches * points * columns * columns,
            bytes_accessed=4 * batches * points * columns,
            transcendentals=0,
        ),
    )(region, pattern, basis, tiles)


def reorder_kernel(
    pattern_hbm,
    basis,
    field,
    basis_grad,
    weights_hbm,
    basis_out,
    field_out,
    turned,
    grads,
    pattern,
    weights,
    basis_in,
    field_in,
    grad_in,
    wide,
    sems,
    small_sems,
):
    batches, blocks, points, size = basis_out.shape

    def copies(batch):
        return (
            pltpu.make_async_copy(field.at[batch], field_in.at[batch], sems.at[batch, 0]),
            pltpu.make_async_copy(basis.at[batch], basis_in.at[batch], sems.at[batch, 1]),
            pltpu.make_async_copy(basis_grad.at[:, batch], grad_in.at[:, batch], sems.at[batch, 2]),
        )

    small = (
        pltpu.make_async_copy(pattern_hbm, pattern, small_sems.at[0]),
        pltpu.make_async_copy(weights_hbm, weights, small_sems.at[1]),
    )
    for copy in small:
        copy.start()

    @pl.loop(0, batches)
    def _(batch):
        for copy in copies(batch):
            copy.start()

    for copy in small:
        copy.wait()

    @pl.loop(0, batches)
    def _(batch):
        for copy in copies(batch):
            copy.wait()
        points_here = pl.ds(pl.multiple_of(batch * points, points), points)
        places = [pattern[s, batch] for s in range(blocks)]
        weight = weights[pl.ds(batch, 1), :]
        wide[0] = field_in[batch].astype(F32)
        wide[1] = basis_in[batch].astype(F32)
        for c in range(PARTS):
            wide[2 + c] = grad_in[c, batch].astype(F32)
        for s, place in enumerate(places):
            strided = pl.ds(s, points, stride=blocks)
            values = wide[0, strided, :].astype(BF16)
            field_out[batch, place] = values
            rows = pl.ds(pl.multiple_of(place * size, size), size)
            turned[rows, points_here] = (values.T.astype(F32) * weight).astype(BF16)
            basis_out[batch, place] = wide[1, strided, :].astype(BF16)
            for c in range(PARTS):
                grads[c, place, points_here, :] = wide[2 + c, strided, :].astype(BF16)


def reorder(pattern, basis, field, basis_grad, weights, points, blocks):
    batches, rows, size = basis.shape
    hbm = pl.BlockSpec(memory_space=pl.ANY)
    vmem = pl.BlockSpec(memory_space=pltpu.VMEM)
    ordered = jax.ShapeDtypeStruct((batches, blocks, points, size), BF16)
    return pl.pallas_call(
        reorder_kernel,
        out_shape=(
            ordered,
            ordered,
            jax.ShapeDtypeStruct((blocks * size, batches * points), BF16),
            jax.ShapeDtypeStruct((PARTS, blocks, batches * points, size), BF16),
        ),
        in_specs=[hbm] * 5,
        out_specs=(vmem,) * 4,
        scratch_shapes=[
            pltpu.SMEM((blocks, batches), jnp.int32),
            pltpu.VMEM(weights.shape, F32),
            pltpu.VMEM((batches, rows, size), BF16),
            pltpu.VMEM((batches, rows, size), BF16),
            pltpu.VMEM((PARTS, batches, rows, size), BF16),
            pltpu.VMEM((2 + PARTS, rows, size), F32),
            pltpu.SemaphoreType.DMA((batches, 3)),
            pltpu.SemaphoreType.DMA((2,)),
        ],
        compiler_params=pltpu.CompilerParams(vmem_limit_bytes=VMEM_LIMIT),
        cost_estimate=pl.CostEstimate(
            flops=0, bytes_accessed=2 * (2 + PARTS) * batches * rows * size, transcendentals=0
        ),
    )(in_hbm(pattern.T), in_hbm(basis), in_hbm(field), in_hbm(basis_grad), in_hbm(weights))


def moment_kernel(turned, grads, moments):
    blocks, _, size = grads.shape[1:]
    for c in range(PARTS):
        for p in range(0, blocks, 2):
            rows = slice(max(p - 1, 0) * size, min(p + 3, blocks) * size)
            right = jnp.concatenate([grads[c, p], grads[c, p + 1]], axis=1)
            moments[c, rows, p * size : (p + 2) * size] = jnp.dot(
                turned[rows, :], right, preferred_element_type=F32
            )


def build_moments(turned, grads):
    blocks, depth, size = grads.shape[1:]
    vmem = pl.BlockSpec(memory_space=pltpu.VMEM)
    return pl.pallas_call(
        moment_kernel,
        out_shape=jax.ShapeDtypeStruct((PARTS, blocks * size, blocks * size), F32),
        in_specs=[vmem, vmem],
        out_specs=vmem,
        compiler_params=pltpu.CompilerParams(vmem_limit_bytes=VMEM_LIMIT),
        cost_estimate=pl.CostEstimate(
            flops=2 * PARTS * depth * (blocks * size) ** 2, bytes_accessed=0, transcendentals=0
        ),
    )(turned, grads)


def atom_kernel(region, fn_atom, batch_atom, weight_grad, hot, grad_columns):
    batches, points = weight_grad.shape[1:]
    size = fn_atom.shape[1]
    blocks = region.shape[1]
    me = lax.axis_index("grid")
    atoms = lax.broadcasted_iota(jnp.int32, (hot.shape[0], size), 0)
    ids = jnp.concatenate([batch_atom[...], jnp.full((1, size - batches), -1, jnp.int32)], axis=1)
    hot[:, blocks * size :] = jnp.where(atoms == ids, 1.0, 0.0).astype(BF16)

    @pl.loop(0, blocks)
    def _(position):
        ids = fn_atom[pl.ds(region[me, position], 1), :]
        columns = pl.ds(pl.multiple_of(position * size, size), size)
        hot[:, columns] = jnp.where(atoms == ids, 1.0, 0.0).astype(BF16)

    for c in range(PARTS):
        padding = jnp.zeros((size - batches, points), F32)
        grad_columns[c] = jnp.concatenate([weight_grad[c], padding], axis=0).T


def atom_matrix(region, fn_atom, batch_atom, weight_grad, blocks, size, atom_total):
    vmem = pl.BlockSpec(memory_space=pltpu.VMEM)
    return pl.pallas_call(
        atom_kernel,
        out_shape=(
            jax.ShapeDtypeStruct((atom_total, (blocks + 1) * size), BF16),
            jax.ShapeDtypeStruct((PARTS, weight_grad.shape[2], size), F32),
        ),
        in_specs=[pl.BlockSpec(memory_space=pltpu.SMEM)] + [vmem] * 3,
        out_specs=(vmem, vmem),
        compiler_params=pltpu.CompilerParams(vmem_limit_bytes=VMEM_LIMIT),
        cost_estimate=pl.CostEstimate(flops=1000000000, bytes_accessed=2 * atom_total * size, transcendentals=0),
    )(region, fn_atom.reshape(-1, size), batch_atom.reshape(1, -1), weight_grad)


def combine_kernel(
    region, basis, field, moments, hot, grad_columns, *rest, owner_rows, slabs, width, step
):
    *pieces, product_out, out, stage, matrix, energies = rest
    batches, blocks, points, size = basis.shape
    me = lax.axis_index("grid")
    me_atoms = lax.axis_index("atoms")
    half = (width - 1) // 2
    stage_rows(stage, pieces[0], pieces[1:slabs], pieces[slabs:], SHARE)
    rows = [region[me, position] for position in range(blocks)]
    found = [owner_and_slot(region, me, position, owner_rows) for position in range(blocks)]
    totals = [[jnp.zeros((8, size), F32) for _ in range(blocks)] for _ in range(PARTS)]
    for p in range(blocks):
        owner, slot, count = found[p]
        first = jnp.bitwise_xor(me, owner) * TRAVEL
        for q in range(blocks):
            if abs(q - p) > half:
                matrix[p * size : (p + 1) * size, q * size : (q + 1) * size] = jnp.zeros((size, size), BF16)
                continue
            k = rows[q] - rows[p] + half
            place = jnp.where(
                k == 0,
                travel_place(slot, count, 0),
                jnp.where(k == 1, travel_place(slot, count, 1), travel_place(slot, count, 2)),
            )
            inside = jnp.logical_and(k >= 0, k < width)
            tile = stage[first + place].astype(F32)
            tile = jnp.where(inside, tile, 0.0)
            matrix[p * size : (p + 1) * size, q * size : (q + 1) * size] = tile.astype(BF16)
            turned = tile.T
            for c in range(PARTS):
                terms = turned * moments[c, q * size : (q + 1) * size, p * size : (p + 1) * size]
                totals[c][p] = totals[c][p] + jnp.sum(terms.reshape(-1, 8, size), axis=0)
    derivative = [
        jnp.concatenate([jnp.sum(total, axis=0, keepdims=True) for total in totals[c]], axis=1) for c in range(PARTS)
    ]

    energies[...] = jnp.zeros_like(energies)
    lanes = lax.broadcasted_iota(jnp.int32, (points, size), 1)

    @pl.loop(0, batches // step)
    def _(group):
        left = [
            jnp.concatenate([basis[group * step + inner, p] for p in range(blocks)], axis=1) for inner in range(step)
        ]
        left = jnp.concatenate(left, axis=0)
        energy = [jnp.zeros((points, size), F32) for _ in range(step)]
        for q in range(0, blocks, 2):
            product = jnp.dot(left, matrix[:, q * size : (q + 2) * size], preferred_element_type=F32)
            for inner in range(step):
                batch = group * step + inner
                for column in range(2):
                    part = product[inner * points : (inner + 1) * points, column * size : (column + 1) * size]
                    product_out[batch, q + column] = part.astype(BF16)
                    energy[inner] = energy[inner] + part * field[batch, q + column].astype(F32)
        for inner in range(step):
            total = jnp.sum(energy[inner], axis=1, keepdims=True)
            energies[...] = jnp.where(lanes == group * step + inner, total, energies[...])

    lefts = []
    for c in range(PARTS):
        term = jnp.sum(energies[...] * grad_columns[c], axis=0, keepdims=True)
        lefts.append(jnp.concatenate([-2.0 * derivative[c], term], axis=1))
    left = jnp.concatenate(lefts, axis=0)
    high, middle, low = (piece.astype(F32) for piece in split(left))
    left = jnp.concatenate([high, middle, low, jnp.zeros((16 - 3 * PARTS, left.shape[1]), F32)], axis=0).astype(BF16)
    chunk = out.shape[-1]
    for device in range(out.shape[0]):
        sums = lax.dot_general(
            left, hot[device * chunk : (device + 1) * chunk, :], NT, preferred_element_type=F32
        )
        value = sums[:PARTS] + sums[PARTS : 2 * PARTS] + sums[2 * PARTS : 3 * PARTS]
        out[jnp.bitwise_xor(me_atoms, device)] = value


def combine(region, prepared, pieces, shapes):
    basis, field, moments, hot, grad_columns = prepared
    slabs, atom_devices, atom_total, points, blocks, width, owner_rows = shapes
    batches, _, _, size = basis.shape
    step = 8 if batches % 8 == 0 else 1
    vmem = pl.BlockSpec(memory_space=pltpu.VMEM)
    return pl.pallas_call(
        functools.partial(combine_kernel, owner_rows=owner_rows, slabs=slabs, width=width, step=step),
        out_shape=(
            jax.ShapeDtypeStruct(basis.shape, BF16),
            jax.ShapeDtypeStruct((atom_devices, PARTS, atom_total // atom_devices), F32),
        ),
        in_specs=[pl.BlockSpec(memory_space=pltpu.SMEM)] + [vmem] * (5 + len(pieces)),
        out_specs=(vmem, vmem),
        scratch_shapes=[
            pltpu.VMEM((slabs * TRAVEL, size, size), BF16),
            pltpu.VMEM((blocks * size, blocks * size), BF16),
            pltpu.VMEM((points, size), F32),
        ],
        compiler_params=pltpu.CompilerParams(vmem_limit_bytes=VMEM_LIMIT),
    )(region, basis, field, moments, hot, grad_columns, *pieces)


def write_kernel(pattern, product, out, wide, staged, sems):
    batches, blocks, points, size = product.shape

    def copy(batch):
        return pltpu.make_async_copy(staged.at[batch], out.at[batch], sems.at[batch])

    @pl.loop(0, batches // 2)
    def _(pair):
        for inner in range(2):
            batch = pair * 2 + inner
            for t in range(blocks):
                wide[inner, pl.ds(t, points, stride=blocks), :] = product[batch, pattern[t, batch]].astype(F32)
            staged[batch] = wide[inner].astype(BF16)
            copy(batch).start()

    @pl.loop(0, batches)
    def _(batch):
        copy(batch).wait()


def write(pattern, product):
    batches, blocks, points, size = product.shape
    shape = (batches, points * blocks, size)
    return pl.pallas_call(
        write_kernel,
        out_shape=jax.ShapeDtypeStruct(shape, BF16),
        in_specs=[pl.BlockSpec(memory_space=pltpu.SMEM), pl.BlockSpec(memory_space=pltpu.VMEM)],
        out_specs=pl.BlockSpec(memory_space=pl.ANY),
        scratch_shapes=[
            pltpu.VMEM((2, points * blocks, size), F32),
            pltpu.VMEM(shape, BF16),
            pltpu.SemaphoreType.DMA((batches,)),
        ],
        compiler_params=pltpu.CompilerParams(vmem_limit_bytes=VMEM_LIMIT),
        cost_estimate=pl.CostEstimate(flops=0, bytes_accessed=4 * math.prod(shape), transcendentals=0),
    )(pattern.T, product)


def swap_halves(near, ready, atom_devices):
    near, ready = lax.optimization_barrier((near, ready))
    swap = [(i, i ^ 1) for i in range(atom_devices)]
    return near, [lax.ppermute(piece, "atoms", swap) for piece in near], ready


def tree_sum(values):
    if len(values) == 1:
        return values[0]
    half = len(values) // 2
    return tree_sum(values[:half]) + tree_sum(values[half:])


def exchange_all(parts, axis, count):
    moved = {d: lax.ppermute(parts[d], axis, [(i, i ^ d) for i in range(count)]) for d in range(1, count)}
    return [parts[0]] + [moved[d] for d in range(1, count)]


def sum_parts(partial_grad, product, slabs, atom_devices):
    total = tree_sum(exchange_all([partial_grad[d] for d in range(atom_devices)], "atoms", atom_devices))
    total, product = lax.optimization_barrier((total, product))
    return tree_sum(exchange_all([total] * slabs, "grid", slabs)), product


def local(
    basis,
    basis_grad,
    exchange_field,
    weights,
    weight_grad,
    density,
    region,
    pattern,
    fn_atom,
    batch_atom,
):
    batches, points, blocks, size = basis.shape
    owner_rows, width = density.shape[:2]
    slabs = lax.axis_size("grid")
    atom_devices = lax.axis_size("atoms")
    atom_total = fn_atom.shape[0] // (10 * slabs * atom_devices) * slabs * atom_devices
    shapes = (slabs, atom_devices, atom_total, points, blocks, width, owner_rows)
    flat_basis = basis.reshape(batches, points * blocks, size)
    flat_field = exchange_field.reshape(batches, points * blocks, size)
    flat_grad = basis_grad.reshape(PARTS, batches, points * blocks, size)
    own, near = fetch_rows(region, density, slabs, SHARE)
    if region.shape[1] == blocks:
        basis_wide, field_wide, turned, grads = reorder(
            pattern, flat_basis, flat_field, flat_grad, weights, points, blocks
        )
        ready = (basis_wide, field_wide, build_moments(turned, grads), batch_atom)
        near, far, (basis_wide, field_wide, moments, batch_atom) = swap_halves(near, ready, atom_devices)
        hot, grad_columns = atom_matrix(region, fn_atom, batch_atom, weight_grad, blocks, size, atom_total)
        ready = (basis_wide, field_wide, moments, hot, grad_columns)
        product, partial_grad = combine(region, ready, [own, *near, *far], shapes)
        gradient, product = sum_parts(partial_grad, product, slabs, atom_devices)
        contracted = write(pattern, product)
        return contracted.reshape(basis.shape), gradient
    ready = relayout(in_hbm(flat_basis), in_hbm(flat_field), points, blocks)
    near, far, (basis_wide, field_wide) = swap_halves(near, ready, atom_devices)
    tiles, partial_grad = partial_gradient(
        region,
        pattern,
        basis_wide,
        field_wide,
        in_hbm(flat_grad),
        weights,
        weight_grad,
        fn_atom,
        batch_atom,
        [own, *near, *far],
        shapes,
    )
    gradient, basis_wide = sum_parts(partial_grad, basis_wide, slabs, atom_devices)
    contracted = contract(region, pattern, basis_wide, tiles, points, blocks, width)
    return contracted.reshape(basis.shape), gradient


def solution(mesh):
    placed = (
        P(("groups", "grid", "atoms"), None, None, None),
        P(None, ("groups", "grid", "atoms"), None, None, None),
        P(("groups", "grid", "atoms"), None, None, None),
        P(("groups", "grid", "atoms"), None),
        P(None, ("groups", "grid", "atoms"), None),
        P(("groups", "grid"), None, None, None),
        P("groups", None),
        P(("groups", "grid", "atoms"), None),
        P("groups"),
        P(("groups", "grid", "atoms")),
    )
    return jax.shard_map(
        local,
        mesh=mesh,
        in_specs=placed,
        out_specs=(P(("groups", "grid", "atoms"), None, None, None), P(None, ("groups", "atoms"))),
        check_vma=False,
    )
```

```python
import functools
import math

import jax
import jax.numpy as jnp
from jax import lax
from jax.experimental import pallas as pl
from jax.experimental.pallas import tpu as pltpu
from jax.sharding import PartitionSpec as P

TRAVEL = 5
PARTS = 3
F32 = jnp.float32
BF16 = jnp.bfloat16
NT = (((1,), (1,)), ((), ()))
VMEM_LIMIT = 32 * 1024 * 1024


def owner_and_slot(region, slab, position, owner_rows):
    owner = lax.div(region[slab, position], owner_rows)
    slot = jnp.int32(0)
    count = jnp.int32(0)
    for other in range(region.shape[1]):
        same = jnp.where(lax.div(region[slab, other], owner_rows) == owner, 1, 0)
        count = count + same
        slot = slot + jnp.where(other < position, same, 0)
    return owner, slot, count


def travel_place(slot, count, k):
    if k == 0:
        return jnp.where(slot == 0, 4, 2)
    if k == 1:
        return jnp.where(slot == 0, 0, 3)
    return jnp.where(jnp.logical_and(slot == 0, count == 2), 1, 4)


def partners(slabs):
    shifts = list(reversed(range(1, slabs)))
    pairs = [(shifts[i], shifts[i + 1]) for i in range(0, slabs - 2, 2)]
    return pairs + [(shifts[-1],) * 2]


def send_kernel(region_hbm, density, *rest):
    *outs, region, sems, region_sem = rest
    fetch = pltpu.make_async_copy(region_hbm, region, region_sem)
    fetch.start()
    fetch.wait()
    me = lax.axis_index("grid")
    core = lax.rem(lax.axis_index("atoms"), 2)
    slabs, size = region.shape
    owner_rows = density.shape[0]
    rows = density.shape[-2]
    copies = []
    for number, ((low, high), out) in enumerate(zip([(0, 0)] + partners(slabs), outs)):
        slab = jnp.bitwise_xor(me, jnp.where(core == 0, low, high))
        base = jnp.int32(owner_rows)
        count = jnp.int32(0)
        for position in range(size):
            row = region[slab, position] - me * owner_rows
            mine = jnp.logical_and(row >= 0, row < owner_rows)
            base = jnp.minimum(base, jnp.where(mine, row, owner_rows))
            count = count + jnp.where(mine, 1, 0)
        base = jnp.where(count == 0, 0, base)
        after = jnp.minimum(base + 1, owner_rows - 1)
        lower = base == 0
        edge = jnp.where(jnp.logical_and(count == 2, jnp.logical_not(lower)), after, base)
        kept = out.shape[1]
        first = 0 if kept == rows else pl.multiple_of(core * kept, kept)
        here = pl.ds(first, kept)
        pairs = (
            (density.at[base, pl.ds(1, 2), here, :], out.at[pl.ds(0, 2)]),
            (density.at[after, pl.ds(0, 2), here, :], out.at[pl.ds(2, 2)]),
            (density.at[edge, jnp.where(lower, 0, 2), here, :], out.at[4]),
        )
        for part, (source, target) in enumerate(pairs):
            copies.append(pltpu.make_async_copy(source, target, sems.at[number, part]))
    for copy in copies:
        copy.start()
    for copy in copies:
        copy.wait()


def in_hbm(array):
    return pltpu.with_memory_space_constraint(array, pltpu.HBM)


def rows_to_send(region, density, slabs):
    size = density.shape[-1]
    exchanges = partners(slabs)
    kept = [size] + [size if low != high else size // 2 for low, high in exchanges]
    hbm = pl.BlockSpec(memory_space=pl.ANY)
    return pl.pallas_call(
        send_kernel,
        out_shape=[jax.ShapeDtypeStruct((TRAVEL, rows, size), density.dtype) for rows in kept],
        in_specs=[hbm, hbm],
        out_specs=[pl.BlockSpec(memory_space=pltpu.VMEM)] * len(kept),
        scratch_shapes=[
            pltpu.SMEM(region.shape, jnp.int32),
            pltpu.SemaphoreType.DMA((len(kept), 3)),
            pltpu.SemaphoreType.DMA,
        ],
        compiler_params=pltpu.CompilerParams(vmem_limit_bytes=VMEM_LIMIT),
    )(in_hbm(region), in_hbm(density))


def fetch_rows(region, density, slabs, atom_devices):
    own, *outgoing = rows_to_send(region, density, slabs)
    near = []
    for shifts, piece in zip(partners(slabs), outgoing):
        moves = [
            (z * atom_devices + a, (z ^ shifts[a % 2]) * atom_devices + a) for z in range(slabs) for a in range(atom_devices)
        ]
        near.append(lax.ppermute(piece, ("grid", "atoms"), moves))
    return own, near


def stage_rows(stage, own, near, far, slabs):
    core = lax.rem(lax.axis_index("atoms"), 2)
    for place in range(TRAVEL):
        stage[place] = own[place]
    for (low, high), here, there in zip(partners(slabs), near, far):
        kept = here.shape[1]
        mine = jnp.where(core == 0, low, high) * TRAVEL
        other = jnp.where(core == 0, high, low) * TRAVEL
        for place in range(TRAVEL):
            if low != high:
                stage[mine + place] = here[place]
                stage[other + place] = there[place]
            else:
                stage[mine + place, pl.ds(pl.multiple_of(core * kept, kept), kept), :] = here[place]
                stage[mine + place, pl.ds(pl.multiple_of((1 - core) * kept, kept), kept), :] = there[place]


def block_major(x_ref, wide, points, blocks):
    wide[...] = x_ref[0].astype(F32)
    return [wide[pl.ds(s, points, stride=blocks), :] for s in range(blocks)]


def relayout_kernel(basis, field, basis_out, field_out, wide, *, points, blocks):
    size = basis.shape[-1]
    for source, target in ((basis, basis_out), (field, field_out)):
        for s, part in enumerate(block_major(source, wide, points, blocks)):
            target[0, :, s * size : (s + 1) * size] = part.astype(BF16)


def relayout(basis, field, points, blocks):
    batches, rows, size = basis.shape
    here = pl.BlockSpec((1, rows, size), lambda b: (b, 0, 0))
    there = pl.BlockSpec((1, points, blocks * size), lambda b: (b, 0, 0))
    shape = jax.ShapeDtypeStruct((batches, points, blocks * size), BF16)
    return pl.pallas_call(
        functools.partial(relayout_kernel, points=points, blocks=blocks),
        grid=(batches,),
        out_shape=(shape, shape),
        in_specs=[here, here],
        out_specs=(there, there),
        scratch_shapes=[pltpu.VMEM((rows, size), F32)],
        compiler_params=pltpu.CompilerParams(vmem_limit_bytes=VMEM_LIMIT),
        cost_estimate=pl.CostEstimate(flops=0, bytes_accessed=8 * batches * rows * size, transcendentals=0),
    )(basis, field)


def batch_matrix(region, pattern, tiles, slab, batch, blocks, width):
    half = (width - 1) // 2
    none = tiles.shape[0] - 1
    places = [pattern[batch, s] for s in range(blocks)]
    rows = [region[slab, place] for place in places]
    strips = []
    for s in range(blocks):
        strip = []
        for t in range(blocks):
            k = rows[t] - rows[s] + half
            inside = jnp.logical_and(k >= 0, k < width)
            strip.append(tiles[jnp.where(inside, places[s] * width + k, none)])
        strips.append(jnp.concatenate(strip, axis=1))
    return jnp.concatenate(strips, axis=0)


def split(values):
    high = values.astype(BF16)
    rest = values - high.astype(F32)
    middle = rest.astype(BF16)
    low = (rest - middle.astype(F32)).astype(BF16)
    return high, middle, low


def gradient_kernel(
    region,
    pattern,
    basis,
    field,
    basis_grad,
    weights,
    weight_grad,
    fn_atom,
    batch_atom,
    places,
    *rest,
    points,
    blocks,
    width,
    owner_rows,
    slabs,
):
    *pieces, tiles, out, stage, spread, sums, energy_sums = rest
    batch = pl.program_id(0)
    batches = pl.num_programs(0)
    me = lax.axis_index("grid")
    me_atoms = lax.axis_index("atoms")
    size = tiles.shape[-1]
    region_size = region.shape[1]

    @pl.when(batch == 0)
    def _():
        tiles[region_size * width] = jnp.zeros((size, size), BF16)
        stage_rows(stage, pieces[0], pieces[1 : 1 + slabs // 2], pieces[1 + slabs // 2 :], slabs)
        for position in range(region_size):
            owner, slot, count = owner_and_slot(region, me, position, owner_rows)
            shift = jnp.bitwise_xor(me, owner)
            for k in range(width):
                tiles[position * width + k] = stage[shift * TRAVEL + travel_place(slot, count, k)]

    matrix = batch_matrix(region, pattern, tiles, me, batch, blocks, width)
    potential = lax.dot_general(field[0], matrix, NT, preferred_element_type=F32)
    rows = jnp.concatenate(
        [weights[pl.ds(batch, 1), :]]
        + [weight_grad[c, pl.ds(batch, 1), :] for c in range(PARTS)]
        + [jnp.zeros((8 - 1 - PARTS, points), F32)],
        axis=0,
    )
    columns = rows.T
    weight = columns[:, 0:1]
    energy = jnp.zeros((points, size), F32)
    for s in range(blocks):
        here = potential[:, s * size : (s + 1) * size]
        energy = energy + basis[0, :, s * size : (s + 1) * size].astype(F32) * here
        spread[pl.ds(s, points, stride=blocks), :] = here * weight
    scaled = spread[...]
    place = pl.ds(pl.multiple_of(batch * 8, 8), 8)
    for c in range(PARTS):
        terms = basis_grad[c, 0].astype(F32) * scaled
        sums[c, place, :] = jnp.sum(terms.reshape(-1, 8, size), axis=0)
        terms = energy * columns[:, 1 + c : 2 + c]
        energy_sums[c, place, :] = jnp.sum(terms.reshape(-1, 8, size), axis=0)

    @pl.when(batch == batches - 1)
    def _():
        padded = max(8, region_size)
        chosen = lax.broadcasted_iota(jnp.int32, (padded, places.shape[1]), 0) == places[...]
        chosen = chosen.astype(BF16)
        blocks_sum = []
        for c in range(PARTS):
            total = jnp.zeros((padded, size), F32)
            for piece in split(sums[c]):
                total = total + jnp.dot(chosen, piece, preferred_element_type=F32)
            blocks_sum.append(-2.0 * total)
        lefts = []
        for position in range(region_size):
            stack = jnp.concatenate([total[position : position + 1] for total in blocks_sum], axis=0)
            high, middle, low = (piece.astype(F32) for piece in split(stack))
            lefts.append(jnp.concatenate([high, middle, low, jnp.zeros((16 - 3 * PARTS, size), F32)], axis=0))
        left = jnp.concatenate(lefts, axis=1).astype(BF16)
        chunk = out.shape[-1]
        scale = [jnp.sum(energy_sums[c], axis=1, keepdims=True) for c in range(PARTS)]
        for device in range(out.shape[0]):
            atoms = lax.broadcasted_iota(jnp.int32, (chunk, size), 0) + device * chunk
            hot = [
                jnp.where(atoms == fn_atom[pl.ds(region[me, position], 1), :], 1.0, 0.0).astype(BF16)
                for position in range(region_size)
            ]
            found = lax.dot_general(left, jnp.concatenate(hot, axis=1), NT, preferred_element_type=F32)
            atoms = lax.broadcasted_iota(jnp.int32, (batch_atom.shape[0], chunk), 1) + device * chunk
            mine = atoms == batch_atom[...]
            for c in range(PARTS):
                value = found[c : c + 1] + found[PARTS + c : PARTS + c + 1] + found[2 * PARTS + c : 2 * PARTS + c + 1]
                value = value + jnp.sum(jnp.where(mine, scale[c], 0.0), axis=0, keepdims=True)
                out[jnp.bitwise_xor(me_atoms, device), c : c + 1, :] = value


def partial_gradient(
    region, pattern, basis, field, basis_grad, weights, weight_grad, fn_atom, batch_atom, pieces, shapes
):
    slabs, atom_devices, atom_total, points, blocks, width, owner_rows = shapes
    batches, _, columns = basis.shape
    size = columns // blocks
    region_size = region.shape[1]
    fn_atom = fn_atom.reshape(-1, size)
    places = jnp.broadcast_to(pattern[:, None, :], (batches, 8 // blocks, blocks)).reshape(1, -1)
    batch_atom = jnp.broadcast_to(batch_atom[:, None], (batches, 8)).reshape(-1, 1)
    block = pl.BlockSpec((1, points, columns), lambda b, *_: (b, 0, 0))
    whole = pl.BlockSpec(memory_space=pltpu.VMEM)
    tile_shape = (region_size * width + 1, size, size)
    out_shape = (atom_devices, PARTS, atom_total // atom_devices)
    return pl.pallas_call(
        functools.partial(
            gradient_kernel, points=points, blocks=blocks, width=width, owner_rows=owner_rows, slabs=slabs
        ),
        grid_spec=pltpu.PrefetchScalarGridSpec(
            num_scalar_prefetch=2,
            grid=(batches,),
            in_specs=[
                block,
                block,
                pl.BlockSpec((PARTS, 1, points * blocks, size), lambda b, *_: (0, b, 0, 0)),
            ]
            + [whole] * (5 + len(pieces)),
            out_specs=(whole, whole),
            scratch_shapes=[
                pltpu.VMEM((slabs * TRAVEL, size, size), BF16),
                pltpu.VMEM((points * blocks, size), F32),
                pltpu.VMEM((PARTS, batches * 8, size), F32),
                pltpu.VMEM((PARTS, batches * 8, size), F32),
            ],
        ),
        out_shape=(jax.ShapeDtypeStruct(tile_shape, BF16), jax.ShapeDtypeStruct(out_shape, F32)),
        compiler_params=pltpu.CompilerParams(vmem_limit_bytes=VMEM_LIMIT),
    )(region, pattern, basis, field, basis_grad, weights, weight_grad, fn_atom, batch_atom, places, *pieces)


def product_kernel(region, pattern, basis, tiles, out, spread, *, points, blocks, width):
    me = lax.axis_index("grid")
    size = tiles.shape[-1]
    matrix = batch_matrix(region, pattern, tiles, me, pl.program_id(0), blocks, width)
    product = jnp.dot(basis[0], matrix, preferred_element_type=F32)
    for t in range(blocks):
        spread[pl.ds(t, points, stride=blocks), :] = product[:, t * size : (t + 1) * size]
    out[0] = spread[...].astype(BF16)


def contract(region, pattern, basis, tiles, points, blocks, width):
    batches, _, columns = basis.shape
    size = columns // blocks
    return pl.pallas_call(
        functools.partial(product_kernel, points=points, blocks=blocks, width=width),
        grid_spec=pltpu.PrefetchScalarGridSpec(
            num_scalar_prefetch=2,
            grid=(batches,),
            in_specs=[
                pl.BlockSpec((1, points, columns), lambda b, *_: (b, 0, 0)),
                pl.BlockSpec(memory_space=pltpu.VMEM),
            ],
            out_specs=pl.BlockSpec((1, points * blocks, size), lambda b, *_: (b, 0, 0)),
            scratch_shapes=[pltpu.VMEM((points * blocks, size), F32)],
        ),
        out_shape=jax.ShapeDtypeStruct((batches, points * blocks, size), BF16),
        compiler_params=pltpu.CompilerParams(vmem_limit_bytes=VMEM_LIMIT),
        cost_estimate=pl.CostEstimate(
            flops=2 * batches * points * columns * columns,
            bytes_accessed=4 * batches * points * columns,
            transcendentals=0,
        ),
    )(region, pattern, basis, tiles)


def reorder_kernel(
    pattern_hbm,
    basis,
    field,
    basis_grad,
    weights_hbm,
    basis_out,
    field_out,
    turned,
    grads,
    pattern,
    weights,
    basis_in,
    field_in,
    grad_in,
    wide,
    sems,
    small_sems,
):
    batches, blocks, points, size = basis_out.shape

    def copies(batch):
        return (
            pltpu.make_async_copy(field.at[batch], field_in.at[batch], sems.at[batch, 0]),
            pltpu.make_async_copy(basis.at[batch], basis_in.at[batch], sems.at[batch, 1]),
            pltpu.make_async_copy(basis_grad.at[:, batch], grad_in.at[:, batch], sems.at[batch, 2]),
        )

    small = (
        pltpu.make_async_copy(pattern_hbm, pattern, small_sems.at[0]),
        pltpu.make_async_copy(weights_hbm, weights, small_sems.at[1]),
    )
    for copy in small:
        copy.start()

    @pl.loop(0, batches)
    def _(batch):
        for copy in copies(batch):
            copy.start()

    for copy in small:
        copy.wait()

    @pl.loop(0, batches)
    def _(batch):
        for copy in copies(batch):
            copy.wait()
        points_here = pl.ds(pl.multiple_of(batch * points, points), points)
        places = [pattern[s, batch] for s in range(blocks)]
        weight = weights[pl.ds(batch, 1), :]
        wide[0] = field_in[batch].astype(F32)
        wide[1] = basis_in[batch].astype(F32)
        for c in range(PARTS):
            wide[2 + c] = grad_in[c, batch].astype(F32)
        for s, place in enumerate(places):
            strided = pl.ds(s, points, stride=blocks)
            values = wide[0, strided, :].astype(BF16)
            field_out[batch, place] = values
            rows = pl.ds(pl.multiple_of(place * size, size), size)
            turned[rows, points_here] = (values.T.astype(F32) * weight).astype(BF16)
            basis_out[batch, place] = wide[1, strided, :].astype(BF16)
            for c in range(PARTS):
                grads[c, place, points_here, :] = wide[2 + c, strided, :].astype(BF16)


def reorder(pattern, basis, field, basis_grad, weights, points, blocks):
    batches, rows, size = basis.shape
    hbm = pl.BlockSpec(memory_space=pl.ANY)
    vmem = pl.BlockSpec(memory_space=pltpu.VMEM)
    ordered = jax.ShapeDtypeStruct((batches, blocks, points, size), BF16)
    return pl.pallas_call(
        reorder_kernel,
        out_shape=(
            ordered,
            ordered,
            jax.ShapeDtypeStruct((blocks * size, batches * points), BF16),
            jax.ShapeDtypeStruct((PARTS, blocks, batches * points, size), BF16),
        ),
        in_specs=[hbm] * 5,
        out_specs=(vmem,) * 4,
        scratch_shapes=[
            pltpu.SMEM((blocks, batches), jnp.int32),
            pltpu.VMEM(weights.shape, F32),
            pltpu.VMEM((batches, rows, size), BF16),
            pltpu.VMEM((batches, rows, size), BF16),
            pltpu.VMEM((PARTS, batches, rows, size), BF16),
            pltpu.VMEM((2 + PARTS, rows, size), F32),
            pltpu.SemaphoreType.DMA((batches, 3)),
            pltpu.SemaphoreType.DMA((2,)),
        ],
        compiler_params=pltpu.CompilerParams(vmem_limit_bytes=VMEM_LIMIT),
        cost_estimate=pl.CostEstimate(
            flops=0, bytes_accessed=2 * (2 + PARTS) * batches * rows * size, transcendentals=0
        ),
    )(in_hbm(pattern.T), in_hbm(basis), in_hbm(field), in_hbm(basis_grad), in_hbm(weights))


def moment_kernel(turned, grads, moments):
    blocks, _, size = grads.shape[1:]
    for c in range(PARTS):
        for p in range(0, blocks, 2):
            rows = slice(max(p - 1, 0) * size, min(p + 3, blocks) * size)
            right = jnp.concatenate([grads[c, p], grads[c, p + 1]], axis=1)
            moments[c, rows, p * size : (p + 2) * size] = jnp.dot(
                turned[rows, :], right, preferred_element_type=F32
            )


def build_moments(turned, grads):
    blocks, depth, size = grads.shape[1:]
    vmem = pl.BlockSpec(memory_space=pltpu.VMEM)
    return pl.pallas_call(
        moment_kernel,
        out_shape=jax.ShapeDtypeStruct((PARTS, blocks * size, blocks * size), F32),
        in_specs=[vmem, vmem],
        out_specs=vmem,
        compiler_params=pltpu.CompilerParams(vmem_limit_bytes=VMEM_LIMIT),
        cost_estimate=pl.CostEstimate(
            flops=2 * PARTS * depth * (blocks * size) ** 2, bytes_accessed=0, transcendentals=0
        ),
    )(turned, grads)


def atom_kernel(region, fn_atom, batch_atom, weight_grad, hot, grad_columns):
    batches, points = weight_grad.shape[1:]
    size = fn_atom.shape[1]
    blocks = region.shape[1]
    me = lax.axis_index("grid")
    atoms = lax.broadcasted_iota(jnp.int32, (hot.shape[0], size), 0)
    ids = jnp.concatenate([batch_atom[...], jnp.full((1, size - batches), -1, jnp.int32)], axis=1)
    hot[:, blocks * size :] = jnp.where(atoms == ids, 1.0, 0.0).astype(BF16)

    @pl.loop(0, blocks)
    def _(position):
        ids = fn_atom[pl.ds(region[me, position], 1), :]
        columns = pl.ds(pl.multiple_of(position * size, size), size)
        hot[:, columns] = jnp.where(atoms == ids, 1.0, 0.0).astype(BF16)

    for c in range(PARTS):
        padding = jnp.zeros((size - batches, points), F32)
        grad_columns[c] = jnp.concatenate([weight_grad[c], padding], axis=0).T


def atom_matrix(region, fn_atom, batch_atom, weight_grad, blocks, size, atom_total):
    vmem = pl.BlockSpec(memory_space=pltpu.VMEM)
    return pl.pallas_call(
        atom_kernel,
        out_shape=(
            jax.ShapeDtypeStruct((atom_total, (blocks + 1) * size), BF16),
            jax.ShapeDtypeStruct((PARTS, weight_grad.shape[2], size), F32),
        ),
        in_specs=[pl.BlockSpec(memory_space=pltpu.SMEM)] + [vmem] * 3,
        out_specs=(vmem, vmem),
        compiler_params=pltpu.CompilerParams(vmem_limit_bytes=VMEM_LIMIT),
        cost_estimate=pl.CostEstimate(flops=1000000000, bytes_accessed=2 * atom_total * size, transcendentals=0),
    )(region, fn_atom.reshape(-1, size), batch_atom.reshape(1, -1), weight_grad)


def combine_kernel(
    region, basis, field, moments, hot, grad_columns, *rest, owner_rows, slabs, width, step
):
    *pieces, product_out, out, stage, matrix, energies = rest
    batches, blocks, points, size = basis.shape
    me = lax.axis_index("grid")
    me_atoms = lax.axis_index("atoms")
    half = (width - 1) // 2
    stage_rows(stage, pieces[0], pieces[1 : 1 + slabs // 2], pieces[1 + slabs // 2 :], slabs)
    rows = [region[me, position] for position in range(blocks)]
    found = [owner_and_slot(region, me, position, owner_rows) for position in range(blocks)]
    totals = [[jnp.zeros((8, size), F32) for _ in range(blocks)] for _ in range(PARTS)]
    for p in range(blocks):
        owner, slot, count = found[p]
        first = jnp.bitwise_xor(me, owner) * TRAVEL
        for q in range(blocks):
            if abs(q - p) > half:
                matrix[p * size : (p + 1) * size, q * size : (q + 1) * size] = jnp.zeros((size, size), BF16)
                continue
            k = rows[q] - rows[p] + half
            place = jnp.where(
                k == 0,
                travel_place(slot, count, 0),
                jnp.where(k == 1, travel_place(slot, count, 1), travel_place(slot, count, 2)),
            )
            inside = jnp.logical_and(k >= 0, k < width)
            tile = stage[first + place].astype(F32)
            tile = jnp.where(inside, tile, 0.0)
            matrix[p * size : (p + 1) * size, q * size : (q + 1) * size] = tile.astype(BF16)
            turned = tile.T
            for c in range(PARTS):
                terms = turned * moments[c, q * size : (q + 1) * size, p * size : (p + 1) * size]
                totals[c][p] = totals[c][p] + jnp.sum(terms.reshape(-1, 8, size), axis=0)
    derivative = [
        jnp.concatenate([jnp.sum(total, axis=0, keepdims=True) for total in totals[c]], axis=1) for c in range(PARTS)
    ]

    energies[...] = jnp.zeros_like(energies)
    lanes = lax.broadcasted_iota(jnp.int32, (points, size), 1)

    @pl.loop(0, batches // step)
    def _(group):
        left = [
            jnp.concatenate([basis[group * step + inner, p] for p in range(blocks)], axis=1) for inner in range(step)
        ]
        left = jnp.concatenate(left, axis=0)
        energy = [jnp.zeros((points, size), F32) for _ in range(step)]
        for q in range(0, blocks, 2):
            product = jnp.dot(left, matrix[:, q * size : (q + 2) * size], preferred_element_type=F32)
            for inner in range(step):
                batch = group * step + inner
                for column in range(2):
                    part = product[inner * points : (inner + 1) * points, column * size : (column + 1) * size]
                    product_out[batch, q + column] = part.astype(BF16)
                    energy[inner] = energy[inner] + part * field[batch, q + column].astype(F32)
        for inner in range(step):
            total = jnp.sum(energy[inner], axis=1, keepdims=True)
            energies[...] = jnp.where(lanes == group * step + inner, total, energies[...])

    lefts = []
    for c in range(PARTS):
        term = jnp.sum(energies[...] * grad_columns[c], axis=0, keepdims=True)
        lefts.append(jnp.concatenate([-2.0 * derivative[c], term], axis=1))
    left = jnp.concatenate(lefts, axis=0)
    high, middle, low = (piece.astype(F32) for piece in split(left))
    left = jnp.concatenate([high, middle, low, jnp.zeros((16 - 3 * PARTS, left.shape[1]), F32)], axis=0).astype(BF16)
    chunk = out.shape[-1]
    for device in range(out.shape[0]):
        sums = lax.dot_general(
            left, hot[device * chunk : (device + 1) * chunk, :], NT, preferred_element_type=F32
        )
        value = sums[:PARTS] + sums[PARTS : 2 * PARTS] + sums[2 * PARTS : 3 * PARTS]
        out[jnp.bitwise_xor(me_atoms, device)] = value


def combine(region, prepared, pieces, shapes):
    basis, field, moments, hot, grad_columns = prepared
    slabs, atom_devices, atom_total, points, blocks, width, owner_rows = shapes
    batches, _, _, size = basis.shape
    step = 16 if batches % 16 == 0 else 1
    vmem = pl.BlockSpec(memory_space=pltpu.VMEM)
    return pl.pallas_call(
        functools.partial(combine_kernel, owner_rows=owner_rows, slabs=slabs, width=width, step=step),
        out_shape=(
            jax.ShapeDtypeStruct(basis.shape, BF16),
            jax.ShapeDtypeStruct((atom_devices, PARTS, atom_total // atom_devices), F32),
        ),
        in_specs=[pl.BlockSpec(memory_space=pltpu.SMEM)] + [vmem] * (5 + len(pieces)),
        out_specs=(vmem, vmem),
        scratch_shapes=[
            pltpu.VMEM((slabs * TRAVEL, size, size), BF16),
            pltpu.VMEM((blocks * size, blocks * size), BF16),
            pltpu.VMEM((points, size), F32),
        ],
        compiler_params=pltpu.CompilerParams(vmem_limit_bytes=VMEM_LIMIT),
    )(region, basis, field, moments, hot, grad_columns, *pieces)


def write_kernel(pattern, product, out, wide, staged, sems):
    batches, blocks, points, size = product.shape

    def copy(batch):
        return pltpu.make_async_copy(staged.at[batch], out.at[batch], sems.at[batch])

    @pl.loop(0, batches // 2)
    def _(pair):
        for inner in range(2):
            batch = pair * 2 + inner
            for t in range(blocks):
                wide[inner, pl.ds(t, points, stride=blocks), :] = product[batch, pattern[t, batch]].astype(F32)
            staged[batch] = wide[inner].astype(BF16)
            copy(batch).start()

    @pl.loop(0, batches)
    def _(batch):
        copy(batch).wait()


def write(pattern, product):
    batches, blocks, points, size = product.shape
    shape = (batches, points * blocks, size)
    return pl.pallas_call(
        write_kernel,
        out_shape=jax.ShapeDtypeStruct(shape, BF16),
        in_specs=[pl.BlockSpec(memory_space=pltpu.SMEM), pl.BlockSpec(memory_space=pltpu.VMEM)],
        out_specs=pl.BlockSpec(memory_space=pl.ANY),
        scratch_shapes=[
            pltpu.VMEM((2, points * blocks, size), F32),
            pltpu.VMEM(shape, BF16),
            pltpu.SemaphoreType.DMA((batches,)),
        ],
        compiler_params=pltpu.CompilerParams(vmem_limit_bytes=VMEM_LIMIT),
        cost_estimate=pl.CostEstimate(flops=0, bytes_accessed=4 * math.prod(shape), transcendentals=0),
    )(pattern.T, product)


def swap_halves(near, ready, atom_devices):
    near, ready = lax.optimization_barrier((near, ready))
    swap = [(i, i ^ 1) for i in range(atom_devices)]
    return near, [lax.ppermute(piece, "atoms", swap) for piece in near], ready


def tree_sum(values):
    if len(values) == 1:
        return values[0]
    half = len(values) // 2
    return tree_sum(values[:half]) + tree_sum(values[half:])


def exchange_all(parts, axis, count):
    moved = {d: lax.ppermute(parts[d], axis, [(i, i ^ d) for i in range(count)]) for d in range(1, count)}
    return [parts[0]] + [moved[d] for d in range(1, count)]


def sum_parts(partial_grad, product, slabs, atom_devices):
    total = tree_sum(exchange_all([partial_grad[d] for d in range(atom_devices)], "atoms", atom_devices))
    total, product = lax.optimization_barrier((total, product))
    return tree_sum(exchange_all([total] * slabs, "grid", slabs)), product


def local(
    basis,
    basis_grad,
    exchange_field,
    weights,
    weight_grad,
    density,
    region,
    pattern,
    fn_atom,
    batch_atom,
):
    batches, points, blocks, size = basis.shape
    owner_rows, width = density.shape[:2]
    slabs = lax.axis_size("grid")
    atom_devices = lax.axis_size("atoms")
    atom_total = fn_atom.shape[0] // (10 * slabs * atom_devices) * slabs * atom_devices
    shapes = (slabs, atom_devices, atom_total, points, blocks, width, owner_rows)
    flat_basis = basis.reshape(batches, points * blocks, size)
    flat_field = exchange_field.reshape(batches, points * blocks, size)
    flat_grad = basis_grad.reshape(PARTS, batches, points * blocks, size)
    own, near = fetch_rows(region, density, slabs, atom_devices)
    if region.shape[1] == blocks:
        basis_wide, field_wide, turned, grads = reorder(
            pattern, flat_basis, flat_field, flat_grad, weights, points, blocks
        )
        ready = (basis_wide, field_wide, build_moments(turned, grads), batch_atom)
        near, far, (basis_wide, field_wide, moments, batch_atom) = swap_halves(near, ready, atom_devices)
        hot, grad_columns = atom_matrix(region, fn_atom, batch_atom, weight_grad, blocks, size, atom_total)
        ready = (basis_wide, field_wide, moments, hot, grad_columns)
        product, partial_grad = combine(region, ready, [own, *near, *far], shapes)
        gradient, product = sum_parts(partial_grad, product, slabs, atom_devices)
        contracted = write(pattern, product)
        return contracted.reshape(basis.shape), gradient
    ready = relayout(in_hbm(flat_basis), in_hbm(flat_field), points, blocks)
    near, far, (basis_wide, field_wide) = swap_halves(near, ready, atom_devices)
    tiles, partial_grad = partial_gradient(
        region,
        pattern,
        basis_wide,
        field_wide,
        in_hbm(flat_grad),
        weights,
        weight_grad,
        fn_atom,
        batch_atom,
        [own, *near, *far],
        shapes,
    )
    gradient, basis_wide = sum_parts(partial_grad, basis_wide, slabs, atom_devices)
    contracted = contract(region, pattern, basis_wide, tiles, points, blocks, width)
    return contracted.reshape(basis.shape), gradient


def solution(mesh):
    placed = (
        P(("groups", "grid", "atoms"), None, None, None),
        P(None, ("groups", "grid", "atoms"), None, None, None),
        P(("groups", "grid", "atoms"), None, None, None),
        P(("groups", "grid", "atoms"), None),
        P(None, ("groups", "grid", "atoms"), None),
        P(("groups", "grid"), None, None, None),
        P("groups", None),
        P(("groups", "grid", "atoms"), None),
        P("groups"),
        P(("groups", "grid", "atoms")),
    )
    return jax.shard_map(
        local,
        mesh=mesh,
        in_specs=placed,
        out_specs=(P(("groups", "grid", "atoms"), None, None, None), P(None, ("groups", "atoms"))),
        check_vma=False,
    )
```

```python
import functools
import math

import jax
import jax.numpy as jnp
from jax import lax
from jax.experimental import pallas as pl
from jax.experimental.pallas import tpu as pltpu
from jax.sharding import PartitionSpec as P

TRAVEL = 5
AHEAD = 2
PARTS = 3
F32 = jnp.float32
BF16 = jnp.bfloat16
NT = (((1,), (1,)), ((), ()))
VMEM_LIMIT = 32 * 1024 * 1024


def owner_and_slot(region, slab, position, owner_rows):
    owner = lax.div(region[slab, position], owner_rows)
    slot = jnp.int32(0)
    count = jnp.int32(0)
    for other in range(region.shape[1]):
        same = jnp.where(lax.div(region[slab, other], owner_rows) == owner, 1, 0)
        count = count + same
        slot = slot + jnp.where(other < position, same, 0)
    return owner, slot, count


def travel_place(slot, count, k):
    if k == 0:
        return jnp.where(slot == 0, 4, 2)
    if k == 1:
        return jnp.where(slot == 0, 0, 3)
    return jnp.where(jnp.logical_and(slot == 0, count == 2), 1, 4)


def partners(slabs):
    return [(1, 1)] + [(shift + 1, shift) for shift in range(2, slabs, 2)]


def send_kernel(region_hbm, density, pattern, weights, basis, field, basis_grad, *rest):
    *outs, first_pattern, first_weights, first_basis, first_field, first_grad, region, sems, other_sems = rest
    ahead = first_basis.shape[0]
    fetch = pltpu.make_async_copy(region_hbm, region, other_sems.at[0])
    fetch.start()
    others = (
        pltpu.make_async_copy(pattern, first_pattern, other_sems.at[1]),
        pltpu.make_async_copy(weights, first_weights, other_sems.at[2]),
        pltpu.make_async_copy(field.at[pl.ds(0, ahead)], first_field, other_sems.at[3]),
        pltpu.make_async_copy(basis.at[pl.ds(0, ahead)], first_basis, other_sems.at[4]),
        pltpu.make_async_copy(basis_grad.at[:, pl.ds(0, ahead)], first_grad, other_sems.at[5]),
    )
    fetch.wait()
    me = lax.axis_index("grid")
    core = lax.rem(lax.axis_index("atoms"), 2)
    slabs, size = region.shape
    owner_rows = density.shape[0]
    rows = density.shape[-2]
    copies = []
    for number, ((low, high), out) in enumerate(zip([(0, 0)] + partners(slabs), outs)):
        slab = jnp.bitwise_xor(me, jnp.where(core == 0, low, high))
        base = jnp.int32(owner_rows)
        count = jnp.int32(0)
        for position in range(size):
            row = region[slab, position] - me * owner_rows
            mine = jnp.logical_and(row >= 0, row < owner_rows)
            base = jnp.minimum(base, jnp.where(mine, row, owner_rows))
            count = count + jnp.where(mine, 1, 0)
        base = jnp.where(count == 0, 0, base)
        after = jnp.minimum(base + 1, owner_rows - 1)
        lower = base == 0
        edge = jnp.where(jnp.logical_and(count == 2, jnp.logical_not(lower)), after, base)
        kept = out.shape[1]
        first = 0 if kept == rows else pl.multiple_of(core * kept, kept)
        here = pl.ds(first, kept)
        pairs = (
            (density.at[base, pl.ds(1, 2), here, :], out.at[pl.ds(0, 2)]),
            (density.at[after, pl.ds(0, 2), here, :], out.at[pl.ds(2, 2)]),
            (density.at[edge, jnp.where(lower, 0, 2), here, :], out.at[4]),
        )
        for part, (source, target) in enumerate(pairs):
            copies.append(pltpu.make_async_copy(source, target, sems.at[number, part]))
    for copy in (*copies, *others):
        copy.start()
    for copy in (*copies, *others):
        copy.wait()


def in_hbm(array):
    return pltpu.with_memory_space_constraint(array, pltpu.HBM)


def rows_to_send(region, density, pattern, weights, basis, field, basis_grad, slabs):
    size = density.shape[-1]
    exchanges = partners(slabs)
    kept = [size] + [size if low != high else size // 2 for low, high in exchanges]
    ahead = jax.ShapeDtypeStruct((AHEAD, *basis.shape[1:]), BF16)
    operands = (region, density, pattern.T, weights, basis, field, basis_grad)
    return pl.pallas_call(
        send_kernel,
        out_shape=[
            *(jax.ShapeDtypeStruct((TRAVEL, rows, size), density.dtype) for rows in kept),
            jax.ShapeDtypeStruct(pattern.T.shape, jnp.int32),
            jax.ShapeDtypeStruct(weights.shape, F32),
            ahead,
            ahead,
            jax.ShapeDtypeStruct((PARTS, AHEAD, *basis.shape[1:]), BF16),
        ],
        in_specs=[pl.BlockSpec(memory_space=pl.ANY)] * len(operands),
        out_specs=[pl.BlockSpec(memory_space=pltpu.VMEM)] * (len(kept) + 5),
        scratch_shapes=[
            pltpu.SMEM(region.shape, jnp.int32),
            pltpu.SemaphoreType.DMA((len(kept), 3)),
            pltpu.SemaphoreType.DMA((6,)),
        ],
        compiler_params=pltpu.CompilerParams(vmem_limit_bytes=VMEM_LIMIT),
    )(*(in_hbm(operand) for operand in operands))


def fetch_rows(region, density, pattern, weights, basis, field, basis_grad, slabs, atom_devices):
    own, *rest = rows_to_send(region, density, pattern, weights, basis, field, basis_grad, slabs)
    outgoing, first = rest[: slabs // 2], rest[slabs // 2 :]
    near = []
    for shifts, piece in zip(partners(slabs), outgoing):
        moves = [
            (z * atom_devices + a, (z ^ shifts[a % 2]) * atom_devices + a) for z in range(slabs) for a in range(atom_devices)
        ]
        near.append(lax.ppermute(piece, ("grid", "atoms"), moves))
    return own, near, first


def stage_rows(stage, own, near, far, slabs):
    core = lax.rem(lax.axis_index("atoms"), 2)
    for place in range(TRAVEL):
        stage[place] = own[place]
    for (low, high), here, there in zip(partners(slabs), near, far):
        kept = here.shape[1]
        mine = jnp.where(core == 0, low, high) * TRAVEL
        other = jnp.where(core == 0, high, low) * TRAVEL
        for place in range(TRAVEL):
            if low != high:
                stage[mine + place] = here[place]
                stage[other + place] = there[place]
            else:
                stage[mine + place, pl.ds(pl.multiple_of(core * kept, kept), kept), :] = here[place]
                stage[mine + place, pl.ds(pl.multiple_of((1 - core) * kept, kept), kept), :] = there[place]


def block_major(x_ref, wide, points, blocks):
    wide[...] = x_ref[0].astype(F32)
    return [wide[pl.ds(s, points, stride=blocks), :] for s in range(blocks)]


def relayout_kernel(basis, field, basis_out, field_out, wide, *, points, blocks):
    size = basis.shape[-1]
    for source, target in ((basis, basis_out), (field, field_out)):
        for s, part in enumerate(block_major(source, wide, points, blocks)):
            target[0, :, s * size : (s + 1) * size] = part.astype(BF16)


def relayout(basis, field, points, blocks):
    batches, rows, size = basis.shape
    here = pl.BlockSpec((1, rows, size), lambda b: (b, 0, 0))
    there = pl.BlockSpec((1, points, blocks * size), lambda b: (b, 0, 0))
    shape = jax.ShapeDtypeStruct((batches, points, blocks * size), BF16)
    return pl.pallas_call(
        functools.partial(relayout_kernel, points=points, blocks=blocks),
        grid=(batches,),
        out_shape=(shape, shape),
        in_specs=[here, here],
        out_specs=(there, there),
        scratch_shapes=[pltpu.VMEM((rows, size), F32)],
        compiler_params=pltpu.CompilerParams(vmem_limit_bytes=VMEM_LIMIT),
        cost_estimate=pl.CostEstimate(flops=0, bytes_accessed=8 * batches * rows * size, transcendentals=0),
    )(basis, field)


def batch_matrix(region, pattern, tiles, slab, batch, blocks, width):
    half = (width - 1) // 2
    none = tiles.shape[0] - 1
    places = [pattern[batch, s] for s in range(blocks)]
    rows = [region[slab, place] for place in places]
    strips = []
    for s in range(blocks):
        strip = []
        for t in range(blocks):
            k = rows[t] - rows[s] + half
            inside = jnp.logical_and(k >= 0, k < width)
            strip.append(tiles[jnp.where(inside, places[s] * width + k, none)])
        strips.append(jnp.concatenate(strip, axis=1))
    return jnp.concatenate(strips, axis=0)


def split(values):
    high = values.astype(BF16)
    rest = values - high.astype(F32)
    middle = rest.astype(BF16)
    low = (rest - middle.astype(F32)).astype(BF16)
    return high, middle, low


def gradient_kernel(
    region,
    pattern,
    basis,
    field,
    basis_grad,
    weights,
    weight_grad,
    fn_atom,
    batch_atom,
    places,
    *rest,
    points,
    blocks,
    width,
    owner_rows,
    slabs,
):
    *pieces, tiles, out, stage, spread, sums, energy_sums = rest
    batch = pl.program_id(0)
    batches = pl.num_programs(0)
    me = lax.axis_index("grid")
    me_atoms = lax.axis_index("atoms")
    size = tiles.shape[-1]
    region_size = region.shape[1]

    @pl.when(batch == 0)
    def _():
        tiles[region_size * width] = jnp.zeros((size, size), BF16)
        stage_rows(stage, pieces[0], pieces[1 : 1 + slabs // 2], pieces[1 + slabs // 2 :], slabs)
        for position in range(region_size):
            owner, slot, count = owner_and_slot(region, me, position, owner_rows)
            shift = jnp.bitwise_xor(me, owner)
            for k in range(width):
                tiles[position * width + k] = stage[shift * TRAVEL + travel_place(slot, count, k)]

    matrix = batch_matrix(region, pattern, tiles, me, batch, blocks, width)
    potential = lax.dot_general(field[0], matrix, NT, preferred_element_type=F32)
    rows = jnp.concatenate(
        [weights[pl.ds(batch, 1), :]]
        + [weight_grad[c, pl.ds(batch, 1), :] for c in range(PARTS)]
        + [jnp.zeros((8 - 1 - PARTS, points), F32)],
        axis=0,
    )
    columns = rows.T
    weight = columns[:, 0:1]
    energy = jnp.zeros((points, size), F32)
    for s in range(blocks):
        here = potential[:, s * size : (s + 1) * size]
        energy = energy + basis[0, :, s * size : (s + 1) * size].astype(F32) * here
        spread[pl.ds(s, points, stride=blocks), :] = here * weight
    scaled = spread[...]
    place = pl.ds(pl.multiple_of(batch * 8, 8), 8)
    for c in range(PARTS):
        terms = basis_grad[c, 0].astype(F32) * scaled
        sums[c, place, :] = jnp.sum(terms.reshape(-1, 8, size), axis=0)
        terms = energy * columns[:, 1 + c : 2 + c]
        energy_sums[c, place, :] = jnp.sum(terms.reshape(-1, 8, size), axis=0)

    @pl.when(batch == batches - 1)
    def _():
        padded = max(8, region_size)
        chosen = lax.broadcasted_iota(jnp.int32, (padded, places.shape[1]), 0) == places[...]
        chosen = chosen.astype(BF16)
        blocks_sum = []
        for c in range(PARTS):
            total = jnp.zeros((padded, size), F32)
            for piece in split(sums[c]):
                total = total + jnp.dot(chosen, piece, preferred_element_type=F32)
            blocks_sum.append(-2.0 * total)
        lefts = []
        for position in range(region_size):
            stack = jnp.concatenate([total[position : position + 1] for total in blocks_sum], axis=0)
            high, middle, low = (piece.astype(F32) for piece in split(stack))
            lefts.append(jnp.concatenate([high, middle, low, jnp.zeros((16 - 3 * PARTS, size), F32)], axis=0))
        left = jnp.concatenate(lefts, axis=1).astype(BF16)
        chunk = out.shape[-1]
        scale = [jnp.sum(energy_sums[c], axis=1, keepdims=True) for c in range(PARTS)]
        for device in range(out.shape[0]):
            atoms = lax.broadcasted_iota(jnp.int32, (chunk, size), 0) + device * chunk
            hot = [
                jnp.where(atoms == fn_atom[pl.ds(region[me, position], 1), :], 1.0, 0.0).astype(BF16)
                for position in range(region_size)
            ]
            found = lax.dot_general(left, jnp.concatenate(hot, axis=1), NT, preferred_element_type=F32)
            atoms = lax.broadcasted_iota(jnp.int32, (batch_atom.shape[0], chunk), 1) + device * chunk
            mine = atoms == batch_atom[...]
            for c in range(PARTS):
                value = found[c : c + 1] + found[PARTS + c : PARTS + c + 1] + found[2 * PARTS + c : 2 * PARTS + c + 1]
                value = value + jnp.sum(jnp.where(mine, scale[c], 0.0), axis=0, keepdims=True)
                out[jnp.bitwise_xor(me_atoms, device), c : c + 1, :] = value


def partial_gradient(
    region, pattern, basis, field, basis_grad, weights, weight_grad, fn_atom, batch_atom, pieces, shapes
):
    slabs, atom_devices, atom_total, points, blocks, width, owner_rows = shapes
    batches, _, columns = basis.shape
    size = columns // blocks
    region_size = region.shape[1]
    fn_atom = fn_atom.reshape(-1, size)
    places = jnp.broadcast_to(pattern[:, None, :], (batches, 8 // blocks, blocks)).reshape(1, -1)
    batch_atom = jnp.broadcast_to(batch_atom[:, None], (batches, 8)).reshape(-1, 1)
    block = pl.BlockSpec((1, points, columns), lambda b, *_: (b, 0, 0))
    whole = pl.BlockSpec(memory_space=pltpu.VMEM)
    tile_shape = (region_size * width + 1, size, size)
    out_shape = (atom_devices, PARTS, atom_total // atom_devices)
    return pl.pallas_call(
        functools.partial(
            gradient_kernel, points=points, blocks=blocks, width=width, owner_rows=owner_rows, slabs=slabs
        ),
        grid_spec=pltpu.PrefetchScalarGridSpec(
            num_scalar_prefetch=2,
            grid=(batches,),
            in_specs=[
                block,
                block,
                pl.BlockSpec((PARTS, 1, points * blocks, size), lambda b, *_: (0, b, 0, 0)),
            ]
            + [whole] * (5 + len(pieces)),
            out_specs=(whole, whole),
            scratch_shapes=[
                pltpu.VMEM((slabs * TRAVEL, size, size), BF16),
                pltpu.VMEM((points * blocks, size), F32),
                pltpu.VMEM((PARTS, batches * 8, size), F32),
                pltpu.VMEM((PARTS, batches * 8, size), F32),
            ],
        ),
        out_shape=(jax.ShapeDtypeStruct(tile_shape, BF16), jax.ShapeDtypeStruct(out_shape, F32)),
        compiler_params=pltpu.CompilerParams(vmem_limit_bytes=VMEM_LIMIT),
    )(region, pattern, basis, field, basis_grad, weights, weight_grad, fn_atom, batch_atom, places, *pieces)


def product_kernel(region, pattern, basis, tiles, out, spread, *, points, blocks, width):
    me = lax.axis_index("grid")
    size = tiles.shape[-1]
    matrix = batch_matrix(region, pattern, tiles, me, pl.program_id(0), blocks, width)
    product = jnp.dot(basis[0], matrix, preferred_element_type=F32)
    for t in range(blocks):
        spread[pl.ds(t, points, stride=blocks), :] = product[:, t * size : (t + 1) * size]
    out[0] = spread[...].astype(BF16)


def contract(region, pattern, basis, tiles, points, blocks, width):
    batches, _, columns = basis.shape
    size = columns // blocks
    return pl.pallas_call(
        functools.partial(product_kernel, points=points, blocks=blocks, width=width),
        grid_spec=pltpu.PrefetchScalarGridSpec(
            num_scalar_prefetch=2,
            grid=(batches,),
            in_specs=[
                pl.BlockSpec((1, points, columns), lambda b, *_: (b, 0, 0)),
                pl.BlockSpec(memory_space=pltpu.VMEM),
            ],
            out_specs=pl.BlockSpec((1, points * blocks, size), lambda b, *_: (b, 0, 0)),
            scratch_shapes=[pltpu.VMEM((points * blocks, size), F32)],
        ),
        out_shape=jax.ShapeDtypeStruct((batches, points * blocks, size), BF16),
        compiler_params=pltpu.CompilerParams(vmem_limit_bytes=VMEM_LIMIT),
        cost_estimate=pl.CostEstimate(
            flops=2 * batches * points * columns * columns,
            bytes_accessed=4 * batches * points * columns,
            transcendentals=0,
        ),
    )(region, pattern, basis, tiles)


def reorder_kernel(
    basis,
    field,
    basis_grad,
    pattern,
    weights,
    first_basis,
    first_field,
    first_grad,
    basis_out,
    field_out,
    turned,
    grads,
    basis_in,
    field_in,
    grad_in,
    wide,
    sems,
):
    batches, blocks, points, size = basis_out.shape

    def copies(batch):
        return (
            pltpu.make_async_copy(field.at[batch], field_in.at[batch], sems.at[batch, 0]),
            pltpu.make_async_copy(basis.at[batch], basis_in.at[batch], sems.at[batch, 1]),
            pltpu.make_async_copy(basis_grad.at[:, batch], grad_in.at[:, batch], sems.at[batch, 2]),
        )

    @pl.loop(AHEAD, batches)
    def _(batch):
        for copy in copies(batch):
            copy.start()

    def put_in_order(batch, field_here, basis_here, grads_here):
        points_here = pl.ds(pl.multiple_of(batch * points, points), points)
        places = [pattern[s, batch] for s in range(blocks)]
        weight = weights[pl.ds(batch, 1), :]
        wide[0] = field_here[...].astype(F32)
        wide[1] = basis_here[...].astype(F32)
        for c in range(PARTS):
            wide[2 + c] = grads_here[c].astype(F32)
        for s, place in enumerate(places):
            strided = pl.ds(s, points, stride=blocks)
            values = wide[0, strided, :].astype(BF16)
            field_out[batch, place] = values
            rows = pl.ds(pl.multiple_of(place * size, size), size)
            turned[rows, points_here] = (values.T.astype(F32) * weight).astype(BF16)
            basis_out[batch, place] = wide[1, strided, :].astype(BF16)
            for c in range(PARTS):
                grads[c, place, points_here, :] = wide[2 + c, strided, :].astype(BF16)

    @pl.loop(0, AHEAD)
    def _(batch):
        put_in_order(batch, first_field.at[batch], first_basis.at[batch], first_grad.at[:, batch])

    @pl.loop(AHEAD, batches)
    def _(batch):
        for copy in copies(batch):
            copy.wait()
        put_in_order(batch, field_in.at[batch], basis_in.at[batch], grad_in.at[:, batch])


def reorder(basis, field, basis_grad, first, points, blocks):
    batches, rows, size = basis.shape
    hbm = pl.BlockSpec(memory_space=pl.ANY)
    vmem = pl.BlockSpec(memory_space=pltpu.VMEM)
    ordered = jax.ShapeDtypeStruct((batches, blocks, points, size), BF16)
    return pl.pallas_call(
        reorder_kernel,
        out_shape=(
            ordered,
            ordered,
            jax.ShapeDtypeStruct((blocks * size, batches * points), BF16),
            jax.ShapeDtypeStruct((PARTS, blocks, batches * points, size), BF16),
        ),
        in_specs=[hbm] * 3 + [pl.BlockSpec(memory_space=pltpu.SMEM)] + [vmem] * 4,
        out_specs=(vmem,) * 4,
        scratch_shapes=[
            pltpu.VMEM((batches, rows, size), BF16),
            pltpu.VMEM((batches, rows, size), BF16),
            pltpu.VMEM((PARTS, batches, rows, size), BF16),
            pltpu.VMEM((2 + PARTS, rows, size), F32),
            pltpu.SemaphoreType.DMA((batches, 3)),
        ],
        compiler_params=pltpu.CompilerParams(vmem_limit_bytes=VMEM_LIMIT),
        cost_estimate=pl.CostEstimate(
            flops=0, bytes_accessed=2 * (2 + PARTS) * batches * rows * size, transcendentals=0
        ),
    )(in_hbm(basis), in_hbm(field), in_hbm(basis_grad), *first)


def moment_kernel(turned, grads, moments):
    blocks, _, size = grads.shape[1:]
    for c in range(PARTS):
        for p in range(0, blocks, 2):
            rows = slice(max(p - 1, 0) * size, min(p + 3, blocks) * size)
            right = jnp.concatenate([grads[c, p], grads[c, p + 1]], axis=1)
            moments[c, rows, p * size : (p + 2) * size] = jnp.dot(
                turned[rows, :], right, preferred_element_type=F32
            )


def build_moments(turned, grads):
    blocks, depth, size = grads.shape[1:]
    vmem = pl.BlockSpec(memory_space=pltpu.VMEM)
    return pl.pallas_call(
        moment_kernel,
        out_shape=jax.ShapeDtypeStruct((PARTS, blocks * size, blocks * size), F32),
        in_specs=[vmem, vmem],
        out_specs=vmem,
        compiler_params=pltpu.CompilerParams(vmem_limit_bytes=VMEM_LIMIT),
        cost_estimate=pl.CostEstimate(
            flops=2 * PARTS * depth * (blocks * size) ** 2, bytes_accessed=0, transcendentals=0
        ),
    )(turned, grads)


def atom_kernel(region, fn_atom, batch_atom, weight_grad, hot, grad_columns):
    batches, points = weight_grad.shape[1:]
    size = fn_atom.shape[1]
    blocks = region.shape[1]
    me = lax.axis_index("grid")
    atoms = lax.broadcasted_iota(jnp.int32, (hot.shape[0], size), 0)
    ids = jnp.concatenate([batch_atom[...], jnp.full((1, size - batches), -1, jnp.int32)], axis=1)
    hot[:, blocks * size :] = jnp.where(atoms == ids, 1.0, 0.0).astype(BF16)

    @pl.loop(0, blocks)
    def _(position):
        ids = fn_atom[pl.ds(region[me, position], 1), :]
        columns = pl.ds(pl.multiple_of(position * size, size), size)
        hot[:, columns] = jnp.where(atoms == ids, 1.0, 0.0).astype(BF16)

    for c in range(PARTS):
        padding = jnp.zeros((size - batches, points), F32)
        grad_columns[c] = jnp.concatenate([weight_grad[c], padding], axis=0).T


def atom_matrix(region, fn_atom, batch_atom, weight_grad, blocks, size, atom_total):
    vmem = pl.BlockSpec(memory_space=pltpu.VMEM)
    return pl.pallas_call(
        atom_kernel,
        out_shape=(
            jax.ShapeDtypeStruct((atom_total, (blocks + 1) * size), BF16),
            jax.ShapeDtypeStruct((PARTS, weight_grad.shape[2], size), F32),
        ),
        in_specs=[pl.BlockSpec(memory_space=pltpu.SMEM)] + [vmem] * 3,
        out_specs=(vmem, vmem),
        compiler_params=pltpu.CompilerParams(vmem_limit_bytes=VMEM_LIMIT),
        cost_estimate=pl.CostEstimate(flops=1000000000, bytes_accessed=2 * atom_total * size, transcendentals=0),
    )(region, fn_atom.reshape(-1, size), batch_atom.reshape(1, -1), weight_grad)


def combine_kernel(
    region, basis, field, moments, hot, grad_columns, *rest, owner_rows, slabs, width, step
):
    *pieces, product_out, out, stage, matrix, energies = rest
    batches, blocks, points, size = basis.shape
    me = lax.axis_index("grid")
    me_atoms = lax.axis_index("atoms")
    half = (width - 1) // 2
    stage_rows(stage, pieces[0], pieces[1 : 1 + slabs // 2], pieces[1 + slabs // 2 :], slabs)
    rows = [region[me, position] for position in range(blocks)]
    found = [owner_and_slot(region, me, position, owner_rows) for position in range(blocks)]
    totals = [[jnp.zeros((8, size), F32) for _ in range(blocks)] for _ in range(PARTS)]
    for p in range(blocks):
        owner, slot, count = found[p]
        first = jnp.bitwise_xor(me, owner) * TRAVEL
        for q in range(blocks):
            if abs(q - p) > half:
                matrix[p * size : (p + 1) * size, q * size : (q + 1) * size] = jnp.zeros((size, size), BF16)
                continue
            k = rows[q] - rows[p] + half
            place = jnp.where(
                k == 0,
                travel_place(slot, count, 0),
                jnp.where(k == 1, travel_place(slot, count, 1), travel_place(slot, count, 2)),
            )
            inside = jnp.logical_and(k >= 0, k < width)
            tile = jnp.where(inside, stage[first + place], jnp.zeros((size, size), BF16))
            matrix[p * size : (p + 1) * size, q * size : (q + 1) * size] = tile
            turned = tile.T.astype(F32)
            for c in range(PARTS):
                terms = turned * moments[c, q * size : (q + 1) * size, p * size : (p + 1) * size]
                totals[c][p] = totals[c][p] + jnp.sum(terms.reshape(-1, 8, size), axis=0)
    derivative = [
        jnp.concatenate([jnp.sum(total, axis=0, keepdims=True) for total in totals[c]], axis=1) for c in range(PARTS)
    ]

    energies[...] = jnp.zeros_like(energies)
    lanes = lax.broadcasted_iota(jnp.int32, (points, size), 1)

    @pl.loop(0, batches // step)
    def _(group):
        left = [
            jnp.concatenate([basis[group * step + inner, p] for p in range(blocks)], axis=1) for inner in range(step)
        ]
        left = jnp.concatenate(left, axis=0)
        energy = [jnp.zeros((points, size), F32) for _ in range(step)]
        for q in range(0, blocks, 2):
            product = jnp.dot(left, matrix[:, q * size : (q + 2) * size], preferred_element_type=F32)
            for inner in range(step):
                batch = group * step + inner
                for column in range(2):
                    part = product[inner * points : (inner + 1) * points, column * size : (column + 1) * size]
                    product_out[batch, q + column] = part.astype(BF16)
                    energy[inner] = energy[inner] + part * field[batch, q + column].astype(F32)
        for inner in range(step):
            total = jnp.sum(energy[inner], axis=1, keepdims=True)
            energies[...] = jnp.where(lanes == group * step + inner, total, energies[...])

    lefts = []
    for c in range(PARTS):
        term = jnp.sum(energies[...] * grad_columns[c], axis=0, keepdims=True)
        lefts.append(jnp.concatenate([-2.0 * derivative[c], term], axis=1))
    left = jnp.concatenate(lefts, axis=0)
    high, middle, low = (piece.astype(F32) for piece in split(left))
    left = jnp.concatenate([high, middle, low, jnp.zeros((16 - 3 * PARTS, left.shape[1]), F32)], axis=0).astype(BF16)
    chunk = out.shape[-1]
    for device in range(out.shape[0]):
        sums = lax.dot_general(
            left, hot[device * chunk : (device + 1) * chunk, :], NT, preferred_element_type=F32
        )
        value = sums[:PARTS] + sums[PARTS : 2 * PARTS] + sums[2 * PARTS : 3 * PARTS]
        out[jnp.bitwise_xor(me_atoms, device)] = value


def combine(region, prepared, pieces, shapes):
    basis, field, moments, hot, grad_columns = prepared
    slabs, atom_devices, atom_total, points, blocks, width, owner_rows = shapes
    batches, _, _, size = basis.shape
    step = 16 if batches % 16 == 0 else 1
    vmem = pl.BlockSpec(memory_space=pltpu.VMEM)
    return pl.pallas_call(
        functools.partial(combine_kernel, owner_rows=owner_rows, slabs=slabs, width=width, step=step),
        out_shape=(
            jax.ShapeDtypeStruct(basis.shape, BF16),
            jax.ShapeDtypeStruct((atom_devices, PARTS, atom_total // atom_devices), F32),
        ),
        in_specs=[pl.BlockSpec(memory_space=pltpu.SMEM)] + [vmem] * (5 + len(pieces)),
        out_specs=(vmem, vmem),
        scratch_shapes=[
            pltpu.VMEM((slabs * TRAVEL, size, size), BF16),
            pltpu.VMEM((blocks * size, blocks * size), BF16),
            pltpu.VMEM((points, size), F32),
        ],
        compiler_params=pltpu.CompilerParams(vmem_limit_bytes=VMEM_LIMIT),
    )(region, basis, field, moments, hot, grad_columns, *pieces)


def write_kernel(pattern, product, out, wide, staged, sems):
    batches, blocks, points, size = product.shape

    def copy(batch):
        return pltpu.make_async_copy(staged.at[batch], out.at[batch], sems.at[batch])

    @pl.loop(0, batches // 2)
    def _(pair):
        for inner in range(2):
            batch = pair * 2 + inner
            for t in range(blocks):
                wide[inner, pl.ds(t, points, stride=blocks), :] = product[batch, pattern[t, batch]].astype(F32)
            staged[batch] = wide[inner].astype(BF16)
            copy(batch).start()

    @pl.loop(0, batches)
    def _(batch):
        copy(batch).wait()


def write(pattern, product):
    batches, blocks, points, size = product.shape
    shape = (batches, points * blocks, size)
    return pl.pallas_call(
        write_kernel,
        out_shape=jax.ShapeDtypeStruct(shape, BF16),
        in_specs=[pl.BlockSpec(memory_space=pltpu.SMEM), pl.BlockSpec(memory_space=pltpu.VMEM)],
        out_specs=pl.BlockSpec(memory_space=pl.ANY),
        scratch_shapes=[
            pltpu.VMEM((2, points * blocks, size), F32),
            pltpu.VMEM(shape, BF16),
            pltpu.SemaphoreType.DMA((batches,)),
        ],
        compiler_params=pltpu.CompilerParams(vmem_limit_bytes=VMEM_LIMIT),
        cost_estimate=pl.CostEstimate(flops=0, bytes_accessed=4 * math.prod(shape), transcendentals=0),
    )(pattern.T, product)


def swap_halves(near, ready, atom_devices):
    near, ready = lax.optimization_barrier((near, ready))
    swap = [(i, i ^ 1) for i in range(atom_devices)]
    return near, [lax.ppermute(piece, "atoms", swap) for piece in near], ready


def tree_sum(values):
    if len(values) == 1:
        return values[0]
    half = len(values) // 2
    return tree_sum(values[:half]) + tree_sum(values[half:])


def exchange_all(parts, axis, count):
    farthest_first = range(count - 1, 0, -1)
    return [parts[0]] + [lax.ppermute(parts[d], axis, [(i, i ^ d) for i in range(count)]) for d in farthest_first]


def sum_parts(partial_grad, product, slabs, atom_devices):
    total = tree_sum(exchange_all([partial_grad[d] for d in range(atom_devices)], "atoms", atom_devices))
    total, product = lax.optimization_barrier((total, product))
    return tree_sum(exchange_all([total] * slabs, "grid", slabs)), product


def local(
    basis,
    basis_grad,
    exchange_field,
    weights,
    weight_grad,
    density,
    region,
    pattern,
    fn_atom,
    batch_atom,
):
    batches, points, blocks, size = basis.shape
    owner_rows, width = density.shape[:2]
    slabs = lax.axis_size("grid")
    atom_devices = lax.axis_size("atoms")
    atom_total = fn_atom.shape[0] // (10 * slabs * atom_devices) * slabs * atom_devices
    shapes = (slabs, atom_devices, atom_total, points, blocks, width, owner_rows)
    flat_basis = basis.reshape(batches, points * blocks, size)
    flat_field = exchange_field.reshape(batches, points * blocks, size)
    flat_grad = basis_grad.reshape(PARTS, batches, points * blocks, size)
    own, near, first = fetch_rows(
        region, density, pattern, weights, flat_basis, flat_field, flat_grad, slabs, atom_devices
    )
    if region.shape[1] == blocks:
        basis_wide, field_wide, turned, grads = reorder(flat_basis, flat_field, flat_grad, first, points, blocks)
        ready = (basis_wide, field_wide, build_moments(turned, grads), batch_atom)
        near, far, (basis_wide, field_wide, moments, batch_atom) = swap_halves(near, ready, atom_devices)
        hot, grad_columns = atom_matrix(region, fn_atom, batch_atom, weight_grad, blocks, size, atom_total)
        ready = (basis_wide, field_wide, moments, hot, grad_columns)
        product, partial_grad = combine(region, ready, [own, *near, *far], shapes)
        gradient, product = sum_parts(partial_grad, product, slabs, atom_devices)
        contracted = write(pattern, product)
        return contracted.reshape(basis.shape), gradient
    ready = relayout(in_hbm(flat_basis), in_hbm(flat_field), points, blocks)
    near, far, (basis_wide, field_wide) = swap_halves(near, ready, atom_devices)
    tiles, partial_grad = partial_gradient(
        region,
        pattern,
        basis_wide,
        field_wide,
        in_hbm(flat_grad),
        weights,
        weight_grad,
        fn_atom,
        batch_atom,
        [own, *near, *far],
        shapes,
    )
    gradient, basis_wide = sum_parts(partial_grad, basis_wide, slabs, atom_devices)
    contracted = contract(region, pattern, basis_wide, tiles, points, blocks, width)
    return contracted.reshape(basis.shape), gradient


def solution(mesh):
    placed = (
        P(("groups", "grid", "atoms"), None, None, None),
        P(None, ("groups", "grid", "atoms"), None, None, None),
        P(("groups", "grid", "atoms"), None, None, None),
        P(("groups", "grid", "atoms"), None),
        P(None, ("groups", "grid", "atoms"), None),
        P(("groups", "grid"), None, None, None),
        P("groups", None),
        P(("groups", "grid", "atoms"), None),
        P("groups"),
        P(("groups", "grid", "atoms")),
    )
    return jax.shard_map(
        local,
        mesh=mesh,
        in_specs=placed,
        out_specs=(P(("groups", "grid", "atoms"), None, None, None), P(None, ("groups", "atoms"))),
        check_vma=False,
    )
```

```python
import functools
import math

import jax
import jax.numpy as jnp
from jax import lax
from jax.experimental import pallas as pl
from jax.experimental.pallas import tpu as pltpu
from jax.sharding import PartitionSpec as P

TRAVEL = 5
PARTS = 3
F32 = jnp.float32
BF16 = jnp.bfloat16
NT = (((1,), (1,)), ((), ()))
TN = (((0,), (0,)), ((), ()))
VMEM_LIMIT = 32 * 1024 * 1024


def owner_and_slot(region, slab, position, owner_rows):
    owner = lax.div(region[slab, position], owner_rows)
    slot = jnp.int32(0)
    count = jnp.int32(0)
    for other in range(region.shape[1]):
        same = jnp.where(lax.div(region[slab, other], owner_rows) == owner, 1, 0)
        count = count + same
        slot = slot + jnp.where(other < position, same, 0)
    return owner, slot, count


def travel_place(slot, count, k):
    if k == 0:
        return jnp.where(slot == 0, 4, 2)
    if k == 1:
        return jnp.where(slot == 0, 0, 3)
    return jnp.where(jnp.logical_and(slot == 0, count == 2), 1, 4)


def partners(slabs):
    return [(1, 1)] + [(shift + 1, shift) for shift in range(2, slabs, 2)]


def send_kernel(region_hbm, density, *rest):
    *outs, region, sems, region_sem = rest
    fetch = pltpu.make_async_copy(region_hbm, region, region_sem)
    fetch.start()
    fetch.wait()
    me = lax.axis_index("grid")
    core = lax.rem(lax.axis_index("atoms"), 2)
    slabs, size = region.shape
    owner_rows = density.shape[0]
    rows = density.shape[-2]
    copies = []
    for number, ((low, high), out) in enumerate(zip([(0, 0)] + partners(slabs), outs)):
        slab = jnp.bitwise_xor(me, jnp.where(core == 0, low, high))
        base = jnp.int32(owner_rows)
        count = jnp.int32(0)
        for position in range(size):
            row = region[slab, position] - me * owner_rows
            mine = jnp.logical_and(row >= 0, row < owner_rows)
            base = jnp.minimum(base, jnp.where(mine, row, owner_rows))
            count = count + jnp.where(mine, 1, 0)
        base = jnp.where(count == 0, 0, base)
        after = jnp.minimum(base + 1, owner_rows - 1)
        lower = base == 0
        edge = jnp.where(jnp.logical_and(count == 2, jnp.logical_not(lower)), after, base)
        kept = out.shape[1]
        first = 0 if kept == rows else pl.multiple_of(core * kept, kept)
        here = pl.ds(first, kept)
        pairs = (
            (density.at[base, pl.ds(1, 2), here, :], out.at[pl.ds(0, 2)]),
            (density.at[after, pl.ds(0, 2), here, :], out.at[pl.ds(2, 2)]),
            (density.at[edge, jnp.where(lower, 0, 2), here, :], out.at[4]),
        )
        for part, (source, target) in enumerate(pairs):
            copies.append(pltpu.make_async_copy(source, target, sems.at[number, part]))
    for copy in copies:
        copy.start()
    for copy in copies:
        copy.wait()


def in_hbm(array):
    return pltpu.with_memory_space_constraint(array, pltpu.HBM)


def rows_to_send(region, density, slabs):
    size = density.shape[-1]
    exchanges = partners(slabs)
    kept = [size] + [size if low != high else size // 2 for low, high in exchanges]
    hbm = pl.BlockSpec(memory_space=pl.ANY)
    return pl.pallas_call(
        send_kernel,
        out_shape=[jax.ShapeDtypeStruct((TRAVEL, rows, size), density.dtype) for rows in kept],
        in_specs=[hbm, hbm],
        out_specs=[pl.BlockSpec(memory_space=pltpu.VMEM)] * len(kept),
        scratch_shapes=[
            pltpu.SMEM(region.shape, jnp.int32),
            pltpu.SemaphoreType.DMA((len(kept), 3)),
            pltpu.SemaphoreType.DMA,
        ],
        compiler_params=pltpu.CompilerParams(vmem_limit_bytes=VMEM_LIMIT),
    )(in_hbm(region), in_hbm(density))


def fetch_rows(region, density, slabs, atom_devices):
    own, *outgoing = rows_to_send(region, density, slabs)
    near = []
    for shifts, piece in zip(partners(slabs), outgoing):
        moves = [
            (z * atom_devices + a, (z ^ shifts[a % 2]) * atom_devices + a) for z in range(slabs) for a in range(atom_devices)
        ]
        near.append(lax.ppermute(piece, ("grid", "atoms"), moves))
    return own, near


def stage_rows(stage, own, near, far, slabs):
    core = lax.rem(lax.axis_index("atoms"), 2)
    for place in range(TRAVEL):
        stage[place] = own[place]
    for (low, high), here, there in zip(partners(slabs), near, far):
        kept = here.shape[1]
        mine = jnp.where(core == 0, low, high) * TRAVEL
        other = jnp.where(core == 0, high, low) * TRAVEL
        for place in range(TRAVEL):
            if low != high:
                stage[mine + place] = here[place]
                stage[other + place] = there[place]
            else:
                stage[mine + place, pl.ds(pl.multiple_of(core * kept, kept), kept), :] = here[place]
                stage[mine + place, pl.ds(pl.multiple_of((1 - core) * kept, kept), kept), :] = there[place]


def block_major(x_ref, wide, points, blocks):
    wide[...] = x_ref[0].astype(F32)
    return [wide[pl.ds(s, points, stride=blocks), :] for s in range(blocks)]


def relayout_kernel(basis, field, basis_out, field_out, wide, *, points, blocks):
    size = basis.shape[-1]
    for source, target in ((basis, basis_out), (field, field_out)):
        for s, part in enumerate(block_major(source, wide, points, blocks)):
            target[0, :, s * size : (s + 1) * size] = part.astype(BF16)


def relayout(basis, field, points, blocks):
    batches, rows, size = basis.shape
    here = pl.BlockSpec((1, rows, size), lambda b: (b, 0, 0))
    there = pl.BlockSpec((1, points, blocks * size), lambda b: (b, 0, 0))
    shape = jax.ShapeDtypeStruct((batches, points, blocks * size), BF16)
    return pl.pallas_call(
        functools.partial(relayout_kernel, points=points, blocks=blocks),
        grid=(batches,),
        out_shape=(shape, shape),
        in_specs=[here, here],
        out_specs=(there, there),
        scratch_shapes=[pltpu.VMEM((rows, size), F32)],
        compiler_params=pltpu.CompilerParams(vmem_limit_bytes=VMEM_LIMIT),
        cost_estimate=pl.CostEstimate(flops=0, bytes_accessed=8 * batches * rows * size, transcendentals=0),
    )(basis, field)


def batch_matrix(region, pattern, tiles, slab, batch, blocks, width):
    half = (width - 1) // 2
    none = tiles.shape[0] - 1
    places = [pattern[batch, s] for s in range(blocks)]
    rows = [region[slab, place] for place in places]
    strips = []
    for s in range(blocks):
        strip = []
        for t in range(blocks):
            k = rows[t] - rows[s] + half
            inside = jnp.logical_and(k >= 0, k < width)
            strip.append(tiles[jnp.where(inside, places[s] * width + k, none)])
        strips.append(jnp.concatenate(strip, axis=1))
    return jnp.concatenate(strips, axis=0)


def split(values):
    high = values.astype(BF16)
    rest = values - high.astype(F32)
    middle = rest.astype(BF16)
    low = (rest - middle.astype(F32)).astype(BF16)
    return high, middle, low


def gradient_kernel(
    region,
    pattern,
    basis,
    field,
    basis_grad,
    weights,
    weight_grad,
    fn_atom,
    batch_atom,
    places,
    *rest,
    points,
    blocks,
    width,
    owner_rows,
    slabs,
):
    *pieces, tiles, out, stage, spread, sums, energy_sums = rest
    batch = pl.program_id(0)
    batches = pl.num_programs(0)
    me = lax.axis_index("grid")
    me_atoms = lax.axis_index("atoms")
    size = tiles.shape[-1]
    region_size = region.shape[1]

    @pl.when(batch == 0)
    def _():
        tiles[region_size * width] = jnp.zeros((size, size), BF16)
        stage_rows(stage, pieces[0], pieces[1 : 1 + slabs // 2], pieces[1 + slabs // 2 :], slabs)
        for position in range(region_size):
            owner, slot, count = owner_and_slot(region, me, position, owner_rows)
            shift = jnp.bitwise_xor(me, owner)
            for k in range(width):
                tiles[position * width + k] = stage[shift * TRAVEL + travel_place(slot, count, k)]

    matrix = batch_matrix(region, pattern, tiles, me, batch, blocks, width)
    potential = lax.dot_general(field[0], matrix, NT, preferred_element_type=F32)
    rows = jnp.concatenate(
        [weights[pl.ds(batch, 1), :]]
        + [weight_grad[c, pl.ds(batch, 1), :] for c in range(PARTS)]
        + [jnp.zeros((8 - 1 - PARTS, points), F32)],
        axis=0,
    )
    columns = rows.T
    weight = columns[:, 0:1]
    energy = jnp.zeros((points, size), F32)
    for s in range(blocks):
        here = potential[:, s * size : (s + 1) * size]
        energy = energy + basis[0, :, s * size : (s + 1) * size].astype(F32) * here
        spread[pl.ds(s, points, stride=blocks), :] = here * weight
    scaled = spread[...]
    place = pl.ds(pl.multiple_of(batch * 8, 8), 8)
    for c in range(PARTS):
        terms = basis_grad[c, 0].astype(F32) * scaled
        sums[c, place, :] = jnp.sum(terms.reshape(-1, 8, size), axis=0)
        terms = energy * columns[:, 1 + c : 2 + c]
        energy_sums[c, place, :] = jnp.sum(terms.reshape(-1, 8, size), axis=0)

    @pl.when(batch == batches - 1)
    def _():
        padded = max(8, region_size)
        chosen = lax.broadcasted_iota(jnp.int32, (padded, places.shape[1]), 0) == places[...]
        chosen = chosen.astype(BF16)
        blocks_sum = []
        for c in range(PARTS):
            total = jnp.zeros((padded, size), F32)
            for piece in split(sums[c]):
                total = total + jnp.dot(chosen, piece, preferred_element_type=F32)
            blocks_sum.append(-2.0 * total)
        lefts = []
        for position in range(region_size):
            stack = jnp.concatenate([total[position : position + 1] for total in blocks_sum], axis=0)
            high, middle, low = (piece.astype(F32) for piece in split(stack))
            lefts.append(jnp.concatenate([high, middle, low, jnp.zeros((16 - 3 * PARTS, size), F32)], axis=0))
        left = jnp.concatenate(lefts, axis=1).astype(BF16)
        chunk = out.shape[-1]
        scale = [jnp.sum(energy_sums[c], axis=1, keepdims=True) for c in range(PARTS)]
        for device in range(out.shape[0]):
            atoms = lax.broadcasted_iota(jnp.int32, (chunk, size), 0) + device * chunk
            hot = [
                jnp.where(atoms == fn_atom[pl.ds(region[me, position], 1), :], 1.0, 0.0).astype(BF16)
                for position in range(region_size)
            ]
            found = lax.dot_general(left, jnp.concatenate(hot, axis=1), NT, preferred_element_type=F32)
            atoms = lax.broadcasted_iota(jnp.int32, (batch_atom.shape[0], chunk), 1) + device * chunk
            mine = atoms == batch_atom[...]
            for c in range(PARTS):
                value = found[c : c + 1] + found[PARTS + c : PARTS + c + 1] + found[2 * PARTS + c : 2 * PARTS + c + 1]
                value = value + jnp.sum(jnp.where(mine, scale[c], 0.0), axis=0, keepdims=True)
                out[jnp.bitwise_xor(me_atoms, device), c : c + 1, :] = value


def partial_gradient(
    region, pattern, basis, field, basis_grad, weights, weight_grad, fn_atom, batch_atom, pieces, shapes
):
    slabs, atom_devices, atom_total, points, blocks, width, owner_rows = shapes
    batches, _, columns = basis.shape
    size = columns // blocks
    region_size = region.shape[1]
    fn_atom = fn_atom.reshape(-1, size)
    places = jnp.broadcast_to(pattern[:, None, :], (batches, 8 // blocks, blocks)).reshape(1, -1)
    batch_atom = jnp.broadcast_to(batch_atom[:, None], (batches, 8)).reshape(-1, 1)
    block = pl.BlockSpec((1, points, columns), lambda b, *_: (b, 0, 0))
    whole = pl.BlockSpec(memory_space=pltpu.VMEM)
    tile_shape = (region_size * width + 1, size, size)
    out_shape = (atom_devices, PARTS, atom_total // atom_devices)
    return pl.pallas_call(
        functools.partial(
            gradient_kernel, points=points, blocks=blocks, width=width, owner_rows=owner_rows, slabs=slabs
        ),
        grid_spec=pltpu.PrefetchScalarGridSpec(
            num_scalar_prefetch=2,
            grid=(batches,),
            in_specs=[
                block,
                block,
                pl.BlockSpec((PARTS, 1, points * blocks, size), lambda b, *_: (0, b, 0, 0)),
            ]
            + [whole] * (5 + len(pieces)),
            out_specs=(whole, whole),
            scratch_shapes=[
                pltpu.VMEM((slabs * TRAVEL, size, size), BF16),
                pltpu.VMEM((points * blocks, size), F32),
                pltpu.VMEM((PARTS, batches * 8, size), F32),
                pltpu.VMEM((PARTS, batches * 8, size), F32),
            ],
        ),
        out_shape=(jax.ShapeDtypeStruct(tile_shape, BF16), jax.ShapeDtypeStruct(out_shape, F32)),
        compiler_params=pltpu.CompilerParams(vmem_limit_bytes=VMEM_LIMIT),
    )(region, pattern, basis, field, basis_grad, weights, weight_grad, fn_atom, batch_atom, places, *pieces)


def product_kernel(region, pattern, basis, tiles, out, spread, *, points, blocks, width):
    me = lax.axis_index("grid")
    size = tiles.shape[-1]
    matrix = batch_matrix(region, pattern, tiles, me, pl.program_id(0), blocks, width)
    product = jnp.dot(basis[0], matrix, preferred_element_type=F32)
    for t in range(blocks):
        spread[pl.ds(t, points, stride=blocks), :] = product[:, t * size : (t + 1) * size]
    out[0] = spread[...].astype(BF16)


def contract(region, pattern, basis, tiles, points, blocks, width):
    batches, _, columns = basis.shape
    size = columns // blocks
    return pl.pallas_call(
        functools.partial(product_kernel, points=points, blocks=blocks, width=width),
        grid_spec=pltpu.PrefetchScalarGridSpec(
            num_scalar_prefetch=2,
            grid=(batches,),
            in_specs=[
                pl.BlockSpec((1, points, columns), lambda b, *_: (b, 0, 0)),
                pl.BlockSpec(memory_space=pltpu.VMEM),
            ],
            out_specs=pl.BlockSpec((1, points * blocks, size), lambda b, *_: (b, 0, 0)),
            scratch_shapes=[pltpu.VMEM((points * blocks, size), F32)],
        ),
        out_shape=jax.ShapeDtypeStruct((batches, points * blocks, size), BF16),
        compiler_params=pltpu.CompilerParams(vmem_limit_bytes=VMEM_LIMIT),
        cost_estimate=pl.CostEstimate(
            flops=2 * batches * points * columns * columns,
            bytes_accessed=4 * batches * points * columns,
            transcendentals=0,
        ),
    )(region, pattern, basis, tiles)


def reorder_kernel(
    pattern_hbm,
    basis,
    field,
    basis_grad,
    weights_hbm,
    basis_out,
    field_out,
    weighted,
    grads,
    pattern,
    weights,
    columns,
    basis_in,
    field_in,
    grad_in,
    wide,
    sems,
    small_sems,
):
    batches, blocks, points, size = basis_out.shape

    def copies(batch):
        return (
            pltpu.make_async_copy(field.at[batch], field_in.at[batch], sems.at[batch, 0]),
            pltpu.make_async_copy(basis.at[batch], basis_in.at[batch], sems.at[batch, 1]),
            pltpu.make_async_copy(basis_grad.at[:, batch], grad_in.at[:, batch], sems.at[batch, 2]),
        )

    small = (
        pltpu.make_async_copy(pattern_hbm, pattern, small_sems.at[0]),
        pltpu.make_async_copy(weights_hbm, weights, small_sems.at[1]),
    )
    for copy in small:
        copy.start()

    @pl.loop(0, batches)
    def _(batch):
        for copy in copies(batch):
            copy.start()

    for copy in small:
        copy.wait()
    rows = jnp.concatenate([weights[...], jnp.zeros((size - batches, points), F32)], axis=0).T
    for batch in range(batches):
        columns[batch] = jnp.broadcast_to(rows[:, batch : batch + 1], (points, size))

    @pl.loop(0, batches)
    def _(batch):
        for copy in copies(batch):
            copy.wait()
        points_here = pl.ds(pl.multiple_of(batch * points, points), points)
        places = [pattern[s, batch] for s in range(blocks)]
        wide[0] = field_in[batch].astype(F32)
        wide[1] = basis_in[batch].astype(F32)
        for c in range(PARTS):
            wide[2 + c] = grad_in[c, batch].astype(F32)
        for s, place in enumerate(places):
            strided = pl.ds(s, points, stride=blocks)
            values = wide[0, strided, :]
            field_out[batch, place] = values.astype(BF16)
            weighted[place, points_here, :] = (values * columns[batch]).astype(BF16)
            basis_out[batch, place] = wide[1, strided, :].astype(BF16)
            for c in range(PARTS):
                grads[c, place, points_here, :] = wide[2 + c, strided, :].astype(BF16)


def reorder(pattern, basis, field, basis_grad, weights, points, blocks):
    batches, rows, size = basis.shape
    hbm = pl.BlockSpec(memory_space=pl.ANY)
    vmem = pl.BlockSpec(memory_space=pltpu.VMEM)
    ordered = jax.ShapeDtypeStruct((batches, blocks, points, size), BF16)
    return pl.pallas_call(
        reorder_kernel,
        out_shape=(
            ordered,
            ordered,
            jax.ShapeDtypeStruct((blocks, batches * points, size), BF16),
            jax.ShapeDtypeStruct((PARTS, blocks, batches * points, size), BF16),
        ),
        in_specs=[hbm] * 5,
        out_specs=(vmem,) * 4,
        scratch_shapes=[
            pltpu.SMEM((blocks, batches), jnp.int32),
            pltpu.VMEM(weights.shape, F32),
            pltpu.VMEM((batches, points, size), F32),
            pltpu.VMEM((batches, rows, size), BF16),
            pltpu.VMEM((batches, rows, size), BF16),
            pltpu.VMEM((PARTS, batches, rows, size), BF16),
            pltpu.VMEM((2 + PARTS, rows, size), F32),
            pltpu.SemaphoreType.DMA((batches, 3)),
            pltpu.SemaphoreType.DMA((2,)),
        ],
        compiler_params=pltpu.CompilerParams(vmem_limit_bytes=VMEM_LIMIT),
        cost_estimate=pl.CostEstimate(
            flops=0, bytes_accessed=2 * (2 + PARTS) * batches * rows * size, transcendentals=0
        ),
    )(in_hbm(pattern.T), in_hbm(basis), in_hbm(field), in_hbm(basis_grad), in_hbm(weights))


def moment_kernel(weighted, grads, moments):
    blocks, _, size = grads.shape[1:]
    for p in range(0, blocks, 2):
        first, last = max(p - 1, 0), min(p + 3, blocks)
        left = jnp.concatenate([weighted[place] for place in range(first, last)], axis=1)
        for c in range(PARTS):
            right = jnp.concatenate([grads[c, p], grads[c, p + 1]], axis=1)
            moments[c, first * size : last * size, p * size : (p + 2) * size] = lax.dot_general(
                left, right, TN, preferred_element_type=F32
            )


def build_moments(weighted, grads):
    blocks, depth, size = grads.shape[1:]
    vmem = pl.BlockSpec(memory_space=pltpu.VMEM)
    return pl.pallas_call(
        moment_kernel,
        out_shape=jax.ShapeDtypeStruct((PARTS, blocks * size, blocks * size), F32),
        in_specs=[vmem, vmem],
        out_specs=vmem,
        compiler_params=pltpu.CompilerParams(vmem_limit_bytes=VMEM_LIMIT),
        cost_estimate=pl.CostEstimate(
            flops=2 * PARTS * depth * (blocks * size) ** 2, bytes_accessed=0, transcendentals=0
        ),
    )(weighted, grads)


def atom_kernel(region, fn_atom, batch_atom, weight_grad, hot, grad_columns):
    batches, points = weight_grad.shape[1:]
    size = fn_atom.shape[1]
    blocks = region.shape[1]
    me = lax.axis_index("grid")
    atoms = lax.broadcasted_iota(jnp.int32, (hot.shape[0], size), 0)
    ids = jnp.concatenate([batch_atom[...], jnp.full((1, size - batches), -1, jnp.int32)], axis=1)
    hot[:, blocks * size :] = jnp.where(atoms == ids, 1.0, 0.0).astype(BF16)

    @pl.loop(0, blocks)
    def _(position):
        ids = fn_atom[pl.ds(region[me, position], 1), :]
        columns = pl.ds(pl.multiple_of(position * size, size), size)
        hot[:, columns] = jnp.where(atoms == ids, 1.0, 0.0).astype(BF16)

    for c in range(PARTS):
        padding = jnp.zeros((size - batches, points), F32)
        grad_columns[c] = jnp.concatenate([weight_grad[c], padding], axis=0).T


def atom_matrix(region, fn_atom, batch_atom, weight_grad, blocks, size, atom_total):
    vmem = pl.BlockSpec(memory_space=pltpu.VMEM)
    return pl.pallas_call(
        atom_kernel,
        out_shape=(
            jax.ShapeDtypeStruct((atom_total, (blocks + 1) * size), BF16),
            jax.ShapeDtypeStruct((PARTS, weight_grad.shape[2], size), F32),
        ),
        in_specs=[pl.BlockSpec(memory_space=pltpu.SMEM)] + [vmem] * 3,
        out_specs=(vmem, vmem),
        compiler_params=pltpu.CompilerParams(vmem_limit_bytes=VMEM_LIMIT),
        cost_estimate=pl.CostEstimate(flops=1000000000, bytes_accessed=2 * atom_total * size, transcendentals=0),
    )(region, fn_atom.reshape(-1, size), batch_atom.reshape(1, -1), weight_grad)


def combine_kernel(
    region, basis, field, moments, hot, grad_columns, *rest, owner_rows, slabs, width, step
):
    *pieces, product_out, out, stage, matrix, energies = rest
    batches, blocks, points, size = basis.shape
    me = lax.axis_index("grid")
    me_atoms = lax.axis_index("atoms")
    half = (width - 1) // 2
    stage_rows(stage, pieces[0], pieces[1 : 1 + slabs // 2], pieces[1 + slabs // 2 :], slabs)
    rows = [region[me, position] for position in range(blocks)]
    found = [owner_and_slot(region, me, position, owner_rows) for position in range(blocks)]
    totals = [[jnp.zeros((8, size), F32) for _ in range(blocks)] for _ in range(PARTS)]
    for p in range(blocks):
        owner, slot, count = found[p]
        first = jnp.bitwise_xor(me, owner) * TRAVEL
        for q in range(blocks):
            if abs(q - p) > half:
                matrix[p * size : (p + 1) * size, q * size : (q + 1) * size] = jnp.zeros((size, size), BF16)
                continue
            k = rows[q] - rows[p] + half
            place = jnp.where(
                k == 0,
                travel_place(slot, count, 0),
                jnp.where(k == 1, travel_place(slot, count, 1), travel_place(slot, count, 2)),
            )
            inside = jnp.logical_and(k >= 0, k < width)
            tile = jnp.where(inside, stage[first + place], jnp.zeros((size, size), BF16))
            matrix[p * size : (p + 1) * size, q * size : (q + 1) * size] = tile
            turned = tile.T.astype(F32)
            for c in range(PARTS):
                terms = turned * moments[c, q * size : (q + 1) * size, p * size : (p + 1) * size]
                totals[c][p] = totals[c][p] + jnp.sum(terms.reshape(-1, 8, size), axis=0)
    derivative = [
        jnp.concatenate([jnp.sum(total, axis=0, keepdims=True) for total in totals[c]], axis=1) for c in range(PARTS)
    ]

    energies[...] = jnp.zeros_like(energies)
    lanes = lax.broadcasted_iota(jnp.int32, (points, size), 1)

    @pl.loop(0, batches // step)
    def _(group):
        left = [
            jnp.concatenate([basis[group * step + inner, p] for p in range(blocks)], axis=1) for inner in range(step)
        ]
        left = jnp.concatenate(left, axis=0)
        energy = [jnp.zeros((points, size), F32) for _ in range(step)]
        for q in range(0, blocks, 2):
            product = jnp.dot(left, matrix[:, q * size : (q + 2) * size], preferred_element_type=F32)
            for inner in range(step):
                batch = group * step + inner
                for column in range(2):
                    part = product[inner * points : (inner + 1) * points, column * size : (column + 1) * size]
                    product_out[batch, q + column] = part.astype(BF16)
                    energy[inner] = energy[inner] + part * field[batch, q + column].astype(F32)
        for inner in range(step):
            total = jnp.sum(energy[inner], axis=1, keepdims=True)
            energies[...] = jnp.where(lanes == group * step + inner, total, energies[...])

    lefts = []
    for c in range(PARTS):
        term = jnp.sum(energies[...] * grad_columns[c], axis=0, keepdims=True)
        lefts.append(jnp.concatenate([-2.0 * derivative[c], term], axis=1))
    left = jnp.concatenate(lefts, axis=0)
    high, middle, low = (piece.astype(F32) for piece in split(left))
    left = jnp.concatenate([high, middle, low, jnp.zeros((16 - 3 * PARTS, left.shape[1]), F32)], axis=0).astype(BF16)
    chunk = out.shape[-1]
    for device in range(out.shape[0]):
        sums = lax.dot_general(
            left, hot[device * chunk : (device + 1) * chunk, :], NT, preferred_element_type=F32
        )
        value = sums[:PARTS] + sums[PARTS : 2 * PARTS] + sums[2 * PARTS : 3 * PARTS]
        out[jnp.bitwise_xor(me_atoms, device)] = value


def combine(region, prepared, pieces, shapes):
    basis, field, moments, hot, grad_columns = prepared
    slabs, atom_devices, atom_total, points, blocks, width, owner_rows = shapes
    batches, _, _, size = basis.shape
    step = 16 if batches % 16 == 0 else 1
    vmem = pl.BlockSpec(memory_space=pltpu.VMEM)
    return pl.pallas_call(
        functools.partial(combine_kernel, owner_rows=owner_rows, slabs=slabs, width=width, step=step),
        out_shape=(
            jax.ShapeDtypeStruct(basis.shape, BF16),
            jax.ShapeDtypeStruct((atom_devices, PARTS, atom_total // atom_devices), F32),
        ),
        in_specs=[pl.BlockSpec(memory_space=pltpu.SMEM)] + [vmem] * (5 + len(pieces)),
        out_specs=(vmem, vmem),
        scratch_shapes=[
            pltpu.VMEM((slabs * TRAVEL, size, size), BF16),
            pltpu.VMEM((blocks * size, blocks * size), BF16),
            pltpu.VMEM((points, size), F32),
        ],
        compiler_params=pltpu.CompilerParams(vmem_limit_bytes=VMEM_LIMIT),
    )(region, basis, field, moments, hot, grad_columns, *pieces)


def write_kernel(pattern, product, out, wide, staged, sems):
    batches, blocks, points, size = product.shape

    def copy(batch):
        return pltpu.make_async_copy(staged.at[batch], out.at[batch], sems.at[batch])

    @pl.loop(0, batches // 2)
    def _(pair):
        for inner in range(2):
            batch = pair * 2 + inner
            for t in range(blocks):
                wide[inner, pl.ds(t, points, stride=blocks), :] = product[batch, pattern[t, batch]].astype(F32)
            staged[batch] = wide[inner].astype(BF16)
            copy(batch).start()

    @pl.loop(0, batches)
    def _(batch):
        copy(batch).wait()


def write(pattern, product):
    batches, blocks, points, size = product.shape
    shape = (batches, points * blocks, size)
    return pl.pallas_call(
        write_kernel,
        out_shape=jax.ShapeDtypeStruct(shape, BF16),
        in_specs=[pl.BlockSpec(memory_space=pltpu.SMEM), pl.BlockSpec(memory_space=pltpu.VMEM)],
        out_specs=pl.BlockSpec(memory_space=pl.ANY),
        scratch_shapes=[
            pltpu.VMEM((2, points * blocks, size), F32),
            pltpu.VMEM(shape, BF16),
            pltpu.SemaphoreType.DMA((batches,)),
        ],
        compiler_params=pltpu.CompilerParams(vmem_limit_bytes=VMEM_LIMIT),
        cost_estimate=pl.CostEstimate(flops=0, bytes_accessed=4 * math.prod(shape), transcendentals=0),
    )(pattern.T, product)


def swap_halves(near, ready, atom_devices):
    near, ready = lax.optimization_barrier((near, ready))
    swap = [(i, i ^ 1) for i in range(atom_devices)]
    return near, [lax.ppermute(piece, "atoms", swap) for piece in near], ready


def tree_sum(values):
    if len(values) == 1:
        return values[0]
    half = len(values) // 2
    return tree_sum(values[:half]) + tree_sum(values[half:])


def exchange_all(parts, axis, count):
    moved = {d: lax.ppermute(parts[d], axis, [(i, i ^ d) for i in range(count)]) for d in range(1, count)}
    return [parts[0]] + [moved[d] for d in range(1, count)]


def sum_parts(partial_grad, product, slabs, atom_devices):
    total = tree_sum(exchange_all([partial_grad[d] for d in range(atom_devices)], "atoms", atom_devices))
    total, product = lax.optimization_barrier((total, product))
    return tree_sum(exchange_all([total] * slabs, "grid", slabs)), product


def local(
    basis,
    basis_grad,
    exchange_field,
    weights,
    weight_grad,
    density,
    region,
    pattern,
    fn_atom,
    batch_atom,
):
    batches, points, blocks, size = basis.shape
    owner_rows, width = density.shape[:2]
    slabs = lax.axis_size("grid")
    atom_devices = lax.axis_size("atoms")
    atom_total = fn_atom.shape[0] // (10 * slabs * atom_devices) * slabs * atom_devices
    shapes = (slabs, atom_devices, atom_total, points, blocks, width, owner_rows)
    flat_basis = basis.reshape(batches, points * blocks, size)
    flat_field = exchange_field.reshape(batches, points * blocks, size)
    flat_grad = basis_grad.reshape(PARTS, batches, points * blocks, size)
    own, near = fetch_rows(region, density, slabs, atom_devices)
    if region.shape[1] == blocks:
        basis_wide, field_wide, weighted, grads = reorder(
            pattern, flat_basis, flat_field, flat_grad, weights, points, blocks
        )
        ready = (basis_wide, field_wide, build_moments(weighted, grads), batch_atom)
        near, far, (basis_wide, field_wide, moments, batch_atom) = swap_halves(near, ready, atom_devices)
        hot, grad_columns = atom_matrix(region, fn_atom, batch_atom, weight_grad, blocks, size, atom_total)
        ready = (basis_wide, field_wide, moments, hot, grad_columns)
        product, partial_grad = combine(region, ready, [own, *near, *far], shapes)
        gradient, product = sum_parts(partial_grad, product, slabs, atom_devices)
        contracted = write(pattern, product)
        return contracted.reshape(basis.shape), gradient
    ready = relayout(in_hbm(flat_basis), in_hbm(flat_field), points, blocks)
    near, far, (basis_wide, field_wide) = swap_halves(near, ready, atom_devices)
    tiles, partial_grad = partial_gradient(
        region,
        pattern,
        basis_wide,
        field_wide,
        in_hbm(flat_grad),
        weights,
        weight_grad,
        fn_atom,
        batch_atom,
        [own, *near, *far],
        shapes,
    )
    gradient, basis_wide = sum_parts(partial_grad, basis_wide, slabs, atom_devices)
    contracted = contract(region, pattern, basis_wide, tiles, points, blocks, width)
    return contracted.reshape(basis.shape), gradient


def solution(mesh):
    placed = (
        P(("groups", "grid", "atoms"), None, None, None),
        P(None, ("groups", "grid", "atoms"), None, None, None),
        P(("groups", "grid", "atoms"), None, None, None),
        P(("groups", "grid", "atoms"), None),
        P(None, ("groups", "grid", "atoms"), None),
        P(("groups", "grid"), None, None, None),
        P("groups", None),
        P(("groups", "grid", "atoms"), None),
        P("groups"),
        P(("groups", "grid", "atoms")),
    )
    return jax.shard_map(
        local,
        mesh=mesh,
        in_specs=placed,
        out_specs=(P(("groups", "grid", "atoms"), None, None, None), P(None, ("groups", "atoms"))),
        check_vma=False,
    )
```

```python
import functools
import math

import jax
import jax.numpy as jnp
from jax import lax
from jax.experimental import pallas as pl
from jax.experimental.pallas import tpu as pltpu
from jax.sharding import PartitionSpec as P

TRAVEL = 5
PARTS = 3
F32 = jnp.float32
BF16 = jnp.bfloat16
NT = (((1,), (1,)), ((), ()))
TN = (((0,), (0,)), ((), ()))
VMEM_LIMIT = 32 * 1024 * 1024


def owner_and_slot(region, slab, position, owner_rows):
    owner = lax.div(region[slab, position], owner_rows)
    slot = jnp.int32(0)
    count = jnp.int32(0)
    for other in range(region.shape[1]):
        same = jnp.where(lax.div(region[slab, other], owner_rows) == owner, 1, 0)
        count = count + same
        slot = slot + jnp.where(other < position, same, 0)
    return owner, slot, count


def travel_place(slot, count, k):
    if k == 0:
        return jnp.where(slot == 0, 4, 2)
    if k == 1:
        return jnp.where(slot == 0, 0, 3)
    return jnp.where(jnp.logical_and(slot == 0, count == 2), 1, 4)


def partners(slabs):
    return [(shift + 1, shift) for shift in range(2, slabs, 2)] + [(0, 1)]


def send_kernel(region_hbm, density, *rest):
    *outs, region, sems, region_sem = rest
    fetch = pltpu.make_async_copy(region_hbm, region, region_sem)
    fetch.start()
    fetch.wait()
    me = lax.axis_index("grid")
    core = lax.rem(lax.axis_index("atoms"), 2)
    slabs, size = region.shape
    owner_rows = density.shape[0]
    copies = []
    for number, ((low, high), out) in enumerate(zip([(0, 0)] + partners(slabs), outs)):
        slab = jnp.bitwise_xor(me, jnp.where(core == 0, low, high))
        base = jnp.int32(owner_rows)
        count = jnp.int32(0)
        for position in range(size):
            row = region[slab, position] - me * owner_rows
            mine = jnp.logical_and(row >= 0, row < owner_rows)
            base = jnp.minimum(base, jnp.where(mine, row, owner_rows))
            count = count + jnp.where(mine, 1, 0)
        base = jnp.where(count == 0, 0, base)
        after = jnp.minimum(base + 1, owner_rows - 1)
        lower = base == 0
        edge = jnp.where(jnp.logical_and(count == 2, jnp.logical_not(lower)), after, base)
        pairs = (
            (density.at[base, pl.ds(1, 2)], out.at[pl.ds(0, 2)]),
            (density.at[after, pl.ds(0, 2)], out.at[pl.ds(2, 2)]),
            (density.at[edge, jnp.where(lower, 0, 2)], out.at[4]),
        )
        for part, (source, target) in enumerate(pairs):
            copies.append(pltpu.make_async_copy(source, target, sems.at[number, part]))
    for copy in copies:
        copy.start()
    for copy in copies:
        copy.wait()


def in_hbm(array):
    return pltpu.with_memory_space_constraint(array, pltpu.HBM)


def rows_to_send(region, density, slabs):
    size = density.shape[-1]
    count = 1 + len(partners(slabs))
    hbm = pl.BlockSpec(memory_space=pl.ANY)
    return pl.pallas_call(
        send_kernel,
        out_shape=[jax.ShapeDtypeStruct((TRAVEL, size, size), density.dtype)] * count,
        in_specs=[hbm, hbm],
        out_specs=[pl.BlockSpec(memory_space=pltpu.VMEM)] * count,
        scratch_shapes=[
            pltpu.SMEM(region.shape, jnp.int32),
            pltpu.SemaphoreType.DMA((count, 3)),
            pltpu.SemaphoreType.DMA,
        ],
        compiler_params=pltpu.CompilerParams(vmem_limit_bytes=VMEM_LIMIT),
    )(in_hbm(region), in_hbm(density))


def fetch_rows(region, density, slabs, atom_devices):
    own, *outgoing = rows_to_send(region, density, slabs)
    near = []
    for shifts, piece in zip(partners(slabs), outgoing):
        moves = [
            (z * atom_devices + a, (z ^ shifts[a % 2]) * atom_devices + a)
            for z in range(slabs)
            for a in range(atom_devices)
            if shifts[a % 2]
        ]
        near.append(lax.ppermute(piece, ("grid", "atoms"), moves))
    return own, near


def stage_rows(stage, own, near, far, slabs):
    core = lax.rem(lax.axis_index("atoms"), 2)
    for place in range(TRAVEL):
        stage[place] = own[place]
    for (low, high), here, there in zip(partners(slabs), near, far):
        mine = jnp.where(core == 0, low, high) * TRAVEL
        other = jnp.where(core == 0, high, low) * TRAVEL
        for place in range(TRAVEL):
            if low:
                stage[mine + place] = here[place]
                stage[other + place] = there[place]
            else:
                stage[high * TRAVEL + place] = jnp.where(core == 0, there[place], here[place])


def block_major(x_ref, wide, points, blocks):
    wide[...] = x_ref[0].astype(F32)
    return [wide[pl.ds(s, points, stride=blocks), :] for s in range(blocks)]


def relayout_kernel(basis, field, basis_out, field_out, wide, *, points, blocks):
    size = basis.shape[-1]
    for source, target in ((basis, basis_out), (field, field_out)):
        for s, part in enumerate(block_major(source, wide, points, blocks)):
            target[0, :, s * size : (s + 1) * size] = part.astype(BF16)


def relayout(basis, field, points, blocks):
    batches, rows, size = basis.shape
    here = pl.BlockSpec((1, rows, size), lambda b: (b, 0, 0))
    there = pl.BlockSpec((1, points, blocks * size), lambda b: (b, 0, 0))
    shape = jax.ShapeDtypeStruct((batches, points, blocks * size), BF16)
    return pl.pallas_call(
        functools.partial(relayout_kernel, points=points, blocks=blocks),
        grid=(batches,),
        out_shape=(shape, shape),
        in_specs=[here, here],
        out_specs=(there, there),
        scratch_shapes=[pltpu.VMEM((rows, size), F32)],
        compiler_params=pltpu.CompilerParams(vmem_limit_bytes=VMEM_LIMIT),
        cost_estimate=pl.CostEstimate(flops=0, bytes_accessed=8 * batches * rows * size, transcendentals=0),
    )(basis, field)


def batch_matrix(region, pattern, tiles, slab, batch, blocks, width):
    half = (width - 1) // 2
    none = tiles.shape[0] - 1
    places = [pattern[batch, s] for s in range(blocks)]
    rows = [region[slab, place] for place in places]
    strips = []
    for s in range(blocks):
        strip = []
        for t in range(blocks):
            k = rows[t] - rows[s] + half
            inside = jnp.logical_and(k >= 0, k < width)
            strip.append(tiles[jnp.where(inside, places[s] * width + k, none)])
        strips.append(jnp.concatenate(strip, axis=1))
    return jnp.concatenate(strips, axis=0)


def split(values):
    high = values.astype(BF16)
    rest = values - high.astype(F32)
    middle = rest.astype(BF16)
    low = (rest - middle.astype(F32)).astype(BF16)
    return high, middle, low


def gradient_kernel(
    region,
    pattern,
    basis,
    field,
    basis_grad,
    weights,
    weight_grad,
    fn_atom,
    batch_atom,
    places,
    *rest,
    points,
    blocks,
    width,
    owner_rows,
    slabs,
):
    *pieces, tiles, out, stage, spread, sums, energy_sums = rest
    batch = pl.program_id(0)
    batches = pl.num_programs(0)
    me = lax.axis_index("grid")
    me_atoms = lax.axis_index("atoms")
    size = tiles.shape[-1]
    region_size = region.shape[1]

    @pl.when(batch == 0)
    def _():
        tiles[region_size * width] = jnp.zeros((size, size), BF16)
        stage_rows(stage, pieces[0], pieces[1 : 1 + slabs // 2], pieces[1 + slabs // 2 :], slabs)
        for position in range(region_size):
            owner, slot, count = owner_and_slot(region, me, position, owner_rows)
            shift = jnp.bitwise_xor(me, owner)
            for k in range(width):
                tiles[position * width + k] = stage[shift * TRAVEL + travel_place(slot, count, k)]

    matrix = batch_matrix(region, pattern, tiles, me, batch, blocks, width)
    potential = lax.dot_general(field[0], matrix, NT, preferred_element_type=F32)
    rows = jnp.concatenate(
        [weights[pl.ds(batch, 1), :]]
        + [weight_grad[c, pl.ds(batch, 1), :] for c in range(PARTS)]
        + [jnp.zeros((8 - 1 - PARTS, points), F32)],
        axis=0,
    )
    columns = rows.T
    weight = columns[:, 0:1]
    energy = jnp.zeros((points, size), F32)
    for s in range(blocks):
        here = potential[:, s * size : (s + 1) * size]
        energy = energy + basis[0, :, s * size : (s + 1) * size].astype(F32) * here
        spread[pl.ds(s, points, stride=blocks), :] = here * weight
    scaled = spread[...]
    place = pl.ds(pl.multiple_of(batch * 8, 8), 8)
    for c in range(PARTS):
        terms = basis_grad[c, 0].astype(F32) * scaled
        sums[c, place, :] = jnp.sum(terms.reshape(-1, 8, size), axis=0)
        terms = energy * columns[:, 1 + c : 2 + c]
        energy_sums[c, place, :] = jnp.sum(terms.reshape(-1, 8, size), axis=0)

    @pl.when(batch == batches - 1)
    def _():
        padded = max(8, region_size)
        chosen = lax.broadcasted_iota(jnp.int32, (padded, places.shape[1]), 0) == places[...]
        chosen = chosen.astype(BF16)
        blocks_sum = []
        for c in range(PARTS):
            total = jnp.zeros((padded, size), F32)
            for piece in split(sums[c]):
                total = total + jnp.dot(chosen, piece, preferred_element_type=F32)
            blocks_sum.append(-2.0 * total)
        lefts = []
        for position in range(region_size):
            stack = jnp.concatenate([total[position : position + 1] for total in blocks_sum], axis=0)
            high, middle, low = (piece.astype(F32) for piece in split(stack))
            lefts.append(jnp.concatenate([high, middle, low, jnp.zeros((16 - 3 * PARTS, size), F32)], axis=0))
        left = jnp.concatenate(lefts, axis=1).astype(BF16)
        chunk = out.shape[-1]
        scale = [jnp.sum(energy_sums[c], axis=1, keepdims=True) for c in range(PARTS)]
        for device in range(out.shape[0]):
            atoms = lax.broadcasted_iota(jnp.int32, (chunk, size), 0) + device * chunk
            hot = [
                jnp.where(atoms == fn_atom[pl.ds(region[me, position], 1), :], 1.0, 0.0).astype(BF16)
                for position in range(region_size)
            ]
            found = lax.dot_general(left, jnp.concatenate(hot, axis=1), NT, preferred_element_type=F32)
            atoms = lax.broadcasted_iota(jnp.int32, (batch_atom.shape[0], chunk), 1) + device * chunk
            mine = atoms == batch_atom[...]
            for c in range(PARTS):
                value = found[c : c + 1] + found[PARTS + c : PARTS + c + 1] + found[2 * PARTS + c : 2 * PARTS + c + 1]
                value = value + jnp.sum(jnp.where(mine, scale[c], 0.0), axis=0, keepdims=True)
                out[jnp.bitwise_xor(me_atoms, device), c : c + 1, :] = value


def partial_gradient(
    region, pattern, basis, field, basis_grad, weights, weight_grad, fn_atom, batch_atom, pieces, shapes
):
    slabs, atom_devices, atom_total, points, blocks, width, owner_rows = shapes
    batches, _, columns = basis.shape
    size = columns // blocks
    region_size = region.shape[1]
    fn_atom = fn_atom.reshape(-1, size)
    places = jnp.broadcast_to(pattern[:, None, :], (batches, 8 // blocks, blocks)).reshape(1, -1)
    batch_atom = jnp.broadcast_to(batch_atom[:, None], (batches, 8)).reshape(-1, 1)
    block = pl.BlockSpec((1, points, columns), lambda b, *_: (b, 0, 0))
    whole = pl.BlockSpec(memory_space=pltpu.VMEM)
    tile_shape = (region_size * width + 1, size, size)
    out_shape = (atom_devices, PARTS, atom_total // atom_devices)
    return pl.pallas_call(
        functools.partial(
            gradient_kernel, points=points, blocks=blocks, width=width, owner_rows=owner_rows, slabs=slabs
        ),
        grid_spec=pltpu.PrefetchScalarGridSpec(
            num_scalar_prefetch=2,
            grid=(batches,),
            in_specs=[
                block,
                block,
                pl.BlockSpec((PARTS, 1, points * blocks, size), lambda b, *_: (0, b, 0, 0)),
            ]
            + [whole] * (5 + len(pieces)),
            out_specs=(whole, whole),
            scratch_shapes=[
                pltpu.VMEM((slabs * TRAVEL, size, size), BF16),
                pltpu.VMEM((points * blocks, size), F32),
                pltpu.VMEM((PARTS, batches * 8, size), F32),
                pltpu.VMEM((PARTS, batches * 8, size), F32),
            ],
        ),
        out_shape=(jax.ShapeDtypeStruct(tile_shape, BF16), jax.ShapeDtypeStruct(out_shape, F32)),
        compiler_params=pltpu.CompilerParams(vmem_limit_bytes=VMEM_LIMIT),
    )(region, pattern, basis, field, basis_grad, weights, weight_grad, fn_atom, batch_atom, places, *pieces)


def product_kernel(region, pattern, basis, tiles, out, spread, *, points, blocks, width):
    me = lax.axis_index("grid")
    size = tiles.shape[-1]
    matrix = batch_matrix(region, pattern, tiles, me, pl.program_id(0), blocks, width)
    product = jnp.dot(basis[0], matrix, preferred_element_type=F32)
    for t in range(blocks):
        spread[pl.ds(t, points, stride=blocks), :] = product[:, t * size : (t + 1) * size]
    out[0] = spread[...].astype(BF16)


def contract(region, pattern, basis, tiles, points, blocks, width):
    batches, _, columns = basis.shape
    size = columns // blocks
    return pl.pallas_call(
        functools.partial(product_kernel, points=points, blocks=blocks, width=width),
        grid_spec=pltpu.PrefetchScalarGridSpec(
            num_scalar_prefetch=2,
            grid=(batches,),
            in_specs=[
                pl.BlockSpec((1, points, columns), lambda b, *_: (b, 0, 0)),
                pl.BlockSpec(memory_space=pltpu.VMEM),
            ],
            out_specs=pl.BlockSpec((1, points * blocks, size), lambda b, *_: (b, 0, 0)),
            scratch_shapes=[pltpu.VMEM((points * blocks, size), F32)],
        ),
        out_shape=jax.ShapeDtypeStruct((batches, points * blocks, size), BF16),
        compiler_params=pltpu.CompilerParams(vmem_limit_bytes=VMEM_LIMIT),
        cost_estimate=pl.CostEstimate(
            flops=2 * batches * points * columns * columns,
            bytes_accessed=4 * batches * points * columns,
            transcendentals=0,
        ),
    )(region, pattern, basis, tiles)


def reorder_kernel(
    pattern_hbm,
    basis,
    field,
    basis_grad,
    weights_hbm,
    basis_out,
    field_out,
    weighted,
    grads,
    pattern,
    weights,
    columns,
    basis_in,
    field_in,
    grad_in,
    wide,
    sems,
    small_sems,
):
    batches, blocks, points, size = basis_out.shape

    def copies(batch):
        return (
            pltpu.make_async_copy(field.at[batch], field_in.at[batch], sems.at[batch, 0]),
            pltpu.make_async_copy(basis.at[batch], basis_in.at[batch], sems.at[batch, 1]),
            pltpu.make_async_copy(basis_grad.at[:, batch], grad_in.at[:, batch], sems.at[batch, 2]),
        )

    small = (
        pltpu.make_async_copy(pattern_hbm, pattern, small_sems.at[0]),
        pltpu.make_async_copy(weights_hbm, weights, small_sems.at[1]),
    )
    for copy in small:
        copy.start()

    @pl.loop(0, batches)
    def _(batch):
        for copy in copies(batch):
            copy.start()

    for copy in small:
        copy.wait()
    rows = jnp.concatenate([weights[...], jnp.zeros((size - batches, points), F32)], axis=0).T
    for batch in range(batches):
        columns[batch] = jnp.broadcast_to(rows[:, batch : batch + 1], (points, size))

    @pl.loop(0, batches)
    def _(batch):
        for copy in copies(batch):
            copy.wait()
        points_here = pl.ds(pl.multiple_of(batch * points, points), points)
        places = [pattern[s, batch] for s in range(blocks)]
        wide[0] = field_in[batch].astype(F32)
        wide[1] = basis_in[batch].astype(F32)
        for c in range(PARTS):
            wide[2 + c] = grad_in[c, batch].astype(F32)
        for s, place in enumerate(places):
            strided = pl.ds(s, points, stride=blocks)
            values = wide[0, strided, :]
            field_out[batch, place] = values.astype(BF16)
            weighted[place, points_here, :] = (values * columns[batch]).astype(BF16)
            basis_out[batch, place] = wide[1, strided, :].astype(BF16)
            for c in range(PARTS):
                grads[c, place, points_here, :] = wide[2 + c, strided, :].astype(BF16)


def reorder(pattern, basis, field, basis_grad, weights, points, blocks):
    batches, rows, size = basis.shape
    hbm = pl.BlockSpec(memory_space=pl.ANY)
    vmem = pl.BlockSpec(memory_space=pltpu.VMEM)
    ordered = jax.ShapeDtypeStruct((batches, blocks, points, size), BF16)
    return pl.pallas_call(
        reorder_kernel,
        out_shape=(
            ordered,
            ordered,
            jax.ShapeDtypeStruct((blocks, batches * points, size), BF16),
            jax.ShapeDtypeStruct((PARTS, blocks, batches * points, size), BF16),
        ),
        in_specs=[hbm] * 5,
        out_specs=(vmem,) * 4,
        scratch_shapes=[
            pltpu.SMEM((blocks, batches), jnp.int32),
            pltpu.VMEM(weights.shape, F32),
            pltpu.VMEM((batches, points, size), F32),
            pltpu.VMEM((batches, rows, size), BF16),
            pltpu.VMEM((batches, rows, size), BF16),
            pltpu.VMEM((PARTS, batches, rows, size), BF16),
            pltpu.VMEM((2 + PARTS, rows, size), F32),
            pltpu.SemaphoreType.DMA((batches, 3)),
            pltpu.SemaphoreType.DMA((2,)),
        ],
        compiler_params=pltpu.CompilerParams(vmem_limit_bytes=VMEM_LIMIT),
        cost_estimate=pl.CostEstimate(
            flops=0, bytes_accessed=2 * (2 + PARTS) * batches * rows * size, transcendentals=0
        ),
    )(in_hbm(pattern.T), in_hbm(basis), in_hbm(field), in_hbm(basis_grad), in_hbm(weights))


def moment_kernel(weighted, grads, moments):
    blocks, _, size = grads.shape[1:]
    for p in range(0, blocks, 2):
        first, last = max(p - 1, 0), min(p + 3, blocks)
        left = jnp.concatenate([weighted[place] for place in range(first, last)], axis=1)
        for c in range(PARTS):
            right = jnp.concatenate([grads[c, p], grads[c, p + 1]], axis=1)
            moments[c, first * size : last * size, p * size : (p + 2) * size] = lax.dot_general(
                left, right, TN, preferred_element_type=F32
            )


def build_moments(weighted, grads):
    blocks, depth, size = grads.shape[1:]
    vmem = pl.BlockSpec(memory_space=pltpu.VMEM)
    return pl.pallas_call(
        moment_kernel,
        out_shape=jax.ShapeDtypeStruct((PARTS, blocks * size, blocks * size), F32),
        in_specs=[vmem, vmem],
        out_specs=vmem,
        compiler_params=pltpu.CompilerParams(vmem_limit_bytes=VMEM_LIMIT),
        cost_estimate=pl.CostEstimate(
            flops=2 * PARTS * depth * (blocks * size) ** 2, bytes_accessed=0, transcendentals=0
        ),
    )(weighted, grads)


def atom_kernel(region, fn_atom, batch_atom, weight_grad, hot, grad_columns):
    batches, points = weight_grad.shape[1:]
    size = fn_atom.shape[1]
    blocks = region.shape[1]
    me = lax.axis_index("grid")
    atoms = lax.broadcasted_iota(jnp.int32, (hot.shape[0], size), 0)
    ids = jnp.concatenate([batch_atom[...], jnp.full((1, size - batches), -1, jnp.int32)], axis=1)
    hot[:, blocks * size :] = jnp.where(atoms == ids, 1.0, 0.0).astype(BF16)

    @pl.loop(0, blocks)
    def _(position):
        ids = fn_atom[pl.ds(region[me, position], 1), :]
        columns = pl.ds(pl.multiple_of(position * size, size), size)
        hot[:, columns] = jnp.where(atoms == ids, 1.0, 0.0).astype(BF16)

    for c in range(PARTS):
        padding = jnp.zeros((size - batches, points), F32)
        grad_columns[c] = jnp.concatenate([weight_grad[c], padding], axis=0).T


def atom_matrix(region, fn_atom, batch_atom, weight_grad, blocks, size, atom_total):
    vmem = pl.BlockSpec(memory_space=pltpu.VMEM)
    return pl.pallas_call(
        atom_kernel,
        out_shape=(
            jax.ShapeDtypeStruct((atom_total, (blocks + 1) * size), BF16),
            jax.ShapeDtypeStruct((PARTS, weight_grad.shape[2], size), F32),
        ),
        in_specs=[pl.BlockSpec(memory_space=pltpu.SMEM)] + [vmem] * 3,
        out_specs=(vmem, vmem),
        compiler_params=pltpu.CompilerParams(vmem_limit_bytes=VMEM_LIMIT),
        cost_estimate=pl.CostEstimate(flops=1000000000, bytes_accessed=2 * atom_total * size, transcendentals=0),
    )(region, fn_atom.reshape(-1, size), batch_atom.reshape(1, -1), weight_grad)


def combine_kernel(
    region, basis, field, moments, hot, grad_columns, *rest, owner_rows, slabs, width, step
):
    *pieces, product_out, out, stage, matrix, energies = rest
    batches, blocks, points, size = basis.shape
    me = lax.axis_index("grid")
    me_atoms = lax.axis_index("atoms")
    half = (width - 1) // 2
    stage_rows(stage, pieces[0], pieces[1 : 1 + slabs // 2], pieces[1 + slabs // 2 :], slabs)
    rows = [region[me, position] for position in range(blocks)]
    found = [owner_and_slot(region, me, position, owner_rows) for position in range(blocks)]
    totals = [[jnp.zeros((8, size), F32) for _ in range(blocks)] for _ in range(PARTS)]
    for p in range(blocks):
        owner, slot, count = found[p]
        first = jnp.bitwise_xor(me, owner) * TRAVEL
        for q in range(blocks):
            if abs(q - p) > half:
                matrix[p * size : (p + 1) * size, q * size : (q + 1) * size] = jnp.zeros((size, size), BF16)
                continue
            k = rows[q] - rows[p] + half
            place = jnp.where(
                k == 0,
                travel_place(slot, count, 0),
                jnp.where(k == 1, travel_place(slot, count, 1), travel_place(slot, count, 2)),
            )
            inside = jnp.logical_and(k >= 0, k < width)
            tile = jnp.where(inside, stage[first + place], jnp.zeros((size, size), BF16))
            matrix[p * size : (p + 1) * size, q * size : (q + 1) * size] = tile
            turned = tile.T.astype(F32)
            for c in range(PARTS):
                terms = turned * moments[c, q * size : (q + 1) * size, p * size : (p + 1) * size]
                totals[c][p] = totals[c][p] + jnp.sum(terms.reshape(-1, 8, size), axis=0)
    derivative = [
        jnp.concatenate([jnp.sum(total, axis=0, keepdims=True) for total in totals[c]], axis=1) for c in range(PARTS)
    ]

    energies[...] = jnp.zeros_like(energies)
    lanes = lax.broadcasted_iota(jnp.int32, (points, size), 1)

    @pl.loop(0, batches // step)
    def _(group):
        left = [
            jnp.concatenate([basis[group * step + inner, p] for p in range(blocks)], axis=1) for inner in range(step)
        ]
        left = jnp.concatenate(left, axis=0)
        energy = [jnp.zeros((points, size), F32) for _ in range(step)]
        for q in range(0, blocks, 2):
            product = jnp.dot(left, matrix[:, q * size : (q + 2) * size], preferred_element_type=F32)
            for inner in range(step):
                batch = group * step + inner
                for column in range(2):
                    part = product[inner * points : (inner + 1) * points, column * size : (column + 1) * size]
                    product_out[batch, q + column] = part.astype(BF16)
                    energy[inner] = energy[inner] + part * field[batch, q + column].astype(F32)
        for inner in range(step):
            total = jnp.sum(energy[inner], axis=1, keepdims=True)
            energies[...] = jnp.where(lanes == group * step + inner, total, energies[...])

    lefts = []
    for c in range(PARTS):
        term = jnp.sum(energies[...] * grad_columns[c], axis=0, keepdims=True)
        lefts.append(jnp.concatenate([-2.0 * derivative[c], term], axis=1))
    left = jnp.concatenate(lefts, axis=0)
    high, middle, low = (piece.astype(F32) for piece in split(left))
    left = jnp.concatenate([high, middle, low, jnp.zeros((16 - 3 * PARTS, left.shape[1]), F32)], axis=0).astype(BF16)
    chunk = out.shape[-1]
    for device in range(out.shape[0]):
        sums = lax.dot_general(
            left, hot[device * chunk : (device + 1) * chunk, :], NT, preferred_element_type=F32
        )
        value = sums[:PARTS] + sums[PARTS : 2 * PARTS] + sums[2 * PARTS : 3 * PARTS]
        out[jnp.bitwise_xor(me_atoms, device)] = value


def combine(region, prepared, pieces, shapes):
    basis, field, moments, hot, grad_columns = prepared
    slabs, atom_devices, atom_total, points, blocks, width, owner_rows = shapes
    batches, _, _, size = basis.shape
    step = 16 if batches % 16 == 0 else 1
    vmem = pl.BlockSpec(memory_space=pltpu.VMEM)
    return pl.pallas_call(
        functools.partial(combine_kernel, owner_rows=owner_rows, slabs=slabs, width=width, step=step),
        out_shape=(
            jax.ShapeDtypeStruct(basis.shape, BF16),
            jax.ShapeDtypeStruct((atom_devices, PARTS, atom_total // atom_devices), F32),
        ),
        in_specs=[pl.BlockSpec(memory_space=pltpu.SMEM)] + [vmem] * (5 + len(pieces)),
        out_specs=(vmem, vmem),
        scratch_shapes=[
            pltpu.VMEM((slabs * TRAVEL, size, size), BF16),
            pltpu.VMEM((blocks * size, blocks * size), BF16),
            pltpu.VMEM((points, size), F32),
        ],
        compiler_params=pltpu.CompilerParams(vmem_limit_bytes=VMEM_LIMIT),
    )(region, basis, field, moments, hot, grad_columns, *pieces)


def write_kernel(pattern, product, out, wide, staged, sems):
    batches, blocks, points, size = product.shape

    def copy(batch):
        return pltpu.make_async_copy(staged.at[batch], out.at[batch], sems.at[batch])

    @pl.loop(0, batches // 2)
    def _(pair):
        for inner in range(2):
            batch = pair * 2 + inner
            for t in range(blocks):
                wide[inner, pl.ds(t, points, stride=blocks), :] = product[batch, pattern[t, batch]].astype(F32)
            staged[batch] = wide[inner].astype(BF16)
            copy(batch).start()

    @pl.loop(0, batches)
    def _(batch):
        copy(batch).wait()


def write(pattern, product):
    batches, blocks, points, size = product.shape
    shape = (batches, points * blocks, size)
    return pl.pallas_call(
        write_kernel,
        out_shape=jax.ShapeDtypeStruct(shape, BF16),
        in_specs=[pl.BlockSpec(memory_space=pltpu.SMEM), pl.BlockSpec(memory_space=pltpu.VMEM)],
        out_specs=pl.BlockSpec(memory_space=pl.ANY),
        scratch_shapes=[
            pltpu.VMEM((2, points * blocks, size), F32),
            pltpu.VMEM(shape, BF16),
            pltpu.SemaphoreType.DMA((batches,)),
        ],
        compiler_params=pltpu.CompilerParams(vmem_limit_bytes=VMEM_LIMIT),
        cost_estimate=pl.CostEstimate(flops=0, bytes_accessed=4 * math.prod(shape), transcendentals=0),
    )(pattern.T, product)


def swap_halves(near, ready, atom_devices):
    near, ready = lax.optimization_barrier((near, ready))
    swap = [(i, i ^ 1) for i in range(atom_devices)]
    moves = [swap] * (len(near) - 1) + [swap[1::2]]
    return near, [lax.ppermute(piece, "atoms", pairs) for piece, pairs in zip(near, moves)], ready


def tree_sum(values):
    if len(values) == 1:
        return values[0]
    half = len(values) // 2
    return tree_sum(values[:half]) + tree_sum(values[half:])


def exchange_all(parts, axis, count):
    moved = [lax.ppermute(parts[d], axis, [(i, i ^ d) for i in range(count)]) for d in range(count - 1, 0, -1)]
    moved[:-1] = lax.optimization_barrier(tuple(moved[:-1]))
    return [parts[0], *moved]


def sum_parts(partial_grad, product, slabs, atom_devices):
    total = tree_sum(exchange_all([partial_grad[d] for d in range(atom_devices)], "atoms", atom_devices))
    total, product = lax.optimization_barrier((total, product))
    return tree_sum(exchange_all([total] * slabs, "grid", slabs)), product


def local(
    basis,
    basis_grad,
    exchange_field,
    weights,
    weight_grad,
    density,
    region,
    pattern,
    fn_atom,
    batch_atom,
):
    batches, points, blocks, size = basis.shape
    owner_rows, width = density.shape[:2]
    slabs = lax.axis_size("grid")
    atom_devices = lax.axis_size("atoms")
    atom_total = fn_atom.shape[0] // (10 * slabs * atom_devices) * slabs * atom_devices
    shapes = (slabs, atom_devices, atom_total, points, blocks, width, owner_rows)
    flat_basis = basis.reshape(batches, points * blocks, size)
    flat_field = exchange_field.reshape(batches, points * blocks, size)
    flat_grad = basis_grad.reshape(PARTS, batches, points * blocks, size)
    own, near = fetch_rows(region, density, slabs, atom_devices)
    if region.shape[1] == blocks:
        basis_wide, field_wide, weighted, grads = reorder(
            pattern, flat_basis, flat_field, flat_grad, weights, points, blocks
        )
        ready = (basis_wide, field_wide, build_moments(weighted, grads), batch_atom)
        near, far, (basis_wide, field_wide, moments, batch_atom) = swap_halves(near, ready, atom_devices)
        hot, grad_columns = atom_matrix(region, fn_atom, batch_atom, weight_grad, blocks, size, atom_total)
        ready = (basis_wide, field_wide, moments, hot, grad_columns)
        product, partial_grad = combine(region, ready, [own, *near, *far], shapes)
        gradient, product = sum_parts(partial_grad, product, slabs, atom_devices)
        contracted = write(pattern, product)
        return contracted.reshape(basis.shape), gradient
    ready = relayout(in_hbm(flat_basis), in_hbm(flat_field), points, blocks)
    near, far, (basis_wide, field_wide) = swap_halves(near, ready, atom_devices)
    tiles, partial_grad = partial_gradient(
        region,
        pattern,
        basis_wide,
        field_wide,
        in_hbm(flat_grad),
        weights,
        weight_grad,
        fn_atom,
        batch_atom,
        [own, *near, *far],
        shapes,
    )
    gradient, basis_wide = sum_parts(partial_grad, basis_wide, slabs, atom_devices)
    contracted = contract(region, pattern, basis_wide, tiles, points, blocks, width)
    return contracted.reshape(basis.shape), gradient


def solution(mesh):
    placed = (
        P(("groups", "grid", "atoms"), None, None, None),
        P(None, ("groups", "grid", "atoms"), None, None, None),
        P(("groups", "grid", "atoms"), None, None, None),
        P(("groups", "grid", "atoms"), None),
        P(None, ("groups", "grid", "atoms"), None),
        P(("groups", "grid"), None, None, None),
        P("groups", None),
        P(("groups", "grid", "atoms"), None),
        P("groups"),
        P(("groups", "grid", "atoms")),
    )
    return jax.shard_map(
        local,
        mesh=mesh,
        in_specs=placed,
        out_specs=(P(("groups", "grid", "atoms"), None, None, None), P(None, ("groups", "atoms"))),
        check_vma=False,
    )
```

```python
import functools
import math

import jax
import jax.numpy as jnp
from jax import lax
from jax.experimental import pallas as pl
from jax.experimental.pallas import tpu as pltpu
from jax.sharding import PartitionSpec as P

TRAVEL = 5
PARTS = 3
F32 = jnp.float32
BF16 = jnp.bfloat16
NT = (((1,), (1,)), ((), ()))
TN = (((0,), (0,)), ((), ()))
VMEM_LIMIT = 32 * 1024 * 1024


def owner_and_slot(region, slab, position, owner_rows):
    owner = lax.div(region[slab, position], owner_rows)
    slot = jnp.int32(0)
    count = jnp.int32(0)
    for other in range(region.shape[1]):
        same = jnp.where(lax.div(region[slab, other], owner_rows) == owner, 1, 0)
        count = count + same
        slot = slot + jnp.where(other < position, same, 0)
    return owner, slot, count


def travel_place(slot, count, k):
    if k == 0:
        return jnp.where(slot == 0, 4, 2)
    if k == 1:
        return jnp.where(slot == 0, 0, 3)
    return jnp.where(jnp.logical_and(slot == 0, count == 2), 1, 4)


def partners(slabs):
    return [(1, 1)] + [(shift + 1, shift) for shift in range(2, slabs, 2)]


def send_kernel(region_hbm, density, *rest):
    *outs, region, sems, region_sem = rest
    fetch = pltpu.make_async_copy(region_hbm, region, region_sem)
    fetch.start()
    fetch.wait()
    me = lax.axis_index("grid")
    core = lax.rem(lax.axis_index("atoms"), 2)
    slabs, size = region.shape
    owner_rows = density.shape[0]
    rows = density.shape[-2]
    copies = []
    for number, ((low, high), out) in enumerate(zip([(0, 0)] + partners(slabs), outs)):
        slab = jnp.bitwise_xor(me, jnp.where(core == 0, low, high))
        base = jnp.int32(owner_rows)
        count = jnp.int32(0)
        for position in range(size):
            row = region[slab, position] - me * owner_rows
            mine = jnp.logical_and(row >= 0, row < owner_rows)
            base = jnp.minimum(base, jnp.where(mine, row, owner_rows))
            count = count + jnp.where(mine, 1, 0)
        base = jnp.where(count == 0, 0, base)
        after = jnp.minimum(base + 1, owner_rows - 1)
        lower = base == 0
        edge = jnp.where(jnp.logical_and(count == 2, jnp.logical_not(lower)), after, base)
        kept = out.shape[1]
        first = 0 if kept == rows else pl.multiple_of(core * kept, kept)
        here = pl.ds(first, kept)
        pairs = (
            (density.at[base, pl.ds(1, 2), here, :], out.at[pl.ds(0, 2)]),
            (density.at[after, pl.ds(0, 2), here, :], out.at[pl.ds(2, 2)]),
            (density.at[edge, jnp.where(lower, 0, 2), here, :], out.at[4]),
        )
        for part, (source, target) in enumerate(pairs):
            copies.append(pltpu.make_async_copy(source, target, sems.at[number, part]))
    for copy in copies:
        copy.start()
    for copy in copies:
        copy.wait()


def in_hbm(array):
    return pltpu.with_memory_space_constraint(array, pltpu.HBM)


def rows_to_send(region, density, slabs):
    size = density.shape[-1]
    exchanges = partners(slabs)
    kept = [size] + [size if low != high else size // 2 for low, high in exchanges]
    hbm = pl.BlockSpec(memory_space=pl.ANY)
    return pl.pallas_call(
        send_kernel,
        out_shape=[jax.ShapeDtypeStruct((TRAVEL, rows, size), density.dtype) for rows in kept],
        in_specs=[hbm, hbm],
        out_specs=[pl.BlockSpec(memory_space=pltpu.VMEM)] * len(kept),
        scratch_shapes=[
            pltpu.SMEM(region.shape, jnp.int32),
            pltpu.SemaphoreType.DMA((len(kept), 3)),
            pltpu.SemaphoreType.DMA,
        ],
        compiler_params=pltpu.CompilerParams(vmem_limit_bytes=VMEM_LIMIT),
    )(in_hbm(region), in_hbm(density))


def fetch_rows(region, density, slabs, atom_devices):
    own, *outgoing = rows_to_send(region, density, slabs)
    near = []
    for shifts, piece in zip(partners(slabs), outgoing):
        moves = [
            (z * atom_devices + a, (z ^ shifts[a % 2]) * atom_devices + a) for z in range(slabs) for a in range(atom_devices)
        ]
        near.append(lax.ppermute(piece, ("grid", "atoms"), moves))
    return own, near


def stage_rows(stage, own, near, far, slabs):
    core = lax.rem(lax.axis_index("atoms"), 2)
    for place in range(TRAVEL):
        stage[place] = own[place]
    for (low, high), here, there in zip(partners(slabs), near, far):
        kept = here.shape[1]
        mine = jnp.where(core == 0, low, high) * TRAVEL
        other = jnp.where(core == 0, high, low) * TRAVEL
        for place in range(TRAVEL):
            if low != high:
                stage[mine + place] = here[place]
                stage[other + place] = there[place]
            else:
                stage[mine + place, pl.ds(pl.multiple_of(core * kept, kept), kept), :] = here[place]
                stage[mine + place, pl.ds(pl.multiple_of((1 - core) * kept, kept), kept), :] = there[place]


def block_major(x_ref, wide, points, blocks):
    wide[...] = x_ref[0].astype(F32)
    return [wide[pl.ds(s, points, stride=blocks), :] for s in range(blocks)]


def relayout_kernel(basis, field, basis_out, field_out, wide, *, points, blocks):
    size = basis.shape[-1]
    for source, target in ((basis, basis_out), (field, field_out)):
        for s, part in enumerate(block_major(source, wide, points, blocks)):
            target[0, :, s * size : (s + 1) * size] = part.astype(BF16)


def relayout(basis, field, points, blocks):
    batches, rows, size = basis.shape
    here = pl.BlockSpec((1, rows, size), lambda b: (b, 0, 0))
    there = pl.BlockSpec((1, points, blocks * size), lambda b: (b, 0, 0))
    shape = jax.ShapeDtypeStruct((batches, points, blocks * size), BF16)
    return pl.pallas_call(
        functools.partial(relayout_kernel, points=points, blocks=blocks),
        grid=(batches,),
        out_shape=(shape, shape),
        in_specs=[here, here],
        out_specs=(there, there),
        scratch_shapes=[pltpu.VMEM((rows, size), F32)],
        compiler_params=pltpu.CompilerParams(vmem_limit_bytes=VMEM_LIMIT),
        cost_estimate=pl.CostEstimate(flops=0, bytes_accessed=8 * batches * rows * size, transcendentals=0),
    )(basis, field)


def batch_matrix(region, pattern, tiles, slab, batch, blocks, width):
    half = (width - 1) // 2
    none = tiles.shape[0] - 1
    places = [pattern[batch, s] for s in range(blocks)]
    rows = [region[slab, place] for place in places]
    strips = []
    for s in range(blocks):
        strip = []
        for t in range(blocks):
            k = rows[t] - rows[s] + half
            inside = jnp.logical_and(k >= 0, k < width)
            strip.append(tiles[jnp.where(inside, places[s] * width + k, none)])
        strips.append(jnp.concatenate(strip, axis=1))
    return jnp.concatenate(strips, axis=0)


def split(values):
    high = values.astype(BF16)
    rest = values - high.astype(F32)
    middle = rest.astype(BF16)
    low = (rest - middle.astype(F32)).astype(BF16)
    return high, middle, low


def gradient_kernel(
    region,
    pattern,
    basis,
    field,
    basis_grad,
    weights,
    weight_grad,
    fn_atom,
    batch_atom,
    places,
    *rest,
    points,
    blocks,
    width,
    owner_rows,
    slabs,
):
    *pieces, tiles, out, stage, spread, sums, energy_sums = rest
    batch = pl.program_id(0)
    batches = pl.num_programs(0)
    me = lax.axis_index("grid")
    me_atoms = lax.axis_index("atoms")
    size = tiles.shape[-1]
    region_size = region.shape[1]

    @pl.when(batch == 0)
    def _():
        tiles[region_size * width] = jnp.zeros((size, size), BF16)
        stage_rows(stage, pieces[0], pieces[1 : 1 + slabs // 2], pieces[1 + slabs // 2 :], slabs)
        for position in range(region_size):
            owner, slot, count = owner_and_slot(region, me, position, owner_rows)
            shift = jnp.bitwise_xor(me, owner)
            for k in range(width):
                tiles[position * width + k] = stage[shift * TRAVEL + travel_place(slot, count, k)]

    matrix = batch_matrix(region, pattern, tiles, me, batch, blocks, width)
    potential = lax.dot_general(field[0], matrix, NT, preferred_element_type=F32)
    rows = jnp.concatenate(
        [weights[pl.ds(batch, 1), :]]
        + [weight_grad[c, pl.ds(batch, 1), :] for c in range(PARTS)]
        + [jnp.zeros((8 - 1 - PARTS, points), F32)],
        axis=0,
    )
    columns = rows.T
    weight = columns[:, 0:1]
    energy = jnp.zeros((points, size), F32)
    for s in range(blocks):
        here = potential[:, s * size : (s + 1) * size]
        energy = energy + basis[0, :, s * size : (s + 1) * size].astype(F32) * here
        spread[pl.ds(s, points, stride=blocks), :] = here * weight
    scaled = spread[...]
    place = pl.ds(pl.multiple_of(batch * 8, 8), 8)
    for c in range(PARTS):
        terms = basis_grad[c, 0].astype(F32) * scaled
        sums[c, place, :] = jnp.sum(terms.reshape(-1, 8, size), axis=0)
        terms = energy * columns[:, 1 + c : 2 + c]
        energy_sums[c, place, :] = jnp.sum(terms.reshape(-1, 8, size), axis=0)

    @pl.when(batch == batches - 1)
    def _():
        padded = max(8, region_size)
        chosen = lax.broadcasted_iota(jnp.int32, (padded, places.shape[1]), 0) == places[...]
        chosen = chosen.astype(BF16)
        blocks_sum = []
        for c in range(PARTS):
            total = jnp.zeros((padded, size), F32)
            for piece in split(sums[c]):
                total = total + jnp.dot(chosen, piece, preferred_element_type=F32)
            blocks_sum.append(-2.0 * total)
        lefts = []
        for position in range(region_size):
            stack = jnp.concatenate([total[position : position + 1] for total in blocks_sum], axis=0)
            high, middle, low = (piece.astype(F32) for piece in split(stack))
            lefts.append(jnp.concatenate([high, middle, low, jnp.zeros((16 - 3 * PARTS, size), F32)], axis=0))
        left = jnp.concatenate(lefts, axis=1).astype(BF16)
        chunk = out.shape[-1]
        scale = [jnp.sum(energy_sums[c], axis=1, keepdims=True) for c in range(PARTS)]
        for device in range(out.shape[0]):
            atoms = lax.broadcasted_iota(jnp.int32, (chunk, size), 0) + device * chunk
            hot = [
                jnp.where(atoms == fn_atom[pl.ds(region[me, position], 1), :], 1.0, 0.0).astype(BF16)
                for position in range(region_size)
            ]
            found = lax.dot_general(left, jnp.concatenate(hot, axis=1), NT, preferred_element_type=F32)
            atoms = lax.broadcasted_iota(jnp.int32, (batch_atom.shape[0], chunk), 1) + device * chunk
            mine = atoms == batch_atom[...]
            for c in range(PARTS):
                value = found[c : c + 1] + found[PARTS + c : PARTS + c + 1] + found[2 * PARTS + c : 2 * PARTS + c + 1]
                value = value + jnp.sum(jnp.where(mine, scale[c], 0.0), axis=0, keepdims=True)
                out[jnp.bitwise_xor(me_atoms, device), c : c + 1, :] = value


def partial_gradient(
    region, pattern, basis, field, basis_grad, weights, weight_grad, fn_atom, batch_atom, pieces, shapes
):
    slabs, atom_devices, atom_total, points, blocks, width, owner_rows = shapes
    batches, _, columns = basis.shape
    size = columns // blocks
    region_size = region.shape[1]
    fn_atom = fn_atom.reshape(-1, size)
    places = jnp.broadcast_to(pattern[:, None, :], (batches, 8 // blocks, blocks)).reshape(1, -1)
    batch_atom = jnp.broadcast_to(batch_atom[:, None], (batches, 8)).reshape(-1, 1)
    block = pl.BlockSpec((1, points, columns), lambda b, *_: (b, 0, 0))
    whole = pl.BlockSpec(memory_space=pltpu.VMEM)
    tile_shape = (region_size * width + 1, size, size)
    out_shape = (atom_devices, PARTS, atom_total // atom_devices)
    return pl.pallas_call(
        functools.partial(
            gradient_kernel, points=points, blocks=blocks, width=width, owner_rows=owner_rows, slabs=slabs
        ),
        grid_spec=pltpu.PrefetchScalarGridSpec(
            num_scalar_prefetch=2,
            grid=(batches,),
            in_specs=[
                block,
                block,
                pl.BlockSpec((PARTS, 1, points * blocks, size), lambda b, *_: (0, b, 0, 0)),
            ]
            + [whole] * (5 + len(pieces)),
            out_specs=(whole, whole),
            scratch_shapes=[
                pltpu.VMEM((slabs * TRAVEL, size, size), BF16),
                pltpu.VMEM((points * blocks, size), F32),
                pltpu.VMEM((PARTS, batches * 8, size), F32),
                pltpu.VMEM((PARTS, batches * 8, size), F32),
            ],
        ),
        out_shape=(jax.ShapeDtypeStruct(tile_shape, BF16), jax.ShapeDtypeStruct(out_shape, F32)),
        compiler_params=pltpu.CompilerParams(vmem_limit_bytes=VMEM_LIMIT),
    )(region, pattern, basis, field, basis_grad, weights, weight_grad, fn_atom, batch_atom, places, *pieces)


def product_kernel(region, pattern, basis, tiles, out, spread, *, points, blocks, width):
    me = lax.axis_index("grid")
    size = tiles.shape[-1]
    matrix = batch_matrix(region, pattern, tiles, me, pl.program_id(0), blocks, width)
    product = jnp.dot(basis[0], matrix, preferred_element_type=F32)
    for t in range(blocks):
        spread[pl.ds(t, points, stride=blocks), :] = product[:, t * size : (t + 1) * size]
    out[0] = spread[...].astype(BF16)


def contract(region, pattern, basis, tiles, points, blocks, width):
    batches, _, columns = basis.shape
    size = columns // blocks
    return pl.pallas_call(
        functools.partial(product_kernel, points=points, blocks=blocks, width=width),
        grid_spec=pltpu.PrefetchScalarGridSpec(
            num_scalar_prefetch=2,
            grid=(batches,),
            in_specs=[
                pl.BlockSpec((1, points, columns), lambda b, *_: (b, 0, 0)),
                pl.BlockSpec(memory_space=pltpu.VMEM),
            ],
            out_specs=pl.BlockSpec((1, points * blocks, size), lambda b, *_: (b, 0, 0)),
            scratch_shapes=[pltpu.VMEM((points * blocks, size), F32)],
        ),
        out_shape=jax.ShapeDtypeStruct((batches, points * blocks, size), BF16),
        compiler_params=pltpu.CompilerParams(vmem_limit_bytes=VMEM_LIMIT),
        cost_estimate=pl.CostEstimate(
            flops=2 * batches * points * columns * columns,
            bytes_accessed=4 * batches * points * columns,
            transcendentals=0,
        ),
    )(region, pattern, basis, tiles)


def reorder_kernel(
    pattern_hbm,
    basis,
    field,
    basis_grad,
    weights_hbm,
    basis_out,
    field_out,
    weighted,
    grads,
    pattern,
    weights,
    columns,
    basis_in,
    field_in,
    grad_in,
    wide,
    sems,
    small_sems,
):
    batches, blocks, points, size = basis_out.shape

    def copies(batch):
        return (
            pltpu.make_async_copy(field.at[batch], field_in.at[batch], sems.at[batch, 0]),
            pltpu.make_async_copy(basis.at[batch], basis_in.at[batch], sems.at[batch, 1]),
            pltpu.make_async_copy(basis_grad.at[:, batch], grad_in.at[:, batch], sems.at[batch, 2]),
        )

    small = (
        pltpu.make_async_copy(pattern_hbm, pattern, small_sems.at[0]),
        pltpu.make_async_copy(weights_hbm, weights, small_sems.at[1]),
    )
    for copy in small:
        copy.start()

    @pl.loop(0, batches)
    def _(batch):
        for copy in copies(batch):
            copy.start()

    for copy in small:
        copy.wait()
    rows = jnp.concatenate([weights[...], jnp.zeros((size - batches, points), F32)], axis=0).T
    for batch in range(batches):
        columns[batch] = jnp.broadcast_to(rows[:, batch : batch + 1], (points, size))

    @pl.loop(0, batches)
    def _(batch):
        for copy in copies(batch):
            copy.wait()
        points_here = pl.ds(pl.multiple_of(batch * points, points), points)
        places = [pattern[s, batch] for s in range(blocks)]
        wide[0] = field_in[batch].astype(F32)
        wide[1] = basis_in[batch].astype(F32)
        for c in range(PARTS):
            wide[2 + c] = grad_in[c, batch].astype(F32)
        for s, place in enumerate(places):
            strided = pl.ds(s, points, stride=blocks)
            values = wide[0, strided, :]
            field_out[batch, place] = values.astype(BF16)
            weighted[place, points_here, :] = (values * columns[batch]).astype(BF16)
            basis_out[batch, place] = wide[1, strided, :].astype(BF16)
            for c in range(PARTS):
                grads[c, place, points_here, :] = wide[2 + c, strided, :].astype(BF16)


def reorder(pattern, basis, field, basis_grad, weights, points, blocks):
    batches, rows, size = basis.shape
    hbm = pl.BlockSpec(memory_space=pl.ANY)
    vmem = pl.BlockSpec(memory_space=pltpu.VMEM)
    ordered = jax.ShapeDtypeStruct((batches, blocks, points, size), BF16)
    return pl.pallas_call(
        reorder_kernel,
        out_shape=(
            ordered,
            ordered,
            jax.ShapeDtypeStruct((blocks, batches * points, size), BF16),
            jax.ShapeDtypeStruct((PARTS, blocks, batches * points, size), BF16),
        ),
        in_specs=[hbm] * 5,
        out_specs=(vmem,) * 4,
        scratch_shapes=[
            pltpu.SMEM((blocks, batches), jnp.int32),
            pltpu.VMEM(weights.shape, F32),
            pltpu.VMEM((batches, points, size), F32),
            pltpu.VMEM((batches, rows, size), BF16),
            pltpu.VMEM((batches, rows, size), BF16),
            pltpu.VMEM((PARTS, batches, rows, size), BF16),
            pltpu.VMEM((2 + PARTS, rows, size), F32),
            pltpu.SemaphoreType.DMA((batches, 3)),
            pltpu.SemaphoreType.DMA((2,)),
        ],
        compiler_params=pltpu.CompilerParams(vmem_limit_bytes=VMEM_LIMIT),
        cost_estimate=pl.CostEstimate(
            flops=0, bytes_accessed=2 * (2 + PARTS) * batches * rows * size, transcendentals=0
        ),
    )(in_hbm(pattern.T), in_hbm(basis), in_hbm(field), in_hbm(basis_grad), in_hbm(weights))


def moment_kernel(weighted, grads, moments):
    blocks, _, size = grads.shape[1:]
    for p in range(0, blocks, 2):
        first, last = max(p - 1, 0), min(p + 3, blocks)
        left = jnp.concatenate([weighted[place] for place in range(first, last)], axis=1)
        for c in range(PARTS):
            right = jnp.concatenate([grads[c, p], grads[c, p + 1]], axis=1)
            moments[c, first * size : last * size, p * size : (p + 2) * size] = lax.dot_general(
                left, right, TN, preferred_element_type=F32
            )


def build_moments(weighted, grads):
    blocks, depth, size = grads.shape[1:]
    vmem = pl.BlockSpec(memory_space=pltpu.VMEM)
    return pl.pallas_call(
        moment_kernel,
        out_shape=jax.ShapeDtypeStruct((PARTS, blocks * size, blocks * size), F32),
        in_specs=[vmem, vmem],
        out_specs=vmem,
        compiler_params=pltpu.CompilerParams(vmem_limit_bytes=VMEM_LIMIT),
        cost_estimate=pl.CostEstimate(
            flops=2 * PARTS * depth * (blocks * size) ** 2, bytes_accessed=0, transcendentals=0
        ),
    )(weighted, grads)


def atom_kernel(region, fn_atom, batch_atom, weight_grad, hot, grad_columns):
    batches, points = weight_grad.shape[1:]
    size = fn_atom.shape[1]
    blocks = region.shape[1]
    me = lax.axis_index("grid")
    atoms = lax.broadcasted_iota(jnp.int32, (hot.shape[0], size), 0)
    ids = jnp.concatenate([batch_atom[...], jnp.full((1, size - batches), -1, jnp.int32)], axis=1)
    hot[:, blocks * size :] = jnp.where(atoms == ids, 1.0, 0.0).astype(BF16)

    @pl.loop(0, blocks)
    def _(position):
        ids = fn_atom[pl.ds(region[me, position], 1), :]
        columns = pl.ds(pl.multiple_of(position * size, size), size)
        hot[:, columns] = jnp.where(atoms == ids, 1.0, 0.0).astype(BF16)

    for c in range(PARTS):
        padding = jnp.zeros((size - batches, points), F32)
        grad_columns[c] = jnp.concatenate([weight_grad[c], padding], axis=0).T


def atom_matrix(region, fn_atom, batch_atom, weight_grad, blocks, size, atom_total):
    vmem = pl.BlockSpec(memory_space=pltpu.VMEM)
    return pl.pallas_call(
        atom_kernel,
        out_shape=(
            jax.ShapeDtypeStruct((atom_total, (blocks + 1) * size), BF16),
            jax.ShapeDtypeStruct((PARTS, weight_grad.shape[2], size), F32),
        ),
        in_specs=[pl.BlockSpec(memory_space=pltpu.SMEM)] + [vmem] * 3,
        out_specs=(vmem, vmem),
        compiler_params=pltpu.CompilerParams(vmem_limit_bytes=VMEM_LIMIT),
        cost_estimate=pl.CostEstimate(flops=1000000000, bytes_accessed=2 * atom_total * size, transcendentals=0),
    )(region, fn_atom.reshape(-1, size), batch_atom.reshape(1, -1), weight_grad)


def combine_kernel(
    region, basis, field, moments, hot, grad_columns, *rest, owner_rows, slabs, width, step
):
    *pieces, product_out, out, stage, matrix, energies = rest
    batches, blocks, points, size = basis.shape
    me = lax.axis_index("grid")
    me_atoms = lax.axis_index("atoms")
    half = (width - 1) // 2
    stage_rows(stage, pieces[0], pieces[1 : 1 + slabs // 2], pieces[1 + slabs // 2 :], slabs)
    rows = [region[me, position] for position in range(blocks)]
    found = [owner_and_slot(region, me, position, owner_rows) for position in range(blocks)]
    totals = [[jnp.zeros((8, size), F32) for _ in range(blocks)] for _ in range(PARTS)]
    for p in range(blocks):
        owner, slot, count = found[p]
        first = jnp.bitwise_xor(me, owner) * TRAVEL
        for q in range(blocks):
            if abs(q - p) > half:
                matrix[p * size : (p + 1) * size, q * size : (q + 1) * size] = jnp.zeros((size, size), BF16)
                continue
            k = rows[q] - rows[p] + half
            place = jnp.where(
                k == 0,
                travel_place(slot, count, 0),
                jnp.where(k == 1, travel_place(slot, count, 1), travel_place(slot, count, 2)),
            )
            inside = jnp.logical_and(k >= 0, k < width)
            tile = jnp.where(inside, stage[first + place], jnp.zeros((size, size), BF16))
            matrix[p * size : (p + 1) * size, q * size : (q + 1) * size] = tile
            turned = tile.T.astype(F32)
            for c in range(PARTS):
                terms = turned * moments[c, q * size : (q + 1) * size, p * size : (p + 1) * size]
                totals[c][p] = totals[c][p] + jnp.sum(terms.reshape(-1, 8, size), axis=0)
    derivative = [
        jnp.concatenate([jnp.sum(total, axis=0, keepdims=True) for total in totals[c]], axis=1) for c in range(PARTS)
    ]

    energies[...] = jnp.zeros_like(energies)
    lanes = lax.broadcasted_iota(jnp.int32, (points, size), 1)

    @pl.loop(0, batches // step)
    def _(group):
        left = [
            jnp.concatenate([basis[group * step + inner, p] for p in range(blocks)], axis=1) for inner in range(step)
        ]
        left = jnp.concatenate(left, axis=0)
        energy = [jnp.zeros((points, size), F32) for _ in range(step)]
        for q in range(0, blocks, 2):
            product = jnp.dot(left, matrix[:, q * size : (q + 2) * size], preferred_element_type=F32)
            for inner in range(step):
                batch = group * step + inner
                for column in range(2):
                    part = product[inner * points : (inner + 1) * points, column * size : (column + 1) * size]
                    product_out[batch, q + column] = part.astype(BF16)
                    energy[inner] = energy[inner] + part * field[batch, q + column].astype(F32)
        for inner in range(step):
            total = jnp.sum(energy[inner], axis=1, keepdims=True)
            energies[...] = jnp.where(lanes == group * step + inner, total, energies[...])

    lefts = []
    for c in range(PARTS):
        term = jnp.sum(energies[...] * grad_columns[c], axis=0, keepdims=True)
        lefts.append(jnp.concatenate([-2.0 * derivative[c], term], axis=1))
    left = jnp.concatenate(lefts, axis=0)
    high, middle, low = (piece.astype(F32) for piece in split(left))
    left = jnp.concatenate([high, middle, low, jnp.zeros((16 - 3 * PARTS, left.shape[1]), F32)], axis=0).astype(BF16)
    chunk = out.shape[-1]
    for device in range(out.shape[0]):
        sums = lax.dot_general(
            left, hot[device * chunk : (device + 1) * chunk, :], NT, preferred_element_type=F32
        )
        value = sums[:PARTS] + sums[PARTS : 2 * PARTS] + sums[2 * PARTS : 3 * PARTS]
        out[jnp.bitwise_xor(me_atoms, device)] = value


def combine(region, prepared, pieces, shapes):
    basis, field, moments, hot, grad_columns = prepared
    slabs, atom_devices, atom_total, points, blocks, width, owner_rows = shapes
    batches, _, _, size = basis.shape
    step = 16 if batches % 16 == 0 else 1
    vmem = pl.BlockSpec(memory_space=pltpu.VMEM)
    return pl.pallas_call(
        functools.partial(combine_kernel, owner_rows=owner_rows, slabs=slabs, width=width, step=step),
        out_shape=(
            jax.ShapeDtypeStruct(basis.shape, BF16),
            jax.ShapeDtypeStruct((atom_devices, PARTS, atom_total // atom_devices), F32),
        ),
        in_specs=[pl.BlockSpec(memory_space=pltpu.SMEM)] + [vmem] * (5 + len(pieces)),
        out_specs=(vmem, vmem),
        scratch_shapes=[
            pltpu.VMEM((slabs * TRAVEL, size, size), BF16),
            pltpu.VMEM((blocks * size, blocks * size), BF16),
            pltpu.VMEM((points, size), F32),
        ],
        compiler_params=pltpu.CompilerParams(vmem_limit_bytes=VMEM_LIMIT),
    )(region, basis, field, moments, hot, grad_columns, *pieces)


def write_kernel(pattern, product, out, wide, staged, sems):
    batches, blocks, points, size = product.shape

    def copy(batch):
        return pltpu.make_async_copy(staged.at[batch], out.at[batch], sems.at[batch])

    @pl.loop(0, batches // 2)
    def _(pair):
        for inner in range(2):
            batch = pair * 2 + inner
            for t in range(blocks):
                wide[inner, pl.ds(t, points, stride=blocks), :] = product[batch, pattern[t, batch]].astype(F32)
            staged[batch] = wide[inner].astype(BF16)
            copy(batch).start()

    @pl.loop(0, batches)
    def _(batch):
        copy(batch).wait()


def write(pattern, product):
    batches, blocks, points, size = product.shape
    shape = (batches, points * blocks, size)
    return pl.pallas_call(
        write_kernel,
        out_shape=jax.ShapeDtypeStruct(shape, BF16),
        in_specs=[pl.BlockSpec(memory_space=pltpu.SMEM), pl.BlockSpec(memory_space=pltpu.VMEM)],
        out_specs=pl.BlockSpec(memory_space=pl.ANY),
        scratch_shapes=[
            pltpu.VMEM((2, points * blocks, size), F32),
            pltpu.VMEM(shape, BF16),
            pltpu.SemaphoreType.DMA((batches,)),
        ],
        compiler_params=pltpu.CompilerParams(vmem_limit_bytes=VMEM_LIMIT),
        cost_estimate=pl.CostEstimate(flops=0, bytes_accessed=4 * math.prod(shape), transcendentals=0),
    )(pattern.T, product)


def swap_halves(near, ready, atom_devices):
    near, ready = lax.optimization_barrier((near, ready))
    swap = [(i, i ^ 1) for i in range(atom_devices)]
    return near, [lax.ppermute(piece, "atoms", swap) for piece in near], ready


def tree_sum(values):
    if len(values) == 1:
        return values[0]
    half = len(values) // 2
    return tree_sum(values[:half]) + tree_sum(values[half:])


def exchange_all(parts, axis, count):
    return [parts[0]] + [
        lax.ppermute(parts[d], axis, [(i, i ^ d) for i in range(count)]) for d in range(count - 1, 0, -1)
    ]


def sum_parts(partial_grad, contracted, slabs, atom_devices):
    parts = exchange_all([partial_grad[d] for d in range(atom_devices)], "atoms", atom_devices)
    parts, contracted = lax.optimization_barrier((parts, contracted))
    own, *far, near = exchange_all([tree_sum(parts)] * slabs, "grid", slabs)
    far = lax.optimization_barrier(far)
    return tree_sum([own, *far, near]), contracted


def local(
    basis,
    basis_grad,
    exchange_field,
    weights,
    weight_grad,
    density,
    region,
    pattern,
    fn_atom,
    batch_atom,
):
    batches, points, blocks, size = basis.shape
    owner_rows, width = density.shape[:2]
    slabs = lax.axis_size("grid")
    atom_devices = lax.axis_size("atoms")
    atom_total = fn_atom.shape[0] // (10 * slabs * atom_devices) * slabs * atom_devices
    shapes = (slabs, atom_devices, atom_total, points, blocks, width, owner_rows)
    flat_basis = basis.reshape(batches, points * blocks, size)
    flat_field = exchange_field.reshape(batches, points * blocks, size)
    flat_grad = basis_grad.reshape(PARTS, batches, points * blocks, size)
    own, near = fetch_rows(region, density, slabs, atom_devices)
    if region.shape[1] == blocks:
        basis_wide, field_wide, weighted, grads = reorder(
            pattern, flat_basis, flat_field, flat_grad, weights, points, blocks
        )
        ready = (basis_wide, field_wide, build_moments(weighted, grads), batch_atom)
        near, far, (basis_wide, field_wide, moments, batch_atom) = swap_halves(near, ready, atom_devices)
        hot, grad_columns = atom_matrix(region, fn_atom, batch_atom, weight_grad, blocks, size, atom_total)
        ready = (basis_wide, field_wide, moments, hot, grad_columns)
        product, partial_grad = combine(region, ready, [own, *near, *far], shapes)
        gradient, contracted = sum_parts(partial_grad, write(pattern, product), slabs, atom_devices)
        return contracted.reshape(basis.shape), gradient
    ready = relayout(in_hbm(flat_basis), in_hbm(flat_field), points, blocks)
    near, far, (basis_wide, field_wide) = swap_halves(near, ready, atom_devices)
    tiles, partial_grad = partial_gradient(
        region,
        pattern,
        basis_wide,
        field_wide,
        in_hbm(flat_grad),
        weights,
        weight_grad,
        fn_atom,
        batch_atom,
        [own, *near, *far],
        shapes,
    )
    contracted = contract(region, pattern, basis_wide, tiles, points, blocks, width)
    gradient, contracted = sum_parts(partial_grad, contracted, slabs, atom_devices)
    return contracted.reshape(basis.shape), gradient


def solution(mesh):
    placed = (
        P(("groups", "grid", "atoms"), None, None, None),
        P(None, ("groups", "grid", "atoms"), None, None, None),
        P(("groups", "grid", "atoms"), None, None, None),
        P(("groups", "grid", "atoms"), None),
        P(None, ("groups", "grid", "atoms"), None),
        P(("groups", "grid"), None, None, None),
        P("groups", None),
        P(("groups", "grid", "atoms"), None),
        P("groups"),
        P(("groups", "grid", "atoms")),
    )
    return jax.shard_map(
        local,
        mesh=mesh,
        in_specs=placed,
        out_specs=(P(("groups", "grid", "atoms"), None, None, None), P(None, ("groups", "atoms"))),
        check_vma=False,
    )
```

```python
import functools
import math

import jax
import jax.numpy as jnp
from jax import lax
from jax.experimental import pallas as pl
from jax.experimental.pallas import tpu as pltpu
from jax.sharding import PartitionSpec as P

TRAVEL = 5
PARTS = 3
F32 = jnp.float32
BF16 = jnp.bfloat16
NT = (((1,), (1,)), ((), ()))
TN = (((0,), (0,)), ((), ()))
VMEM_LIMIT = 32 * 1024 * 1024


def owner_and_slot(region, slab, position, owner_rows):
    owner = lax.div(region[slab, position], owner_rows)
    slot = jnp.int32(0)
    count = jnp.int32(0)
    for other in range(region.shape[1]):
        same = jnp.where(lax.div(region[slab, other], owner_rows) == owner, 1, 0)
        count = count + same
        slot = slot + jnp.where(other < position, same, 0)
    return owner, slot, count


def travel_place(slot, count, k):
    if k == 0:
        return jnp.where(slot == 0, 4, 2)
    if k == 1:
        return jnp.where(slot == 0, 0, 3)
    return jnp.where(jnp.logical_and(slot == 0, count == 2), 1, 4)


def partners(slabs):
    return [(1, 1)] + [(shift + 1, shift) for shift in range(2, slabs, 2)]


def moves_over_grid(shifts, slabs, atom_devices):
    return [
        (z * atom_devices + a, (z ^ shifts[a % 2]) * atom_devices + a) for z in range(slabs) for a in range(atom_devices)
    ]


def send_kernel(region_hbm, density, *rest):
    *outs, region, sems, region_sem = rest
    fetch = pltpu.make_async_copy(region_hbm, region, region_sem)
    fetch.start()
    fetch.wait()
    me = lax.axis_index("grid")
    core = lax.rem(lax.axis_index("atoms"), 2)
    slabs, size = region.shape
    owner_rows = density.shape[0]
    rows = density.shape[-2]
    copies = []
    for number, ((low, high), out) in enumerate(zip([(0, 0)] + partners(slabs), outs)):
        slab = jnp.bitwise_xor(me, jnp.where(core == 0, low, high))
        base = jnp.int32(owner_rows)
        count = jnp.int32(0)
        for position in range(size):
            row = region[slab, position] - me * owner_rows
            mine = jnp.logical_and(row >= 0, row < owner_rows)
            base = jnp.minimum(base, jnp.where(mine, row, owner_rows))
            count = count + jnp.where(mine, 1, 0)
        base = jnp.where(count == 0, 0, base)
        after = jnp.minimum(base + 1, owner_rows - 1)
        lower = base == 0
        edge = jnp.where(jnp.logical_and(count == 2, jnp.logical_not(lower)), after, base)
        kept = out.shape[1]
        first = 0 if kept == rows else pl.multiple_of(core * kept, kept)
        here = pl.ds(first, kept)
        pairs = (
            (density.at[base, pl.ds(1, 2), here, :], out.at[pl.ds(0, 2)]),
            (density.at[after, pl.ds(0, 2), here, :], out.at[pl.ds(2, 2)]),
            (density.at[edge, jnp.where(lower, 0, 2), here, :], out.at[4]),
        )
        for part, (source, target) in enumerate(pairs):
            copies.append(pltpu.make_async_copy(source, target, sems.at[number, part]))
    for copy in copies:
        copy.start()
    for copy in copies:
        copy.wait()


def in_hbm(array):
    return pltpu.with_memory_space_constraint(array, pltpu.HBM)


def rows_to_send(region, density, slabs):
    size = density.shape[-1]
    exchanges = partners(slabs)
    kept = [size] + [size if low != high else size // 2 for low, high in exchanges]
    hbm = pl.BlockSpec(memory_space=pl.ANY)
    return pl.pallas_call(
        send_kernel,
        out_shape=[jax.ShapeDtypeStruct((TRAVEL, rows, size), density.dtype) for rows in kept],
        in_specs=[hbm, hbm],
        out_specs=[pl.BlockSpec(memory_space=pltpu.VMEM)] * len(kept),
        scratch_shapes=[
            pltpu.SMEM(region.shape, jnp.int32),
            pltpu.SemaphoreType.DMA((len(kept), 3)),
            pltpu.SemaphoreType.DMA,
        ],
        compiler_params=pltpu.CompilerParams(vmem_limit_bytes=VMEM_LIMIT),
    )(in_hbm(region), in_hbm(density))


def fetch_rows(region, density, slabs, atom_devices):
    own, *outgoing = rows_to_send(region, density, slabs)
    near = []
    for shifts, piece in zip(partners(slabs), outgoing):
        near.append(lax.ppermute(piece, ("grid", "atoms"), moves_over_grid(shifts, slabs, atom_devices)))
    return own, near


def stage_rows(stage, own, near, far, slabs):
    core = lax.rem(lax.axis_index("atoms"), 2)
    for place in range(TRAVEL):
        stage[place] = own[place]
    for (low, high), here, there in zip(partners(slabs), near, far):
        kept = here.shape[1]
        mine = jnp.where(core == 0, low, high) * TRAVEL
        other = jnp.where(core == 0, high, low) * TRAVEL
        for place in range(TRAVEL):
            if low != high:
                stage[mine + place] = here[place]
                stage[other + place] = there[place]
            else:
                stage[mine + place, pl.ds(pl.multiple_of(core * kept, kept), kept), :] = here[place]
                stage[mine + place, pl.ds(pl.multiple_of((1 - core) * kept, kept), kept), :] = there[place]


def block_major(x_ref, wide, points, blocks):
    wide[...] = x_ref[0].astype(F32)
    return [wide[pl.ds(s, points, stride=blocks), :] for s in range(blocks)]


def relayout_kernel(basis, field, basis_out, field_out, wide, *, points, blocks):
    size = basis.shape[-1]
    for source, target in ((basis, basis_out), (field, field_out)):
        for s, part in enumerate(block_major(source, wide, points, blocks)):
            target[0, :, s * size : (s + 1) * size] = part.astype(BF16)


def relayout(basis, field, points, blocks):
    batches, rows, size = basis.shape
    here = pl.BlockSpec((1, rows, size), lambda b: (b, 0, 0))
    there = pl.BlockSpec((1, points, blocks * size), lambda b: (b, 0, 0))
    shape = jax.ShapeDtypeStruct((batches, points, blocks * size), BF16)
    return pl.pallas_call(
        functools.partial(relayout_kernel, points=points, blocks=blocks),
        grid=(batches,),
        out_shape=(shape, shape),
        in_specs=[here, here],
        out_specs=(there, there),
        scratch_shapes=[pltpu.VMEM((rows, size), F32)],
        compiler_params=pltpu.CompilerParams(vmem_limit_bytes=VMEM_LIMIT),
        cost_estimate=pl.CostEstimate(flops=0, bytes_accessed=8 * batches * rows * size, transcendentals=0),
    )(basis, field)


def batch_matrix(region, pattern, tiles, slab, batch, blocks, width):
    half = (width - 1) // 2
    none = tiles.shape[0] - 1
    places = [pattern[batch, s] for s in range(blocks)]
    rows = [region[slab, place] for place in places]
    strips = []
    for s in range(blocks):
        strip = []
        for t in range(blocks):
            k = rows[t] - rows[s] + half
            inside = jnp.logical_and(k >= 0, k < width)
            strip.append(tiles[jnp.where(inside, places[s] * width + k, none)])
        strips.append(jnp.concatenate(strip, axis=1))
    return jnp.concatenate(strips, axis=0)


def split(values):
    high = values.astype(BF16)
    rest = values - high.astype(F32)
    middle = rest.astype(BF16)
    low = (rest - middle.astype(F32)).astype(BF16)
    return high, middle, low


def gradient_kernel(
    region,
    pattern,
    basis,
    field,
    basis_grad,
    weights,
    weight_grad,
    fn_atom,
    batch_atom,
    places,
    *rest,
    points,
    blocks,
    width,
    owner_rows,
    slabs,
):
    *pieces, tiles, out, stage, spread, sums, energy_sums = rest
    batch = pl.program_id(0)
    batches = pl.num_programs(0)
    me = lax.axis_index("grid")
    me_atoms = lax.axis_index("atoms")
    size = tiles.shape[-1]
    region_size = region.shape[1]

    @pl.when(batch == 0)
    def _():
        tiles[region_size * width] = jnp.zeros((size, size), BF16)
        stage_rows(stage, pieces[0], pieces[1 : 1 + slabs // 2], pieces[1 + slabs // 2 :], slabs)
        for position in range(region_size):
            owner, slot, count = owner_and_slot(region, me, position, owner_rows)
            shift = jnp.bitwise_xor(me, owner)
            for k in range(width):
                tiles[position * width + k] = stage[shift * TRAVEL + travel_place(slot, count, k)]

    matrix = batch_matrix(region, pattern, tiles, me, batch, blocks, width)
    potential = lax.dot_general(field[0], matrix, NT, preferred_element_type=F32)
    rows = jnp.concatenate(
        [weights[pl.ds(batch, 1), :]]
        + [weight_grad[c, pl.ds(batch, 1), :] for c in range(PARTS)]
        + [jnp.zeros((8 - 1 - PARTS, points), F32)],
        axis=0,
    )
    columns = rows.T
    weight = columns[:, 0:1]
    energy = jnp.zeros((points, size), F32)
    for s in range(blocks):
        here = potential[:, s * size : (s + 1) * size]
        energy = energy + basis[0, :, s * size : (s + 1) * size].astype(F32) * here
        spread[pl.ds(s, points, stride=blocks), :] = here * weight
    scaled = spread[...]
    place = pl.ds(pl.multiple_of(batch * 8, 8), 8)
    for c in range(PARTS):
        terms = basis_grad[c, 0].astype(F32) * scaled
        sums[c, place, :] = jnp.sum(terms.reshape(-1, 8, size), axis=0)
        terms = energy * columns[:, 1 + c : 2 + c]
        energy_sums[c, place, :] = jnp.sum(terms.reshape(-1, 8, size), axis=0)

    @pl.when(batch == batches - 1)
    def _():
        padded = max(8, region_size)
        chosen = lax.broadcasted_iota(jnp.int32, (padded, places.shape[1]), 0) == places[...]
        chosen = chosen.astype(BF16)
        blocks_sum = []
        for c in range(PARTS):
            total = jnp.zeros((padded, size), F32)
            for piece in split(sums[c]):
                total = total + jnp.dot(chosen, piece, preferred_element_type=F32)
            blocks_sum.append(-2.0 * total)
        lefts = []
        for position in range(region_size):
            stack = jnp.concatenate([total[position : position + 1] for total in blocks_sum], axis=0)
            high, middle, low = (piece.astype(F32) for piece in split(stack))
            lefts.append(jnp.concatenate([high, middle, low, jnp.zeros((16 - 3 * PARTS, size), F32)], axis=0))
        left = jnp.concatenate(lefts, axis=1).astype(BF16)
        chunk = out.shape[-1]
        scale = [jnp.sum(energy_sums[c], axis=1, keepdims=True) for c in range(PARTS)]
        for device in range(out.shape[0]):
            atoms = lax.broadcasted_iota(jnp.int32, (chunk, size), 0) + device * chunk
            hot = [
                jnp.where(atoms == fn_atom[pl.ds(region[me, position], 1), :], 1.0, 0.0).astype(BF16)
                for position in range(region_size)
            ]
            found = lax.dot_general(left, jnp.concatenate(hot, axis=1), NT, preferred_element_type=F32)
            atoms = lax.broadcasted_iota(jnp.int32, (batch_atom.shape[0], chunk), 1) + device * chunk
            mine = atoms == batch_atom[...]
            for c in range(PARTS):
                value = found[c : c + 1] + found[PARTS + c : PARTS + c + 1] + found[2 * PARTS + c : 2 * PARTS + c + 1]
                value = value + jnp.sum(jnp.where(mine, scale[c], 0.0), axis=0, keepdims=True)
                place = jnp.bitwise_xor(me_atoms, device)
                out[place, 0, c : c + 1, :] = value
                out[jnp.bitwise_xor(place, 1), 1, c : c + 1, :] = value


def partial_gradient(
    region, pattern, basis, field, basis_grad, weights, weight_grad, fn_atom, batch_atom, pieces, shapes
):
    slabs, atom_devices, atom_total, points, blocks, width, owner_rows = shapes
    batches, _, columns = basis.shape
    size = columns // blocks
    region_size = region.shape[1]
    fn_atom = fn_atom.reshape(-1, size)
    places = jnp.broadcast_to(pattern[:, None, :], (batches, 8 // blocks, blocks)).reshape(1, -1)
    batch_atom = jnp.broadcast_to(batch_atom[:, None], (batches, 8)).reshape(-1, 1)
    block = pl.BlockSpec((1, points, columns), lambda b, *_: (b, 0, 0))
    whole = pl.BlockSpec(memory_space=pltpu.VMEM)
    tile_shape = (region_size * width + 1, size, size)
    out_shape = (atom_devices, 2, PARTS, atom_total // atom_devices)
    return pl.pallas_call(
        functools.partial(
            gradient_kernel, points=points, blocks=blocks, width=width, owner_rows=owner_rows, slabs=slabs
        ),
        grid_spec=pltpu.PrefetchScalarGridSpec(
            num_scalar_prefetch=2,
            grid=(batches,),
            in_specs=[
                block,
                block,
                pl.BlockSpec((PARTS, 1, points * blocks, size), lambda b, *_: (0, b, 0, 0)),
            ]
            + [whole] * (5 + len(pieces)),
            out_specs=(whole, whole),
            scratch_shapes=[
                pltpu.VMEM((slabs * TRAVEL, size, size), BF16),
                pltpu.VMEM((points * blocks, size), F32),
                pltpu.VMEM((PARTS, batches * 8, size), F32),
                pltpu.VMEM((PARTS, batches * 8, size), F32),
            ],
        ),
        out_shape=(jax.ShapeDtypeStruct(tile_shape, BF16), jax.ShapeDtypeStruct(out_shape, F32)),
        compiler_params=pltpu.CompilerParams(vmem_limit_bytes=VMEM_LIMIT),
    )(region, pattern, basis, field, basis_grad, weights, weight_grad, fn_atom, batch_atom, places, *pieces)


def product_kernel(region, pattern, basis, tiles, out, spread, *, points, blocks, width):
    me = lax.axis_index("grid")
    size = tiles.shape[-1]
    matrix = batch_matrix(region, pattern, tiles, me, pl.program_id(0), blocks, width)
    product = jnp.dot(basis[0], matrix, preferred_element_type=F32)
    for t in range(blocks):
        spread[pl.ds(t, points, stride=blocks), :] = product[:, t * size : (t + 1) * size]
    out[0] = spread[...].astype(BF16)


def contract(region, pattern, basis, tiles, points, blocks, width):
    batches, _, columns = basis.shape
    size = columns // blocks
    return pl.pallas_call(
        functools.partial(product_kernel, points=points, blocks=blocks, width=width),
        grid_spec=pltpu.PrefetchScalarGridSpec(
            num_scalar_prefetch=2,
            grid=(batches,),
            in_specs=[
                pl.BlockSpec((1, points, columns), lambda b, *_: (b, 0, 0)),
                pl.BlockSpec(memory_space=pltpu.VMEM),
            ],
            out_specs=pl.BlockSpec((1, points * blocks, size), lambda b, *_: (b, 0, 0)),
            scratch_shapes=[pltpu.VMEM((points * blocks, size), F32)],
        ),
        out_shape=jax.ShapeDtypeStruct((batches, points * blocks, size), BF16),
        compiler_params=pltpu.CompilerParams(vmem_limit_bytes=VMEM_LIMIT),
        cost_estimate=pl.CostEstimate(
            flops=2 * batches * points * columns * columns,
            bytes_accessed=4 * batches * points * columns,
            transcendentals=0,
        ),
    )(region, pattern, basis, tiles)


def reorder_kernel(
    pattern_hbm,
    basis,
    field,
    basis_grad,
    weights_hbm,
    basis_out,
    field_out,
    weighted,
    grads,
    pattern,
    weights,
    columns,
    basis_in,
    field_in,
    grad_in,
    wide,
    sems,
    small_sems,
):
    batches, blocks, points, size = basis_out.shape

    def copies(batch):
        return (
            pltpu.make_async_copy(field.at[batch], field_in.at[batch], sems.at[batch, 0]),
            pltpu.make_async_copy(basis.at[batch], basis_in.at[batch], sems.at[batch, 1]),
            pltpu.make_async_copy(basis_grad.at[:, batch], grad_in.at[:, batch], sems.at[batch, 2]),
        )

    small = (
        pltpu.make_async_copy(pattern_hbm, pattern, small_sems.at[0]),
        pltpu.make_async_copy(weights_hbm, weights, small_sems.at[1]),
    )
    for copy in small:
        copy.start()

    @pl.loop(0, batches)
    def _(batch):
        for copy in copies(batch):
            copy.start()

    for copy in small:
        copy.wait()
    rows = jnp.concatenate([weights[...], jnp.zeros((size - batches, points), F32)], axis=0).T
    for batch in range(batches):
        columns[batch] = jnp.broadcast_to(rows[:, batch : batch + 1], (points, size))

    @pl.loop(0, batches)
    def _(batch):
        for copy in copies(batch):
            copy.wait()
        points_here = pl.ds(pl.multiple_of(batch * points, points), points)
        places = [pattern[s, batch] for s in range(blocks)]
        wide[0] = field_in[batch].astype(F32)
        wide[1] = basis_in[batch].astype(F32)
        for c in range(PARTS):
            wide[2 + c] = grad_in[c, batch].astype(F32)
        for s, place in enumerate(places):
            strided = pl.ds(s, points, stride=blocks)
            values = wide[0, strided, :]
            field_out[batch, place] = values.astype(BF16)
            weighted[place, points_here, :] = (values * columns[batch]).astype(BF16)
            basis_out[batch, place] = wide[1, strided, :].astype(BF16)
            for c in range(PARTS):
                grads[c, place, points_here, :] = wide[2 + c, strided, :].astype(BF16)


def reorder(pattern, basis, field, basis_grad, weights, points, blocks):
    batches, rows, size = basis.shape
    hbm = pl.BlockSpec(memory_space=pl.ANY)
    vmem = pl.BlockSpec(memory_space=pltpu.VMEM)
    ordered = jax.ShapeDtypeStruct((batches, blocks, points, size), BF16)
    return pl.pallas_call(
        reorder_kernel,
        out_shape=(
            ordered,
            ordered,
            jax.ShapeDtypeStruct((blocks, batches * points, size), BF16),
            jax.ShapeDtypeStruct((PARTS, blocks, batches * points, size), BF16),
        ),
        in_specs=[hbm] * 5,
        out_specs=(vmem,) * 4,
        scratch_shapes=[
            pltpu.SMEM((blocks, batches), jnp.int32),
            pltpu.VMEM(weights.shape, F32),
            pltpu.VMEM((batches, points, size), F32),
            pltpu.VMEM((batches, rows, size), BF16),
            pltpu.VMEM((batches, rows, size), BF16),
            pltpu.VMEM((PARTS, batches, rows, size), BF16),
            pltpu.VMEM((2 + PARTS, rows, size), F32),
            pltpu.SemaphoreType.DMA((batches, 3)),
            pltpu.SemaphoreType.DMA((2,)),
        ],
        compiler_params=pltpu.CompilerParams(vmem_limit_bytes=VMEM_LIMIT),
        cost_estimate=pl.CostEstimate(
            flops=0, bytes_accessed=2 * (2 + PARTS) * batches * rows * size, transcendentals=0
        ),
    )(in_hbm(pattern.T), in_hbm(basis), in_hbm(field), in_hbm(basis_grad), in_hbm(weights))


def moment_kernel(weighted, grads, moments):
    blocks, _, size = grads.shape[1:]
    for p in range(0, blocks, 2):
        first, last = max(p - 1, 0), min(p + 3, blocks)
        left = jnp.concatenate([weighted[place] for place in range(first, last)], axis=1)
        for c in range(PARTS):
            right = jnp.concatenate([grads[c, p], grads[c, p + 1]], axis=1)
            moments[c, first * size : last * size, p * size : (p + 2) * size] = lax.dot_general(
                left, right, TN, preferred_element_type=F32
            )


def build_moments(weighted, grads):
    blocks, depth, size = grads.shape[1:]
    vmem = pl.BlockSpec(memory_space=pltpu.VMEM)
    return pl.pallas_call(
        moment_kernel,
        out_shape=jax.ShapeDtypeStruct((PARTS, blocks * size, blocks * size), F32),
        in_specs=[vmem, vmem],
        out_specs=vmem,
        compiler_params=pltpu.CompilerParams(vmem_limit_bytes=VMEM_LIMIT),
        cost_estimate=pl.CostEstimate(
            flops=2 * PARTS * depth * (blocks * size) ** 2, bytes_accessed=0, transcendentals=0
        ),
    )(weighted, grads)


def atom_kernel(region, fn_atom, batch_atom, weight_grad, hot, grad_columns):
    batches, points = weight_grad.shape[1:]
    size = fn_atom.shape[1]
    blocks = region.shape[1]
    me = lax.axis_index("grid")
    atoms = lax.broadcasted_iota(jnp.int32, (hot.shape[0], size), 0)
    ids = jnp.concatenate([batch_atom[...], jnp.full((1, size - batches), -1, jnp.int32)], axis=1)
    hot[:, blocks * size :] = jnp.where(atoms == ids, 1.0, 0.0).astype(BF16)

    @pl.loop(0, blocks)
    def _(position):
        ids = fn_atom[pl.ds(region[me, position], 1), :]
        columns = pl.ds(pl.multiple_of(position * size, size), size)
        hot[:, columns] = jnp.where(atoms == ids, 1.0, 0.0).astype(BF16)

    for c in range(PARTS):
        padding = jnp.zeros((size - batches, points), F32)
        grad_columns[c] = jnp.concatenate([weight_grad[c], padding], axis=0).T


def atom_matrix(region, fn_atom, batch_atom, weight_grad, blocks, size, atom_total):
    vmem = pl.BlockSpec(memory_space=pltpu.VMEM)
    return pl.pallas_call(
        atom_kernel,
        out_shape=(
            jax.ShapeDtypeStruct((atom_total, (blocks + 1) * size), BF16),
            jax.ShapeDtypeStruct((PARTS, weight_grad.shape[2], size), F32),
        ),
        in_specs=[pl.BlockSpec(memory_space=pltpu.SMEM)] + [vmem] * 3,
        out_specs=(vmem, vmem),
        compiler_params=pltpu.CompilerParams(vmem_limit_bytes=VMEM_LIMIT),
        cost_estimate=pl.CostEstimate(flops=1000000000, bytes_accessed=2 * atom_total * size, transcendentals=0),
    )(region, fn_atom.reshape(-1, size), batch_atom.reshape(1, -1), weight_grad)


def combine_kernel(
    region, basis, field, moments, hot, grad_columns, *rest, owner_rows, slabs, width, step
):
    *pieces, product_out, out, stage, matrix, energies = rest
    batches, blocks, points, size = basis.shape
    me = lax.axis_index("grid")
    me_atoms = lax.axis_index("atoms")
    half = (width - 1) // 2
    stage_rows(stage, pieces[0], pieces[1 : 1 + slabs // 2], pieces[1 + slabs // 2 :], slabs)
    rows = [region[me, position] for position in range(blocks)]
    found = [owner_and_slot(region, me, position, owner_rows) for position in range(blocks)]
    totals = [[jnp.zeros((8, size), F32) for _ in range(blocks)] for _ in range(PARTS)]
    for p in range(blocks):
        owner, slot, count = found[p]
        first = jnp.bitwise_xor(me, owner) * TRAVEL
        for q in range(blocks):
            if abs(q - p) > half:
                matrix[p * size : (p + 1) * size, q * size : (q + 1) * size] = jnp.zeros((size, size), BF16)
                continue
            k = rows[q] - rows[p] + half
            place = jnp.where(
                k == 0,
                travel_place(slot, count, 0),
                jnp.where(k == 1, travel_place(slot, count, 1), travel_place(slot, count, 2)),
            )
            inside = jnp.logical_and(k >= 0, k < width)
            tile = jnp.where(inside, stage[first + place], jnp.zeros((size, size), BF16))
            matrix[p * size : (p + 1) * size, q * size : (q + 1) * size] = tile
            turned = tile.T.astype(F32)
            for c in range(PARTS):
                terms = turned * moments[c, q * size : (q + 1) * size, p * size : (p + 1) * size]
                totals[c][p] = totals[c][p] + jnp.sum(terms.reshape(-1, 8, size), axis=0)
    derivative = [
        jnp.concatenate([jnp.sum(total, axis=0, keepdims=True) for total in totals[c]], axis=1) for c in range(PARTS)
    ]

    energies[...] = jnp.zeros_like(energies)
    lanes = lax.broadcasted_iota(jnp.int32, (points, size), 1)

    @pl.loop(0, batches // step)
    def _(group):
        left = [
            jnp.concatenate([basis[group * step + inner, p] for p in range(blocks)], axis=1) for inner in range(step)
        ]
        left = jnp.concatenate(left, axis=0)
        energy = [jnp.zeros((points, size), F32) for _ in range(step)]
        for q in range(0, blocks, 2):
            product = jnp.dot(left, matrix[:, q * size : (q + 2) * size], preferred_element_type=F32)
            for inner in range(step):
                batch = group * step + inner
                for column in range(2):
                    part = product[inner * points : (inner + 1) * points, column * size : (column + 1) * size]
                    product_out[batch, q + column] = part.astype(BF16)
                    energy[inner] = energy[inner] + part * field[batch, q + column].astype(F32)
        for inner in range(step):
            total = jnp.sum(energy[inner], axis=1, keepdims=True)
            energies[...] = jnp.where(lanes == group * step + inner, total, energies[...])

    lefts = []
    for c in range(PARTS):
        term = jnp.sum(energies[...] * grad_columns[c], axis=0, keepdims=True)
        lefts.append(jnp.concatenate([-2.0 * derivative[c], term], axis=1))
    left = jnp.concatenate(lefts, axis=0)
    high, middle, low = (piece.astype(F32) for piece in split(left))
    left = jnp.concatenate([high, middle, low, jnp.zeros((16 - 3 * PARTS, left.shape[1]), F32)], axis=0).astype(BF16)
    chunk = out.shape[-1]
    for device in range(out.shape[0]):
        sums = lax.dot_general(
            left, hot[device * chunk : (device + 1) * chunk, :], NT, preferred_element_type=F32
        )
        value = sums[:PARTS] + sums[PARTS : 2 * PARTS] + sums[2 * PARTS : 3 * PARTS]
        place = jnp.bitwise_xor(me_atoms, device)
        out[place, 0] = value
        out[jnp.bitwise_xor(place, 1), 1] = value


def combine(region, prepared, pieces, shapes):
    basis, field, moments, hot, grad_columns = prepared
    slabs, atom_devices, atom_total, points, blocks, width, owner_rows = shapes
    batches, _, _, size = basis.shape
    step = 16 if batches % 16 == 0 else 1
    vmem = pl.BlockSpec(memory_space=pltpu.VMEM)
    return pl.pallas_call(
        functools.partial(combine_kernel, owner_rows=owner_rows, slabs=slabs, width=width, step=step),
        out_shape=(
            jax.ShapeDtypeStruct(basis.shape, BF16),
            jax.ShapeDtypeStruct((atom_devices, 2, PARTS, atom_total // atom_devices), F32),
        ),
        in_specs=[pl.BlockSpec(memory_space=pltpu.SMEM)] + [vmem] * (5 + len(pieces)),
        out_specs=(vmem, vmem),
        scratch_shapes=[
            pltpu.VMEM((slabs * TRAVEL, size, size), BF16),
            pltpu.VMEM((blocks * size, blocks * size), BF16),
            pltpu.VMEM((points, size), F32),
        ],
        compiler_params=pltpu.CompilerParams(vmem_limit_bytes=VMEM_LIMIT),
    )(region, basis, field, moments, hot, grad_columns, *pieces)


def write_kernel(pattern, product, out, wide, staged, sems):
    batches, blocks, points, size = product.shape

    def copy(batch):
        return pltpu.make_async_copy(staged.at[batch], out.at[batch], sems.at[batch])

    @pl.loop(0, batches // 2)
    def _(pair):
        for inner in range(2):
            batch = pair * 2 + inner
            for t in range(blocks):
                wide[inner, pl.ds(t, points, stride=blocks), :] = product[batch, pattern[t, batch]].astype(F32)
            staged[batch] = wide[inner].astype(BF16)
            copy(batch).start()

    @pl.loop(0, batches)
    def _(batch):
        copy(batch).wait()


def write(pattern, product):
    batches, blocks, points, size = product.shape
    shape = (batches, points * blocks, size)
    return pl.pallas_call(
        write_kernel,
        out_shape=jax.ShapeDtypeStruct(shape, BF16),
        in_specs=[pl.BlockSpec(memory_space=pltpu.SMEM), pl.BlockSpec(memory_space=pltpu.VMEM)],
        out_specs=pl.BlockSpec(memory_space=pl.ANY),
        scratch_shapes=[
            pltpu.VMEM((2, points * blocks, size), F32),
            pltpu.VMEM(shape, BF16),
            pltpu.SemaphoreType.DMA((batches,)),
        ],
        compiler_params=pltpu.CompilerParams(vmem_limit_bytes=VMEM_LIMIT),
        cost_estimate=pl.CostEstimate(flops=0, bytes_accessed=4 * math.prod(shape), transcendentals=0),
    )(pattern.T, product)


def swap_halves(near, ready, atom_devices):
    near, ready = lax.optimization_barrier((near, ready))
    swap = [(i, i ^ 1) for i in range(atom_devices)]
    return near, [lax.ppermute(piece, "atoms", swap) for piece in near], ready


def tree_sum(values):
    if len(values) == 1:
        return values[0]
    half = len(values) // 2
    return tree_sum(values[:half]) + tree_sum(values[half:])


def pair_sums(values):
    return [values[i] + values[i + 1] for i in range(0, len(values), 2)]


def sum_parts(partial_grad, contracted, slabs, atom_devices):
    parts = [partial_grad[0]]
    for d in range(1, atom_devices):
        parts.append(lax.ppermute(partial_grad[d], "atoms", [(i, i ^ d) for i in range(atom_devices)]))
    parts, contracted = lax.optimization_barrier((parts, contracted))
    both = tree_sum(pair_sums(parts))
    swap = [(i, i ^ 1) for i in range(atom_devices)]
    far = []
    for shifts in partners(slabs):
        if shifts[0] != shifts[1]:
            far.append(lax.ppermute(both, ("grid", "atoms"), moves_over_grid(shifts, slabs, atom_devices)))
    near = lax.ppermute(both[0], "grid", [(i, i ^ 1) for i in range(slabs)])
    far = lax.optimization_barrier(far)
    swapped = [lax.ppermute(piece[1], "atoms", swap) for piece in far]
    sums = [both[0] + near] + [piece[0] + other for piece, other in zip(far, swapped)]
    return tree_sum(sums), contracted


def local(
    basis,
    basis_grad,
    exchange_field,
    weights,
    weight_grad,
    density,
    region,
    pattern,
    fn_atom,
    batch_atom,
):
    batches, points, blocks, size = basis.shape
    owner_rows, width = density.shape[:2]
    slabs = lax.axis_size("grid")
    atom_devices = lax.axis_size("atoms")
    atom_total = fn_atom.shape[0] // (10 * slabs * atom_devices) * slabs * atom_devices
    shapes = (slabs, atom_devices, atom_total, points, blocks, width, owner_rows)
    flat_basis = basis.reshape(batches, points * blocks, size)
    flat_field = exchange_field.reshape(batches, points * blocks, size)
    flat_grad = basis_grad.reshape(PARTS, batches, points * blocks, size)
    own, near = fetch_rows(region, density, slabs, atom_devices)
    if region.shape[1] == blocks:
        basis_wide, field_wide, weighted, grads = reorder(
            pattern, flat_basis, flat_field, flat_grad, weights, points, blocks
        )
        ready = (basis_wide, field_wide, build_moments(weighted, grads), batch_atom)
        near, far, (basis_wide, field_wide, moments, batch_atom) = swap_halves(near, ready, atom_devices)
        hot, grad_columns = atom_matrix(region, fn_atom, batch_atom, weight_grad, blocks, size, atom_total)
        ready = (basis_wide, field_wide, moments, hot, grad_columns)
        product, partial_grad = combine(region, ready, [own, *near, *far], shapes)
        gradient, contracted = sum_parts(partial_grad, write(pattern, product), slabs, atom_devices)
        return contracted.reshape(basis.shape), gradient
    ready = relayout(in_hbm(flat_basis), in_hbm(flat_field), points, blocks)
    near, far, (basis_wide, field_wide) = swap_halves(near, ready, atom_devices)
    tiles, partial_grad = partial_gradient(
        region,
        pattern,
        basis_wide,
        field_wide,
        in_hbm(flat_grad),
        weights,
        weight_grad,
        fn_atom,
        batch_atom,
        [own, *near, *far],
        shapes,
    )
    contracted = contract(region, pattern, basis_wide, tiles, points, blocks, width)
    gradient, contracted = sum_parts(partial_grad, contracted, slabs, atom_devices)
    return contracted.reshape(basis.shape), gradient


def solution(mesh):
    placed = (
        P(("groups", "grid", "atoms"), None, None, None),
        P(None, ("groups", "grid", "atoms"), None, None, None),
        P(("groups", "grid", "atoms"), None, None, None),
        P(("groups", "grid", "atoms"), None),
        P(None, ("groups", "grid", "atoms"), None),
        P(("groups", "grid"), None, None, None),
        P("groups", None),
        P(("groups", "grid", "atoms"), None),
        P("groups"),
        P(("groups", "grid", "atoms")),
    )
    return jax.shard_map(
        local,
        mesh=mesh,
        in_specs=placed,
        out_specs=(P(("groups", "grid", "atoms"), None, None, None), P(None, ("groups", "atoms"))),
        check_vma=False,
    )
```

```python
import functools
import math

import jax
import jax.numpy as jnp
from jax import lax
from jax.experimental import pallas as pl
from jax.experimental.pallas import tpu as pltpu
from jax.sharding import PartitionSpec as P

TRAVEL = 5
PARTS = 3
F32 = jnp.float32
BF16 = jnp.bfloat16
NT = (((1,), (1,)), ((), ()))
TN = (((0,), (0,)), ((), ()))
VMEM_LIMIT = 32 * 1024 * 1024


def owner_and_slot(region, slab, position, owner_rows):
    owner = lax.div(region[slab, position], owner_rows)
    slot = jnp.int32(0)
    count = jnp.int32(0)
    for other in range(region.shape[1]):
        same = jnp.where(lax.div(region[slab, other], owner_rows) == owner, 1, 0)
        count = count + same
        slot = slot + jnp.where(other < position, same, 0)
    return owner, slot, count


def travel_place(slot, count, k):
    if k == 0:
        return jnp.where(slot == 0, 4, 2)
    if k == 1:
        return jnp.where(slot == 0, 0, 3)
    return jnp.where(jnp.logical_and(slot == 0, count == 2), 1, 4)


def partners(slabs):
    return [(1, 1)] + [(shift + 1, shift) for shift in range(2, slabs, 2)]


def moves_over_grid(shifts, slabs, atom_devices):
    return [
        (z * atom_devices + a, (z ^ shifts[a % 2]) * atom_devices + a) for z in range(slabs) for a in range(atom_devices)
    ]


def send_kernel(region_hbm, density, *rest):
    *outs, region, held, region_sem, sems = rest
    fetch = pltpu.make_async_copy(region_hbm, region, region_sem)
    fetch.start()
    count_here = density.shape[0] // sems.shape[0]
    fetches = []
    for part in range(sems.shape[0]):
        here = pl.ds(part * count_here, count_here)
        fetches.append(pltpu.make_async_copy(density.at[here], held.at[here], sems.at[part]))
    for copy in fetches:
        copy.start()
    fetch.wait()
    me = lax.axis_index("grid")
    core = lax.rem(lax.axis_index("atoms"), 2)
    slabs, size = region.shape
    owner_rows = density.shape[0]
    rows = density.shape[-2]
    picks = []
    for low, high in [(0, 0)] + partners(slabs):
        slab = jnp.bitwise_xor(me, jnp.where(core == 0, low, high))
        base = jnp.int32(owner_rows)
        count = jnp.int32(0)
        for position in range(size):
            row = region[slab, position] - me * owner_rows
            mine = jnp.logical_and(row >= 0, row < owner_rows)
            base = jnp.minimum(base, jnp.where(mine, row, owner_rows))
            count = count + jnp.where(mine, 1, 0)
        base = jnp.where(count == 0, 0, base)
        after = jnp.minimum(base + 1, owner_rows - 1)
        lower = base == 0
        edge = jnp.where(jnp.logical_and(count == 2, jnp.logical_not(lower)), after, base)
        picks.append(((base, 1), (base, 2), (after, 0), (after, 1), (edge, jnp.where(lower, 0, 2))))
    for copy in fetches:
        copy.wait()
    for out, places in zip(outs, picks):
        kept = out.shape[1]
        for place, (row, k) in enumerate(places):
            if kept == rows:
                out[place] = held[row, k]
            else:
                out[place] = held[row, k, pl.ds(pl.multiple_of(core * kept, kept), kept), :]


def in_hbm(array):
    return pltpu.with_memory_space_constraint(array, pltpu.HBM)


def rows_to_send(region, density, slabs):
    size = density.shape[-1]
    exchanges = partners(slabs)
    kept = [size] + [size if low != high else size // 2 for low, high in exchanges]
    hbm = pl.BlockSpec(memory_space=pl.ANY)
    return pl.pallas_call(
        send_kernel,
        out_shape=[jax.ShapeDtypeStruct((TRAVEL, rows, size), density.dtype) for rows in kept],
        in_specs=[hbm, hbm],
        out_specs=[pl.BlockSpec(memory_space=pltpu.VMEM)] * len(kept),
        scratch_shapes=[
            pltpu.SMEM(region.shape, jnp.int32),
            pltpu.VMEM(density.shape, density.dtype),
            pltpu.SemaphoreType.DMA,
            pltpu.SemaphoreType.DMA((5 if density.shape[0] % 5 == 0 else 1,)),
        ],
        compiler_params=pltpu.CompilerParams(vmem_limit_bytes=VMEM_LIMIT),
    )(in_hbm(region), in_hbm(density))


def fetch_rows(region, density, slabs, atom_devices):
    own, *outgoing = rows_to_send(region, density, slabs)
    near = []
    for shifts, piece in zip(partners(slabs), outgoing):
        near.append(lax.ppermute(piece, ("grid", "atoms"), moves_over_grid(shifts, slabs, atom_devices)))
    return own, near


def stage_rows(stage, own, near, far, slabs):
    core = lax.rem(lax.axis_index("atoms"), 2)
    for place in range(TRAVEL):
        stage[place] = own[place]
    for (low, high), here, there in zip(partners(slabs), near, far):
        kept = here.shape[1]
        mine = jnp.where(core == 0, low, high) * TRAVEL
        other = jnp.where(core == 0, high, low) * TRAVEL
        for place in range(TRAVEL):
            if low != high:
                stage[mine + place] = here[place]
                stage[other + place] = there[place]
            else:
                stage[mine + place, pl.ds(pl.multiple_of(core * kept, kept), kept), :] = here[place]
                stage[mine + place, pl.ds(pl.multiple_of((1 - core) * kept, kept), kept), :] = there[place]


def block_major(x_ref, wide, points, blocks):
    wide[...] = x_ref[0].astype(F32)
    return [wide[pl.ds(s, points, stride=blocks), :] for s in range(blocks)]


def relayout_kernel(basis, field, basis_out, field_out, wide, *, points, blocks):
    size = basis.shape[-1]
    for source, target in ((basis, basis_out), (field, field_out)):
        for s, part in enumerate(block_major(source, wide, points, blocks)):
            target[0, :, s * size : (s + 1) * size] = part.astype(BF16)


def relayout(basis, field, points, blocks):
    batches, rows, size = basis.shape
    here = pl.BlockSpec((1, rows, size), lambda b: (b, 0, 0))
    there = pl.BlockSpec((1, points, blocks * size), lambda b: (b, 0, 0))
    shape = jax.ShapeDtypeStruct((batches, points, blocks * size), BF16)
    return pl.pallas_call(
        functools.partial(relayout_kernel, points=points, blocks=blocks),
        grid=(batches,),
        out_shape=(shape, shape),
        in_specs=[here, here],
        out_specs=(there, there),
        scratch_shapes=[pltpu.VMEM((rows, size), F32)],
        compiler_params=pltpu.CompilerParams(vmem_limit_bytes=VMEM_LIMIT),
        cost_estimate=pl.CostEstimate(flops=0, bytes_accessed=8 * batches * rows * size, transcendentals=0),
    )(basis, field)


def batch_matrix(region, pattern, tiles, slab, batch, blocks, width):
    half = (width - 1) // 2
    none = tiles.shape[0] - 1
    places = [pattern[batch, s] for s in range(blocks)]
    rows = [region[slab, place] for place in places]
    strips = []
    for s in range(blocks):
        strip = []
        for t in range(blocks):
            k = rows[t] - rows[s] + half
            inside = jnp.logical_and(k >= 0, k < width)
            strip.append(tiles[jnp.where(inside, places[s] * width + k, none)])
        strips.append(jnp.concatenate(strip, axis=1))
    return jnp.concatenate(strips, axis=0)


def split(values):
    high = values.astype(BF16)
    rest = values - high.astype(F32)
    middle = rest.astype(BF16)
    low = (rest - middle.astype(F32)).astype(BF16)
    return high, middle, low


def gradient_kernel(
    region,
    pattern,
    basis,
    field,
    basis_grad,
    weights,
    weight_grad,
    fn_atom,
    batch_atom,
    places,
    *rest,
    points,
    blocks,
    width,
    owner_rows,
    slabs,
):
    *pieces, tiles, out, stage, spread, sums, energy_sums = rest
    batch = pl.program_id(0)
    batches = pl.num_programs(0)
    me = lax.axis_index("grid")
    me_atoms = lax.axis_index("atoms")
    size = tiles.shape[-1]
    region_size = region.shape[1]

    @pl.when(batch == 0)
    def _():
        tiles[region_size * width] = jnp.zeros((size, size), BF16)
        stage_rows(stage, pieces[0], pieces[1 : 1 + slabs // 2], pieces[1 + slabs // 2 :], slabs)
        for position in range(region_size):
            owner, slot, count = owner_and_slot(region, me, position, owner_rows)
            shift = jnp.bitwise_xor(me, owner)
            for k in range(width):
                tiles[position * width + k] = stage[shift * TRAVEL + travel_place(slot, count, k)]

    matrix = batch_matrix(region, pattern, tiles, me, batch, blocks, width)
    potential = lax.dot_general(field[0], matrix, NT, preferred_element_type=F32)
    rows = jnp.concatenate(
        [weights[pl.ds(batch, 1), :]]
        + [weight_grad[c, pl.ds(batch, 1), :] for c in range(PARTS)]
        + [jnp.zeros((8 - 1 - PARTS, points), F32)],
        axis=0,
    )
    columns = rows.T
    weight = columns[:, 0:1]
    energy = jnp.zeros((points, size), F32)
    for s in range(blocks):
        here = potential[:, s * size : (s + 1) * size]
        energy = energy + basis[0, :, s * size : (s + 1) * size].astype(F32) * here
        spread[pl.ds(s, points, stride=blocks), :] = here * weight
    scaled = spread[...]
    place = pl.ds(pl.multiple_of(batch * 8, 8), 8)
    for c in range(PARTS):
        terms = basis_grad[c, 0].astype(F32) * scaled
        sums[c, place, :] = jnp.sum(terms.reshape(-1, 8, size), axis=0)
        terms = energy * columns[:, 1 + c : 2 + c]
        energy_sums[c, place, :] = jnp.sum(terms.reshape(-1, 8, size), axis=0)

    @pl.when(batch == batches - 1)
    def _():
        padded = max(8, region_size)
        chosen = lax.broadcasted_iota(jnp.int32, (padded, places.shape[1]), 0) == places[...]
        chosen = chosen.astype(BF16)
        blocks_sum = []
        for c in range(PARTS):
            total = jnp.zeros((padded, size), F32)
            for piece in split(sums[c]):
                total = total + jnp.dot(chosen, piece, preferred_element_type=F32)
            blocks_sum.append(-2.0 * total)
        lefts = []
        for position in range(region_size):
            stack = jnp.concatenate([total[position : position + 1] for total in blocks_sum], axis=0)
            high, middle, low = (piece.astype(F32) for piece in split(stack))
            lefts.append(jnp.concatenate([high, middle, low, jnp.zeros((16 - 3 * PARTS, size), F32)], axis=0))
        left = jnp.concatenate(lefts, axis=1).astype(BF16)
        chunk = out.shape[-1]
        scale = [jnp.sum(energy_sums[c], axis=1, keepdims=True) for c in range(PARTS)]
        for device in range(out.shape[0]):
            atoms = lax.broadcasted_iota(jnp.int32, (chunk, size), 0) + device * chunk
            hot = [
                jnp.where(atoms == fn_atom[pl.ds(region[me, position], 1), :], 1.0, 0.0).astype(BF16)
                for position in range(region_size)
            ]
            found = lax.dot_general(left, jnp.concatenate(hot, axis=1), NT, preferred_element_type=F32)
            atoms = lax.broadcasted_iota(jnp.int32, (batch_atom.shape[0], chunk), 1) + device * chunk
            mine = atoms == batch_atom[...]
            for c in range(PARTS):
                value = found[c : c + 1] + found[PARTS + c : PARTS + c + 1] + found[2 * PARTS + c : 2 * PARTS + c + 1]
                value = value + jnp.sum(jnp.where(mine, scale[c], 0.0), axis=0, keepdims=True)
                place = jnp.bitwise_xor(me_atoms, device)
                out[place, 0, c : c + 1, :] = value
                out[jnp.bitwise_xor(place, 1), 1, c : c + 1, :] = value


def partial_gradient(
    region, pattern, basis, field, basis_grad, weights, weight_grad, fn_atom, batch_atom, pieces, shapes
):
    slabs, atom_devices, atom_total, points, blocks, width, owner_rows = shapes
    batches, _, columns = basis.shape
    size = columns // blocks
    region_size = region.shape[1]
    fn_atom = fn_atom.reshape(-1, size)
    places = jnp.broadcast_to(pattern[:, None, :], (batches, 8 // blocks, blocks)).reshape(1, -1)
    batch_atom = jnp.broadcast_to(batch_atom[:, None], (batches, 8)).reshape(-1, 1)
    block = pl.BlockSpec((1, points, columns), lambda b, *_: (b, 0, 0))
    whole = pl.BlockSpec(memory_space=pltpu.VMEM)
    tile_shape = (region_size * width + 1, size, size)
    out_shape = (atom_devices, 2, PARTS, atom_total // atom_devices)
    return pl.pallas_call(
        functools.partial(
            gradient_kernel, points=points, blocks=blocks, width=width, owner_rows=owner_rows, slabs=slabs
        ),
        grid_spec=pltpu.PrefetchScalarGridSpec(
            num_scalar_prefetch=2,
            grid=(batches,),
            in_specs=[
                block,
                block,
                pl.BlockSpec((PARTS, 1, points * blocks, size), lambda b, *_: (0, b, 0, 0)),
            ]
            + [whole] * (5 + len(pieces)),
            out_specs=(whole, whole),
            scratch_shapes=[
                pltpu.VMEM((slabs * TRAVEL, size, size), BF16),
                pltpu.VMEM((points * blocks, size), F32),
                pltpu.VMEM((PARTS, batches * 8, size), F32),
                pltpu.VMEM((PARTS, batches * 8, size), F32),
            ],
        ),
        out_shape=(jax.ShapeDtypeStruct(tile_shape, BF16), jax.ShapeDtypeStruct(out_shape, F32)),
        compiler_params=pltpu.CompilerParams(vmem_limit_bytes=VMEM_LIMIT),
    )(region, pattern, basis, field, basis_grad, weights, weight_grad, fn_atom, batch_atom, places, *pieces)


def product_kernel(region, pattern, basis, tiles, out, spread, *, points, blocks, width):
    me = lax.axis_index("grid")
    size = tiles.shape[-1]
    matrix = batch_matrix(region, pattern, tiles, me, pl.program_id(0), blocks, width)
    product = jnp.dot(basis[0], matrix, preferred_element_type=F32)
    for t in range(blocks):
        spread[pl.ds(t, points, stride=blocks), :] = product[:, t * size : (t + 1) * size]
    out[0] = spread[...].astype(BF16)


def contract(region, pattern, basis, tiles, points, blocks, width):
    batches, _, columns = basis.shape
    size = columns // blocks
    return pl.pallas_call(
        functools.partial(product_kernel, points=points, blocks=blocks, width=width),
        grid_spec=pltpu.PrefetchScalarGridSpec(
            num_scalar_prefetch=2,
            grid=(batches,),
            in_specs=[
                pl.BlockSpec((1, points, columns), lambda b, *_: (b, 0, 0)),
                pl.BlockSpec(memory_space=pltpu.VMEM),
            ],
            out_specs=pl.BlockSpec((1, points * blocks, size), lambda b, *_: (b, 0, 0)),
            scratch_shapes=[pltpu.VMEM((points * blocks, size), F32)],
        ),
        out_shape=jax.ShapeDtypeStruct((batches, points * blocks, size), BF16),
        compiler_params=pltpu.CompilerParams(vmem_limit_bytes=VMEM_LIMIT),
        cost_estimate=pl.CostEstimate(
            flops=2 * batches * points * columns * columns,
            bytes_accessed=4 * batches * points * columns,
            transcendentals=0,
        ),
    )(region, pattern, basis, tiles)


def reorder_kernel(
    pattern_hbm,
    basis,
    field,
    basis_grad,
    weights_hbm,
    basis_out,
    field_out,
    weighted,
    grads,
    pattern,
    weights,
    columns,
    gather,
    basis_in,
    field_in,
    grad_in,
    wide,
    sems,
    small_sems,
):
    batches, blocks, points, size = basis_out.shape

    def copies(batch):
        return (
            pltpu.make_async_copy(field.at[batch], field_in.at[batch], sems.at[batch, 0]),
            pltpu.make_async_copy(basis.at[batch], basis_in.at[batch], sems.at[batch, 1]),
            pltpu.make_async_copy(basis_grad.at[:, batch], grad_in.at[:, batch], sems.at[batch, 2]),
        )

    small = (
        pltpu.make_async_copy(pattern_hbm, pattern, small_sems.at[0]),
        pltpu.make_async_copy(weights_hbm, weights, small_sems.at[1]),
    )
    for copy in small:
        copy.start()

    @pl.loop(0, batches)
    def _(batch):
        for copy in copies(batch):
            copy.start()

    for copy in small:
        copy.wait()
    rows = jnp.concatenate([weights[...], jnp.zeros((size - batches, points), F32)], axis=0).T
    for batch in range(batches):
        columns[batch] = jnp.broadcast_to(rows[:, batch : batch + 1], (points, size))
    depth = gather.shape[0]
    some = depth // blocks
    source = lax.broadcasted_iota(jnp.int32, (some, depth), 1)
    target = lax.broadcasted_iota(jnp.int32, (some, depth), 0) * blocks
    for s in range(blocks):
        gather[s * some : (s + 1) * some, :] = jnp.where(source == target + s, 1.0, 0.0).astype(BF16)

    @pl.loop(0, batches)
    def _(batch):
        for copy in copies(batch):
            copy.wait()
        points_here = pl.ds(pl.multiple_of(batch * points, points), points)
        places = [pattern[s, batch] for s in range(blocks)]
        for c in range(PARTS):
            wide[c] = grad_in[c, batch].astype(F32)
        for first in range(0, points, some):
            here = pl.ds(first * blocks, depth)
            both = jnp.concatenate([field_in[batch, here, :], basis_in[batch, here, :]], axis=1)
            both = jnp.dot(gather[...], both, preferred_element_type=F32)
            for s, place in enumerate(places):
                values = both[s * some : (s + 1) * some, :size]
                field_out[batch, place, pl.ds(first, some), :] = values.astype(BF16)
                scaled = values * columns[batch, pl.ds(first, some), :]
                weighted[place, pl.ds(pl.multiple_of(batch * points + first, some), some), :] = scaled.astype(BF16)
                values = both[s * some : (s + 1) * some, size:]
                basis_out[batch, place, pl.ds(first, some), :] = values.astype(BF16)
        for s, place in enumerate(places):
            strided = pl.ds(s, points, stride=blocks)
            for c in range(PARTS):
                grads[c, place, points_here, :] = wide[c, strided, :].astype(BF16)


def reorder(pattern, basis, field, basis_grad, weights, points, blocks):
    batches, rows, size = basis.shape
    hbm = pl.BlockSpec(memory_space=pl.ANY)
    vmem = pl.BlockSpec(memory_space=pltpu.VMEM)
    ordered = jax.ShapeDtypeStruct((batches, blocks, points, size), BF16)
    return pl.pallas_call(
        reorder_kernel,
        out_shape=(
            ordered,
            ordered,
            jax.ShapeDtypeStruct((blocks, batches * points, size), BF16),
            jax.ShapeDtypeStruct((PARTS, blocks, batches * points, size), BF16),
        ),
        in_specs=[hbm] * 5,
        out_specs=(vmem,) * 4,
        scratch_shapes=[
            pltpu.SMEM((blocks, batches), jnp.int32),
            pltpu.VMEM(weights.shape, F32),
            pltpu.VMEM((batches, points, size), F32),
            pltpu.VMEM((min(rows, 256), min(rows, 256)), BF16),
            pltpu.VMEM((batches, rows, size), BF16),
            pltpu.VMEM((batches, rows, size), BF16),
            pltpu.VMEM((PARTS, batches, rows, size), BF16),
            pltpu.VMEM((PARTS, rows, size), F32),
            pltpu.SemaphoreType.DMA((batches, 3)),
            pltpu.SemaphoreType.DMA((2,)),
        ],
        compiler_params=pltpu.CompilerParams(vmem_limit_bytes=VMEM_LIMIT),
        cost_estimate=pl.CostEstimate(
            flops=0, bytes_accessed=2 * (2 + PARTS) * batches * rows * size, transcendentals=0
        ),
    )(in_hbm(pattern.T), in_hbm(basis), in_hbm(field), in_hbm(basis_grad), in_hbm(weights))


def moment_kernel(weighted, grads, moments):
    blocks, _, size = grads.shape[1:]
    for p in range(0, blocks, 2):
        first, last = max(p - 1, 0), min(p + 3, blocks)
        left = jnp.concatenate([weighted[place] for place in range(first, last)], axis=1)
        for c in range(PARTS):
            right = jnp.concatenate([grads[c, p], grads[c, p + 1]], axis=1)
            moments[c, first * size : last * size, p * size : (p + 2) * size] = lax.dot_general(
                left, right, TN, preferred_element_type=F32
            )


def build_moments(weighted, grads):
    blocks, depth, size = grads.shape[1:]
    vmem = pl.BlockSpec(memory_space=pltpu.VMEM)
    return pl.pallas_call(
        moment_kernel,
        out_shape=jax.ShapeDtypeStruct((PARTS, blocks * size, blocks * size), F32),
        in_specs=[vmem, vmem],
        out_specs=vmem,
        compiler_params=pltpu.CompilerParams(vmem_limit_bytes=VMEM_LIMIT),
        cost_estimate=pl.CostEstimate(
            flops=2 * PARTS * depth * (blocks * size) ** 2, bytes_accessed=0, transcendentals=0
        ),
    )(weighted, grads)


def atom_kernel(region, fn_atom, batch_atom, weight_grad, hot, grad_columns):
    batches, points = weight_grad.shape[1:]
    size = fn_atom.shape[1]
    blocks = region.shape[1]
    me = lax.axis_index("grid")
    atoms = lax.broadcasted_iota(jnp.int32, (hot.shape[0], size), 0)
    ids = jnp.concatenate([batch_atom[...], jnp.full((1, size - batches), -1, jnp.int32)], axis=1)
    hot[:, blocks * size :] = jnp.where(atoms == ids, 1.0, 0.0).astype(BF16)

    @pl.loop(0, blocks)
    def _(position):
        ids = fn_atom[pl.ds(region[me, position], 1), :]
        columns = pl.ds(pl.multiple_of(position * size, size), size)
        hot[:, columns] = jnp.where(atoms == ids, 1.0, 0.0).astype(BF16)

    for c in range(PARTS):
        padding = jnp.zeros((size - batches, points), F32)
        grad_columns[c] = jnp.concatenate([weight_grad[c], padding], axis=0).T


def atom_matrix(region, fn_atom, batch_atom, weight_grad, blocks, size, atom_total):
    vmem = pl.BlockSpec(memory_space=pltpu.VMEM)
    return pl.pallas_call(
        atom_kernel,
        out_shape=(
            jax.ShapeDtypeStruct((atom_total, (blocks + 1) * size), BF16),
            jax.ShapeDtypeStruct((PARTS, weight_grad.shape[2], size), F32),
        ),
        in_specs=[pl.BlockSpec(memory_space=pltpu.SMEM)] + [vmem] * 3,
        out_specs=(vmem, vmem),
        compiler_params=pltpu.CompilerParams(vmem_limit_bytes=VMEM_LIMIT),
        cost_estimate=pl.CostEstimate(flops=1000000000, bytes_accessed=2 * atom_total * size, transcendentals=0),
    )(region, fn_atom.reshape(-1, size), batch_atom.reshape(1, -1), weight_grad)


def combine_kernel(
    region, basis, field, moments, hot, grad_columns, *rest, owner_rows, slabs, width, step
):
    *pieces, product_out, out, stage, matrix, energies = rest
    batches, blocks, points, size = basis.shape
    me = lax.axis_index("grid")
    me_atoms = lax.axis_index("atoms")
    half = (width - 1) // 2
    stage_rows(stage, pieces[0], pieces[1 : 1 + slabs // 2], pieces[1 + slabs // 2 :], slabs)
    rows = [region[me, position] for position in range(blocks)]
    found = [owner_and_slot(region, me, position, owner_rows) for position in range(blocks)]
    totals = [[jnp.zeros((8, size), F32) for _ in range(blocks)] for _ in range(PARTS)]
    for p in range(blocks):
        owner, slot, count = found[p]
        first = jnp.bitwise_xor(me, owner) * TRAVEL
        for q in range(blocks):
            if abs(q - p) > half:
                matrix[p * size : (p + 1) * size, q * size : (q + 1) * size] = jnp.zeros((size, size), BF16)
                continue
            k = rows[q] - rows[p] + half
            place = jnp.where(
                k == 0,
                travel_place(slot, count, 0),
                jnp.where(k == 1, travel_place(slot, count, 1), travel_place(slot, count, 2)),
            )
            inside = jnp.logical_and(k >= 0, k < width)
            tile = jnp.where(inside, stage[first + place], jnp.zeros((size, size), BF16))
            matrix[p * size : (p + 1) * size, q * size : (q + 1) * size] = tile
            turned = tile.T.astype(F32)
            for c in range(PARTS):
                terms = turned * moments[c, q * size : (q + 1) * size, p * size : (p + 1) * size]
                totals[c][p] = totals[c][p] + jnp.sum(terms.reshape(-1, 8, size), axis=0)
    derivative = [
        jnp.concatenate([jnp.sum(total, axis=0, keepdims=True) for total in totals[c]], axis=1) for c in range(PARTS)
    ]

    energies[...] = jnp.zeros_like(energies)
    lanes = lax.broadcasted_iota(jnp.int32, (points, size), 1)

    @pl.loop(0, batches // step)
    def _(group):
        left = [
            jnp.concatenate([basis[group * step + inner, p] for p in range(blocks)], axis=1) for inner in range(step)
        ]
        left = jnp.concatenate(left, axis=0)
        energy = [jnp.zeros((points, size), F32) for _ in range(step)]
        for q in range(0, blocks, 2):
            product = jnp.dot(left, matrix[:, q * size : (q + 2) * size], preferred_element_type=F32)
            for inner in range(step):
                batch = group * step + inner
                for column in range(2):
                    part = product[inner * points : (inner + 1) * points, column * size : (column + 1) * size]
                    product_out[batch, q + column] = part.astype(BF16)
                    energy[inner] = energy[inner] + part * field[batch, q + column].astype(F32)
        for inner in range(step):
            total = jnp.sum(energy[inner], axis=1, keepdims=True)
            energies[...] = jnp.where(lanes == group * step + inner, total, energies[...])

    lefts = []
    for c in range(PARTS):
        term = jnp.sum(energies[...] * grad_columns[c], axis=0, keepdims=True)
        lefts.append(jnp.concatenate([-2.0 * derivative[c], term], axis=1))
    left = jnp.concatenate(lefts, axis=0)
    high, middle, low = (piece.astype(F32) for piece in split(left))
    left = jnp.concatenate([high, middle, low, jnp.zeros((16 - 3 * PARTS, left.shape[1]), F32)], axis=0).astype(BF16)
    chunk = out.shape[-1]
    for device in range(out.shape[0]):
        sums = lax.dot_general(
            left, hot[device * chunk : (device + 1) * chunk, :], NT, preferred_element_type=F32
        )
        value = sums[:PARTS] + sums[PARTS : 2 * PARTS] + sums[2 * PARTS : 3 * PARTS]
        place = jnp.bitwise_xor(me_atoms, device)
        out[place, 0] = value
        out[jnp.bitwise_xor(place, 1), 1] = value


def combine(region, prepared, pieces, shapes):
    basis, field, moments, hot, grad_columns = prepared
    slabs, atom_devices, atom_total, points, blocks, width, owner_rows = shapes
    batches, _, _, size = basis.shape
    step = 16 if batches % 16 == 0 else 1
    vmem = pl.BlockSpec(memory_space=pltpu.VMEM)
    return pl.pallas_call(
        functools.partial(combine_kernel, owner_rows=owner_rows, slabs=slabs, width=width, step=step),
        out_shape=(
            jax.ShapeDtypeStruct(basis.shape, BF16),
            jax.ShapeDtypeStruct((atom_devices, 2, PARTS, atom_total // atom_devices), F32),
        ),
        in_specs=[pl.BlockSpec(memory_space=pltpu.SMEM)] + [vmem] * (5 + len(pieces)),
        out_specs=(vmem, vmem),
        scratch_shapes=[
            pltpu.VMEM((slabs * TRAVEL, size, size), BF16),
            pltpu.VMEM((blocks * size, blocks * size), BF16),
            pltpu.VMEM((points, size), F32),
        ],
        compiler_params=pltpu.CompilerParams(vmem_limit_bytes=VMEM_LIMIT),
    )(region, basis, field, moments, hot, grad_columns, *pieces)


def write_kernel(pattern, product, out, wide, staged, sems):
    batches, blocks, points, size = product.shape

    def copy(batch):
        return pltpu.make_async_copy(staged.at[batch], out.at[batch], sems.at[batch])

    @pl.loop(0, batches // 2)
    def _(pair):
        for inner in range(2):
            batch = pair * 2 + inner
            for t in range(blocks):
                wide[inner, pl.ds(t, points, stride=blocks), :] = product[batch, pattern[t, batch]].astype(F32)
            staged[batch] = wide[inner].astype(BF16)
            copy(batch).start()

    @pl.loop(0, batches)
    def _(batch):
        copy(batch).wait()


def write(pattern, product):
    batches, blocks, points, size = product.shape
    shape = (batches, points * blocks, size)
    return pl.pallas_call(
        write_kernel,
        out_shape=jax.ShapeDtypeStruct(shape, BF16),
        in_specs=[pl.BlockSpec(memory_space=pltpu.SMEM), pl.BlockSpec(memory_space=pltpu.VMEM)],
        out_specs=pl.BlockSpec(memory_space=pl.ANY),
        scratch_shapes=[
            pltpu.VMEM((2, points * blocks, size), F32),
            pltpu.VMEM(shape, BF16),
            pltpu.SemaphoreType.DMA((batches,)),
        ],
        compiler_params=pltpu.CompilerParams(vmem_limit_bytes=VMEM_LIMIT),
        cost_estimate=pl.CostEstimate(flops=0, bytes_accessed=4 * math.prod(shape), transcendentals=0),
    )(pattern.T, product)


def swap_halves(near, ready, atom_devices):
    near, ready = lax.optimization_barrier((near, ready))
    swap = [(i, i ^ 1) for i in range(atom_devices)]
    return near, [lax.ppermute(piece, "atoms", swap) for piece in near], ready


def tree_sum(values):
    if len(values) == 1:
        return values[0]
    half = len(values) // 2
    return tree_sum(values[:half]) + tree_sum(values[half:])


def pair_sums(values):
    return [values[i] + values[i + 1] for i in range(0, len(values), 2)]


def sum_parts(partial_grad, contracted, slabs, atom_devices):
    parts = [partial_grad[0]]
    for d in range(1, atom_devices):
        parts.append(lax.ppermute(partial_grad[d], "atoms", [(i, i ^ d) for i in range(atom_devices)]))
    parts, contracted = lax.optimization_barrier((parts, contracted))
    both = tree_sum(pair_sums(parts))
    swap = [(i, i ^ 1) for i in range(atom_devices)]
    far = []
    for shifts in partners(slabs):
        if shifts[0] != shifts[1]:
            far.append(lax.ppermute(both, ("grid", "atoms"), moves_over_grid(shifts, slabs, atom_devices)))
    near = lax.ppermute(both[0], "grid", [(i, i ^ 1) for i in range(slabs)])
    far = lax.optimization_barrier(far)
    swapped = [lax.ppermute(piece[1], "atoms", swap) for piece in far]
    sums = [both[0] + near] + [piece[0] + other for piece, other in zip(far, swapped)]
    return tree_sum(sums), contracted


def local(
    basis,
    basis_grad,
    exchange_field,
    weights,
    weight_grad,
    density,
    region,
    pattern,
    fn_atom,
    batch_atom,
):
    batches, points, blocks, size = basis.shape
    owner_rows, width = density.shape[:2]
    slabs = lax.axis_size("grid")
    atom_devices = lax.axis_size("atoms")
    atom_total = fn_atom.shape[0] // (10 * slabs * atom_devices) * slabs * atom_devices
    shapes = (slabs, atom_devices, atom_total, points, blocks, width, owner_rows)
    flat_basis = basis.reshape(batches, points * blocks, size)
    flat_field = exchange_field.reshape(batches, points * blocks, size)
    flat_grad = basis_grad.reshape(PARTS, batches, points * blocks, size)
    own, near = fetch_rows(region, density, slabs, atom_devices)
    if region.shape[1] == blocks:
        basis_wide, field_wide, weighted, grads = reorder(
            pattern, flat_basis, flat_field, flat_grad, weights, points, blocks
        )
        ready = (basis_wide, field_wide, build_moments(weighted, grads), batch_atom)
        near, far, (basis_wide, field_wide, moments, batch_atom) = swap_halves(near, ready, atom_devices)
        hot, grad_columns = atom_matrix(region, fn_atom, batch_atom, weight_grad, blocks, size, atom_total)
        ready = (basis_wide, field_wide, moments, hot, grad_columns)
        product, partial_grad = combine(region, ready, [own, *near, *far], shapes)
        gradient, contracted = sum_parts(partial_grad, write(pattern, product), slabs, atom_devices)
        return contracted.reshape(basis.shape), gradient
    ready = relayout(in_hbm(flat_basis), in_hbm(flat_field), points, blocks)
    near, far, (basis_wide, field_wide) = swap_halves(near, ready, atom_devices)
    tiles, partial_grad = partial_gradient(
        region,
        pattern,
        basis_wide,
        field_wide,
        in_hbm(flat_grad),
        weights,
        weight_grad,
        fn_atom,
        batch_atom,
        [own, *near, *far],
        shapes,
    )
    contracted = contract(region, pattern, basis_wide, tiles, points, blocks, width)
    gradient, contracted = sum_parts(partial_grad, contracted, slabs, atom_devices)
    return contracted.reshape(basis.shape), gradient


def solution(mesh):
    placed = (
        P(("groups", "grid", "atoms"), None, None, None),
        P(None, ("groups", "grid", "atoms"), None, None, None),
        P(("groups", "grid", "atoms"), None, None, None),
        P(("groups", "grid", "atoms"), None),
        P(None, ("groups", "grid", "atoms"), None),
        P(("groups", "grid"), None, None, None),
        P("groups", None),
        P(("groups", "grid", "atoms"), None),
        P("groups"),
        P(("groups", "grid", "atoms")),
    )
    return jax.shard_map(
        local,
        mesh=mesh,
        in_specs=placed,
        out_specs=(P(("groups", "grid", "atoms"), None, None, None), P(None, ("groups", "atoms"))),
        check_vma=False,
    )
```

```python
import functools
import math

import jax
import jax.numpy as jnp
from jax import lax
from jax.experimental import pallas as pl
from jax.experimental.pallas import tpu as pltpu
from jax.sharding import PartitionSpec as P

TRAVEL = 5
PARTS = 3
F32 = jnp.float32
BF16 = jnp.bfloat16
NT = (((1,), (1,)), ((), ()))
TN = (((0,), (0,)), ((), ()))
VMEM_LIMIT = 32 * 1024 * 1024


def owner_and_slot(region, slab, position, owner_rows):
    owner = lax.div(region[slab, position], owner_rows)
    slot = jnp.int32(0)
    count = jnp.int32(0)
    for other in range(region.shape[1]):
        same = jnp.where(lax.div(region[slab, other], owner_rows) == owner, 1, 0)
        count = count + same
        slot = slot + jnp.where(other < position, same, 0)
    return owner, slot, count


def travel_place(slot, count, k):
    if k == 0:
        return jnp.where(slot == 0, 4, 2)
    if k == 1:
        return jnp.where(slot == 0, 0, 3)
    return jnp.where(jnp.logical_and(slot == 0, count == 2), 1, 4)


def partners(slabs):
    return [(1, 1)] + [(shift + 1, shift) for shift in range(2, slabs, 2)]


def moves_over_grid(shifts, slabs, atom_devices):
    return [
        (z * atom_devices + a, (z ^ shifts[a % 2]) * atom_devices + a) for z in range(slabs) for a in range(atom_devices)
    ]


def send_kernel(region_hbm, density, *rest):
    *outs, region, held, region_sem, sems = rest
    fetch = pltpu.make_async_copy(region_hbm, region, region_sem)
    fetch.start()
    count_here = density.shape[0] // sems.shape[0]
    fetches = []
    for part in range(sems.shape[0]):
        here = pl.ds(part * count_here, count_here)
        fetches.append(pltpu.make_async_copy(density.at[here], held.at[here], sems.at[part]))
    for copy in fetches:
        copy.start()
    fetch.wait()
    me = lax.axis_index("grid")
    core = lax.rem(lax.axis_index("atoms"), 2)
    slabs, size = region.shape
    owner_rows = density.shape[0]
    picks = []
    for low, high in [(0, 0)] + partners(slabs):
        slab = jnp.bitwise_xor(me, jnp.where(core == 0, low, high))
        base = jnp.int32(owner_rows)
        count = jnp.int32(0)
        for position in range(size):
            row = region[slab, position] - me * owner_rows
            mine = jnp.logical_and(row >= 0, row < owner_rows)
            base = jnp.minimum(base, jnp.where(mine, row, owner_rows))
            count = count + jnp.where(mine, 1, 0)
        base = jnp.where(count == 0, 0, base)
        after = jnp.minimum(base + 1, owner_rows - 1)
        lower = base == 0
        edge = jnp.where(jnp.logical_and(count == 2, jnp.logical_not(lower)), after, base)
        picks.append(((base, 1), (base, 2), (after, 0), (after, 1), (edge, jnp.where(lower, 0, 2))))
    for copy in fetches:
        copy.wait()
    for out, places in zip(outs, picks):
        for place, (row, k) in enumerate(places):
            out[place] = held[row, k]


def in_hbm(array):
    return pltpu.with_memory_space_constraint(array, pltpu.HBM)


def rows_to_send(region, density, slabs):
    size = density.shape[-1]
    count = 1 + len(partners(slabs))
    hbm = pl.BlockSpec(memory_space=pl.ANY)
    return pl.pallas_call(
        send_kernel,
        out_shape=[jax.ShapeDtypeStruct((TRAVEL, size, size), density.dtype)] * count,
        in_specs=[hbm, hbm],
        out_specs=[pl.BlockSpec(memory_space=pltpu.VMEM)] * count,
        scratch_shapes=[
            pltpu.SMEM(region.shape, jnp.int32),
            pltpu.VMEM(density.shape, density.dtype),
            pltpu.SemaphoreType.DMA,
            pltpu.SemaphoreType.DMA((5 if density.shape[0] % 5 == 0 else 1,)),
        ],
        compiler_params=pltpu.CompilerParams(vmem_limit_bytes=VMEM_LIMIT),
    )(in_hbm(region), in_hbm(density))


def fetch_rows(region, density, slabs, atom_devices):
    own, *outgoing = rows_to_send(region, density, slabs)
    near = []
    for shifts, piece in zip(partners(slabs), outgoing):
        near.append(lax.ppermute(piece, ("grid", "atoms"), moves_over_grid(shifts, slabs, atom_devices)))
    return own, near


def stage_rows(stage, own, near, far, slabs):
    core = lax.rem(lax.axis_index("atoms"), 2)
    first, *pairs = partners(slabs)
    for place in range(TRAVEL):
        stage[place] = own[place]
        stage[first[0] * TRAVEL + place] = near[0][place]
    for (low, high), here, there in zip(pairs, near[1:], far):
        mine = jnp.where(core == 0, low, high) * TRAVEL
        other = jnp.where(core == 0, high, low) * TRAVEL
        for place in range(TRAVEL):
            stage[mine + place] = here[place]
            stage[other + place] = there[place]


def block_major(x_ref, wide, points, blocks):
    wide[...] = x_ref[0].astype(F32)
    return [wide[pl.ds(s, points, stride=blocks), :] for s in range(blocks)]


def relayout_kernel(basis, field, basis_out, field_out, wide, *, points, blocks):
    size = basis.shape[-1]
    for source, target in ((basis, basis_out), (field, field_out)):
        for s, part in enumerate(block_major(source, wide, points, blocks)):
            target[0, :, s * size : (s + 1) * size] = part.astype(BF16)


def relayout(basis, field, points, blocks):
    batches, rows, size = basis.shape
    here = pl.BlockSpec((1, rows, size), lambda b: (b, 0, 0))
    there = pl.BlockSpec((1, points, blocks * size), lambda b: (b, 0, 0))
    shape = jax.ShapeDtypeStruct((batches, points, blocks * size), BF16)
    return pl.pallas_call(
        functools.partial(relayout_kernel, points=points, blocks=blocks),
        grid=(batches,),
        out_shape=(shape, shape),
        in_specs=[here, here],
        out_specs=(there, there),
        scratch_shapes=[pltpu.VMEM((rows, size), F32)],
        compiler_params=pltpu.CompilerParams(vmem_limit_bytes=VMEM_LIMIT),
        cost_estimate=pl.CostEstimate(flops=0, bytes_accessed=8 * batches * rows * size, transcendentals=0),
    )(basis, field)


def batch_matrix(region, pattern, tiles, slab, batch, blocks, width):
    half = (width - 1) // 2
    none = tiles.shape[0] - 1
    places = [pattern[batch, s] for s in range(blocks)]
    rows = [region[slab, place] for place in places]
    strips = []
    for s in range(blocks):
        strip = []
        for t in range(blocks):
            k = rows[t] - rows[s] + half
            inside = jnp.logical_and(k >= 0, k < width)
            strip.append(tiles[jnp.where(inside, places[s] * width + k, none)])
        strips.append(jnp.concatenate(strip, axis=1))
    return jnp.concatenate(strips, axis=0)


def split(values):
    high = values.astype(BF16)
    rest = values - high.astype(F32)
    middle = rest.astype(BF16)
    low = (rest - middle.astype(F32)).astype(BF16)
    return high, middle, low


def gradient_kernel(
    region,
    pattern,
    basis,
    field,
    basis_grad,
    weights,
    weight_grad,
    fn_atom,
    batch_atom,
    places,
    *rest,
    points,
    blocks,
    width,
    owner_rows,
    slabs,
):
    *pieces, tiles, out, stage, spread, sums, energy_sums = rest
    batch = pl.program_id(0)
    batches = pl.num_programs(0)
    me = lax.axis_index("grid")
    me_atoms = lax.axis_index("atoms")
    size = tiles.shape[-1]
    region_size = region.shape[1]

    @pl.when(batch == 0)
    def _():
        tiles[region_size * width] = jnp.zeros((size, size), BF16)
        stage_rows(stage, pieces[0], pieces[1 : 1 + slabs // 2], pieces[1 + slabs // 2 :], slabs)
        for position in range(region_size):
            owner, slot, count = owner_and_slot(region, me, position, owner_rows)
            shift = jnp.bitwise_xor(me, owner)
            for k in range(width):
                tiles[position * width + k] = stage[shift * TRAVEL + travel_place(slot, count, k)]

    matrix = batch_matrix(region, pattern, tiles, me, batch, blocks, width)
    potential = lax.dot_general(field[0], matrix, NT, preferred_element_type=F32)
    rows = jnp.concatenate(
        [weights[pl.ds(batch, 1), :]]
        + [weight_grad[c, pl.ds(batch, 1), :] for c in range(PARTS)]
        + [jnp.zeros((8 - 1 - PARTS, points), F32)],
        axis=0,
    )
    columns = rows.T
    weight = columns[:, 0:1]
    energy = jnp.zeros((points, size), F32)
    for s in range(blocks):
        here = potential[:, s * size : (s + 1) * size]
        energy = energy + basis[0, :, s * size : (s + 1) * size].astype(F32) * here
        spread[pl.ds(s, points, stride=blocks), :] = here * weight
    scaled = spread[...]
    place = pl.ds(pl.multiple_of(batch * 8, 8), 8)
    for c in range(PARTS):
        terms = basis_grad[c, 0].astype(F32) * scaled
        sums[c, place, :] = jnp.sum(terms.reshape(-1, 8, size), axis=0)
        terms = energy * columns[:, 1 + c : 2 + c]
        energy_sums[c, place, :] = jnp.sum(terms.reshape(-1, 8, size), axis=0)

    @pl.when(batch == batches - 1)
    def _():
        padded = max(8, region_size)
        chosen = lax.broadcasted_iota(jnp.int32, (padded, places.shape[1]), 0) == places[...]
        chosen = chosen.astype(BF16)
        blocks_sum = []
        for c in range(PARTS):
            total = jnp.zeros((padded, size), F32)
            for piece in split(sums[c]):
                total = total + jnp.dot(chosen, piece, preferred_element_type=F32)
            blocks_sum.append(-2.0 * total)
        lefts = []
        for position in range(region_size):
            stack = jnp.concatenate([total[position : position + 1] for total in blocks_sum], axis=0)
            high, middle, low = (piece.astype(F32) for piece in split(stack))
            lefts.append(jnp.concatenate([high, middle, low, jnp.zeros((16 - 3 * PARTS, size), F32)], axis=0))
        left = jnp.concatenate(lefts, axis=1).astype(BF16)
        chunk = out.shape[-1]
        scale = [jnp.sum(energy_sums[c], axis=1, keepdims=True) for c in range(PARTS)]
        for device in range(out.shape[0]):
            atoms = lax.broadcasted_iota(jnp.int32, (chunk, size), 0) + device * chunk
            hot = [
                jnp.where(atoms == fn_atom[pl.ds(region[me, position], 1), :], 1.0, 0.0).astype(BF16)
                for position in range(region_size)
            ]
            found = lax.dot_general(left, jnp.concatenate(hot, axis=1), NT, preferred_element_type=F32)
            atoms = lax.broadcasted_iota(jnp.int32, (batch_atom.shape[0], chunk), 1) + device * chunk
            mine = atoms == batch_atom[...]
            for c in range(PARTS):
                value = found[c : c + 1] + found[PARTS + c : PARTS + c + 1] + found[2 * PARTS + c : 2 * PARTS + c + 1]
                value = value + jnp.sum(jnp.where(mine, scale[c], 0.0), axis=0, keepdims=True)
                place = jnp.bitwise_xor(me_atoms, device)
                out[place, 0, c : c + 1, :] = value
                out[jnp.bitwise_xor(place, 1), 1, c : c + 1, :] = value


def partial_gradient(
    region, pattern, basis, field, basis_grad, weights, weight_grad, fn_atom, batch_atom, pieces, shapes
):
    slabs, atom_devices, atom_total, points, blocks, width, owner_rows = shapes
    batches, _, columns = basis.shape
    size = columns // blocks
    region_size = region.shape[1]
    fn_atom = fn_atom.reshape(-1, size)
    places = jnp.broadcast_to(pattern[:, None, :], (batches, 8 // blocks, blocks)).reshape(1, -1)
    batch_atom = jnp.broadcast_to(batch_atom[:, None], (batches, 8)).reshape(-1, 1)
    block = pl.BlockSpec((1, points, columns), lambda b, *_: (b, 0, 0))
    whole = pl.BlockSpec(memory_space=pltpu.VMEM)
    tile_shape = (region_size * width + 1, size, size)
    out_shape = (atom_devices, 2, PARTS, atom_total // atom_devices)
    return pl.pallas_call(
        functools.partial(
            gradient_kernel, points=points, blocks=blocks, width=width, owner_rows=owner_rows, slabs=slabs
        ),
        grid_spec=pltpu.PrefetchScalarGridSpec(
            num_scalar_prefetch=2,
            grid=(batches,),
            in_specs=[
                block,
                block,
                pl.BlockSpec((PARTS, 1, points * blocks, size), lambda b, *_: (0, b, 0, 0)),
            ]
            + [whole] * (5 + len(pieces)),
            out_specs=(whole, whole),
            scratch_shapes=[
                pltpu.VMEM((slabs * TRAVEL, size, size), BF16),
                pltpu.VMEM((points * blocks, size), F32),
                pltpu.VMEM((PARTS, batches * 8, size), F32),
                pltpu.VMEM((PARTS, batches * 8, size), F32),
            ],
        ),
        out_shape=(jax.ShapeDtypeStruct(tile_shape, BF16), jax.ShapeDtypeStruct(out_shape, F32)),
        compiler_params=pltpu.CompilerParams(vmem_limit_bytes=VMEM_LIMIT),
    )(region, pattern, basis, field, basis_grad, weights, weight_grad, fn_atom, batch_atom, places, *pieces)


def product_kernel(region, pattern, basis, tiles, out, spread, *, points, blocks, width):
    me = lax.axis_index("grid")
    size = tiles.shape[-1]
    matrix = batch_matrix(region, pattern, tiles, me, pl.program_id(0), blocks, width)
    product = jnp.dot(basis[0], matrix, preferred_element_type=F32)
    for t in range(blocks):
        spread[pl.ds(t, points, stride=blocks), :] = product[:, t * size : (t + 1) * size]
    out[0] = spread[...].astype(BF16)


def contract(region, pattern, basis, tiles, points, blocks, width):
    batches, _, columns = basis.shape
    size = columns // blocks
    return pl.pallas_call(
        functools.partial(product_kernel, points=points, blocks=blocks, width=width),
        grid_spec=pltpu.PrefetchScalarGridSpec(
            num_scalar_prefetch=2,
            grid=(batches,),
            in_specs=[
                pl.BlockSpec((1, points, columns), lambda b, *_: (b, 0, 0)),
                pl.BlockSpec(memory_space=pltpu.VMEM),
            ],
            out_specs=pl.BlockSpec((1, points * blocks, size), lambda b, *_: (b, 0, 0)),
            scratch_shapes=[pltpu.VMEM((points * blocks, size), F32)],
        ),
        out_shape=jax.ShapeDtypeStruct((batches, points * blocks, size), BF16),
        compiler_params=pltpu.CompilerParams(vmem_limit_bytes=VMEM_LIMIT),
        cost_estimate=pl.CostEstimate(
            flops=2 * batches * points * columns * columns,
            bytes_accessed=4 * batches * points * columns,
            transcendentals=0,
        ),
    )(region, pattern, basis, tiles)


def reorder_kernel(
    pattern_hbm,
    basis,
    field,
    basis_grad,
    weights_hbm,
    basis_out,
    field_out,
    weighted,
    grads,
    pattern,
    weights,
    columns,
    basis_in,
    field_in,
    grad_in,
    wide,
    sems,
    small_sems,
):
    batches, blocks, points, size = basis_out.shape

    def copies(batch):
        return (
            pltpu.make_async_copy(field.at[batch], field_in.at[batch], sems.at[batch, 0]),
            pltpu.make_async_copy(basis.at[batch], basis_in.at[batch], sems.at[batch, 1]),
            pltpu.make_async_copy(basis_grad.at[:, batch], grad_in.at[:, batch], sems.at[batch, 2]),
        )

    small = (
        pltpu.make_async_copy(pattern_hbm, pattern, small_sems.at[0]),
        pltpu.make_async_copy(weights_hbm, weights, small_sems.at[1]),
    )
    for copy in small:
        copy.start()

    @pl.loop(0, batches)
    def _(batch):
        for copy in copies(batch):
            copy.start()

    for copy in small:
        copy.wait()
    rows = jnp.concatenate([weights[...], jnp.zeros((size - batches, points), F32)], axis=0).T
    for batch in range(batches):
        columns[batch] = jnp.broadcast_to(rows[:, batch : batch + 1], (points, size))

    @pl.loop(0, batches)
    def _(batch):
        for copy in copies(batch):
            copy.wait()
        points_here = pl.ds(pl.multiple_of(batch * points, points), points)
        places = [pattern[s, batch] for s in range(blocks)]
        wide[0] = field_in[batch].astype(F32)
        wide[1] = basis_in[batch].astype(F32)
        for c in range(PARTS):
            wide[2 + c] = grad_in[c, batch].astype(F32)
        for s, place in enumerate(places):
            strided = pl.ds(s, points, stride=blocks)
            values = wide[0, strided, :]
            field_out[batch, place] = values.astype(BF16)
            weighted[place, points_here, :] = (values * columns[batch]).astype(BF16)
            basis_out[batch, place] = wide[1, strided, :].astype(BF16)
            for c in range(PARTS):
                grads[c, place, points_here, :] = wide[2 + c, strided, :].astype(BF16)


def reorder(pattern, basis, field, basis_grad, weights, points, blocks):
    batches, rows, size = basis.shape
    hbm = pl.BlockSpec(memory_space=pl.ANY)
    vmem = pl.BlockSpec(memory_space=pltpu.VMEM)
    ordered = jax.ShapeDtypeStruct((batches, blocks, points, size), BF16)
    return pl.pallas_call(
        reorder_kernel,
        out_shape=(
            ordered,
            ordered,
            jax.ShapeDtypeStruct((blocks, batches * points, size), BF16),
            jax.ShapeDtypeStruct((PARTS, blocks, batches * points, size), BF16),
        ),
        in_specs=[hbm] * 5,
        out_specs=(vmem,) * 4,
        scratch_shapes=[
            pltpu.SMEM((blocks, batches), jnp.int32),
            pltpu.VMEM(weights.shape, F32),
            pltpu.VMEM((batches, points, size), F32),
            pltpu.VMEM((batches, rows, size), BF16),
            pltpu.VMEM((batches, rows, size), BF16),
            pltpu.VMEM((PARTS, batches, rows, size), BF16),
            pltpu.VMEM((2 + PARTS, rows, size), F32),
            pltpu.SemaphoreType.DMA((batches, 3)),
            pltpu.SemaphoreType.DMA((2,)),
        ],
        compiler_params=pltpu.CompilerParams(vmem_limit_bytes=VMEM_LIMIT),
        cost_estimate=pl.CostEstimate(
            flops=0, bytes_accessed=2 * (2 + PARTS) * batches * rows * size, transcendentals=0
        ),
    )(in_hbm(pattern.T), in_hbm(basis), in_hbm(field), in_hbm(basis_grad), in_hbm(weights))


def moment_kernel(weighted, grads, moments):
    blocks, _, size = grads.shape[1:]
    for p in range(0, blocks, 2):
        first, last = max(p - 1, 0), min(p + 3, blocks)
        left = jnp.concatenate([weighted[place] for place in range(first, last)], axis=1)
        for c in range(PARTS):
            right = jnp.concatenate([grads[c, p], grads[c, p + 1]], axis=1)
            moments[c, first * size : last * size, p * size : (p + 2) * size] = lax.dot_general(
                left, right, TN, preferred_element_type=F32
            )


def build_moments(weighted, grads):
    blocks, depth, size = grads.shape[1:]
    vmem = pl.BlockSpec(memory_space=pltpu.VMEM)
    return pl.pallas_call(
        moment_kernel,
        out_shape=jax.ShapeDtypeStruct((PARTS, blocks * size, blocks * size), F32),
        in_specs=[vmem, vmem],
        out_specs=vmem,
        compiler_params=pltpu.CompilerParams(vmem_limit_bytes=VMEM_LIMIT),
        cost_estimate=pl.CostEstimate(
            flops=2 * PARTS * depth * (blocks * size) ** 2, bytes_accessed=0, transcendentals=0
        ),
    )(weighted, grads)


def atom_kernel(region, fn_atom, batch_atom, weight_grad, hot, grad_columns):
    batches, points = weight_grad.shape[1:]
    size = fn_atom.shape[1]
    blocks = region.shape[1]
    me = lax.axis_index("grid")
    atoms = lax.broadcasted_iota(jnp.int32, (hot.shape[0], size), 0)
    ids = jnp.concatenate([batch_atom[...], jnp.full((1, size - batches), -1, jnp.int32)], axis=1)
    hot[:, blocks * size :] = jnp.where(atoms == ids, 1.0, 0.0).astype(BF16)

    @pl.loop(0, blocks)
    def _(position):
        ids = fn_atom[pl.ds(region[me, position], 1), :]
        columns = pl.ds(pl.multiple_of(position * size, size), size)
        hot[:, columns] = jnp.where(atoms == ids, 1.0, 0.0).astype(BF16)

    for c in range(PARTS):
        padding = jnp.zeros((size - batches, points), F32)
        grad_columns[c] = jnp.concatenate([weight_grad[c], padding], axis=0).T


def atom_matrix(region, fn_atom, batch_atom, weight_grad, blocks, size, atom_total):
    vmem = pl.BlockSpec(memory_space=pltpu.VMEM)
    return pl.pallas_call(
        atom_kernel,
        out_shape=(
            jax.ShapeDtypeStruct((atom_total, (blocks + 1) * size), BF16),
            jax.ShapeDtypeStruct((PARTS, weight_grad.shape[2], size), F32),
        ),
        in_specs=[pl.BlockSpec(memory_space=pltpu.SMEM)] + [vmem] * 3,
        out_specs=(vmem, vmem),
        compiler_params=pltpu.CompilerParams(vmem_limit_bytes=VMEM_LIMIT),
        cost_estimate=pl.CostEstimate(flops=1000000000, bytes_accessed=2 * atom_total * size, transcendentals=0),
    )(region, fn_atom.reshape(-1, size), batch_atom.reshape(1, -1), weight_grad)


def combine_kernel(
    region, basis, field, moments, hot, grad_columns, *rest, owner_rows, slabs, width, step
):
    *pieces, product_out, out, stage, matrix, energies = rest
    batches, blocks, points, size = basis.shape
    me = lax.axis_index("grid")
    me_atoms = lax.axis_index("atoms")
    half = (width - 1) // 2
    stage_rows(stage, pieces[0], pieces[1 : 1 + slabs // 2], pieces[1 + slabs // 2 :], slabs)
    rows = [region[me, position] for position in range(blocks)]
    found = [owner_and_slot(region, me, position, owner_rows) for position in range(blocks)]
    totals = [[jnp.zeros((8, size), F32) for _ in range(blocks)] for _ in range(PARTS)]
    for p in range(blocks):
        owner, slot, count = found[p]
        first = jnp.bitwise_xor(me, owner) * TRAVEL
        for q in range(blocks):
            if abs(q - p) > half:
                matrix[p * size : (p + 1) * size, q * size : (q + 1) * size] = jnp.zeros((size, size), BF16)
                continue
            k = rows[q] - rows[p] + half
            place = jnp.where(
                k == 0,
                travel_place(slot, count, 0),
                jnp.where(k == 1, travel_place(slot, count, 1), travel_place(slot, count, 2)),
            )
            inside = jnp.logical_and(k >= 0, k < width)
            tile = jnp.where(inside, stage[first + place], jnp.zeros((size, size), BF16))
            matrix[p * size : (p + 1) * size, q * size : (q + 1) * size] = tile
            turned = tile.T.astype(F32)
            for c in range(PARTS):
                terms = turned * moments[c, q * size : (q + 1) * size, p * size : (p + 1) * size]
                totals[c][p] = totals[c][p] + jnp.sum(terms.reshape(-1, 8, size), axis=0)
    derivative = [
        jnp.concatenate([jnp.sum(total, axis=0, keepdims=True) for total in totals[c]], axis=1) for c in range(PARTS)
    ]

    energies[...] = jnp.zeros_like(energies)
    lanes = lax.broadcasted_iota(jnp.int32, (points, size), 1)

    @pl.loop(0, batches // step)
    def _(group):
        left = [
            jnp.concatenate([basis[group * step + inner, p] for p in range(blocks)], axis=1) for inner in range(step)
        ]
        left = jnp.concatenate(left, axis=0)
        energy = [jnp.zeros((points, size), F32) for _ in range(step)]
        for q in range(0, blocks, 2):
            product = jnp.dot(left, matrix[:, q * size : (q + 2) * size], preferred_element_type=F32)
            for inner in range(step):
                batch = group * step + inner
                for column in range(2):
                    part = product[inner * points : (inner + 1) * points, column * size : (column + 1) * size]
                    product_out[batch, q + column] = part.astype(BF16)
                    energy[inner] = energy[inner] + part * field[batch, q + column].astype(F32)
        for inner in range(step):
            total = jnp.sum(energy[inner], axis=1, keepdims=True)
            energies[...] = jnp.where(lanes == group * step + inner, total, energies[...])

    lefts = []
    for c in range(PARTS):
        term = jnp.sum(energies[...] * grad_columns[c], axis=0, keepdims=True)
        lefts.append(jnp.concatenate([-2.0 * derivative[c], term], axis=1))
    left = jnp.concatenate(lefts, axis=0)
    high, middle, low = (piece.astype(F32) for piece in split(left))
    left = jnp.concatenate([high, middle, low, jnp.zeros((16 - 3 * PARTS, left.shape[1]), F32)], axis=0).astype(BF16)
    chunk = out.shape[-1]
    for device in range(out.shape[0]):
        sums = lax.dot_general(
            left, hot[device * chunk : (device + 1) * chunk, :], NT, preferred_element_type=F32
        )
        value = sums[:PARTS] + sums[PARTS : 2 * PARTS] + sums[2 * PARTS : 3 * PARTS]
        place = jnp.bitwise_xor(me_atoms, device)
        out[place, 0] = value
        out[jnp.bitwise_xor(place, 1), 1] = value


def combine(region, prepared, pieces, shapes):
    basis, field, moments, hot, grad_columns = prepared
    slabs, atom_devices, atom_total, points, blocks, width, owner_rows = shapes
    batches, _, _, size = basis.shape
    step = 16 if batches % 16 == 0 else 1
    vmem = pl.BlockSpec(memory_space=pltpu.VMEM)
    return pl.pallas_call(
        functools.partial(combine_kernel, owner_rows=owner_rows, slabs=slabs, width=width, step=step),
        out_shape=(
            jax.ShapeDtypeStruct(basis.shape, BF16),
            jax.ShapeDtypeStruct((atom_devices, 2, PARTS, atom_total // atom_devices), F32),
        ),
        in_specs=[pl.BlockSpec(memory_space=pltpu.SMEM)] + [vmem] * (5 + len(pieces)),
        out_specs=(vmem, vmem),
        scratch_shapes=[
            pltpu.VMEM((slabs * TRAVEL, size, size), BF16),
            pltpu.VMEM((blocks * size, blocks * size), BF16),
            pltpu.VMEM((points, size), F32),
        ],
        compiler_params=pltpu.CompilerParams(vmem_limit_bytes=VMEM_LIMIT),
    )(region, basis, field, moments, hot, grad_columns, *pieces)


def write_kernel(pattern, product, out, wide, staged, sems):
    batches, blocks, points, size = product.shape

    def copy(batch):
        return pltpu.make_async_copy(staged.at[batch], out.at[batch], sems.at[batch])

    @pl.loop(0, batches // 2)
    def _(pair):
        for inner in range(2):
            batch = pair * 2 + inner
            for t in range(blocks):
                wide[inner, pl.ds(t, points, stride=blocks), :] = product[batch, pattern[t, batch]].astype(F32)
            staged[batch] = wide[inner].astype(BF16)
            copy(batch).start()

    @pl.loop(0, batches)
    def _(batch):
        copy(batch).wait()


def write(pattern, product):
    batches, blocks, points, size = product.shape
    shape = (batches, points * blocks, size)
    return pl.pallas_call(
        write_kernel,
        out_shape=jax.ShapeDtypeStruct(shape, BF16),
        in_specs=[pl.BlockSpec(memory_space=pltpu.SMEM), pl.BlockSpec(memory_space=pltpu.VMEM)],
        out_specs=pl.BlockSpec(memory_space=pl.ANY),
        scratch_shapes=[
            pltpu.VMEM((2, points * blocks, size), F32),
            pltpu.VMEM(shape, BF16),
            pltpu.SemaphoreType.DMA((batches,)),
        ],
        compiler_params=pltpu.CompilerParams(vmem_limit_bytes=VMEM_LIMIT),
        cost_estimate=pl.CostEstimate(flops=0, bytes_accessed=4 * math.prod(shape), transcendentals=0),
    )(pattern.T, product)


def swap_between_cores(near, ready, atom_devices):
    near, ready = lax.optimization_barrier((near, ready))
    swap = [(i, i ^ 1) for i in range(atom_devices)]
    return near, [lax.ppermute(piece, "atoms", swap) for piece in near[1:]], ready


def tree_sum(values):
    if len(values) == 1:
        return values[0]
    half = len(values) // 2
    return tree_sum(values[:half]) + tree_sum(values[half:])


def pair_sums(values):
    return [values[i] + values[i + 1] for i in range(0, len(values), 2)]


def sum_parts(partial_grad, contracted, slabs, atom_devices):
    parts = [partial_grad[0]]
    for d in range(1, atom_devices):
        parts.append(lax.ppermute(partial_grad[d], "atoms", [(i, i ^ d) for i in range(atom_devices)]))
    parts, contracted = lax.optimization_barrier((parts, contracted))
    both = tree_sum(pair_sums(parts))
    swap = [(i, i ^ 1) for i in range(atom_devices)]
    far = []
    for shifts in partners(slabs)[1:]:
        far.append(lax.ppermute(both, ("grid", "atoms"), moves_over_grid(shifts, slabs, atom_devices)))
    near = lax.ppermute(both[0], "grid", [(i, i ^ 1) for i in range(slabs)])
    far = lax.optimization_barrier(far)
    swapped = [lax.ppermute(piece[1], "atoms", swap) for piece in far]
    sums = [both[0] + near] + [piece[0] + other for piece, other in zip(far, swapped)]
    return tree_sum(sums), contracted


def local(
    basis,
    basis_grad,
    exchange_field,
    weights,
    weight_grad,
    density,
    region,
    pattern,
    fn_atom,
    batch_atom,
):
    batches, points, blocks, size = basis.shape
    owner_rows, width = density.shape[:2]
    slabs = lax.axis_size("grid")
    atom_devices = lax.axis_size("atoms")
    atom_total = fn_atom.shape[0] // (10 * slabs * atom_devices) * slabs * atom_devices
    shapes = (slabs, atom_devices, atom_total, points, blocks, width, owner_rows)
    flat_basis = basis.reshape(batches, points * blocks, size)
    flat_field = exchange_field.reshape(batches, points * blocks, size)
    flat_grad = basis_grad.reshape(PARTS, batches, points * blocks, size)
    own, near = fetch_rows(region, density, slabs, atom_devices)
    if region.shape[1] == blocks:
        basis_wide, field_wide, weighted, grads = reorder(
            pattern, flat_basis, flat_field, flat_grad, weights, points, blocks
        )
        ready = (basis_wide, field_wide, build_moments(weighted, grads), batch_atom)
        near, far, (basis_wide, field_wide, moments, batch_atom) = swap_between_cores(near, ready, atom_devices)
        hot, grad_columns = atom_matrix(region, fn_atom, batch_atom, weight_grad, blocks, size, atom_total)
        ready = (basis_wide, field_wide, moments, hot, grad_columns)
        product, partial_grad = combine(region, ready, [own, *near, *far], shapes)
        gradient, contracted = sum_parts(partial_grad, write(pattern, product), slabs, atom_devices)
        return contracted.reshape(basis.shape), gradient
    ready = relayout(in_hbm(flat_basis), in_hbm(flat_field), points, blocks)
    near, far, (basis_wide, field_wide) = swap_between_cores(near, ready, atom_devices)
    tiles, partial_grad = partial_gradient(
        region,
        pattern,
        basis_wide,
        field_wide,
        in_hbm(flat_grad),
        weights,
        weight_grad,
        fn_atom,
        batch_atom,
        [own, *near, *far],
        shapes,
    )
    contracted = contract(region, pattern, basis_wide, tiles, points, blocks, width)
    gradient, contracted = sum_parts(partial_grad, contracted, slabs, atom_devices)
    return contracted.reshape(basis.shape), gradient


def solution(mesh):
    placed = (
        P(("groups", "grid", "atoms"), None, None, None),
        P(None, ("groups", "grid", "atoms"), None, None, None),
        P(("groups", "grid", "atoms"), None, None, None),
        P(("groups", "grid", "atoms"), None),
        P(None, ("groups", "grid", "atoms"), None),
        P(("groups", "grid"), None, None, None),
        P("groups", None),
        P(("groups", "grid", "atoms"), None),
        P("groups"),
        P(("groups", "grid", "atoms")),
    )
    return jax.shard_map(
        local,
        mesh=mesh,
        in_specs=placed,
        out_specs=(P(("groups", "grid", "atoms"), None, None, None), P(None, ("groups", "atoms"))),
        check_vma=False,
    )
```

```python
import functools
import math

import jax
import jax.numpy as jnp
from jax import lax
from jax.experimental import pallas as pl
from jax.experimental.pallas import tpu as pltpu
from jax.sharding import PartitionSpec as P

TRAVEL = 5
PARTS = 3
F32 = jnp.float32
BF16 = jnp.bfloat16
NT = (((1,), (1,)), ((), ()))
TN = (((0,), (0,)), ((), ()))
VMEM_LIMIT = 32 * 1024 * 1024


def owner_and_slot(region, slab, position, owner_rows):
    owner = lax.div(region[slab, position], owner_rows)
    slot = jnp.int32(0)
    count = jnp.int32(0)
    for other in range(region.shape[1]):
        same = jnp.where(lax.div(region[slab, other], owner_rows) == owner, 1, 0)
        count = count + same
        slot = slot + jnp.where(other < position, same, 0)
    return owner, slot, count


def travel_place(slot, count, k):
    if k == 0:
        return jnp.where(slot == 0, 4, 2)
    if k == 1:
        return jnp.where(slot == 0, 0, 3)
    return jnp.where(jnp.logical_and(slot == 0, count == 2), 1, 4)


def partners(slabs):
    return [(1, 1)] + [(shift + 1, shift) for shift in range(2, slabs, 2)]


def moves_over_grid(shifts, slabs, atom_devices):
    return [
        (z * atom_devices + a, (z ^ shifts[a % 2]) * atom_devices + a) for z in range(slabs) for a in range(atom_devices)
    ]


def send_kernel(region_hbm, density, *rest):
    *outs, region, held, region_sem, sems = rest
    fetch = pltpu.make_async_copy(region_hbm, region, region_sem)
    fetch.start()
    count_here = density.shape[0] // sems.shape[0]
    fetches = []
    for part in range(sems.shape[0]):
        here = pl.ds(part * count_here, count_here)
        fetches.append(pltpu.make_async_copy(density.at[here], held.at[here], sems.at[part]))
    for copy in fetches:
        copy.start()
    fetch.wait()
    me = lax.axis_index("grid")
    core = lax.rem(lax.axis_index("atoms"), 2)
    slabs, size = region.shape
    owner_rows = density.shape[0]
    picks = []
    for low, high in [(0, 0)] + partners(slabs):
        slab = jnp.bitwise_xor(me, jnp.where(core == 0, low, high))
        base = jnp.int32(owner_rows)
        count = jnp.int32(0)
        for position in range(size):
            row = region[slab, position] - me * owner_rows
            mine = jnp.logical_and(row >= 0, row < owner_rows)
            base = jnp.minimum(base, jnp.where(mine, row, owner_rows))
            count = count + jnp.where(mine, 1, 0)
        base = jnp.where(count == 0, 0, base)
        after = jnp.minimum(base + 1, owner_rows - 1)
        lower = base == 0
        edge = jnp.where(jnp.logical_and(count == 2, jnp.logical_not(lower)), after, base)
        picks.append(((base, 1), (base, 2), (after, 0), (after, 1), (edge, jnp.where(lower, 0, 2))))
    for copy in fetches:
        copy.wait()
    for out, places in zip(outs, picks):
        for place, (row, k) in enumerate(places):
            out[place] = held[row, k]


def in_hbm(array):
    return pltpu.with_memory_space_constraint(array, pltpu.HBM)


def rows_to_send(region, density, slabs):
    size = density.shape[-1]
    count = 1 + len(partners(slabs))
    hbm = pl.BlockSpec(memory_space=pl.ANY)
    return pl.pallas_call(
        send_kernel,
        out_shape=[jax.ShapeDtypeStruct((TRAVEL, size, size), density.dtype)] * count,
        in_specs=[hbm, hbm],
        out_specs=[pl.BlockSpec(memory_space=pltpu.VMEM)] * count,
        scratch_shapes=[
            pltpu.SMEM(region.shape, jnp.int32),
            pltpu.VMEM(density.shape, density.dtype),
            pltpu.SemaphoreType.DMA,
            pltpu.SemaphoreType.DMA((5 if density.shape[0] % 5 == 0 else 1,)),
        ],
        compiler_params=pltpu.CompilerParams(vmem_limit_bytes=VMEM_LIMIT),
    )(in_hbm(region), in_hbm(density))


def fetch_rows(region, density, slabs, atom_devices):
    own, *outgoing = rows_to_send(region, density, slabs)
    near = []
    for shifts, piece in zip(partners(slabs), outgoing):
        near.append(lax.ppermute(piece, ("grid", "atoms"), moves_over_grid(shifts, slabs, atom_devices)))
    return own, near


def stage_rows(stage, own, near, far, slabs):
    core = lax.rem(lax.axis_index("atoms"), 2)
    first, *pairs = partners(slabs)
    for place in range(TRAVEL):
        stage[place] = own[place]
        stage[first[0] * TRAVEL + place] = near[0][place]
    for (low, high), here, there in zip(pairs, near[1:], far):
        mine = jnp.where(core == 0, low, high) * TRAVEL
        other = jnp.where(core == 0, high, low) * TRAVEL
        for place in range(TRAVEL):
            stage[mine + place] = here[place]
            stage[other + place] = there[place]


def block_major(x_ref, wide, points, blocks):
    wide[...] = x_ref[0].astype(F32)
    return [wide[pl.ds(s, points, stride=blocks), :] for s in range(blocks)]


def relayout_kernel(basis, field, basis_out, field_out, wide, *, points, blocks):
    size = basis.shape[-1]
    for source, target in ((basis, basis_out), (field, field_out)):
        for s, part in enumerate(block_major(source, wide, points, blocks)):
            target[0, :, s * size : (s + 1) * size] = part.astype(BF16)


def relayout(basis, field, points, blocks):
    batches, rows, size = basis.shape
    here = pl.BlockSpec((1, rows, size), lambda b: (b, 0, 0))
    there = pl.BlockSpec((1, points, blocks * size), lambda b: (b, 0, 0))
    shape = jax.ShapeDtypeStruct((batches, points, blocks * size), BF16)
    return pl.pallas_call(
        functools.partial(relayout_kernel, points=points, blocks=blocks),
        grid=(batches,),
        out_shape=(shape, shape),
        in_specs=[here, here],
        out_specs=(there, there),
        scratch_shapes=[pltpu.VMEM((rows, size), F32)],
        compiler_params=pltpu.CompilerParams(vmem_limit_bytes=VMEM_LIMIT),
        cost_estimate=pl.CostEstimate(flops=0, bytes_accessed=8 * batches * rows * size, transcendentals=0),
    )(basis, field)


def batch_matrix(region, pattern, tiles, slab, batch, blocks, width):
    half = (width - 1) // 2
    none = tiles.shape[0] - 1
    places = [pattern[batch, s] for s in range(blocks)]
    rows = [region[slab, place] for place in places]
    strips = []
    for s in range(blocks):
        strip = []
        for t in range(blocks):
            k = rows[t] - rows[s] + half
            inside = jnp.logical_and(k >= 0, k < width)
            strip.append(tiles[jnp.where(inside, places[s] * width + k, none)])
        strips.append(jnp.concatenate(strip, axis=1))
    return jnp.concatenate(strips, axis=0)


def split(values):
    high = values.astype(BF16)
    rest = values - high.astype(F32)
    middle = rest.astype(BF16)
    low = (rest - middle.astype(F32)).astype(BF16)
    return high, middle, low


def gradient_kernel(
    region,
    pattern,
    basis,
    field,
    basis_grad,
    weights,
    weight_grad,
    fn_atom,
    batch_atom,
    places,
    *rest,
    points,
    blocks,
    width,
    owner_rows,
    slabs,
):
    *pieces, tiles, out, stage, spread, sums, energy_sums = rest
    batch = pl.program_id(0)
    batches = pl.num_programs(0)
    me = lax.axis_index("grid")
    me_atoms = lax.axis_index("atoms")
    size = tiles.shape[-1]
    region_size = region.shape[1]

    @pl.when(batch == 0)
    def _():
        tiles[region_size * width] = jnp.zeros((size, size), BF16)
        stage_rows(stage, pieces[0], pieces[1 : 1 + slabs // 2], pieces[1 + slabs // 2 :], slabs)
        for position in range(region_size):
            owner, slot, count = owner_and_slot(region, me, position, owner_rows)
            shift = jnp.bitwise_xor(me, owner)
            for k in range(width):
                tiles[position * width + k] = stage[shift * TRAVEL + travel_place(slot, count, k)]

    matrix = batch_matrix(region, pattern, tiles, me, batch, blocks, width)
    potential = lax.dot_general(field[0], matrix, NT, preferred_element_type=F32)
    rows = jnp.concatenate(
        [weights[pl.ds(batch, 1), :]]
        + [weight_grad[c, pl.ds(batch, 1), :] for c in range(PARTS)]
        + [jnp.zeros((8 - 1 - PARTS, points), F32)],
        axis=0,
    )
    columns = rows.T
    weight = columns[:, 0:1]
    energy = jnp.zeros((points, size), F32)
    for s in range(blocks):
        here = potential[:, s * size : (s + 1) * size]
        energy = energy + basis[0, :, s * size : (s + 1) * size].astype(F32) * here
        spread[pl.ds(s, points, stride=blocks), :] = here * weight
    scaled = spread[...]
    place = pl.ds(pl.multiple_of(batch * 8, 8), 8)
    for c in range(PARTS):
        terms = basis_grad[c, 0].astype(F32) * scaled
        sums[c, place, :] = jnp.sum(terms.reshape(-1, 8, size), axis=0)
        terms = energy * columns[:, 1 + c : 2 + c]
        energy_sums[c, place, :] = jnp.sum(terms.reshape(-1, 8, size), axis=0)

    @pl.when(batch == batches - 1)
    def _():
        padded = max(8, region_size)
        chosen = lax.broadcasted_iota(jnp.int32, (padded, places.shape[1]), 0) == places[...]
        chosen = chosen.astype(BF16)
        blocks_sum = []
        for c in range(PARTS):
            total = jnp.zeros((padded, size), F32)
            for piece in split(sums[c]):
                total = total + jnp.dot(chosen, piece, preferred_element_type=F32)
            blocks_sum.append(-2.0 * total)
        lefts = []
        for position in range(region_size):
            stack = jnp.concatenate([total[position : position + 1] for total in blocks_sum], axis=0)
            high, middle, low = (piece.astype(F32) for piece in split(stack))
            lefts.append(jnp.concatenate([high, middle, low, jnp.zeros((16 - 3 * PARTS, size), F32)], axis=0))
        left = jnp.concatenate(lefts, axis=1).astype(BF16)
        chunk = out.shape[-1]
        scale = [jnp.sum(energy_sums[c], axis=1, keepdims=True) for c in range(PARTS)]
        for device in range(out.shape[0]):
            atoms = lax.broadcasted_iota(jnp.int32, (chunk, size), 0) + device * chunk
            hot = [
                jnp.where(atoms == fn_atom[pl.ds(region[me, position], 1), :], 1.0, 0.0).astype(BF16)
                for position in range(region_size)
            ]
            found = lax.dot_general(left, jnp.concatenate(hot, axis=1), NT, preferred_element_type=F32)
            atoms = lax.broadcasted_iota(jnp.int32, (batch_atom.shape[0], chunk), 1) + device * chunk
            mine = atoms == batch_atom[...]
            for c in range(PARTS):
                value = found[c : c + 1] + found[PARTS + c : PARTS + c + 1] + found[2 * PARTS + c : 2 * PARTS + c + 1]
                value = value + jnp.sum(jnp.where(mine, scale[c], 0.0), axis=0, keepdims=True)
                place = jnp.bitwise_xor(me_atoms, device)
                out[place, 0, c : c + 1, :] = value
                out[jnp.bitwise_xor(place, 1), 1, c : c + 1, :] = value


def partial_gradient(
    region, pattern, basis, field, basis_grad, weights, weight_grad, fn_atom, batch_atom, pieces, shapes
):
    slabs, atom_devices, atom_total, points, blocks, width, owner_rows = shapes
    batches, _, columns = basis.shape
    size = columns // blocks
    region_size = region.shape[1]
    fn_atom = fn_atom.reshape(-1, size)
    places = jnp.broadcast_to(pattern[:, None, :], (batches, 8 // blocks, blocks)).reshape(1, -1)
    batch_atom = jnp.broadcast_to(batch_atom[:, None], (batches, 8)).reshape(-1, 1)
    block = pl.BlockSpec((1, points, columns), lambda b, *_: (b, 0, 0))
    whole = pl.BlockSpec(memory_space=pltpu.VMEM)
    tile_shape = (region_size * width + 1, size, size)
    out_shape = (atom_devices, 2, PARTS, atom_total // atom_devices)
    return pl.pallas_call(
        functools.partial(
            gradient_kernel, points=points, blocks=blocks, width=width, owner_rows=owner_rows, slabs=slabs
        ),
        grid_spec=pltpu.PrefetchScalarGridSpec(
            num_scalar_prefetch=2,
            grid=(batches,),
            in_specs=[
                block,
                block,
                pl.BlockSpec((PARTS, 1, points * blocks, size), lambda b, *_: (0, b, 0, 0)),
            ]
            + [whole] * (5 + len(pieces)),
            out_specs=(whole, whole),
            scratch_shapes=[
                pltpu.VMEM((slabs * TRAVEL, size, size), BF16),
                pltpu.VMEM((points * blocks, size), F32),
                pltpu.VMEM((PARTS, batches * 8, size), F32),
                pltpu.VMEM((PARTS, batches * 8, size), F32),
            ],
        ),
        out_shape=(jax.ShapeDtypeStruct(tile_shape, BF16), jax.ShapeDtypeStruct(out_shape, F32)),
        compiler_params=pltpu.CompilerParams(vmem_limit_bytes=VMEM_LIMIT),
    )(region, pattern, basis, field, basis_grad, weights, weight_grad, fn_atom, batch_atom, places, *pieces)


def product_kernel(region, pattern, basis, tiles, out, spread, *, points, blocks, width):
    me = lax.axis_index("grid")
    size = tiles.shape[-1]
    matrix = batch_matrix(region, pattern, tiles, me, pl.program_id(0), blocks, width)
    product = jnp.dot(basis[0], matrix, preferred_element_type=F32)
    for t in range(blocks):
        spread[pl.ds(t, points, stride=blocks), :] = product[:, t * size : (t + 1) * size]
    out[0] = spread[...].astype(BF16)


def contract(region, pattern, basis, tiles, points, blocks, width):
    batches, _, columns = basis.shape
    size = columns // blocks
    return pl.pallas_call(
        functools.partial(product_kernel, points=points, blocks=blocks, width=width),
        grid_spec=pltpu.PrefetchScalarGridSpec(
            num_scalar_prefetch=2,
            grid=(batches,),
            in_specs=[
                pl.BlockSpec((1, points, columns), lambda b, *_: (b, 0, 0)),
                pl.BlockSpec(memory_space=pltpu.VMEM),
            ],
            out_specs=pl.BlockSpec((1, points * blocks, size), lambda b, *_: (b, 0, 0)),
            scratch_shapes=[pltpu.VMEM((points * blocks, size), F32)],
        ),
        out_shape=jax.ShapeDtypeStruct((batches, points * blocks, size), BF16),
        compiler_params=pltpu.CompilerParams(vmem_limit_bytes=VMEM_LIMIT),
        cost_estimate=pl.CostEstimate(
            flops=2 * batches * points * columns * columns,
            bytes_accessed=4 * batches * points * columns,
            transcendentals=0,
        ),
    )(region, pattern, basis, tiles)


def reorder_kernel(
    pattern_hbm,
    basis,
    field,
    basis_grad,
    weights_hbm,
    basis_out,
    field_out,
    weighted,
    grads,
    pattern,
    weights,
    columns,
    basis_in,
    field_in,
    grad_in,
    wide,
    sems,
    small_sems,
):
    batches, blocks, points, size = basis_out.shape

    def copies(batch):
        return (
            pltpu.make_async_copy(field.at[batch], field_in.at[batch], sems.at[batch, 0]),
            pltpu.make_async_copy(basis.at[batch], basis_in.at[batch], sems.at[batch, 1]),
            *(
                pltpu.make_async_copy(basis_grad.at[c, batch], grad_in.at[c, batch], sems.at[batch, 2 + c])
                for c in range(PARTS)
            ),
        )

    small = (
        pltpu.make_async_copy(pattern_hbm, pattern, small_sems.at[0]),
        pltpu.make_async_copy(weights_hbm, weights, small_sems.at[1]),
    )
    for copy in small:
        copy.start()

    @pl.loop(0, batches)
    def _(batch):
        for copy in copies(batch):
            copy.start()

    for copy in small:
        copy.wait()
    rows = jnp.concatenate([weights[...], jnp.zeros((size - batches, points), F32)], axis=0).T
    for batch in range(batches):
        columns[batch] = jnp.broadcast_to(rows[:, batch : batch + 1], (points, size))

    @pl.loop(0, batches)
    def _(batch):
        for copy in copies(batch):
            copy.wait()
        points_here = pl.ds(pl.multiple_of(batch * points, points), points)
        places = [pattern[s, batch] for s in range(blocks)]
        wide[0] = field_in[batch].astype(F32)
        wide[1] = basis_in[batch].astype(F32)
        for c in range(PARTS):
            wide[2 + c] = grad_in[c, batch].astype(F32)
        for s, place in enumerate(places):
            strided = pl.ds(s, points, stride=blocks)
            values = wide[0, strided, :]
            field_out[batch, place] = values.astype(BF16)
            weighted[place, points_here, :] = (values * columns[batch]).astype(BF16)
            basis_out[batch, place] = wide[1, strided, :].astype(BF16)
            for c in range(PARTS):
                grads[c, place, points_here, :] = wide[2 + c, strided, :].astype(BF16)


def reorder(pattern, basis, field, basis_grad, weights, points, blocks):
    batches, rows, size = basis.shape
    hbm = pl.BlockSpec(memory_space=pl.ANY)
    vmem = pl.BlockSpec(memory_space=pltpu.VMEM)
    ordered = jax.ShapeDtypeStruct((batches, blocks, points, size), BF16)
    return pl.pallas_call(
        reorder_kernel,
        out_shape=(
            ordered,
            ordered,
            jax.ShapeDtypeStruct((blocks, batches * points, size), BF16),
            jax.ShapeDtypeStruct((PARTS, blocks, batches * points, size), BF16),
        ),
        in_specs=[hbm] * 5,
        out_specs=(vmem,) * 4,
        scratch_shapes=[
            pltpu.SMEM((blocks, batches), jnp.int32),
            pltpu.VMEM(weights.shape, F32),
            pltpu.VMEM((batches, points, size), F32),
            pltpu.VMEM((batches, rows, size), BF16),
            pltpu.VMEM((batches, rows, size), BF16),
            pltpu.VMEM((PARTS, batches, rows, size), BF16),
            pltpu.VMEM((2 + PARTS, rows, size), F32),
            pltpu.SemaphoreType.DMA((batches, 2 + PARTS)),
            pltpu.SemaphoreType.DMA((2,)),
        ],
        compiler_params=pltpu.CompilerParams(vmem_limit_bytes=VMEM_LIMIT),
        cost_estimate=pl.CostEstimate(
            flops=0, bytes_accessed=2 * (2 + PARTS) * batches * rows * size, transcendentals=0
        ),
    )(in_hbm(pattern.T), in_hbm(basis), in_hbm(field), in_hbm(basis_grad), in_hbm(weights))


def moment_kernel(weighted, grads, moments):
    blocks, _, size = grads.shape[1:]
    for p in range(0, blocks, 2):
        first, last = max(p - 1, 0), min(p + 3, blocks)
        left = jnp.concatenate([weighted[place] for place in range(first, last)], axis=1)
        for c in range(PARTS):
            right = jnp.concatenate([grads[c, p], grads[c, p + 1]], axis=1)
            moments[c, first * size : last * size, p * size : (p + 2) * size] = lax.dot_general(
                left, right, TN, preferred_element_type=F32
            )


def build_moments(weighted, grads):
    blocks, depth, size = grads.shape[1:]
    vmem = pl.BlockSpec(memory_space=pltpu.VMEM)
    return pl.pallas_call(
        moment_kernel,
        out_shape=jax.ShapeDtypeStruct((PARTS, blocks * size, blocks * size), F32),
        in_specs=[vmem, vmem],
        out_specs=vmem,
        compiler_params=pltpu.CompilerParams(vmem_limit_bytes=VMEM_LIMIT),
        cost_estimate=pl.CostEstimate(
            flops=2 * PARTS * depth * (blocks * size) ** 2, bytes_accessed=0, transcendentals=0
        ),
    )(weighted, grads)


def atom_kernel(region, fn_atom, batch_atom, weight_grad, hot, grad_columns):
    batches, points = weight_grad.shape[1:]
    size = fn_atom.shape[1]
    blocks = region.shape[1]
    me = lax.axis_index("grid")
    atoms = lax.broadcasted_iota(jnp.int32, (hot.shape[0], size), 0)
    ids = jnp.concatenate([batch_atom[...], jnp.full((1, size - batches), -1, jnp.int32)], axis=1)
    hot[:, blocks * size :] = jnp.where(atoms == ids, 1.0, 0.0).astype(BF16)

    @pl.loop(0, blocks)
    def _(position):
        ids = fn_atom[pl.ds(region[me, position], 1), :]
        columns = pl.ds(pl.multiple_of(position * size, size), size)
        hot[:, columns] = jnp.where(atoms == ids, 1.0, 0.0).astype(BF16)

    for c in range(PARTS):
        padding = jnp.zeros((size - batches, points), F32)
        grad_columns[c] = jnp.concatenate([weight_grad[c], padding], axis=0).T


def atom_matrix(region, fn_atom, batch_atom, weight_grad, blocks, size, atom_total):
    vmem = pl.BlockSpec(memory_space=pltpu.VMEM)
    return pl.pallas_call(
        atom_kernel,
        out_shape=(
            jax.ShapeDtypeStruct((atom_total, (blocks + 1) * size), BF16),
            jax.ShapeDtypeStruct((PARTS, weight_grad.shape[2], size), F32),
        ),
        in_specs=[pl.BlockSpec(memory_space=pltpu.SMEM)] + [vmem] * 3,
        out_specs=(vmem, vmem),
        compiler_params=pltpu.CompilerParams(vmem_limit_bytes=VMEM_LIMIT),
        cost_estimate=pl.CostEstimate(flops=1000000000, bytes_accessed=2 * atom_total * size, transcendentals=0),
    )(region, fn_atom.reshape(-1, size), batch_atom.reshape(1, -1), weight_grad)


def combine_kernel(
    region, basis, field, moments, hot, grad_columns, *rest, owner_rows, slabs, width
):
    *pieces, product_out, out, stage, matrix = rest
    batches, blocks, points, size = basis.shape
    me = lax.axis_index("grid")
    me_atoms = lax.axis_index("atoms")
    half = (width - 1) // 2
    stage_rows(stage, pieces[0], pieces[1 : 1 + slabs // 2], pieces[1 + slabs // 2 :], slabs)
    rows = [region[me, position] for position in range(blocks)]
    found = [owner_and_slot(region, me, position, owner_rows) for position in range(blocks)]
    totals = [[jnp.zeros((8, size), F32) for _ in range(blocks)] for _ in range(PARTS)]
    for p in range(blocks):
        owner, slot, count = found[p]
        first = jnp.bitwise_xor(me, owner) * TRAVEL
        for q in range(blocks):
            if abs(q - p) > half:
                matrix[p * size : (p + 1) * size, q * size : (q + 1) * size] = jnp.zeros((size, size), BF16)
                continue
            k = rows[q] - rows[p] + half
            place = jnp.where(
                k == 0,
                travel_place(slot, count, 0),
                jnp.where(k == 1, travel_place(slot, count, 1), travel_place(slot, count, 2)),
            )
            inside = jnp.logical_and(k >= 0, k < width)
            tile = jnp.where(inside, stage[first + place], jnp.zeros((size, size), BF16))
            matrix[p * size : (p + 1) * size, q * size : (q + 1) * size] = tile
            turned = tile.T.astype(F32)
            for c in range(PARTS):
                terms = turned * moments[c, q * size : (q + 1) * size, p * size : (p + 1) * size]
                totals[c][p] = totals[c][p] + jnp.sum(terms.reshape(-1, 8, size), axis=0)
    derivative = [
        jnp.concatenate([jnp.sum(total, axis=0, keepdims=True) for total in totals[c]], axis=1) for c in range(PARTS)
    ]

    energies = jnp.zeros((points, size), F32)
    lanes = lax.broadcasted_iota(jnp.int32, (points, size), 1)
    left = [jnp.concatenate([basis[batch, p] for p in range(blocks)], axis=1) for batch in range(batches)]
    left = jnp.concatenate(left, axis=0)
    energy = [jnp.zeros((points, size), F32) for _ in range(batches)]
    for q in range(0, blocks, 2):
        product = jnp.dot(left, matrix[:, q * size : (q + 2) * size], preferred_element_type=F32)
        for batch in range(batches):
            for column in range(2):
                part = product[batch * points : (batch + 1) * points, column * size : (column + 1) * size]
                product_out[batch, q + column] = part.astype(BF16)
                energy[batch] = energy[batch] + part * field[batch, q + column].astype(F32)
    for batch in range(batches):
        energies = jnp.where(lanes == batch, jnp.sum(energy[batch], axis=1, keepdims=True), energies)

    lefts = []
    for c in range(PARTS):
        term = jnp.sum(energies * grad_columns[c], axis=0, keepdims=True)
        lefts.append(jnp.concatenate([-2.0 * derivative[c], term], axis=1))
    left = jnp.concatenate(lefts, axis=0)
    high, middle, low = (piece.astype(F32) for piece in split(left))
    left = jnp.concatenate([high, middle, low, jnp.zeros((16 - 3 * PARTS, left.shape[1]), F32)], axis=0).astype(BF16)
    chunk = out.shape[-1]
    for device in range(out.shape[0]):
        sums = lax.dot_general(
            left, hot[device * chunk : (device + 1) * chunk, :], NT, preferred_element_type=F32
        )
        value = sums[:PARTS] + sums[PARTS : 2 * PARTS] + sums[2 * PARTS : 3 * PARTS]
        place = jnp.bitwise_xor(me_atoms, device)
        out[place, 0] = value
        out[jnp.bitwise_xor(place, 1), 1] = value


def combine(region, prepared, pieces, shapes):
    basis, field, moments, hot, grad_columns = prepared
    slabs, atom_devices, atom_total, points, blocks, width, owner_rows = shapes
    batches, _, _, size = basis.shape
    vmem = pl.BlockSpec(memory_space=pltpu.VMEM)
    return pl.pallas_call(
        functools.partial(combine_kernel, owner_rows=owner_rows, slabs=slabs, width=width),
        out_shape=(
            jax.ShapeDtypeStruct(basis.shape, BF16),
            jax.ShapeDtypeStruct((atom_devices, 2, PARTS, atom_total // atom_devices), F32),
        ),
        in_specs=[pl.BlockSpec(memory_space=pltpu.SMEM)] + [vmem] * (5 + len(pieces)),
        out_specs=(vmem, vmem),
        scratch_shapes=[
            pltpu.VMEM((slabs * TRAVEL, size, size), BF16),
            pltpu.VMEM((blocks * size, blocks * size), BF16),
        ],
        compiler_params=pltpu.CompilerParams(vmem_limit_bytes=VMEM_LIMIT),
    )(region, basis, field, moments, hot, grad_columns, *pieces)


def write_kernel(pattern, product, out, wide, staged, sems):
    batches, blocks, points, size = product.shape

    def copy(batch):
        return pltpu.make_async_copy(staged.at[batch], out.at[batch], sems.at[batch])

    @pl.loop(0, batches // 2)
    def _(pair):
        for inner in range(2):
            batch = pair * 2 + inner
            for t in range(blocks):
                wide[inner, pl.ds(t, points, stride=blocks), :] = product[batch, pattern[t, batch]].astype(F32)
            staged[batch] = wide[inner].astype(BF16)
            copy(batch).start()

    @pl.loop(0, batches)
    def _(batch):
        copy(batch).wait()


def write(pattern, product):
    batches, blocks, points, size = product.shape
    shape = (batches, points * blocks, size)
    return pl.pallas_call(
        write_kernel,
        out_shape=jax.ShapeDtypeStruct(shape, BF16),
        in_specs=[pl.BlockSpec(memory_space=pltpu.SMEM), pl.BlockSpec(memory_space=pltpu.VMEM)],
        out_specs=pl.BlockSpec(memory_space=pl.ANY),
        scratch_shapes=[
            pltpu.VMEM((2, points * blocks, size), F32),
            pltpu.VMEM(shape, BF16),
            pltpu.SemaphoreType.DMA((batches,)),
        ],
        compiler_params=pltpu.CompilerParams(vmem_limit_bytes=VMEM_LIMIT),
        cost_estimate=pl.CostEstimate(flops=0, bytes_accessed=4 * math.prod(shape), transcendentals=0),
    )(pattern.T, product)


def swap_between_cores(near, ready, atom_devices):
    near, ready = lax.optimization_barrier((near, ready))
    swap = [(i, i ^ 1) for i in range(atom_devices)]
    return near, [lax.ppermute(piece, "atoms", swap) for piece in near[1:]], ready


def tree_sum(values):
    if len(values) == 1:
        return values[0]
    half = len(values) // 2
    return tree_sum(values[:half]) + tree_sum(values[half:])


def pair_sums(values):
    return [values[i] + values[i + 1] for i in range(0, len(values), 2)]


def sum_parts(partial_grad, contracted, slabs, atom_devices):
    parts = [partial_grad[0]]
    for d in range(1, atom_devices):
        parts.append(lax.ppermute(partial_grad[d], "atoms", [(i, i ^ d) for i in range(atom_devices)]))
    parts, contracted = lax.optimization_barrier((parts, contracted))
    both = tree_sum(pair_sums(parts))
    swap = [(i, i ^ 1) for i in range(atom_devices)]
    far = []
    for shifts in partners(slabs)[1:]:
        far.append(lax.ppermute(both, ("grid", "atoms"), moves_over_grid(shifts, slabs, atom_devices)))
    near = lax.ppermute(both[0], "grid", [(i, i ^ 1) for i in range(slabs)])
    far = lax.optimization_barrier(far)
    swapped = [lax.ppermute(piece[1], "atoms", swap) for piece in far]
    sums = [both[0] + near] + [piece[0] + other for piece, other in zip(far, swapped)]
    return tree_sum(sums), contracted


def local(
    basis,
    basis_grad,
    exchange_field,
    weights,
    weight_grad,
    density,
    region,
    pattern,
    fn_atom,
    batch_atom,
):
    batches, points, blocks, size = basis.shape
    owner_rows, width = density.shape[:2]
    slabs = lax.axis_size("grid")
    atom_devices = lax.axis_size("atoms")
    atom_total = fn_atom.shape[0] // (10 * slabs * atom_devices) * slabs * atom_devices
    shapes = (slabs, atom_devices, atom_total, points, blocks, width, owner_rows)
    flat_basis = basis.reshape(batches, points * blocks, size)
    flat_field = exchange_field.reshape(batches, points * blocks, size)
    flat_grad = basis_grad.reshape(PARTS, batches, points * blocks, size)
    own, near = fetch_rows(region, density, slabs, atom_devices)
    if region.shape[1] == blocks:
        basis_wide, field_wide, weighted, grads = reorder(
            pattern, flat_basis, flat_field, flat_grad, weights, points, blocks
        )
        ready = (basis_wide, field_wide, build_moments(weighted, grads), batch_atom)
        near, far, (basis_wide, field_wide, moments, batch_atom) = swap_between_cores(near, ready, atom_devices)
        hot, grad_columns = atom_matrix(region, fn_atom, batch_atom, weight_grad, blocks, size, atom_total)
        ready = (basis_wide, field_wide, moments, hot, grad_columns)
        product, partial_grad = combine(region, ready, [own, *near, *far], shapes)
        gradient, contracted = sum_parts(partial_grad, write(pattern, product), slabs, atom_devices)
        return contracted.reshape(basis.shape), gradient
    ready = relayout(in_hbm(flat_basis), in_hbm(flat_field), points, blocks)
    near, far, (basis_wide, field_wide) = swap_between_cores(near, ready, atom_devices)
    tiles, partial_grad = partial_gradient(
        region,
        pattern,
        basis_wide,
        field_wide,
        in_hbm(flat_grad),
        weights,
        weight_grad,
        fn_atom,
        batch_atom,
        [own, *near, *far],
        shapes,
    )
    contracted = contract(region, pattern, basis_wide, tiles, points, blocks, width)
    gradient, contracted = sum_parts(partial_grad, contracted, slabs, atom_devices)
    return contracted.reshape(basis.shape), gradient


def solution(mesh):
    placed = (
        P(("groups", "grid", "atoms"), None, None, None),
        P(None, ("groups", "grid", "atoms"), None, None, None),
        P(("groups", "grid", "atoms"), None, None, None),
        P(("groups", "grid", "atoms"), None),
        P(None, ("groups", "grid", "atoms"), None),
        P(("groups", "grid"), None, None, None),
        P("groups", None),
        P(("groups", "grid", "atoms"), None),
        P("groups"),
        P(("groups", "grid", "atoms")),
    )
    return jax.shard_map(
        local,
        mesh=mesh,
        in_specs=placed,
        out_specs=(P(("groups", "grid", "atoms"), None, None, None), P(None, ("groups", "atoms"))),
        check_vma=False,
    )
```

```python
import functools
import math

import jax
import jax.numpy as jnp
from jax import lax
from jax.experimental import pallas as pl
from jax.experimental.pallas import tpu as pltpu
from jax.sharding import PartitionSpec as P

TRAVEL = 5
PARTS = 3
F32 = jnp.float32
BF16 = jnp.bfloat16
NT = (((1,), (1,)), ((), ()))
TN = (((0,), (0,)), ((), ()))
VMEM_LIMIT = 32 * 1024 * 1024


def owner_and_slot(region, slab, position, owner_rows):
    owner = lax.div(region[slab, position], owner_rows)
    slot = jnp.int32(0)
    count = jnp.int32(0)
    for other in range(region.shape[1]):
        same = jnp.where(lax.div(region[slab, other], owner_rows) == owner, 1, 0)
        count = count + same
        slot = slot + jnp.where(other < position, same, 0)
    return owner, slot, count


def travel_place(slot, count, k):
    if k == 0:
        return jnp.where(slot == 0, 4, 2)
    if k == 1:
        return jnp.where(slot == 0, 0, 3)
    return jnp.where(jnp.logical_and(slot == 0, count == 2), 1, 4)


def partners(slabs):
    return [(1, 1)] + [(shift + 1, shift) for shift in range(2, slabs, 2)]


def moves_over_grid(shifts, slabs, atom_devices):
    return [
        (z * atom_devices + a, (z ^ shifts[a % 2]) * atom_devices + a) for z in range(slabs) for a in range(atom_devices)
    ]


def send_kernel(region_hbm, density, *rest):
    *outs, region, held, region_sem, sems = rest
    fetch = pltpu.make_async_copy(region_hbm, region, region_sem)
    fetch.start()
    count_here = density.shape[0] // sems.shape[0]
    fetches = []
    for part in range(sems.shape[0]):
        here = pl.ds(part * count_here, count_here)
        fetches.append(pltpu.make_async_copy(density.at[here], held.at[here], sems.at[part]))
    for copy in fetches:
        copy.start()
    fetch.wait()
    me = lax.axis_index("grid")
    core = lax.rem(lax.axis_index("atoms"), 2)
    slabs, size = region.shape
    owner_rows = density.shape[0]
    picks = []
    for low, high in [(0, 0)] + partners(slabs):
        slab = jnp.bitwise_xor(me, jnp.where(core == 0, low, high))
        base = jnp.int32(owner_rows)
        count = jnp.int32(0)
        for position in range(size):
            row = region[slab, position] - me * owner_rows
            mine = jnp.logical_and(row >= 0, row < owner_rows)
            base = jnp.minimum(base, jnp.where(mine, row, owner_rows))
            count = count + jnp.where(mine, 1, 0)
        base = jnp.where(count == 0, 0, base)
        after = jnp.minimum(base + 1, owner_rows - 1)
        lower = base == 0
        edge = jnp.where(jnp.logical_and(count == 2, jnp.logical_not(lower)), after, base)
        picks.append(((base, 1), (base, 2), (after, 0), (after, 1), (edge, jnp.where(lower, 0, 2))))
    for copy in fetches:
        copy.wait()
    for out, places in zip(outs, picks):
        for place, (row, k) in enumerate(places):
            out[place] = held[row, k]


def in_hbm(array):
    return pltpu.with_memory_space_constraint(array, pltpu.HBM)


def rows_to_send(region, density, slabs):
    size = density.shape[-1]
    count = 1 + len(partners(slabs))
    hbm = pl.BlockSpec(memory_space=pl.ANY)
    return pl.pallas_call(
        send_kernel,
        out_shape=[jax.ShapeDtypeStruct((TRAVEL, size, size), density.dtype)] * count,
        in_specs=[hbm, hbm],
        out_specs=[pl.BlockSpec(memory_space=pltpu.VMEM)] * count,
        scratch_shapes=[
            pltpu.SMEM(region.shape, jnp.int32),
            pltpu.VMEM(density.shape, density.dtype),
            pltpu.SemaphoreType.DMA,
            pltpu.SemaphoreType.DMA((5 if density.shape[0] % 5 == 0 else 1,)),
        ],
        compiler_params=pltpu.CompilerParams(vmem_limit_bytes=VMEM_LIMIT),
    )(in_hbm(region), in_hbm(density))


def fetch_rows(region, density, slabs, atom_devices):
    own, *outgoing = rows_to_send(region, density, slabs)
    near = []
    for shifts, piece in zip(partners(slabs), outgoing):
        near.append(lax.ppermute(piece, ("grid", "atoms"), moves_over_grid(shifts, slabs, atom_devices)))
    return own, near


def stage_rows(stage, own, near, far, slabs):
    core = lax.rem(lax.axis_index("atoms"), 2)
    first, *pairs = partners(slabs)
    for place in range(TRAVEL):
        stage[place] = own[place]
        stage[first[0] * TRAVEL + place] = near[0][place]
    for (low, high), here, there in zip(pairs, near[1:], far):
        mine = jnp.where(core == 0, low, high) * TRAVEL
        other = jnp.where(core == 0, high, low) * TRAVEL
        for place in range(TRAVEL):
            stage[mine + place] = here[place]
            stage[other + place] = there[place]


def block_major(x_ref, wide, points, blocks):
    wide[...] = x_ref[0].astype(F32)
    return [wide[pl.ds(s, points, stride=blocks), :] for s in range(blocks)]


def relayout_kernel(basis, field, basis_out, field_out, wide, *, points, blocks):
    size = basis.shape[-1]
    for source, target in ((basis, basis_out), (field, field_out)):
        for s, part in enumerate(block_major(source, wide, points, blocks)):
            target[0, :, s * size : (s + 1) * size] = part.astype(BF16)


def relayout(basis, field, points, blocks):
    batches, rows, size = basis.shape
    here = pl.BlockSpec((1, rows, size), lambda b: (b, 0, 0))
    there = pl.BlockSpec((1, points, blocks * size), lambda b: (b, 0, 0))
    shape = jax.ShapeDtypeStruct((batches, points, blocks * size), BF16)
    return pl.pallas_call(
        functools.partial(relayout_kernel, points=points, blocks=blocks),
        grid=(batches,),
        out_shape=(shape, shape),
        in_specs=[here, here],
        out_specs=(there, there),
        scratch_shapes=[pltpu.VMEM((rows, size), F32)],
        compiler_params=pltpu.CompilerParams(vmem_limit_bytes=VMEM_LIMIT),
        cost_estimate=pl.CostEstimate(flops=0, bytes_accessed=8 * batches * rows * size, transcendentals=0),
    )(basis, field)


def batch_matrix(region, pattern, tiles, slab, batch, blocks, width):
    half = (width - 1) // 2
    none = tiles.shape[0] - 1
    places = [pattern[batch, s] for s in range(blocks)]
    rows = [region[slab, place] for place in places]
    strips = []
    for s in range(blocks):
        strip = []
        for t in range(blocks):
            k = rows[t] - rows[s] + half
            inside = jnp.logical_and(k >= 0, k < width)
            strip.append(tiles[jnp.where(inside, places[s] * width + k, none)])
        strips.append(jnp.concatenate(strip, axis=1))
    return jnp.concatenate(strips, axis=0)


def split(values):
    high = values.astype(BF16)
    rest = values - high.astype(F32)
    middle = rest.astype(BF16)
    low = (rest - middle.astype(F32)).astype(BF16)
    return high, middle, low


def gradient_kernel(
    region,
    pattern,
    basis,
    field,
    basis_grad,
    weights,
    weight_grad,
    fn_atom,
    batch_atom,
    places,
    *rest,
    points,
    blocks,
    width,
    owner_rows,
    slabs,
):
    *pieces, tiles, out, stage, spread, sums, energy_sums = rest
    batch = pl.program_id(0)
    batches = pl.num_programs(0)
    me = lax.axis_index("grid")
    me_atoms = lax.axis_index("atoms")
    size = tiles.shape[-1]
    region_size = region.shape[1]

    @pl.when(batch == 0)
    def _():
        tiles[region_size * width] = jnp.zeros((size, size), BF16)
        stage_rows(stage, pieces[0], pieces[1 : 1 + slabs // 2], pieces[1 + slabs // 2 :], slabs)
        for position in range(region_size):
            owner, slot, count = owner_and_slot(region, me, position, owner_rows)
            shift = jnp.bitwise_xor(me, owner)
            for k in range(width):
                tiles[position * width + k] = stage[shift * TRAVEL + travel_place(slot, count, k)]

    matrix = batch_matrix(region, pattern, tiles, me, batch, blocks, width)
    potential = lax.dot_general(field[0], matrix, NT, preferred_element_type=F32)
    rows = jnp.concatenate(
        [weights[pl.ds(batch, 1), :]]
        + [weight_grad[c, pl.ds(batch, 1), :] for c in range(PARTS)]
        + [jnp.zeros((8 - 1 - PARTS, points), F32)],
        axis=0,
    )
    columns = rows.T
    weight = columns[:, 0:1]
    energy = jnp.zeros((points, size), F32)
    for s in range(blocks):
        here = potential[:, s * size : (s + 1) * size]
        energy = energy + basis[0, :, s * size : (s + 1) * size].astype(F32) * here
        spread[pl.ds(s, points, stride=blocks), :] = here * weight
    scaled = spread[...]
    place = pl.ds(pl.multiple_of(batch * 8, 8), 8)
    for c in range(PARTS):
        terms = basis_grad[c, 0].astype(F32) * scaled
        sums[c, place, :] = jnp.sum(terms.reshape(-1, 8, size), axis=0)
        terms = energy * columns[:, 1 + c : 2 + c]
        energy_sums[c, place, :] = jnp.sum(terms.reshape(-1, 8, size), axis=0)

    @pl.when(batch == batches - 1)
    def _():
        padded = max(8, region_size)
        chosen = lax.broadcasted_iota(jnp.int32, (padded, places.shape[1]), 0) == places[...]
        chosen = chosen.astype(BF16)
        blocks_sum = []
        for c in range(PARTS):
            total = jnp.zeros((padded, size), F32)
            for piece in split(sums[c]):
                total = total + jnp.dot(chosen, piece, preferred_element_type=F32)
            blocks_sum.append(-2.0 * total)
        lefts = []
        for position in range(region_size):
            stack = jnp.concatenate([total[position : position + 1] for total in blocks_sum], axis=0)
            high, middle, low = (piece.astype(F32) for piece in split(stack))
            lefts.append(jnp.concatenate([high, middle, low, jnp.zeros((16 - 3 * PARTS, size), F32)], axis=0))
        left = jnp.concatenate(lefts, axis=1).astype(BF16)
        chunk = out.shape[-1]
        scale = [jnp.sum(energy_sums[c], axis=1, keepdims=True) for c in range(PARTS)]
        for device in range(out.shape[0]):
            atoms = lax.broadcasted_iota(jnp.int32, (chunk, size), 0) + device * chunk
            hot = [
                jnp.where(atoms == fn_atom[pl.ds(region[me, position], 1), :], 1.0, 0.0).astype(BF16)
                for position in range(region_size)
            ]
            found = lax.dot_general(left, jnp.concatenate(hot, axis=1), NT, preferred_element_type=F32)
            atoms = lax.broadcasted_iota(jnp.int32, (batch_atom.shape[0], chunk), 1) + device * chunk
            mine = atoms == batch_atom[...]
            for c in range(PARTS):
                value = found[c : c + 1] + found[PARTS + c : PARTS + c + 1] + found[2 * PARTS + c : 2 * PARTS + c + 1]
                value = value + jnp.sum(jnp.where(mine, scale[c], 0.0), axis=0, keepdims=True)
                place = jnp.bitwise_xor(me_atoms, device)
                out[place, 0, c : c + 1, :] = value
                out[jnp.bitwise_xor(place, 1), 1, c : c + 1, :] = value


def partial_gradient(
    region, pattern, basis, field, basis_grad, weights, weight_grad, fn_atom, batch_atom, pieces, shapes
):
    slabs, atom_devices, atom_total, points, blocks, width, owner_rows = shapes
    batches, _, columns = basis.shape
    size = columns // blocks
    region_size = region.shape[1]
    fn_atom = fn_atom.reshape(-1, size)
    places = jnp.broadcast_to(pattern[:, None, :], (batches, 8 // blocks, blocks)).reshape(1, -1)
    batch_atom = jnp.broadcast_to(batch_atom[:, None], (batches, 8)).reshape(-1, 1)
    block = pl.BlockSpec((1, points, columns), lambda b, *_: (b, 0, 0))
    whole = pl.BlockSpec(memory_space=pltpu.VMEM)
    tile_shape = (region_size * width + 1, size, size)
    out_shape = (atom_devices, 2, PARTS, atom_total // atom_devices)
    return pl.pallas_call(
        functools.partial(
            gradient_kernel, points=points, blocks=blocks, width=width, owner_rows=owner_rows, slabs=slabs
        ),
        grid_spec=pltpu.PrefetchScalarGridSpec(
            num_scalar_prefetch=2,
            grid=(batches,),
            in_specs=[
                block,
                block,
                pl.BlockSpec((PARTS, 1, points * blocks, size), lambda b, *_: (0, b, 0, 0)),
            ]
            + [whole] * (5 + len(pieces)),
            out_specs=(whole, whole),
            scratch_shapes=[
                pltpu.VMEM((slabs * TRAVEL, size, size), BF16),
                pltpu.VMEM((points * blocks, size), F32),
                pltpu.VMEM((PARTS, batches * 8, size), F32),
                pltpu.VMEM((PARTS, batches * 8, size), F32),
            ],
        ),
        out_shape=(jax.ShapeDtypeStruct(tile_shape, BF16), jax.ShapeDtypeStruct(out_shape, F32)),
        compiler_params=pltpu.CompilerParams(vmem_limit_bytes=VMEM_LIMIT),
    )(region, pattern, basis, field, basis_grad, weights, weight_grad, fn_atom, batch_atom, places, *pieces)


def product_kernel(region, pattern, basis, tiles, out, spread, *, points, blocks, width):
    me = lax.axis_index("grid")
    size = tiles.shape[-1]
    matrix = batch_matrix(region, pattern, tiles, me, pl.program_id(0), blocks, width)
    product = jnp.dot(basis[0], matrix, preferred_element_type=F32)
    for t in range(blocks):
        spread[pl.ds(t, points, stride=blocks), :] = product[:, t * size : (t + 1) * size]
    out[0] = spread[...].astype(BF16)


def contract(region, pattern, basis, tiles, points, blocks, width):
    batches, _, columns = basis.shape
    size = columns // blocks
    return pl.pallas_call(
        functools.partial(product_kernel, points=points, blocks=blocks, width=width),
        grid_spec=pltpu.PrefetchScalarGridSpec(
            num_scalar_prefetch=2,
            grid=(batches,),
            in_specs=[
                pl.BlockSpec((1, points, columns), lambda b, *_: (b, 0, 0)),
                pl.BlockSpec(memory_space=pltpu.VMEM),
            ],
            out_specs=pl.BlockSpec((1, points * blocks, size), lambda b, *_: (b, 0, 0)),
            scratch_shapes=[pltpu.VMEM((points * blocks, size), F32)],
        ),
        out_shape=jax.ShapeDtypeStruct((batches, points * blocks, size), BF16),
        compiler_params=pltpu.CompilerParams(vmem_limit_bytes=VMEM_LIMIT),
        cost_estimate=pl.CostEstimate(
            flops=2 * batches * points * columns * columns,
            bytes_accessed=4 * batches * points * columns,
            transcendentals=0,
        ),
    )(region, pattern, basis, tiles)


def reorder_kernel(
    pattern_hbm,
    basis,
    field,
    basis_grad,
    weights_hbm,
    basis_out,
    field_out,
    weighted,
    grads,
    pattern,
    weights,
    columns,
    landed,
    wide,
    sems,
    small_sems,
):
    batches, blocks, points, size = basis_out.shape

    def copies(batch):
        return (
            pltpu.make_async_copy(field.at[batch], landed.at[batch, 0], sems.at[batch]),
            pltpu.make_async_copy(basis.at[batch], landed.at[batch, 1], sems.at[batch]),
            pltpu.make_async_copy(basis_grad.at[:, batch], landed.at[batch, pl.ds(2, PARTS)], sems.at[batch]),
        )

    small = (
        pltpu.make_async_copy(pattern_hbm, pattern, small_sems.at[0]),
        pltpu.make_async_copy(weights_hbm, weights, small_sems.at[1]),
    )
    for copy in small:
        copy.start()

    @pl.loop(0, batches)
    def _(batch):
        for copy in copies(batch):
            copy.start()

    for copy in small:
        copy.wait()
    rows = jnp.concatenate([weights[...], jnp.zeros((size - batches, points), F32)], axis=0).T
    for batch in range(batches):
        columns[batch] = jnp.broadcast_to(rows[:, batch : batch + 1], (points, size))

    @pl.loop(0, batches)
    def _(batch):
        pltpu.make_async_copy(landed.at[batch], landed.at[batch], sems.at[batch]).wait()
        points_here = pl.ds(pl.multiple_of(batch * points, points), points)
        places = [pattern[s, batch] for s in range(blocks)]
        for array in range(2 + PARTS):
            wide[array] = landed[batch, array].astype(F32)
        for s, place in enumerate(places):
            strided = pl.ds(s, points, stride=blocks)
            values = wide[0, strided, :]
            field_out[batch, place] = values.astype(BF16)
            weighted[place, points_here, :] = (values * columns[batch]).astype(BF16)
            basis_out[batch, place] = wide[1, strided, :].astype(BF16)
            for c in range(PARTS):
                grads[c, place, points_here, :] = wide[2 + c, strided, :].astype(BF16)


def reorder(pattern, basis, field, basis_grad, weights, points, blocks):
    batches, rows, size = basis.shape
    hbm = pl.BlockSpec(memory_space=pl.ANY)
    vmem = pl.BlockSpec(memory_space=pltpu.VMEM)
    ordered = jax.ShapeDtypeStruct((batches, blocks, points, size), BF16)
    return pl.pallas_call(
        reorder_kernel,
        out_shape=(
            ordered,
            ordered,
            jax.ShapeDtypeStruct((blocks, batches * points, size), BF16),
            jax.ShapeDtypeStruct((PARTS, blocks, batches * points, size), BF16),
        ),
        in_specs=[hbm] * 5,
        out_specs=(vmem,) * 4,
        scratch_shapes=[
            pltpu.SMEM((blocks, batches), jnp.int32),
            pltpu.VMEM(weights.shape, F32),
            pltpu.VMEM((batches, points, size), F32),
            pltpu.VMEM((batches, 2 + PARTS, rows, size), BF16),
            pltpu.VMEM((2 + PARTS, rows, size), F32),
            pltpu.SemaphoreType.DMA((batches,)),
            pltpu.SemaphoreType.DMA((2,)),
        ],
        compiler_params=pltpu.CompilerParams(vmem_limit_bytes=VMEM_LIMIT),
        cost_estimate=pl.CostEstimate(
            flops=0, bytes_accessed=2 * (2 + PARTS) * batches * rows * size, transcendentals=0
        ),
    )(in_hbm(pattern.T), in_hbm(basis), in_hbm(field), in_hbm(basis_grad), in_hbm(weights))


def moment_kernel(weighted, grads, moments):
    blocks, _, size = grads.shape[1:]
    for p in range(0, blocks, 2):
        first, last = max(p - 1, 0), min(p + 3, blocks)
        left = jnp.concatenate([weighted[place] for place in range(first, last)], axis=1)
        for c in range(PARTS):
            right = jnp.concatenate([grads[c, p], grads[c, p + 1]], axis=1)
            moments[c, first * size : last * size, p * size : (p + 2) * size] = lax.dot_general(
                left, right, TN, preferred_element_type=F32
            )


def build_moments(weighted, grads):
    blocks, depth, size = grads.shape[1:]
    vmem = pl.BlockSpec(memory_space=pltpu.VMEM)
    return pl.pallas_call(
        moment_kernel,
        out_shape=jax.ShapeDtypeStruct((PARTS, blocks * size, blocks * size), F32),
        in_specs=[vmem, vmem],
        out_specs=vmem,
        compiler_params=pltpu.CompilerParams(vmem_limit_bytes=VMEM_LIMIT),
        cost_estimate=pl.CostEstimate(
            flops=2 * PARTS * depth * (blocks * size) ** 2, bytes_accessed=0, transcendentals=0
        ),
    )(weighted, grads)


def atom_kernel(region, fn_atom, batch_atom, weight_grad, hot, grad_columns):
    batches, points = weight_grad.shape[1:]
    size = fn_atom.shape[1]
    blocks = region.shape[1]
    me = lax.axis_index("grid")
    atoms = lax.broadcasted_iota(jnp.int32, (hot.shape[0], size), 0)
    ids = jnp.concatenate([batch_atom[...], jnp.full((1, size - batches), -1, jnp.int32)], axis=1)
    hot[:, blocks * size :] = jnp.where(atoms == ids, 1.0, 0.0).astype(BF16)

    @pl.loop(0, blocks)
    def _(position):
        ids = fn_atom[pl.ds(region[me, position], 1), :]
        columns = pl.ds(pl.multiple_of(position * size, size), size)
        hot[:, columns] = jnp.where(atoms == ids, 1.0, 0.0).astype(BF16)

    for c in range(PARTS):
        padding = jnp.zeros((size - batches, points), F32)
        grad_columns[c] = jnp.concatenate([weight_grad[c], padding], axis=0).T


def atom_matrix(region, fn_atom, batch_atom, weight_grad, blocks, size, atom_total):
    vmem = pl.BlockSpec(memory_space=pltpu.VMEM)
    return pl.pallas_call(
        atom_kernel,
        out_shape=(
            jax.ShapeDtypeStruct((atom_total, (blocks + 1) * size), BF16),
            jax.ShapeDtypeStruct((PARTS, weight_grad.shape[2], size), F32),
        ),
        in_specs=[pl.BlockSpec(memory_space=pltpu.SMEM)] + [vmem] * 3,
        out_specs=(vmem, vmem),
        compiler_params=pltpu.CompilerParams(vmem_limit_bytes=VMEM_LIMIT),
        cost_estimate=pl.CostEstimate(flops=1000000000, bytes_accessed=2 * atom_total * size, transcendentals=0),
    )(region, fn_atom.reshape(-1, size), batch_atom.reshape(1, -1), weight_grad)


def combine_kernel(
    region, basis, field, moments, hot, grad_columns, *rest, owner_rows, slabs, width
):
    *pieces, product_out, out, stage, matrix = rest
    batches, blocks, points, size = basis.shape
    me = lax.axis_index("grid")
    me_atoms = lax.axis_index("atoms")
    half = (width - 1) // 2
    stage_rows(stage, pieces[0], pieces[1 : 1 + slabs // 2], pieces[1 + slabs // 2 :], slabs)
    rows = [region[me, position] for position in range(blocks)]
    found = [owner_and_slot(region, me, position, owner_rows) for position in range(blocks)]
    totals = [[jnp.zeros((8, size), F32) for _ in range(blocks)] for _ in range(PARTS)]
    for p in range(blocks):
        owner, slot, count = found[p]
        first = jnp.bitwise_xor(me, owner) * TRAVEL
        for q in range(blocks):
            if abs(q - p) > half:
                matrix[p * size : (p + 1) * size, q * size : (q + 1) * size] = jnp.zeros((size, size), BF16)
                continue
            k = rows[q] - rows[p] + half
            place = jnp.where(
                k == 0,
                travel_place(slot, count, 0),
                jnp.where(k == 1, travel_place(slot, count, 1), travel_place(slot, count, 2)),
            )
            inside = jnp.logical_and(k >= 0, k < width)
            tile = jnp.where(inside, stage[first + place], jnp.zeros((size, size), BF16))
            matrix[p * size : (p + 1) * size, q * size : (q + 1) * size] = tile
            turned = tile.T.astype(F32)
            for c in range(PARTS):
                terms = turned * moments[c, q * size : (q + 1) * size, p * size : (p + 1) * size]
                totals[c][p] = totals[c][p] + jnp.sum(terms.reshape(-1, 8, size), axis=0)
    derivative = [
        jnp.concatenate([jnp.sum(total, axis=0, keepdims=True) for total in totals[c]], axis=1) for c in range(PARTS)
    ]

    energies = jnp.zeros((points, size), F32)
    lanes = lax.broadcasted_iota(jnp.int32, (points, size), 1)
    left = [jnp.concatenate([basis[batch, p] for p in range(blocks)], axis=1) for batch in range(batches)]
    left = jnp.concatenate(left, axis=0)
    energy = [jnp.zeros((points, size), F32) for _ in range(batches)]
    for q in range(0, blocks, 2):
        product = jnp.dot(left, matrix[:, q * size : (q + 2) * size], preferred_element_type=F32)
        for batch in range(batches):
            for column in range(2):
                part = product[batch * points : (batch + 1) * points, column * size : (column + 1) * size]
                product_out[batch, q + column] = part.astype(BF16)
                energy[batch] = energy[batch] + part * field[batch, q + column].astype(F32)
    for batch in range(batches):
        energies = jnp.where(lanes == batch, jnp.sum(energy[batch], axis=1, keepdims=True), energies)

    lefts = []
    for c in range(PARTS):
        term = jnp.sum(energies * grad_columns[c], axis=0, keepdims=True)
        lefts.append(jnp.concatenate([-2.0 * derivative[c], term], axis=1))
    left = jnp.concatenate(lefts, axis=0)
    high, middle, low = (piece.astype(F32) for piece in split(left))
    left = jnp.concatenate([high, middle, low, jnp.zeros((16 - 3 * PARTS, left.shape[1]), F32)], axis=0).astype(BF16)
    chunk = out.shape[-1]
    for device in range(out.shape[0]):
        sums = lax.dot_general(
            left, hot[device * chunk : (device + 1) * chunk, :], NT, preferred_element_type=F32
        )
        value = sums[:PARTS] + sums[PARTS : 2 * PARTS] + sums[2 * PARTS : 3 * PARTS]
        place = jnp.bitwise_xor(me_atoms, device)
        out[place, 0] = value
        out[jnp.bitwise_xor(place, 1), 1] = value


def combine(region, prepared, pieces, shapes):
    basis, field, moments, hot, grad_columns = prepared
    slabs, atom_devices, atom_total, points, blocks, width, owner_rows = shapes
    batches, _, _, size = basis.shape
    vmem = pl.BlockSpec(memory_space=pltpu.VMEM)
    return pl.pallas_call(
        functools.partial(combine_kernel, owner_rows=owner_rows, slabs=slabs, width=width),
        out_shape=(
            jax.ShapeDtypeStruct(basis.shape, BF16),
            jax.ShapeDtypeStruct((atom_devices, 2, PARTS, atom_total // atom_devices), F32),
        ),
        in_specs=[pl.BlockSpec(memory_space=pltpu.SMEM)] + [vmem] * (5 + len(pieces)),
        out_specs=(vmem, vmem),
        scratch_shapes=[
            pltpu.VMEM((slabs * TRAVEL, size, size), BF16),
            pltpu.VMEM((blocks * size, blocks * size), BF16),
        ],
        compiler_params=pltpu.CompilerParams(vmem_limit_bytes=VMEM_LIMIT),
    )(region, basis, field, moments, hot, grad_columns, *pieces)


def write_kernel(pattern, product, out, wide, staged, sems):
    batches, blocks, points, size = product.shape

    def copy(batch):
        return pltpu.make_async_copy(staged.at[batch], out.at[batch], sems.at[batch])

    @pl.loop(0, batches // 2)
    def _(pair):
        for inner in range(2):
            batch = pair * 2 + inner
            for t in range(blocks):
                wide[inner, pl.ds(t, points, stride=blocks), :] = product[batch, pattern[t, batch]].astype(F32)
            staged[batch] = wide[inner].astype(BF16)
            copy(batch).start()

    @pl.loop(0, batches)
    def _(batch):
        copy(batch).wait()


def write(pattern, product):
    batches, blocks, points, size = product.shape
    shape = (batches, points * blocks, size)
    return pl.pallas_call(
        write_kernel,
        out_shape=jax.ShapeDtypeStruct(shape, BF16),
        in_specs=[pl.BlockSpec(memory_space=pltpu.SMEM), pl.BlockSpec(memory_space=pltpu.VMEM)],
        out_specs=pl.BlockSpec(memory_space=pl.ANY),
        scratch_shapes=[
            pltpu.VMEM((2, points * blocks, size), F32),
            pltpu.VMEM(shape, BF16),
            pltpu.SemaphoreType.DMA((batches,)),
        ],
        compiler_params=pltpu.CompilerParams(vmem_limit_bytes=VMEM_LIMIT),
        cost_estimate=pl.CostEstimate(flops=0, bytes_accessed=4 * math.prod(shape), transcendentals=0),
    )(pattern.T, product)


def swap_between_cores(near, ready, atom_devices):
    near, ready = lax.optimization_barrier((near, ready))
    swap = [(i, i ^ 1) for i in range(atom_devices)]
    return near, [lax.ppermute(piece, "atoms", swap) for piece in near[1:]], ready


def tree_sum(values):
    if len(values) == 1:
        return values[0]
    half = len(values) // 2
    return tree_sum(values[:half]) + tree_sum(values[half:])


def pair_sums(values):
    return [values[i] + values[i + 1] for i in range(0, len(values), 2)]


def sum_parts(partial_grad, contracted, slabs, atom_devices):
    parts = [partial_grad[0]]
    for d in range(1, atom_devices):
        parts.append(lax.ppermute(partial_grad[d], "atoms", [(i, i ^ d) for i in range(atom_devices)]))
    parts, contracted = lax.optimization_barrier((parts, contracted))
    both = tree_sum(pair_sums(parts))
    swap = [(i, i ^ 1) for i in range(atom_devices)]
    far = []
    for shifts in partners(slabs)[1:]:
        far.append(lax.ppermute(both, ("grid", "atoms"), moves_over_grid(shifts, slabs, atom_devices)))
    near = lax.ppermute(both[0], "grid", [(i, i ^ 1) for i in range(slabs)])
    far = lax.optimization_barrier(far)
    swapped = [lax.ppermute(piece[1], "atoms", swap) for piece in far]
    sums = [both[0] + near] + [piece[0] + other for piece, other in zip(far, swapped)]
    return tree_sum(sums), contracted


def local(
    basis,
    basis_grad,
    exchange_field,
    weights,
    weight_grad,
    density,
    region,
    pattern,
    fn_atom,
    batch_atom,
):
    batches, points, blocks, size = basis.shape
    owner_rows, width = density.shape[:2]
    slabs = lax.axis_size("grid")
    atom_devices = lax.axis_size("atoms")
    atom_total = fn_atom.shape[0] // (10 * slabs * atom_devices) * slabs * atom_devices
    shapes = (slabs, atom_devices, atom_total, points, blocks, width, owner_rows)
    flat_basis = basis.reshape(batches, points * blocks, size)
    flat_field = exchange_field.reshape(batches, points * blocks, size)
    flat_grad = basis_grad.reshape(PARTS, batches, points * blocks, size)
    own, near = fetch_rows(region, density, slabs, atom_devices)
    if region.shape[1] == blocks:
        basis_wide, field_wide, weighted, grads = reorder(
            pattern, flat_basis, flat_field, flat_grad, weights, points, blocks
        )
        ready = (basis_wide, field_wide, build_moments(weighted, grads), batch_atom)
        near, far, (basis_wide, field_wide, moments, batch_atom) = swap_between_cores(near, ready, atom_devices)
        hot, grad_columns = atom_matrix(region, fn_atom, batch_atom, weight_grad, blocks, size, atom_total)
        ready = (basis_wide, field_wide, moments, hot, grad_columns)
        product, partial_grad = combine(region, ready, [own, *near, *far], shapes)
        gradient, contracted = sum_parts(partial_grad, write(pattern, product), slabs, atom_devices)
        return contracted.reshape(basis.shape), gradient
    ready = relayout(in_hbm(flat_basis), in_hbm(flat_field), points, blocks)
    near, far, (basis_wide, field_wide) = swap_between_cores(near, ready, atom_devices)
    tiles, partial_grad = partial_gradient(
        region,
        pattern,
        basis_wide,
        field_wide,
        in_hbm(flat_grad),
        weights,
        weight_grad,
        fn_atom,
        batch_atom,
        [own, *near, *far],
        shapes,
    )
    contracted = contract(region, pattern, basis_wide, tiles, points, blocks, width)
    gradient, contracted = sum_parts(partial_grad, contracted, slabs, atom_devices)
    return contracted.reshape(basis.shape), gradient


def solution(mesh):
    placed = (
        P(("groups", "grid", "atoms"), None, None, None),
        P(None, ("groups", "grid", "atoms"), None, None, None),
        P(("groups", "grid", "atoms"), None, None, None),
        P(("groups", "grid", "atoms"), None),
        P(None, ("groups", "grid", "atoms"), None),
        P(("groups", "grid"), None, None, None),
        P("groups", None),
        P(("groups", "grid", "atoms"), None),
        P("groups"),
        P(("groups", "grid", "atoms")),
    )
    return jax.shard_map(
        local,
        mesh=mesh,
        in_specs=placed,
        out_specs=(P(("groups", "grid", "atoms"), None, None, None), P(None, ("groups", "atoms"))),
        check_vma=False,
    )
```

```python
import functools
import math

import jax
import jax.numpy as jnp
from jax import lax
from jax.experimental import pallas as pl
from jax.experimental.pallas import tpu as pltpu
from jax.sharding import PartitionSpec as P

TRAVEL = 5
PARTS = 3
F32 = jnp.float32
BF16 = jnp.bfloat16
NT = (((1,), (1,)), ((), ()))
TN = (((0,), (0,)), ((), ()))
VMEM_LIMIT = 32 * 1024 * 1024


def owner_and_slot(region, slab, position, owner_rows):
    owner = lax.div(region[slab, position], owner_rows)
    slot = jnp.int32(0)
    count = jnp.int32(0)
    for other in range(region.shape[1]):
        same = jnp.where(lax.div(region[slab, other], owner_rows) == owner, 1, 0)
        count = count + same
        slot = slot + jnp.where(other < position, same, 0)
    return owner, slot, count


def travel_place(slot, count, k):
    if k == 0:
        return jnp.where(slot == 0, 4, 2)
    if k == 1:
        return jnp.where(slot == 0, 0, 3)
    return jnp.where(jnp.logical_and(slot == 0, count == 2), 1, 4)


def partners(slabs):
    return [(1, 1)] + [(shift + 1, shift) for shift in range(2, slabs, 2)]


def moves_over_grid(shifts, slabs, atom_devices):
    return [
        (z * atom_devices + a, (z ^ shifts[a % 2]) * atom_devices + a) for z in range(slabs) for a in range(atom_devices)
    ]


def send_kernel(region_hbm, density, *rest):
    *outs, region, held, region_sem, sems = rest
    fetch = pltpu.make_async_copy(region_hbm, region, region_sem)
    fetch.start()
    count_here = density.shape[0] // sems.shape[0]
    fetches = []
    for part in range(sems.shape[0]):
        here = pl.ds(part * count_here, count_here)
        fetches.append(pltpu.make_async_copy(density.at[here], held.at[here], sems.at[part]))
    for copy in fetches:
        copy.start()
    fetch.wait()
    me = lax.axis_index("grid")
    core = lax.rem(lax.axis_index("atoms"), 2)
    slabs, size = region.shape
    owner_rows = density.shape[0]
    picks = []
    for low, high in [(0, 0)] + partners(slabs):
        slab = jnp.bitwise_xor(me, jnp.where(core == 0, low, high))
        base = jnp.int32(owner_rows)
        count = jnp.int32(0)
        for position in range(size):
            row = region[slab, position] - me * owner_rows
            mine = jnp.logical_and(row >= 0, row < owner_rows)
            base = jnp.minimum(base, jnp.where(mine, row, owner_rows))
            count = count + jnp.where(mine, 1, 0)
        base = jnp.where(count == 0, 0, base)
        after = jnp.minimum(base + 1, owner_rows - 1)
        lower = base == 0
        edge = jnp.where(jnp.logical_and(count == 2, jnp.logical_not(lower)), after, base)
        picks.append(((base, 1), (base, 2), (after, 0), (after, 1), (edge, jnp.where(lower, 0, 2))))
    for copy in fetches:
        copy.wait()
    for out, places in zip(outs, picks):
        for place, (row, k) in enumerate(places):
            out[place] = held[row, k]


def in_hbm(array):
    return pltpu.with_memory_space_constraint(array, pltpu.HBM)


def rows_to_send(region, density, slabs):
    size = density.shape[-1]
    count = 1 + len(partners(slabs))
    hbm = pl.BlockSpec(memory_space=pl.ANY)
    return pl.pallas_call(
        send_kernel,
        out_shape=[jax.ShapeDtypeStruct((TRAVEL, size, size), density.dtype)] * count,
        in_specs=[hbm, hbm],
        out_specs=[pl.BlockSpec(memory_space=pltpu.VMEM)] * count,
        scratch_shapes=[
            pltpu.SMEM(region.shape, jnp.int32),
            pltpu.VMEM(density.shape, density.dtype),
            pltpu.SemaphoreType.DMA,
            pltpu.SemaphoreType.DMA((5 if density.shape[0] % 5 == 0 else 1,)),
        ],
        compiler_params=pltpu.CompilerParams(vmem_limit_bytes=VMEM_LIMIT),
    )(in_hbm(region), in_hbm(density))


def fetch_rows(region, density, slabs, atom_devices):
    own, *outgoing = rows_to_send(region, density, slabs)
    near = []
    for shifts, piece in zip(partners(slabs), outgoing):
        near.append(lax.ppermute(piece, ("grid", "atoms"), moves_over_grid(shifts, slabs, atom_devices)))
    return own, near


def stage_rows(stage, own, near, far, slabs):
    core = lax.rem(lax.axis_index("atoms"), 2)
    first, *pairs = partners(slabs)
    for place in range(TRAVEL):
        stage[place] = own[place]
        stage[first[0] * TRAVEL + place] = near[0][place]
    for (low, high), here, there in zip(pairs, near[1:], far):
        mine = jnp.where(core == 0, low, high) * TRAVEL
        other = jnp.where(core == 0, high, low) * TRAVEL
        for place in range(TRAVEL):
            stage[mine + place] = here[place]
            stage[other + place] = there[place]


def block_major(x_ref, wide, points, blocks):
    wide[...] = x_ref[0].astype(F32)
    return [wide[pl.ds(s, points, stride=blocks), :] for s in range(blocks)]


def relayout_kernel(basis, field, basis_out, field_out, wide, *, points, blocks):
    size = basis.shape[-1]
    for source, target in ((basis, basis_out), (field, field_out)):
        for s, part in enumerate(block_major(source, wide, points, blocks)):
            target[0, :, s * size : (s + 1) * size] = part.astype(BF16)


def relayout(basis, field, points, blocks):
    batches, rows, size = basis.shape
    here = pl.BlockSpec((1, rows, size), lambda b: (b, 0, 0))
    there = pl.BlockSpec((1, points, blocks * size), lambda b: (b, 0, 0))
    shape = jax.ShapeDtypeStruct((batches, points, blocks * size), BF16)
    return pl.pallas_call(
        functools.partial(relayout_kernel, points=points, blocks=blocks),
        grid=(batches,),
        out_shape=(shape, shape),
        in_specs=[here, here],
        out_specs=(there, there),
        scratch_shapes=[pltpu.VMEM((rows, size), F32)],
        compiler_params=pltpu.CompilerParams(vmem_limit_bytes=VMEM_LIMIT),
        cost_estimate=pl.CostEstimate(flops=0, bytes_accessed=8 * batches * rows * size, transcendentals=0),
    )(basis, field)


def batch_matrix(region, pattern, tiles, slab, batch, blocks, width):
    half = (width - 1) // 2
    none = tiles.shape[0] - 1
    places = [pattern[batch, s] for s in range(blocks)]
    rows = [region[slab, place] for place in places]
    strips = []
    for s in range(blocks):
        strip = []
        for t in range(blocks):
            k = rows[t] - rows[s] + half
            inside = jnp.logical_and(k >= 0, k < width)
            strip.append(tiles[jnp.where(inside, places[s] * width + k, none)])
        strips.append(jnp.concatenate(strip, axis=1))
    return jnp.concatenate(strips, axis=0)


def split(values):
    high = values.astype(BF16)
    rest = values - high.astype(F32)
    middle = rest.astype(BF16)
    low = (rest - middle.astype(F32)).astype(BF16)
    return high, middle, low


def gradient_kernel(
    region,
    pattern,
    basis,
    field,
    basis_grad,
    weights,
    weight_grad,
    fn_atom,
    batch_atom,
    places,
    *rest,
    points,
    blocks,
    width,
    owner_rows,
    slabs,
):
    *pieces, tiles, out, stage, spread, sums, energy_sums = rest
    batch = pl.program_id(0)
    batches = pl.num_programs(0)
    me = lax.axis_index("grid")
    me_atoms = lax.axis_index("atoms")
    size = tiles.shape[-1]
    region_size = region.shape[1]

    @pl.when(batch == 0)
    def _():
        tiles[region_size * width] = jnp.zeros((size, size), BF16)
        stage_rows(stage, pieces[0], pieces[1 : 1 + slabs // 2], pieces[1 + slabs // 2 :], slabs)
        for position in range(region_size):
            owner, slot, count = owner_and_slot(region, me, position, owner_rows)
            shift = jnp.bitwise_xor(me, owner)
            for k in range(width):
                tiles[position * width + k] = stage[shift * TRAVEL + travel_place(slot, count, k)]

    matrix = batch_matrix(region, pattern, tiles, me, batch, blocks, width)
    potential = lax.dot_general(field[0], matrix, NT, preferred_element_type=F32)
    rows = jnp.concatenate(
        [weights[pl.ds(batch, 1), :]]
        + [weight_grad[c, pl.ds(batch, 1), :] for c in range(PARTS)]
        + [jnp.zeros((8 - 1 - PARTS, points), F32)],
        axis=0,
    )
    columns = rows.T
    weight = columns[:, 0:1]
    energy = jnp.zeros((points, size), F32)
    for s in range(blocks):
        here = potential[:, s * size : (s + 1) * size]
        energy = energy + basis[0, :, s * size : (s + 1) * size].astype(F32) * here
        spread[pl.ds(s, points, stride=blocks), :] = here * weight
    scaled = spread[...]
    place = pl.ds(pl.multiple_of(batch * 8, 8), 8)
    for c in range(PARTS):
        terms = basis_grad[c, 0].astype(F32) * scaled
        sums[c, place, :] = jnp.sum(terms.reshape(-1, 8, size), axis=0)
        terms = energy * columns[:, 1 + c : 2 + c]
        energy_sums[c, place, :] = jnp.sum(terms.reshape(-1, 8, size), axis=0)

    @pl.when(batch == batches - 1)
    def _():
        padded = max(8, region_size)
        chosen = lax.broadcasted_iota(jnp.int32, (padded, places.shape[1]), 0) == places[...]
        chosen = chosen.astype(BF16)
        blocks_sum = []
        for c in range(PARTS):
            total = jnp.zeros((padded, size), F32)
            for piece in split(sums[c]):
                total = total + jnp.dot(chosen, piece, preferred_element_type=F32)
            blocks_sum.append(-2.0 * total)
        lefts = []
        for position in range(region_size):
            stack = jnp.concatenate([total[position : position + 1] for total in blocks_sum], axis=0)
            high, middle, low = (piece.astype(F32) for piece in split(stack))
            lefts.append(jnp.concatenate([high, middle, low, jnp.zeros((16 - 3 * PARTS, size), F32)], axis=0))
        left = jnp.concatenate(lefts, axis=1).astype(BF16)
        chunk = out.shape[-1]
        scale = [jnp.sum(energy_sums[c], axis=1, keepdims=True) for c in range(PARTS)]
        for device in range(out.shape[0]):
            atoms = lax.broadcasted_iota(jnp.int32, (chunk, size), 0) + device * chunk
            hot = [
                jnp.where(atoms == fn_atom[pl.ds(region[me, position], 1), :], 1.0, 0.0).astype(BF16)
                for position in range(region_size)
            ]
            found = lax.dot_general(left, jnp.concatenate(hot, axis=1), NT, preferred_element_type=F32)
            atoms = lax.broadcasted_iota(jnp.int32, (batch_atom.shape[0], chunk), 1) + device * chunk
            mine = atoms == batch_atom[...]
            for c in range(PARTS):
                value = found[c : c + 1] + found[PARTS + c : PARTS + c + 1] + found[2 * PARTS + c : 2 * PARTS + c + 1]
                value = value + jnp.sum(jnp.where(mine, scale[c], 0.0), axis=0, keepdims=True)
                place = jnp.bitwise_xor(me_atoms, device)
                out[place, 0, c : c + 1, :] = value
                out[jnp.bitwise_xor(place, 1), 1, c : c + 1, :] = value


def partial_gradient(
    region, pattern, basis, field, basis_grad, weights, weight_grad, fn_atom, batch_atom, pieces, shapes
):
    slabs, atom_devices, atom_total, points, blocks, width, owner_rows = shapes
    batches, _, columns = basis.shape
    size = columns // blocks
    region_size = region.shape[1]
    fn_atom = fn_atom.reshape(-1, size)
    places = jnp.broadcast_to(pattern[:, None, :], (batches, 8 // blocks, blocks)).reshape(1, -1)
    batch_atom = jnp.broadcast_to(batch_atom[:, None], (batches, 8)).reshape(-1, 1)
    block = pl.BlockSpec((1, points, columns), lambda b, *_: (b, 0, 0))
    whole = pl.BlockSpec(memory_space=pltpu.VMEM)
    tile_shape = (region_size * width + 1, size, size)
    out_shape = (atom_devices, 2, PARTS, atom_total // atom_devices)
    return pl.pallas_call(
        functools.partial(
            gradient_kernel, points=points, blocks=blocks, width=width, owner_rows=owner_rows, slabs=slabs
        ),
        grid_spec=pltpu.PrefetchScalarGridSpec(
            num_scalar_prefetch=2,
            grid=(batches,),
            in_specs=[
                block,
                block,
                pl.BlockSpec((PARTS, 1, points * blocks, size), lambda b, *_: (0, b, 0, 0)),
            ]
            + [whole] * (5 + len(pieces)),
            out_specs=(whole, whole),
            scratch_shapes=[
                pltpu.VMEM((slabs * TRAVEL, size, size), BF16),
                pltpu.VMEM((points * blocks, size), F32),
                pltpu.VMEM((PARTS, batches * 8, size), F32),
                pltpu.VMEM((PARTS, batches * 8, size), F32),
            ],
        ),
        out_shape=(jax.ShapeDtypeStruct(tile_shape, BF16), jax.ShapeDtypeStruct(out_shape, F32)),
        compiler_params=pltpu.CompilerParams(vmem_limit_bytes=VMEM_LIMIT),
    )(region, pattern, basis, field, basis_grad, weights, weight_grad, fn_atom, batch_atom, places, *pieces)


def product_kernel(region, pattern, basis, tiles, out, spread, *, points, blocks, width):
    me = lax.axis_index("grid")
    size = tiles.shape[-1]
    matrix = batch_matrix(region, pattern, tiles, me, pl.program_id(0), blocks, width)
    product = jnp.dot(basis[0], matrix, preferred_element_type=F32)
    for t in range(blocks):
        spread[pl.ds(t, points, stride=blocks), :] = product[:, t * size : (t + 1) * size]
    out[0] = spread[...].astype(BF16)


def contract(region, pattern, basis, tiles, points, blocks, width):
    batches, _, columns = basis.shape
    size = columns // blocks
    return pl.pallas_call(
        functools.partial(product_kernel, points=points, blocks=blocks, width=width),
        grid_spec=pltpu.PrefetchScalarGridSpec(
            num_scalar_prefetch=2,
            grid=(batches,),
            in_specs=[
                pl.BlockSpec((1, points, columns), lambda b, *_: (b, 0, 0)),
                pl.BlockSpec(memory_space=pltpu.VMEM),
            ],
            out_specs=pl.BlockSpec((1, points * blocks, size), lambda b, *_: (b, 0, 0)),
            scratch_shapes=[pltpu.VMEM((points * blocks, size), F32)],
        ),
        out_shape=jax.ShapeDtypeStruct((batches, points * blocks, size), BF16),
        compiler_params=pltpu.CompilerParams(vmem_limit_bytes=VMEM_LIMIT),
        cost_estimate=pl.CostEstimate(
            flops=2 * batches * points * columns * columns,
            bytes_accessed=4 * batches * points * columns,
            transcendentals=0,
        ),
    )(region, pattern, basis, tiles)


def reorder_kernel(
    pattern_hbm,
    basis,
    field,
    basis_grad,
    weights_hbm,
    basis_out,
    field_out,
    weighted,
    grads,
    pattern,
    weights,
    columns,
    landed,
    wide,
    sems,
    small_sems,
):
    batches, blocks, points, size = basis_out.shape

    def copies(batch):
        return (
            pltpu.make_async_copy(field.at[batch], landed.at[batch, 0], sems.at[batch]),
            pltpu.make_async_copy(basis.at[batch], landed.at[batch, 1], sems.at[batch]),
            pltpu.make_async_copy(basis_grad.at[:, batch], landed.at[batch, pl.ds(2, PARTS)], sems.at[batch]),
        )

    small = (
        pltpu.make_async_copy(pattern_hbm, pattern, small_sems.at[0]),
        pltpu.make_async_copy(weights_hbm, weights, small_sems.at[1]),
    )
    for copy in small:
        copy.start()

    @pl.loop(0, batches)
    def _(batch):
        for copy in copies(batch):
            copy.start()

    for copy in small:
        copy.wait()
    rows = jnp.concatenate([weights[...], jnp.zeros((size - batches, points), F32)], axis=0).T
    for batch in range(batches):
        columns[batch] = jnp.broadcast_to(rows[:, batch : batch + 1], (points, size))

    @pl.loop(0, batches)
    def _(batch):
        pltpu.make_async_copy(landed.at[batch], landed.at[batch], sems.at[batch]).wait()
        points_here = pl.ds(pl.multiple_of(batch * points, points), points)
        places = [pattern[s, batch] for s in range(blocks)]
        for array in range(2 + PARTS):
            wide[array] = landed[batch, array].astype(F32)
        for s, place in enumerate(places):
            strided = pl.ds(s, points, stride=blocks)
            values = wide[0, strided, :]
            field_out[batch, place] = values.astype(BF16)
            weighted[place, points_here, :] = (values * columns[batch]).astype(BF16)
            basis_out[batch, place] = wide[1, strided, :].astype(BF16)
            for c in range(PARTS):
                grads[c, place, points_here, :] = wide[2 + c, strided, :].astype(BF16)


def reorder(pattern, basis, field, basis_grad, weights, points, blocks):
    batches, rows, size = basis.shape
    hbm = pl.BlockSpec(memory_space=pl.ANY)
    vmem = pl.BlockSpec(memory_space=pltpu.VMEM)
    ordered = jax.ShapeDtypeStruct((batches, blocks, points, size), BF16)
    return pl.pallas_call(
        reorder_kernel,
        out_shape=(
            ordered,
            ordered,
            jax.ShapeDtypeStruct((blocks, batches * points, size), BF16),
            jax.ShapeDtypeStruct((PARTS, blocks, batches * points, size), BF16),
        ),
        in_specs=[hbm] * 5,
        out_specs=(vmem,) * 4,
        scratch_shapes=[
            pltpu.SMEM((blocks, batches), jnp.int32),
            pltpu.VMEM(weights.shape, F32),
            pltpu.VMEM((batches, points, size), F32),
            pltpu.VMEM((batches, 2 + PARTS, rows, size), BF16),
            pltpu.VMEM((2 + PARTS, rows, size), F32),
            pltpu.SemaphoreType.DMA((batches,)),
            pltpu.SemaphoreType.DMA((2,)),
        ],
        compiler_params=pltpu.CompilerParams(vmem_limit_bytes=VMEM_LIMIT),
        cost_estimate=pl.CostEstimate(
            flops=0, bytes_accessed=2 * (2 + PARTS) * batches * rows * size, transcendentals=0
        ),
    )(in_hbm(pattern.T), in_hbm(basis), in_hbm(field), in_hbm(basis_grad), in_hbm(weights))


def moment_kernel(weighted, grads, moments):
    blocks, _, size = grads.shape[1:]
    for p in range(0, blocks, 2):
        first, last = max(p - 1, 0), min(p + 3, blocks)
        left = jnp.concatenate([weighted[place] for place in range(first, last)], axis=1)
        for c in range(PARTS):
            right = jnp.concatenate([grads[c, p], grads[c, p + 1]], axis=1)
            moments[c, first * size : last * size, p * size : (p + 2) * size] = lax.dot_general(
                left, right, TN, preferred_element_type=F32
            )


def build_moments(weighted, grads):
    blocks, depth, size = grads.shape[1:]
    vmem = pl.BlockSpec(memory_space=pltpu.VMEM)
    return pl.pallas_call(
        moment_kernel,
        out_shape=jax.ShapeDtypeStruct((PARTS, blocks * size, blocks * size), F32),
        in_specs=[vmem, vmem],
        out_specs=vmem,
        compiler_params=pltpu.CompilerParams(vmem_limit_bytes=VMEM_LIMIT),
        cost_estimate=pl.CostEstimate(
            flops=2 * PARTS * depth * (blocks * size) ** 2, bytes_accessed=0, transcendentals=0
        ),
    )(weighted, grads)


def atom_kernel(region, fn_atom, batch_atom, weight_grad, hot, grad_columns):
    batches, points = weight_grad.shape[1:]
    size = fn_atom.shape[1]
    blocks = region.shape[1]
    me = lax.axis_index("grid")
    atoms = lax.broadcasted_iota(jnp.int32, (hot.shape[0], size), 0)
    ids = jnp.concatenate([batch_atom[...], jnp.full((1, size - batches), -1, jnp.int32)], axis=1)
    hot[:, blocks * size :] = jnp.where(atoms == ids, 1.0, 0.0).astype(BF16)

    @pl.loop(0, blocks)
    def _(position):
        ids = fn_atom[pl.ds(region[me, position], 1), :]
        columns = pl.ds(pl.multiple_of(position * size, size), size)
        hot[:, columns] = jnp.where(atoms == ids, 1.0, 0.0).astype(BF16)

    for c in range(PARTS):
        padding = jnp.zeros((size - batches, points), F32)
        grad_columns[c] = jnp.concatenate([weight_grad[c], padding], axis=0).T


def atom_matrix(region, fn_atom, batch_atom, weight_grad, blocks, size, atom_total):
    vmem = pl.BlockSpec(memory_space=pltpu.VMEM)
    return pl.pallas_call(
        atom_kernel,
        out_shape=(
            jax.ShapeDtypeStruct((atom_total, (blocks + 1) * size), BF16),
            jax.ShapeDtypeStruct((PARTS, weight_grad.shape[2], size), F32),
        ),
        in_specs=[pl.BlockSpec(memory_space=pltpu.SMEM)] + [vmem] * 3,
        out_specs=(vmem, vmem),
        compiler_params=pltpu.CompilerParams(vmem_limit_bytes=VMEM_LIMIT),
        cost_estimate=pl.CostEstimate(flops=1000000000, bytes_accessed=2 * atom_total * size, transcendentals=0),
    )(region, fn_atom.reshape(-1, size), batch_atom.reshape(1, -1), weight_grad)


def combine_kernel(
    region, basis, field, moments, hot, grad_columns, *rest, owner_rows, slabs, width
):
    *pieces, product_out, out, stage, matrix = rest
    batches, blocks, points, size = basis.shape
    me = lax.axis_index("grid")
    me_atoms = lax.axis_index("atoms")
    half = (width - 1) // 2
    stage_rows(stage, pieces[0], pieces[1 : 1 + slabs // 2], pieces[1 + slabs // 2 :], slabs)
    rows = [region[me, position] for position in range(blocks)]
    found = [owner_and_slot(region, me, position, owner_rows) for position in range(blocks)]
    totals = [[jnp.zeros((8, size), F32) for _ in range(blocks)] for _ in range(PARTS)]
    for p in range(blocks):
        owner, slot, count = found[p]
        first = jnp.bitwise_xor(me, owner) * TRAVEL
        for q in range(blocks):
            if abs(q - p) > half:
                matrix[p * size : (p + 1) * size, q * size : (q + 1) * size] = jnp.zeros((size, size), BF16)
                continue
            k = rows[q] - rows[p] + half
            place = jnp.where(
                k == 0,
                travel_place(slot, count, 0),
                jnp.where(k == 1, travel_place(slot, count, 1), travel_place(slot, count, 2)),
            )
            inside = jnp.logical_and(k >= 0, k < width)
            tile = jnp.where(inside, stage[first + place], jnp.zeros((size, size), BF16))
            matrix[p * size : (p + 1) * size, q * size : (q + 1) * size] = tile
            turned = tile.T.astype(F32)
            for c in range(PARTS):
                terms = turned * moments[c, q * size : (q + 1) * size, p * size : (p + 1) * size]
                totals[c][p] = totals[c][p] + jnp.sum(terms.reshape(-1, 8, size), axis=0)
    derivative = [
        jnp.concatenate([jnp.sum(total, axis=0, keepdims=True) for total in totals[c]], axis=1) for c in range(PARTS)
    ]

    energies = jnp.zeros((points, size), F32)
    lanes = lax.broadcasted_iota(jnp.int32, (points, size), 1)
    left = [jnp.concatenate([basis[batch, p] for p in range(blocks)], axis=1) for batch in range(batches)]
    left = jnp.concatenate(left, axis=0)
    energy = [jnp.zeros((points, size), F32) for _ in range(batches)]
    for q in range(0, blocks, 2):
        product = jnp.dot(left, matrix[:, q * size : (q + 2) * size], preferred_element_type=F32)
        for batch in range(batches):
            for column in range(2):
                part = product[batch * points : (batch + 1) * points, column * size : (column + 1) * size]
                product_out[batch, q + column] = part.astype(BF16)
                energy[batch] = energy[batch] + part * field[batch, q + column].astype(F32)
    for batch in range(batches):
        energies = jnp.where(lanes == batch, jnp.sum(energy[batch], axis=1, keepdims=True), energies)

    lefts = []
    for c in range(PARTS):
        term = jnp.sum(energies * grad_columns[c], axis=0, keepdims=True)
        lefts.append(jnp.concatenate([-2.0 * derivative[c], term], axis=1))
    left = jnp.concatenate(lefts, axis=0)
    high, middle, low = (piece.astype(F32) for piece in split(left))
    left = jnp.concatenate([high, middle, low, jnp.zeros((16 - 3 * PARTS, left.shape[1]), F32)], axis=0).astype(BF16)
    chunk = out.shape[-1]
    for device in range(out.shape[0]):
        sums = lax.dot_general(
            left, hot[device * chunk : (device + 1) * chunk, :], NT, preferred_element_type=F32
        )
        value = sums[:PARTS] + sums[PARTS : 2 * PARTS] + sums[2 * PARTS : 3 * PARTS]
        place = jnp.bitwise_xor(me_atoms, device)
        out[place, 0] = value
        out[jnp.bitwise_xor(place, 1), 1] = value


def combine(region, prepared, pieces, shapes):
    basis, field, moments, hot, grad_columns = prepared
    slabs, atom_devices, atom_total, points, blocks, width, owner_rows = shapes
    batches, _, _, size = basis.shape
    vmem = pl.BlockSpec(memory_space=pltpu.VMEM)
    return pl.pallas_call(
        functools.partial(combine_kernel, owner_rows=owner_rows, slabs=slabs, width=width),
        out_shape=(
            jax.ShapeDtypeStruct(basis.shape, BF16),
            jax.ShapeDtypeStruct((atom_devices, 2, PARTS, atom_total // atom_devices), F32),
        ),
        in_specs=[pl.BlockSpec(memory_space=pltpu.SMEM)] + [vmem] * (5 + len(pieces)),
        out_specs=(vmem, vmem),
        scratch_shapes=[
            pltpu.VMEM((slabs * TRAVEL, size, size), BF16),
            pltpu.VMEM((blocks * size, blocks * size), BF16),
        ],
        compiler_params=pltpu.CompilerParams(vmem_limit_bytes=VMEM_LIMIT),
    )(region, basis, field, moments, hot, grad_columns, *pieces)


def write_kernel(pattern, product, out, wide, staged, sems):
    batches, blocks, points, size = product.shape

    def copy(batch):
        return pltpu.make_async_copy(staged.at[batch], out.at[batch], sems.at[batch])

    @pl.loop(0, batches // 2)
    def _(pair):
        for inner in range(2):
            batch = pair * 2 + inner
            for t in range(blocks):
                wide[inner, pl.ds(t, points, stride=blocks), :] = product[batch, pattern[t, batch]].astype(F32)
            staged[batch] = wide[inner].astype(BF16)
            copy(batch).start()

    @pl.loop(0, batches)
    def _(batch):
        copy(batch).wait()


def write(pattern, product):
    batches, blocks, points, size = product.shape
    shape = (batches, points * blocks, size)
    return pl.pallas_call(
        write_kernel,
        out_shape=jax.ShapeDtypeStruct(shape, BF16),
        in_specs=[pl.BlockSpec(memory_space=pltpu.SMEM), pl.BlockSpec(memory_space=pltpu.VMEM)],
        out_specs=pl.BlockSpec(memory_space=pl.ANY),
        scratch_shapes=[
            pltpu.VMEM((2, points * blocks, size), F32),
            pltpu.VMEM(shape, BF16),
            pltpu.SemaphoreType.DMA((batches,)),
        ],
        compiler_params=pltpu.CompilerParams(vmem_limit_bytes=VMEM_LIMIT),
        cost_estimate=pl.CostEstimate(flops=0, bytes_accessed=4 * math.prod(shape), transcendentals=0),
    )(pattern.T, product)


def swap_between_cores(near, ready, atom_devices):
    far, ready = lax.optimization_barrier((near[1:], ready))
    near = [near[0], *far]
    swap = [(i, i ^ 1) for i in range(atom_devices)]
    return near, [lax.ppermute(piece, "atoms", swap) for piece in near[1:]], ready


def tree_sum(values):
    if len(values) == 1:
        return values[0]
    half = len(values) // 2
    return tree_sum(values[:half]) + tree_sum(values[half:])


def pair_sums(values):
    return [values[i] + values[i + 1] for i in range(0, len(values), 2)]


def sum_parts(partial_grad, contracted, slabs, atom_devices):
    parts = [partial_grad[0]]
    for d in range(1, atom_devices):
        parts.append(lax.ppermute(partial_grad[d], "atoms", [(i, i ^ d) for i in range(atom_devices)]))
    parts, contracted = lax.optimization_barrier((parts, contracted))
    both = tree_sum(pair_sums(parts))
    swap = [(i, i ^ 1) for i in range(atom_devices)]
    far = []
    for shifts in partners(slabs)[1:]:
        far.append(lax.ppermute(both, ("grid", "atoms"), moves_over_grid(shifts, slabs, atom_devices)))
    near = lax.ppermute(both[0], "grid", [(i, i ^ 1) for i in range(slabs)])
    far = lax.optimization_barrier(far)
    swapped = [lax.ppermute(piece[1], "atoms", swap) for piece in far]
    sums = [both[0] + near] + [piece[0] + other for piece, other in zip(far, swapped)]
    return tree_sum(sums), contracted


def local(
    basis,
    basis_grad,
    exchange_field,
    weights,
    weight_grad,
    density,
    region,
    pattern,
    fn_atom,
    batch_atom,
):
    batches, points, blocks, size = basis.shape
    owner_rows, width = density.shape[:2]
    slabs = lax.axis_size("grid")
    atom_devices = lax.axis_size("atoms")
    atom_total = fn_atom.shape[0] // (10 * slabs * atom_devices) * slabs * atom_devices
    shapes = (slabs, atom_devices, atom_total, points, blocks, width, owner_rows)
    flat_basis = basis.reshape(batches, points * blocks, size)
    flat_field = exchange_field.reshape(batches, points * blocks, size)
    flat_grad = basis_grad.reshape(PARTS, batches, points * blocks, size)
    own, near = fetch_rows(region, density, slabs, atom_devices)
    if region.shape[1] == blocks:
        basis_wide, field_wide, weighted, grads = reorder(
            pattern, flat_basis, flat_field, flat_grad, weights, points, blocks
        )
        ready = (basis_wide, field_wide, build_moments(weighted, grads), batch_atom)
        near, far, (basis_wide, field_wide, moments, batch_atom) = swap_between_cores(near, ready, atom_devices)
        hot, grad_columns = atom_matrix(region, fn_atom, batch_atom, weight_grad, blocks, size, atom_total)
        ready = (basis_wide, field_wide, moments, hot, grad_columns)
        product, partial_grad = combine(region, ready, [own, *near, *far], shapes)
        gradient, contracted = sum_parts(partial_grad, write(pattern, product), slabs, atom_devices)
        return contracted.reshape(basis.shape), gradient
    ready = relayout(in_hbm(flat_basis), in_hbm(flat_field), points, blocks)
    near, far, (basis_wide, field_wide) = swap_between_cores(near, ready, atom_devices)
    tiles, partial_grad = partial_gradient(
        region,
        pattern,
        basis_wide,
        field_wide,
        in_hbm(flat_grad),
        weights,
        weight_grad,
        fn_atom,
        batch_atom,
        [own, *near, *far],
        shapes,
    )
    contracted = contract(region, pattern, basis_wide, tiles, points, blocks, width)
    gradient, contracted = sum_parts(partial_grad, contracted, slabs, atom_devices)
    return contracted.reshape(basis.shape), gradient


def solution(mesh):
    placed = (
        P(("groups", "grid", "atoms"), None, None, None),
        P(None, ("groups", "grid", "atoms"), None, None, None),
        P(("groups", "grid", "atoms"), None, None, None),
        P(("groups", "grid", "atoms"), None),
        P(None, ("groups", "grid", "atoms"), None),
        P(("groups", "grid"), None, None, None),
        P("groups", None),
        P(("groups", "grid", "atoms"), None),
        P("groups"),
        P(("groups", "grid", "atoms")),
    )
    return jax.shard_map(
        local,
        mesh=mesh,
        in_specs=placed,
        out_specs=(P(("groups", "grid", "atoms"), None, None, None), P(None, ("groups", "atoms"))),
        check_vma=False,
    )
```

```python
import functools
import math

import jax
import jax.numpy as jnp
from jax import lax
from jax.experimental import pallas as pl
from jax.experimental.pallas import tpu as pltpu
from jax.sharding import PartitionSpec as P

TRAVEL = 5
PARTS = 3
F32 = jnp.float32
BF16 = jnp.bfloat16
NT = (((1,), (1,)), ((), ()))
TN = (((0,), (0,)), ((), ()))
VMEM_LIMIT = 32 * 1024 * 1024


def owner_and_slot(region, slab, position, owner_rows):
    owner = lax.div(region[slab, position], owner_rows)
    slot = jnp.int32(0)
    count = jnp.int32(0)
    for other in range(region.shape[1]):
        same = jnp.where(lax.div(region[slab, other], owner_rows) == owner, 1, 0)
        count = count + same
        slot = slot + jnp.where(other < position, same, 0)
    return owner, slot, count


def travel_place(slot, count, k):
    if k == 0:
        return jnp.where(slot == 0, 4, 2)
    if k == 1:
        return jnp.where(slot == 0, 0, 3)
    return jnp.where(jnp.logical_and(slot == 0, count == 2), 1, 4)


def partners(slabs):
    return [(1, 1)] + [(shift + 1, shift) for shift in range(2, slabs, 2)]


def moves_over_grid(shifts, slabs, atom_devices):
    return [
        (z * atom_devices + a, (z ^ shifts[a % 2]) * atom_devices + a) for z in range(slabs) for a in range(atom_devices)
    ]


def send_kernel(region_hbm, density, *rest):
    *outs, region, held, region_sem, sems = rest
    fetch = pltpu.make_async_copy(region_hbm, region, region_sem)
    fetch.start()
    count_here = density.shape[0] // sems.shape[0]
    fetches = []
    for part in range(sems.shape[0]):
        here = pl.ds(part * count_here, count_here)
        fetches.append(pltpu.make_async_copy(density.at[here], held.at[here], sems.at[part]))
    for copy in fetches:
        copy.start()
    fetch.wait()
    me = lax.axis_index("grid")
    core = lax.rem(lax.axis_index("atoms"), 2)
    slabs, size = region.shape
    owner_rows = density.shape[0]
    picks = []
    for low, high in [(0, 0)] + partners(slabs):
        slab = jnp.bitwise_xor(me, jnp.where(core == 0, low, high))
        base = jnp.int32(owner_rows)
        count = jnp.int32(0)
        for position in range(size):
            row = region[slab, position] - me * owner_rows
            mine = jnp.logical_and(row >= 0, row < owner_rows)
            base = jnp.minimum(base, jnp.where(mine, row, owner_rows))
            count = count + jnp.where(mine, 1, 0)
        base = jnp.where(count == 0, 0, base)
        after = jnp.minimum(base + 1, owner_rows - 1)
        lower = base == 0
        edge = jnp.where(jnp.logical_and(count == 2, jnp.logical_not(lower)), after, base)
        picks.append(((base, 1), (base, 2), (after, 0), (after, 1), (edge, jnp.where(lower, 0, 2))))
    for copy in fetches:
        copy.wait()
    for out, places in zip(outs, picks):
        for place, (row, k) in enumerate(places):
            out[place] = held[row, k]


def in_hbm(array):
    return pltpu.with_memory_space_constraint(array, pltpu.HBM)


def rows_to_send(region, density, slabs):
    size = density.shape[-1]
    count = 1 + len(partners(slabs))
    hbm = pl.BlockSpec(memory_space=pl.ANY)
    return pl.pallas_call(
        send_kernel,
        out_shape=[jax.ShapeDtypeStruct((TRAVEL, size, size), density.dtype)] * count,
        in_specs=[hbm, hbm],
        out_specs=[pl.BlockSpec(memory_space=pltpu.VMEM)] * count,
        scratch_shapes=[
            pltpu.SMEM(region.shape, jnp.int32),
            pltpu.VMEM(density.shape, density.dtype),
            pltpu.SemaphoreType.DMA,
            pltpu.SemaphoreType.DMA((5 if density.shape[0] % 5 == 0 else 1,)),
        ],
        compiler_params=pltpu.CompilerParams(vmem_limit_bytes=VMEM_LIMIT),
    )(in_hbm(region), in_hbm(density))


def fetch_rows(region, density, slabs, atom_devices):
    own, *outgoing = rows_to_send(region, density, slabs)
    near = []
    for shifts, piece in zip(partners(slabs), outgoing):
        near.append(lax.ppermute(piece, ("grid", "atoms"), moves_over_grid(shifts, slabs, atom_devices)))
    return own, near


def stage_rows(stage, own, near, far, slabs):
    core = lax.rem(lax.axis_index("atoms"), 2)
    first, *pairs = partners(slabs)
    for place in range(TRAVEL):
        stage[place] = own[place]
        stage[first[0] * TRAVEL + place] = near[0][place]
    for (low, high), here, there in zip(pairs, near[1:], far):
        mine = jnp.where(core == 0, low, high) * TRAVEL
        other = jnp.where(core == 0, high, low) * TRAVEL
        for place in range(TRAVEL):
            stage[mine + place] = here[place]
            stage[other + place] = there[place]


def block_major(x_ref, wide, points, blocks):
    wide[...] = x_ref[0].astype(F32)
    return [wide[pl.ds(s, points, stride=blocks), :] for s in range(blocks)]


def relayout_kernel(basis, field, basis_out, field_out, wide, *, points, blocks):
    size = basis.shape[-1]
    for source, target in ((basis, basis_out), (field, field_out)):
        for s, part in enumerate(block_major(source, wide, points, blocks)):
            target[0, :, s * size : (s + 1) * size] = part.astype(BF16)


def relayout(basis, field, points, blocks):
    batches, rows, size = basis.shape
    here = pl.BlockSpec((1, rows, size), lambda b: (b, 0, 0))
    there = pl.BlockSpec((1, points, blocks * size), lambda b: (b, 0, 0))
    shape = jax.ShapeDtypeStruct((batches, points, blocks * size), BF16)
    return pl.pallas_call(
        functools.partial(relayout_kernel, points=points, blocks=blocks),
        grid=(batches,),
        out_shape=(shape, shape),
        in_specs=[here, here],
        out_specs=(there, there),
        scratch_shapes=[pltpu.VMEM((rows, size), F32)],
        compiler_params=pltpu.CompilerParams(vmem_limit_bytes=VMEM_LIMIT),
        cost_estimate=pl.CostEstimate(flops=0, bytes_accessed=8 * batches * rows * size, transcendentals=0),
    )(basis, field)


def batch_matrix(region, pattern, tiles, slab, batch, blocks, width):
    half = (width - 1) // 2
    none = tiles.shape[0] - 1
    places = [pattern[batch, s] for s in range(blocks)]
    rows = [region[slab, place] for place in places]
    strips = []
    for s in range(blocks):
        strip = []
        for t in range(blocks):
            k = rows[t] - rows[s] + half
            inside = jnp.logical_and(k >= 0, k < width)
            strip.append(tiles[jnp.where(inside, places[s] * width + k, none)])
        strips.append(jnp.concatenate(strip, axis=1))
    return jnp.concatenate(strips, axis=0)


def split(values):
    high = values.astype(BF16)
    rest = values - high.astype(F32)
    middle = rest.astype(BF16)
    low = (rest - middle.astype(F32)).astype(BF16)
    return high, middle, low


def gradient_kernel(
    region,
    pattern,
    basis,
    field,
    basis_grad,
    weights,
    weight_grad,
    fn_atom,
    batch_atom,
    places,
    *rest,
    points,
    blocks,
    width,
    owner_rows,
    slabs,
):
    *pieces, tiles, out, stage, spread, sums, energy_sums = rest
    batch = pl.program_id(0)
    batches = pl.num_programs(0)
    me = lax.axis_index("grid")
    me_atoms = lax.axis_index("atoms")
    size = tiles.shape[-1]
    region_size = region.shape[1]

    @pl.when(batch == 0)
    def _():
        tiles[region_size * width] = jnp.zeros((size, size), BF16)
        stage_rows(stage, pieces[0], pieces[1 : 1 + slabs // 2], pieces[1 + slabs // 2 :], slabs)
        for position in range(region_size):
            owner, slot, count = owner_and_slot(region, me, position, owner_rows)
            shift = jnp.bitwise_xor(me, owner)
            for k in range(width):
                tiles[position * width + k] = stage[shift * TRAVEL + travel_place(slot, count, k)]

    matrix = batch_matrix(region, pattern, tiles, me, batch, blocks, width)
    potential = lax.dot_general(field[0], matrix, NT, preferred_element_type=F32)
    rows = jnp.concatenate(
        [weights[pl.ds(batch, 1), :]]
        + [weight_grad[c, pl.ds(batch, 1), :] for c in range(PARTS)]
        + [jnp.zeros((8 - 1 - PARTS, points), F32)],
        axis=0,
    )
    columns = rows.T
    weight = columns[:, 0:1]
    energy = jnp.zeros((points, size), F32)
    for s in range(blocks):
        here = potential[:, s * size : (s + 1) * size]
        energy = energy + basis[0, :, s * size : (s + 1) * size].astype(F32) * here
        spread[pl.ds(s, points, stride=blocks), :] = here * weight
    scaled = spread[...]
    place = pl.ds(pl.multiple_of(batch * 8, 8), 8)
    for c in range(PARTS):
        terms = basis_grad[c, 0].astype(F32) * scaled
        sums[c, place, :] = jnp.sum(terms.reshape(-1, 8, size), axis=0)
        terms = energy * columns[:, 1 + c : 2 + c]
        energy_sums[c, place, :] = jnp.sum(terms.reshape(-1, 8, size), axis=0)

    @pl.when(batch == batches - 1)
    def _():
        padded = max(8, region_size)
        chosen = lax.broadcasted_iota(jnp.int32, (padded, places.shape[1]), 0) == places[...]
        chosen = chosen.astype(BF16)
        blocks_sum = []
        for c in range(PARTS):
            total = jnp.zeros((padded, size), F32)
            for piece in split(sums[c]):
                total = total + jnp.dot(chosen, piece, preferred_element_type=F32)
            blocks_sum.append(-2.0 * total)
        lefts = []
        for position in range(region_size):
            stack = jnp.concatenate([total[position : position + 1] for total in blocks_sum], axis=0)
            high, middle, low = (piece.astype(F32) for piece in split(stack))
            lefts.append(jnp.concatenate([high, middle, low, jnp.zeros((16 - 3 * PARTS, size), F32)], axis=0))
        left = jnp.concatenate(lefts, axis=1).astype(BF16)
        chunk = out.shape[-1]
        scale = [jnp.sum(energy_sums[c], axis=1, keepdims=True) for c in range(PARTS)]
        for device in range(out.shape[0]):
            atoms = lax.broadcasted_iota(jnp.int32, (chunk, size), 0) + device * chunk
            hot = [
                jnp.where(atoms == fn_atom[pl.ds(region[me, position], 1), :], 1.0, 0.0).astype(BF16)
                for position in range(region_size)
            ]
            found = lax.dot_general(left, jnp.concatenate(hot, axis=1), NT, preferred_element_type=F32)
            atoms = lax.broadcasted_iota(jnp.int32, (batch_atom.shape[0], chunk), 1) + device * chunk
            mine = atoms == batch_atom[...]
            for c in range(PARTS):
                value = found[c : c + 1] + found[PARTS + c : PARTS + c + 1] + found[2 * PARTS + c : 2 * PARTS + c + 1]
                value = value + jnp.sum(jnp.where(mine, scale[c], 0.0), axis=0, keepdims=True)
                place = jnp.bitwise_xor(me_atoms, device)
                out[place, 0, c : c + 1, :] = value
                out[jnp.bitwise_xor(place, 1), 1, c : c + 1, :] = value


def partial_gradient(
    region, pattern, basis, field, basis_grad, weights, weight_grad, fn_atom, batch_atom, pieces, shapes
):
    slabs, atom_devices, atom_total, points, blocks, width, owner_rows = shapes
    batches, _, columns = basis.shape
    size = columns // blocks
    region_size = region.shape[1]
    fn_atom = fn_atom.reshape(-1, size)
    places = jnp.broadcast_to(pattern[:, None, :], (batches, 8 // blocks, blocks)).reshape(1, -1)
    batch_atom = jnp.broadcast_to(batch_atom[:, None], (batches, 8)).reshape(-1, 1)
    block = pl.BlockSpec((1, points, columns), lambda b, *_: (b, 0, 0))
    whole = pl.BlockSpec(memory_space=pltpu.VMEM)
    tile_shape = (region_size * width + 1, size, size)
    out_shape = (atom_devices, 2, PARTS, atom_total // atom_devices)
    return pl.pallas_call(
        functools.partial(
            gradient_kernel, points=points, blocks=blocks, width=width, owner_rows=owner_rows, slabs=slabs
        ),
        grid_spec=pltpu.PrefetchScalarGridSpec(
            num_scalar_prefetch=2,
            grid=(batches,),
            in_specs=[
                block,
                block,
                pl.BlockSpec((PARTS, 1, points * blocks, size), lambda b, *_: (0, b, 0, 0)),
            ]
            + [whole] * (5 + len(pieces)),
            out_specs=(whole, whole),
            scratch_shapes=[
                pltpu.VMEM((slabs * TRAVEL, size, size), BF16),
                pltpu.VMEM((points * blocks, size), F32),
                pltpu.VMEM((PARTS, batches * 8, size), F32),
                pltpu.VMEM((PARTS, batches * 8, size), F32),
            ],
        ),
        out_shape=(jax.ShapeDtypeStruct(tile_shape, BF16), jax.ShapeDtypeStruct(out_shape, F32)),
        compiler_params=pltpu.CompilerParams(vmem_limit_bytes=VMEM_LIMIT),
    )(region, pattern, basis, field, basis_grad, weights, weight_grad, fn_atom, batch_atom, places, *pieces)


def product_kernel(region, pattern, basis, tiles, out, spread, *, points, blocks, width):
    me = lax.axis_index("grid")
    size = tiles.shape[-1]
    matrix = batch_matrix(region, pattern, tiles, me, pl.program_id(0), blocks, width)
    product = jnp.dot(basis[0], matrix, preferred_element_type=F32)
    for t in range(blocks):
        spread[pl.ds(t, points, stride=blocks), :] = product[:, t * size : (t + 1) * size]
    out[0] = spread[...].astype(BF16)


def contract(region, pattern, basis, tiles, points, blocks, width):
    batches, _, columns = basis.shape
    size = columns // blocks
    return pl.pallas_call(
        functools.partial(product_kernel, points=points, blocks=blocks, width=width),
        grid_spec=pltpu.PrefetchScalarGridSpec(
            num_scalar_prefetch=2,
            grid=(batches,),
            in_specs=[
                pl.BlockSpec((1, points, columns), lambda b, *_: (b, 0, 0)),
                pl.BlockSpec(memory_space=pltpu.VMEM),
            ],
            out_specs=pl.BlockSpec((1, points * blocks, size), lambda b, *_: (b, 0, 0)),
            scratch_shapes=[pltpu.VMEM((points * blocks, size), F32)],
        ),
        out_shape=jax.ShapeDtypeStruct((batches, points * blocks, size), BF16),
        compiler_params=pltpu.CompilerParams(vmem_limit_bytes=VMEM_LIMIT),
        cost_estimate=pl.CostEstimate(
            flops=2 * batches * points * columns * columns,
            bytes_accessed=4 * batches * points * columns,
            transcendentals=0,
        ),
    )(region, pattern, basis, tiles)


def reorder_kernel(
    pattern_hbm,
    basis,
    field,
    basis_grad,
    weights_hbm,
    basis_out,
    field_out,
    weighted,
    grads,
    pattern,
    weights,
    columns,
    landed,
    wide,
    sems,
    small_sems,
):
    batches, blocks, points, size = basis_out.shape

    def copies(batch):
        return (
            pltpu.make_async_copy(field.at[batch], landed.at[batch, 0], sems.at[batch]),
            pltpu.make_async_copy(basis.at[batch], landed.at[batch, 1], sems.at[batch]),
            pltpu.make_async_copy(basis_grad.at[:, batch], landed.at[batch, pl.ds(2, PARTS)], sems.at[batch]),
        )

    small = (
        pltpu.make_async_copy(pattern_hbm, pattern, small_sems.at[0]),
        pltpu.make_async_copy(weights_hbm, weights, small_sems.at[1]),
    )
    for copy in small:
        copy.start()

    @pl.loop(0, batches)
    def _(batch):
        for copy in copies(batch):
            copy.start()

    for copy in small:
        copy.wait()
    rows = jnp.concatenate([weights[...], jnp.zeros((size - batches, points), F32)], axis=0).T
    for batch in range(batches):
        columns[batch] = jnp.broadcast_to(rows[:, batch : batch + 1], (points, size))

    @pl.loop(0, batches)
    def _(batch):
        pltpu.make_async_copy(landed.at[batch], landed.at[batch], sems.at[batch]).wait()
        points_here = pl.ds(pl.multiple_of(batch * points, points), points)
        places = [pattern[s, batch] for s in range(blocks)]
        for array in range(2 + PARTS):
            wide[array] = landed[batch, array].astype(F32)
        for s, place in enumerate(places):
            strided = pl.ds(s, points, stride=blocks)
            values = wide[0, strided, :]
            field_out[batch, place] = values.astype(BF16)
            weighted[place, points_here, :] = (values * columns[batch]).astype(BF16)
            basis_out[batch, place] = wide[1, strided, :].astype(BF16)
            for c in range(PARTS):
                grads[c, place, points_here, :] = wide[2 + c, strided, :].astype(BF16)


def reorder(pattern, basis, field, basis_grad, weights, points, blocks):
    batches, rows, size = basis.shape
    hbm = pl.BlockSpec(memory_space=pl.ANY)
    vmem = pl.BlockSpec(memory_space=pltpu.VMEM)
    ordered = jax.ShapeDtypeStruct((batches, blocks, points, size), BF16)
    return pl.pallas_call(
        reorder_kernel,
        out_shape=(
            ordered,
            ordered,
            jax.ShapeDtypeStruct((blocks, batches * points, size), BF16),
            jax.ShapeDtypeStruct((PARTS, blocks, batches * points, size), BF16),
        ),
        in_specs=[hbm] * 5,
        out_specs=(vmem,) * 4,
        scratch_shapes=[
            pltpu.SMEM((blocks, batches), jnp.int32),
            pltpu.VMEM(weights.shape, F32),
            pltpu.VMEM((batches, points, size), F32),
            pltpu.VMEM((batches, 2 + PARTS, rows, size), BF16),
            pltpu.VMEM((2 + PARTS, rows, size), F32),
            pltpu.SemaphoreType.DMA((batches,)),
            pltpu.SemaphoreType.DMA((2,)),
        ],
        compiler_params=pltpu.CompilerParams(vmem_limit_bytes=VMEM_LIMIT),
        cost_estimate=pl.CostEstimate(
            flops=0, bytes_accessed=2 * (2 + PARTS) * batches * rows * size, transcendentals=0
        ),
    )(in_hbm(pattern.T), in_hbm(basis), in_hbm(field), in_hbm(basis_grad), in_hbm(weights))


def moment_terms(blocks):
    return [(p, c) for p in range(0, blocks, 2) for c in range(PARTS)]


def moment_term(weighted, grads, moments, p, c):
    blocks, _, size = grads.shape[1:]
    first, last = max(p - 1, 0), min(p + 3, blocks)
    left = jnp.concatenate([weighted[place] for place in range(first, last)], axis=1)
    right = jnp.concatenate([grads[c, p], grads[c, p + 1]], axis=1)
    moments[c, first * size : last * size, p * size : (p + 2) * size] = lax.dot_general(
        left, right, TN, preferred_element_type=F32
    )


def moment_kernel(weighted, grads, moments):
    for p, c in moment_terms(grads.shape[1])[:-1]:
        moment_term(weighted, grads, moments, p, c)


def build_moments(weighted, grads):
    blocks, depth, size = grads.shape[1:]
    vmem = pl.BlockSpec(memory_space=pltpu.VMEM)
    return pl.pallas_call(
        moment_kernel,
        out_shape=jax.ShapeDtypeStruct((PARTS, blocks * size, blocks * size), F32),
        in_specs=[vmem, vmem],
        out_specs=vmem,
        compiler_params=pltpu.CompilerParams(vmem_limit_bytes=VMEM_LIMIT),
        cost_estimate=pl.CostEstimate(
            flops=2 * PARTS * depth * (blocks * size) ** 2, bytes_accessed=0, transcendentals=0
        ),
    )(weighted, grads)


def atom_kernel(
    region, fn_atom, batch_atom, weight_grad, before, weighted, grads, hot, grad_columns, moments
):
    moment_term(weighted, grads, moments, *moment_terms(grads.shape[1])[-1])
    batches, points = weight_grad.shape[1:]
    size = fn_atom.shape[1]
    blocks = region.shape[1]
    me = lax.axis_index("grid")
    atoms = lax.broadcasted_iota(jnp.int32, (hot.shape[0], size), 0)
    ids = jnp.concatenate([batch_atom[...], jnp.full((1, size - batches), -1, jnp.int32)], axis=1)
    hot[:, blocks * size :] = jnp.where(atoms == ids, 1.0, 0.0).astype(BF16)

    @pl.loop(0, blocks)
    def _(position):
        ids = fn_atom[pl.ds(region[me, position], 1), :]
        columns = pl.ds(pl.multiple_of(position * size, size), size)
        hot[:, columns] = jnp.where(atoms == ids, 1.0, 0.0).astype(BF16)

    for c in range(PARTS):
        padding = jnp.zeros((size - batches, points), F32)
        grad_columns[c] = jnp.concatenate([weight_grad[c], padding], axis=0).T


def atom_matrix(region, fn_atom, batch_atom, weight_grad, moments, weighted, grads, blocks, size, atom_total):
    vmem = pl.BlockSpec(memory_space=pltpu.VMEM)
    return pl.pallas_call(
        atom_kernel,
        out_shape=(
            jax.ShapeDtypeStruct((atom_total, (blocks + 1) * size), BF16),
            jax.ShapeDtypeStruct((PARTS, weight_grad.shape[2], size), F32),
            jax.ShapeDtypeStruct(moments.shape, F32),
        ),
        in_specs=[pl.BlockSpec(memory_space=pltpu.SMEM)] + [vmem] * 6,
        out_specs=(vmem,) * 3,
        input_output_aliases={4: 2},
        compiler_params=pltpu.CompilerParams(vmem_limit_bytes=VMEM_LIMIT),
        cost_estimate=pl.CostEstimate(flops=1000000000, bytes_accessed=2 * atom_total * size, transcendentals=0),
    )(region, fn_atom.reshape(-1, size), batch_atom.reshape(1, -1), weight_grad, moments, weighted, grads)


def combine_kernel(
    region, basis, field, moments, hot, grad_columns, *rest, owner_rows, slabs, width
):
    *pieces, product_out, out, stage, matrix = rest
    batches, blocks, points, size = basis.shape
    me = lax.axis_index("grid")
    me_atoms = lax.axis_index("atoms")
    half = (width - 1) // 2
    stage_rows(stage, pieces[0], pieces[1 : 1 + slabs // 2], pieces[1 + slabs // 2 :], slabs)
    rows = [region[me, position] for position in range(blocks)]
    found = [owner_and_slot(region, me, position, owner_rows) for position in range(blocks)]
    totals = [[jnp.zeros((8, size), F32) for _ in range(blocks)] for _ in range(PARTS)]
    for p in range(blocks):
        owner, slot, count = found[p]
        first = jnp.bitwise_xor(me, owner) * TRAVEL
        for q in range(blocks):
            if abs(q - p) > half:
                matrix[p * size : (p + 1) * size, q * size : (q + 1) * size] = jnp.zeros((size, size), BF16)
                continue
            k = rows[q] - rows[p] + half
            place = jnp.where(
                k == 0,
                travel_place(slot, count, 0),
                jnp.where(k == 1, travel_place(slot, count, 1), travel_place(slot, count, 2)),
            )
            inside = jnp.logical_and(k >= 0, k < width)
            tile = jnp.where(inside, stage[first + place], jnp.zeros((size, size), BF16))
            matrix[p * size : (p + 1) * size, q * size : (q + 1) * size] = tile
            turned = tile.T.astype(F32)
            for c in range(PARTS):
                terms = turned * moments[c, q * size : (q + 1) * size, p * size : (p + 1) * size]
                totals[c][p] = totals[c][p] + jnp.sum(terms.reshape(-1, 8, size), axis=0)
    derivative = [
        jnp.concatenate([jnp.sum(total, axis=0, keepdims=True) for total in totals[c]], axis=1) for c in range(PARTS)
    ]

    energies = jnp.zeros((points, size), F32)
    lanes = lax.broadcasted_iota(jnp.int32, (points, size), 1)
    left = [jnp.concatenate([basis[batch, p] for p in range(blocks)], axis=1) for batch in range(batches)]
    left = jnp.concatenate(left, axis=0)
    energy = [jnp.zeros((points, size), F32) for _ in range(batches)]
    for q in range(0, blocks, 2):
        product = jnp.dot(left, matrix[:, q * size : (q + 2) * size], preferred_element_type=F32)
        for batch in range(batches):
            for column in range(2):
                part = product[batch * points : (batch + 1) * points, column * size : (column + 1) * size]
                product_out[batch, q + column] = part.astype(BF16)
                energy[batch] = energy[batch] + part * field[batch, q + column].astype(F32)
    for batch in range(batches):
        energies = jnp.where(lanes == batch, jnp.sum(energy[batch], axis=1, keepdims=True), energies)

    lefts = []
    for c in range(PARTS):
        term = jnp.sum(energies * grad_columns[c], axis=0, keepdims=True)
        lefts.append(jnp.concatenate([-2.0 * derivative[c], term], axis=1))
    left = jnp.concatenate(lefts, axis=0)
    high, middle, low = (piece.astype(F32) for piece in split(left))
    left = jnp.concatenate([high, middle, low, jnp.zeros((16 - 3 * PARTS, left.shape[1]), F32)], axis=0).astype(BF16)
    chunk = out.shape[-1]
    for device in range(out.shape[0]):
        sums = lax.dot_general(
            left, hot[device * chunk : (device + 1) * chunk, :], NT, preferred_element_type=F32
        )
        value = sums[:PARTS] + sums[PARTS : 2 * PARTS] + sums[2 * PARTS : 3 * PARTS]
        place = jnp.bitwise_xor(me_atoms, device)
        out[place, 0] = value
        out[jnp.bitwise_xor(place, 1), 1] = value


def combine(region, prepared, pieces, shapes):
    basis, field, moments, hot, grad_columns = prepared
    slabs, atom_devices, atom_total, points, blocks, width, owner_rows = shapes
    batches, _, _, size = basis.shape
    vmem = pl.BlockSpec(memory_space=pltpu.VMEM)
    return pl.pallas_call(
        functools.partial(combine_kernel, owner_rows=owner_rows, slabs=slabs, width=width),
        out_shape=(
            jax.ShapeDtypeStruct(basis.shape, BF16),
            jax.ShapeDtypeStruct((atom_devices, 2, PARTS, atom_total // atom_devices), F32),
        ),
        in_specs=[pl.BlockSpec(memory_space=pltpu.SMEM)] + [vmem] * (5 + len(pieces)),
        out_specs=(vmem, vmem),
        scratch_shapes=[
            pltpu.VMEM((slabs * TRAVEL, size, size), BF16),
            pltpu.VMEM((blocks * size, blocks * size), BF16),
        ],
        compiler_params=pltpu.CompilerParams(vmem_limit_bytes=VMEM_LIMIT),
    )(region, basis, field, moments, hot, grad_columns, *pieces)


def write_kernel(pattern, product, out, wide, staged, sems):
    batches, blocks, points, size = product.shape

    def copy(batch):
        return pltpu.make_async_copy(staged.at[batch], out.at[batch], sems.at[batch])

    @pl.loop(0, batches // 2)
    def _(pair):
        for inner in range(2):
            batch = pair * 2 + inner
            for t in range(blocks):
                wide[inner, pl.ds(t, points, stride=blocks), :] = product[batch, pattern[t, batch]].astype(F32)
            staged[batch] = wide[inner].astype(BF16)
            copy(batch).start()

    @pl.loop(0, batches)
    def _(batch):
        copy(batch).wait()


def write(pattern, product):
    batches, blocks, points, size = product.shape
    shape = (batches, points * blocks, size)
    return pl.pallas_call(
        write_kernel,
        out_shape=jax.ShapeDtypeStruct(shape, BF16),
        in_specs=[pl.BlockSpec(memory_space=pltpu.SMEM), pl.BlockSpec(memory_space=pltpu.VMEM)],
        out_specs=pl.BlockSpec(memory_space=pl.ANY),
        scratch_shapes=[
            pltpu.VMEM((2, points * blocks, size), F32),
            pltpu.VMEM(shape, BF16),
            pltpu.SemaphoreType.DMA((batches,)),
        ],
        compiler_params=pltpu.CompilerParams(vmem_limit_bytes=VMEM_LIMIT),
        cost_estimate=pl.CostEstimate(flops=0, bytes_accessed=4 * math.prod(shape), transcendentals=0),
    )(pattern.T, product)


def swap_between_cores(near, ready, atom_devices):
    far, ready = lax.optimization_barrier((near[1:], ready))
    near = [near[0], *far]
    swap = [(i, i ^ 1) for i in range(atom_devices)]
    return near, [lax.ppermute(piece, "atoms", swap) for piece in near[1:]], ready


def tree_sum(values):
    if len(values) == 1:
        return values[0]
    half = len(values) // 2
    return tree_sum(values[:half]) + tree_sum(values[half:])


def pair_sums(values):
    return [values[i] + values[i + 1] for i in range(0, len(values), 2)]


def sum_parts(partial_grad, contracted, slabs, atom_devices):
    parts = [partial_grad[0]]
    for d in range(1, atom_devices):
        parts.append(lax.ppermute(partial_grad[d], "atoms", [(i, i ^ d) for i in range(atom_devices)]))
    parts, contracted = lax.optimization_barrier((parts, contracted))
    both = tree_sum(pair_sums(parts))
    swap = [(i, i ^ 1) for i in range(atom_devices)]
    far = []
    for shifts in partners(slabs)[1:]:
        far.append(lax.ppermute(both, ("grid", "atoms"), moves_over_grid(shifts, slabs, atom_devices)))
    near = lax.ppermute(both[0], "grid", [(i, i ^ 1) for i in range(slabs)])
    far = lax.optimization_barrier(far)
    swapped = [lax.ppermute(piece[1], "atoms", swap) for piece in far]
    sums = [both[0] + near] + [piece[0] + other for piece, other in zip(far, swapped)]
    return tree_sum(sums), contracted


def local(
    basis,
    basis_grad,
    exchange_field,
    weights,
    weight_grad,
    density,
    region,
    pattern,
    fn_atom,
    batch_atom,
):
    batches, points, blocks, size = basis.shape
    owner_rows, width = density.shape[:2]
    slabs = lax.axis_size("grid")
    atom_devices = lax.axis_size("atoms")
    atom_total = fn_atom.shape[0] // (10 * slabs * atom_devices) * slabs * atom_devices
    shapes = (slabs, atom_devices, atom_total, points, blocks, width, owner_rows)
    flat_basis = basis.reshape(batches, points * blocks, size)
    flat_field = exchange_field.reshape(batches, points * blocks, size)
    flat_grad = basis_grad.reshape(PARTS, batches, points * blocks, size)
    own, near = fetch_rows(region, density, slabs, atom_devices)
    if region.shape[1] == blocks:
        basis_wide, field_wide, weighted, grads = reorder(
            pattern, flat_basis, flat_field, flat_grad, weights, points, blocks
        )
        ready = (basis_wide, field_wide, build_moments(weighted, grads), batch_atom)
        near, far, (basis_wide, field_wide, moments, batch_atom) = swap_between_cores(near, ready, atom_devices)
        hot, grad_columns, moments = atom_matrix(
            region, fn_atom, batch_atom, weight_grad, moments, weighted, grads, blocks, size, atom_total
        )
        ready = (basis_wide, field_wide, moments, hot, grad_columns)
        product, partial_grad = combine(region, ready, [own, *near, *far], shapes)
        gradient, contracted = sum_parts(partial_grad, write(pattern, product), slabs, atom_devices)
        return contracted.reshape(basis.shape), gradient
    ready = relayout(in_hbm(flat_basis), in_hbm(flat_field), points, blocks)
    near, far, (basis_wide, field_wide) = swap_between_cores(near, ready, atom_devices)
    tiles, partial_grad = partial_gradient(
        region,
        pattern,
        basis_wide,
        field_wide,
        in_hbm(flat_grad),
        weights,
        weight_grad,
        fn_atom,
        batch_atom,
        [own, *near, *far],
        shapes,
    )
    contracted = contract(region, pattern, basis_wide, tiles, points, blocks, width)
    gradient, contracted = sum_parts(partial_grad, contracted, slabs, atom_devices)
    return contracted.reshape(basis.shape), gradient


def solution(mesh):
    placed = (
        P(("groups", "grid", "atoms"), None, None, None),
        P(None, ("groups", "grid", "atoms"), None, None, None),
        P(("groups", "grid", "atoms"), None, None, None),
        P(("groups", "grid", "atoms"), None),
        P(None, ("groups", "grid", "atoms"), None),
        P(("groups", "grid"), None, None, None),
        P("groups", None),
        P(("groups", "grid", "atoms"), None),
        P("groups"),
        P(("groups", "grid", "atoms")),
    )
    return jax.shard_map(
        local,
        mesh=mesh,
        in_specs=placed,
        out_specs=(P(("groups", "grid", "atoms"), None, None, None), P(None, ("groups", "atoms"))),
        check_vma=False,
    )
```

```python
import functools
import math

import jax
import jax.numpy as jnp
from jax import lax
from jax.experimental import pallas as pl
from jax.experimental.pallas import tpu as pltpu
from jax.sharding import PartitionSpec as P

TRAVEL = 5
PARTS = 3
F32 = jnp.float32
BF16 = jnp.bfloat16
NT = (((1,), (1,)), ((), ()))
TN = (((0,), (0,)), ((), ()))
VMEM_LIMIT = 32 * 1024 * 1024


def owner_and_slot(region, slab, position, owner_rows):
    owner = lax.div(region[slab, position], owner_rows)
    slot = jnp.int32(0)
    count = jnp.int32(0)
    for other in range(region.shape[1]):
        same = jnp.where(lax.div(region[slab, other], owner_rows) == owner, 1, 0)
        count = count + same
        slot = slot + jnp.where(other < position, same, 0)
    return owner, slot, count


def travel_place(slot, count, k):
    if k == 0:
        return jnp.where(slot == 0, 4, 2)
    if k == 1:
        return jnp.where(slot == 0, 0, 3)
    return jnp.where(jnp.logical_and(slot == 0, count == 2), 1, 4)


def partners(slabs):
    return [(1, 1)] + [(shift + 1, shift) for shift in range(2, slabs, 2)]


def moves_over_grid(shifts, slabs, atom_devices):
    return [
        (z * atom_devices + a, (z ^ shifts[a % 2]) * atom_devices + a) for z in range(slabs) for a in range(atom_devices)
    ]


def send_kernel(region_hbm, density, *rest):
    *outs, region, held, region_sem, sems = rest
    fetch = pltpu.make_async_copy(region_hbm, region, region_sem)
    fetch.start()
    count_here = density.shape[0] // sems.shape[0]
    fetches = []
    for part in range(sems.shape[0]):
        here = pl.ds(part * count_here, count_here)
        fetches.append(pltpu.make_async_copy(density.at[here], held.at[here], sems.at[part]))
    for copy in fetches:
        copy.start()
    fetch.wait()
    me = lax.axis_index("grid")
    core = lax.rem(lax.axis_index("atoms"), 2)
    slabs, size = region.shape
    owner_rows = density.shape[0]
    picks = []
    for low, high in [(0, 0)] + partners(slabs):
        slab = jnp.bitwise_xor(me, jnp.where(core == 0, low, high))
        base = jnp.int32(owner_rows)
        count = jnp.int32(0)
        for position in range(size):
            row = region[slab, position] - me * owner_rows
            mine = jnp.logical_and(row >= 0, row < owner_rows)
            base = jnp.minimum(base, jnp.where(mine, row, owner_rows))
            count = count + jnp.where(mine, 1, 0)
        base = jnp.where(count == 0, 0, base)
        after = jnp.minimum(base + 1, owner_rows - 1)
        lower = base == 0
        edge = jnp.where(jnp.logical_and(count == 2, jnp.logical_not(lower)), after, base)
        picks.append(((base, 1), (base, 2), (after, 0), (after, 1), (edge, jnp.where(lower, 0, 2))))
    for copy in fetches:
        copy.wait()
    for out, places in zip(outs, picks):
        for place, (row, k) in enumerate(places):
            out[place] = held[row, k]


def in_hbm(array):
    return pltpu.with_memory_space_constraint(array, pltpu.HBM)


def rows_to_send(region, density, slabs):
    size = density.shape[-1]
    count = 1 + len(partners(slabs))
    hbm = pl.BlockSpec(memory_space=pl.ANY)
    return pl.pallas_call(
        send_kernel,
        out_shape=[jax.ShapeDtypeStruct((TRAVEL, size, size), density.dtype)] * count,
        in_specs=[hbm, hbm],
        out_specs=[pl.BlockSpec(memory_space=pltpu.VMEM)] * count,
        scratch_shapes=[
            pltpu.SMEM(region.shape, jnp.int32),
            pltpu.VMEM(density.shape, density.dtype),
            pltpu.SemaphoreType.DMA,
            pltpu.SemaphoreType.DMA((5 if density.shape[0] % 5 == 0 else 1,)),
        ],
        compiler_params=pltpu.CompilerParams(vmem_limit_bytes=VMEM_LIMIT),
    )(in_hbm(region), in_hbm(density))


def fetch_rows(region, density, slabs, atom_devices):
    own, *outgoing = rows_to_send(region, density, slabs)
    near = []
    for shifts, piece in zip(partners(slabs), outgoing):
        near.append(lax.ppermute(piece, ("grid", "atoms"), moves_over_grid(shifts, slabs, atom_devices)))
    return own, near


def stage_rows(stage, own, near, far, slabs):
    core = lax.rem(lax.axis_index("atoms"), 2)
    first, *pairs = partners(slabs)
    for place in range(TRAVEL):
        stage[place] = own[place]
        stage[first[0] * TRAVEL + place] = near[0][place]
    for (low, high), here, there in zip(pairs, near[1:], far):
        mine = jnp.where(core == 0, low, high) * TRAVEL
        other = jnp.where(core == 0, high, low) * TRAVEL
        for place in range(TRAVEL):
            stage[mine + place] = here[place]
            stage[other + place] = there[place]


def block_major(x_ref, wide, points, blocks):
    wide[...] = x_ref[0].astype(F32)
    return [wide[pl.ds(s, points, stride=blocks), :] for s in range(blocks)]


def relayout_kernel(basis, field, basis_out, field_out, wide, *, points, blocks):
    size = basis.shape[-1]
    for source, target in ((basis, basis_out), (field, field_out)):
        for s, part in enumerate(block_major(source, wide, points, blocks)):
            target[0, :, s * size : (s + 1) * size] = part.astype(BF16)


def relayout(basis, field, points, blocks):
    batches, rows, size = basis.shape
    here = pl.BlockSpec((1, rows, size), lambda b: (b, 0, 0))
    there = pl.BlockSpec((1, points, blocks * size), lambda b: (b, 0, 0))
    shape = jax.ShapeDtypeStruct((batches, points, blocks * size), BF16)
    return pl.pallas_call(
        functools.partial(relayout_kernel, points=points, blocks=blocks),
        grid=(batches,),
        out_shape=(shape, shape),
        in_specs=[here, here],
        out_specs=(there, there),
        scratch_shapes=[pltpu.VMEM((rows, size), F32)],
        compiler_params=pltpu.CompilerParams(vmem_limit_bytes=VMEM_LIMIT),
        cost_estimate=pl.CostEstimate(flops=0, bytes_accessed=8 * batches * rows * size, transcendentals=0),
    )(basis, field)


def batch_matrix(region, pattern, tiles, slab, batch, blocks, width):
    half = (width - 1) // 2
    none = tiles.shape[0] - 1
    places = [pattern[batch, s] for s in range(blocks)]
    rows = [region[slab, place] for place in places]
    strips = []
    for s in range(blocks):
        strip = []
        for t in range(blocks):
            k = rows[t] - rows[s] + half
            inside = jnp.logical_and(k >= 0, k < width)
            strip.append(tiles[jnp.where(inside, places[s] * width + k, none)])
        strips.append(jnp.concatenate(strip, axis=1))
    return jnp.concatenate(strips, axis=0)


def split(values):
    high = values.astype(BF16)
    rest = values - high.astype(F32)
    middle = rest.astype(BF16)
    low = (rest - middle.astype(F32)).astype(BF16)
    return high, middle, low


def gradient_kernel(
    region,
    pattern,
    basis,
    field,
    basis_grad,
    weights,
    weight_grad,
    fn_atom,
    batch_atom,
    places,
    *rest,
    points,
    blocks,
    width,
    owner_rows,
    slabs,
):
    *pieces, tiles, out, stage, spread, sums, energy_sums = rest
    batch = pl.program_id(0)
    batches = pl.num_programs(0)
    me = lax.axis_index("grid")
    me_atoms = lax.axis_index("atoms")
    size = tiles.shape[-1]
    region_size = region.shape[1]

    @pl.when(batch == 0)
    def _():
        tiles[region_size * width] = jnp.zeros((size, size), BF16)
        stage_rows(stage, pieces[0], pieces[1 : 1 + slabs // 2], pieces[1 + slabs // 2 :], slabs)
        for position in range(region_size):
            owner, slot, count = owner_and_slot(region, me, position, owner_rows)
            shift = jnp.bitwise_xor(me, owner)
            for k in range(width):
                tiles[position * width + k] = stage[shift * TRAVEL + travel_place(slot, count, k)]

    matrix = batch_matrix(region, pattern, tiles, me, batch, blocks, width)
    potential = lax.dot_general(field[0], matrix, NT, preferred_element_type=F32)
    rows = jnp.concatenate(
        [weights[pl.ds(batch, 1), :]]
        + [weight_grad[c, pl.ds(batch, 1), :] for c in range(PARTS)]
        + [jnp.zeros((8 - 1 - PARTS, points), F32)],
        axis=0,
    )
    columns = rows.T
    weight = columns[:, 0:1]
    energy = jnp.zeros((points, size), F32)
    for s in range(blocks):
        here = potential[:, s * size : (s + 1) * size]
        energy = energy + basis[0, :, s * size : (s + 1) * size].astype(F32) * here
        spread[pl.ds(s, points, stride=blocks), :] = here * weight
    scaled = spread[...]
    place = pl.ds(pl.multiple_of(batch * 8, 8), 8)
    for c in range(PARTS):
        terms = basis_grad[c, 0].astype(F32) * scaled
        sums[c, place, :] = jnp.sum(terms.reshape(-1, 8, size), axis=0)
        terms = energy * columns[:, 1 + c : 2 + c]
        energy_sums[c, place, :] = jnp.sum(terms.reshape(-1, 8, size), axis=0)

    @pl.when(batch == batches - 1)
    def _():
        padded = max(8, region_size)
        chosen = lax.broadcasted_iota(jnp.int32, (padded, places.shape[1]), 0) == places[...]
        chosen = chosen.astype(BF16)
        blocks_sum = []
        for c in range(PARTS):
            total = jnp.zeros((padded, size), F32)
            for piece in split(sums[c]):
                total = total + jnp.dot(chosen, piece, preferred_element_type=F32)
            blocks_sum.append(-2.0 * total)
        lefts = []
        for position in range(region_size):
            stack = jnp.concatenate([total[position : position + 1] for total in blocks_sum], axis=0)
            high, middle, low = (piece.astype(F32) for piece in split(stack))
            lefts.append(jnp.concatenate([high, middle, low, jnp.zeros((16 - 3 * PARTS, size), F32)], axis=0))
        left = jnp.concatenate(lefts, axis=1).astype(BF16)
        chunk = out.shape[-1]
        scale = [jnp.sum(energy_sums[c], axis=1, keepdims=True) for c in range(PARTS)]
        for device in range(out.shape[0]):
            atoms = lax.broadcasted_iota(jnp.int32, (chunk, size), 0) + device * chunk
            hot = [
                jnp.where(atoms == fn_atom[pl.ds(region[me, position], 1), :], 1.0, 0.0).astype(BF16)
                for position in range(region_size)
            ]
            found = lax.dot_general(left, jnp.concatenate(hot, axis=1), NT, preferred_element_type=F32)
            atoms = lax.broadcasted_iota(jnp.int32, (batch_atom.shape[0], chunk), 1) + device * chunk
            mine = atoms == batch_atom[...]
            for c in range(PARTS):
                value = found[c : c + 1] + found[PARTS + c : PARTS + c + 1] + found[2 * PARTS + c : 2 * PARTS + c + 1]
                value = value + jnp.sum(jnp.where(mine, scale[c], 0.0), axis=0, keepdims=True)
                place = jnp.bitwise_xor(me_atoms, device)
                out[place, 0, c : c + 1, :] = value
                out[jnp.bitwise_xor(place, 1), 1, c : c + 1, :] = value


def partial_gradient(
    region, pattern, basis, field, basis_grad, weights, weight_grad, fn_atom, batch_atom, pieces, shapes
):
    slabs, atom_devices, atom_total, points, blocks, width, owner_rows = shapes
    batches, _, columns = basis.shape
    size = columns // blocks
    region_size = region.shape[1]
    fn_atom = fn_atom.reshape(-1, size)
    places = jnp.broadcast_to(pattern[:, None, :], (batches, 8 // blocks, blocks)).reshape(1, -1)
    batch_atom = jnp.broadcast_to(batch_atom[:, None], (batches, 8)).reshape(-1, 1)
    block = pl.BlockSpec((1, points, columns), lambda b, *_: (b, 0, 0))
    whole = pl.BlockSpec(memory_space=pltpu.VMEM)
    tile_shape = (region_size * width + 1, size, size)
    out_shape = (atom_devices, 2, PARTS, atom_total // atom_devices)
    return pl.pallas_call(
        functools.partial(
            gradient_kernel, points=points, blocks=blocks, width=width, owner_rows=owner_rows, slabs=slabs
        ),
        grid_spec=pltpu.PrefetchScalarGridSpec(
            num_scalar_prefetch=2,
            grid=(batches,),
            in_specs=[
                block,
                block,
                pl.BlockSpec((PARTS, 1, points * blocks, size), lambda b, *_: (0, b, 0, 0)),
            ]
            + [whole] * (5 + len(pieces)),
            out_specs=(whole, whole),
            scratch_shapes=[
                pltpu.VMEM((slabs * TRAVEL, size, size), BF16),
                pltpu.VMEM((points * blocks, size), F32),
                pltpu.VMEM((PARTS, batches * 8, size), F32),
                pltpu.VMEM((PARTS, batches * 8, size), F32),
            ],
        ),
        out_shape=(jax.ShapeDtypeStruct(tile_shape, BF16), jax.ShapeDtypeStruct(out_shape, F32)),
        compiler_params=pltpu.CompilerParams(vmem_limit_bytes=VMEM_LIMIT),
    )(region, pattern, basis, field, basis_grad, weights, weight_grad, fn_atom, batch_atom, places, *pieces)


def product_kernel(region, pattern, basis, tiles, out, spread, *, points, blocks, width):
    me = lax.axis_index("grid")
    size = tiles.shape[-1]
    matrix = batch_matrix(region, pattern, tiles, me, pl.program_id(0), blocks, width)
    product = jnp.dot(basis[0], matrix, preferred_element_type=F32)
    for t in range(blocks):
        spread[pl.ds(t, points, stride=blocks), :] = product[:, t * size : (t + 1) * size]
    out[0] = spread[...].astype(BF16)


def contract(region, pattern, basis, tiles, points, blocks, width):
    batches, _, columns = basis.shape
    size = columns // blocks
    return pl.pallas_call(
        functools.partial(product_kernel, points=points, blocks=blocks, width=width),
        grid_spec=pltpu.PrefetchScalarGridSpec(
            num_scalar_prefetch=2,
            grid=(batches,),
            in_specs=[
                pl.BlockSpec((1, points, columns), lambda b, *_: (b, 0, 0)),
                pl.BlockSpec(memory_space=pltpu.VMEM),
            ],
            out_specs=pl.BlockSpec((1, points * blocks, size), lambda b, *_: (b, 0, 0)),
            scratch_shapes=[pltpu.VMEM((points * blocks, size), F32)],
        ),
        out_shape=jax.ShapeDtypeStruct((batches, points * blocks, size), BF16),
        compiler_params=pltpu.CompilerParams(vmem_limit_bytes=VMEM_LIMIT),
        cost_estimate=pl.CostEstimate(
            flops=2 * batches * points * columns * columns,
            bytes_accessed=4 * batches * points * columns,
            transcendentals=0,
        ),
    )(region, pattern, basis, tiles)


def reorder_kernel(
    pattern_hbm,
    basis,
    field,
    basis_grad,
    weights_hbm,
    basis_out,
    field_out,
    weighted,
    grads,
    pattern,
    weights,
    columns,
    landed,
    wide,
    sems,
    small_sems,
):
    batches, blocks, points, size = basis_out.shape

    def copies(batch):
        return (
            pltpu.make_async_copy(field.at[batch], landed.at[batch, 0], sems.at[batch]),
            pltpu.make_async_copy(basis.at[batch], landed.at[batch, 1], sems.at[batch]),
            pltpu.make_async_copy(basis_grad.at[:, batch], landed.at[batch, pl.ds(2, PARTS)], sems.at[batch]),
        )

    small = (
        pltpu.make_async_copy(pattern_hbm, pattern, small_sems.at[0]),
        pltpu.make_async_copy(weights_hbm, weights, small_sems.at[1]),
    )
    for copy in small:
        copy.start()

    @pl.loop(0, batches)
    def _(batch):
        for copy in copies(batch):
            copy.start()

    for copy in small:
        copy.wait()
    rows = jnp.concatenate([weights[...], jnp.zeros((size - batches, points), F32)], axis=0).T
    for batch in range(batches):
        columns[batch] = jnp.broadcast_to(rows[:, batch : batch + 1], (points, size))

    @pl.loop(0, batches)
    def _(batch):
        pltpu.make_async_copy(landed.at[batch], landed.at[batch], sems.at[batch]).wait()
        points_here = pl.ds(pl.multiple_of(batch * points, points), points)
        places = [pattern[s, batch] for s in range(blocks)]
        for array in range(2 + PARTS):
            wide[array] = landed[batch, array].astype(F32)
        for s, place in enumerate(places):
            strided = pl.ds(s, points, stride=blocks)
            values = wide[0, strided, :]
            field_out[batch, place] = values.astype(BF16)
            weighted[place, points_here, :] = (values * columns[batch]).astype(BF16)
            basis_out[batch, place] = wide[1, strided, :].astype(BF16)
            for c in range(PARTS):
                grads[c, place, points_here, :] = wide[2 + c, strided, :].astype(BF16)


def reorder(pattern, basis, field, basis_grad, weights, points, blocks):
    batches, rows, size = basis.shape
    hbm = pl.BlockSpec(memory_space=pl.ANY)
    vmem = pl.BlockSpec(memory_space=pltpu.VMEM)
    ordered = jax.ShapeDtypeStruct((batches, blocks, points, size), BF16)
    return pl.pallas_call(
        reorder_kernel,
        out_shape=(
            ordered,
            ordered,
            jax.ShapeDtypeStruct((blocks, batches * points, size), BF16),
            jax.ShapeDtypeStruct((PARTS, blocks, batches * points, size), BF16),
        ),
        in_specs=[hbm] * 5,
        out_specs=(vmem,) * 4,
        scratch_shapes=[
            pltpu.SMEM((blocks, batches), jnp.int32),
            pltpu.VMEM(weights.shape, F32),
            pltpu.VMEM((batches, points, size), F32),
            pltpu.VMEM((batches, 2 + PARTS, rows, size), BF16),
            pltpu.VMEM((2 + PARTS, rows, size), F32),
            pltpu.SemaphoreType.DMA((batches,)),
            pltpu.SemaphoreType.DMA((2,)),
        ],
        compiler_params=pltpu.CompilerParams(vmem_limit_bytes=VMEM_LIMIT),
        cost_estimate=pl.CostEstimate(
            flops=0, bytes_accessed=2 * (2 + PARTS) * batches * rows * size, transcendentals=0
        ),
    )(in_hbm(pattern.T), in_hbm(basis), in_hbm(field), in_hbm(basis_grad), in_hbm(weights))


def moment_terms(blocks):
    return [(p, c) for p in range(0, blocks, 2) for c in range(PARTS)]


def moment_term(weighted, grads, moments, p, c):
    blocks, _, size = grads.shape[1:]
    first, last = max(p - 1, 0), min(p + 3, blocks)
    left = jnp.concatenate([weighted[place] for place in range(first, last)], axis=1)
    right = jnp.concatenate([grads[c, p], grads[c, p + 1]], axis=1)
    moments[c, first * size : last * size, p * size : (p + 2) * size] = lax.dot_general(
        left, right, TN, preferred_element_type=F32
    )


def moment_kernel(weighted, grads, moments):
    for p, c in moment_terms(grads.shape[1])[:-1]:
        moment_term(weighted, grads, moments, p, c)


def build_moments(weighted, grads):
    blocks, depth, size = grads.shape[1:]
    vmem = pl.BlockSpec(memory_space=pltpu.VMEM)
    return pl.pallas_call(
        moment_kernel,
        out_shape=jax.ShapeDtypeStruct((PARTS, blocks * size, blocks * size), F32),
        in_specs=[vmem, vmem],
        out_specs=vmem,
        compiler_params=pltpu.CompilerParams(vmem_limit_bytes=VMEM_LIMIT),
        cost_estimate=pl.CostEstimate(
            flops=2 * PARTS * depth * (blocks * size) ** 2, bytes_accessed=0, transcendentals=0
        ),
    )(weighted, grads)


def atom_kernel(
    region, fn_atom, batch_atom, weight_grad, before, weighted, grads, hot, grad_columns, moments
):
    moment_term(weighted, grads, moments, *moment_terms(grads.shape[1])[-1])
    batches, points = weight_grad.shape[1:]
    size = fn_atom.shape[1]
    blocks = region.shape[1]
    me = lax.axis_index("grid")
    atoms = lax.broadcasted_iota(jnp.int32, (hot.shape[0], size), 0)
    ids = jnp.concatenate([batch_atom[...], jnp.full((1, size - batches), -1, jnp.int32)], axis=1)
    hot[:, blocks * size :] = jnp.where(atoms == ids, 1.0, 0.0).astype(BF16)

    @pl.loop(0, blocks)
    def _(position):
        ids = fn_atom[pl.ds(region[me, position], 1), :]
        columns = pl.ds(pl.multiple_of(position * size, size), size)
        hot[:, columns] = jnp.where(atoms == ids, 1.0, 0.0).astype(BF16)

    for c in range(PARTS):
        padding = jnp.zeros((size - batches, points), F32)
        grad_columns[c] = jnp.concatenate([weight_grad[c], padding], axis=0).T


def atom_matrix(region, fn_atom, batch_atom, weight_grad, moments, weighted, grads, blocks, size, atom_total):
    vmem = pl.BlockSpec(memory_space=pltpu.VMEM)
    return pl.pallas_call(
        atom_kernel,
        out_shape=(
            jax.ShapeDtypeStruct((atom_total, (blocks + 1) * size), BF16),
            jax.ShapeDtypeStruct((PARTS, weight_grad.shape[2], size), F32),
            jax.ShapeDtypeStruct(moments.shape, F32),
        ),
        in_specs=[pl.BlockSpec(memory_space=pltpu.SMEM)] + [vmem] * 6,
        out_specs=(vmem,) * 3,
        input_output_aliases={4: 2},
        compiler_params=pltpu.CompilerParams(vmem_limit_bytes=VMEM_LIMIT),
        cost_estimate=pl.CostEstimate(flops=1000000000, bytes_accessed=2 * atom_total * size, transcendentals=0),
    )(region, fn_atom.reshape(-1, size), batch_atom.reshape(1, -1), weight_grad, moments, weighted, grads)


def combine_kernel(
    region, basis, field, moments, hot, grad_columns, *rest, owner_rows, slabs, width
):
    *pieces, product_out, out, stage, matrix = rest
    batches, blocks, points, size = basis.shape
    me = lax.axis_index("grid")
    me_atoms = lax.axis_index("atoms")
    half = (width - 1) // 2
    stage_rows(stage, pieces[0], pieces[1 : 1 + slabs // 2], pieces[1 + slabs // 2 :], slabs)
    rows = [region[me, position] for position in range(blocks)]
    found = [owner_and_slot(region, me, position, owner_rows) for position in range(blocks)]
    totals = [[jnp.zeros((8, size), F32) for _ in range(blocks)] for _ in range(PARTS)]
    for p in range(blocks):
        owner, slot, count = found[p]
        first = jnp.bitwise_xor(me, owner) * TRAVEL
        for q in range(blocks):
            if abs(q - p) > half:
                matrix[p * size : (p + 1) * size, q * size : (q + 1) * size] = jnp.zeros((size, size), BF16)
                continue
            k = rows[q] - rows[p] + half
            place = jnp.where(
                k == 0,
                travel_place(slot, count, 0),
                jnp.where(k == 1, travel_place(slot, count, 1), travel_place(slot, count, 2)),
            )
            inside = jnp.logical_and(k >= 0, k < width)
            tile = jnp.where(inside, stage[first + place], jnp.zeros((size, size), BF16))
            matrix[p * size : (p + 1) * size, q * size : (q + 1) * size] = tile
            turned = tile.T.astype(F32)
            for c in range(PARTS):
                terms = turned * moments[c, q * size : (q + 1) * size, p * size : (p + 1) * size]
                totals[c][p] = totals[c][p] + jnp.sum(terms.reshape(-1, 8, size), axis=0)
    derivative = [
        jnp.concatenate([jnp.sum(total, axis=0, keepdims=True) for total in totals[c]], axis=1) for c in range(PARTS)
    ]

    energies = jnp.zeros((points, size), F32)
    lanes = lax.broadcasted_iota(jnp.int32, (points, size), 1)
    left = [jnp.concatenate([basis[batch, p] for p in range(blocks)], axis=1) for batch in range(batches)]
    left = jnp.concatenate(left, axis=0)
    energy = [jnp.zeros((points, size), F32) for _ in range(batches)]
    for q in range(0, blocks, 2):
        product = jnp.dot(left, matrix[:, q * size : (q + 2) * size], preferred_element_type=F32)
        for batch in range(batches):
            for column in range(2):
                part = product[batch * points : (batch + 1) * points, column * size : (column + 1) * size]
                product_out[batch, q + column] = part.astype(BF16)
                energy[batch] = energy[batch] + part * field[batch, q + column].astype(F32)
    for batch in range(batches):
        energies = jnp.where(lanes == batch, jnp.sum(energy[batch], axis=1, keepdims=True), energies)

    lefts = []
    for c in range(PARTS):
        term = jnp.sum(energies * grad_columns[c], axis=0, keepdims=True)
        lefts.append(jnp.concatenate([-2.0 * derivative[c], term], axis=1))
    left = jnp.concatenate(lefts, axis=0)
    high, middle, low = (piece.astype(F32) for piece in split(left))
    left = jnp.concatenate([high, middle, low, jnp.zeros((16 - 3 * PARTS, left.shape[1]), F32)], axis=0).astype(BF16)
    chunk = out.shape[-1]
    for device in range(out.shape[0]):
        sums = lax.dot_general(
            left, hot[device * chunk : (device + 1) * chunk, :], NT, preferred_element_type=F32
        )
        value = sums[:PARTS] + sums[PARTS : 2 * PARTS] + sums[2 * PARTS : 3 * PARTS]
        place = jnp.bitwise_xor(me_atoms, device)
        out[place, 0] = value
        out[jnp.bitwise_xor(place, 1), 1] = value


def combine(region, prepared, pieces, shapes):
    basis, field, moments, hot, grad_columns = prepared
    slabs, atom_devices, atom_total, points, blocks, width, owner_rows = shapes
    batches, _, _, size = basis.shape
    vmem = pl.BlockSpec(memory_space=pltpu.VMEM)
    return pl.pallas_call(
        functools.partial(combine_kernel, owner_rows=owner_rows, slabs=slabs, width=width),
        out_shape=(
            jax.ShapeDtypeStruct(basis.shape, BF16),
            jax.ShapeDtypeStruct((atom_devices, 2, PARTS, atom_total // atom_devices), F32),
        ),
        in_specs=[pl.BlockSpec(memory_space=pltpu.SMEM)] + [vmem] * (5 + len(pieces)),
        out_specs=(vmem, vmem),
        scratch_shapes=[
            pltpu.VMEM((slabs * TRAVEL, size, size), BF16),
            pltpu.VMEM((blocks * size, blocks * size), BF16),
        ],
        compiler_params=pltpu.CompilerParams(vmem_limit_bytes=VMEM_LIMIT),
    )(region, basis, field, moments, hot, grad_columns, *pieces)


def write_kernel(pattern, product, out, wide, staged, sems):
    batches, blocks, points, size = product.shape

    def copy(batch):
        return pltpu.make_async_copy(staged.at[batch], out.at[batch], sems.at[batch])

    @pl.loop(0, batches // 2)
    def _(pair):
        for inner in range(2):
            batch = pair * 2 + inner
            for t in range(blocks):
                wide[inner, pl.ds(t, points, stride=blocks), :] = product[batch, pattern[t, batch]].astype(F32)
            staged[batch] = wide[inner].astype(BF16)
            copy(batch).start()

    @pl.loop(0, batches)
    def _(batch):
        copy(batch).wait()


def write(pattern, product):
    batches, blocks, points, size = product.shape
    shape = (batches, points * blocks, size)
    return pl.pallas_call(
        write_kernel,
        out_shape=jax.ShapeDtypeStruct(shape, BF16),
        in_specs=[pl.BlockSpec(memory_space=pltpu.SMEM), pl.BlockSpec(memory_space=pltpu.VMEM)],
        out_specs=pl.BlockSpec(memory_space=pl.ANY),
        scratch_shapes=[
            pltpu.VMEM((2, points * blocks, size), F32),
            pltpu.VMEM(shape, BF16),
            pltpu.SemaphoreType.DMA((batches,)),
        ],
        compiler_params=pltpu.CompilerParams(vmem_limit_bytes=VMEM_LIMIT),
        cost_estimate=pl.CostEstimate(flops=0, bytes_accessed=4 * math.prod(shape), transcendentals=0),
    )(pattern.T, product)


def swap_between_cores(near, ready, atom_devices):
    far, ready = lax.optimization_barrier((near[1:], ready))
    near = [near[0], *far]
    swap = [(i, i ^ 1) for i in range(atom_devices)]
    return near, [lax.ppermute(piece, "atoms", swap) for piece in near[1:]], ready


def tree_sum(values):
    if len(values) == 1:
        return values[0]
    half = len(values) // 2
    return tree_sum(values[:half]) + tree_sum(values[half:])


def pair_sums(values):
    return [values[i] + values[i + 1] for i in range(0, len(values), 2)]


def sum_parts(partial_grad, contracted, slabs, atom_devices):
    parts = [partial_grad[0]]
    for d in range(1, atom_devices):
        parts.append(lax.ppermute(partial_grad[d], "atoms", [(i, i ^ d) for i in range(atom_devices)]))
    parts, contracted = lax.optimization_barrier((parts[::-1], contracted))
    parts = parts[::-1]
    both = tree_sum(pair_sums(parts))
    swap = [(i, i ^ 1) for i in range(atom_devices)]
    far = []
    for shifts in partners(slabs)[1:]:
        far.append(lax.ppermute(both, ("grid", "atoms"), moves_over_grid(shifts, slabs, atom_devices)))
    near = lax.ppermute(both[0], "grid", [(i, i ^ 1) for i in range(slabs)])
    far = lax.optimization_barrier(far)
    swapped = [lax.ppermute(piece[1], "atoms", swap) for piece in far]
    sums = [both[0] + near] + [piece[0] + other for piece, other in zip(far, swapped)]
    return tree_sum(sums), contracted


def local(
    basis,
    basis_grad,
    exchange_field,
    weights,
    weight_grad,
    density,
    region,
    pattern,
    fn_atom,
    batch_atom,
):
    batches, points, blocks, size = basis.shape
    owner_rows, width = density.shape[:2]
    slabs = lax.axis_size("grid")
    atom_devices = lax.axis_size("atoms")
    atom_total = fn_atom.shape[0] // (10 * slabs * atom_devices) * slabs * atom_devices
    shapes = (slabs, atom_devices, atom_total, points, blocks, width, owner_rows)
    flat_basis = basis.reshape(batches, points * blocks, size)
    flat_field = exchange_field.reshape(batches, points * blocks, size)
    flat_grad = basis_grad.reshape(PARTS, batches, points * blocks, size)
    own, near = fetch_rows(region, density, slabs, atom_devices)
    if region.shape[1] == blocks:
        basis_wide, field_wide, weighted, grads = reorder(
            pattern, flat_basis, flat_field, flat_grad, weights, points, blocks
        )
        ready = (basis_wide, field_wide, build_moments(weighted, grads), batch_atom)
        near, far, (basis_wide, field_wide, moments, batch_atom) = swap_between_cores(near, ready, atom_devices)
        hot, grad_columns, moments = atom_matrix(
            region, fn_atom, batch_atom, weight_grad, moments, weighted, grads, blocks, size, atom_total
        )
        ready = (basis_wide, field_wide, moments, hot, grad_columns)
        product, partial_grad = combine(region, ready, [own, *near, *far], shapes)
        gradient, contracted = sum_parts(partial_grad, write(pattern, product), slabs, atom_devices)
        return contracted.reshape(basis.shape), gradient
    ready = relayout(in_hbm(flat_basis), in_hbm(flat_field), points, blocks)
    near, far, (basis_wide, field_wide) = swap_between_cores(near, ready, atom_devices)
    tiles, partial_grad = partial_gradient(
        region,
        pattern,
        basis_wide,
        field_wide,
        in_hbm(flat_grad),
        weights,
        weight_grad,
        fn_atom,
        batch_atom,
        [own, *near, *far],
        shapes,
    )
    contracted = contract(region, pattern, basis_wide, tiles, points, blocks, width)
    gradient, contracted = sum_parts(partial_grad, contracted, slabs, atom_devices)
    return contracted.reshape(basis.shape), gradient


def solution(mesh):
    placed = (
        P(("groups", "grid", "atoms"), None, None, None),
        P(None, ("groups", "grid", "atoms"), None, None, None),
        P(("groups", "grid", "atoms"), None, None, None),
        P(("groups", "grid", "atoms"), None),
        P(None, ("groups", "grid", "atoms"), None),
        P(("groups", "grid"), None, None, None),
        P("groups", None),
        P(("groups", "grid", "atoms"), None),
        P("groups"),
        P(("groups", "grid", "atoms")),
    )
    return jax.shard_map(
        local,
        mesh=mesh,
        in_specs=placed,
        out_specs=(P(("groups", "grid", "atoms"), None, None, None), P(None, ("groups", "atoms"))),
        check_vma=False,
    )
```

```python
import functools
import math

import jax
import jax.numpy as jnp
from jax import lax
from jax.experimental import pallas as pl
from jax.experimental.pallas import tpu as pltpu
from jax.sharding import PartitionSpec as P

TRAVEL = 5
PARTS = 3
F32 = jnp.float32
BF16 = jnp.bfloat16
NT = (((1,), (1,)), ((), ()))
TN = (((0,), (0,)), ((), ()))
VMEM_LIMIT = 32 * 1024 * 1024


def owner_and_slot(region, slab, position, owner_rows):
    owner = lax.div(region[slab, position], owner_rows)
    slot = jnp.int32(0)
    count = jnp.int32(0)
    for other in range(region.shape[1]):
        same = jnp.where(lax.div(region[slab, other], owner_rows) == owner, 1, 0)
        count = count + same
        slot = slot + jnp.where(other < position, same, 0)
    return owner, slot, count


def travel_place(slot, count, k):
    if k == 0:
        return jnp.where(slot == 0, 4, 2)
    if k == 1:
        return jnp.where(slot == 0, 0, 3)
    return jnp.where(jnp.logical_and(slot == 0, count == 2), 1, 4)


def partners(slabs):
    return [(1, 1)] + [(shift + 1, shift) for shift in range(2, slabs, 2)]


def moves_over_grid(shifts, slabs, atom_devices):
    return [
        (z * atom_devices + a, (z ^ shifts[a % 2]) * atom_devices + a) for z in range(slabs) for a in range(atom_devices)
    ]


def send_kernel(region_hbm, density, *rest):
    *outs, region, held, region_sem, sems = rest
    fetch = pltpu.make_async_copy(region_hbm, region, region_sem)
    fetch.start()
    count_here = density.shape[0] // sems.shape[0]
    fetches = []
    for part in range(sems.shape[0]):
        here = pl.ds(part * count_here, count_here)
        fetches.append(pltpu.make_async_copy(density.at[here], held.at[here], sems.at[part]))
    for copy in fetches:
        copy.start()
    fetch.wait()
    me = lax.axis_index("grid")
    core = lax.rem(lax.axis_index("atoms"), 2)
    slabs, size = region.shape
    owner_rows = density.shape[0]
    picks = []
    for low, high in [(0, 0)] + partners(slabs):
        slab = jnp.bitwise_xor(me, jnp.where(core == 0, low, high))
        base = jnp.int32(owner_rows)
        count = jnp.int32(0)
        for position in range(size):
            row = region[slab, position] - me * owner_rows
            mine = jnp.logical_and(row >= 0, row < owner_rows)
            base = jnp.minimum(base, jnp.where(mine, row, owner_rows))
            count = count + jnp.where(mine, 1, 0)
        base = jnp.where(count == 0, 0, base)
        after = jnp.minimum(base + 1, owner_rows - 1)
        lower = base == 0
        edge = jnp.where(jnp.logical_and(count == 2, jnp.logical_not(lower)), after, base)
        picks.append(((base, 1), (base, 2), (after, 0), (after, 1), (edge, jnp.where(lower, 0, 2))))
    for copy in fetches:
        copy.wait()
    for out, places in zip(outs, picks):
        for place, (row, k) in enumerate(places):
            out[place] = held[row, k]


def in_hbm(array):
    return pltpu.with_memory_space_constraint(array, pltpu.HBM)


def rows_to_send(region, density, slabs):
    size = density.shape[-1]
    count = 1 + len(partners(slabs))
    hbm = pl.BlockSpec(memory_space=pl.ANY)
    return pl.pallas_call(
        send_kernel,
        out_shape=[jax.ShapeDtypeStruct((TRAVEL, size, size), density.dtype)] * count,
        in_specs=[hbm, hbm],
        out_specs=[pl.BlockSpec(memory_space=pltpu.VMEM)] * count,
        scratch_shapes=[
            pltpu.SMEM(region.shape, jnp.int32),
            pltpu.VMEM(density.shape, density.dtype),
            pltpu.SemaphoreType.DMA,
            pltpu.SemaphoreType.DMA((5 if density.shape[0] % 5 == 0 else 1,)),
        ],
        compiler_params=pltpu.CompilerParams(vmem_limit_bytes=VMEM_LIMIT),
    )(in_hbm(region), in_hbm(density))


def fetch_rows(region, density, slabs, atom_devices):
    own, *outgoing = rows_to_send(region, density, slabs)
    near = []
    for shifts, piece in zip(partners(slabs), outgoing):
        near.append(lax.ppermute(piece, ("grid", "atoms"), moves_over_grid(shifts, slabs, atom_devices)))
    return own, near


def stage_rows(stage, own, near, far, slabs):
    core = lax.rem(lax.axis_index("atoms"), 2)
    first, *pairs = partners(slabs)
    for place in range(TRAVEL):
        stage[place] = own[place]
        stage[first[0] * TRAVEL + place] = near[0][place]
    for (low, high), here, there in zip(pairs, near[1:], far):
        mine = jnp.where(core == 0, low, high) * TRAVEL
        other = jnp.where(core == 0, high, low) * TRAVEL
        for place in range(TRAVEL):
            stage[mine + place] = here[place]
            stage[other + place] = there[place]


def block_major(x_ref, wide, points, blocks):
    wide[...] = x_ref[0].astype(F32)
    return [wide[pl.ds(s, points, stride=blocks), :] for s in range(blocks)]


def relayout_kernel(basis, field, basis_out, field_out, wide, *, points, blocks):
    size = basis.shape[-1]
    for source, target in ((basis, basis_out), (field, field_out)):
        for s, part in enumerate(block_major(source, wide, points, blocks)):
            target[0, :, s * size : (s + 1) * size] = part.astype(BF16)


def relayout(basis, field, points, blocks):
    batches, rows, size = basis.shape
    here = pl.BlockSpec((1, rows, size), lambda b: (b, 0, 0))
    there = pl.BlockSpec((1, points, blocks * size), lambda b: (b, 0, 0))
    shape = jax.ShapeDtypeStruct((batches, points, blocks * size), BF16)
    return pl.pallas_call(
        functools.partial(relayout_kernel, points=points, blocks=blocks),
        grid=(batches,),
        out_shape=(shape, shape),
        in_specs=[here, here],
        out_specs=(there, there),
        scratch_shapes=[pltpu.VMEM((rows, size), F32)],
        compiler_params=pltpu.CompilerParams(vmem_limit_bytes=VMEM_LIMIT),
        cost_estimate=pl.CostEstimate(flops=0, bytes_accessed=8 * batches * rows * size, transcendentals=0),
    )(basis, field)


def batch_matrix(region, pattern, tiles, slab, batch, blocks, width):
    half = (width - 1) // 2
    none = tiles.shape[0] - 1
    places = [pattern[batch, s] for s in range(blocks)]
    rows = [region[slab, place] for place in places]
    strips = []
    for s in range(blocks):
        strip = []
        for t in range(blocks):
            k = rows[t] - rows[s] + half
            inside = jnp.logical_and(k >= 0, k < width)
            strip.append(tiles[jnp.where(inside, places[s] * width + k, none)])
        strips.append(jnp.concatenate(strip, axis=1))
    return jnp.concatenate(strips, axis=0)


def split(values):
    high = values.astype(BF16)
    rest = values - high.astype(F32)
    middle = rest.astype(BF16)
    low = (rest - middle.astype(F32)).astype(BF16)
    return high, middle, low


def gradient_kernel(
    region,
    pattern,
    basis,
    field,
    basis_grad,
    weights,
    weight_grad,
    fn_atom,
    batch_atom,
    places,
    *rest,
    points,
    blocks,
    width,
    owner_rows,
    slabs,
):
    *pieces, tiles, out, stage, spread, sums, energy_sums = rest
    batch = pl.program_id(0)
    batches = pl.num_programs(0)
    me = lax.axis_index("grid")
    me_atoms = lax.axis_index("atoms")
    size = tiles.shape[-1]
    region_size = region.shape[1]

    @pl.when(batch == 0)
    def _():
        tiles[region_size * width] = jnp.zeros((size, size), BF16)
        stage_rows(stage, pieces[0], pieces[1 : 1 + slabs // 2], pieces[1 + slabs // 2 :], slabs)
        for position in range(region_size):
            owner, slot, count = owner_and_slot(region, me, position, owner_rows)
            shift = jnp.bitwise_xor(me, owner)
            for k in range(width):
                tiles[position * width + k] = stage[shift * TRAVEL + travel_place(slot, count, k)]

    matrix = batch_matrix(region, pattern, tiles, me, batch, blocks, width)
    potential = lax.dot_general(field[0], matrix, NT, preferred_element_type=F32)
    rows = jnp.concatenate(
        [weights[pl.ds(batch, 1), :]]
        + [weight_grad[c, pl.ds(batch, 1), :] for c in range(PARTS)]
        + [jnp.zeros((8 - 1 - PARTS, points), F32)],
        axis=0,
    )
    columns = rows.T
    weight = columns[:, 0:1]
    energy = jnp.zeros((points, size), F32)
    for s in range(blocks):
        here = potential[:, s * size : (s + 1) * size]
        energy = energy + basis[0, :, s * size : (s + 1) * size].astype(F32) * here
        spread[pl.ds(s, points, stride=blocks), :] = here * weight
    scaled = spread[...]
    place = pl.ds(pl.multiple_of(batch * 8, 8), 8)
    for c in range(PARTS):
        terms = basis_grad[c, 0].astype(F32) * scaled
        sums[c, place, :] = jnp.sum(terms.reshape(-1, 8, size), axis=0)
        terms = energy * columns[:, 1 + c : 2 + c]
        energy_sums[c, place, :] = jnp.sum(terms.reshape(-1, 8, size), axis=0)

    @pl.when(batch == batches - 1)
    def _():
        padded = max(8, region_size)
        chosen = lax.broadcasted_iota(jnp.int32, (padded, places.shape[1]), 0) == places[...]
        chosen = chosen.astype(BF16)
        blocks_sum = []
        for c in range(PARTS):
            total = jnp.zeros((padded, size), F32)
            for piece in split(sums[c]):
                total = total + jnp.dot(chosen, piece, preferred_element_type=F32)
            blocks_sum.append(-2.0 * total)
        lefts = []
        for position in range(region_size):
            stack = jnp.concatenate([total[position : position + 1] for total in blocks_sum], axis=0)
            high, middle, low = (piece.astype(F32) for piece in split(stack))
            lefts.append(jnp.concatenate([high, middle, low, jnp.zeros((16 - 3 * PARTS, size), F32)], axis=0))
        left = jnp.concatenate(lefts, axis=1).astype(BF16)
        chunk = out.shape[-1]
        scale = [jnp.sum(energy_sums[c], axis=1, keepdims=True) for c in range(PARTS)]
        for device in range(out.shape[0]):
            atoms = lax.broadcasted_iota(jnp.int32, (chunk, size), 0) + device * chunk
            hot = [
                jnp.where(atoms == fn_atom[pl.ds(region[me, position], 1), :], 1.0, 0.0).astype(BF16)
                for position in range(region_size)
            ]
            found = lax.dot_general(left, jnp.concatenate(hot, axis=1), NT, preferred_element_type=F32)
            atoms = lax.broadcasted_iota(jnp.int32, (batch_atom.shape[0], chunk), 1) + device * chunk
            mine = atoms == batch_atom[...]
            for c in range(PARTS):
                value = found[c : c + 1] + found[PARTS + c : PARTS + c + 1] + found[2 * PARTS + c : 2 * PARTS + c + 1]
                value = value + jnp.sum(jnp.where(mine, scale[c], 0.0), axis=0, keepdims=True)
                place = jnp.bitwise_xor(me_atoms, device)
                out[place, 0, c : c + 1, :] = value
                out[jnp.bitwise_xor(place, 1), 1, c : c + 1, :] = value


def partial_gradient(
    region, pattern, basis, field, basis_grad, weights, weight_grad, fn_atom, batch_atom, pieces, shapes
):
    slabs, atom_devices, atom_total, points, blocks, width, owner_rows = shapes
    batches, _, columns = basis.shape
    size = columns // blocks
    region_size = region.shape[1]
    fn_atom = fn_atom.reshape(-1, size)
    places = jnp.broadcast_to(pattern[:, None, :], (batches, 8 // blocks, blocks)).reshape(1, -1)
    batch_atom = jnp.broadcast_to(batch_atom[:, None], (batches, 8)).reshape(-1, 1)
    block = pl.BlockSpec((1, points, columns), lambda b, *_: (b, 0, 0))
    whole = pl.BlockSpec(memory_space=pltpu.VMEM)
    tile_shape = (region_size * width + 1, size, size)
    out_shape = (atom_devices, 2, PARTS, atom_total // atom_devices)
    return pl.pallas_call(
        functools.partial(
            gradient_kernel, points=points, blocks=blocks, width=width, owner_rows=owner_rows, slabs=slabs
        ),
        grid_spec=pltpu.PrefetchScalarGridSpec(
            num_scalar_prefetch=2,
            grid=(batches,),
            in_specs=[
                block,
                block,
                pl.BlockSpec((PARTS, 1, points * blocks, size), lambda b, *_: (0, b, 0, 0)),
            ]
            + [whole] * (5 + len(pieces)),
            out_specs=(whole, whole),
            scratch_shapes=[
                pltpu.VMEM((slabs * TRAVEL, size, size), BF16),
                pltpu.VMEM((points * blocks, size), F32),
                pltpu.VMEM((PARTS, batches * 8, size), F32),
                pltpu.VMEM((PARTS, batches * 8, size), F32),
            ],
        ),
        out_shape=(jax.ShapeDtypeStruct(tile_shape, BF16), jax.ShapeDtypeStruct(out_shape, F32)),
        compiler_params=pltpu.CompilerParams(vmem_limit_bytes=VMEM_LIMIT),
    )(region, pattern, basis, field, basis_grad, weights, weight_grad, fn_atom, batch_atom, places, *pieces)


def product_kernel(region, pattern, basis, tiles, out, spread, *, points, blocks, width):
    me = lax.axis_index("grid")
    size = tiles.shape[-1]
    matrix = batch_matrix(region, pattern, tiles, me, pl.program_id(0), blocks, width)
    product = jnp.dot(basis[0], matrix, preferred_element_type=F32)
    for t in range(blocks):
        spread[pl.ds(t, points, stride=blocks), :] = product[:, t * size : (t + 1) * size]
    out[0] = spread[...].astype(BF16)


def contract(region, pattern, basis, tiles, points, blocks, width):
    batches, _, columns = basis.shape
    size = columns // blocks
    return pl.pallas_call(
        functools.partial(product_kernel, points=points, blocks=blocks, width=width),
        grid_spec=pltpu.PrefetchScalarGridSpec(
            num_scalar_prefetch=2,
            grid=(batches,),
            in_specs=[
                pl.BlockSpec((1, points, columns), lambda b, *_: (b, 0, 0)),
                pl.BlockSpec(memory_space=pltpu.VMEM),
            ],
            out_specs=pl.BlockSpec((1, points * blocks, size), lambda b, *_: (b, 0, 0)),
            scratch_shapes=[pltpu.VMEM((points * blocks, size), F32)],
        ),
        out_shape=jax.ShapeDtypeStruct((batches, points * blocks, size), BF16),
        compiler_params=pltpu.CompilerParams(vmem_limit_bytes=VMEM_LIMIT),
        cost_estimate=pl.CostEstimate(
            flops=2 * batches * points * columns * columns,
            bytes_accessed=4 * batches * points * columns,
            transcendentals=0,
        ),
    )(region, pattern, basis, tiles)


def reorder_kernel(
    pattern_hbm,
    basis,
    field,
    basis_grad,
    weights_hbm,
    basis_out,
    field_out,
    weighted,
    grads,
    pattern,
    weights,
    columns,
    landed,
    wide,
    sems,
    small_sems,
):
    batches, blocks, points, size = basis_out.shape

    def copies(batch):
        return (
            pltpu.make_async_copy(field.at[batch], landed.at[batch, 0], sems.at[batch]),
            pltpu.make_async_copy(basis.at[batch], landed.at[batch, 1], sems.at[batch]),
            pltpu.make_async_copy(basis_grad.at[:, batch], landed.at[batch, pl.ds(2, PARTS)], sems.at[batch]),
        )

    small = (
        pltpu.make_async_copy(pattern_hbm, pattern, small_sems.at[0]),
        pltpu.make_async_copy(weights_hbm, weights, small_sems.at[1]),
    )
    for copy in small:
        copy.start()

    @pl.loop(0, batches)
    def _(batch):
        for copy in copies(batch):
            copy.start()

    for copy in small:
        copy.wait()
    rows = jnp.concatenate([weights[...], jnp.zeros((size - batches, points), F32)], axis=0).T
    for batch in range(batches):
        columns[batch] = jnp.broadcast_to(rows[:, batch : batch + 1], (points, size))

    @pl.loop(0, batches, unroll=2)
    def _(batch):
        pltpu.make_async_copy(landed.at[batch], landed.at[batch], sems.at[batch]).wait()
        points_here = pl.ds(pl.multiple_of(batch * points, points), points)
        places = [pattern[s, batch] for s in range(blocks)]
        for array in range(2 + PARTS):
            wide[array] = landed[batch, array].astype(F32)
        for s, place in enumerate(places):
            strided = pl.ds(s, points, stride=blocks)
            values = wide[0, strided, :]
            field_out[batch, place] = values.astype(BF16)
            weighted[place, points_here, :] = (values * columns[batch]).astype(BF16)
            basis_out[batch, place] = wide[1, strided, :].astype(BF16)
            for c in range(PARTS):
                grads[c, place, points_here, :] = wide[2 + c, strided, :].astype(BF16)


def reorder(pattern, basis, field, basis_grad, weights, points, blocks):
    batches, rows, size = basis.shape
    hbm = pl.BlockSpec(memory_space=pl.ANY)
    vmem = pl.BlockSpec(memory_space=pltpu.VMEM)
    ordered = jax.ShapeDtypeStruct((batches, blocks, points, size), BF16)
    return pl.pallas_call(
        reorder_kernel,
        out_shape=(
            ordered,
            ordered,
            jax.ShapeDtypeStruct((blocks, batches * points, size), BF16),
            jax.ShapeDtypeStruct((PARTS, blocks, batches * points, size), BF16),
        ),
        in_specs=[hbm] * 5,
        out_specs=(vmem,) * 4,
        scratch_shapes=[
            pltpu.SMEM((blocks, batches), jnp.int32),
            pltpu.VMEM(weights.shape, F32),
            pltpu.VMEM((batches, points, size), F32),
            pltpu.VMEM((batches, 2 + PARTS, rows, size), BF16),
            pltpu.VMEM((2 + PARTS, rows, size), F32),
            pltpu.SemaphoreType.DMA((batches,)),
            pltpu.SemaphoreType.DMA((2,)),
        ],
        compiler_params=pltpu.CompilerParams(vmem_limit_bytes=VMEM_LIMIT),
        cost_estimate=pl.CostEstimate(
            flops=0, bytes_accessed=2 * (2 + PARTS) * batches * rows * size, transcendentals=0
        ),
    )(in_hbm(pattern.T), in_hbm(basis), in_hbm(field), in_hbm(basis_grad), in_hbm(weights))


def moment_kernel(weighted, grads, moments):
    blocks, _, size = grads.shape[1:]
    for p in range(0, blocks, 2):
        first, last = max(p - 1, 0), min(p + 3, blocks)
        left = jnp.concatenate([weighted[place] for place in range(first, last)], axis=1)
        for c in range(PARTS):
            right = jnp.concatenate([grads[c, p], grads[c, p + 1]], axis=1)
            moments[c, first * size : last * size, p * size : (p + 2) * size] = lax.dot_general(
                left, right, TN, preferred_element_type=F32
            )


def build_moments(weighted, grads):
    blocks, depth, size = grads.shape[1:]
    vmem = pl.BlockSpec(memory_space=pltpu.VMEM)
    return pl.pallas_call(
        moment_kernel,
        out_shape=jax.ShapeDtypeStruct((PARTS, blocks * size, blocks * size), F32),
        in_specs=[vmem, vmem],
        out_specs=vmem,
        compiler_params=pltpu.CompilerParams(vmem_limit_bytes=VMEM_LIMIT),
        cost_estimate=pl.CostEstimate(
            flops=2 * PARTS * depth * (blocks * size) ** 2, bytes_accessed=0, transcendentals=0
        ),
    )(weighted, grads)


def atom_kernel(region, fn_atom, batch_atom, weight_grad, hot, grad_columns):
    batches, points = weight_grad.shape[1:]
    size = fn_atom.shape[1]
    blocks = region.shape[1]
    me = lax.axis_index("grid")
    atoms = lax.broadcasted_iota(jnp.int32, (hot.shape[0], size), 0)
    ids = jnp.concatenate([batch_atom[...], jnp.full((1, size - batches), -1, jnp.int32)], axis=1)
    hot[:, blocks * size :] = jnp.where(atoms == ids, 1.0, 0.0).astype(BF16)

    @pl.loop(0, blocks)
    def _(position):
        ids = fn_atom[pl.ds(region[me, position], 1), :]
        columns = pl.ds(pl.multiple_of(position * size, size), size)
        hot[:, columns] = jnp.where(atoms == ids, 1.0, 0.0).astype(BF16)

    for c in range(PARTS):
        padding = jnp.zeros((size - batches, points), F32)
        grad_columns[c] = jnp.concatenate([weight_grad[c], padding], axis=0).T


def atom_matrix(region, fn_atom, batch_atom, weight_grad, blocks, size, atom_total):
    vmem = pl.BlockSpec(memory_space=pltpu.VMEM)
    return pl.pallas_call(
        atom_kernel,
        out_shape=(
            jax.ShapeDtypeStruct((atom_total, (blocks + 1) * size), BF16),
            jax.ShapeDtypeStruct((PARTS, weight_grad.shape[2], size), F32),
        ),
        in_specs=[pl.BlockSpec(memory_space=pltpu.SMEM)] + [vmem] * 3,
        out_specs=(vmem, vmem),
        compiler_params=pltpu.CompilerParams(vmem_limit_bytes=VMEM_LIMIT),
        cost_estimate=pl.CostEstimate(flops=1000000000, bytes_accessed=2 * atom_total * size, transcendentals=0),
    )(region, fn_atom.reshape(-1, size), batch_atom.reshape(1, -1), weight_grad)


def combine_kernel(
    region, basis, field, moments, hot, grad_columns, *rest, owner_rows, slabs, width
):
    *pieces, product_out, out, stage, matrix = rest
    batches, blocks, points, size = basis.shape
    me = lax.axis_index("grid")
    me_atoms = lax.axis_index("atoms")
    half = (width - 1) // 2
    stage_rows(stage, pieces[0], pieces[1 : 1 + slabs // 2], pieces[1 + slabs // 2 :], slabs)
    rows = [region[me, position] for position in range(blocks)]
    found = [owner_and_slot(region, me, position, owner_rows) for position in range(blocks)]
    totals = [[jnp.zeros((8, size), F32) for _ in range(blocks)] for _ in range(PARTS)]
    for p in range(blocks):
        owner, slot, count = found[p]
        first = jnp.bitwise_xor(me, owner) * TRAVEL
        for q in range(blocks):
            if abs(q - p) > half:
                matrix[p * size : (p + 1) * size, q * size : (q + 1) * size] = jnp.zeros((size, size), BF16)
                continue
            k = rows[q] - rows[p] + half
            place = jnp.where(
                k == 0,
                travel_place(slot, count, 0),
                jnp.where(k == 1, travel_place(slot, count, 1), travel_place(slot, count, 2)),
            )
            inside = jnp.logical_and(k >= 0, k < width)
            tile = jnp.where(inside, stage[first + place], jnp.zeros((size, size), BF16))
            matrix[p * size : (p + 1) * size, q * size : (q + 1) * size] = tile
            turned = tile.T.astype(F32)
            for c in range(PARTS):
                terms = turned * moments[c, q * size : (q + 1) * size, p * size : (p + 1) * size]
                totals[c][p] = totals[c][p] + jnp.sum(terms.reshape(-1, 8, size), axis=0)
    derivative = [
        jnp.concatenate([jnp.sum(total, axis=0, keepdims=True) for total in totals[c]], axis=1) for c in range(PARTS)
    ]

    energies = jnp.zeros((points, size), F32)
    lanes = lax.broadcasted_iota(jnp.int32, (points, size), 1)
    left = [jnp.concatenate([basis[batch, p] for p in range(blocks)], axis=1) for batch in range(batches)]
    left = jnp.concatenate(left, axis=0)
    energy = [jnp.zeros((points, size), F32) for _ in range(batches)]
    for q in range(0, blocks, 2):
        product = jnp.dot(left, matrix[:, q * size : (q + 2) * size], preferred_element_type=F32)
        for batch in range(batches):
            for column in range(2):
                part = product[batch * points : (batch + 1) * points, column * size : (column + 1) * size]
                product_out[batch, q + column] = part.astype(BF16)
                energy[batch] = energy[batch] + part * field[batch, q + column].astype(F32)
    for batch in range(batches):
        energies = jnp.where(lanes == batch, jnp.sum(energy[batch], axis=1, keepdims=True), energies)

    lefts = []
    for c in range(PARTS):
        term = jnp.sum(energies * grad_columns[c], axis=0, keepdims=True)
        lefts.append(jnp.concatenate([-2.0 * derivative[c], term], axis=1))
    left = jnp.concatenate(lefts, axis=0)
    high, middle, low = (piece.astype(F32) for piece in split(left))
    left = jnp.concatenate([high, middle, low, jnp.zeros((16 - 3 * PARTS, left.shape[1]), F32)], axis=0).astype(BF16)
    chunk = out.shape[-1]
    for device in range(out.shape[0]):
        sums = lax.dot_general(
            left, hot[device * chunk : (device + 1) * chunk, :], NT, preferred_element_type=F32
        )
        value = sums[:PARTS] + sums[PARTS : 2 * PARTS] + sums[2 * PARTS : 3 * PARTS]
        place = jnp.bitwise_xor(me_atoms, device)
        out[place, 0] = value
        out[jnp.bitwise_xor(place, 1), 1] = value


def combine(region, prepared, pieces, shapes):
    basis, field, moments, hot, grad_columns = prepared
    slabs, atom_devices, atom_total, points, blocks, width, owner_rows = shapes
    batches, _, _, size = basis.shape
    vmem = pl.BlockSpec(memory_space=pltpu.VMEM)
    return pl.pallas_call(
        functools.partial(combine_kernel, owner_rows=owner_rows, slabs=slabs, width=width),
        out_shape=(
            jax.ShapeDtypeStruct(basis.shape, BF16),
            jax.ShapeDtypeStruct((atom_devices, 2, PARTS, atom_total // atom_devices), F32),
        ),
        in_specs=[pl.BlockSpec(memory_space=pltpu.SMEM)] + [vmem] * (5 + len(pieces)),
        out_specs=(vmem, vmem),
        scratch_shapes=[
            pltpu.VMEM((slabs * TRAVEL, size, size), BF16),
            pltpu.VMEM((blocks * size, blocks * size), BF16),
        ],
        compiler_params=pltpu.CompilerParams(vmem_limit_bytes=VMEM_LIMIT),
    )(region, basis, field, moments, hot, grad_columns, *pieces)


def write_kernel(pattern, product, out, wide, staged, sems):
    batches, blocks, points, size = product.shape

    def copy(batch):
        return pltpu.make_async_copy(staged.at[batch], out.at[batch], sems.at[batch])

    @pl.loop(0, batches // 2)
    def _(pair):
        for inner in range(2):
            batch = pair * 2 + inner
            for t in range(blocks):
                wide[inner, pl.ds(t, points, stride=blocks), :] = product[batch, pattern[t, batch]].astype(F32)
            staged[batch] = wide[inner].astype(BF16)
            copy(batch).start()

    @pl.loop(0, batches)
    def _(batch):
        copy(batch).wait()


def write(pattern, product):
    batches, blocks, points, size = product.shape
    shape = (batches, points * blocks, size)
    return pl.pallas_call(
        write_kernel,
        out_shape=jax.ShapeDtypeStruct(shape, BF16),
        in_specs=[pl.BlockSpec(memory_space=pltpu.SMEM), pl.BlockSpec(memory_space=pltpu.VMEM)],
        out_specs=pl.BlockSpec(memory_space=pl.ANY),
        scratch_shapes=[
            pltpu.VMEM((2, points * blocks, size), F32),
            pltpu.VMEM(shape, BF16),
            pltpu.SemaphoreType.DMA((batches,)),
        ],
        compiler_params=pltpu.CompilerParams(vmem_limit_bytes=VMEM_LIMIT),
        cost_estimate=pl.CostEstimate(flops=0, bytes_accessed=4 * math.prod(shape), transcendentals=0),
    )(pattern.T, product)


def swap_between_cores(near, ready, atom_devices):
    far, ready = lax.optimization_barrier((near[1:], ready))
    near = [near[0], *far]
    swap = [(i, i ^ 1) for i in range(atom_devices)]
    return near, [lax.ppermute(piece, "atoms", swap) for piece in near[1:]], ready


def tree_sum(values):
    if len(values) == 1:
        return values[0]
    half = len(values) // 2
    return tree_sum(values[:half]) + tree_sum(values[half:])


def pair_sums(values):
    return [values[i] + values[i + 1] for i in range(0, len(values), 2)]


def sum_parts(partial_grad, contracted, slabs, atom_devices):
    parts = [partial_grad[0]]
    for d in range(1, atom_devices):
        parts.append(lax.ppermute(partial_grad[d], "atoms", [(i, i ^ d) for i in range(atom_devices)]))
    parts, contracted = lax.optimization_barrier((parts, contracted))
    both = tree_sum(pair_sums(parts))
    swap = [(i, i ^ 1) for i in range(atom_devices)]
    far = []
    for shifts in partners(slabs)[1:]:
        far.append(lax.ppermute(both, ("grid", "atoms"), moves_over_grid(shifts, slabs, atom_devices)))
    near = lax.ppermute(both[0], "grid", [(i, i ^ 1) for i in range(slabs)])
    far = lax.optimization_barrier(far)
    swapped = [lax.ppermute(piece[1], "atoms", swap) for piece in far]
    sums = [both[0] + near] + [piece[0] + other for piece, other in zip(far, swapped)]
    return tree_sum(sums), contracted


def local(
    basis,
    basis_grad,
    exchange_field,
    weights,
    weight_grad,
    density,
    region,
    pattern,
    fn_atom,
    batch_atom,
):
    batches, points, blocks, size = basis.shape
    owner_rows, width = density.shape[:2]
    slabs = lax.axis_size("grid")
    atom_devices = lax.axis_size("atoms")
    atom_total = fn_atom.shape[0] // (10 * slabs * atom_devices) * slabs * atom_devices
    shapes = (slabs, atom_devices, atom_total, points, blocks, width, owner_rows)
    flat_basis = basis.reshape(batches, points * blocks, size)
    flat_field = exchange_field.reshape(batches, points * blocks, size)
    flat_grad = basis_grad.reshape(PARTS, batches, points * blocks, size)
    own, near = fetch_rows(region, density, slabs, atom_devices)
    if region.shape[1] == blocks:
        basis_wide, field_wide, weighted, grads = reorder(
            pattern, flat_basis, flat_field, flat_grad, weights, points, blocks
        )
        ready = (basis_wide, field_wide, build_moments(weighted, grads), batch_atom)
        near, far, (basis_wide, field_wide, moments, batch_atom) = swap_between_cores(near, ready, atom_devices)
        hot, grad_columns = atom_matrix(region, fn_atom, batch_atom, weight_grad, blocks, size, atom_total)
        ready = (basis_wide, field_wide, moments, hot, grad_columns)
        product, partial_grad = combine(region, ready, [own, *near, *far], shapes)
        gradient, contracted = sum_parts(partial_grad, write(pattern, product), slabs, atom_devices)
        return contracted.reshape(basis.shape), gradient
    ready = relayout(in_hbm(flat_basis), in_hbm(flat_field), points, blocks)
    near, far, (basis_wide, field_wide) = swap_between_cores(near, ready, atom_devices)
    tiles, partial_grad = partial_gradient(
        region,
        pattern,
        basis_wide,
        field_wide,
        in_hbm(flat_grad),
        weights,
        weight_grad,
        fn_atom,
        batch_atom,
        [own, *near, *far],
        shapes,
    )
    contracted = contract(region, pattern, basis_wide, tiles, points, blocks, width)
    gradient, contracted = sum_parts(partial_grad, contracted, slabs, atom_devices)
    return contracted.reshape(basis.shape), gradient


def solution(mesh):
    placed = (
        P(("groups", "grid", "atoms"), None, None, None),
        P(None, ("groups", "grid", "atoms"), None, None, None),
        P(("groups", "grid", "atoms"), None, None, None),
        P(("groups", "grid", "atoms"), None),
        P(None, ("groups", "grid", "atoms"), None),
        P(("groups", "grid"), None, None, None),
        P("groups", None),
        P(("groups", "grid", "atoms"), None),
        P("groups"),
        P(("groups", "grid", "atoms")),
    )
    return jax.shard_map(
        local,
        mesh=mesh,
        in_specs=placed,
        out_specs=(P(("groups", "grid", "atoms"), None, None, None), P(None, ("groups", "atoms"))),
        check_vma=False,
    )
```
